32 devices in a mesh: dp: 4 (over z), wide: 8 (over y, x, core).
Axes of the slice: x: 2, y: 2, z: 4, core: 2. Of those that a mesh axis runs over, the one named last changes fastest.
Arguments:
- tokens: bfloat16 [32768, 1024], P(('dp', 'wide')), may hold values from -6 to 6
- cotangent: bfloat16 [32768, 1024], P(('dp', 'wide')), may hold values from -6 to 6
- lengths: int32 [32, 2], P(('dp', 'wide')), may hold values from 0 to 1024, as said below
- in_weight: bfloat16 [1024, 3072], P(('dp', 'wide')), may hold values from -0.1875 to 0.1875
- query_bias: bfloat16 [1024], P(('dp', 'wide')), may hold values from -3 to 3
- value_bias: bfloat16 [1024], P(('dp', 'wide')), may hold values from -3 to 3
- out_weight: bfloat16 [1024, 1024], P(('dp', 'wide')), may hold values from -0.1875 to 0.1875
- out_bias: bfloat16 [1024], P(('dp', 'wide')), may hold values from -3 to 3
- head_scale: bfloat16 [16], replicated, may hold values from 0.29882812 to 3
- pre_gain: bfloat16 [1024], P(('dp', 'wide')), may hold values from 0.25 to 1.75
- pre_bias: bfloat16 [1024], P(('dp', 'wide')), may hold values from -3 to 3
- post_gain: bfloat16 [1024], P(('dp', 'wide')), may hold values from 0.25 to 1.75
- post_bias: bfloat16 [1024], P(('dp', 'wide')), may hold values from -3 to 3
- feed_gain: bfloat16 [1024], P(('dp', 'wide')), may hold values from 0.25 to 1.75
- feed_bias: bfloat16 [1024], P(('dp', 'wide')), may hold values from -3 to 3
- up_weight: bfloat16 [1024, 4096], P(None, 'wide'), may hold values from -0.1875 to 0.1875
- up_bias: bfloat16 [4096], P('wide'), may hold values from -3 to 3
- mid_gain: bfloat16 [4096], P('wide'), may hold values from 0.25 to 1.75
- mid_bias: bfloat16 [4096], P('wide'), may hold values from -3 to 3
- down_weight: bfloat16 [4096, 1024], P('wide'), may hold values from -0.09375 to 0.09375
- down_bias: bfloat16 [1024], replicated, may hold values from -3 to 3
Outputs:
- mixed: bfloat16 [32768, 1024], P(('dp', 'wide'))
- tokens_grad: bfloat16 [32768, 1024], P(('dp', 'wide'))
- in_weight_grad: float32 [1024, 3072], P(('dp', 'wide'))
- query_bias_grad: float32 [1024], P(('dp', 'wide'))
- value_bias_grad: float32 [1024], P(('dp', 'wide'))
- out_weight_grad: float32 [1024, 1024], P(('dp', 'wide'))
- out_bias_grad: float32 [1024], P(('dp', 'wide'))
- head_scale_grad: float32 [16], replicated
- pre_gain_grad: float32 [1024], P(('dp', 'wide'))
- pre_bias_grad: float32 [1024], P(('dp', 'wide'))
- post_gain_grad: float32 [1024], P(('dp', 'wide'))
- post_bias_grad: float32 [1024], P(('dp', 'wide'))
- feed_gain_grad: float32 [1024], P(('dp', 'wide'))
- feed_bias_grad: float32 [1024], P(('dp', 'wide'))
- up_weight_grad: float32 [1024, 4096], P(None, 'wide')
- up_bias_grad: float32 [4096], P('wide')
- mid_gain_grad: float32 [4096], P('wide')
- mid_bias_grad: float32 [4096], P('wide')
- down_weight_grad: float32 [4096, 1024], P('wide')
- down_bias_grad: float32 [1024], replicated
The draws below stay inside these ranges and needn't reach their ends.
Inputs may be any that keep to these rules, and one draw needn't show every extreme that they name: `lengths`: each pack holds either one sequence of 1024 rows and a 0, or two sequences of 512 rows; both kinds occur in every draw.
All inputs are finite; a program needn't handle non-finite values.
Results may differ from the reference program's by a relative error of at most 0.017.
Values may be sent and summed in bfloat16 or wider, within the bound.
A program may use at most 320 MiB of HBM per device.

```python
import math
import jax
import jax.numpy as jnp
from jax import lax

D = 1024
H = 16
HD = 64
FF = 4096
ROWS_DEV = 1024
PACKS = 32
TOKENS = 32768


def draw_lengths(key, part):
    key = jax.random.fold_in(key, 11)
    pick_key, shuffle_key = jax.random.split(key)
    groups = jax.random.randint(pick_key, (PACKS,), 0, 2)
    shuffled = jax.random.permutation(shuffle_key, PACKS)
    groups = groups.at[shuffled[0]].set(0).at[shuffled[1]].set(1)
    leading = jnp.where(groups == 0, ROWS_DEV, ROWS_DEV // 2)
    return jnp.stack([leading, ROWS_DEV - leading], axis=1).astype(jnp.int32)


def spiked(result, rng, source, target, blocks, factor):
    owner, partner = [(jnp.arange(result.shape[axis_at]) // (result.shape[axis_at] // blocks)).reshape([-1 if axis == axis_at else 1 for axis in range(result.ndim)]) for axis_at in (source, target)]
    chosen = jax.random.permutation(rng, blocks)[partner]
    strong = (owner == chosen) | (owner == (partner + blocks // 2) % blocks)
    return jnp.where(strong, factor * result, result)


def block_scale(stream_key, dims, pieces, least, high):
    gain = 1.0
    for dim, blocks in pieces:
        heights = jax.random.uniform(jax.random.fold_in(jax.random.fold_in(stream_key, 6), dim), (blocks,), jnp.float32, least / len(pieces), high / len(pieces))
        gain = gain * jnp.repeat(jnp.exp(heights), dims[dim] // blocks).reshape((-1,) + (1,) * (len(dims) - 1 - dim))
    return gain


def gaussian(own_key, shape, width, most, pieces=(), dtype=jnp.bfloat16):
    values = jax.random.normal(own_key, shape, jnp.float32) * width
    if len(pieces) > 0:
        values = block_scale(own_key, shape, pieces, -0.22, 0.18) * values
    return jnp.clip(values, min=-most, max=most).astype(dtype)


def bell_draw_with(stream_key, extent, deviation, bound, cuts, heavy, dtype=jnp.bfloat16):
    result = deviation * jax.random.normal(stream_key, extent, jnp.float32)
    if cuts:
        result = result * block_scale(stream_key, extent, cuts, -0.22, 0.18)
    return jnp.clip(spiked(result, jax.random.fold_in(stream_key, 3), *heavy), -bound, bound).astype(dtype)


def setup_inputs(seed: int = 0) -> dict:
    key_of = jax.random.split(jax.random.key(seed), 22)
    tokens = bell_draw_with(key_of[0], (TOKENS, D), 1.0, 6.0, ((0, 32),), (0, 1, 32, 2.75))
    cotangent = gaussian(key_of[1], (TOKENS, D), 1.0, 6.0, ((0, 32),))
    lengths = draw_lengths(jax.random.fold_in(key_of[21], 71), 0)
    in_weight = gaussian(key_of[3], (D, 3 * D), D ** -0.5, 0.1875, ((0, 32),))
    query_bias = gaussian(key_of[4], (D,), 0.5, 3.0, ((0, 32),))
    value_bias = gaussian(key_of[5], (D,), 0.5, 3.0, ((0, 32),))
    out_weight = gaussian(key_of[6], (D, D), D ** -0.5, 0.1875, ((0, 32),))
    out_bias = gaussian(key_of[7], (D,), 0.5, 3.0, ((0, 32),))
    head_scale = jnp.clip(jnp.exp(jax.random.uniform(key_of[8], (H,), jnp.float32, math.log(0.29882812), math.log(3.0))), 0.29882812, 3.0).astype(jnp.bfloat16)
    pre_gain = jnp.clip(1.0 + 0.15 * jax.random.normal(key_of[9], (D,), jnp.float32), 0.25, 1.75).astype(jnp.bfloat16)
    pre_bias = gaussian(key_of[10], (D,), 0.5, 3.0, ((0, 32),))
    post_gain = jnp.clip(1.0 + 0.15 * jax.random.normal(key_of[11], (D,), jnp.float32), 0.25, 1.75).astype(jnp.bfloat16)
    post_bias = gaussian(key_of[12], (D,), 0.5, 3.0, ((0, 32),))
    feed_gain = jnp.clip(1.0 + 0.15 * jax.random.normal(key_of[13], (D,), jnp.float32), 0.25, 1.75).astype(jnp.bfloat16)
    feed_bias = gaussian(key_of[14], (D,), 0.5, 3.0, ((0, 32),))
    up_weight = gaussian(key_of[15], (D, FF), D ** -0.5, 0.1875, ((1, 8),))
    up_bias = gaussian(key_of[16], (FF,), 0.5, 3.0, ((0, 8),))
    mid_gain = jnp.clip(1.0 + 0.15 * jax.random.normal(key_of[17], (FF,), jnp.float32), 0.25, 1.75).astype(jnp.bfloat16)
    mid_bias = gaussian(key_of[18], (FF,), 0.5, 3.0, ((0, 8),))
    down_weight = gaussian(key_of[19], (FF, D), FF ** -0.5, 0.09375, ((0, 8),))
    down_bias = gaussian(key_of[20], (D,), 0.5, 3.0)
    return dict(tokens=tokens, cotangent=cotangent, lengths=lengths, in_weight=in_weight, query_bias=query_bias, value_bias=value_bias, out_weight=out_weight, out_bias=out_bias, head_scale=head_scale, pre_gain=pre_gain, pre_bias=pre_bias, post_gain=post_gain, post_bias=post_bias, feed_gain=feed_gain, feed_bias=feed_bias, up_weight=up_weight, up_bias=up_bias, mid_gain=mid_gain, mid_bias=mid_bias, down_weight=down_weight, down_bias=down_bias)


EPS = 1e-05
HIGH = lax.Precision.HIGHEST
MASKED = -1e+30

@jax.custom_vjp
def low(v):
    return lax.optimization_barrier(v.astype(jnp.bfloat16)).astype(jnp.float32)

@jax.custom_vjp
def low_back(v):
    return v

def low_keep(v):
    return (low(v), None)

def low_pass(kept, grad):
    return (grad,)

def back_keep(v):
    return (v, None)

def back_low(kept, grad):
    return (low(grad),)
low.defvjp(low_keep, low_pass)
low_back.defvjp(back_keep, back_low)

def both_ways(values):
    return low(low_back(values))

def normalize(values, gain_row, bias_row):
    center = values - lax.optimization_barrier(jnp.mean(values, axis=-1, keepdims=True))
    spread = lax.optimization_barrier(jnp.mean(center * center, axis=-1, keepdims=True))
    return center * lax.rsqrt(spread + EPS) * gain_row + bias_row

def matmul(left_side, right_side):
    return jnp.dot(left_side, right_side, precision=HIGH, preferred_element_type=jnp.float32)

def pack_layer(rows_in, pack_lengths, in_weight, query_bias, value_bias, out_weight, out_bias, head_scale, pre_gain, pre_bias, post_gain, post_bias, feed_gain, feed_bias, up_weight, up_bias, mid_gain, mid_bias, down_weight, down_bias):
    first_normed = low(normalize(rows_in, pre_gain, pre_bias))
    projected = matmul(first_normed, in_weight)
    query_rows = both_ways(projected[:, :D] + query_bias).reshape(ROWS_DEV, H, HD)
    key_rows = both_ways(projected[:, D:2 * D]).reshape(ROWS_DEV, H, HD)
    value_rows = both_ways(projected[:, 2 * D:] + value_bias).reshape(ROWS_DEV, H, HD)
    position = lax.iota(jnp.int32, ROWS_DEV)
    segment = (position >= pack_lengths[0]).astype(jnp.int32)
    allowed = (position[None, :] <= position[:, None]) & (segment[None, :] == segment[:, None])
    scores = low_back(jnp.einsum('qhd,khd->hqk', query_rows, key_rows, precision=HIGH) * HD ** (-0.5))
    scores = jnp.where(allowed[None], scores, MASKED)
    weights = jax.nn.softmax(scores, axis=-1)
    attended = low_back(jnp.einsum('hqk,khd->qhd', low(weights), value_rows, precision=HIGH))
    scaled = low((attended * head_scale[None, :, None]).reshape(ROWS_DEV, D))
    branch = low_back(matmul(scaled, out_weight) + out_bias)
    middle = rows_in + normalize(branch, post_gain, post_bias)
    feed_normed = low(normalize(middle, feed_gain, feed_bias))
    pre_act = low_back(matmul(feed_normed, up_weight) + up_bias)
    mid_out = low(normalize(jax.nn.gelu(pre_act, approximate=False), mid_gain, mid_bias))
    return middle + low_back(matmul(mid_out, down_weight)) + down_bias

def forward(lengths, tokens_f, *params):

    def one_pack(packed):
        return pack_layer(packed[0], packed[1], *params)
    mixed = lax.map(jax.checkpoint(one_pack), (tokens_f.reshape(PACKS, ROWS_DEV, D), lengths))
    return mixed.reshape(TOKENS, D)

def reference(tokens, cotangent, lengths, in_weight, query_bias, value_bias, out_weight, out_bias, head_scale, pre_gain, pre_bias, post_gain, post_bias, feed_gain, feed_bias, up_weight, up_bias, mid_gain, mid_bias, down_weight, down_bias):
    floats = [array.astype(jnp.float32) for array in (tokens, in_weight, query_bias, value_bias, out_weight, out_bias, head_scale, pre_gain, pre_bias, post_gain, post_bias, feed_gain, feed_bias, up_weight, up_bias, mid_gain, mid_bias, down_weight, down_bias)]

    def run_layer(*values):
        return forward(lengths, *values)
    mixed, pull_back = jax.vjp(run_layer, *floats)
    grads = pull_back(cotangent.astype(jnp.float32))
    return (mixed.astype(jnp.bfloat16), grads[0].astype(jnp.bfloat16), grads[1], grads[2], grads[3], grads[4], grads[5], grads[6], grads[7], grads[8], grads[9], grads[10], grads[11], grads[12], grads[13], grads[14], grads[15], grads[16], grads[17], grads[18])
```

```python
import functools

import jax
import jax.numpy as jnp
from jax import lax
from jax.experimental import pallas as pl
from jax.experimental.pallas import tpu as pltpu
from jax.sharding import PartitionSpec as P

EPS = 1e-05
ROOT_HALF = 0.7071067811865476
INV_ROOT_TAU = 0.3989422804014327
LOG2E = 1.4426950408889634
MASKED = -1e30
BF = jnp.bfloat16
F32 = jnp.float32
TILE = 256
UNITS = 512
MESH = pl.DeviceIdType.MESH
VMEM_LIMIT = 60 * 1024 * 1024
ANY = pl.BlockSpec(memory_space=pl.ANY)


def dot_nn(left, right):
    return lax.dot_general(left, right, (((1,), (0,)), ((), ())), preferred_element_type=F32)


def dot_nt(left, right):
    return lax.dot_general(left, right, (((1,), (1,)), ((), ())), preferred_element_type=F32)


def dot_tn(left, right):
    return lax.dot_general(left, right, (((0,), (0,)), ((), ())), preferred_element_type=F32)


def params(**more):
    return pltpu.CompilerParams(
        dimension_semantics=("arbitrary",), vmem_limit_bytes=VMEM_LIMIT, **more
    )


def whole(shape):
    zeros = (0,) * len(shape)
    return pl.BlockSpec(shape, lambda *_: zeros, pipeline_mode=pl.Buffered(1))


def row_norm(values):
    center = values - jnp.mean(values, axis=-1, keepdims=True)
    inv = lax.rsqrt(jnp.mean(center * center, axis=-1, keepdims=True) + EPS)
    return center * inv, inv


def norm_back(grad, gain, normed, inv):
    scaled = grad * gain
    first = jnp.mean(scaled, axis=-1, keepdims=True)
    cross = jnp.mean(scaled * normed, axis=-1, keepdims=True)
    return inv * (scaled - first - normed * cross)


def column_sum(values):
    return jnp.sum(values, axis=0, keepdims=True)


def lane_fold(values):
    total = values[:, :128]
    for start in range(128, values.shape[1], 128):
        total = total + values[:, start : start + 128]
    return total


def in_proj_kernel(tokens_ref, weight_ref, gain_ref, shift_ref, bias_ref, first_ref, out_ref):
    @pl.when(pl.program_id(0) == 0)
    def _():
        for start in range(0, tokens_ref.shape[0], TILE):
            rows = pl.ds(start, TILE)
            normed, _ = row_norm(tokens_ref[rows].astype(F32))
            first_ref[rows] = (normed * gain_ref[...] + shift_ref[...]).astype(BF)

    for start in range(0, tokens_ref.shape[0], TILE):
        rows = pl.ds(start, TILE)
        out_ref[rows] = (dot_nn(first_ref[rows], weight_ref[...]) + bias_ref[...]).astype(BF)


def in_proj(tokens, weights, gain, shift, bias):
    rows, width = tokens.shape
    columns = bias.shape[1]
    return pl.pallas_call(
        in_proj_kernel,
        grid=(columns // 512,),
        in_specs=[
            whole((rows, width)),
            pl.BlockSpec((width, 512), lambda j: (0, j)),
            whole((1, width)),
            whole((1, width)),
            pl.BlockSpec((1, 512), lambda j: (0, j)),
        ],
        out_specs=[whole((rows, width)), pl.BlockSpec((rows, 512), lambda j: (0, j))],
        out_shape=[
            jax.ShapeDtypeStruct((rows, width), BF),
            jax.ShapeDtypeStruct((rows, columns), BF),
        ],
        compiler_params=params(),
        name="in_proj",
    )(tokens, weights, gain, shift, bias)


def attention_pair(cross, q_ref, k_ref, v_ref, hs_ref, scaled_ref, out_ref, lse_ref, vext_ref):
    rows = q_ref.shape[0]
    half = rows // 2
    factor = LOG2E * (q_ref.shape[1] // 2) ** (-0.5)
    low_lanes = lax.broadcasted_iota(jnp.int32, (1, 128), 1) < 64
    below = lax.broadcasted_iota(jnp.int32, (TILE, TILE), 1) <= lax.broadcasted_iota(
        jnp.int32, (TILE, TILE), 0
    )
    vext_ref[:, :128] = v_ref[...]
    vext_ref[:, 128:] = jnp.ones((rows, 128), BF)
    for start in range(0, rows, TILE):
        stop = start + TILE
        query = q_ref[start:stop]
        results = []
        for head in range(2):
            mine = low_lanes if head == 0 else ~low_lanes
            own = jnp.where(mine, query, jnp.zeros_like(query))
            raw = dot_nt(own, k_ref[:stop])
            parts = []
            if start >= half:
                parts.append((raw[:, :half], cross))
                if start > half:
                    parts.append((raw[:, half:start], None))
            elif start > 0:
                parts.append((raw[:, :start], None))
            parts.append((jnp.where(below, raw[:, start:stop], MASKED), None))
            peak = None
            for piece, shift in parts:
                top = jnp.max(piece, axis=-1, keepdims=True)
                if shift is not None:
                    top = top + shift
                peak = top if peak is None else jnp.maximum(peak, top)
            weights = []
            for piece, shift in parts:
                level = peak if shift is None else peak - shift
                weights.append(jnp.exp2((piece - level) * factor).astype(BF))
            weights = weights[0] if len(weights) == 1 else jnp.concatenate(weights, axis=1)
            both = dot_nn(weights, vext_ref[:stop])
            total = both[:, 128:]
            results.append((both[:, :128] / total, peak * factor + jnp.log2(total)))
        mixed = jnp.where(low_lanes, results[0][0], results[1][0])
        out_ref[start:stop] = mixed
        scaled_ref[start:stop] = (mixed * hs_ref[...]).astype(BF)
        lse = jnp.where(low_lanes, results[0][1], results[1][1]).T
        lse_ref[0, 0:1, start:stop] = lse[0:1]
        lse_ref[0, 1:2, start:stop] = lse[64:65]


def attention_kernel(cross_ref, *refs):
    attention_pair(cross_ref[0, 0], *refs)


def attention(cross, projected, head_lanes):
    rows = projected.shape[0]
    width = projected.shape[1] // 3
    pairs = width // 128
    return pl.pallas_call(
        attention_kernel,
        grid=(pairs,),
        in_specs=[
            pl.BlockSpec(memory_space=pltpu.SMEM),
            pl.BlockSpec((rows, 128), lambda p: (0, p)),
            pl.BlockSpec((rows, 128), lambda p: (0, pairs + p)),
            pl.BlockSpec((rows, 128), lambda p: (0, 2 * pairs + p)),
            pl.BlockSpec((1, 128), lambda p: (0, p)),
        ],
        out_specs=[
            pl.BlockSpec((rows, 128), lambda p: (0, p)),
            pl.BlockSpec((rows, 128), lambda p: (0, p)),
            pl.BlockSpec((1, 8, rows), lambda p: (p, 0, 0)),
        ],
        out_shape=[
            jax.ShapeDtypeStruct((rows, width), BF),
            jax.ShapeDtypeStruct((rows, width), F32),
            jax.ShapeDtypeStruct((pairs, 8, rows), F32),
        ],
        scratch_shapes=[pltpu.VMEM((rows, 256), BF)],
        compiler_params=params(),
        name="attention",
    )(cross, projected, projected, projected, head_lanes)


def out_proj_rows(rows, scaled, weight, vec_ref, tokens_ref, branch_ref, middle_ref, feed_ref):
    branch = dot_nn(scaled, weight) + vec_ref[2:3]
    normed, _ = row_norm(branch)
    middle = tokens_ref[rows].astype(F32) + (normed * vec_ref[5:6] + vec_ref[6:7])
    again, _ = row_norm(middle)
    branch_ref[rows] = branch
    middle_ref[rows] = middle
    feed_ref[rows] = (again * vec_ref[7:8] + vec_ref[8:9]).astype(BF)


def out_proj_kernel(scaled_ref, weight_ref, vec_ref, tokens_ref, branch_ref, middle_ref, feed_ref):
    rows = pl.ds(0, TILE)
    out_proj_rows(
        rows, scaled_ref[...], weight_ref[...], vec_ref, tokens_ref, branch_ref, middle_ref, feed_ref
    )


def out_proj(scaled, weights, vectors, tokens):
    rows, width = tokens.shape
    by_row = pl.BlockSpec((TILE, width), lambda i: (i, 0))
    return pl.pallas_call(
        out_proj_kernel,
        grid=(rows // TILE,),
        in_specs=[
            by_row,
            pl.BlockSpec((width, width), lambda i: (0, 3), pipeline_mode=pl.Buffered(1)),
            whole(vectors.shape),
            by_row,
        ],
        out_specs=[by_row, by_row, by_row],
        out_shape=[
            jax.ShapeDtypeStruct((rows, width), F32),
            jax.ShapeDtypeStruct((rows, width), F32),
            jax.ShapeDtypeStruct((rows, width), BF),
        ],
        compiler_params=params(),
        name="out_proj",
    )(scaled, weights, vectors, tokens)


def phi_and_slope(value):
    bell = jnp.exp2(value * value * (-0.5 * LOG2E))
    t = 1.0 / (1.0 + (0.3275911 * ROOT_HALF) * jnp.abs(value))
    series = t * (
        0.5 * 0.254829592
        + t
        * (
            0.5 * -0.284496736
            + t * (0.5 * 1.421413741 + t * (0.5 * -1.453152027 + t * (0.5 * 1.061405429)))
        )
    )
    tail = series * bell
    area = jnp.where(value < 0.0, tail, 1.0 - tail)
    return value * area, area + value * bell * INV_ROOT_TAU


def up_kernel(units, feed_ref, up_ref, vec_ref, act_ref, slope_ref, mean_ref, inv_ref, sums_ref):
    step = pl.program_id(0)
    rows_all = feed_ref.shape[0]

    @pl.when(step == 0)
    def _():
        sums_ref[...] = jnp.zeros_like(sums_ref)

    bias = vec_ref[0, 0:1].astype(F32)
    for start in range(0, rows_all, TILE):
        rows = pl.ds(start, TILE)
        pre = dot_nn(feed_ref[rows], up_ref[0]) + bias
        act, slope = phi_and_slope(pre)
        act_ref[0, rows] = act.astype(BF)
        slope_ref[0, rows] = slope.astype(BF)
        sums_ref[0, rows] += lane_fold(act)
        sums_ref[1, rows] += lane_fold(act * act)

    @pl.when(step == pl.num_programs(0) - 1)
    def _():
        for start in range(0, rows_all, TILE):
            rows = pl.ds(start, TILE)
            mean = jnp.sum(sums_ref[0, rows], axis=1, keepdims=True) / units
            square = jnp.sum(sums_ref[1, rows], axis=1, keepdims=True) / units
            inv = lax.rsqrt(square - mean * mean + EPS)
            mean_ref[rows] = jnp.broadcast_to(mean, (TILE, 128))
            inv_ref[rows] = jnp.broadcast_to(inv, (TILE, 128))


def up_pass(feed, up, vec):
    rows, width = feed.shape
    steps = up.shape[0]
    block = pl.BlockSpec((1, rows, UNITS), lambda j: (j, 0, 0))
    return pl.pallas_call(
        functools.partial(up_kernel, steps * UNITS),
        grid=(steps,),
        in_specs=[
            whole((rows, width)),
            pl.BlockSpec((1, width, UNITS), lambda j: (j, 0, 0)),
            pl.BlockSpec((1, vec.shape[1], UNITS), lambda j: (j, 0, 0)),
        ],
        out_specs=[block, block, whole((rows, 128)), whole((rows, 128))],
        out_shape=[
            jax.ShapeDtypeStruct((steps, rows, UNITS), BF),
            jax.ShapeDtypeStruct((steps, rows, UNITS), BF),
            jax.ShapeDtypeStruct((rows, 128), F32),
            jax.ShapeDtypeStruct((rows, 128), F32),
        ],
        scratch_shapes=[pltpu.VMEM((2, rows, 128), F32)],
        compiler_params=params(),
        name="up_pass",
    )(feed, up, vec)


def down_kernel(
    units,
    act_ref,
    mean_ref,
    inv_ref,
    vec_ref,
    down_ref,
    cot_ref,
    middle_ref,
    shift_ref,
    mixed_ref,
    down_grad_ref,
    e_ref,
    first_ref,
    cross_ref,
    vec_grad_ref,
    total_ref,
    sums_ref,
    low_ref,
):
    step = pl.program_id(0)
    last = pl.num_programs(0) - 1
    rows_all = cot_ref.shape[0]

    @pl.when(step == 0)
    def _():
        total_ref[...] = jnp.zeros_like(total_ref)
        sums_ref[...] = jnp.zeros_like(sums_ref)

    gain = vec_ref[0, 1:2].astype(F32)
    shift = vec_ref[0, 2:3].astype(F32)
    gain_grad = jnp.zeros((1, UNITS), F32)
    bias_grad = jnp.zeros((1, UNITS), F32)
    for start in range(0, rows_all, TILE):
        rows = pl.ds(start, TILE)
        normed = (act_ref[0, rows].astype(F32) - mean_ref[rows, 0:1]) * inv_ref[rows, 0:1]
        low = (normed * gain + shift).astype(BF)
        low_ref[rows] = low
        total_ref[rows] += dot_nn(low, down_ref[0])
        grad = dot_nt(cot_ref[rows], down_ref[0])
        gain_grad = gain_grad + column_sum(grad * normed)
        bias_grad = bias_grad + column_sum(grad)
        e = grad * gain
        e_ref[0, rows] = e.astype(BF)
        sums_ref[0, rows] += lane_fold(e)
        sums_ref[1, rows] += lane_fold(e * normed)
    vec_grad_ref[0, 0:1] = gain_grad
    vec_grad_ref[0, 1:2] = bias_grad
    down_grad_ref[0] = dot_tn(low_ref[...], cot_ref[...]).astype(BF)

    @pl.when(step == last)
    def _():
        cot_sum = jnp.zeros((1, cot_ref.shape[1]), F32)
        for start in range(0, rows_all, TILE):
            rows = pl.ds(start, TILE)
            mixed_ref[rows] = (middle_ref[rows] + total_ref[rows] + shift_ref[...]).astype(BF)
            first = jnp.sum(sums_ref[0, rows], axis=1, keepdims=True) / units
            cross = jnp.sum(sums_ref[1, rows], axis=1, keepdims=True) / units
            first_ref[rows] = jnp.broadcast_to(first, (TILE, 128))
            cross_ref[rows] = jnp.broadcast_to(cross, (TILE, 128))


def down_pass(act, mean, inv, vec, down, cotangent, middle, shift):
    rows, width = cotangent.shape
    steps = act.shape[0]
    block = pl.BlockSpec((1, rows, UNITS), lambda j: (j, 0, 0))
    return pl.pallas_call(
        functools.partial(down_kernel, steps * UNITS),
        grid=(steps,),
        in_specs=[
            block,
            whole((rows, 128)),
            whole((rows, 128)),
            pl.BlockSpec((1, vec.shape[1], UNITS), lambda j: (j, 0, 0)),
            pl.BlockSpec((1, UNITS, width), lambda j: (j, 0, 0)),
            whole((rows, width)),
            whole((rows, width)),
            whole((1, width)),
        ],
        out_specs=[
            whole((rows, width)),
            pl.BlockSpec((1, UNITS, width), lambda j: (j, 0, 0)),
            block,
            whole((rows, 128)),
            whole((rows, 128)),
            pl.BlockSpec((1, 8, UNITS), lambda j: (j, 0, 0)),
        ],
        out_shape=[
            jax.ShapeDtypeStruct((rows, width), BF),
            jax.ShapeDtypeStruct((steps, UNITS, width), BF),
            jax.ShapeDtypeStruct((steps, rows, UNITS), BF),
            jax.ShapeDtypeStruct((rows, 128), F32),
            jax.ShapeDtypeStruct((rows, 128), F32),
            jax.ShapeDtypeStruct((steps, 8, UNITS), F32),
        ],
        scratch_shapes=[
            pltpu.VMEM((rows, width), F32),
            pltpu.VMEM((2, rows, 128), F32),
            pltpu.VMEM((rows, UNITS), BF),
        ],
        compiler_params=params(),
        name="down_pass",
    )(act, mean, inv, vec, down, cotangent, middle, shift)


def up_back_kernel(
    act_ref,
    slope_ref,
    e_ref,
    mean_ref,
    inv_ref,
    first_ref,
    cross_ref,
    up_ref,
    feed_ref,
    up_grad_ref,
    bias_grad_ref,
    total_ref,
    turned_ref,
    low_ref,
):
    step = pl.program_id(0)
    rows_all = feed_ref.shape[0]

    @pl.when(step == 0)
    def _():
        total_ref[...] = jnp.zeros_like(total_ref)
        turned_ref[...] = feed_ref[...].T

    bias_grad = jnp.zeros((1, UNITS), F32)
    for start in range(0, rows_all, TILE):
        rows = pl.ds(start, TILE)
        inv = inv_ref[rows, 0:1]
        normed = (act_ref[0, rows].astype(F32) - mean_ref[rows, 0:1]) * inv
        grad_act = inv * (
            e_ref[0, rows].astype(F32) - first_ref[rows, 0:1] - normed * cross_ref[rows, 0:1]
        )
        low = (grad_act * slope_ref[0, rows].astype(F32)).astype(BF)
        bias_grad = bias_grad + column_sum(low.astype(F32))
        low_ref[rows] = low
        total_ref[rows] += dot_nt(low, up_ref[0])
    bias_grad_ref[0, 0:1] = bias_grad
    up_grad_ref[0] = dot_nn(turned_ref[...], low_ref[...]).astype(BF)


def up_back(act, slope, e, mean, inv, first, cross, up, feed):
    rows, width = feed.shape
    steps = act.shape[0]
    block = pl.BlockSpec((1, rows, UNITS), lambda j: (j, 0, 0))
    narrow = whole((rows, 128))
    return pl.pallas_call(
        up_back_kernel,
        grid=(steps,),
        in_specs=[
            block,
            block,
            block,
            narrow,
            narrow,
            narrow,
            narrow,
            pl.BlockSpec((1, width, UNITS), lambda j: (j, 0, 0)),
            whole((rows, width)),
        ],
        out_specs=[
            pl.BlockSpec((1, width, UNITS), lambda j: (j, 0, 0)),
            pl.BlockSpec((1, 8, UNITS), lambda j: (j, 0, 0)),
            whole((rows, width)),
        ],
        out_shape=[
            jax.ShapeDtypeStruct((steps, width, UNITS), BF),
            jax.ShapeDtypeStruct((steps, 8, UNITS), F32),
            jax.ShapeDtypeStruct((rows, width), F32),
        ],
        scratch_shapes=[pltpu.VMEM((width, rows), BF), pltpu.VMEM((rows, UNITS), BF)],
        compiler_params=params(),
        name="up_back",
    )(act, slope, e, mean, inv, first, cross, up, feed)


def out_back_kernel(
    grad_feed_ref,
    cot_ref,
    middle_ref,
    branch_ref,
    scaled_ref,
    attended_ref,
    weight_ref,
    vec_ref,
    hs_ref,
    heads_ref,
    grad_middle_ref,
    ga_ref,
    out_grad_ref,
    delta_ref,
    sums_ref,
    total_ref,
):
    step = pl.program_id(0)

    @pl.when(step == 0)
    def _():
        total_ref[...] = jnp.zeros_like(total_ref)
        sums_ref[...] = jnp.zeros_like(sums_ref)

    grad_feed = grad_feed_ref[...]
    normed, inv = row_norm(middle_ref[...])
    cot = cot_ref[...].astype(F32)
    grad_middle = cot + norm_back(grad_feed, vec_ref[7:8], normed, inv)
    grad_middle_ref[...] = grad_middle
    sums_ref[7:8] += column_sum(grad_feed * normed)
    sums_ref[8:9] += column_sum(grad_feed)
    sums_ref[9:10] += column_sum(cot)
    normed, inv = row_norm(branch_ref[...])
    low = norm_back(grad_middle, vec_ref[5:6], normed, inv).astype(BF)
    sums_ref[5:6] += column_sum(grad_middle * normed)
    sums_ref[6:7] += column_sum(grad_middle)
    sums_ref[2:3] += column_sum(low.astype(F32))
    scaled = scaled_ref[...]
    total_ref[...] += dot_tn(scaled, low)
    grad_scaled = dot_nt(low, weight_ref[...])
    grad_out = (grad_scaled * hs_ref[...]).astype(BF)
    ga_ref[...] = grad_out
    product = grad_out.astype(F32) * attended_ref[...]
    high = product.astype(BF)
    rest = (product - high.astype(F32)).astype(BF)
    delta = dot_nn(high, heads_ref[...]) + dot_nn(rest, heads_ref[...])
    delta_ref[...] = delta.T[: delta_ref.shape[0]]

    @pl.when(step == pl.num_programs(0) - 1)
    def _():
        out_grad_ref[...] = total_ref[...].astype(BF)


def out_back(
    grad_feed, cotangent, middle, branch, scaled, attended, weights, vectors, head_lanes, heads_map
):
    rows, width = cotangent.shape
    heads = 2 * width // 128
    by_row = pl.BlockSpec((TILE, width), lambda i: (i, 0))
    return pl.pallas_call(
        out_back_kernel,
        grid=(rows // TILE,),
        in_specs=[
            by_row,
            by_row,
            by_row,
            by_row,
            by_row,
            by_row,
            pl.BlockSpec((width, width), lambda i: (0, 3), pipeline_mode=pl.Buffered(1)),
            whole(vectors.shape),
            whole((1, width)),
            whole(heads_map.shape),
        ],
        out_specs=[
            by_row,
            by_row,
            whole((width, width)),
            pl.BlockSpec((heads, TILE), lambda i: (0, i)),
            whole((16, width)),
        ],
        out_shape=[
            jax.ShapeDtypeStruct((rows, width), F32),
            jax.ShapeDtypeStruct((rows, width), BF),
            jax.ShapeDtypeStruct((width, width), BF),
            jax.ShapeDtypeStruct((heads, rows), F32),
            jax.ShapeDtypeStruct((16, width), F32),
        ],
        scratch_shapes=[pltpu.VMEM((width, width), F32)],
        compiler_params=params(),
        name="out_back",
    )(
        grad_feed,
        cotangent,
        middle,
        branch,
        scaled,
        attended,
        weights,
        vectors,
        head_lanes,
        heads_map,
    )


def attention_back_head(
    head, cross, q_ref, k_ref, v_ref, ga_ref, lse_ref, delta_ref, dq_ref, dk_ref, dv_ref
):
    rows = q_ref.shape[0]
    half = rows // 2
    factor = LOG2E * (q_ref.shape[1] // 2) ** (-0.5)
    low_lanes = lax.broadcasted_iota(jnp.int32, (1, 128), 1) < 64
    mine = low_lanes if head == 0 else ~low_lanes
    above = lax.broadcasted_iota(jnp.int32, (TILE, TILE), 0) <= lax.broadcasted_iota(
        jnp.int32, (TILE, TILE), 1
    )
    zero = jnp.zeros((rows, 128), BF)
    query = jnp.where(mine, q_ref[...], zero)
    grad = jnp.where(mine, ga_ref[...], zero)
    key_own = jnp.where(mine, k_ref[...], zero)
    for start in range(0, rows, TILE):
        stop = start + TILE
        raw = dot_nt(k_ref[start:stop], query[start:])
        level = lse_ref[0, head : head + 1, start:]
        parts = [jnp.where(above, raw[:, :TILE] * factor - level[:, :TILE], MASKED)]
        if start < half:
            if stop < half:
                parts.append(raw[:, TILE : half - start] * factor - level[:, TILE : half - start])
            parts.append(raw[:, half - start :] * factor - (level[:, half - start :] - cross))
        elif stop < rows:
            parts.append(raw[:, TILE:] * factor - level[:, TILE:])
        exponent = parts[0] if len(parts) == 1 else jnp.concatenate(parts, axis=1)
        weights = jnp.exp2(exponent)
        grad_weights = dot_nt(v_ref[start:stop], grad[start:])
        grad_scores = (weights * (grad_weights - delta_ref[head : head + 1, start:])).astype(BF)
        dv = dot_nn(weights.astype(BF), grad[start:])
        dk = dot_nn(grad_scores, query[start:])
        dq = dot_tn(grad_scores, key_own[start:stop])
        if head == 0:
            dv_ref[start:stop] = dv
            dk_ref[start:stop] = dk
        else:
            dv_ref[start:stop] += dv
            dk_ref[start:stop] += dk
        if head == 0 and start == 0:
            dq_ref[...] = dq
        else:
            dq_ref[start:] += dq


def in_back_kernel(
    cross_ref,
    q_ref,
    k_ref,
    v_ref,
    ga_ref,
    lse_ref,
    delta_ref,
    wq_ref,
    wk_ref,
    wv_ref,
    first_ref,
    out_grad_ref,
    tokens_ref,
    gain_ref,
    grad_middle_ref,
    chunk_ref,
    bias_ref,
    tokens_grad_ref,
    sums_ref,
    dq_ref,
    dk_ref,
    dv_ref,
    turned_ref,
    total_ref,
):
    step = pl.program_id(0)
    rows_all = q_ref.shape[0]

    @pl.when(step == 0)
    def _():
        turned_ref[...] = first_ref[...].T
        total_ref[...] = jnp.zeros_like(total_ref)

    delta = delta_ref.at[0]
    for head in range(2):
        attention_back_head(
            head,
            cross_ref[0, 0],
            q_ref,
            k_ref,
            v_ref,
            ga_ref,
            lse_ref,
            delta,
            dq_ref,
            dk_ref,
            dv_ref,
        )
    factor = (q_ref.shape[1] // 2) ** (-0.5)
    dq = (dq_ref[...] * factor).astype(BF)
    dk = (dk_ref[...] * factor).astype(BF)
    dv = dv_ref[...].astype(BF)
    bias_ref[0, 0:1] = column_sum(dq.astype(F32))
    bias_ref[0, 1:2] = column_sum(dv.astype(F32))
    grads = jnp.concatenate([dq, dk, dv], axis=1)
    weights = jnp.concatenate([wq_ref[...], wk_ref[...], wv_ref[...]], axis=1)
    for start in range(0, rows_all, TILE):
        rows = pl.ds(start, TILE)
        total_ref[rows] += dot_nt(grads[start : start + TILE], weights)
        part = jnp.concatenate([dot_nn(turned_ref[rows], grads).astype(BF), out_grad_ref[rows]], axis=1)
        chunk_ref[0, :, start // TILE] = part.reshape(8, 32, 512)

    @pl.when(step == pl.num_programs(0) - 1)
    def _():
        gain_grad = jnp.zeros((1, total_ref.shape[1]), F32)
        shift_grad = jnp.zeros((1, total_ref.shape[1]), F32)
        for start in range(0, rows_all, TILE):
            rows = pl.ds(start, TILE)
            normed, inv = row_norm(tokens_ref[rows].astype(F32))
            grad = total_ref[rows]
            gain_grad = gain_grad + column_sum(grad * normed)
            shift_grad = shift_grad + column_sum(grad)
            back = norm_back(grad, gain_ref[...], normed, inv)
            tokens_grad_ref[rows] = (grad_middle_ref[rows] + back).astype(BF)
        sums_ref[0:1] = gain_grad
        sums_ref[1:2] = shift_grad


def in_back(cross, projected, ga, lse, delta, weights, first, out_grad, tokens, gain, grad_middle):
    rows, width = tokens.shape
    pairs = width // 128
    column = pl.BlockSpec((rows, 128), lambda p: (0, p))
    square = whole((rows, width))
    return pl.pallas_call(
        in_back_kernel,
        grid=(pairs,),
        in_specs=[
            pl.BlockSpec(memory_space=pltpu.SMEM),
            column,
            pl.BlockSpec((rows, 128), lambda p: (0, pairs + p)),
            pl.BlockSpec((rows, 128), lambda p: (0, 2 * pairs + p)),
            column,
            pl.BlockSpec((1, 8, rows), lambda p: (p, 0, 0)),
            pl.BlockSpec((1, 2, rows), lambda p: (p, 0, 0)),
            pl.BlockSpec((width, 128), lambda p: (0, p)),
            pl.BlockSpec((width, 128), lambda p: (0, pairs + p)),
            pl.BlockSpec((width, 128), lambda p: (0, 2 * pairs + p)),
            square,
            column,
            square,
            whole((1, width)),
            square,
        ],
        out_specs=[
            pl.BlockSpec((1, 8, width // TILE, 32, 512), lambda p: (p, 0, 0, 0, 0)),
            pl.BlockSpec((1, 8, 128), lambda p: (p, 0, 0)),
            square,
            whole((8, width)),
        ],
        out_shape=[
            jax.ShapeDtypeStruct((pairs, 8, width // TILE, 32, 512), BF),
            jax.ShapeDtypeStruct((pairs, 8, 128), F32),
            jax.ShapeDtypeStruct((rows, width), BF),
            jax.ShapeDtypeStruct((8, width), F32),
        ],
        scratch_shapes=[
            pltpu.VMEM((rows, 128), F32),
            pltpu.VMEM((rows, 128), F32),
            pltpu.VMEM((rows, 128), F32),
            pltpu.VMEM((width, rows), BF),
            pltpu.VMEM((rows, width), F32),
        ],
        compiler_params=params(),
        name="in_back",
    )(
        cross,
        projected,
        projected,
        projected,
        ga,
        lse,
        delta,
        weights,
        weights,
        weights,
        first,
        out_grad,
        tokens,
        gain,
        grad_middle,
    )


class Place:
    def __init__(self):
        self.z = lax.axis_index("dp")
        wide = lax.axis_index("wide")
        self.y = wide // 4
        self.x = (wide // 2) % 2
        self.c = wide % 2
        self.core = (self.z, wide + 1 - 2 * self.c)
        self.side = (self.z, wide + 2 - 4 * self.x)
        self.over = (self.z, wide + 4 - 8 * self.y)
        self.ranks = (self.z + 1 - 2 * (self.z % 2), (self.z + 2) % 4, 3 - self.z)
        self.planes = tuple((rank, wide) for rank in self.ranks)

    def greet(self, planes=True):
        barrier = pltpu.get_barrier_semaphore()
        peers = (self.core, self.side, self.over) + (self.planes if planes else ())
        for peer in peers:
            pl.semaphore_signal(barrier, inc=1, device_id=peer, device_id_type=MESH)
        pl.semaphore_wait(barrier, len(peers))


class WideGather:
    copies = 13

    def __init__(self, place, source, target, send, recv, first, last):
        rows = target.shape[-2]
        y, x, c = place.y, place.x, place.c
        here, side, over, far = (y, x, c), (y, 1 - x, c), (1 - y, x, c), (1 - y, 1 - x, c)
        upper, lower, both = pl.ds(0, rows // 2), pl.ds(rows // 2, rows // 2), pl.ds(0, rows)

        def copy(index, slot, part, peer):
            destination = target.at[(*slot, part)]
            return pltpu.make_async_remote_copy(
                src_ref=source.at[part] if source is not None and slot is here else destination,
                dst_ref=destination,
                send_sem=send.at[first + index],
                recv_sem=recv.at[first + index],
                device_id=peer,
                device_id_type=MESH,
            )

        self.all = (
            copy(0, here, upper, place.side),
            copy(1, here, lower, place.over),
            copy(2, here, upper, place.over),
            copy(3, here, lower, place.side),
            copy(4, here, both, place.core),
            copy(5, side, upper, place.over),
            copy(6, side, upper, place.core),
            copy(7, over, lower, place.side),
            copy(8, over, lower, place.core),
            copy(9, side, lower, place.core),
            copy(10, over, upper, place.core),
            copy(11, far, upper, place.core),
            copy(12, far, lower, place.core),
        )
        self.own = None
        if source is not None:
            self.own = pltpu.make_async_copy(source, target.at[here], last)

    def start(self):
        if self.own is not None:
            self.own.start()
        for index in range(5):
            self.all[index].start()

    def relay(self, stage):
        waits, starts = (((0, 1), (5, 7, 6, 8)), ((2, 3), (9, 10)), ((5, 7), (11, 12)))[stage]
        for index in waits:
            self.all[index].wait_recv()
        for index in starts:
            self.all[index].start()

    def finish(self):
        for index in (4, 6, 8, 9, 10, 11, 12):
            self.all[index].wait_recv()
        for copy in self.all:
            copy.wait_send()
        if self.own is not None:
            self.own.wait()


def gather_kernel(
    attn_ref, up_ref, vec_ref, down_ref, attn_out, up_out, vec_out, down_out, send, recv, local
):
    place = Place()
    place.greet()
    own = (place.y, place.x, place.c)
    across = []
    for index, peer in enumerate(place.planes):
        across.append(
            pltpu.make_async_remote_copy(
                src_ref=attn_ref,
                dst_ref=attn_out.at[(place.z, *own)],
                send_sem=send.at[index],
                recv_sem=recv.at[index],
                device_id=peer,
                device_id_type=MESH,
            )
        )
    count = WideGather.copies
    attn = [
        WideGather(place, attn_ref if index == 0 else None, attn_out.at[rank], send, recv, 3 + index * count, local.at[0])
        for index, rank in enumerate((place.z, *place.ranks))
    ]
    units = WideGather(place, vec_ref, vec_out, send, recv, 3 + 4 * count, local.at[1])
    up = WideGather(place, up_ref, up_out, send, recv, 3 + 5 * count, local.at[2])
    down = WideGather(place, down_ref, down_out, send, recv, 3 + 6 * count, local.at[3])
    for copy in across:
        copy.start()
    attn[0].start()
    units.start()
    for index in range(3):
        attn[index].relay(0)
        across[index].wait_recv()
        attn[index + 1].start()
        attn[index].relay(1)
        attn[index].relay(2)
    for stage in range(3):
        attn[3].relay(stage)
    up.start()
    down.start()
    for stage in range(3):
        units.relay(stage)
    for stage in range(3):
        up.relay(stage)
        down.relay(stage)
    for copy in across:
        copy.wait_send()
    for item in (*attn, units, up, down):
        item.finish()


def gather_all(attn, up, vec, down):
    shapes = [
        jax.ShapeDtypeStruct((4, 2, 2, 2, *attn.shape), BF),
        jax.ShapeDtypeStruct((2, 2, 2, *up.shape), BF),
        jax.ShapeDtypeStruct((2, 2, 2, *vec.shape), BF),
        jax.ShapeDtypeStruct((2, 2, 2, *down.shape), BF),
    ]
    copies = 3 + 7 * WideGather.copies
    return pl.pallas_call(
        gather_kernel,
        in_specs=[ANY] * 4,
        out_specs=[ANY] * 4,
        out_shape=shapes,
        scratch_shapes=[
            pltpu.SemaphoreType.DMA((copies,)),
            pltpu.SemaphoreType.DMA((copies,)),
            pltpu.SemaphoreType.DMA((4,)),
        ],
        compiler_params=pltpu.CompilerParams(collective_id=0, has_side_effects=True),
        name="gather_all",
    )(attn, up, vec, down)


class Reduction:
    stages = 6

    @staticmethod
    def scratch():
        return [
            pltpu.VMEM((2, 2, 2, 4, 32, 512), BF),
            pltpu.VMEM((2, 2, 2, 4, 32, 512), BF),
            pltpu.VMEM((3, 2, 2, 4, 32, 512), BF),
            pltpu.VMEM((2, 2, 4, 16, 512), BF),
            pltpu.VMEM((2, 2, 4, 16, 512), BF),
            pltpu.VMEM((2, 4, 16, 512), BF),
            pltpu.VMEM((2, 4, 16, 512), BF),
            pltpu.VMEM((2, 4, 32, 512), BF),
            pltpu.VMEM((2, 3, 32, 512), BF),
            pltpu.VMEM((2, 32, 512), BF),
            pltpu.VMEM((4, 3, 32, 512), BF),
            pltpu.SemaphoreType.DMA((11, 4)),
            pltpu.SemaphoreType.DMA((11, 4)),
            pltpu.SemaphoreType.DMA((2,)),
        ]

    def __init__(self, place, refs):
        self.place = place
        (
            self.mine,
            self.partner,
            self.chip,
            self.from_x,
            self.from_y,
            self.then_y,
            self.then_x,
            self.plane,
            self.from_z,
            self.sums,
            self.shared,
            self.send,
            self.recv,
            self.local,
        ) = refs

    def copy(self, index, slot, source, target, peer):
        return pltpu.make_async_remote_copy(
            src_ref=source,
            dst_ref=target,
            send_sem=self.send.at[index, slot],
            recv_sem=self.recv.at[index, slot],
            device_id=peer,
            device_id_type=MESH,
        )

    def to_core(self, chunk, source):
        slot = chunk % 2
        return self.copy(0, slot, source, self.partner.at[slot], self.place.core)

    def load(self, chunk, source):
        slot = chunk % 2
        return pltpu.make_async_copy(source, self.mine.at[slot], self.local.at[slot])

    def first_hop(self, chunk):
        p, slot, chip = self.place, chunk % 2, self.chip.at[chunk % 3]
        return (
            self.copy(1, slot, chip.at[:, 1 - p.x, :, pl.ds(0, 16)], self.from_x.at[slot], p.side),
            self.copy(2, slot, chip.at[1 - p.y, :, :, pl.ds(16, 16)], self.from_y.at[slot], p.over),
        )

    def second_hop(self, chunk):
        p, slot, chip = self.place, chunk % 2, self.chip.at[chunk % 3]
        return (
            self.copy(3, slot, chip.at[1 - p.y, p.x, :, pl.ds(0, 16)], self.then_y.at[slot], p.over),
            self.copy(4, slot, chip.at[p.y, 1 - p.x, :, pl.ds(16, 16)], self.then_x.at[slot], p.side),
        )

    def to_planes(self, chunk):
        p, slot = self.place, chunk % 2
        return [
            self.copy(5 + k, slot, self.plane.at[slot, p.ranks[k]], self.from_z.at[slot, k], p.planes[k])
            for k in range(3)
        ]

    def share(self, chunk):
        p = self.place
        return [
            self.copy(8 + k, chunk % 4, self.sums.at[chunk % 2], self.shared.at[chunk % 4, k], p.planes[k])
            for k in range(3)
        ]

    def stage0(self, chunk, away, home):
        self.to_core(chunk, away).start()
        self.load(chunk, home).start()

    def stage1(self, chunk, away, home):
        slot = chunk % 2
        self.load(chunk, home).wait()
        self.to_core(chunk, away).wait()
        self.chip[chunk % 3] = self.mine[slot] + self.partner[slot]
        for copy in self.first_hop(chunk):
            copy.start()

    def stage2(self, chunk):
        p, slot, index = self.place, chunk % 2, chunk % 3
        for copy in self.first_hop(chunk):
            copy.wait()
        for k in range(2):
            self.chip[index, k, p.x, :, 0:16] += self.from_x[slot, k]
            self.chip[index, p.y, k, :, 16:32] += self.from_y[slot, k]
        for copy in self.second_hop(chunk):
            copy.start()

    def stage3(self, chunk):
        p, slot, index = self.place, chunk % 2, chunk % 3
        for copy in self.second_hop(chunk):
            copy.wait()
        self.plane[slot, :, 0:16] = self.chip[index, p.y, p.x, :, 0:16] + self.then_y[slot]
        self.plane[slot, :, 16:32] = self.chip[index, p.y, p.x, :, 16:32] + self.then_x[slot]
        for copy in self.to_planes(chunk):
            copy.start()

    def stage4(self, chunk):
        slot = chunk % 2
        for copy in self.to_planes(chunk):
            copy.wait()
        total = self.plane[slot, self.place.z].astype(F32)
        for k in range(3):
            total = total + self.from_z[slot, k].astype(F32)
        return total


def reduce_kernel(down_ref, up_ref, attn_ref, vec_ref, down_out, up_out, attn_out, *scratch):
    place = Place()
    step = pl.program_id(0)
    engine = Reduction(place, scratch)

    @pl.when(step == 0)
    def _():
        place.greet()

    c = place.c
    ends = (8, 16, 24, 25)

    def sources(chunk):
        down = down_ref.at[:, :, :, chunk % 8 // 2, :, :, pl.ds(pl.multiple_of(chunk % 2 * 512, 512), 512)]
        up = up_ref.at[:, :, :, chunk % 8]
        attn = attn_ref.at[chunk % 8]
        return [(view.at[:, :, 1 - c], view.at[:, :, c]) for view in (down, up, attn, vec_ref)]

    def guarded(stage, low, high, action):
        chunk = step - stage

        @pl.when((chunk >= low) & (chunk < high))
        def _():
            action(chunk)

    def publish(chunk, shape_out):
        for copy in engine.share(chunk):
            copy.wait()

        def store(rank, value):
            shape_out(chunk, rank, value)

        store(place.z, engine.sums[chunk % 2])
        for k in range(3):
            store(place.ranks[k], engine.shared[chunk % 4, k])

    def put_down(chunk, rank, value):
        for half in range(2):

            @pl.when(chunk % 2 == half)
            def _():
                down_out[chunk // 2, rank, :, half * 512 : half * 512 + 512] = value

    def put_up(chunk, rank, value):
        up_out[chunk - 8, rank] = value

    def finish_shared(chunk):
        total = engine.stage4(chunk)
        engine.sums[chunk % 2] = total.astype(BF)
        for copy in engine.share(chunk):
            copy.start()

    def finish_own(chunk):
        attn_out[chunk - 16] = engine.stage4(chunk)

    guarded(5, 0, 8, lambda chunk: publish(chunk, put_down))
    guarded(5, 8, 16, lambda chunk: publish(chunk, put_up))
    guarded(4, 0, 16, finish_shared)
    guarded(4, 16, 25, finish_own)
    guarded(3, 0, 25, engine.stage3)
    guarded(2, 0, 25, engine.stage2)
    guarded(1, 0, 25, lambda chunk: engine.stage1(chunk, *sources(chunk)[2]))
    for index in range(4):
        low = 0 if index == 0 else ends[index - 1]
        guarded(0, low, ends[index], lambda chunk: engine.stage0(chunk, *sources(chunk)[index]))


def reduce_all(down, up, attn, vec):
    return pl.pallas_call(
        reduce_kernel,
        grid=(25 + 5,),
        in_specs=[ANY] * 4,
        out_specs=[
            whole((4, 4, 32, 1024)),
            whole((8, 4, 32, 512)),
            whole((9, 32, 512)),
        ],
        out_shape=[
            jax.ShapeDtypeStruct((4, 4, 32, 1024), BF),
            jax.ShapeDtypeStruct((8, 4, 32, 512), BF),
            jax.ShapeDtypeStruct((9, 32, 512), F32),
        ],
        scratch_shapes=Reduction.scratch(),
        compiler_params=params(collective_id=1, has_side_effects=True),
        name="reduce_all",
    )(down, up, attn, vec)


def layer(tokens, cotangent, lengths, weights, vectors, up, down, unit_vec, head_scale, down_bias):
    rows, width = tokens.shape
    heads = head_scale.shape[0]
    cross = jnp.where(lengths[0:1, 0:1] == rows, 0.0, MASKED).astype(F32)
    scale = head_scale.astype(F32)
    head_lanes = jnp.repeat(scale, width // heads)[None, :]
    heads_map = (
        lax.broadcasted_iota(jnp.int32, (width, 128), 0) // (width // heads)
        == lax.broadcasted_iota(jnp.int32, (width, 128), 1)
    ).astype(BF)
    bias = jnp.concatenate([vectors[0:1], jnp.zeros((1, width), F32), vectors[1:2]], axis=1)
    first, projected = in_proj(tokens, weights, vectors[3:4], vectors[4:5], bias)
    scaled, attended, lse = attention(cross, projected, head_lanes)
    branch, middle, feed = out_proj(scaled, weights, vectors, tokens)
    act, slope, mean, inv = up_pass(feed, up, unit_vec)
    mixed, down_grad, e, e_mean, e_cross, unit_grad = down_pass(
        act, mean, inv, unit_vec, down, cotangent, middle, down_bias.astype(F32)[None]
    )
    up_grad, up_bias_grad, grad_feed = up_back(
        act, slope, e, mean, inv, e_mean, e_cross, up, feed
    )
    grad_middle, ga, out_grad, delta, sums = out_back(
        grad_feed,
        cotangent,
        middle,
        branch,
        scaled,
        attended,
        weights,
        vectors,
        head_lanes,
        heads_map,
    )
    chunks, proj_bias, tokens_grad, pre_sums = in_back(
        cross,
        projected,
        ga,
        lse,
        delta.reshape(heads // 2, 2, rows),
        weights,
        first,
        out_grad,
        tokens,
        vectors[3:4],
        grad_middle,
    )
    scale_grad = jnp.sum(delta, axis=1) / scale
    vec_grads = [
        proj_bias[:, 0].reshape(width),
        proj_bias[:, 1].reshape(width),
        sums[2],
        pre_sums[0],
        pre_sums[1],
        sums[5],
        sums[6],
        sums[7],
        sums[8],
    ]
    unit_grads = [up_bias_grad[:, 0], unit_grad[:, 0], unit_grad[:, 1]]
    return mixed, tokens_grad, chunks, up_grad, down_grad, vec_grads, unit_grads, sums[9], scale_grad


def body(
    axes,
    tokens,
    cotangent,
    lengths,
    in_weight,
    query_bias,
    value_bias,
    out_weight,
    out_bias,
    head_scale,
    pre_gain,
    pre_bias,
    post_gain,
    post_bias,
    feed_gain,
    feed_bias,
    up_weight,
    up_bias,
    mid_gain,
    mid_bias,
    down_weight,
    down_bias,
):
    planes, wide = axes
    every = ("dp", "wide")
    staged = (planes, wide) == (4, 8)
    rows, width = tokens.shape
    units = down_weight.shape[0] * wide
    steps = units // UNITS
    share = in_weight.shape[0]
    columns = [
        query_bias,
        value_bias,
        out_bias,
        pre_gain,
        pre_bias,
        post_gain,
        post_bias,
        feed_gain,
        feed_bias,
    ]
    packed = jnp.stack(columns, axis=1)
    packed = jnp.pad(packed, ((0, 0), (0, 128 - len(columns))))
    packed = jnp.concatenate([in_weight, out_weight, packed], axis=1)
    unit_rows = jnp.pad(jnp.stack([up_bias, mid_gain, mid_bias]), ((0, 29), (0, 0)))
    if staged:
        weights, up, unit_vec, down = gather_all(packed, up_weight, unit_rows, down_weight)
        weights = weights.reshape(width, packed.shape[1])
        up = up.reshape(steps, width, UNITS)
        unit_vec = unit_vec.reshape(steps, 32, UNITS)
        down = down.reshape(steps, UNITS, width)
    else:
        weights = lax.all_gather(packed, every, axis=0, tiled=True)
        up = lax.all_gather(up_weight, "wide", axis=1, tiled=True)
        up = up.reshape(width, steps, UNITS).transpose(1, 0, 2)
        unit_vec = lax.all_gather(unit_rows, "wide", axis=1, tiled=True)
        unit_vec = unit_vec.reshape(32, steps, UNITS).transpose(1, 0, 2)
        down = lax.all_gather(down_weight, "wide", axis=0, tiled=True)
        down = down.reshape(steps, UNITS, width)
    vectors = weights[:, 4 * width : 4 * width + 16].astype(F32).T
    (mixed, tokens_grad, chunks, up_grad, down_grad, vec_grads, unit_grads, down_sum, scale_sum) = (
        layer(
            tokens,
            cotangent,
            lengths,
            weights,
            vectors,
            up,
            down,
            unit_vec,
            head_scale,
            down_bias,
        )
    )
    heads = head_scale.shape[0]
    pairs = width // 128
    if staged:
        own = jnp.stack([item.astype(BF) for item in unit_grads], axis=1)
        both = jnp.stack(
            [
                down_sum[:UNITS],
                down_sum[UNITS:],
                jnp.pad(scale_sum, (0, UNITS - heads)),
                jnp.zeros((UNITS,), F32),
                jnp.zeros((UNITS,), F32),
            ]
        ).astype(BF)
        split = jnp.stack(vec_grads).astype(BF).reshape(len(columns), planes, wide, share)
        split = jnp.pad(split.transpose(2, 1, 0, 3), ((0, 0), (0, 0), (0, 15), (0, UNITS - share)))
        vec_chunk = jnp.concatenate(
            [
                jnp.broadcast_to(own[:, None], (wide, planes, 3, UNITS)),
                jnp.broadcast_to(both, (wide, planes, 5, UNITS)),
                split,
            ],
            axis=2,
        )
        down_total, up_total, shares = reduce_all(
            down_grad.reshape(2, 2, 2, 4, 4, 32, width),
            up_grad.reshape(2, 2, 2, 8, 4, 32, UNITS),
            chunks.reshape(pairs, 2, 2, 2, 4, 32, 512),
            vec_chunk.reshape(2, 2, 2, 4, 32, UNITS),
        )
        up_total = up_total.astype(F32).reshape(width, UNITS)
        down_total = down_total.astype(F32).reshape(UNITS, width)
        unit_totals = [shares[8, index] for index in range(3)]
        down_sum = jnp.concatenate([shares[8, 3], shares[8, 4]])
        scale_sum = shares[8, 5, :heads]
        vec_totals = [shares[8, 8 + index, :share] for index in range(len(columns))]
        in_total = shares[:pairs, :, :384].reshape(pairs, share, 3, 128)
        in_total = in_total.transpose(1, 2, 0, 3).reshape(share, 3 * width)
        out_total = shares[:pairs, :, 384:].transpose(1, 0, 2).reshape(share, width)
    else:

        def scatter(value, axis=0, over=every):
            return lax.psum_scatter(value, over, scatter_dimension=axis, tiled=True)

        def both_ways(value, axis):
            part = scatter(value.astype(BF), axis, "wide")
            return lax.psum(part, "dp").astype(F32)

        up_total = both_ways(up_grad.transpose(1, 0, 2).reshape(width, units), 1)
        down_total = both_ways(down_grad.reshape(units, width), 0)
        unit_totals = [
            lax.psum(scatter(item.reshape(units), 0, "wide"), "dp") for item in unit_grads
        ]
        down_sum, scale_sum = lax.psum((down_sum, scale_sum), every)
        vec_totals = [scatter(item) for item in vec_grads]
        natural = chunks.transpose(0, 2, 1, 3, 4).reshape(pairs, width, 512)
        in_total = natural[:, :, :384].reshape(pairs, width, 3, 128)
        in_total = scatter(in_total.transpose(1, 2, 0, 3).reshape(width, 3 * width).astype(F32))
        out_total = scatter(
            natural[:, :, 384:].transpose(1, 0, 2).reshape(width, width).astype(F32)
        )
    return (
        mixed,
        tokens_grad,
        in_total,
        vec_totals[0],
        vec_totals[1],
        out_total,
        vec_totals[2],
        scale_sum,
        vec_totals[3],
        vec_totals[4],
        vec_totals[5],
        vec_totals[6],
        vec_totals[7],
        vec_totals[8],
        up_total,
        unit_totals[0],
        unit_totals[1],
        unit_totals[2],
        down_total,
        down_sum,
    )


def solution(mesh):
    by_all = P(("dp", "wide"))
    rows_all = P(("dp", "wide"), None)
    axes = (mesh.shape["dp"], mesh.shape["wide"])
    return jax.shard_map(
        functools.partial(body, axes),
        mesh=mesh,
        in_specs=(
            rows_all,
            rows_all,
            rows_all,
            rows_all,
            by_all,
            by_all,
            rows_all,
            by_all,
            P(),
            by_all,
            by_all,
            by_all,
            by_all,
            by_all,
            by_all,
            P(None, "wide"),
            P("wide"),
            P("wide"),
            P("wide"),
            P("wide", None),
            P(),
        ),
        out_specs=(
            rows_all,
            rows_all,
            rows_all,
            by_all,
            by_all,
            rows_all,
            by_all,
            P(),
            by_all,
            by_all,
            by_all,
            by_all,
            by_all,
            by_all,
            P(None, "wide"),
            P("wide"),
            P("wide"),
            P("wide"),
            P("wide", None),
            P(),
        ),
        check_vma=False,
    )
```

```python
import functools

import jax
import jax.numpy as jnp
from jax import lax
from jax.experimental import pallas as pl
from jax.experimental.pallas import tpu as pltpu
from jax.sharding import PartitionSpec as P

EPS = 1e-05
ROOT_HALF = 0.7071067811865476
INV_ROOT_TAU = 0.3989422804014327
LOG2E = 1.4426950408889634
MASKED = -1e30
BF = jnp.bfloat16
F32 = jnp.float32
TILE = 256
UNITS = 512
MESH = pl.DeviceIdType.MESH
VMEM_LIMIT = 60 * 1024 * 1024
ANY = pl.BlockSpec(memory_space=pl.ANY)


def dot_nn(left, right):
    return lax.dot_general(left, right, (((1,), (0,)), ((), ())), preferred_element_type=F32)


def dot_nt(left, right):
    return lax.dot_general(left, right, (((1,), (1,)), ((), ())), preferred_element_type=F32)


def dot_tn(left, right):
    return lax.dot_general(left, right, (((0,), (0,)), ((), ())), preferred_element_type=F32)


def params(**more):
    return pltpu.CompilerParams(
        dimension_semantics=("arbitrary",), vmem_limit_bytes=VMEM_LIMIT, **more
    )


def whole(shape):
    zeros = (0,) * len(shape)
    return pl.BlockSpec(shape, lambda *_: zeros, pipeline_mode=pl.Buffered(1))


def row_norm(values):
    center = values - jnp.mean(values, axis=-1, keepdims=True)
    inv = lax.rsqrt(jnp.mean(center * center, axis=-1, keepdims=True) + EPS)
    return center * inv, inv


def norm_back(grad, gain, normed, inv):
    scaled = grad * gain
    first = jnp.mean(scaled, axis=-1, keepdims=True)
    cross = jnp.mean(scaled * normed, axis=-1, keepdims=True)
    return inv * (scaled - first - normed * cross)


def column_sum(values):
    return jnp.sum(values, axis=0, keepdims=True)


def lane_fold(values):
    total = values[:, :128]
    for start in range(128, values.shape[1], 128):
        total = total + values[:, start : start + 128]
    return total


def attention_pair(cross, q_ref, k_ref, v_ref, hs_ref, scaled_ref, out_ref, lse_ref, vext_ref):
    rows = q_ref.shape[0]
    half = rows // 2
    factor = LOG2E * (q_ref.shape[1] // 2) ** (-0.5)
    low_lanes = lax.broadcasted_iota(jnp.int32, (1, 128), 1) < 64
    below = lax.broadcasted_iota(jnp.int32, (TILE, TILE), 1) <= lax.broadcasted_iota(
        jnp.int32, (TILE, TILE), 0
    )
    vext_ref[:, :128] = v_ref[...]
    vext_ref[:, 128:] = jnp.ones((rows, 128), BF)
    for start in range(0, rows, TILE):
        stop = start + TILE
        query = q_ref[start:stop]
        results = []
        for head in range(2):
            mine = low_lanes if head == 0 else ~low_lanes
            own = jnp.where(mine, query, jnp.zeros_like(query))
            raw = dot_nt(own, k_ref[:stop])
            parts = []
            if start >= half:
                parts.append((raw[:, :half], cross))
                if start > half:
                    parts.append((raw[:, half:start], None))
            elif start > 0:
                parts.append((raw[:, :start], None))
            parts.append((jnp.where(below, raw[:, start:stop], MASKED), None))
            peak = None
            for piece, shift in parts:
                top = jnp.max(piece, axis=-1, keepdims=True)
                if shift is not None:
                    top = top + shift
                peak = top if peak is None else jnp.maximum(peak, top)
            weights = []
            for piece, shift in parts:
                level = peak if shift is None else peak - shift
                weights.append(jnp.exp2((piece - level) * factor).astype(BF))
            weights = weights[0] if len(weights) == 1 else jnp.concatenate(weights, axis=1)
            both = dot_nn(weights, vext_ref[:stop])
            total = both[:, 128:]
            results.append((both[:, :128] / total, peak * factor + jnp.log2(total)))
        mixed = jnp.where(low_lanes, results[0][0], results[1][0])
        out_ref[start:stop] = mixed
        scaled_ref[start:stop] = (mixed * hs_ref[...]).astype(BF)
        lse = jnp.where(low_lanes, results[0][1], results[1][1]).T
        lse_ref[0, 0:1, start:stop] = lse[0:1]
        lse_ref[0, 1:2, start:stop] = lse[64:65]


def project_pair(first_ref, weights, bias, proj_ref):
    for start in range(0, first_ref.shape[0], TILE):
        rows = pl.ds(start, TILE)
        proj_ref[0, rows] = (dot_nn(first_ref[rows], weights) + bias).astype(BF)


def three(proj_ref):
    return [proj_ref.at[0, :, pl.ds(part * 128, 128)] for part in range(3)]


def plain_first_kernel(
    cross_ref,
    tokens_ref,
    wq_ref,
    wk_ref,
    wv_ref,
    vectors_ref,
    bq_ref,
    bv_ref,
    hs_ref,
    first_ref,
    proj_ref,
    scaled_ref,
    attended_ref,
    lse_ref,
    vext_ref,
):
    @pl.when(pl.program_id(0) == 0)
    def _():
        for start in range(0, tokens_ref.shape[0], TILE):
            rows = pl.ds(start, TILE)
            normed, _ = row_norm(tokens_ref[rows].astype(F32))
            first_ref[rows] = (normed * vectors_ref[3:4] + vectors_ref[4:5]).astype(BF)

    weights = jnp.concatenate([wq_ref[...], wk_ref[...], wv_ref[...]], axis=1)
    bias = jnp.concatenate([bq_ref[0:1], jnp.zeros((1, 128), F32), bv_ref[1:2]], axis=1)
    project_pair(first_ref, weights, bias, proj_ref)
    attention_pair(
        cross_ref[0, 0], *three(proj_ref), hs_ref, scaled_ref, attended_ref, lse_ref, vext_ref
    )


def plain_first(cross, tokens, weights, vectors, head_lanes):
    rows, width = tokens.shape
    pairs = width // 128
    column = pl.BlockSpec((rows, 128), lambda p: (0, p))
    bias = pl.BlockSpec((16, 128), lambda p: (0, p))
    return pl.pallas_call(
        plain_first_kernel,
        grid=(pairs,),
        in_specs=[
            pl.BlockSpec(memory_space=pltpu.SMEM),
            whole((rows, width)),
            pl.BlockSpec((width, 128), lambda p: (0, p)),
            pl.BlockSpec((width, 128), lambda p: (0, pairs + p)),
            pl.BlockSpec((width, 128), lambda p: (0, 2 * pairs + p)),
            whole(vectors.shape),
            bias,
            bias,
            pl.BlockSpec((1, 128), lambda p: (0, p)),
        ],
        out_specs=[
            whole((rows, width)),
            pl.BlockSpec((1, rows, 384), lambda p: (p, 0, 0)),
            column,
            column,
            pl.BlockSpec((1, 8, rows), lambda p: (p, 0, 0)),
        ],
        out_shape=[
            jax.ShapeDtypeStruct((rows, width), BF),
            jax.ShapeDtypeStruct((pairs, rows, 384), BF),
            jax.ShapeDtypeStruct((rows, width), BF),
            jax.ShapeDtypeStruct((rows, width), F32),
            jax.ShapeDtypeStruct((pairs, 8, rows), F32),
        ],
        scratch_shapes=[pltpu.VMEM((rows, 256), BF)],
        compiler_params=params(),
        name="plain_first",
    )(cross, tokens, weights, weights, weights, vectors, vectors, vectors, head_lanes)


def out_proj_rows(scaled_ref, weight_ref, vec_ref, tokens_ref, branch_ref, middle_ref):
    branch = dot_nn(scaled_ref[...], weight_ref[...]) + vec_ref[2:3]
    normed, _ = row_norm(branch)
    middle = tokens_ref[...].astype(F32) + (normed * vec_ref[5:6] + vec_ref[6:7])
    again, _ = row_norm(middle)
    branch_ref[...] = branch
    middle_ref[...] = middle
    return (again * vec_ref[7:8] + vec_ref[8:9]).astype(BF)


def out_proj_kernel(scaled_ref, weight_ref, vec_ref, tokens_ref, branch_ref, middle_ref, feed_ref):
    feed_ref[...] = out_proj_rows(
        scaled_ref, weight_ref, vec_ref, tokens_ref, branch_ref, middle_ref
    )


def out_proj(scaled, weights, vectors, tokens):
    rows, width = tokens.shape
    by_row = pl.BlockSpec((TILE, width), lambda i: (i, 0))
    return pl.pallas_call(
        out_proj_kernel,
        grid=(rows // TILE,),
        in_specs=[
            by_row,
            whole((width, width)),
            whole(vectors.shape),
            by_row,
        ],
        out_specs=[by_row, by_row, by_row],
        out_shape=[
            jax.ShapeDtypeStruct((rows, width), F32),
            jax.ShapeDtypeStruct((rows, width), F32),
            jax.ShapeDtypeStruct((rows, width), BF),
        ],
        compiler_params=params(),
        name="out_proj",
    )(scaled, weights, vectors, tokens)


def phi_and_slope(value):
    bell = jnp.exp2(value * value * (-0.5 * LOG2E))
    t = 1.0 / (1.0 + (0.3275911 * ROOT_HALF) * jnp.abs(value))
    series = t * (
        0.5 * 0.254829592
        + t
        * (
            0.5 * -0.284496736
            + t * (0.5 * 1.421413741 + t * (0.5 * -1.453152027 + t * (0.5 * 1.061405429)))
        )
    )
    tail = series * bell
    area = jnp.where(value < 0.0, tail, 1.0 - tail)
    return value * area, area + value * bell * INV_ROOT_TAU


def up_step(feed_ref, up_ref, vec_ref, act_ref, slope_ref, sums_ref):
    bias = vec_ref[0, 0:1].astype(F32)
    for start in range(0, feed_ref.shape[0], TILE):
        rows = pl.ds(start, TILE)
        pre = dot_nn(feed_ref[rows], up_ref[0]) + bias
        act, slope = phi_and_slope(pre)
        act_ref[0, rows] = act.astype(BF)
        slope_ref[0, rows] = slope.astype(BF)
        sums_ref[0, rows] += lane_fold(act)
        sums_ref[1, rows] += lane_fold(act * act)


def up_stats(units, mean_ref, inv_ref, sums_ref):
    for start in range(0, mean_ref.shape[0], TILE):
        rows = pl.ds(start, TILE)
        mean = jnp.sum(sums_ref[0, rows], axis=1, keepdims=True) / units
        square = jnp.sum(sums_ref[1, rows], axis=1, keepdims=True) / units
        inv = lax.rsqrt(square - mean * mean + EPS)
        mean_ref[rows] = jnp.broadcast_to(mean, (TILE, 128))
        inv_ref[rows] = jnp.broadcast_to(inv, (TILE, 128))


def up_kernel(units, feed_ref, up_ref, vec_ref, act_ref, slope_ref, mean_ref, inv_ref, sums_ref):
    step = pl.program_id(0)

    @pl.when(step == 0)
    def _():
        sums_ref[...] = jnp.zeros_like(sums_ref)

    up_step(feed_ref, up_ref, vec_ref, act_ref, slope_ref, sums_ref)

    @pl.when(step == pl.num_programs(0) - 1)
    def _():
        up_stats(units, mean_ref, inv_ref, sums_ref)


def up_pass(feed, up, vec):
    rows, width = feed.shape
    steps = up.shape[0]
    block = pl.BlockSpec((1, rows, UNITS), lambda j: (j, 0, 0))
    return pl.pallas_call(
        functools.partial(up_kernel, steps * UNITS),
        grid=(steps,),
        in_specs=[
            whole((rows, width)),
            pl.BlockSpec((1, width, UNITS), lambda j: (j, 0, 0)),
            pl.BlockSpec((1, vec.shape[1], UNITS), lambda j: (j, 0, 0)),
        ],
        out_specs=[block, block, whole((rows, 128)), whole((rows, 128))],
        out_shape=[
            jax.ShapeDtypeStruct((steps, rows, UNITS), BF),
            jax.ShapeDtypeStruct((steps, rows, UNITS), BF),
            jax.ShapeDtypeStruct((rows, 128), F32),
            jax.ShapeDtypeStruct((rows, 128), F32),
        ],
        scratch_shapes=[pltpu.VMEM((2, rows, 128), F32)],
        compiler_params=params(),
        name="up_pass",
    )(feed, up, vec)


def down_kernel(
    units,
    act_ref,
    mean_ref,
    inv_ref,
    vec_ref,
    down_ref,
    cot_ref,
    middle_ref,
    shift_ref,
    mixed_ref,
    down_grad_ref,
    e_ref,
    first_ref,
    cross_ref,
    vec_grad_ref,
    total_ref,
    sums_ref,
    low_ref,
):
    step = pl.program_id(0)
    last = pl.num_programs(0) - 1
    rows_all = cot_ref.shape[0]

    @pl.when(step == 0)
    def _():
        total_ref[...] = jnp.zeros_like(total_ref)
        sums_ref[...] = jnp.zeros_like(sums_ref)

    gain = vec_ref[0, 1:2].astype(F32)
    shift = vec_ref[0, 2:3].astype(F32)
    gain_grad = jnp.zeros((1, UNITS), F32)
    bias_grad = jnp.zeros((1, UNITS), F32)
    for start in range(0, rows_all, TILE):
        rows = pl.ds(start, TILE)
        normed = (act_ref[0, rows].astype(F32) - mean_ref[rows, 0:1]) * inv_ref[rows, 0:1]
        low = (normed * gain + shift).astype(BF)
        low_ref[rows] = low
        total_ref[rows] += dot_nn(low, down_ref[0])
        grad = dot_nt(cot_ref[rows], down_ref[0])
        gain_grad = gain_grad + column_sum(grad * normed)
        bias_grad = bias_grad + column_sum(grad)
        e = grad * gain
        e_ref[0, rows] = e.astype(BF)
        sums_ref[0, rows] += lane_fold(e)
        sums_ref[1, rows] += lane_fold(e * normed)
    vec_grad_ref[0, 0:1] = gain_grad
    vec_grad_ref[0, 1:2] = bias_grad
    down_grad_ref[0] = dot_tn(low_ref[...], cot_ref[...]).astype(BF)

    @pl.when(step == last)
    def _():
        cot_sum = jnp.zeros((1, cot_ref.shape[1]), F32)
        for start in range(0, rows_all, TILE):
            rows = pl.ds(start, TILE)
            mixed_ref[rows] = (middle_ref[rows] + total_ref[rows] + shift_ref[...]).astype(BF)
            first = jnp.sum(sums_ref[0, rows], axis=1, keepdims=True) / units
            cross = jnp.sum(sums_ref[1, rows], axis=1, keepdims=True) / units
            first_ref[rows] = jnp.broadcast_to(first, (TILE, 128))
            cross_ref[rows] = jnp.broadcast_to(cross, (TILE, 128))


def down_pass(act, mean, inv, vec, down, cotangent, middle, shift):
    rows, width = cotangent.shape
    steps = act.shape[0]
    block = pl.BlockSpec((1, rows, UNITS), lambda j: (j, 0, 0))
    return pl.pallas_call(
        functools.partial(down_kernel, steps * UNITS),
        grid=(steps,),
        in_specs=[
            block,
            whole((rows, 128)),
            whole((rows, 128)),
            pl.BlockSpec((1, vec.shape[1], UNITS), lambda j: (j, 0, 0)),
            pl.BlockSpec((1, UNITS, width), lambda j: (j, 0, 0)),
            whole((rows, width)),
            whole((rows, width)),
            whole((1, width)),
        ],
        out_specs=[
            whole((rows, width)),
            pl.BlockSpec((1, UNITS, width), lambda j: (j, 0, 0)),
            block,
            whole((rows, 128)),
            whole((rows, 128)),
            pl.BlockSpec((1, 8, UNITS), lambda j: (j, 0, 0)),
        ],
        out_shape=[
            jax.ShapeDtypeStruct((rows, width), BF),
            jax.ShapeDtypeStruct((steps, UNITS, width), BF),
            jax.ShapeDtypeStruct((steps, rows, UNITS), BF),
            jax.ShapeDtypeStruct((rows, 128), F32),
            jax.ShapeDtypeStruct((rows, 128), F32),
            jax.ShapeDtypeStruct((steps, 8, UNITS), F32),
        ],
        scratch_shapes=[
            pltpu.VMEM((rows, width), F32),
            pltpu.VMEM((2, rows, 128), F32),
            pltpu.VMEM((rows, UNITS), BF),
        ],
        compiler_params=params(),
        name="down_pass",
    )(act, mean, inv, vec, down, cotangent, middle, shift)


def up_back_kernel(
    act_ref,
    slope_ref,
    e_ref,
    mean_ref,
    inv_ref,
    first_ref,
    cross_ref,
    up_ref,
    feed_ref,
    up_grad_ref,
    bias_grad_ref,
    total_ref,
    turned_ref,
    low_ref,
):
    step = pl.program_id(0)
    rows_all = feed_ref.shape[0]

    @pl.when(step == 0)
    def _():
        total_ref[...] = jnp.zeros_like(total_ref)
        turned_ref[...] = feed_ref[...].T

    bias_grad = jnp.zeros((1, UNITS), F32)
    for start in range(0, rows_all, TILE):
        rows = pl.ds(start, TILE)
        inv = inv_ref[rows, 0:1]
        normed = (act_ref[0, rows].astype(F32) - mean_ref[rows, 0:1]) * inv
        grad_act = inv * (
            e_ref[0, rows].astype(F32) - first_ref[rows, 0:1] - normed * cross_ref[rows, 0:1]
        )
        low = (grad_act * slope_ref[0, rows].astype(F32)).astype(BF)
        bias_grad = bias_grad + column_sum(low.astype(F32))
        low_ref[rows] = low
        total_ref[rows] += dot_nt(low, up_ref[0])
    bias_grad_ref[0, 0:1] = bias_grad
    up_grad_ref[0] = dot_nn(turned_ref[...], low_ref[...]).astype(BF)


def up_back(act, slope, e, mean, inv, first, cross, up, feed):
    rows, width = feed.shape
    steps = act.shape[0]
    block = pl.BlockSpec((1, rows, UNITS), lambda j: (j, 0, 0))
    narrow = whole((rows, 128))
    return pl.pallas_call(
        up_back_kernel,
        grid=(steps,),
        in_specs=[
            block,
            block,
            block,
            narrow,
            narrow,
            narrow,
            narrow,
            pl.BlockSpec((1, width, UNITS), lambda j: (j, 0, 0)),
            whole((rows, width)),
        ],
        out_specs=[
            pl.BlockSpec((1, width, UNITS), lambda j: (j, 0, 0)),
            pl.BlockSpec((1, 8, UNITS), lambda j: (j, 0, 0)),
            whole((rows, width)),
        ],
        out_shape=[
            jax.ShapeDtypeStruct((steps, width, UNITS), BF),
            jax.ShapeDtypeStruct((steps, 8, UNITS), F32),
            jax.ShapeDtypeStruct((rows, width), F32),
        ],
        scratch_shapes=[pltpu.VMEM((width, rows), BF), pltpu.VMEM((rows, UNITS), BF)],
        compiler_params=params(),
        name="up_back",
    )(act, slope, e, mean, inv, first, cross, up, feed)


def out_back_kernel(
    grad_feed_ref,
    cot_ref,
    middle_ref,
    branch_ref,
    scaled_ref,
    attended_ref,
    weight_ref,
    vec_ref,
    hs_ref,
    heads_ref,
    grad_middle_ref,
    ga_ref,
    out_grad_ref,
    delta_ref,
    sums_ref,
    total_ref,
):
    step = pl.program_id(0)

    @pl.when(step == 0)
    def _():
        total_ref[...] = jnp.zeros_like(total_ref)
        sums_ref[...] = jnp.zeros_like(sums_ref)

    grad_feed = grad_feed_ref[...]
    normed, inv = row_norm(middle_ref[...])
    cot = cot_ref[...].astype(F32)
    grad_middle = cot + norm_back(grad_feed, vec_ref[7:8], normed, inv)
    grad_middle_ref[...] = grad_middle
    sums_ref[7:8] += column_sum(grad_feed * normed)
    sums_ref[8:9] += column_sum(grad_feed)
    sums_ref[9:10] += column_sum(cot)
    normed, inv = row_norm(branch_ref[...])
    low = norm_back(grad_middle, vec_ref[5:6], normed, inv).astype(BF)
    sums_ref[5:6] += column_sum(grad_middle * normed)
    sums_ref[6:7] += column_sum(grad_middle)
    sums_ref[2:3] += column_sum(low.astype(F32))
    scaled = scaled_ref[...]
    total_ref[...] += dot_tn(scaled, low)
    grad_scaled = dot_nt(low, weight_ref[...])
    grad_out = (grad_scaled * hs_ref[...]).astype(BF)
    ga_ref[...] = grad_out
    product = grad_out.astype(F32) * attended_ref[...]
    high = product.astype(BF)
    rest = (product - high.astype(F32)).astype(BF)
    delta = dot_nn(high, heads_ref[...]) + dot_nn(rest, heads_ref[...])
    delta_ref[...] = delta.T[: delta_ref.shape[0]]

    @pl.when(step == pl.num_programs(0) - 1)
    def _():
        out_grad_ref[...] = total_ref[...].astype(BF)


def out_back(
    grad_feed, cotangent, middle, branch, scaled, attended, weights, vectors, head_lanes, heads_map
):
    rows, width = cotangent.shape
    heads = 2 * width // 128
    by_row = pl.BlockSpec((TILE, width), lambda i: (i, 0))
    return pl.pallas_call(
        out_back_kernel,
        grid=(rows // TILE,),
        in_specs=[
            by_row,
            by_row,
            by_row,
            by_row,
            by_row,
            by_row,
            whole((width, width)),
            whole(vectors.shape),
            whole((1, width)),
            whole(heads_map.shape),
        ],
        out_specs=[
            by_row,
            by_row,
            whole((width, width)),
            pl.BlockSpec((heads, TILE), lambda i: (0, i)),
            whole((16, width)),
        ],
        out_shape=[
            jax.ShapeDtypeStruct((rows, width), F32),
            jax.ShapeDtypeStruct((rows, width), BF),
            jax.ShapeDtypeStruct((width, width), BF),
            jax.ShapeDtypeStruct((heads, rows), F32),
            jax.ShapeDtypeStruct((16, width), F32),
        ],
        scratch_shapes=[pltpu.VMEM((width, width), F32)],
        compiler_params=params(),
        name="out_back",
    )(
        grad_feed,
        cotangent,
        middle,
        branch,
        scaled,
        attended,
        weights,
        vectors,
        head_lanes,
        heads_map,
    )


def attention_back_head(
    head, cross, q_ref, k_ref, v_ref, ga_ref, lse_ref, delta_ref, dq_ref, dk_ref, dv_ref
):
    rows = q_ref.shape[0]
    half = rows // 2
    factor = LOG2E * (q_ref.shape[1] // 2) ** (-0.5)
    low_lanes = lax.broadcasted_iota(jnp.int32, (1, 128), 1) < 64
    mine = low_lanes if head == 0 else ~low_lanes
    above = lax.broadcasted_iota(jnp.int32, (TILE, TILE), 0) <= lax.broadcasted_iota(
        jnp.int32, (TILE, TILE), 1
    )
    zero = jnp.zeros((rows, 128), BF)
    query = jnp.where(mine, q_ref[...], zero)
    grad = jnp.where(mine, ga_ref[...], zero)
    key_own = jnp.where(mine, k_ref[...], zero)
    for start in range(0, rows, TILE):
        stop = start + TILE
        raw = dot_nt(k_ref[start:stop], query[start:])
        level = lse_ref[0, head : head + 1, start:]
        parts = [jnp.where(above, raw[:, :TILE] * factor - level[:, :TILE], MASKED)]
        if start < half:
            if stop < half:
                parts.append(raw[:, TILE : half - start] * factor - level[:, TILE : half - start])
            parts.append(raw[:, half - start :] * factor - (level[:, half - start :] - cross))
        elif stop < rows:
            parts.append(raw[:, TILE:] * factor - level[:, TILE:])
        exponent = parts[0] if len(parts) == 1 else jnp.concatenate(parts, axis=1)
        weights = jnp.exp2(exponent)
        grad_weights = dot_nt(v_ref[start:stop], grad[start:])
        grad_scores = (weights * (grad_weights - delta_ref[head : head + 1, start:])).astype(BF)
        dv = dot_nn(weights.astype(BF), grad[start:])
        dk = dot_nn(grad_scores, query[start:])
        dq = dot_tn(grad_scores, key_own[start:stop])
        if head == 0:
            dv_ref[start:stop] = dv
            dk_ref[start:stop] = dk
        else:
            dv_ref[start:stop] += dv
            dk_ref[start:stop] += dk
        if head == 0 and start == 0:
            dq_ref[...] = dq
        else:
            dq_ref[start:] += dq


def in_back_kernel(
    cross_ref,
    proj_ref,
    ga_ref,
    lse_ref,
    delta_ref,
    wq_ref,
    wk_ref,
    wv_ref,
    first_ref,
    out_grad_ref,
    tokens_ref,
    gain_ref,
    grad_middle_ref,
    chunk_ref,
    bias_ref,
    tokens_grad_ref,
    sums_ref,
    dq_ref,
    dk_ref,
    dv_ref,
    turned_ref,
    total_ref,
):
    step = pl.program_id(0)
    q_ref, k_ref, v_ref = three(proj_ref)
    rows_all = tokens_ref.shape[0]

    @pl.when(step == 0)
    def _():
        turned_ref[...] = first_ref[...].T
        total_ref[...] = jnp.zeros_like(total_ref)

    delta = delta_ref.at[0]
    for head in range(2):
        attention_back_head(
            head,
            cross_ref[0, 0],
            q_ref,
            k_ref,
            v_ref,
            ga_ref,
            lse_ref,
            delta,
            dq_ref,
            dk_ref,
            dv_ref,
        )
    factor = (q_ref.shape[1] // 2) ** (-0.5)
    dq = (dq_ref[...] * factor).astype(BF)
    dk = (dk_ref[...] * factor).astype(BF)
    dv = dv_ref[...].astype(BF)
    bias_ref[0, 0:1] = column_sum(dq.astype(F32))
    bias_ref[0, 1:2] = column_sum(dv.astype(F32))
    grads = jnp.concatenate([dq, dk, dv], axis=1)
    weights = jnp.concatenate([wq_ref[...], wk_ref[...], wv_ref[...]], axis=1)
    for start in range(0, rows_all, TILE):
        rows = pl.ds(start, TILE)
        total_ref[rows] += dot_nt(grads[start : start + TILE], weights)
        part = jnp.concatenate([dot_nn(turned_ref[rows], grads).astype(BF), out_grad_ref[rows]], axis=1)
        chunk_ref[0, :, start // TILE] = part.reshape(8, 32, 512)

    @pl.when(step == pl.num_programs(0) - 1)
    def _():
        gain_grad = jnp.zeros((1, total_ref.shape[1]), F32)
        shift_grad = jnp.zeros((1, total_ref.shape[1]), F32)
        for start in range(0, rows_all, TILE):
            rows = pl.ds(start, TILE)
            normed, inv = row_norm(tokens_ref[rows].astype(F32))
            grad = total_ref[rows]
            gain_grad = gain_grad + column_sum(grad * normed)
            shift_grad = shift_grad + column_sum(grad)
            back = norm_back(grad, gain_ref[...], normed, inv)
            tokens_grad_ref[rows] = (grad_middle_ref[rows] + back).astype(BF)
        sums_ref[0:1] = gain_grad
        sums_ref[1:2] = shift_grad


def in_back(cross, projected, ga, lse, delta, weights, first, out_grad, tokens, gain, grad_middle):
    rows, width = tokens.shape
    pairs = width // 128
    column = pl.BlockSpec((rows, 128), lambda p: (0, p))
    square = whole((rows, width))
    return pl.pallas_call(
        in_back_kernel,
        grid=(pairs,),
        in_specs=[
            pl.BlockSpec(memory_space=pltpu.SMEM),
            pl.BlockSpec((1, rows, 384), lambda p: (p, 0, 0)),
            column,
            pl.BlockSpec((1, 8, rows), lambda p: (p, 0, 0)),
            pl.BlockSpec((1, 2, rows), lambda p: (p, 0, 0)),
            pl.BlockSpec((width, 128), lambda p: (0, p)),
            pl.BlockSpec((width, 128), lambda p: (0, pairs + p)),
            pl.BlockSpec((width, 128), lambda p: (0, 2 * pairs + p)),
            square,
            column,
            square,
            whole((1, width)),
            square,
        ],
        out_specs=[
            pl.BlockSpec((1, 8, width // TILE, 32, 512), lambda p: (p, 0, 0, 0, 0)),
            pl.BlockSpec((1, 8, 128), lambda p: (p, 0, 0)),
            square,
            whole((8, width)),
        ],
        out_shape=[
            jax.ShapeDtypeStruct((pairs, 8, width // TILE, 32, 512), BF),
            jax.ShapeDtypeStruct((pairs, 8, 128), F32),
            jax.ShapeDtypeStruct((rows, width), BF),
            jax.ShapeDtypeStruct((8, width), F32),
        ],
        scratch_shapes=[
            pltpu.VMEM((rows, 128), F32),
            pltpu.VMEM((rows, 128), F32),
            pltpu.VMEM((rows, 128), F32),
            pltpu.VMEM((width, rows), BF),
            pltpu.VMEM((rows, width), F32),
        ],
        compiler_params=params(),
        name="in_back",
    )(
        cross,
        projected,
        ga,
        lse,
        delta,
        weights,
        weights,
        weights,
        first,
        out_grad,
        tokens,
        gain,
        grad_middle,
    )


class Place:
    def __init__(self):
        self.z = lax.axis_index("dp")
        wide = lax.axis_index("wide")
        self.y = wide // 4
        self.x = (wide // 2) % 2
        self.c = wide % 2
        self.core = (self.z, wide + 1 - 2 * self.c)
        self.side = (self.z, wide + 2 - 4 * self.x)
        self.over = (self.z, wide + 4 - 8 * self.y)
        self.ranks = (self.z + 1 - 2 * (self.z % 2), (self.z + 2) % 4, 3 - self.z)
        self.planes = tuple((rank, wide) for rank in self.ranks)

    def greet(self, planes=True):
        barrier = pltpu.get_barrier_semaphore()
        peers = (self.core, self.side, self.over) + (self.planes if planes else ())
        for peer in peers:
            pl.semaphore_signal(barrier, inc=1, device_id=peer, device_id_type=MESH)
        pl.semaphore_wait(barrier, len(peers))


class WideGather:
    copies = 13

    def __init__(self, place, source, target, send, recv, first, last):
        rows = target.shape[-2]
        y, x, c = place.y, place.x, place.c
        here, side, over, far = (y, x, c), (y, 1 - x, c), (1 - y, x, c), (1 - y, 1 - x, c)
        upper, lower, both = pl.ds(0, rows // 2), pl.ds(rows // 2, rows // 2), pl.ds(0, rows)

        def copy(index, slot, part, peer):
            destination = target.at[(*slot, part)]
            return pltpu.make_async_remote_copy(
                src_ref=source.at[part] if source is not None and slot is here else destination,
                dst_ref=destination,
                send_sem=send.at[first + index],
                recv_sem=recv.at[first + index],
                device_id=peer,
                device_id_type=MESH,
            )

        self.all = (
            copy(0, here, upper, place.side),
            copy(1, here, lower, place.over),
            copy(2, here, upper, place.over),
            copy(3, here, lower, place.side),
            copy(4, here, both, place.core),
            copy(5, side, upper, place.over),
            copy(6, side, upper, place.core),
            copy(7, over, lower, place.side),
            copy(8, over, lower, place.core),
            copy(9, side, lower, place.core),
            copy(10, over, upper, place.core),
            copy(11, far, upper, place.core),
            copy(12, far, lower, place.core),
        )
        self.own = None
        if source is not None:
            self.own = pltpu.make_async_copy(source, target.at[here], last)

    def start(self):
        if self.own is not None:
            self.own.start()
        for index in range(5):
            self.all[index].start()

    def relay(self, stage):
        waits, starts = (((0, 1), (5, 7, 6, 8)), ((2, 3), (9, 10)), ((5, 7), (11, 12)))[stage]
        for index in waits:
            self.all[index].wait_recv()
        for index in starts:
            self.all[index].start()

    def finish(self):
        for index in (4, 6, 8, 9, 10, 11, 12):
            self.all[index].wait_recv()
        for copy in self.all:
            copy.wait_send()
        if self.own is not None:
            self.own.wait()


class Reduction:
    stages = 6

    @staticmethod
    def scratch():
        return [
            pltpu.VMEM((2, 2, 2, 4, 32, 512), BF),
            pltpu.VMEM((2, 2, 2, 4, 32, 512), BF),
            pltpu.VMEM((3, 2, 2, 4, 32, 512), BF),
            pltpu.VMEM((2, 2, 4, 16, 512), BF),
            pltpu.VMEM((2, 2, 4, 16, 512), BF),
            pltpu.VMEM((2, 4, 16, 512), BF),
            pltpu.VMEM((2, 4, 16, 512), BF),
            pltpu.VMEM((2, 4, 32, 512), BF),
            pltpu.VMEM((2, 3, 32, 512), BF),
            pltpu.VMEM((2, 32, 512), BF),
            pltpu.VMEM((4, 3, 32, 512), BF),
            pltpu.SemaphoreType.DMA((11, 4)),
            pltpu.SemaphoreType.DMA((11, 4)),
            pltpu.SemaphoreType.DMA((2,)),
        ]

    def __init__(self, place, refs):
        self.place = place
        (
            self.mine,
            self.partner,
            self.chip,
            self.from_x,
            self.from_y,
            self.then_y,
            self.then_x,
            self.plane,
            self.from_z,
            self.sums,
            self.shared,
            self.send,
            self.recv,
            self.local,
        ) = refs

    def copy(self, index, slot, source, target, peer):
        return pltpu.make_async_remote_copy(
            src_ref=source,
            dst_ref=target,
            send_sem=self.send.at[index, slot],
            recv_sem=self.recv.at[index, slot],
            device_id=peer,
            device_id_type=MESH,
        )

    def to_core(self, chunk, source):
        slot = chunk % 2
        return self.copy(0, slot, source, self.partner.at[slot], self.place.core)

    def load(self, chunk, source):
        slot = chunk % 2
        return pltpu.make_async_copy(source, self.mine.at[slot], self.local.at[slot])

    def first_hop(self, chunk):
        p, slot, chip = self.place, chunk % 2, self.chip.at[chunk % 3]
        return (
            self.copy(1, slot, chip.at[:, 1 - p.x, :, pl.ds(0, 16)], self.from_x.at[slot], p.side),
            self.copy(2, slot, chip.at[1 - p.y, :, :, pl.ds(16, 16)], self.from_y.at[slot], p.over),
        )

    def second_hop(self, chunk):
        p, slot, chip = self.place, chunk % 2, self.chip.at[chunk % 3]
        return (
            self.copy(3, slot, chip.at[1 - p.y, p.x, :, pl.ds(0, 16)], self.then_y.at[slot], p.over),
            self.copy(4, slot, chip.at[p.y, 1 - p.x, :, pl.ds(16, 16)], self.then_x.at[slot], p.side),
        )

    def to_planes(self, chunk):
        p, slot = self.place, chunk % 2
        return [
            self.copy(5 + k, slot, self.plane.at[slot, p.ranks[k]], self.from_z.at[slot, k], p.planes[k])
            for k in range(3)
        ]

    def share(self, chunk):
        p = self.place
        return [
            self.copy(8 + k, chunk % 4, self.sums.at[chunk % 2], self.shared.at[chunk % 4, k], p.planes[k])
            for k in range(3)
        ]

    def stage0(self, chunk, away, home):
        self.to_core(chunk, away).start()
        self.load(chunk, home).start()

    def stage1(self, chunk, away, home):
        slot = chunk % 2
        self.load(chunk, home).wait()
        self.to_core(chunk, away).wait()
        self.chip[chunk % 3] = self.mine[slot] + self.partner[slot]
        for copy in self.first_hop(chunk):
            copy.start()

    def stage2(self, chunk):
        p, slot, index = self.place, chunk % 2, chunk % 3
        for copy in self.first_hop(chunk):
            copy.wait()
        for k in range(2):
            self.chip[index, k, p.x, :, 0:16] += self.from_x[slot, k]
            self.chip[index, p.y, k, :, 16:32] += self.from_y[slot, k]
        for copy in self.second_hop(chunk):
            copy.start()

    def stage3(self, chunk):
        p, slot, index = self.place, chunk % 2, chunk % 3
        for copy in self.second_hop(chunk):
            copy.wait()
        self.plane[slot, :, 0:16] = self.chip[index, p.y, p.x, :, 0:16] + self.then_y[slot]
        self.plane[slot, :, 16:32] = self.chip[index, p.y, p.x, :, 16:32] + self.then_x[slot]
        for copy in self.to_planes(chunk):
            copy.start()

    def stage4(self, chunk):
        slot = chunk % 2
        for copy in self.to_planes(chunk):
            copy.wait()
        total = self.plane[slot, self.place.z].astype(F32)
        for k in range(3):
            total = total + self.from_z[slot, k].astype(F32)
        return total


def reduce_kernel(down_ref, up_ref, attn_ref, vec_ref, down_out, up_out, attn_out, *scratch):
    place = Place()
    step = pl.program_id(0)
    engine = Reduction(place, scratch)

    @pl.when(step == 0)
    def _():
        place.greet()

    c = place.c
    ends = (8, 16, 24, 25)

    def sources(chunk):
        down = down_ref.at[:, :, :, chunk % 8 // 2, :, :, pl.ds(pl.multiple_of(chunk % 2 * 512, 512), 512)]
        up = up_ref.at[:, :, :, chunk % 8]
        attn = attn_ref.at[chunk % 8]
        return [(view.at[:, :, 1 - c], view.at[:, :, c]) for view in (down, up, attn, vec_ref)]

    def guarded(stage, low, high, action):
        chunk = step - stage

        @pl.when((chunk >= low) & (chunk < high))
        def _():
            action(chunk)

    def publish(chunk, shape_out):
        for copy in engine.share(chunk):
            copy.wait()

        def store(rank, value):
            shape_out(chunk, rank, value)

        store(place.z, engine.sums[chunk % 2])
        for k in range(3):
            store(place.ranks[k], engine.shared[chunk % 4, k])

    def put_down(chunk, rank, value):
        for half in range(2):

            @pl.when(chunk % 2 == half)
            def _():
                down_out[chunk // 2, rank, :, half * 512 : half * 512 + 512] = value

    def put_up(chunk, rank, value):
        up_out[chunk - 8, rank] = value

    def finish_shared(chunk):
        total = engine.stage4(chunk)
        engine.sums[chunk % 2] = total.astype(BF)
        for copy in engine.share(chunk):
            copy.start()

    def finish_own(chunk):
        attn_out[chunk - 16] = engine.stage4(chunk)

    guarded(5, 0, 8, lambda chunk: publish(chunk, put_down))
    guarded(5, 8, 16, lambda chunk: publish(chunk, put_up))
    guarded(4, 0, 16, finish_shared)
    guarded(4, 16, 25, finish_own)
    guarded(3, 0, 25, engine.stage3)
    guarded(2, 0, 25, engine.stage2)
    guarded(1, 0, 25, lambda chunk: engine.stage1(chunk, *sources(chunk)[2]))
    for index in range(4):
        low = 0 if index == 0 else ends[index - 1]
        guarded(0, low, ends[index], lambda chunk: engine.stage0(chunk, *sources(chunk)[index]))


def reduce_all(down, up, attn, vec):
    return pl.pallas_call(
        reduce_kernel,
        grid=(25 + 5,),
        in_specs=[ANY] * 4,
        out_specs=[
            whole((4, 4, 32, 1024)),
            whole((8, 4, 32, 512)),
            whole((9, 32, 512)),
        ],
        out_shape=[
            jax.ShapeDtypeStruct((4, 4, 32, 1024), BF),
            jax.ShapeDtypeStruct((8, 4, 32, 512), BF),
            jax.ShapeDtypeStruct((9, 32, 512), F32),
        ],
        scratch_shapes=Reduction.scratch(),
        compiler_params=params(collective_id=1, has_side_effects=True),
        name="reduce_all",
    )(down, up, attn, vec)


def dma_sems(count):
    return [pltpu.SemaphoreType.DMA((count,)), pltpu.SemaphoreType.DMA((count,))]


class FullGather:
    copies = 3 + 4 * WideGather.copies

    def __init__(self, place, source, target, send, recv, first, last):
        own = (place.y, place.x, place.c)
        mine = target.at[(place.z, *own)]
        self.across = [
            pltpu.make_async_remote_copy(
                src_ref=source if source is not None else mine,
                dst_ref=mine,
                send_sem=send.at[first + index],
                recv_sem=recv.at[first + index],
                device_id=peer,
                device_id_type=MESH,
            )
            for index, peer in enumerate(place.planes)
        ]
        self.parts = [
            WideGather(
                place,
                source if index == 0 else None,
                target.at[rank],
                send,
                recv,
                first + 3 + index * WideGather.copies,
                last,
            )
            for index, rank in enumerate((place.z, *place.ranks))
        ]

    def start(self):
        for copy in self.across:
            copy.start()
        self.parts[0].start()

    def spread(self):
        for index in range(3):
            self.across[index].wait_recv()
            self.parts[index + 1].start()

    def relay(self, stage):
        for part in self.parts:
            part.relay(stage)

    def finish(self):
        for copy in self.across:
            copy.wait_send()
        for part in self.parts:
            part.finish()


def first_kernel(
    cross_ref,
    tokens_ref,
    in_ref,
    vec_ref,
    out_ref,
    up_ref,
    unit_ref,
    hs_ref,
    first_ref,
    proj_ref,
    scaled_ref,
    attended_ref,
    lse_ref,
    vectors_ref,
    in_all,
    out_all,
    up_all,
    unit_all,
    held_ref,
    normed_ref,
    vext_ref,
    send_in,
    recv_in,
    send_out,
    recv_out,
    send_ff,
    recv_ff,
    local,
):
    step = pl.program_id(0)
    place = Place()
    width = tokens_ref.shape[1]
    count = WideGather.copies
    into = FullGather(place, None, held_ref, send_in, recv_in, 0, None)
    out = FullGather(place, out_ref, out_all, send_out, recv_out, 0, local.at[2])
    up = WideGather(place, up_ref, up_all, send_ff, recv_ff, 0, local.at[3])
    unit = WideGather(place, unit_ref, unit_all, send_ff, recv_ff, count, local.at[4])
    keep = pltpu.make_async_copy(held_ref, in_all, local.at[5])

    @pl.when(step == 0)
    def _():
        place.greet()
        mine = held_ref.at[place.z, place.y, place.x, place.c]
        fills = (
            pltpu.make_async_copy(in_ref, mine.at[:, pl.ds(0, 3 * width)], local.at[0]),
            pltpu.make_async_copy(vec_ref, mine.at[:, pl.ds(3 * width, 128)], local.at[1]),
        )
        for copy in fills:
            copy.start()
        for copy in fills:
            copy.wait()
        into.start()
        for start in range(0, tokens_ref.shape[0], TILE):
            rows = pl.ds(start, TILE)
            normed, _ = row_norm(tokens_ref[rows].astype(F32))
            normed_ref[rows] = normed
        for index in range(3):
            into.parts[index].relay(0)
            into.across[index].wait_recv()
            into.parts[index + 1].start()
            into.parts[index].relay(1)
            into.parts[index].relay(2)
        for stage in range(3):
            into.parts[3].relay(stage)
        out.start()
        unit.start()
        up.start()
        into.finish()
        keep.start()
        lanes = lax.broadcasted_iota(jnp.int32, (1, 128), 1) // 32
        for z in range(4):
            for y in range(2):
                tile = jnp.zeros((16, 128), F32)
                for x in range(2):
                    for c in range(2):
                        piece = held_ref[z, y, x, c, 0:16, 3 * width : 3 * width + 128].astype(F32)
                        tile = jnp.where(lanes == 2 * x + c, piece, tile)
                vectors_ref[:, (2 * z + y) * 128 : (2 * z + y + 1) * 128] = tile
        for start in range(0, tokens_ref.shape[0], TILE):
            rows = pl.ds(start, TILE)
            first_ref[rows] = (normed_ref[rows] * vectors_ref[3:4] + vectors_ref[4:5]).astype(BF)

    @pl.when(step == 1)
    def _():
        out.spread()

    @pl.when((step >= 2) & (step <= 4))
    def _():
        for stage in range(3):

            @pl.when(step == 2 + stage)
            def _():
                out.relay(stage)
                unit.relay(stage)

    for stage, at in enumerate((3, 5, 8)):

        @pl.when(step == at)
        def _():
            up.relay(stage)

    @pl.when(step > 0)
    def _():
        pair = step - 1
        columns = [pl.ds(pl.multiple_of(part * width + pair * 128, 128), 128) for part in range(3)]
        weights = jnp.concatenate(
            [held_ref[:, :, :, :, :, cols].reshape(width, 128) for cols in columns], axis=1
        )
        own = pl.ds(pl.multiple_of(pair * 128, 128), 128)
        bias = jnp.concatenate(
            [vectors_ref[0:1, own], jnp.zeros((1, 128), F32), vectors_ref[1:2, own]], axis=1
        )
        project_pair(first_ref, weights, bias, proj_ref)
        attention_pair(
            cross_ref[0, 0], *three(proj_ref), hs_ref, scaled_ref, attended_ref, lse_ref, vext_ref
        )

    @pl.when(step == pl.num_programs(0) - 1)
    def _():
        keep.wait()
        out.finish()
        unit.finish()
        up.finish()


def first_part(cross, tokens, in_weight, vec, out_weight, up_weight, unit_rows, head_lanes):
    rows, width = tokens.shape
    pairs = width // 128

    def at(step):
        return jnp.maximum(step - 1, 0)

    column = pl.BlockSpec((rows, 128), lambda s: (0, at(s)))
    held = (4, 2, 2, 2, 32, 3 * width + 128)
    return pl.pallas_call(
        first_kernel,
        grid=(pairs + 1,),
        in_specs=[
            pl.BlockSpec(memory_space=pltpu.SMEM),
            whole((rows, width)),
            ANY,
            ANY,
            ANY,
            ANY,
            ANY,
            pl.BlockSpec((1, 128), lambda s: (0, at(s))),
        ],
        out_specs=[
            whole((rows, width)),
            pl.BlockSpec((1, rows, 384), lambda s: (at(s), 0, 0)),
            column,
            column,
            pl.BlockSpec((1, 8, rows), lambda s: (at(s), 0, 0)),
            whole((16, width)),
            ANY,
            ANY,
            ANY,
            ANY,
        ],
        out_shape=[
            jax.ShapeDtypeStruct((rows, width), BF),
            jax.ShapeDtypeStruct((pairs, rows, 384), BF),
            jax.ShapeDtypeStruct((rows, width), BF),
            jax.ShapeDtypeStruct((rows, width), F32),
            jax.ShapeDtypeStruct((pairs, 8, rows), F32),
            jax.ShapeDtypeStruct((16, width), F32),
            jax.ShapeDtypeStruct(held, BF),
            jax.ShapeDtypeStruct((4, 2, 2, 2, *out_weight.shape), BF),
            jax.ShapeDtypeStruct((2, 2, 2, *up_weight.shape), BF),
            jax.ShapeDtypeStruct((2, 2, 2, *unit_rows.shape), BF),
        ],
        scratch_shapes=[
            pltpu.VMEM(held, BF),
            pltpu.VMEM((rows, width), F32),
            pltpu.VMEM((rows, 256), BF),
            *dma_sems(FullGather.copies),
            *dma_sems(FullGather.copies),
            *dma_sems(2 * WideGather.copies),
            pltpu.SemaphoreType.DMA((6,)),
        ],
        compiler_params=params(collective_id=0, has_side_effects=True),
        name="first_part",
    )(cross, tokens, in_weight, vec, out_weight, up_weight, unit_rows, head_lanes)


def second_kernel(
    units,
    scaled_ref,
    weight_ref,
    vec_ref,
    tokens_ref,
    up_ref,
    unit_ref,
    down_ref,
    branch_ref,
    middle_ref,
    feed_ref,
    act_ref,
    slope_ref,
    mean_ref,
    inv_ref,
    down_all,
    sums_ref,
    send,
    recv,
    local,
):
    step = pl.program_id(0)
    lead = feed_ref.shape[0] // TILE
    place = Place()
    down = WideGather(place, down_ref, down_all, send, recv, 0, local.at[0])

    @pl.when(step == 0)
    def _():
        place.greet(planes=False)
        down.start()
        sums_ref[...] = jnp.zeros_like(sums_ref)

    for stage, at in enumerate((5, 8, 11)):

        @pl.when(step == at)
        def _():
            down.relay(stage)

    @pl.when(step < lead)
    def _():
        rows = pl.ds(pl.multiple_of(step * TILE, TILE), TILE)
        feed_ref[rows] = out_proj_rows(
            scaled_ref, weight_ref, vec_ref, tokens_ref, branch_ref, middle_ref
        )

    @pl.when(step >= lead)
    def _():
        up_step(feed_ref, up_ref, unit_ref, act_ref, slope_ref, sums_ref)

    @pl.when(step == pl.num_programs(0) - 1)
    def _():
        up_stats(units, mean_ref, inv_ref, sums_ref)
        down.finish()


def second_part(scaled, out_weights, vectors, tokens, up, unit_vec, down_weight):
    rows, width = tokens.shape
    steps = up.shape[0]
    lead = rows // TILE

    def early(step):
        return jnp.minimum(step, lead - 1)

    def late(step):
        return jnp.maximum(step - lead, 0)

    by_row = pl.BlockSpec((TILE, width), lambda s: (early(s), 0))
    block = pl.BlockSpec((1, rows, UNITS), lambda s: (late(s), 0, 0))
    return pl.pallas_call(
        functools.partial(second_kernel, steps * UNITS),
        grid=(lead + steps,),
        in_specs=[
            by_row,
            whole((width, width)),
            whole(vectors.shape),
            by_row,
            pl.BlockSpec((1, width, UNITS), lambda s: (late(s), 0, 0)),
            pl.BlockSpec((1, unit_vec.shape[1], UNITS), lambda s: (late(s), 0, 0)),
            ANY,
        ],
        out_specs=[
            by_row,
            by_row,
            whole((rows, width)),
            block,
            block,
            whole((rows, 128)),
            whole((rows, 128)),
            ANY,
        ],
        out_shape=[
            jax.ShapeDtypeStruct((rows, width), F32),
            jax.ShapeDtypeStruct((rows, width), F32),
            jax.ShapeDtypeStruct((rows, width), BF),
            jax.ShapeDtypeStruct((steps, rows, UNITS), BF),
            jax.ShapeDtypeStruct((steps, rows, UNITS), BF),
            jax.ShapeDtypeStruct((rows, 128), F32),
            jax.ShapeDtypeStruct((rows, 128), F32),
            jax.ShapeDtypeStruct((2, 2, 2, *down_weight.shape), BF),
        ],
        scratch_shapes=[
            pltpu.VMEM((2, rows, 128), F32),
            *dma_sems(WideGather.copies),
            pltpu.SemaphoreType.DMA((1,)),
        ],
        compiler_params=params(collective_id=2, has_side_effects=True),
        name="second_part",
    )(scaled, out_weights, vectors, tokens, up, unit_vec, down_weight)


def layer(staged, tokens, cotangent, lengths, attn, up, down, unit_vec, head_scale, down_bias):
    rows, width = tokens.shape
    heads = head_scale.shape[0]
    pairs = width // 128
    cross = jnp.where(lengths[0:1, 0:1] == rows, 0.0, MASKED).astype(F32)
    scale = head_scale.astype(F32)
    head_lanes = jnp.repeat(scale, width // heads)[None, :]
    heads_map = (
        lax.broadcasted_iota(jnp.int32, (width, 128), 0) // (width // heads)
        == lax.broadcasted_iota(jnp.int32, (width, 128), 1)
    ).astype(BF)
    if staged:
        in_weight, out_weight, vec_block = attn
        (first, projected, scaled, attended, lse, vectors, weights, out_weights, up, unit_vec) = (
            first_part(cross, tokens, in_weight, vec_block, out_weight, up, unit_vec, head_lanes)
        )
        weights = weights.reshape(width, 3 * width + 128)
        out_weights = out_weights.reshape(width, width)
        up = up.reshape(-1, width, UNITS)
        unit_vec = unit_vec.reshape(-1, unit_vec.shape[-2], UNITS)
        branch, middle, feed, act, slope, mean, inv, down = second_part(
            scaled, out_weights, vectors, tokens, up, unit_vec, down
        )
        down = down.reshape(-1, UNITS, width)
    else:
        weights, out_weights, vectors = attn
        first, projected, scaled, attended, lse = plain_first(
            cross, tokens, weights, vectors, head_lanes
        )
        branch, middle, feed = out_proj(scaled, out_weights, vectors, tokens)
        act, slope, mean, inv = up_pass(feed, up, unit_vec)
    mixed, down_grad, e, e_mean, e_cross, unit_grad = down_pass(
        act, mean, inv, unit_vec, down, cotangent, middle, down_bias.astype(F32)[None]
    )
    up_grad, up_bias_grad, grad_feed = up_back(
        act, slope, e, mean, inv, e_mean, e_cross, up, feed
    )
    grad_middle, ga, out_grad, delta, sums = out_back(
        grad_feed,
        cotangent,
        middle,
        branch,
        scaled,
        attended,
        out_weights,
        vectors,
        head_lanes,
        heads_map,
    )
    chunks, proj_bias, tokens_grad, pre_sums = in_back(
        cross,
        projected,
        ga,
        lse,
        delta.reshape(pairs, 2, rows),
        weights,
        first,
        out_grad,
        tokens,
        vectors[3:4],
        grad_middle,
    )
    scale_grad = jnp.sum(delta, axis=1) / scale
    vec_grads = [
        proj_bias[:, 0].reshape(width),
        proj_bias[:, 1].reshape(width),
        sums[2],
        pre_sums[0],
        pre_sums[1],
        sums[5],
        sums[6],
        sums[7],
        sums[8],
    ]
    unit_grads = [up_bias_grad[:, 0], unit_grad[:, 0], unit_grad[:, 1]]
    return mixed, tokens_grad, chunks, up_grad, down_grad, vec_grads, unit_grads, sums[9], scale_grad


def body(
    axes,
    tokens,
    cotangent,
    lengths,
    in_weight,
    query_bias,
    value_bias,
    out_weight,
    out_bias,
    head_scale,
    pre_gain,
    pre_bias,
    post_gain,
    post_bias,
    feed_gain,
    feed_bias,
    up_weight,
    up_bias,
    mid_gain,
    mid_bias,
    down_weight,
    down_bias,
):
    planes, wide = axes
    every = ("dp", "wide")
    staged = (planes, wide) == (4, 8)
    rows, width = tokens.shape
    units = down_weight.shape[0] * wide
    steps = units // UNITS
    share = in_weight.shape[0]
    columns = [
        query_bias,
        value_bias,
        out_bias,
        pre_gain,
        pre_bias,
        post_gain,
        post_bias,
        feed_gain,
        feed_bias,
    ]
    flat = jnp.concatenate(columns).reshape(len(columns), share)
    unit_rows = jnp.concatenate([up_bias, mid_gain, mid_bias]).reshape(3, -1)
    unit_rows = jnp.pad(unit_rows, ((0, 29), (0, 0)))
    if staged:
        vec_block = jnp.pad(jnp.tile(flat, (1, 128 // share)), ((0, 32 - len(columns)), (0, 0)))
        attn = (in_weight, out_weight, vec_block)
        up, unit_vec, down = up_weight, unit_rows, down_weight
    else:
        attn = (
            lax.all_gather(in_weight, every, axis=0, tiled=True),
            lax.all_gather(out_weight, every, axis=0, tiled=True),
            jnp.pad(
                lax.all_gather(flat, every, axis=1, tiled=True), ((0, 16 - len(columns)), (0, 0))
            ).astype(F32),
        )
        up = lax.all_gather(up_weight, "wide", axis=1, tiled=True)
        up = up.reshape(width, steps, UNITS).transpose(1, 0, 2)
        unit_vec = lax.all_gather(unit_rows, "wide", axis=1, tiled=True)
        unit_vec = unit_vec.reshape(32, steps, UNITS).transpose(1, 0, 2)
        down = lax.all_gather(down_weight, "wide", axis=0, tiled=True)
        down = down.reshape(steps, UNITS, width)
    (mixed, tokens_grad, chunks, up_grad, down_grad, vec_grads, unit_grads, down_sum, scale_sum) = (
        layer(
            staged,
            tokens,
            cotangent,
            lengths,
            attn,
            up,
            down,
            unit_vec,
            head_scale,
            down_bias,
        )
    )
    heads = head_scale.shape[0]
    pairs = width // 128
    if staged:
        own = jnp.stack([item.astype(BF) for item in unit_grads], axis=1)
        both = jnp.stack(
            [
                down_sum[:UNITS],
                down_sum[UNITS:],
                jnp.pad(scale_sum, (0, UNITS - heads)),
                jnp.zeros((UNITS,), F32),
                jnp.zeros((UNITS,), F32),
            ]
        ).astype(BF)
        split = jnp.stack(vec_grads).astype(BF).reshape(len(columns), planes, wide, share)
        split = jnp.pad(split.transpose(2, 1, 0, 3), ((0, 0), (0, 0), (0, 15), (0, UNITS - share)))
        vec_chunk = jnp.concatenate(
            [
                jnp.broadcast_to(own[:, None], (wide, planes, 3, UNITS)),
                jnp.broadcast_to(both, (wide, planes, 5, UNITS)),
                split,
            ],
            axis=2,
        )
        down_total, up_total, shares = reduce_all(
            down_grad.reshape(2, 2, 2, 4, 4, 32, width),
            up_grad.reshape(2, 2, 2, 8, 4, 32, UNITS),
            chunks.reshape(pairs, 2, 2, 2, 4, 32, 512),
            vec_chunk.reshape(2, 2, 2, 4, 32, UNITS),
        )
        up_total = up_total.astype(F32).reshape(width, UNITS)
        down_total = down_total.astype(F32).reshape(UNITS, width)
        unit_totals = [shares[8, index] for index in range(3)]
        down_sum = jnp.concatenate([shares[8, 3], shares[8, 4]])
        scale_sum = shares[8, 5, :heads]
        vec_totals = [shares[8, 8 + index, :share] for index in range(len(columns))]
        in_total = shares[:pairs, :, :384].reshape(pairs, share, 3, 128)
        in_total = in_total.transpose(1, 2, 0, 3).reshape(share, 3 * width)
        out_total = shares[:pairs, :, 384:].transpose(1, 0, 2).reshape(share, width)
    else:

        def scatter(value, axis=0, over=every):
            return lax.psum_scatter(value, over, scatter_dimension=axis, tiled=True)

        def both_ways(value, axis):
            part = scatter(value.astype(BF), axis, "wide")
            return lax.psum(part, "dp").astype(F32)

        up_total = both_ways(up_grad.transpose(1, 0, 2).reshape(width, units), 1)
        down_total = both_ways(down_grad.reshape(units, width), 0)
        unit_totals = [
            lax.psum(scatter(item.reshape(units), 0, "wide"), "dp") for item in unit_grads
        ]
        down_sum, scale_sum = lax.psum((down_sum, scale_sum), every)
        vec_totals = [scatter(item) for item in vec_grads]
        natural = chunks.transpose(0, 2, 1, 3, 4).reshape(pairs, width, 512)
        in_total = natural[:, :, :384].reshape(pairs, width, 3, 128)
        in_total = scatter(in_total.transpose(1, 2, 0, 3).reshape(width, 3 * width).astype(F32))
        out_total = scatter(
            natural[:, :, 384:].transpose(1, 0, 2).reshape(width, width).astype(F32)
        )
    return (
        mixed,
        tokens_grad,
        in_total,
        vec_totals[0],
        vec_totals[1],
        out_total,
        vec_totals[2],
        scale_sum,
        vec_totals[3],
        vec_totals[4],
        vec_totals[5],
        vec_totals[6],
        vec_totals[7],
        vec_totals[8],
        up_total,
        unit_totals[0],
        unit_totals[1],
        unit_totals[2],
        down_total,
        down_sum,
    )


def solution(mesh):
    by_all = P(("dp", "wide"))
    rows_all = P(("dp", "wide"), None)
    axes = (mesh.shape["dp"], mesh.shape["wide"])
    return jax.shard_map(
        functools.partial(body, axes),
        mesh=mesh,
        in_specs=(
            rows_all,
            rows_all,
            rows_all,
            rows_all,
            by_all,
            by_all,
            rows_all,
            by_all,
            P(),
            by_all,
            by_all,
            by_all,
            by_all,
            by_all,
            by_all,
            P(None, "wide"),
            P("wide"),
            P("wide"),
            P("wide"),
            P("wide", None),
            P(),
        ),
        out_specs=(
            rows_all,
            rows_all,
            rows_all,
            by_all,
            by_all,
            rows_all,
            by_all,
            P(),
            by_all,
            by_all,
            by_all,
            by_all,
            by_all,
            by_all,
            P(None, "wide"),
            P("wide"),
            P("wide"),
            P("wide"),
            P("wide", None),
            P(),
        ),
        check_vma=False,
    )
```

```python
import functools

import jax
import jax.numpy as jnp
from jax import lax
from jax.experimental import pallas as pl
from jax.experimental.pallas import tpu as pltpu
from jax.sharding import PartitionSpec as P

EPS = 1e-05
ROOT_HALF = 0.7071067811865476
INV_ROOT_TAU = 0.3989422804014327
LOG2E = 1.4426950408889634
MASKED = -1e30
BF = jnp.bfloat16
F32 = jnp.float32
TILE = 256
UNITS = 512
MESH = pl.DeviceIdType.MESH
VMEM_LIMIT = 62 * 1024 * 1024
ANY = pl.BlockSpec(memory_space=pl.ANY)


def dot_nn(left, right):
    return lax.dot_general(left, right, (((1,), (0,)), ((), ())), preferred_element_type=F32)


def dot_nt(left, right):
    return lax.dot_general(left, right, (((1,), (1,)), ((), ())), preferred_element_type=F32)


def dot_tn(left, right):
    return lax.dot_general(left, right, (((0,), (0,)), ((), ())), preferred_element_type=F32)


def params(**more):
    return pltpu.CompilerParams(
        dimension_semantics=("arbitrary",), vmem_limit_bytes=VMEM_LIMIT, **more
    )


def whole(shape):
    zeros = (0,) * len(shape)
    return pl.BlockSpec(shape, lambda *_: zeros, pipeline_mode=pl.Buffered(1))


def row_norm(values):
    center = values - jnp.mean(values, axis=-1, keepdims=True)
    inv = lax.rsqrt(jnp.mean(center * center, axis=-1, keepdims=True) + EPS)
    return center * inv, inv


def norm_back(grad, gain, normed, inv):
    scaled = grad * gain
    first = jnp.mean(scaled, axis=-1, keepdims=True)
    cross = jnp.mean(scaled * normed, axis=-1, keepdims=True)
    return inv * (scaled - first - normed * cross)


def column_sum(values):
    return jnp.sum(values, axis=0, keepdims=True)


def lane_fold(values):
    total = values[:, :128]
    for start in range(128, values.shape[1], 128):
        total = total + values[:, start : start + 128]
    return total


def attention_pair(cross, q_ref, k_ref, v_ref, hs_ref, scaled_ref, out_ref, lse_ref, vext_ref):
    rows = q_ref.shape[0]
    half = rows // 2
    factor = LOG2E * (q_ref.shape[1] // 2) ** (-0.5)
    low_lanes = lax.broadcasted_iota(jnp.int32, (1, 128), 1) < 64
    below = lax.broadcasted_iota(jnp.int32, (TILE, TILE), 1) <= lax.broadcasted_iota(
        jnp.int32, (TILE, TILE), 0
    )
    vext_ref[:, :128] = v_ref[...]
    vext_ref[:, 128:] = jnp.ones((rows, 128), BF)
    for start in range(0, rows, TILE):
        stop = start + TILE
        query = q_ref[start:stop]
        results = []
        for head in range(2):
            mine = low_lanes if head == 0 else ~low_lanes
            own = jnp.where(mine, query, jnp.zeros_like(query))
            raw = dot_nt(own, k_ref[:stop])
            parts = []
            if start >= half:
                parts.append((raw[:, :half], cross))
                if start > half:
                    parts.append((raw[:, half:start], None))
            elif start > 0:
                parts.append((raw[:, :start], None))
            parts.append((jnp.where(below, raw[:, start:stop], MASKED), None))
            peak = None
            for piece, shift in parts:
                top = jnp.max(piece, axis=-1, keepdims=True)
                if shift is not None:
                    top = top + shift
                peak = top if peak is None else jnp.maximum(peak, top)
            weights = []
            for piece, shift in parts:
                level = peak if shift is None else peak - shift
                weights.append(jnp.exp2((piece - level) * factor).astype(BF))
            weights = weights[0] if len(weights) == 1 else jnp.concatenate(weights, axis=1)
            both = dot_nn(weights, vext_ref[:stop])
            total = both[:, 128:]
            results.append((both[:, :128] / total, peak * factor + jnp.log2(total)))
        mixed = jnp.where(low_lanes, results[0][0], results[1][0])
        out_ref[start:stop] = mixed
        scaled_ref[start:stop] = (mixed * hs_ref[...]).astype(BF)
        lse = jnp.where(low_lanes, results[0][1], results[1][1]).T
        lse_ref[0, 0:1, start:stop] = lse[0:1]
        lse_ref[0, 1:2, start:stop] = lse[64:65]


def project_pair(first_ref, weights, bias, proj_ref):
    for start in range(0, first_ref.shape[0], TILE):
        rows = pl.ds(start, TILE)
        proj_ref[0, rows] = (dot_nn(first_ref[rows], weights) + bias).astype(BF)


def three(proj_ref):
    return [proj_ref.at[0, :, pl.ds(part * 128, 128)] for part in range(3)]


def plain_first_kernel(
    cross_ref,
    tokens_ref,
    wq_ref,
    wk_ref,
    wv_ref,
    vectors_ref,
    bq_ref,
    bv_ref,
    hs_ref,
    first_ref,
    proj_ref,
    scaled_ref,
    attended_ref,
    lse_ref,
    vext_ref,
):
    @pl.when(pl.program_id(0) == 0)
    def _():
        for start in range(0, tokens_ref.shape[0], TILE):
            rows = pl.ds(start, TILE)
            normed, _ = row_norm(tokens_ref[rows].astype(F32))
            first_ref[rows] = (normed * vectors_ref[3:4] + vectors_ref[4:5]).astype(BF)

    weights = jnp.concatenate([wq_ref[...], wk_ref[...], wv_ref[...]], axis=1)
    bias = jnp.concatenate([bq_ref[0:1], jnp.zeros((1, 128), F32), bv_ref[1:2]], axis=1)
    project_pair(first_ref, weights, bias, proj_ref)
    attention_pair(
        cross_ref[0, 0], *three(proj_ref), hs_ref, scaled_ref, attended_ref, lse_ref, vext_ref
    )


def plain_first(cross, tokens, weights, vectors, head_lanes):
    rows, width = tokens.shape
    pairs = width // 128
    column = pl.BlockSpec((rows, 128), lambda p: (0, p))
    bias = pl.BlockSpec((16, 128), lambda p: (0, p))
    return pl.pallas_call(
        plain_first_kernel,
        grid=(pairs,),
        in_specs=[
            pl.BlockSpec(memory_space=pltpu.SMEM),
            whole((rows, width)),
            pl.BlockSpec((width, 128), lambda p: (0, p)),
            pl.BlockSpec((width, 128), lambda p: (0, pairs + p)),
            pl.BlockSpec((width, 128), lambda p: (0, 2 * pairs + p)),
            whole(vectors.shape),
            bias,
            bias,
            pl.BlockSpec((1, 128), lambda p: (0, p)),
        ],
        out_specs=[
            whole((rows, width)),
            pl.BlockSpec((1, rows, 384), lambda p: (p, 0, 0)),
            column,
            column,
            pl.BlockSpec((1, 8, rows), lambda p: (p, 0, 0)),
        ],
        out_shape=[
            jax.ShapeDtypeStruct((rows, width), BF),
            jax.ShapeDtypeStruct((pairs, rows, 384), BF),
            jax.ShapeDtypeStruct((rows, width), BF),
            jax.ShapeDtypeStruct((rows, width), F32),
            jax.ShapeDtypeStruct((pairs, 8, rows), F32),
        ],
        scratch_shapes=[pltpu.VMEM((rows, 256), BF)],
        compiler_params=params(),
        name="plain_first",
    )(cross, tokens, weights, weights, weights, vectors, vectors, vectors, head_lanes)


def out_proj_rows(scaled_ref, weight_ref, vec_ref, tokens_ref, branch_ref, middle_ref):
    branch = dot_nn(scaled_ref[...], weight_ref[...]) + vec_ref[2:3]
    normed, _ = row_norm(branch)
    middle = tokens_ref[...].astype(F32) + (normed * vec_ref[5:6] + vec_ref[6:7])
    again, _ = row_norm(middle)
    branch_ref[...] = branch
    middle_ref[...] = middle
    return (again * vec_ref[7:8] + vec_ref[8:9]).astype(BF)


def out_proj_kernel(scaled_ref, weight_ref, vec_ref, tokens_ref, branch_ref, middle_ref, feed_ref):
    feed_ref[...] = out_proj_rows(
        scaled_ref, weight_ref, vec_ref, tokens_ref, branch_ref, middle_ref
    )


def out_proj(scaled, weights, vectors, tokens):
    rows, width = tokens.shape
    by_row = pl.BlockSpec((TILE, width), lambda i: (i, 0))
    return pl.pallas_call(
        out_proj_kernel,
        grid=(rows // TILE,),
        in_specs=[
            by_row,
            whole((width, width)),
            whole(vectors.shape),
            by_row,
        ],
        out_specs=[by_row, by_row, by_row],
        out_shape=[
            jax.ShapeDtypeStruct((rows, width), F32),
            jax.ShapeDtypeStruct((rows, width), F32),
            jax.ShapeDtypeStruct((rows, width), BF),
        ],
        compiler_params=params(),
        name="out_proj",
    )(scaled, weights, vectors, tokens)


def phi_and_slope(value):
    bell = jnp.exp2(value * value * (-0.5 * LOG2E))
    t = 1.0 / (1.0 + (0.3275911 * ROOT_HALF) * jnp.abs(value))
    series = t * (
        0.5 * 0.254829592
        + t
        * (
            0.5 * -0.284496736
            + t * (0.5 * 1.421413741 + t * (0.5 * -1.453152027 + t * (0.5 * 1.061405429)))
        )
    )
    tail = series * bell
    area = jnp.where(value < 0.0, tail, 1.0 - tail)
    return value * area, area + value * bell * INV_ROOT_TAU


def up_step(feed_ref, up_ref, vec_ref, act_ref, slope_ref, sums_ref):
    bias = vec_ref[0, 0:1].astype(F32)
    for start in range(0, feed_ref.shape[0], TILE):
        rows = pl.ds(start, TILE)
        pre = dot_nn(feed_ref[rows], up_ref[0]) + bias
        act, slope = phi_and_slope(pre)
        act_ref[0, rows] = act.astype(BF)
        slope_ref[0, rows] = slope.astype(BF)
        sums_ref[0, rows] += lane_fold(act)
        sums_ref[1, rows] += lane_fold(act * act)


def side_by_side(*columns):
    lane = lax.broadcasted_iota(jnp.int32, (1, 128), 1)
    result = jnp.broadcast_to(columns[-1], (columns[-1].shape[0], 128))
    for index in range(len(columns) - 2, -1, -1):
        result = jnp.where(lane == index, columns[index], result)
    return result


def up_stats(units, stats_ref, sums_ref):
    for start in range(0, stats_ref.shape[0], TILE):
        rows = pl.ds(start, TILE)
        mean = jnp.sum(sums_ref[0, rows], axis=1, keepdims=True) / units
        square = jnp.sum(sums_ref[1, rows], axis=1, keepdims=True) / units
        inv = lax.rsqrt(square - mean * mean + EPS)
        stats_ref[rows] = side_by_side(mean, inv)


def up_kernel(units, feed_ref, up_ref, vec_ref, act_ref, slope_ref, stats_ref, sums_ref):
    step = pl.program_id(0)

    @pl.when(step == 0)
    def _():
        sums_ref[...] = jnp.zeros_like(sums_ref)

    up_step(feed_ref, up_ref, vec_ref, act_ref, slope_ref, sums_ref)

    @pl.when(step == pl.num_programs(0) - 1)
    def _():
        up_stats(units, stats_ref, sums_ref)


def up_pass(feed, up, vec):
    rows, width = feed.shape
    steps = up.shape[0]
    block = pl.BlockSpec((1, rows, UNITS), lambda j: (j, 0, 0))
    return pl.pallas_call(
        functools.partial(up_kernel, steps * UNITS),
        grid=(steps,),
        in_specs=[
            whole((rows, width)),
            pl.BlockSpec((1, width, UNITS), lambda j: (j, 0, 0)),
            pl.BlockSpec((1, vec.shape[1], UNITS), lambda j: (j, 0, 0)),
        ],
        out_specs=[block, block, whole((rows, 128))],
        out_shape=[
            jax.ShapeDtypeStruct((steps, rows, UNITS), BF),
            jax.ShapeDtypeStruct((steps, rows, UNITS), BF),
            jax.ShapeDtypeStruct((rows, 128), F32),
        ],
        scratch_shapes=[pltpu.VMEM((2, rows, 128), F32)],
        compiler_params=params(),
        name="up_pass",
    )(feed, up, vec)


def down_kernel(
    units,
    act_ref,
    stats_ref,
    vec_ref,
    down_ref,
    cot_ref,
    middle_ref,
    shift_ref,
    mixed_ref,
    down_grad_ref,
    e_ref,
    all_stats_ref,
    vec_grad_ref,
    total_ref,
    sums_ref,
    low_ref,
):
    step = pl.program_id(0)
    last = pl.num_programs(0) - 1
    rows_all = cot_ref.shape[0]

    @pl.when(step == 0)
    def _():
        total_ref[...] = jnp.zeros_like(total_ref)
        sums_ref[...] = jnp.zeros_like(sums_ref)

    gain = vec_ref[0, 1:2].astype(F32)
    shift = vec_ref[0, 2:3].astype(F32)
    gain_grad = jnp.zeros((1, UNITS), F32)
    bias_grad = jnp.zeros((1, UNITS), F32)
    for start in range(0, rows_all, TILE):
        rows = pl.ds(start, TILE)
        normed = (act_ref[0, rows].astype(F32) - stats_ref[rows, 0:1]) * stats_ref[rows, 1:2]
        low = (normed * gain + shift).astype(BF)
        low_ref[rows] = low
        total_ref[rows] += dot_nn(low, down_ref[0])
        grad = dot_nt(cot_ref[rows], down_ref[0])
        gain_grad = gain_grad + column_sum(grad * normed)
        bias_grad = bias_grad + column_sum(grad)
        e = grad * gain
        e_ref[0, rows] = e.astype(BF)
        sums_ref[0, rows] += lane_fold(e)
        sums_ref[1, rows] += lane_fold(e * normed)
    vec_grad_ref[0, 0:1] = gain_grad
    vec_grad_ref[0, 1:2] = bias_grad
    down_grad_ref[0] = dot_tn(low_ref[...], cot_ref[...]).astype(BF)

    @pl.when(step == last)
    def _():
        for start in range(0, rows_all, TILE):
            rows = pl.ds(start, TILE)
            mixed_ref[rows] = (middle_ref[rows] + total_ref[rows] + shift_ref[...]).astype(BF)
            first = jnp.sum(sums_ref[0, rows], axis=1, keepdims=True) / units
            cross = jnp.sum(sums_ref[1, rows], axis=1, keepdims=True) / units
            all_stats_ref[rows] = side_by_side(
                stats_ref[rows, 0:1], stats_ref[rows, 1:2], first, cross
            )


def down_pass(act, stats, vec, down, cotangent, middle, shift):
    rows, width = cotangent.shape
    steps = act.shape[0]
    block = pl.BlockSpec((1, rows, UNITS), lambda j: (j, 0, 0))
    return pl.pallas_call(
        functools.partial(down_kernel, steps * UNITS),
        grid=(steps,),
        in_specs=[
            block,
            whole((rows, 128)),
            pl.BlockSpec((1, vec.shape[1], UNITS), lambda j: (j, 0, 0)),
            pl.BlockSpec((1, UNITS, width), lambda j: (j, 0, 0)),
            whole((rows, width)),
            whole((rows, width)),
            whole((1, width)),
        ],
        out_specs=[
            whole((rows, width)),
            pl.BlockSpec((1, UNITS, width), lambda j: (j, 0, 0)),
            block,
            whole((rows, 128)),
            pl.BlockSpec((1, 8, UNITS), lambda j: (j, 0, 0)),
        ],
        out_shape=[
            jax.ShapeDtypeStruct((rows, width), BF),
            jax.ShapeDtypeStruct((steps, UNITS, width), BF),
            jax.ShapeDtypeStruct((steps, rows, UNITS), BF),
            jax.ShapeDtypeStruct((rows, 128), F32),
            jax.ShapeDtypeStruct((steps, 8, UNITS), F32),
        ],
        scratch_shapes=[
            pltpu.VMEM((rows, width), F32),
            pltpu.VMEM((2, rows, 128), F32),
            pltpu.VMEM((rows, UNITS), BF),
        ],
        compiler_params=params(),
        name="down_pass",
    )(act, stats, vec, down, cotangent, middle, shift)


def up_back_step(act, slope, e, stats_ref, up, low_ref, total_ref):
    bias_grad = jnp.zeros((1, UNITS), F32)
    for start in range(0, total_ref.shape[0], TILE):
        rows = pl.ds(start, TILE)
        inv = stats_ref[rows, 1:2]
        normed = (act[rows].astype(F32) - stats_ref[rows, 0:1]) * inv
        grad_act = inv * (
            e[rows].astype(F32) - stats_ref[rows, 2:3] - normed * stats_ref[rows, 3:4]
        )
        low = (grad_act * slope[rows].astype(F32)).astype(BF)
        bias_grad = bias_grad + column_sum(low.astype(F32))
        low_ref[rows, 0:UNITS] = low
        total_ref[rows] += dot_nt(low, up[...])
    return bias_grad


def up_back_kernel(
    act_ref,
    slope_ref,
    e_ref,
    stats_ref,
    up_ref,
    feed_ref,
    up_grad_ref,
    bias_grad_ref,
    total_ref,
    turned_ref,
    low_ref,
):
    @pl.when(pl.program_id(0) == 0)
    def _():
        total_ref[...] = jnp.zeros_like(total_ref)
        turned_ref[...] = feed_ref[...].T

    bias_grad_ref[0, 0:1] = up_back_step(
        act_ref.at[0],
        slope_ref.at[0],
        e_ref.at[0],
        stats_ref,
        up_ref.at[0],
        low_ref,
        total_ref,
    )
    up_grad_ref[0] = dot_nn(turned_ref[...], low_ref[...]).astype(BF)


def up_back(act, slope, e, stats, up, feed):
    rows, width = feed.shape
    steps = act.shape[0]
    block = pl.BlockSpec((1, rows, UNITS), lambda j: (j, 0, 0))
    narrow = whole((rows, 128))
    return pl.pallas_call(
        up_back_kernel,
        grid=(steps,),
        in_specs=[
            block,
            block,
            block,
            narrow,
            pl.BlockSpec((1, width, UNITS), lambda j: (j, 0, 0)),
            whole((rows, width)),
        ],
        out_specs=[
            pl.BlockSpec((1, width, UNITS), lambda j: (j, 0, 0)),
            pl.BlockSpec((1, 8, UNITS), lambda j: (j, 0, 0)),
            whole((rows, width)),
        ],
        out_shape=[
            jax.ShapeDtypeStruct((steps, width, UNITS), BF),
            jax.ShapeDtypeStruct((steps, 8, UNITS), F32),
            jax.ShapeDtypeStruct((rows, width), F32),
        ],
        scratch_shapes=[pltpu.VMEM((width, rows), BF), pltpu.VMEM((rows, UNITS), BF)],
        compiler_params=params(),
        name="up_back",
    )(act, slope, e, stats, up, feed)


def out_back_rows(
    grad_feed, cot_ref, middle_ref, branch_ref, scaled, attended_ref, weight_ref, vec_ref, hs_ref,
    heads_ref, sums_ref
):
    normed, inv = row_norm(middle_ref[...])
    cot = cot_ref[...].astype(F32)
    grad_middle = cot + norm_back(grad_feed, vec_ref[7:8], normed, inv)
    sums_ref[7:8] += column_sum(grad_feed * normed)
    sums_ref[8:9] += column_sum(grad_feed)
    sums_ref[9:10] += column_sum(cot)
    normed, inv = row_norm(branch_ref[...])
    low = norm_back(grad_middle, vec_ref[5:6], normed, inv).astype(BF)
    sums_ref[5:6] += column_sum(grad_middle * normed)
    sums_ref[6:7] += column_sum(grad_middle)
    sums_ref[2:3] += column_sum(low.astype(F32))
    grad_scaled = dot_nt(low, weight_ref[...])
    grad_out = (grad_scaled * hs_ref[...]).astype(BF)
    product = grad_out.astype(F32) * attended_ref[...]
    high = product.astype(BF)
    rest = (product - high.astype(F32)).astype(BF)
    delta = dot_nn(high, heads_ref[...]) + dot_nn(rest, heads_ref[...])
    return grad_middle, low, grad_out, delta


def out_back_kernel(
    grad_feed_ref,
    cot_ref,
    middle_ref,
    branch_ref,
    scaled_ref,
    attended_ref,
    weight_ref,
    vec_ref,
    hs_ref,
    heads_ref,
    grad_middle_ref,
    ga_ref,
    out_grad_ref,
    delta_ref,
    sums_ref,
    total_ref,
):
    step = pl.program_id(0)

    @pl.when(step == 0)
    def _():
        total_ref[...] = jnp.zeros_like(total_ref)
        sums_ref[...] = jnp.zeros_like(sums_ref)

    scaled = scaled_ref[...]
    grad_middle_ref[...], low, ga_ref[...], delta = out_back_rows(
        grad_feed_ref[...], cot_ref, middle_ref, branch_ref, scaled, attended_ref, weight_ref,
        vec_ref, hs_ref, heads_ref, sums_ref
    )
    total_ref[...] += dot_tn(scaled, low)
    delta_ref[...] = delta.T[: delta_ref.shape[0]]

    @pl.when(step == pl.num_programs(0) - 1)
    def _():
        out_grad_ref[...] = total_ref[...].astype(BF)


def out_back(
    grad_feed, cotangent, middle, branch, scaled, attended, weights, vectors, head_lanes, heads_map
):
    rows, width = cotangent.shape
    heads = 2 * width // 128
    by_row = pl.BlockSpec((TILE, width), lambda i: (i, 0))
    return pl.pallas_call(
        out_back_kernel,
        grid=(rows // TILE,),
        in_specs=[
            by_row,
            by_row,
            by_row,
            by_row,
            by_row,
            by_row,
            whole((width, width)),
            whole(vectors.shape),
            whole((1, width)),
            whole(heads_map.shape),
        ],
        out_specs=[
            by_row,
            by_row,
            whole((width, width)),
            pl.BlockSpec((heads, TILE), lambda i: (0, i)),
            whole((16, width)),
        ],
        out_shape=[
            jax.ShapeDtypeStruct((rows, width), F32),
            jax.ShapeDtypeStruct((rows, width), BF),
            jax.ShapeDtypeStruct((width, width), BF),
            jax.ShapeDtypeStruct((heads, rows), F32),
            jax.ShapeDtypeStruct((16, width), F32),
        ],
        scratch_shapes=[pltpu.VMEM((width, width), F32)],
        compiler_params=params(),
        name="out_back",
    )(
        grad_feed,
        cotangent,
        middle,
        branch,
        scaled,
        attended,
        weights,
        vectors,
        head_lanes,
        heads_map,
    )


def attention_back_head(
    head, cross, q_ref, k_ref, v_ref, ga_ref, lse_ref, delta_ref, dq_ref, dk_ref, dv_ref
):
    rows = q_ref.shape[0]
    half = rows // 2
    factor = LOG2E * (q_ref.shape[1] // 2) ** (-0.5)
    low_lanes = lax.broadcasted_iota(jnp.int32, (1, 128), 1) < 64
    mine = low_lanes if head == 0 else ~low_lanes
    above = lax.broadcasted_iota(jnp.int32, (TILE, TILE), 0) <= lax.broadcasted_iota(
        jnp.int32, (TILE, TILE), 1
    )
    zero = jnp.zeros((rows, 128), BF)
    query = jnp.where(mine, q_ref[...], zero)
    grad = jnp.where(mine, ga_ref[...], zero)
    key_own = jnp.where(mine, k_ref[...], zero)
    for start in range(0, rows, TILE):
        stop = start + TILE
        raw = dot_nt(k_ref[start:stop], query[start:])
        level = lse_ref[0, head : head + 1, start:]
        parts = [jnp.where(above, raw[:, :TILE] * factor - level[:, :TILE], MASKED)]
        if start < half:
            if stop < half:
                parts.append(raw[:, TILE : half - start] * factor - level[:, TILE : half - start])
            parts.append(raw[:, half - start :] * factor - (level[:, half - start :] - cross))
        elif stop < rows:
            parts.append(raw[:, TILE:] * factor - level[:, TILE:])
        exponent = parts[0] if len(parts) == 1 else jnp.concatenate(parts, axis=1)
        weights = jnp.exp2(exponent)
        grad_weights = dot_nt(v_ref[start:stop], grad[start:])
        grad_scores = (weights * (grad_weights - delta_ref[:, start:])).astype(BF)
        dv = dot_nn(weights.astype(BF), grad[start:])
        dk = dot_nn(grad_scores, query[start:])
        dq = dot_tn(grad_scores, key_own[start:stop])
        if head == 0:
            dv_ref[start:stop] = dv
            dk_ref[start:stop] = dk
        else:
            dv_ref[start:stop] += dv
            dk_ref[start:stop] += dk
        if head == 0 and start == 0:
            dq_ref[...] = dq
        else:
            dq_ref[start:] += dq


def in_back_pair(dq_ref, dk_ref, dv_ref, weights, turned_ref, out_grad_ref, chunk_ref, total_ref):
    factor = 64 ** (-0.5)
    dq = (dq_ref[...] * factor).astype(BF)
    dk = (dk_ref[...] * factor).astype(BF)
    dv = dv_ref[...].astype(BF)
    grads = jnp.concatenate([dq, dk, dv], axis=1)
    for start in range(0, total_ref.shape[0], TILE):
        rows = pl.ds(start, TILE)
        total_ref[rows] += dot_nt(grads[start : start + TILE], weights)
        part = dot_nn(turned_ref[rows], grads).astype(BF)
        part = jnp.concatenate([part, out_grad_ref[rows]], axis=1)
        chunk_ref[:, start // TILE] = part.reshape(8, 32, 512)
    return column_sum(dq.astype(F32)), column_sum(dv.astype(F32))


def tokens_back(tokens, grad, grad_middle, gain):
    normed, inv = row_norm(tokens.astype(F32))
    back = norm_back(grad, gain, normed, inv)
    return (grad_middle + back).astype(BF), column_sum(grad * normed), column_sum(grad)


def in_back_kernel(
    cross_ref,
    proj_ref,
    ga_ref,
    lse_ref,
    delta_ref,
    wq_ref,
    wk_ref,
    wv_ref,
    first_ref,
    out_grad_ref,
    tokens_ref,
    gain_ref,
    grad_middle_ref,
    chunk_ref,
    bias_ref,
    tokens_grad_ref,
    sums_ref,
    dq_ref,
    dk_ref,
    dv_ref,
    turned_ref,
    total_ref,
):
    step = pl.program_id(0)
    q_ref, k_ref, v_ref = three(proj_ref)
    rows_all = tokens_ref.shape[0]

    @pl.when(step == 0)
    def _():
        turned_ref[...] = first_ref[...].T
        total_ref[...] = jnp.zeros_like(total_ref)

    for head in range(2):
        attention_back_head(
            head,
            cross_ref[0, 0],
            q_ref,
            k_ref,
            v_ref,
            ga_ref,
            lse_ref,
            delta_ref.at[0, pl.ds(head, 1)],
            dq_ref,
            dk_ref,
            dv_ref,
        )
    weights = jnp.concatenate([wq_ref[...], wk_ref[...], wv_ref[...]], axis=1)
    query_sum, value_sum = in_back_pair(
        dq_ref, dk_ref, dv_ref, weights, turned_ref, out_grad_ref, chunk_ref.at[0], total_ref
    )
    bias_ref[0, 0:1] = query_sum
    bias_ref[0, 1:2] = value_sum

    @pl.when(step == pl.num_programs(0) - 1)
    def _():
        gain_grad = jnp.zeros((1, total_ref.shape[1]), F32)
        shift_grad = jnp.zeros((1, total_ref.shape[1]), F32)
        for start in range(0, rows_all, TILE):
            rows = pl.ds(start, TILE)
            tokens_grad_ref[rows], gain_part, shift_part = tokens_back(
                tokens_ref[rows], total_ref[rows], grad_middle_ref[rows], gain_ref[...]
            )
            gain_grad = gain_grad + gain_part
            shift_grad = shift_grad + shift_part
        sums_ref[0:1] = gain_grad
        sums_ref[1:2] = shift_grad


def in_back(cross, projected, ga, lse, delta, weights, first, out_grad, tokens, gain, grad_middle):
    rows, width = tokens.shape
    pairs = width // 128
    column = pl.BlockSpec((rows, 128), lambda p: (0, p))
    square = whole((rows, width))
    return pl.pallas_call(
        in_back_kernel,
        grid=(pairs,),
        in_specs=[
            pl.BlockSpec(memory_space=pltpu.SMEM),
            pl.BlockSpec((1, rows, 384), lambda p: (p, 0, 0)),
            column,
            pl.BlockSpec((1, 8, rows), lambda p: (p, 0, 0)),
            pl.BlockSpec((1, 2, rows), lambda p: (p, 0, 0)),
            pl.BlockSpec((width, 128), lambda p: (0, p)),
            pl.BlockSpec((width, 128), lambda p: (0, pairs + p)),
            pl.BlockSpec((width, 128), lambda p: (0, 2 * pairs + p)),
            square,
            column,
            square,
            whole((1, width)),
            square,
        ],
        out_specs=[
            pl.BlockSpec((1, 8, width // TILE, 32, 512), lambda p: (p, 0, 0, 0, 0)),
            pl.BlockSpec((1, 8, 128), lambda p: (p, 0, 0)),
            square,
            whole((8, width)),
        ],
        out_shape=[
            jax.ShapeDtypeStruct((pairs, 8, width // TILE, 32, 512), BF),
            jax.ShapeDtypeStruct((pairs, 8, 128), F32),
            jax.ShapeDtypeStruct((rows, width), BF),
            jax.ShapeDtypeStruct((8, width), F32),
        ],
        scratch_shapes=[
            pltpu.VMEM((rows, 128), F32),
            pltpu.VMEM((rows, 128), F32),
            pltpu.VMEM((rows, 128), F32),
            pltpu.VMEM((width, rows), BF),
            pltpu.VMEM((rows, width), F32),
        ],
        compiler_params=params(),
        name="in_back",
    )(
        cross,
        projected,
        ga,
        lse,
        delta,
        weights,
        weights,
        weights,
        first,
        out_grad,
        tokens,
        gain,
        grad_middle,
    )


class Place:
    def __init__(self):
        self.z = lax.axis_index("dp")
        wide = lax.axis_index("wide")
        self.y = wide // 4
        self.x = (wide // 2) % 2
        self.c = wide % 2
        self.core = (self.z, wide + 1 - 2 * self.c)
        self.side = (self.z, wide + 2 - 4 * self.x)
        self.over = (self.z, wide + 4 - 8 * self.y)
        self.ranks = (self.z + 1 - 2 * (self.z % 2), (self.z + 2) % 4, 3 - self.z)
        self.planes = tuple((rank, wide) for rank in self.ranks)

    def greet(self, planes=True):
        barrier = pltpu.get_barrier_semaphore()
        peers = (self.core, self.side, self.over) + (self.planes if planes else ())
        for peer in peers:
            pl.semaphore_signal(barrier, inc=1, device_id=peer, device_id_type=MESH)
        pl.semaphore_wait(barrier, len(peers))


class WideGather:
    copies = 13

    def __init__(self, place, source, target, send, recv, first, last):
        rows = target.shape[-2]
        y, x, c = place.y, place.x, place.c
        here, side, over, far = (y, x, c), (y, 1 - x, c), (1 - y, x, c), (1 - y, 1 - x, c)
        upper, lower, both = pl.ds(0, rows // 2), pl.ds(rows // 2, rows // 2), pl.ds(0, rows)

        def copy(index, slot, part, peer):
            destination = target.at[(*slot, part)]
            return pltpu.make_async_remote_copy(
                src_ref=source.at[part] if source is not None and slot is here else destination,
                dst_ref=destination,
                send_sem=send.at[first + index],
                recv_sem=recv.at[first + index],
                device_id=peer,
                device_id_type=MESH,
            )

        self.all = (
            copy(0, here, upper, place.side),
            copy(1, here, lower, place.over),
            copy(2, here, upper, place.over),
            copy(3, here, lower, place.side),
            copy(4, here, both, place.core),
            copy(5, side, upper, place.over),
            copy(6, side, upper, place.core),
            copy(7, over, lower, place.side),
            copy(8, over, lower, place.core),
            copy(9, side, lower, place.core),
            copy(10, over, upper, place.core),
            copy(11, far, upper, place.core),
            copy(12, far, lower, place.core),
        )
        self.own = None
        if source is not None:
            self.own = pltpu.make_async_copy(source, target.at[here], last)

    def start(self):
        if self.own is not None:
            self.own.start()
        for index in range(5):
            self.all[index].start()

    def relay(self, stage):
        waits, starts = (((0, 1), (5, 7, 6, 8)), ((2, 3), (9, 10)), ((5, 7), (11, 12)))[stage]
        for index in waits:
            self.all[index].wait_recv()
        for index in starts:
            self.all[index].start()

    def finish(self):
        for index in (4, 6, 8, 9, 10, 11, 12):
            self.all[index].wait_recv()
        for copy in self.all:
            copy.wait_send()
        if self.own is not None:
            self.own.wait()


LAG = 2


class Reduction:
    slots = 2 * LAG
    keep = 2 * LAG + 2

    @classmethod
    def scratch(cls):
        n, k = cls.slots, cls.keep
        return [
            pltpu.VMEM((3 * LAG, 2, 2, 4, 32, 512), BF),
            pltpu.VMEM((n, 2, 2, 4, 32, 512), BF),
            pltpu.VMEM((n, 2, 4, 16, 512), BF),
            pltpu.VMEM((n, 2, 4, 16, 512), BF),
            pltpu.VMEM((n, 4, 16, 512), BF),
            pltpu.VMEM((n, 4, 16, 512), BF),
            pltpu.VMEM((n, 4, 32, 512), BF),
            pltpu.VMEM((n, 3, 32, 512), BF),
            pltpu.VMEM((n, 32, 512), BF),
            pltpu.VMEM((k, 3, 32, 512), BF),
            pltpu.SemaphoreType.DMA((11, k)),
            pltpu.SemaphoreType.DMA((11, k)),
            pltpu.SemaphoreType.DMA((3 * LAG,)),
        ]

    def __init__(self, place, refs):
        self.place = place
        (
            self.chip,
            self.partner,
            self.from_x,
            self.from_y,
            self.then_y,
            self.then_x,
            self.plane,
            self.from_z,
            self.sums,
            self.shared,
            self.send,
            self.recv,
            self.local,
        ) = refs

    def copy(self, index, slot, source, target, peer):
        return pltpu.make_async_remote_copy(
            src_ref=source,
            dst_ref=target,
            send_sem=self.send.at[index, slot],
            recv_sem=self.recv.at[index, slot],
            device_id=peer,
            device_id_type=MESH,
        )

    def to_core(self, slot, source):
        return self.copy(0, slot, source, self.partner.at[slot], self.place.core)

    def load(self, chunk, source):
        slot = chunk % (3 * LAG)
        return pltpu.make_async_copy(source, self.chip.at[slot], self.local.at[slot])

    def first_hop(self, chunk):
        p, slot, chip = self.place, chunk % self.slots, self.chip.at[chunk % (3 * LAG)]
        return (
            self.copy(1, slot, chip.at[:, 1 - p.x, :, pl.ds(0, 16)], self.from_x.at[slot], p.side),
            self.copy(2, slot, chip.at[1 - p.y, :, :, pl.ds(16, 16)], self.from_y.at[slot], p.over),
        )

    def second_hop(self, chunk):
        p, slot, chip = self.place, chunk % self.slots, self.chip.at[chunk % (3 * LAG)]
        return (
            self.copy(
                3, slot, chip.at[1 - p.y, p.x, :, pl.ds(0, 16)], self.then_y.at[slot], p.over
            ),
            self.copy(
                4, slot, chip.at[p.y, 1 - p.x, :, pl.ds(16, 16)], self.then_x.at[slot], p.side
            ),
        )

    def to_planes(self, slot):
        p = self.place
        return [
            self.copy(
                5 + k, slot, self.plane.at[slot, p.ranks[k]], self.from_z.at[slot, k], p.planes[k]
            )
            for k in range(3)
        ]

    def share(self, slot, place):
        p = self.place
        return [
            self.copy(
                8 + k, place, self.sums.at[slot], self.shared.at[place, k], p.planes[k]
            )
            for k in range(3)
        ]

    def stage0(self, chunk, view):
        slot, c = chunk % self.slots, self.place.c
        self.to_core(slot, view.at[:, :, 1 - c]).start()
        self.load(chunk, view.at[:, :, c]).start()

    def stage1(self, chunk):
        slot, index = chunk % self.slots, chunk % (3 * LAG)
        self.load(chunk, self.partner.at[slot]).wait()
        self.to_core(slot, self.chip.at[index]).wait()
        self.chip[index] += self.partner[slot]
        for copy in self.first_hop(chunk):
            copy.start()

    def stage2(self, chunk):
        p, slot, index = self.place, chunk % self.slots, chunk % (3 * LAG)
        for copy in self.first_hop(chunk):
            copy.wait()
        for k in range(2):
            self.chip[index, k, p.x, :, 0:16] += self.from_x[slot, k]
            self.chip[index, p.y, k, :, 16:32] += self.from_y[slot, k]
        for copy in self.second_hop(chunk):
            copy.start()

    def stage3(self, chunk):
        p, slot = self.place, chunk % self.slots
        for copy in self.second_hop(chunk):
            copy.wait()
        mine = self.chip.at[chunk % (3 * LAG), p.y, p.x]
        self.plane[slot, :, 0:16] = mine[:, 0:16] + self.then_y[slot]
        self.plane[slot, :, 16:32] = mine[:, 16:32] + self.then_x[slot]
        for copy in self.to_planes(slot):
            copy.start()

    def stage4(self, chunk):
        slot = chunk % self.slots
        for copy in self.to_planes(slot):
            copy.wait()
        total = self.plane[slot, self.place.z].astype(F32)
        for k in range(3):
            total = total + self.from_z[slot, k].astype(F32)
        return total

    def spread(self, chunk, total):
        slot, place = chunk % self.slots, chunk % self.keep
        self.sums[slot] = total.astype(BF)
        for copy in self.share(slot, place):
            copy.start()

    def stage5(self, chunk):
        slot, place = chunk % self.slots, chunk % self.keep
        for copy in self.share(slot, place):
            copy.wait()
        blocks = [(self.place.z, self.sums[slot])]
        return blocks + [(self.place.ranks[k], self.shared[place, k]) for k in range(3)]


def dma_sems(count):
    return [pltpu.SemaphoreType.DMA((count,)), pltpu.SemaphoreType.DMA((count,))]


class FullGather:
    copies = 3 + 4 * WideGather.copies

    def __init__(self, place, source, target, send, recv, first, last):
        own = (place.y, place.x, place.c)
        mine = target.at[(place.z, *own)]
        self.across = [
            pltpu.make_async_remote_copy(
                src_ref=source if source is not None else mine,
                dst_ref=mine,
                send_sem=send.at[first + index],
                recv_sem=recv.at[first + index],
                device_id=peer,
                device_id_type=MESH,
            )
            for index, peer in enumerate(place.planes)
        ]
        self.parts = [
            WideGather(
                place,
                source if index == 0 else None,
                target.at[rank],
                send,
                recv,
                first + 3 + index * WideGather.copies,
                last,
            )
            for index, rank in enumerate((place.z, *place.ranks))
        ]

    def start(self):
        for copy in self.across:
            copy.start()
        self.parts[0].start()

    def spread(self):
        for index in range(3):
            self.across[index].wait_recv()
            self.parts[index + 1].start()

    def relay(self, stage):
        for part in self.parts:
            part.relay(stage)

    def finish(self):
        for copy in self.across:
            copy.wait_send()
        for part in self.parts:
            part.finish()


def first_kernel(
    cross_ref,
    tokens_ref,
    in_ref,
    vec_ref,
    out_ref,
    up_ref,
    unit_ref,
    hs_ref,
    turned_ref,
    proj_ref,
    scaled_ref,
    attended_ref,
    lse_ref,
    vectors_ref,
    in_all,
    out_all,
    up_all,
    unit_all,
    held_ref,
    normed_ref,
    first_ref,
    vext_ref,
    send_in,
    recv_in,
    send_out,
    recv_out,
    send_ff,
    recv_ff,
    local,
):
    step = pl.program_id(0)
    place = Place()
    width = tokens_ref.shape[1]
    count = WideGather.copies
    into = FullGather(place, None, held_ref, send_in, recv_in, 0, None)
    out = FullGather(place, out_ref, out_all, send_out, recv_out, 0, local.at[2])
    up = WideGather(place, up_ref, up_all, send_ff, recv_ff, 0, local.at[3])
    unit = WideGather(place, unit_ref, unit_all, send_ff, recv_ff, count, local.at[4])
    keep = pltpu.make_async_copy(held_ref, in_all, local.at[5])

    @pl.when(step == 0)
    def _():
        place.greet()
        mine = held_ref.at[place.z, place.y, place.x, place.c]
        fills = (
            pltpu.make_async_copy(in_ref, mine.at[:, pl.ds(0, 3 * width)], local.at[0]),
            pltpu.make_async_copy(vec_ref, mine.at[:, pl.ds(3 * width, 128)], local.at[1]),
        )
        for copy in fills:
            copy.start()
        for copy in fills:
            copy.wait()
        into.start()
        for start in range(0, tokens_ref.shape[0], TILE):
            rows = pl.ds(start, TILE)
            normed, _ = row_norm(tokens_ref[rows].astype(F32))
            normed_ref[rows] = normed
        for index in range(3):
            into.parts[index].relay(0)
            into.across[index].wait_recv()
            into.parts[index + 1].start()
            into.parts[index].relay(1)
            into.parts[index].relay(2)
        for stage in range(3):
            into.parts[3].relay(stage)
        out.start()
        unit.start()
        up.start()
        into.finish()
        keep.start()
        for z in range(4):
            for y in range(2):
                tile = jnp.zeros((16, 128), F32)
                for x in range(2):
                    for c in range(2):
                        piece = held_ref[z, y, x, c, 0:16, 3 * width : 3 * width + 128].astype(F32)
                        spot = 32 * (2 * x + c)
                        tile = tile + (piece if spot == 0 else pltpu.roll(piece, spot, 1))
                vectors_ref[:, (2 * z + y) * 128 : (2 * z + y + 1) * 128] = tile
        for start in range(0, tokens_ref.shape[0], TILE):
            rows = pl.ds(start, TILE)
            first_ref[rows] = (normed_ref[rows] * vectors_ref[3:4] + vectors_ref[4:5]).astype(BF)

    @pl.when(step == 1)
    def _():
        out.spread()

    @pl.when((step >= 2) & (step <= 4))
    def _():
        for stage in range(3):

            @pl.when(step == 2 + stage)
            def _():
                out.relay(stage)
                unit.relay(stage)

    for stage, at in enumerate((3, 5, 8)):

        @pl.when(step == at)
        def _():
            up.relay(stage)

    @pl.when(step > 0)
    def _():
        pair = step - 1
        columns = [pl.ds(pl.multiple_of(part * width + pair * 128, 128), 128) for part in range(3)]
        weights = jnp.concatenate(
            [held_ref[:, :, :, :, :, cols].reshape(width, 128) for cols in columns], axis=1
        )
        own = pl.ds(pl.multiple_of(pair * 128, 128), 128)
        bias = jnp.concatenate(
            [vectors_ref[0:1, own], jnp.zeros((1, 128), F32), vectors_ref[1:2, own]], axis=1
        )
        project_pair(first_ref, weights, bias, proj_ref)
        attention_pair(
            cross_ref[0, 0], *three(proj_ref), hs_ref, scaled_ref, attended_ref, lse_ref, vext_ref
        )

    @pl.when(step == pl.num_programs(0) - 1)
    def _():
        turned_ref[...] = first_ref[...].T
        keep.wait()
        out.finish()
        unit.finish()
        up.finish()


def first_part(cross, tokens, in_weight, vec, out_weight, up_weight, unit_rows, head_lanes):
    rows, width = tokens.shape
    pairs = width // 128

    def at(step):
        return jnp.maximum(step - 1, 0)

    column = pl.BlockSpec((rows, 128), lambda s: (0, at(s)))
    held = (4, 2, 2, 2, 32, 3 * width + 128)
    return pl.pallas_call(
        first_kernel,
        grid=(pairs + 1,),
        in_specs=[
            pl.BlockSpec(memory_space=pltpu.SMEM),
            whole((rows, width)),
            ANY,
            ANY,
            ANY,
            ANY,
            ANY,
            pl.BlockSpec((1, 128), lambda s: (0, at(s))),
        ],
        out_specs=[
            whole((width, rows)),
            pl.BlockSpec((1, rows, 384), lambda s: (at(s), 0, 0)),
            column,
            column,
            pl.BlockSpec((1, 8, rows), lambda s: (at(s), 0, 0)),
            whole((16, width)),
            ANY,
            ANY,
            ANY,
            ANY,
        ],
        out_shape=[
            jax.ShapeDtypeStruct((width, rows), BF),
            jax.ShapeDtypeStruct((pairs, rows, 384), BF),
            jax.ShapeDtypeStruct((rows, width), BF),
            jax.ShapeDtypeStruct((rows, width), F32),
            jax.ShapeDtypeStruct((pairs, 8, rows), F32),
            jax.ShapeDtypeStruct((16, width), F32),
            jax.ShapeDtypeStruct(held, BF),
            jax.ShapeDtypeStruct((4, 2, 2, 2, *out_weight.shape), BF),
            jax.ShapeDtypeStruct((2, 2, 2, *up_weight.shape), BF),
            jax.ShapeDtypeStruct((2, 2, 2, *unit_rows.shape), BF),
        ],
        scratch_shapes=[
            pltpu.VMEM(held, BF),
            pltpu.VMEM((rows, width), F32),
            pltpu.VMEM((rows, width), BF),
            pltpu.VMEM((rows, 256), BF),
            *dma_sems(FullGather.copies),
            *dma_sems(FullGather.copies),
            *dma_sems(2 * WideGather.copies),
            pltpu.SemaphoreType.DMA((6,)),
        ],
        compiler_params=params(collective_id=0, has_side_effects=True),
        name="first_part",
    )(cross, tokens, in_weight, vec, out_weight, up_weight, unit_rows, head_lanes)


def second_kernel(
    units,
    scaled_ref,
    weight_ref,
    vec_ref,
    tokens_ref,
    up_ref,
    unit_ref,
    down_ref,
    branch_ref,
    middle_ref,
    turned_ref,
    act_ref,
    slope_ref,
    stats_ref,
    down_all,
    feed_ref,
    sums_ref,
    send,
    recv,
    local,
):
    step = pl.program_id(0)
    lead = feed_ref.shape[0] // TILE
    place = Place()
    down = WideGather(place, down_ref, down_all, send, recv, 0, local.at[0])

    @pl.when(step == 0)
    def _():
        place.greet(planes=False)
        down.start()
        sums_ref[...] = jnp.zeros_like(sums_ref)

    for stage, at in enumerate((5, 8, 11)):

        @pl.when(step == at)
        def _():
            down.relay(stage)

    @pl.when(step < lead)
    def _():
        rows = pl.ds(pl.multiple_of(step * TILE, TILE), TILE)
        feed_ref[rows] = out_proj_rows(
            scaled_ref, weight_ref, vec_ref, tokens_ref, branch_ref, middle_ref
        )

    @pl.when(step >= lead)
    def _():
        up_step(feed_ref, up_ref, unit_ref, act_ref, slope_ref, sums_ref)

    @pl.when(step == pl.num_programs(0) - 1)
    def _():
        up_stats(units, stats_ref, sums_ref)
        turned_ref[...] = feed_ref[...].T
        down.finish()


def second_part(scaled, out_weights, vectors, tokens, up, unit_vec, down_weight):
    rows, width = tokens.shape
    steps = up.shape[0]
    lead = rows // TILE

    def early(step):
        return jnp.minimum(step, lead - 1)

    def late(step):
        return jnp.maximum(step - lead, 0)

    by_row = pl.BlockSpec((TILE, width), lambda s: (early(s), 0))
    block = pl.BlockSpec((1, rows, UNITS), lambda s: (late(s), 0, 0))
    return pl.pallas_call(
        functools.partial(second_kernel, steps * UNITS),
        grid=(lead + steps,),
        in_specs=[
            by_row,
            whole((width, width)),
            whole(vectors.shape),
            by_row,
            pl.BlockSpec((1, width, UNITS), lambda s: (late(s), 0, 0)),
            pl.BlockSpec((1, unit_vec.shape[1], UNITS), lambda s: (late(s), 0, 0)),
            ANY,
        ],
        out_specs=[
            by_row,
            by_row,
            whole((width, rows)),
            block,
            block,
            whole((rows, 128)),
            ANY,
        ],
        out_shape=[
            jax.ShapeDtypeStruct((rows, width), F32),
            jax.ShapeDtypeStruct((rows, width), F32),
            jax.ShapeDtypeStruct((width, rows), BF),
            jax.ShapeDtypeStruct((steps, rows, UNITS), BF),
            jax.ShapeDtypeStruct((steps, rows, UNITS), BF),
            jax.ShapeDtypeStruct((rows, 128), F32),
            jax.ShapeDtypeStruct((2, 2, 2, *down_weight.shape), BF),
        ],
        scratch_shapes=[
            pltpu.VMEM((rows, width), BF),
            pltpu.VMEM((2, rows, 128), F32),
            *dma_sems(WideGather.copies),
            pltpu.SemaphoreType.DMA((1,)),
        ],
        compiler_params=params(collective_id=2, has_side_effects=True),
        name="second_part",
    )(scaled, out_weights, vectors, tokens, up, unit_vec, down_weight)


FEED_AT, OUT_AT, HEADS_AT, TOKENS_AT = 0, 8, 16, 32
LAST_CHUNK_AT = 36
BACK_STEPS = LAST_CHUNK_AT + 4 * LAG + 1
OUT_TILE = 128


def chunk_at(time):
    even = time % 2 == 0
    chunk = jnp.where(time < 8, time, (time + 8) // 2)
    chunk = jnp.where(time >= 16, time - 4, chunk)
    chunk = jnp.where(time >= 22, (time + 14) // 2, chunk)
    chunk = jnp.where(time == LAST_CHUNK_AT, 24, chunk)
    there = (time >= 0) & ((time < 8) | ((time >= 16) & (time < 22)) | (even & (time < 33)))
    return chunk, there | (time == LAST_CHUNK_AT)


def back_kernel(
    cross_ref,
    act_ref,
    slope_ref,
    e_ref,
    stats_ref,
    up_ref,
    feed_turned_ref,
    unit_grad_ref,
    down_grad_all,
    cot_ref,
    middle_ref,
    branch_ref,
    scaled_ref,
    attended_ref,
    out_weight_ref,
    vec_ref,
    hs_ref,
    hs_row_ref,
    heads_ref,
    proj_ref,
    lse_ref,
    wq_ref,
    wk_ref,
    wv_ref,
    turned_ref,
    tokens_ref,
    tokens_grad_ref,
    down_out,
    up_out,
    attn_out,
    up_grad_all,
    staged_ref,
    total_ref,
    low_ref,
    out_grad_ref,
    ga_ref,
    grad_middle_ref,
    delta_ref,
    delta_sum_ref,
    sums_ref,
    units_ref,
    dq_ref,
    dk_ref,
    dv_ref,
    chunk_ref,
    store_sems,
    *scratch,
):
    step = pl.program_id(0)
    place = Place()
    engine = Reduction(place, scratch)

    @pl.when(step == 0)
    def _():
        place.greet()
        total_ref[...] = jnp.zeros_like(total_ref)
        sums_ref[...] = jnp.zeros_like(sums_ref)
        units_ref[...] = jnp.zeros_like(units_ref)
        delta_sum_ref[...] = jnp.zeros_like(delta_sum_ref)

    def store(block):
        view = up_grad_all.at[block // 4, block // 2 % 2, block % 2]
        return pltpu.make_async_copy(staged_ref, view, store_sems.at[0])

    @pl.when((step >= 1) & (step <= OUT_AT))
    def _():
        store(step - 1).wait()


    def stage(number, kind, action):
        chunk, there = chunk_at(step - number * LAG)
        up = ((chunk >= 8) & (chunk < 14)) | (chunk == 15) | (chunk == 17)
        wanted = {"all": there, "down": there & (chunk < 8), "up": there & up}
        wanted["shared"] = there & ((chunk < 8) | up)
        wanted["own"] = there & (chunk >= 8) & ~up

        @pl.when(wanted[kind])
        def _():
            action(chunk)

    def up_index(chunk):
        return jnp.where(chunk < 14, chunk - 8, (chunk - 3) // 2)

    def attn_index(chunk):
        return jnp.where(chunk < 18, (chunk - 14) // 2, chunk - 16)

    def put_down(chunk):
        for rank, block in engine.stage5(chunk):
            for half in range(2):

                @pl.when(chunk % 2 == half)
                def _():
                    down_out[chunk // 2, rank, :, half * 512 : half * 512 + 512] = block

    def put_up(chunk):
        for rank, block in engine.stage5(chunk):
            up_out[up_index(chunk), rank] = block

    def put_own(chunk):
        attn_out[attn_index(chunk)] = engine.stage4(chunk)

    def take_down(chunk):
        lanes = pl.ds(pl.multiple_of(chunk % 2 * 512, 512), 512)
        engine.stage0(chunk, down_grad_all.at[:, :, :, chunk // 2, :, :, lanes])

    def take_up(chunk):
        engine.stage0(chunk, up_grad_all.at[:, :, :, up_index(chunk)])

    def take_own(chunk):
        engine.stage0(chunk, chunk_ref.at[attn_index(chunk) % 2])

    stage(5, "down", put_down)
    stage(5, "up", put_up)
    stage(4, "shared", lambda chunk: engine.spread(chunk, engine.stage4(chunk)))
    stage(4, "own", put_own)
    stage(3, "all", engine.stage3)
    stage(2, "all", engine.stage2)
    stage(1, "all", engine.stage1)
    stage(0, "down", take_down)
    stage(0, "up", take_up)


    @pl.when(step < OUT_AT)
    def _():
        units_ref[step, 0:1] = up_back_step(
            act_ref.at[0],
            slope_ref.at[0],
            e_ref.at[0],
            stats_ref,
            up_ref.at[0],
            low_ref,
            total_ref,
        )
        units_ref[step, 1:3] = unit_grad_ref[step, 0:2]
        for start in range(0, total_ref.shape[1], TILE):
            grad = dot_nn(feed_turned_ref[start : start + TILE], low_ref[:, 0:UNITS]).astype(BF)
            staged_ref[start // 128 : (start + TILE) // 128] = grad.reshape(
                TILE // 128, 4, 32, UNITS
            )
        store(step).start()


    @pl.when((step >= OUT_AT) & (step < HEADS_AT))
    def _():
        block = step - OUT_AT
        rows = pl.ds(pl.multiple_of(block * OUT_TILE, OUT_TILE), OUT_TILE)
        grad_middle, low, grad_out, delta = out_back_rows(
            total_ref[rows],
            cot_ref,
            middle_ref,
            branch_ref,
            None,
            attended_ref,
            out_weight_ref,
            vec_ref,
            hs_ref,
            heads_ref,
            sums_ref,
        )
        grad_middle_ref[rows] = grad_middle
        low_ref[rows] = low
        ga_ref[rows] = grad_out
        delta_sum_ref[0:1] += column_sum(delta)
        turned = delta.T
        for head in range(delta_ref.shape[0]):
            delta_ref[head, :, rows] = turned[head : head + 1]

    @pl.when(step == HEADS_AT - 1)
    def _():
        for start in range(0, out_grad_ref.shape[0], TILE):
            part = dot_tn(scaled_ref[:, start : start + TILE], low_ref[...])
            out_grad_ref[start : start + TILE] = part.astype(BF)
        total_ref[...] = jnp.zeros_like(total_ref)


    @pl.when((step >= HEADS_AT) & (step < TOKENS_AT))
    def _():
        index = step - HEADS_AT
        pair = index // 2
        columns = pl.ds(pl.multiple_of(pair * 128, 128), 128)
        for head in range(2):

            @pl.when(index % 2 == head)
            def _():
                attention_back_head(
                    head,
                    cross_ref[0, 0],
                    *three(proj_ref),
                    ga_ref.at[:, columns],
                    lse_ref,
                    delta_ref.at[index],
                    dq_ref,
                    dk_ref,
                    dv_ref,
                )

        @pl.when(index % 2 == 1)
        def _():
            weights = jnp.concatenate([wq_ref[...], wk_ref[...], wv_ref[...]], axis=1)
            query_sum, value_sum = in_back_pair(
                dq_ref,
                dk_ref,
                dv_ref,
                weights,
                turned_ref,
                out_grad_ref.at[:, columns],
                chunk_ref.at[pair % 2].reshape(8, 4, 32, 512),
                total_ref,
            )
            sums_ref[0:1, columns] = query_sum
            sums_ref[1:2, columns] = value_sum

    @pl.when((step >= TOKENS_AT) & (step < TOKENS_AT + 4))
    def _():
        rows = pl.ds(pl.multiple_of((step - TOKENS_AT) * TILE, TILE), TILE)
        tokens_grad_ref[...], gain_grad, shift_grad = tokens_back(
            tokens_ref[...], total_ref[rows], grad_middle_ref[rows], vec_ref[3:4]
        )
        sums_ref[3:4] += gain_grad
        sums_ref[4:5] += shift_grad

    @pl.when(step == LAST_CHUNK_AT)
    def _():
        scale_grad = delta_sum_ref[0:1] / hs_row_ref[...]
        for y in range(2):
            for x in range(2):
                for c in range(2):
                    unit = 4 * y + 2 * x + c
                    units_ref[unit, 3:4] = sums_ref[9:10, 0:UNITS]
                    units_ref[unit, 4:5] = sums_ref[9:10, UNITS : 2 * UNITS]
                    units_ref[unit, 5:6, 0:128] = scale_grad
                    top = units_ref[unit].astype(BF)
                    for z in range(4):
                        start = (2 * z + y) * 128
                        chunk_ref[0, y, x, c, z, 0:16] = top
                        chunk_ref[0, y, x, c, z, 16:32, 0:128] = sums_ref[
                            :, start : start + 128
                        ].astype(BF)

    stage(0, "own", take_own)


def back_part(
    cross,
    act,
    slope,
    e,
    stats,
    up,
    feed_turned,
    unit_grad,
    down_grad,
    cotangent,
    middle,
    branch,
    scaled,
    attended,
    out_weights,
    vectors,
    head_lanes,
    head_row,
    heads_map,
    projected,
    lse,
    weights,
    turned,
    tokens,
):
    rows, width = tokens.shape
    pairs = width // 128

    def clamp(value, high):
        return jnp.minimum(jnp.maximum(value, 0), high)

    def unit(s):
        return clamp(s, 7)

    def pair(s):
        return clamp((s - HEADS_AT) // 2, pairs - 1)

    def tail(s):
        return clamp(s - TOKENS_AT, 3)

    block = pl.BlockSpec((1, rows, UNITS), lambda s: (unit(s), 0, 0))
    narrow = whole((rows, 128))
    by_row = pl.BlockSpec((OUT_TILE, width), lambda s: (clamp(s - OUT_AT, 7), 0))
    square = whole((width, width))
    return pl.pallas_call(
        back_kernel,
        grid=(BACK_STEPS,),
        in_specs=[
            pl.BlockSpec(memory_space=pltpu.SMEM),
            block,
            block,
            block,
            narrow,
            pl.BlockSpec((1, width, UNITS), lambda s: (unit(s), 0, 0)),
            square,
            whole(unit_grad.shape),
            ANY,
            by_row,
            by_row,
            by_row,
            square,
            by_row,
            square,
            whole(vectors.shape),
            whole((1, width)),
            whole((1, 128)),
            whole(heads_map.shape),
            pl.BlockSpec((1, rows, 384), lambda s: (pair(s), 0, 0)),
            pl.BlockSpec((1, 8, rows), lambda s: (pair(s), 0, 0)),
            pl.BlockSpec((width, 128), lambda s: (0, pair(s))),
            pl.BlockSpec((width, 128), lambda s: (0, pairs + pair(s))),
            pl.BlockSpec((width, 128), lambda s: (0, 2 * pairs + pair(s))),
            square,
            pl.BlockSpec((TILE, width), lambda s: (tail(s), 0)),
        ],
        out_specs=[
            pl.BlockSpec((TILE, width), lambda s: (tail(s), 0)),
            whole((4, 4, 32, 1024)),
            whole((8, 4, 32, 512)),
            whole((9, 32, 512)),
            ANY,
        ],
        out_shape=[
            jax.ShapeDtypeStruct((rows, width), BF),
            jax.ShapeDtypeStruct((4, 4, 32, 1024), BF),
            jax.ShapeDtypeStruct((8, 4, 32, 512), BF),
            jax.ShapeDtypeStruct((9, 32, 512), F32),
            jax.ShapeDtypeStruct((2, 2, 2, 8, 4, 32, UNITS), BF),
        ],
        scratch_shapes=[
            pltpu.VMEM((8, 4, 32, UNITS), BF),
            pltpu.VMEM((rows, width), F32),
            pltpu.VMEM((rows, width), BF),
            pltpu.VMEM((width, width), BF),
            pltpu.VMEM((rows, width), BF),
            pltpu.VMEM((rows, width), F32),
            pltpu.VMEM((2 * pairs, 1, rows), F32),
            pltpu.VMEM((8, 128), F32),
            pltpu.VMEM((16, width), F32),
            pltpu.VMEM((8, 16, UNITS), F32),
            pltpu.VMEM((rows, 128), F32),
            pltpu.VMEM((rows, 128), F32),
            pltpu.VMEM((rows, 128), F32),
            pltpu.VMEM((2, 2, 2, 2, 4, 32, 512), BF),
            pltpu.SemaphoreType.DMA((1,)),
            *Reduction.scratch(),
        ],
        compiler_params=params(collective_id=1, has_side_effects=True),
        name="back_part",
    )(
        cross,
        act,
        slope,
        e,
        stats,
        up,
        feed_turned,
        unit_grad,
        down_grad.reshape(2, 2, 2, 4, 4, 32, width),
        cotangent,
        middle,
        branch,
        scaled,
        attended,
        out_weights,
        vectors,
        head_lanes,
        head_row,
        heads_map,
        projected,
        lse,
        weights,
        weights,
        weights,
        turned,
        tokens,
    )


def layer(staged, tokens, cotangent, lengths, attn, up, down, unit_vec, head_scale, down_bias):
    rows, width = tokens.shape
    heads = head_scale.shape[0]
    pairs = width // 128
    cross = jnp.where(lengths[0:1, 0:1] == rows, 0.0, MASKED).astype(F32)
    scale = head_scale.astype(F32)
    head_lanes = jnp.repeat(scale, width // heads)[None, :]
    heads_map = (
        lax.broadcasted_iota(jnp.int32, (width, 128), 0) // (width // heads)
        == lax.broadcasted_iota(jnp.int32, (width, 128), 1)
    ).astype(BF)
    if staged:
        in_weight, out_weight, vec_block = attn
        (turned, projected, scaled, attended, lse, vectors, weights, out_weights, up, unit_vec) = (
            first_part(cross, tokens, in_weight, vec_block, out_weight, up, unit_vec, head_lanes)
        )
        weights = weights.reshape(width, 3 * width + 128)
        out_weights = out_weights.reshape(width, width)
        up = up.reshape(-1, width, UNITS)
        unit_vec = unit_vec.reshape(-1, unit_vec.shape[-2], UNITS)
        branch, middle, feed_turned, act, slope, stats, down = second_part(
            scaled, out_weights, vectors, tokens, up, unit_vec, down
        )
        down = down.reshape(-1, UNITS, width)
    else:
        weights, out_weights, vectors = attn
        first, projected, scaled, attended, lse = plain_first(
            cross, tokens, weights, vectors, head_lanes
        )
        branch, middle, feed = out_proj(scaled, out_weights, vectors, tokens)
        act, slope, stats = up_pass(feed, up, unit_vec)
    mixed, down_grad, e, stats, unit_grad = down_pass(
        act, stats, unit_vec, down, cotangent, middle, down_bias.astype(F32)[None]
    )
    if staged:
        head_row = jnp.pad(scale, (0, 128 - heads), constant_values=1.0)[None, :]
        tokens_grad, down_total, up_total, shares, _ = back_part(
            cross,
            act,
            slope,
            e,
            stats,
            up,
            feed_turned,
            unit_grad,
            down_grad,
            cotangent,
            middle,
            branch,
            scaled,
            attended,
            out_weights,
            vectors,
            head_lanes,
            head_row,
            heads_map,
            projected,
            lse,
            weights,
            turned,
            tokens,
        )
        return mixed, tokens_grad, down_total, up_total, shares
    up_grad, up_bias_grad, grad_feed = up_back(
        act, slope, e, stats, up, feed
    )
    grad_middle, ga, out_grad, delta, sums = out_back(
        grad_feed,
        cotangent,
        middle,
        branch,
        scaled,
        attended,
        out_weights,
        vectors,
        head_lanes,
        heads_map,
    )
    chunks, proj_bias, tokens_grad, pre_sums = in_back(
        cross,
        projected,
        ga,
        lse,
        delta.reshape(pairs, 2, rows),
        weights,
        first,
        out_grad,
        tokens,
        vectors[3:4],
        grad_middle,
    )
    scale_grad = jnp.sum(delta, axis=1) / scale
    vec_grads = [
        proj_bias[:, 0].reshape(width),
        proj_bias[:, 1].reshape(width),
        sums[2],
        pre_sums[0],
        pre_sums[1],
        sums[5],
        sums[6],
        sums[7],
        sums[8],
    ]
    unit_grads = [up_bias_grad[:, 0], unit_grad[:, 0], unit_grad[:, 1]]
    return mixed, tokens_grad, chunks, up_grad, down_grad, vec_grads, unit_grads, sums[9], scale_grad


def body(
    axes,
    tokens,
    cotangent,
    lengths,
    in_weight,
    query_bias,
    value_bias,
    out_weight,
    out_bias,
    head_scale,
    pre_gain,
    pre_bias,
    post_gain,
    post_bias,
    feed_gain,
    feed_bias,
    up_weight,
    up_bias,
    mid_gain,
    mid_bias,
    down_weight,
    down_bias,
):
    planes, wide = axes
    every = ("dp", "wide")
    staged = (planes, wide) == (4, 8)
    rows, width = tokens.shape
    units = down_weight.shape[0] * wide
    steps = units // UNITS
    share = in_weight.shape[0]
    columns = [
        query_bias,
        value_bias,
        out_bias,
        pre_gain,
        pre_bias,
        post_gain,
        post_bias,
        feed_gain,
        feed_bias,
    ]
    unit_rows = jnp.concatenate([up_bias, mid_gain, mid_bias]).reshape(3, -1)
    unit_rows = jnp.pad(unit_rows, ((0, 29), (0, 0)))
    if staged:
        index = lax.broadcasted_iota(jnp.int32, (32, 128), 0)
        vec_block = jnp.zeros((32, 128), BF)
        for row, column in enumerate(columns):
            column = jnp.pad(column, (0, 128 - share))[None, :]
            vec_block = jnp.where(index == row, column, vec_block)
        attn = (in_weight, out_weight, vec_block)
        up, unit_vec, down = up_weight, unit_rows, down_weight
    else:
        flat = jnp.concatenate(columns).reshape(len(columns), share)
        attn = (
            lax.all_gather(in_weight, every, axis=0, tiled=True),
            lax.all_gather(out_weight, every, axis=0, tiled=True),
            jnp.pad(
                lax.all_gather(flat, every, axis=1, tiled=True), ((0, 16 - len(columns)), (0, 0))
            ).astype(F32),
        )
        up = lax.all_gather(up_weight, "wide", axis=1, tiled=True)
        up = up.reshape(width, steps, UNITS).transpose(1, 0, 2)
        unit_vec = lax.all_gather(unit_rows, "wide", axis=1, tiled=True)
        unit_vec = unit_vec.reshape(32, steps, UNITS).transpose(1, 0, 2)
        down = lax.all_gather(down_weight, "wide", axis=0, tiled=True)
        down = down.reshape(steps, UNITS, width)
    results = layer(
        staged,
        tokens,
        cotangent,
        lengths,
        attn,
        up,
        down,
        unit_vec,
        head_scale,
        down_bias,
    )
    heads = head_scale.shape[0]
    pairs = width // 128
    if staged:
        mixed, tokens_grad, down_total, up_total, shares = results
        up_total = up_total.astype(F32).reshape(width, UNITS)
        down_total = down_total.astype(F32).reshape(UNITS, width)
        unit_totals = [shares[8, index] for index in range(3)]
        down_sum = jnp.concatenate([shares[8, 3], shares[8, 4]])
        scale_sum = shares[8, 5, :heads]
        offset = share * lax.rem(lax.axis_index("wide"), 128 // share)
        own = lax.dynamic_slice(shares, (8, 16, offset), (1, len(columns), share))[0]
        vec_totals = [own[index] for index in range(len(columns))]
        in_total = shares[:pairs, :, :384].reshape(pairs, share, 3, 128)
        in_total = in_total.transpose(1, 2, 0, 3).reshape(share, 3 * width)
        out_total = shares[:pairs, :, 384:].transpose(1, 0, 2).reshape(share, width)
    else:
        (mixed, tokens_grad, chunks, up_grad, down_grad, vec_grads, unit_grads) = results[:7]
        down_sum, scale_sum = results[7:]

        def scatter(value, axis=0, over=every):
            return lax.psum_scatter(value, over, scatter_dimension=axis, tiled=True)

        def both_ways(value, axis):
            part = scatter(value.astype(BF), axis, "wide")
            return lax.psum(part, "dp").astype(F32)

        up_total = both_ways(up_grad.transpose(1, 0, 2).reshape(width, units), 1)
        down_total = both_ways(down_grad.reshape(units, width), 0)
        unit_totals = [
            lax.psum(scatter(item.reshape(units), 0, "wide"), "dp") for item in unit_grads
        ]
        down_sum, scale_sum = lax.psum((down_sum, scale_sum), every)
        vec_totals = [scatter(item) for item in vec_grads]
        natural = chunks.transpose(0, 2, 1, 3, 4).reshape(pairs, width, 512)
        in_total = natural[:, :, :384].reshape(pairs, width, 3, 128)
        in_total = scatter(in_total.transpose(1, 2, 0, 3).reshape(width, 3 * width).astype(F32))
        out_total = scatter(
            natural[:, :, 384:].transpose(1, 0, 2).reshape(width, width).astype(F32)
        )
    return (
        mixed,
        tokens_grad,
        in_total,
        vec_totals[0],
        vec_totals[1],
        out_total,
        vec_totals[2],
        scale_sum,
        vec_totals[3],
        vec_totals[4],
        vec_totals[5],
        vec_totals[6],
        vec_totals[7],
        vec_totals[8],
        up_total,
        unit_totals[0],
        unit_totals[1],
        unit_totals[2],
        down_total,
        down_sum,
    )


def solution(mesh):
    by_all = P(("dp", "wide"))
    rows_all = P(("dp", "wide"), None)
    axes = (mesh.shape["dp"], mesh.shape["wide"])
    return jax.shard_map(
        functools.partial(body, axes),
        mesh=mesh,
        in_specs=(
            rows_all,
            rows_all,
            rows_all,
            rows_all,
            by_all,
            by_all,
            rows_all,
            by_all,
            P(),
            by_all,
            by_all,
            by_all,
            by_all,
            by_all,
            by_all,
            P(None, "wide"),
            P("wide"),
            P("wide"),
            P("wide"),
            P("wide", None),
            P(),
        ),
        out_specs=(
            rows_all,
            rows_all,
            rows_all,
            by_all,
            by_all,
            rows_all,
            by_all,
            P(),
            by_all,
            by_all,
            by_all,
            by_all,
            by_all,
            by_all,
            P(None, "wide"),
            P("wide"),
            P("wide"),
            P("wide"),
            P("wide", None),
            P(),
        ),
        check_vma=False,
    )
```

```python
import functools

import jax
import jax.numpy as jnp
from jax import lax
from jax.experimental import pallas as pl
from jax.experimental.pallas import tpu as pltpu
from jax.sharding import PartitionSpec as P

EPS = 1e-05
ROOT_HALF = 0.7071067811865476
INV_ROOT_TAU = 0.3989422804014327
LOG2E = 1.4426950408889634
MASKED = -1e30
BF = jnp.bfloat16
F32 = jnp.float32
TILE = 256
UNITS = 512
SLIM = 64
MESH = pl.DeviceIdType.MESH
VMEM_LIMIT = 62 * 1024 * 1024
ANY = pl.BlockSpec(memory_space=pl.ANY)


def dot_nn(left, right):
    return lax.dot_general(left, right, (((1,), (0,)), ((), ())), preferred_element_type=F32)


def dot_nt(left, right):
    return lax.dot_general(left, right, (((1,), (1,)), ((), ())), preferred_element_type=F32)


def dot_tn(left, right):
    return lax.dot_general(left, right, (((0,), (0,)), ((), ())), preferred_element_type=F32)


def params(**more):
    return pltpu.CompilerParams(
        dimension_semantics=("arbitrary",), vmem_limit_bytes=VMEM_LIMIT, **more
    )


def whole(shape):
    zeros = (0,) * len(shape)
    return pl.BlockSpec(shape, lambda *_: zeros, pipeline_mode=pl.Buffered(1))


def row_norm(values):
    center = values - jnp.mean(values, axis=-1, keepdims=True)
    inv = lax.rsqrt(jnp.mean(center * center, axis=-1, keepdims=True) + EPS)
    return center * inv, inv


def norm_back(grad, gain, normed, inv):
    scaled = grad * gain
    first = jnp.mean(scaled, axis=-1, keepdims=True)
    cross = jnp.mean(scaled * normed, axis=-1, keepdims=True)
    return inv * (scaled - first - normed * cross)


def column_sum(values):
    return jnp.sum(values, axis=0, keepdims=True)


def lane_fold(values):
    total = values[:, :128]
    for start in range(128, values.shape[1], 128):
        total = total + values[:, start : start + 128]
    return total


def cross_flag(lengths_ref, rows_ref):
    return jnp.where(lengths_ref[0, 0] == rows_ref.shape[0], 0.0, MASKED)


def stacked(value, low_lanes):
    zero = jnp.zeros_like(value)
    return jnp.concatenate(
        [jnp.where(low_lanes, value, zero), jnp.where(low_lanes, zero, value)], axis=0
    )


def attention_pair(cross, q_ref, k_ref, v_ref, scale, scaled_ref, out_ref, lse_ref, vext_ref):
    rows = q_ref.shape[0]
    half = rows // 2
    factor = LOG2E * 64 ** (-0.5)
    low_lanes = lax.broadcasted_iota(jnp.int32, (1, 128), 1) < 64
    below = lax.broadcasted_iota(jnp.int32, (TILE, TILE), 1) <= lax.broadcasted_iota(
        jnp.int32, (TILE, TILE), 0
    )
    vext_ref[:, :128] = v_ref[...]
    vext_ref[:, 128:] = jnp.ones((rows, 128), BF)
    for start in range(0, rows, TILE):
        stop = start + TILE
        both = dot_nt(stacked(q_ref[start:stop], low_lanes), k_ref[:stop])
        peaks, weights = [], []
        for head in range(2):
            raw = both[head * TILE : (head + 1) * TILE]
            parts = []
            if start >= half:
                parts.append((raw[:, :half], cross))
                if start > half:
                    parts.append((raw[:, half:start], None))
            elif start > 0:
                parts.append((raw[:, :start], None))
            parts.append((jnp.where(below, raw[:, start:stop], MASKED), None))
            peak = None
            for piece, shift in parts:
                top = jnp.max(piece, axis=-1, keepdims=True)
                if shift is not None:
                    top = top + shift
                peak = top if peak is None else jnp.maximum(peak, top)
            peaks.append(peak)
            pieces = []
            for piece, shift in parts:
                level = peak if shift is None else peak - shift
                pieces.append(jnp.exp2((piece - level) * factor).astype(BF))
            weights.append(pieces[0] if len(pieces) == 1 else jnp.concatenate(pieces, axis=1))
        both = dot_nn(jnp.concatenate(weights, axis=0), vext_ref[:stop])
        total = jnp.where(low_lanes, both[:TILE, 128:], both[TILE:, 128:])
        peak = jnp.where(low_lanes, peaks[0], peaks[1])
        mixed = jnp.where(low_lanes, both[:TILE, :128], both[TILE:, :128]) / total
        out_ref[start:stop] = mixed
        scaled_ref[start:stop] = (mixed * scale).astype(BF)
        lse = (peak * factor + jnp.log2(total)).T
        lse_ref[0, 0:1, start:stop] = lse[0:1]
        lse_ref[0, 1:2, start:stop] = lse[64:65]


def project_pair(first_ref, weights, bias, proj_ref):
    proj_ref[0] = (dot_nn(first_ref[...], weights) + bias).astype(BF)


def three(proj_ref):
    return [proj_ref.at[0, :, pl.ds(part * 128, 128)] for part in range(3)]


def plain_first_kernel(
    lengths_ref,
    tokens_ref,
    wq_ref,
    wk_ref,
    wv_ref,
    vectors_ref,
    bq_ref,
    bv_ref,
    hs_ref,
    first_ref,
    proj_ref,
    scaled_ref,
    attended_ref,
    lse_ref,
    vext_ref,
):
    @pl.when(pl.program_id(0) == 0)
    def _():
        for start in range(0, tokens_ref.shape[0], TILE):
            rows = pl.ds(start, TILE)
            normed, _ = row_norm(tokens_ref[rows].astype(F32))
            first_ref[rows] = (normed * vectors_ref[3:4] + vectors_ref[4:5]).astype(BF)

    weights = jnp.concatenate([wq_ref[...], wk_ref[...], wv_ref[...]], axis=1)
    bias = jnp.concatenate([bq_ref[0:1], jnp.zeros((1, 128), F32), bv_ref[1:2]], axis=1)
    project_pair(first_ref, weights, bias, proj_ref)
    attention_pair(
        cross_flag(lengths_ref, tokens_ref), *three(proj_ref), hs_ref[...], scaled_ref, attended_ref, lse_ref, vext_ref
    )


def plain_first(lengths, tokens, weights, vectors, head_lanes):
    rows, width = tokens.shape
    pairs = width // 128
    column = pl.BlockSpec((rows, 128), lambda p: (0, p))
    bias = pl.BlockSpec((16, 128), lambda p: (0, p))
    return pl.pallas_call(
        plain_first_kernel,
        grid=(pairs,),
        in_specs=[
            pl.BlockSpec(memory_space=pltpu.SMEM),
            whole((rows, width)),
            pl.BlockSpec((width, 128), lambda p: (0, p)),
            pl.BlockSpec((width, 128), lambda p: (0, pairs + p)),
            pl.BlockSpec((width, 128), lambda p: (0, 2 * pairs + p)),
            whole(vectors.shape),
            bias,
            bias,
            pl.BlockSpec((1, 128), lambda p: (0, p)),
        ],
        out_specs=[
            whole((rows, width)),
            pl.BlockSpec((1, rows, 384), lambda p: (p, 0, 0)),
            column,
            column,
            pl.BlockSpec((1, 8, rows), lambda p: (p, 0, 0)),
        ],
        out_shape=[
            jax.ShapeDtypeStruct((rows, width), BF),
            jax.ShapeDtypeStruct((pairs, rows, 384), BF),
            jax.ShapeDtypeStruct((rows, width), BF),
            jax.ShapeDtypeStruct((rows, width), F32),
            jax.ShapeDtypeStruct((pairs, 8, rows), F32),
        ],
        scratch_shapes=[pltpu.VMEM((rows, 256), BF)],
        compiler_params=params(),
        name="plain_first",
    )(lengths, tokens, weights, weights, weights, vectors, vectors, vectors, head_lanes)


def out_proj_rows(scaled_ref, weight_ref, vec_ref, tokens_ref, branch_ref, middle_ref):
    branch = dot_nn(scaled_ref[...], weight_ref[...]) + vec_ref[2:3]
    normed, _ = row_norm(branch)
    middle = tokens_ref[...].astype(F32) + (normed * vec_ref[5:6] + vec_ref[6:7])
    again, _ = row_norm(middle)
    branch_ref[...] = branch
    middle_ref[...] = middle
    return (again * vec_ref[7:8] + vec_ref[8:9]).astype(BF)


def out_proj_kernel(scaled_ref, weight_ref, vec_ref, tokens_ref, branch_ref, middle_ref, feed_ref):
    feed_ref[...] = out_proj_rows(
        scaled_ref, weight_ref, vec_ref, tokens_ref, branch_ref, middle_ref
    )


def out_proj(scaled, weights, vectors, tokens):
    rows, width = tokens.shape
    by_row = pl.BlockSpec((TILE, width), lambda i: (i, 0))
    return pl.pallas_call(
        out_proj_kernel,
        grid=(rows // TILE,),
        in_specs=[
            by_row,
            whole((width, width)),
            whole(vectors.shape),
            by_row,
        ],
        out_specs=[by_row, by_row, by_row],
        out_shape=[
            jax.ShapeDtypeStruct((rows, width), F32),
            jax.ShapeDtypeStruct((rows, width), F32),
            jax.ShapeDtypeStruct((rows, width), BF),
        ],
        compiler_params=params(),
        name="out_proj",
    )(scaled, weights, vectors, tokens)


def phi_and_slope(value):
    bell = jnp.exp2(value * value * (-0.5 * LOG2E))
    t = 1.0 / (1.0 + (0.3275911 * ROOT_HALF) * jnp.abs(value))
    series = t * (
        0.5 * 0.254829592
        + t
        * (
            0.5 * -0.284496736
            + t * (0.5 * 1.421413741 + t * (0.5 * -1.453152027 + t * (0.5 * 1.061405429)))
        )
    )
    tail = series * bell
    area = jnp.where(value < 0.0, tail, 1.0 - tail)
    return value * area, area + value * bell * INV_ROOT_TAU


def up_step(feed_ref, up_ref, vec_ref, act_ref, slope_ref, sums_ref):
    for left in range(0, UNITS, TILE):
        columns = slice(left, left + TILE)
        pre = dot_nn(feed_ref[...], up_ref[0, :, columns])
        bias = vec_ref[0, 0:1, columns].astype(F32)
        for start in range(0, feed_ref.shape[0], SLIM):
            rows = slice(start, start + SLIM)
            act, slope = phi_and_slope(pre[rows] + bias)
            act_ref[0, rows, columns] = act.astype(BF)
            slope_ref[0, rows, columns] = slope.astype(BF)
            sums_ref[0, rows] += lane_fold(act)
            sums_ref[1, rows] += lane_fold(act * act)


def side_by_side(*columns):
    lane = lax.broadcasted_iota(jnp.int32, (1, 128), 1)
    result = jnp.broadcast_to(columns[-1], (columns[-1].shape[0], 128))
    for index in range(len(columns) - 2, -1, -1):
        result = jnp.where(lane == index, columns[index], result)
    return result


def up_stats(units, stats_ref, sums_ref):
    for start in range(0, stats_ref.shape[0], TILE):
        rows = pl.ds(start, TILE)
        mean = jnp.sum(sums_ref[0, rows], axis=1, keepdims=True) / units
        square = jnp.sum(sums_ref[1, rows], axis=1, keepdims=True) / units
        inv = lax.rsqrt(square - mean * mean + EPS)
        stats_ref[rows] = side_by_side(mean, inv)


def up_kernel(units, feed_ref, up_ref, vec_ref, act_ref, slope_ref, stats_ref, sums_ref):
    step = pl.program_id(0)

    @pl.when(step == 0)
    def _():
        sums_ref[...] = jnp.zeros_like(sums_ref)

    up_step(feed_ref, up_ref, vec_ref, act_ref, slope_ref, sums_ref)

    @pl.when(step == pl.num_programs(0) - 1)
    def _():
        up_stats(units, stats_ref, sums_ref)


def up_pass(feed, up, vec):
    rows, width = feed.shape
    steps = up.shape[0]
    block = pl.BlockSpec((1, rows, UNITS), lambda j: (j, 0, 0))
    return pl.pallas_call(
        functools.partial(up_kernel, steps * UNITS),
        grid=(steps,),
        in_specs=[
            whole((rows, width)),
            pl.BlockSpec((1, width, UNITS), lambda j: (j, 0, 0)),
            pl.BlockSpec((1, vec.shape[1], UNITS), lambda j: (j, 0, 0)),
        ],
        out_specs=[block, block, whole((rows, 128))],
        out_shape=[
            jax.ShapeDtypeStruct((steps, rows, UNITS), BF),
            jax.ShapeDtypeStruct((steps, rows, UNITS), BF),
            jax.ShapeDtypeStruct((rows, 128), F32),
        ],
        scratch_shapes=[pltpu.VMEM((2, rows, 128), F32)],
        compiler_params=params(),
        name="up_pass",
    )(feed, up, vec)


def down_kernel(
    units,
    act_ref,
    stats_ref,
    vec_ref,
    down_ref,
    cot_ref,
    middle_ref,
    shift_ref,
    mixed_ref,
    down_grad_ref,
    e_ref,
    all_stats_ref,
    vec_grad_ref,
    total_ref,
    sums_ref,
    low_ref,
):
    step = pl.program_id(0)
    last = pl.num_programs(0) - 1
    rows_all = cot_ref.shape[0]

    @pl.when(step == 0)
    def _():
        total_ref[...] = jnp.zeros_like(total_ref)
        sums_ref[...] = jnp.zeros_like(sums_ref)

    gain = vec_ref[0, 1:2].astype(F32)
    shift = vec_ref[0, 2:3].astype(F32)
    slims = [slice(start, start + SLIM) for start in range(0, rows_all, SLIM)]

    def normalized(rows, columns):
        value = act_ref[0, rows, columns].astype(F32)
        return (value - stats_ref[rows, 0:1]) * stats_ref[rows, 1:2]

    for rows in slims:
        low_ref[rows] = (normalized(rows, slice(0, UNITS)) * gain + shift).astype(BF)
    for left in range(0, UNITS, TILE):
        columns = slice(left, left + TILE)
        grads = dot_nt(cot_ref[...], down_ref[0, columns])
        gain_grad = jnp.zeros((SLIM, TILE), F32)
        bias_grad = jnp.zeros((SLIM, TILE), F32)
        for rows in slims:
            normed = normalized(rows, columns)
            grad = grads[rows]
            gain_grad = gain_grad + grad * normed
            bias_grad = bias_grad + grad
            e = grad * gain[:, columns]
            e_ref[0, rows, columns] = e.astype(BF)
            sums_ref[0, rows] += lane_fold(e)
            sums_ref[1, rows] += lane_fold(e * normed)
        vec_grad_ref[0, 0:1, columns] = column_sum(gain_grad)
        vec_grad_ref[0, 1:2, columns] = column_sum(bias_grad)
    for left in range(0, total_ref.shape[1], TILE):
        columns = slice(left, left + TILE)
        total_ref[:, columns] += dot_nn(low_ref[...], down_ref[0, :, columns])
    for left in range(0, UNITS, TILE):
        columns = slice(left, left + TILE)
        down_grad_ref[0, columns] = dot_tn(low_ref[:, columns], cot_ref[...]).astype(BF)

    @pl.when(step == last)
    def _():
        for start in range(0, rows_all, TILE):
            rows = pl.ds(start, TILE)
            mixed_ref[rows] = (
                middle_ref[rows] + total_ref[rows] + shift_ref[...].astype(F32)
            ).astype(BF)
            first = jnp.sum(sums_ref[0, rows], axis=1, keepdims=True) / units
            cross = jnp.sum(sums_ref[1, rows], axis=1, keepdims=True) / units
            all_stats_ref[rows] = side_by_side(
                stats_ref[rows, 0:1], stats_ref[rows, 1:2], first, cross
            )


def down_pass(act, stats, vec, down, cotangent, middle, shift):
    rows, width = cotangent.shape
    steps = act.shape[0]
    block = pl.BlockSpec((1, rows, UNITS), lambda j: (j, 0, 0))
    return pl.pallas_call(
        functools.partial(down_kernel, steps * UNITS),
        grid=(steps,),
        in_specs=[
            block,
            whole((rows, 128)),
            pl.BlockSpec((1, vec.shape[1], UNITS), lambda j: (j, 0, 0)),
            pl.BlockSpec((1, UNITS, width), lambda j: (j, 0, 0)),
            whole((rows, width)),
            whole((rows, width)),
            whole((1, width)),
        ],
        out_specs=[
            whole((rows, width)),
            pl.BlockSpec((1, UNITS, width), lambda j: (j, 0, 0)),
            block,
            whole((rows, 128)),
            pl.BlockSpec((1, 8, UNITS), lambda j: (j, 0, 0)),
        ],
        out_shape=[
            jax.ShapeDtypeStruct((rows, width), BF),
            jax.ShapeDtypeStruct((steps, UNITS, width), BF),
            jax.ShapeDtypeStruct((steps, rows, UNITS), BF),
            jax.ShapeDtypeStruct((rows, 128), F32),
            jax.ShapeDtypeStruct((steps, 8, UNITS), F32),
        ],
        scratch_shapes=[
            pltpu.VMEM((rows, width), F32),
            pltpu.VMEM((2, rows, 128), F32),
            pltpu.VMEM((rows, UNITS), BF),
        ],
        compiler_params=params(),
        name="down_pass",
    )(act, stats, vec, down, cotangent, middle, shift)


def up_back_step(act, slope, e, stats_ref, up, low_ref, total_ref):
    bias_grad = jnp.zeros((SLIM, UNITS), F32)
    for start in range(0, total_ref.shape[0], SLIM):
        rows = slice(start, start + SLIM)
        inv = stats_ref[rows, 1:2]
        normed = (act[rows].astype(F32) - stats_ref[rows, 0:1]) * inv
        grad_act = inv * (
            e[rows].astype(F32) - stats_ref[rows, 2:3] - normed * stats_ref[rows, 3:4]
        )
        low = (grad_act * slope[rows].astype(F32)).astype(BF)
        bias_grad = bias_grad + low.astype(F32)
        low_ref[rows, 0:UNITS] = low
    for left in range(0, total_ref.shape[1], TILE):
        columns = slice(left, left + TILE)
        total_ref[:, columns] += dot_nt(low_ref[:, 0:UNITS], up[columns])
    return column_sum(bias_grad)


def up_back_kernel(
    act_ref,
    slope_ref,
    e_ref,
    stats_ref,
    up_ref,
    feed_ref,
    up_grad_ref,
    bias_grad_ref,
    total_ref,
    turned_ref,
    low_ref,
):
    @pl.when(pl.program_id(0) == 0)
    def _():
        total_ref[...] = jnp.zeros_like(total_ref)
        turned_ref[...] = feed_ref[...].T

    bias_grad_ref[0, 0:1] = up_back_step(
        act_ref.at[0],
        slope_ref.at[0],
        e_ref.at[0],
        stats_ref,
        up_ref.at[0],
        low_ref,
        total_ref,
    )
    up_grad_ref[0] = dot_nn(turned_ref[...], low_ref[...]).astype(BF)


def up_back(act, slope, e, stats, up, feed):
    rows, width = feed.shape
    steps = act.shape[0]
    block = pl.BlockSpec((1, rows, UNITS), lambda j: (j, 0, 0))
    narrow = whole((rows, 128))
    return pl.pallas_call(
        up_back_kernel,
        grid=(steps,),
        in_specs=[
            block,
            block,
            block,
            narrow,
            pl.BlockSpec((1, width, UNITS), lambda j: (j, 0, 0)),
            whole((rows, width)),
        ],
        out_specs=[
            pl.BlockSpec((1, width, UNITS), lambda j: (j, 0, 0)),
            pl.BlockSpec((1, 8, UNITS), lambda j: (j, 0, 0)),
            whole((rows, width)),
        ],
        out_shape=[
            jax.ShapeDtypeStruct((steps, width, UNITS), BF),
            jax.ShapeDtypeStruct((steps, 8, UNITS), F32),
            jax.ShapeDtypeStruct((rows, width), F32),
        ],
        scratch_shapes=[pltpu.VMEM((width, rows), BF), pltpu.VMEM((rows, UNITS), BF)],
        compiler_params=params(),
        name="up_back",
    )(act, slope, e, stats, up, feed)


def norms_back(grad_feed, cot_ref, middle_ref, branch_ref, vec_ref, sums_ref):
    normed, inv = row_norm(middle_ref[...])
    cot = cot_ref[...].astype(F32)
    grad_middle = cot + norm_back(grad_feed, vec_ref[7:8], normed, inv)
    sums_ref[7:8] += column_sum(grad_feed * normed)
    sums_ref[8:9] += column_sum(grad_feed)
    sums_ref[9:10] += column_sum(cot)
    normed, inv = row_norm(branch_ref[...])
    low = norm_back(grad_middle, vec_ref[5:6], normed, inv).astype(BF)
    sums_ref[5:6] += column_sum(grad_middle * normed)
    sums_ref[6:7] += column_sum(grad_middle)
    sums_ref[2:3] += column_sum(low.astype(F32))
    return grad_middle, low


def heads_back(low, weights, scale, attended):
    grad_out = (dot_nt(low, weights) * scale).astype(BF)
    product = grad_out.astype(F32) * attended
    high = product.astype(BF)
    rest = (product - high.astype(F32)).astype(BF)
    heads = (
        lax.broadcasted_iota(jnp.int32, (product.shape[1], 128), 0) // 64
        == lax.broadcasted_iota(jnp.int32, (product.shape[1], 128), 1)
    ).astype(BF)
    return grad_out, dot_nn(high, heads) + dot_nn(rest, heads)


def out_back_kernel(
    grad_feed_ref,
    cot_ref,
    middle_ref,
    branch_ref,
    scaled_ref,
    attended_ref,
    weight_ref,
    vec_ref,
    hs_ref,
    grad_middle_ref,
    ga_ref,
    out_grad_ref,
    delta_ref,
    sums_ref,
    total_ref,
):
    step = pl.program_id(0)

    @pl.when(step == 0)
    def _():
        total_ref[...] = jnp.zeros_like(total_ref)
        sums_ref[...] = jnp.zeros_like(sums_ref)

    grad_middle, low = norms_back(
        grad_feed_ref[...], cot_ref, middle_ref, branch_ref, vec_ref, sums_ref
    )
    grad_middle_ref[...] = grad_middle
    ga_ref[...], delta = heads_back(low, weight_ref[...], hs_ref[...], attended_ref[...])
    total_ref[...] += dot_tn(scaled_ref[...], low)
    delta_ref[...] = delta.T[: delta_ref.shape[0]]

    @pl.when(step == pl.num_programs(0) - 1)
    def _():
        out_grad_ref[...] = total_ref[...].astype(BF)


def out_back(
    grad_feed, cotangent, middle, branch, scaled, attended, weights, vectors, head_lanes
):
    rows, width = cotangent.shape
    heads = 2 * width // 128
    by_row = pl.BlockSpec((TILE, width), lambda i: (i, 0))
    return pl.pallas_call(
        out_back_kernel,
        grid=(rows // TILE,),
        in_specs=[
            by_row,
            by_row,
            by_row,
            by_row,
            by_row,
            by_row,
            whole((width, width)),
            whole(vectors.shape),
            whole((1, width)),
        ],
        out_specs=[
            by_row,
            by_row,
            whole((width, width)),
            pl.BlockSpec((heads, TILE), lambda i: (0, i)),
            whole((16, width)),
        ],
        out_shape=[
            jax.ShapeDtypeStruct((rows, width), F32),
            jax.ShapeDtypeStruct((rows, width), BF),
            jax.ShapeDtypeStruct((width, width), BF),
            jax.ShapeDtypeStruct((heads, rows), F32),
            jax.ShapeDtypeStruct((16, width), F32),
        ],
        scratch_shapes=[pltpu.VMEM((width, width), F32)],
        compiler_params=params(),
        name="out_back",
    )(
        grad_feed,
        cotangent,
        middle,
        branch,
        scaled,
        attended,
        weights,
        vectors,
        head_lanes,
    )


def attention_back_keys(
    starts, cross, q_ref, k_ref, v_ref, ga_ref, lse_ref, deltas, dq_ref, dk_ref, dv_ref
):
    rows = q_ref.shape[0]
    half = rows // 2
    factor = LOG2E * 64 ** (-0.5)
    low_lanes = lax.broadcasted_iota(jnp.int32, (1, 128), 1) < 64
    above = lax.broadcasted_iota(jnp.int32, (TILE, TILE), 0) <= lax.broadcasted_iota(
        jnp.int32, (TILE, TILE), 1
    )

    def pick(both):
        return jnp.where(low_lanes, both[:TILE], both[TILE:])

    for start in starts:
        stop = start + TILE
        keys = k_ref[start:stop]
        keys_apart = stacked(keys, low_lanes)
        values_apart = stacked(v_ref[start:stop], low_lanes)
        dk = jnp.zeros((TILE, 128), F32)
        dv = jnp.zeros((TILE, 128), F32)
        for left, right in ((start, half), (half, rows)) if start < half else ((start, rows),):
            raw = dot_nt(keys_apart, q_ref[left:right])
            grad_weights = dot_nt(values_apart, ga_ref[left:right])
            weights, grad_scores = [], []
            for head in range(2):
                mine = slice(head * TILE, (head + 1) * TILE)
                level = lse_ref[0, head : head + 1, left:right]
                if start < half <= left:
                    level = level - cross
                exponent = raw[mine] * factor - level
                if left == start:
                    first = jnp.where(above, exponent[:, :TILE], MASKED)
                    exponent = (
                        first
                        if right - left == TILE
                        else jnp.concatenate([first, exponent[:, TILE:]], axis=1)
                    )
                weight = jnp.exp2(exponent)
                weights.append(weight.astype(BF))
                delta = deltas[head][:, left:right]
                grad_scores.append((weight * (grad_weights[mine] - delta)).astype(BF))
            dv = dv + pick(dot_nn(jnp.concatenate(weights, axis=0), ga_ref[left:right]))
            dk = dk + pick(dot_nn(jnp.concatenate(grad_scores, axis=0), q_ref[left:right]))
            dq = jnp.where(low_lanes, dot_tn(grad_scores[0], keys), dot_tn(grad_scores[1], keys))
            if start == 0:
                dq_ref[left:right] = dq
            else:
                dq_ref[left:right] += dq
        dk_ref[start:stop] = dk
        dv_ref[start:stop] = dv


def in_back_pair(dq_ref, dk_ref, dv_ref, weights, turned_ref, out_grad_ref, chunk_ref, total_ref):
    factor = 64 ** (-0.5)
    dq = (dq_ref[...] * factor).astype(BF)
    dk = (dk_ref[...] * factor).astype(BF)
    dv = dv_ref[...].astype(BF)
    grads = jnp.concatenate([dq, dk, dv], axis=1)
    shares = dot_nn(turned_ref[...], grads).astype(BF)
    for start in range(0, total_ref.shape[0], TILE):
        part = jnp.concatenate(
            [shares[start : start + TILE], out_grad_ref[start : start + TILE]], axis=1
        )
        chunk_ref[:, start // TILE] = part.reshape(8, 32, 512)
        columns = slice(start, start + TILE)
        total_ref[:, columns] += dot_nt(grads, weights[columns])
    return column_sum(dq.astype(F32)), column_sum(dv.astype(F32))


def tokens_back(tokens, grad, grad_middle, gain):
    normed, inv = row_norm(tokens.astype(F32))
    back = norm_back(grad, gain, normed, inv)
    return (grad_middle + back).astype(BF), column_sum(grad * normed), column_sum(grad)


def in_back_kernel(
    lengths_ref,
    proj_ref,
    ga_ref,
    lse_ref,
    delta_ref,
    wq_ref,
    wk_ref,
    wv_ref,
    first_ref,
    out_grad_ref,
    tokens_ref,
    gain_ref,
    grad_middle_ref,
    chunk_ref,
    bias_ref,
    tokens_grad_ref,
    sums_ref,
    dq_ref,
    dk_ref,
    dv_ref,
    turned_ref,
    total_ref,
):
    step = pl.program_id(0)
    q_ref, k_ref, v_ref = three(proj_ref)
    rows_all = tokens_ref.shape[0]

    @pl.when(step == 0)
    def _():
        turned_ref[...] = first_ref[...].T
        total_ref[...] = jnp.zeros_like(total_ref)

    deltas = [delta_ref[0, head : head + 1] for head in range(2)]
    attention_back_keys(
        range(0, rows_all, TILE),
        cross_flag(lengths_ref, tokens_ref),
        q_ref,
        k_ref,
        v_ref,
        ga_ref,
        lse_ref,
        deltas,
        dq_ref,
        dk_ref,
        dv_ref,
    )
    weights = jnp.concatenate([wq_ref[...], wk_ref[...], wv_ref[...]], axis=1)
    query_sum, value_sum = in_back_pair(
        dq_ref, dk_ref, dv_ref, weights, turned_ref, out_grad_ref, chunk_ref.at[0], total_ref
    )
    bias_ref[0, 0:1] = query_sum
    bias_ref[0, 1:2] = value_sum

    @pl.when(step == pl.num_programs(0) - 1)
    def _():
        gain_grad = jnp.zeros((1, total_ref.shape[1]), F32)
        shift_grad = jnp.zeros((1, total_ref.shape[1]), F32)
        for start in range(0, rows_all, TILE):
            rows = pl.ds(start, TILE)
            tokens_grad_ref[rows], gain_part, shift_part = tokens_back(
                tokens_ref[rows], total_ref[rows], grad_middle_ref[rows], gain_ref[...]
            )
            gain_grad = gain_grad + gain_part
            shift_grad = shift_grad + shift_part
        sums_ref[0:1] = gain_grad
        sums_ref[1:2] = shift_grad


def in_back(lengths, projected, ga, lse, delta, weights, first, out_grad, tokens, gain, grad_middle):
    rows, width = tokens.shape
    pairs = width // 128
    column = pl.BlockSpec((rows, 128), lambda p: (0, p))
    square = whole((rows, width))
    return pl.pallas_call(
        in_back_kernel,
        grid=(pairs,),
        in_specs=[
            pl.BlockSpec(memory_space=pltpu.SMEM),
            pl.BlockSpec((1, rows, 384), lambda p: (p, 0, 0)),
            column,
            pl.BlockSpec((1, 8, rows), lambda p: (p, 0, 0)),
            pl.BlockSpec((1, 2, rows), lambda p: (p, 0, 0)),
            pl.BlockSpec((width, 128), lambda p: (0, p)),
            pl.BlockSpec((width, 128), lambda p: (0, pairs + p)),
            pl.BlockSpec((width, 128), lambda p: (0, 2 * pairs + p)),
            square,
            column,
            square,
            whole((1, width)),
            square,
        ],
        out_specs=[
            pl.BlockSpec((1, 8, width // TILE, 32, 512), lambda p: (p, 0, 0, 0, 0)),
            pl.BlockSpec((1, 8, 128), lambda p: (p, 0, 0)),
            square,
            whole((8, width)),
        ],
        out_shape=[
            jax.ShapeDtypeStruct((pairs, 8, width // TILE, 32, 512), BF),
            jax.ShapeDtypeStruct((pairs, 8, 128), F32),
            jax.ShapeDtypeStruct((rows, width), BF),
            jax.ShapeDtypeStruct((8, width), F32),
        ],
        scratch_shapes=[
            pltpu.VMEM((rows, 128), F32),
            pltpu.VMEM((rows, 128), F32),
            pltpu.VMEM((rows, 128), F32),
            pltpu.VMEM((width, rows), BF),
            pltpu.VMEM((rows, width), F32),
        ],
        compiler_params=params(),
        name="in_back",
    )(
        lengths,
        projected,
        ga,
        lse,
        delta,
        weights,
        weights,
        weights,
        first,
        out_grad,
        tokens,
        gain,
        grad_middle,
    )


class Place:
    def __init__(self):
        self.z = lax.axis_index("dp")
        wide = lax.axis_index("wide")
        self.y = wide // 4
        self.x = (wide // 2) % 2
        self.c = wide % 2
        self.core = (self.z, wide + 1 - 2 * self.c)
        self.side = (self.z, wide + 2 - 4 * self.x)
        self.over = (self.z, wide + 4 - 8 * self.y)
        self.ranks = (self.z + 1 - 2 * (self.z % 2), (self.z + 2) % 4, 3 - self.z)
        self.planes = tuple((rank, wide) for rank in self.ranks)

    def greet(self, planes=True):
        barrier = pltpu.get_barrier_semaphore()
        peers = (self.core, self.side, self.over) + (self.planes if planes else ())
        for peer in peers:
            pl.semaphore_signal(barrier, inc=1, device_id=peer, device_id_type=MESH)
        pl.semaphore_wait(barrier, len(peers))


class WideGather:
    copies = 13

    def __init__(self, place, source, target, send, recv, first, last):
        rows = target.shape[-2]
        y, x, c = place.y, place.x, place.c
        here, side, over, far = (y, x, c), (y, 1 - x, c), (1 - y, x, c), (1 - y, 1 - x, c)
        upper, lower, both = pl.ds(0, rows // 2), pl.ds(rows // 2, rows // 2), pl.ds(0, rows)

        def copy(index, slot, part, peer):
            destination = target.at[(*slot, part)]
            return pltpu.make_async_remote_copy(
                src_ref=source.at[part] if source is not None and slot is here else destination,
                dst_ref=destination,
                send_sem=send.at[first + index],
                recv_sem=recv.at[first + index],
                device_id=peer,
                device_id_type=MESH,
            )

        self.all = (
            copy(0, here, upper, place.side),
            copy(1, here, lower, place.over),
            copy(2, here, upper, place.over),
            copy(3, here, lower, place.side),
            copy(4, here, both, place.core),
            copy(5, side, upper, place.over),
            copy(6, side, upper, place.core),
            copy(7, over, lower, place.side),
            copy(8, over, lower, place.core),
            copy(9, side, lower, place.core),
            copy(10, over, upper, place.core),
            copy(11, far, upper, place.core),
            copy(12, far, lower, place.core),
        )
        self.own = None
        if source is not None:
            self.own = pltpu.make_async_copy(source, target.at[here], last)

    def start(self):
        if self.own is not None:
            self.own.start()
        for index in range(5):
            self.all[index].start()

    def relay(self, stage):
        waits, starts = (((0, 1), (5, 7, 6, 8)), ((2, 3), (9, 10)), ((5, 7), (11, 12)))[stage]
        for index in waits:
            self.all[index].wait_recv()
        for index in starts:
            self.all[index].start()

    def finish(self):
        for index in (4, 6, 8, 9, 10, 11, 12):
            self.all[index].wait_recv()
        for copy in self.all:
            copy.wait_send()
        if self.own is not None:
            self.own.wait()


LAG = 2


class Reduction:
    slots = 2 * LAG
    keep = 2 * LAG + 2

    @classmethod
    def scratch(cls):
        n, k = cls.slots, cls.keep
        return [
            pltpu.VMEM((3 * LAG, 2, 2, 4, 32, 512), BF),
            pltpu.VMEM((n, 2, 2, 4, 32, 512), BF),
            pltpu.VMEM((n, 2, 4, 16, 512), BF),
            pltpu.VMEM((n, 2, 4, 16, 512), BF),
            pltpu.VMEM((n, 4, 16, 512), BF),
            pltpu.VMEM((n, 4, 16, 512), BF),
            pltpu.VMEM((n, 4, 32, 512), BF),
            pltpu.VMEM((n, 3, 32, 512), BF),
            pltpu.VMEM((n, 32, 512), BF),
            pltpu.VMEM((k, 3, 32, 512), BF),
            pltpu.SemaphoreType.DMA((11, k)),
            pltpu.SemaphoreType.DMA((11, k)),
            pltpu.SemaphoreType.DMA((3 * LAG,)),
        ]

    def __init__(self, place, refs):
        self.place = place
        (
            self.chip,
            self.partner,
            self.from_x,
            self.from_y,
            self.then_y,
            self.then_x,
            self.plane,
            self.from_z,
            self.sums,
            self.shared,
            self.send,
            self.recv,
            self.local,
        ) = refs

    def copy(self, index, slot, source, target, peer):
        return pltpu.make_async_remote_copy(
            src_ref=source,
            dst_ref=target,
            send_sem=self.send.at[index, slot],
            recv_sem=self.recv.at[index, slot],
            device_id=peer,
            device_id_type=MESH,
        )

    def to_core(self, slot, source):
        return self.copy(0, slot, source, self.partner.at[slot], self.place.core)

    def load(self, chunk, source):
        slot = chunk % (3 * LAG)
        return pltpu.make_async_copy(source, self.chip.at[slot], self.local.at[slot])

    def first_hop(self, chunk):
        p, slot, chip = self.place, chunk % self.slots, self.chip.at[chunk % (3 * LAG)]
        return (
            self.copy(1, slot, chip.at[:, 1 - p.x, :, pl.ds(0, 16)], self.from_x.at[slot], p.side),
            self.copy(2, slot, chip.at[1 - p.y, :, :, pl.ds(16, 16)], self.from_y.at[slot], p.over),
        )

    def second_hop(self, chunk):
        p, slot, chip = self.place, chunk % self.slots, self.chip.at[chunk % (3 * LAG)]
        return (
            self.copy(
                3, slot, chip.at[1 - p.y, p.x, :, pl.ds(0, 16)], self.then_y.at[slot], p.over
            ),
            self.copy(
                4, slot, chip.at[p.y, 1 - p.x, :, pl.ds(16, 16)], self.then_x.at[slot], p.side
            ),
        )

    def to_planes(self, slot):
        p = self.place
        return [
            self.copy(
                5 + k, slot, self.plane.at[slot, p.ranks[k]], self.from_z.at[slot, k], p.planes[k]
            )
            for k in range(3)
        ]

    def share(self, slot, place):
        p = self.place
        return [
            self.copy(
                8 + k, place, self.sums.at[slot], self.shared.at[place, k], p.planes[k]
            )
            for k in range(3)
        ]

    def stage0(self, chunk, view):
        slot, c = chunk % self.slots, self.place.c
        self.to_core(slot, view.at[:, :, 1 - c]).start()
        self.load(chunk, view.at[:, :, c]).start()

    def stage1(self, chunk):
        slot, index = chunk % self.slots, chunk % (3 * LAG)
        self.load(chunk, self.partner.at[slot]).wait()
        self.to_core(slot, self.chip.at[index]).wait()
        self.chip[index] += self.partner[slot]
        for copy in self.first_hop(chunk):
            copy.start()

    def stage2(self, chunk):
        p, slot, index = self.place, chunk % self.slots, chunk % (3 * LAG)
        for copy in self.first_hop(chunk):
            copy.wait()
        for k in range(2):
            self.chip[index, k, p.x, :, 0:16] += self.from_x[slot, k]
            self.chip[index, p.y, k, :, 16:32] += self.from_y[slot, k]
        for copy in self.second_hop(chunk):
            copy.start()

    def stage3(self, chunk):
        p, slot = self.place, chunk % self.slots
        for copy in self.second_hop(chunk):
            copy.wait()
        mine = self.chip.at[chunk % (3 * LAG), p.y, p.x]
        self.plane[slot, :, 0:16] = mine[:, 0:16] + self.then_y[slot]
        self.plane[slot, :, 16:32] = mine[:, 16:32] + self.then_x[slot]
        for copy in self.to_planes(slot):
            copy.start()

    def stage4(self, chunk):
        slot = chunk % self.slots
        for copy in self.to_planes(slot):
            copy.wait()
        total = self.plane[slot, self.place.z].astype(F32)
        for k in range(3):
            total = total + self.from_z[slot, k].astype(F32)
        return total

    def spread(self, chunk, total):
        slot, place = chunk % self.slots, chunk % self.keep
        self.sums[slot] = total.astype(BF)
        for copy in self.share(slot, place):
            copy.start()

    def stage5(self, chunk):
        slot, place = chunk % self.slots, chunk % self.keep
        for copy in self.share(slot, place):
            copy.wait()
        blocks = [(self.place.z, self.sums[slot])]
        return blocks + [(self.place.ranks[k], self.shared[place, k]) for k in range(3)]


def dma_sems(count):
    return [pltpu.SemaphoreType.DMA((count,)), pltpu.SemaphoreType.DMA((count,))]


class FullGather:
    copies = 3 + 4 * WideGather.copies

    def __init__(self, place, source, target, send, recv, first, last):
        own = (place.y, place.x, place.c)
        mine = target.at[(place.z, *own)]
        self.across = [
            pltpu.make_async_remote_copy(
                src_ref=source if source is not None else mine,
                dst_ref=mine,
                send_sem=send.at[first + index],
                recv_sem=recv.at[first + index],
                device_id=peer,
                device_id_type=MESH,
            )
            for index, peer in enumerate(place.planes)
        ]
        self.parts = [
            WideGather(
                place,
                source if index == 0 else None,
                target.at[rank],
                send,
                recv,
                first + 3 + index * WideGather.copies,
                last,
            )
            for index, rank in enumerate((place.z, *place.ranks))
        ]

    def start(self):
        for copy in self.across:
            copy.start()
        self.parts[0].start()

    def spread(self):
        for index in range(3):
            self.across[index].wait_recv()
            self.parts[index + 1].start()

    def relay(self, stage):
        for part in self.parts:
            part.relay(stage)

    def finish(self):
        for copy in self.across:
            copy.wait_send()
        for part in self.parts:
            part.finish()


def first_kernel(
    lengths_ref,
    tokens_ref,
    in_ref,
    vec_ref,
    out_ref,
    up_ref,
    unit_ref,
    hs_ref,
    turned_ref,
    proj_ref,
    scaled_ref,
    scaled_turned_ref,
    attended_ref,
    lse_ref,
    vectors_ref,
    scale_ref,
    in_all,
    out_all,
    up_all,
    unit_all,
    held_ref,
    normed_ref,
    first_ref,
    vext_ref,
    send_in,
    recv_in,
    send_out,
    recv_out,
    send_ff,
    recv_ff,
    local,
):
    step = pl.program_id(0)
    place = Place()
    width = tokens_ref.shape[1]
    count = WideGather.copies
    into = FullGather(place, None, held_ref, send_in, recv_in, 0, None)
    out = FullGather(place, out_ref, out_all, send_out, recv_out, 0, local.at[2])
    up = WideGather(place, up_ref, up_all, send_ff, recv_ff, 0, local.at[3])
    unit = WideGather(place, unit_ref, unit_all, send_ff, recv_ff, count, local.at[4])
    keep = pltpu.make_async_copy(held_ref, in_all, local.at[5])

    @pl.when(step == 0)
    def _():
        place.greet()
        mine = held_ref.at[place.z, place.y, place.x, place.c]
        fill = pltpu.make_async_copy(in_ref, mine.at[:, pl.ds(0, 3 * width)], local.at[0])
        fill.start()
        mine[:, 3 * width : 3 * width + 128] = jnp.zeros((32, 128), BF)
        mine[:, 3 * width : 3 * width + 32] = vec_ref[...]
        fill.wait()
        into.start()
        scale = hs_ref[...].astype(F32)
        for pair in range(width // 128):
            own = slice(pair * 128, (pair + 1) * 128)
            low_lanes = lax.broadcasted_iota(jnp.int32, (1, 128), 1) < 64
            scale_ref[0:1, own] = jnp.where(
                low_lanes, scale[:, 2 * pair : 2 * pair + 1], scale[:, 2 * pair + 1 : 2 * pair + 2]
            )
        for start in range(0, tokens_ref.shape[0], TILE):
            rows = pl.ds(start, TILE)
            normed, _ = row_norm(tokens_ref[rows].astype(F32))
            normed_ref[rows] = normed
        for index in range(3):
            into.parts[index].relay(0)
            into.across[index].wait_recv()
            into.parts[index + 1].start()
            into.parts[index].relay(1)
            into.parts[index].relay(2)
        for stage in range(3):
            into.parts[3].relay(stage)
        out.start()
        unit.start()
        up.start()
        into.finish()
        keep.start()
        for z in range(4):
            for y in range(2):
                tile = jnp.zeros((16, 128), F32)
                for x in range(2):
                    for c in range(2):
                        piece = held_ref[z, y, x, c, 0:16, 3 * width : 3 * width + 128].astype(F32)
                        spot = 32 * (2 * x + c)
                        tile = tile + (piece if spot == 0 else pltpu.roll(piece, spot, 1))
                vectors_ref[:, (2 * z + y) * 128 : (2 * z + y + 1) * 128] = tile
        for start in range(0, tokens_ref.shape[0], TILE):
            rows = pl.ds(start, TILE)
            first_ref[rows] = (normed_ref[rows] * vectors_ref[3:4] + vectors_ref[4:5]).astype(BF)

    @pl.when(step == 1)
    def _():
        out.spread()

    @pl.when((step >= 2) & (step <= 4))
    def _():
        for stage in range(3):

            @pl.when(step == 2 + stage)
            def _():
                out.relay(stage)
                unit.relay(stage)

    for stage, at in enumerate((3, 5, 8)):

        @pl.when(step == at)
        def _():
            up.relay(stage)

    @pl.when(step > 0)
    def _():
        pair = step - 1
        columns = [pl.ds(pl.multiple_of(part * width + pair * 128, 128), 128) for part in range(3)]
        weights = jnp.concatenate(
            [held_ref[:, :, :, :, :, cols].reshape(width, 128) for cols in columns], axis=1
        )
        own = pl.ds(pl.multiple_of(pair * 128, 128), 128)
        bias = jnp.concatenate(
            [vectors_ref[0:1, own], jnp.zeros((1, 128), F32), vectors_ref[1:2, own]], axis=1
        )
        project_pair(first_ref, weights, bias, proj_ref)
        attention_pair(
            cross_flag(lengths_ref, tokens_ref),
            *three(proj_ref),
            scale_ref[0:1, own],
            scaled_ref,
            attended_ref,
            lse_ref,
            vext_ref,
        )
        scaled_turned_ref[...] = scaled_ref[...].T

    @pl.when(step == pl.num_programs(0) - 1)
    def _():
        turned_ref[...] = first_ref[...].T
        keep.wait()
        out.finish()
        unit.finish()
        up.finish()


def first_part(lengths, tokens, in_weight, vec, out_weight, up_weight, unit_rows, head_scale):
    rows, width = tokens.shape
    pairs = width // 128

    def at(step):
        return jnp.maximum(step - 1, 0)

    column = pl.BlockSpec((rows, 128), lambda s: (0, at(s)))
    held = (4, 2, 2, 2, 32, 3 * width + 128)
    return pl.pallas_call(
        first_kernel,
        grid=(pairs + 1,),
        in_specs=[
            pl.BlockSpec(memory_space=pltpu.SMEM),
            whole((rows, width)),
            ANY,
            whole(vec.shape),
            ANY,
            ANY,
            ANY,
            whole(head_scale.shape),
        ],
        out_specs=[
            whole((width, rows)),
            pl.BlockSpec((1, rows, 384), lambda s: (at(s), 0, 0)),
            column,
            pl.BlockSpec((128, rows), lambda s: (at(s), 0)),
            column,
            pl.BlockSpec((1, 8, rows), lambda s: (at(s), 0, 0)),
            whole((16, width)),
            whole((8, width)),
            ANY,
            ANY,
            ANY,
            ANY,
        ],
        out_shape=[
            jax.ShapeDtypeStruct((width, rows), BF),
            jax.ShapeDtypeStruct((pairs, rows, 384), BF),
            jax.ShapeDtypeStruct((rows, width), BF),
            jax.ShapeDtypeStruct((width, rows), BF),
            jax.ShapeDtypeStruct((rows, width), F32),
            jax.ShapeDtypeStruct((pairs, 8, rows), F32),
            jax.ShapeDtypeStruct((16, width), F32),
            jax.ShapeDtypeStruct((8, width), F32),
            jax.ShapeDtypeStruct(held, BF),
            jax.ShapeDtypeStruct((4, 2, 2, 2, *out_weight.shape), BF),
            jax.ShapeDtypeStruct((2, 2, 2, *up_weight.shape), BF),
            jax.ShapeDtypeStruct((2, 2, 2, *unit_rows.shape), BF),
        ],
        scratch_shapes=[
            pltpu.VMEM(held, BF),
            pltpu.VMEM((rows, width), F32),
            pltpu.VMEM((rows, width), BF),
            pltpu.VMEM((rows, 256), BF),
            *dma_sems(FullGather.copies),
            *dma_sems(FullGather.copies),
            *dma_sems(2 * WideGather.copies),
            pltpu.SemaphoreType.DMA((6,)),
        ],
        compiler_params=params(collective_id=0, has_side_effects=True),
        name="first_part",
    )(lengths, tokens, in_weight, vec, out_weight, up_weight, unit_rows, head_scale)


def second_kernel(
    units,
    scaled_ref,
    weight_ref,
    vec_ref,
    tokens_ref,
    up_ref,
    unit_ref,
    down_ref,
    branch_ref,
    middle_ref,
    turned_ref,
    act_ref,
    slope_ref,
    stats_ref,
    down_all,
    feed_ref,
    sums_ref,
    send,
    recv,
    local,
):
    step = pl.program_id(0)
    lead = feed_ref.shape[0] // TILE
    place = Place()
    down = WideGather(place, down_ref, down_all, send, recv, 0, local.at[0])

    @pl.when(step == 0)
    def _():
        place.greet(planes=False)
        down.start()
        sums_ref[...] = jnp.zeros_like(sums_ref)

    for stage, at in enumerate((5, 8, 11)):

        @pl.when(step == at)
        def _():
            down.relay(stage)

    @pl.when(step < lead)
    def _():
        rows = pl.ds(pl.multiple_of(step * TILE, TILE), TILE)
        feed_ref[rows] = out_proj_rows(
            scaled_ref, weight_ref, vec_ref, tokens_ref, branch_ref, middle_ref
        )

    @pl.when(step >= lead)
    def _():
        up_step(feed_ref, up_ref, unit_ref, act_ref, slope_ref, sums_ref)

    @pl.when(step == pl.num_programs(0) - 1)
    def _():
        up_stats(units, stats_ref, sums_ref)
        turned_ref[...] = feed_ref[...].T
        down.finish()


def second_part(scaled, out_weights, vectors, tokens, up, unit_vec, down_weight):
    rows, width = tokens.shape
    steps = up.shape[0]
    lead = rows // TILE

    def early(step):
        return jnp.minimum(step, lead - 1)

    def late(step):
        return jnp.maximum(step - lead, 0)

    by_row = pl.BlockSpec((TILE, width), lambda s: (early(s), 0))
    block = pl.BlockSpec((1, rows, UNITS), lambda s: (late(s), 0, 0))
    return pl.pallas_call(
        functools.partial(second_kernel, steps * UNITS),
        grid=(lead + steps,),
        in_specs=[
            by_row,
            whole((width, width)),
            whole(vectors.shape),
            by_row,
            pl.BlockSpec((1, width, UNITS), lambda s: (late(s), 0, 0)),
            pl.BlockSpec((1, unit_vec.shape[1], UNITS), lambda s: (late(s), 0, 0)),
            ANY,
        ],
        out_specs=[
            by_row,
            by_row,
            whole((width, rows)),
            block,
            block,
            whole((rows, 128)),
            ANY,
        ],
        out_shape=[
            jax.ShapeDtypeStruct((rows, width), F32),
            jax.ShapeDtypeStruct((rows, width), F32),
            jax.ShapeDtypeStruct((width, rows), BF),
            jax.ShapeDtypeStruct((steps, rows, UNITS), BF),
            jax.ShapeDtypeStruct((steps, rows, UNITS), BF),
            jax.ShapeDtypeStruct((rows, 128), F32),
            jax.ShapeDtypeStruct((2, 2, 2, *down_weight.shape), BF),
        ],
        scratch_shapes=[
            pltpu.VMEM((rows, width), BF),
            pltpu.VMEM((2, rows, 128), F32),
            *dma_sems(WideGather.copies),
            pltpu.SemaphoreType.DMA((1,)),
        ],
        compiler_params=params(collective_id=2, has_side_effects=True),
        name="second_part",
    )(scaled, out_weights, vectors, tokens, up, unit_vec, down_weight)


NORMS_AT, COLUMNS_AT, HEADS_AT, TOKENS_AT, LAST_CHUNK_AT = 8, 16, 20, 36, 40
BACK_STEPS = LAST_CHUNK_AT + 4 * LAG + 1
OUT_TILE = 128


def chunk_at(time):
    even = time % 2 == 0
    chunk = jnp.where(time < 8, time, (time + 24) // 4)
    chunk = jnp.where(time >= 16, (time + 4) // 2, chunk)
    chunk = jnp.where(time >= 20, time - 8, chunk)
    chunk = jnp.where(time >= 26, (time + 10) // 2, chunk)
    chunk = jnp.where(time == LAST_CHUNK_AT, 24, chunk)
    there = (time >= 0) & (
        (time < 8)
        | ((time < 16) & (time % 4 == 0))
        | ((time >= 16) & (time < 37) & even)
        | ((time >= 20) & (time < 26))
    )
    return chunk, there | (time == LAST_CHUNK_AT)


def back_kernel(
    lengths_ref,
    act_ref,
    slope_ref,
    e_ref,
    stats_ref,
    up_ref,
    feed_turned_ref,
    unit_grad_ref,
    down_grad_all,
    cot_ref,
    middle_ref,
    branch_ref,
    scaled_turned_ref,
    attended_ref,
    out_weight_ref,
    vec_ref,
    hs_ref,
    proj_ref,
    lse_ref,
    wq_ref,
    wk_ref,
    wv_ref,
    turned_ref,
    tokens_ref,
    tokens_grad_ref,
    down_out,
    up_out,
    attn_out,
    up_grad_all,
    staged_ref,
    total_ref,
    low_ref,
    out_grad_ref,
    ga_ref,
    grad_middle_ref,
    delta_ref,
    delta_sum_ref,
    sums_ref,
    units_ref,
    dq_ref,
    dk_ref,
    dv_ref,
    chunk_ref,
    store_sems,
    *scratch,
):
    step = pl.program_id(0)
    place = Place()
    engine = Reduction(place, scratch)

    @pl.when(step == 0)
    def _():
        place.greet()
        total_ref[...] = jnp.zeros_like(total_ref)
        sums_ref[...] = jnp.zeros_like(sums_ref)
        units_ref[...] = jnp.zeros_like(units_ref)

    def store(block):
        view = up_grad_all.at[block // 4, block // 2 % 2, block % 2]
        return pltpu.make_async_copy(staged_ref, view, store_sems.at[0])

    @pl.when((step >= 1) & (step <= NORMS_AT))
    def _():
        store(step - 1).wait()


    def stage(number, kind, action):
        chunk, there = chunk_at(step - number * LAG)
        up = ((chunk >= 8) & (chunk < 14)) | (chunk == 15) | (chunk == 17)
        wanted = {"all": there, "down": there & (chunk < 8), "up": there & up}
        wanted["shared"] = there & ((chunk < 8) | up)
        wanted["own"] = there & (chunk >= 8) & ~up

        @pl.when(wanted[kind])
        def _():
            action(chunk)

    def up_index(chunk):
        return jnp.where(chunk < 14, chunk - 8, (chunk - 3) // 2)

    def attn_index(chunk):
        return jnp.where(chunk < 18, (chunk - 14) // 2, chunk - 16)

    def put_down(chunk):
        for rank, block in engine.stage5(chunk):
            for half in range(2):

                @pl.when(chunk % 2 == half)
                def _():
                    down_out[chunk // 2, rank, :, half * 512 : half * 512 + 512] = block

    def put_up(chunk):
        for rank, block in engine.stage5(chunk):
            up_out[up_index(chunk), rank] = block

    def put_own(chunk):
        attn_out[attn_index(chunk)] = engine.stage4(chunk)

    def take_down(chunk):
        lanes = pl.ds(pl.multiple_of(chunk % 2 * 512, 512), 512)
        engine.stage0(chunk, down_grad_all.at[:, :, :, chunk // 2, :, :, lanes])

    def take_up(chunk):
        engine.stage0(chunk, up_grad_all.at[:, :, :, up_index(chunk)])

    def take_own(chunk):
        engine.stage0(chunk, chunk_ref.at[attn_index(chunk) % 2])

    stage(5, "down", put_down)
    stage(5, "up", put_up)
    stage(4, "shared", lambda chunk: engine.spread(chunk, engine.stage4(chunk)))
    stage(4, "own", put_own)
    stage(3, "all", engine.stage3)
    stage(2, "all", engine.stage2)
    stage(1, "all", engine.stage1)
    stage(0, "down", take_down)
    stage(0, "up", take_up)


    @pl.when(step < NORMS_AT)
    def _():
        units_ref[step, 0:1] = up_back_step(
            act_ref.at[0],
            slope_ref.at[0],
            e_ref.at[0],
            stats_ref,
            up_ref.at[0],
            low_ref,
            total_ref,
        )
        units_ref[step, 1:3] = unit_grad_ref[step, 0:2]
        for left in range(0, UNITS, TILE):
            columns = slice(left, left + TILE)
            grad = dot_nn(feed_turned_ref[...], low_ref[:, columns]).astype(BF)
            staged_ref[:, :, :, columns] = grad.reshape(8, 4, 32, TILE)
        store(step).start()


    @pl.when((step >= NORMS_AT) & (step < COLUMNS_AT))
    def _():
        rows = pl.ds(pl.multiple_of((step - NORMS_AT) * OUT_TILE, OUT_TILE), OUT_TILE)
        grad_middle, low = norms_back(
            total_ref[rows], cot_ref, middle_ref, branch_ref, vec_ref, sums_ref
        )
        grad_middle_ref[rows] = grad_middle
        low_ref[rows] = low

    @pl.when((step >= COLUMNS_AT) & (step < HEADS_AT))
    def _():
        block = step - COLUMNS_AT
        columns = pl.ds(pl.multiple_of(block * TILE, TILE), TILE)
        grad_out, delta = heads_back(
            low_ref[...], out_weight_ref[columns], hs_ref[0:1, columns], attended_ref[...]
        )
        ga_ref[:, columns] = grad_out
        delta_sum_ref[block, 0:1] = column_sum(delta)
        turned = delta.T
        for head in range(4):
            delta_ref[4 * block + head] = turned[head : head + 1]
        out_grad_ref[:, columns] = dot_nn(scaled_turned_ref[...], low_ref[:, columns]).astype(BF)

    @pl.when(step == HEADS_AT - 1)
    def _():
        total_ref[...] = jnp.zeros_like(total_ref)


    @pl.when((step >= HEADS_AT) & (step < TOKENS_AT))
    def _():
        index = step - HEADS_AT
        pair = index // 2
        columns = pl.ds(pl.multiple_of(pair * 128, 128), 128)
        for part, starts in enumerate(((0, 3 * TILE), (TILE, 2 * TILE))):

            @pl.when(index % 2 == part)
            def _():
                attention_back_keys(
                    starts,
                    cross_flag(lengths_ref, total_ref),
                    *three(proj_ref),
                    ga_ref.at[:, columns],
                    lse_ref,
                    [delta_ref[2 * pair], delta_ref[2 * pair + 1]],
                    dq_ref,
                    dk_ref,
                    dv_ref,
                )

        @pl.when(index % 2 == 1)
        def _():
            weights = jnp.concatenate([wq_ref[...], wk_ref[...], wv_ref[...]], axis=1)
            query_sum, value_sum = in_back_pair(
                dq_ref,
                dk_ref,
                dv_ref,
                weights,
                turned_ref,
                out_grad_ref.at[:, columns],
                chunk_ref.at[pair % 2].reshape(8, 4, 32, 512),
                total_ref,
            )
            sums_ref[0:1, columns] = query_sum
            sums_ref[1:2, columns] = value_sum

    @pl.when((step >= TOKENS_AT) & (step < TOKENS_AT + 4))
    def _():
        rows = pl.ds(pl.multiple_of((step - TOKENS_AT) * TILE, TILE), TILE)
        tokens_grad_ref[...], gain_grad, shift_grad = tokens_back(
            tokens_ref[...], total_ref[rows], grad_middle_ref[rows], vec_ref[3:4]
        )
        sums_ref[3:4] += gain_grad
        sums_ref[4:5] += shift_grad

    @pl.when(step == LAST_CHUNK_AT)
    def _():
        for y in range(2):
            for x in range(2):
                for c in range(2):
                    unit = 4 * y + 2 * x + c
                    units_ref[unit, 3:4] = sums_ref[9:10, 0:UNITS]
                    units_ref[unit, 4:5] = sums_ref[9:10, UNITS : 2 * UNITS]
                    for block in range(4):
                        units_ref[unit, 5 + block : 6 + block, 0:128] = delta_sum_ref[block, 0:1]
                    top = units_ref[unit].astype(BF)
                    for z in range(4):
                        start = (2 * z + y) * 128
                        chunk_ref[0, y, x, c, z, 0:16] = top
                        chunk_ref[0, y, x, c, z, 16:32, 0:128] = sums_ref[
                            :, start : start + 128
                        ].astype(BF)

    stage(0, "own", take_own)


def back_part(
    lengths,
    act,
    slope,
    e,
    stats,
    up,
    feed_turned,
    unit_grad,
    down_grad,
    cotangent,
    middle,
    branch,
    scaled_turned,
    attended,
    out_weights,
    vectors,
    head_lanes,
    projected,
    lse,
    weights,
    turned,
    tokens,
):
    rows, width = tokens.shape
    pairs = width // 128

    def clamp(value, high):
        return jnp.minimum(jnp.maximum(value, 0), high)

    def unit(s):
        return clamp(s, 7)

    def pair(s):
        return clamp((s - HEADS_AT) // 2, pairs - 1)

    def tail(s):
        return clamp(s - TOKENS_AT, 3)

    block = pl.BlockSpec((1, rows, UNITS), lambda s: (unit(s), 0, 0))
    narrow = whole((rows, 128))
    by_row = pl.BlockSpec((OUT_TILE, width), lambda s: (clamp(s - NORMS_AT, 7), 0))
    square = whole((width, width))
    return pl.pallas_call(
        back_kernel,
        grid=(BACK_STEPS,),
        in_specs=[
            pl.BlockSpec(memory_space=pltpu.SMEM),
            block,
            block,
            block,
            narrow,
            pl.BlockSpec((1, width, UNITS), lambda s: (unit(s), 0, 0)),
            square,
            whole(unit_grad.shape),
            ANY,
            by_row,
            by_row,
            by_row,
            square,
            pl.BlockSpec((rows, TILE), lambda s: (0, clamp(s - COLUMNS_AT, 3))),
            square,
            whole(vectors.shape),
            whole(head_lanes.shape),
            pl.BlockSpec((1, rows, 384), lambda s: (pair(s), 0, 0)),
            pl.BlockSpec((1, 8, rows), lambda s: (pair(s), 0, 0)),
            pl.BlockSpec((width, 128), lambda s: (0, pair(s))),
            pl.BlockSpec((width, 128), lambda s: (0, pairs + pair(s))),
            pl.BlockSpec((width, 128), lambda s: (0, 2 * pairs + pair(s))),
            square,
            pl.BlockSpec((TILE, width), lambda s: (tail(s), 0)),
        ],
        out_specs=[
            pl.BlockSpec((TILE, width), lambda s: (tail(s), 0)),
            whole((4, 4, 32, 1024)),
            whole((8, 4, 32, 512)),
            whole((9, 32, 512)),
            ANY,
        ],
        out_shape=[
            jax.ShapeDtypeStruct((rows, width), BF),
            jax.ShapeDtypeStruct((4, 4, 32, 1024), BF),
            jax.ShapeDtypeStruct((8, 4, 32, 512), BF),
            jax.ShapeDtypeStruct((9, 32, 512), F32),
            jax.ShapeDtypeStruct((2, 2, 2, 8, 4, 32, UNITS), BF),
        ],
        scratch_shapes=[
            pltpu.VMEM((8, 4, 32, UNITS), BF),
            pltpu.VMEM((rows, width), F32),
            pltpu.VMEM((rows, width), BF),
            pltpu.VMEM((width, width), BF),
            pltpu.VMEM((rows, width), BF),
            pltpu.VMEM((rows, width), F32),
            pltpu.VMEM((2 * pairs, 1, rows), F32),
            pltpu.VMEM((4, 8, 128), F32),
            pltpu.VMEM((16, width), F32),
            pltpu.VMEM((8, 16, UNITS), F32),
            pltpu.VMEM((rows, 128), F32),
            pltpu.VMEM((rows, 128), F32),
            pltpu.VMEM((rows, 128), F32),
            pltpu.VMEM((2, 2, 2, 2, 4, 32, 512), BF),
            pltpu.SemaphoreType.DMA((1,)),
            *Reduction.scratch(),
        ],
        compiler_params=params(collective_id=1, has_side_effects=True),
        name="back_part",
    )(
        lengths,
        act,
        slope,
        e,
        stats,
        up,
        feed_turned,
        unit_grad,
        down_grad.reshape(2, 2, 2, 4, 4, 32, width),
        cotangent,
        middle,
        branch,
        scaled_turned,
        attended,
        out_weights,
        vectors,
        head_lanes,
        projected,
        lse,
        weights,
        weights,
        weights,
        turned,
        tokens,
    )


def layer(staged, tokens, cotangent, lengths, attn, up, down, unit_vec, head_scale, down_bias):
    rows, width = tokens.shape
    heads = head_scale.shape[0]
    pairs = width // 128
    if staged:
        in_weight, out_weight, vec_block = attn
        (
            turned,
            projected,
            scaled,
            scaled_turned,
            attended,
            lse,
            vectors,
            head_lanes,
            weights,
            out_weights,
            up,
            unit_vec,
        ) = first_part(
            lengths, tokens, in_weight, vec_block, out_weight, up, unit_vec, head_scale[None, :]
        )
        weights = weights.reshape(width, 3 * width + 128)
        out_weights = out_weights.reshape(width, width)
        up = up.reshape(-1, width, UNITS)
        unit_vec = unit_vec.reshape(-1, unit_vec.shape[-2], UNITS)
        branch, middle, feed_turned, act, slope, stats, down = second_part(
            scaled, out_weights, vectors, tokens, up, unit_vec, down
        )
        down = down.reshape(-1, UNITS, width)
    else:
        weights, out_weights, vectors = attn
        scale = head_scale.astype(F32)
        head_lanes = jnp.repeat(scale, width // heads)[None, :]
        first, projected, scaled, attended, lse = plain_first(
            lengths, tokens, weights, vectors, head_lanes
        )
        branch, middle, feed = out_proj(scaled, out_weights, vectors, tokens)
        act, slope, stats = up_pass(feed, up, unit_vec)
    mixed, down_grad, e, stats, unit_grad = down_pass(
        act, stats, unit_vec, down, cotangent, middle, down_bias[None, :]
    )
    if staged:
        tokens_grad, down_total, up_total, shares, _ = back_part(
            lengths,
            act,
            slope,
            e,
            stats,
            up,
            feed_turned,
            unit_grad,
            down_grad,
            cotangent,
            middle,
            branch,
            scaled_turned,
            attended,
            out_weights,
            vectors,
            head_lanes,
            projected,
            lse,
            weights,
            turned,
            tokens,
        )
        return mixed, tokens_grad, down_total, up_total, shares
    up_grad, up_bias_grad, grad_feed = up_back(
        act, slope, e, stats, up, feed
    )
    grad_middle, ga, out_grad, delta, sums = out_back(
        grad_feed,
        cotangent,
        middle,
        branch,
        scaled,
        attended,
        out_weights,
        vectors,
        head_lanes,
    )
    chunks, proj_bias, tokens_grad, pre_sums = in_back(
        lengths,
        projected,
        ga,
        lse,
        delta.reshape(pairs, 2, rows),
        weights,
        first,
        out_grad,
        tokens,
        vectors[3:4],
        grad_middle,
    )
    scale_grad = jnp.sum(delta, axis=1) / scale
    vec_grads = [
        proj_bias[:, 0].reshape(width),
        proj_bias[:, 1].reshape(width),
        sums[2],
        pre_sums[0],
        pre_sums[1],
        sums[5],
        sums[6],
        sums[7],
        sums[8],
    ]
    unit_grads = [up_bias_grad[:, 0], unit_grad[:, 0], unit_grad[:, 1]]
    return mixed, tokens_grad, chunks, up_grad, down_grad, vec_grads, unit_grads, sums[9], scale_grad


def body(
    axes,
    tokens,
    cotangent,
    lengths,
    in_weight,
    query_bias,
    value_bias,
    out_weight,
    out_bias,
    head_scale,
    pre_gain,
    pre_bias,
    post_gain,
    post_bias,
    feed_gain,
    feed_bias,
    up_weight,
    up_bias,
    mid_gain,
    mid_bias,
    down_weight,
    down_bias,
):
    planes, wide = axes
    every = ("dp", "wide")
    staged = (planes, wide) == (4, 8)
    rows, width = tokens.shape
    units = down_weight.shape[0] * wide
    steps = units // UNITS
    share = in_weight.shape[0]
    columns = [
        query_bias,
        value_bias,
        out_bias,
        pre_gain,
        pre_bias,
        post_gain,
        post_bias,
        feed_gain,
        feed_bias,
    ]
    index = lax.broadcasted_iota(jnp.int32, (32, up_bias.shape[0]), 0)
    unit_rows = jnp.where(index == 0, up_bias[None, :], jnp.zeros((), BF))
    unit_rows = jnp.where(index == 1, mid_gain[None, :], unit_rows)
    unit_rows = jnp.where(index == 2, mid_bias[None, :], unit_rows)
    if staged:
        index = lax.broadcasted_iota(jnp.int32, (32, share), 0)
        vec_block = jnp.zeros((32, share), BF)
        for row, column in enumerate(columns):
            vec_block = jnp.where(index == row, column[None, :], vec_block)
        attn = (in_weight, out_weight, vec_block)
        up, unit_vec, down = up_weight, unit_rows, down_weight
    else:
        flat = jnp.concatenate(columns).reshape(len(columns), share)
        attn = (
            lax.all_gather(in_weight, every, axis=0, tiled=True),
            lax.all_gather(out_weight, every, axis=0, tiled=True),
            jnp.pad(
                lax.all_gather(flat, every, axis=1, tiled=True), ((0, 16 - len(columns)), (0, 0))
            ).astype(F32),
        )
        up = lax.all_gather(up_weight, "wide", axis=1, tiled=True)
        up = up.reshape(width, steps, UNITS).transpose(1, 0, 2)
        unit_vec = lax.all_gather(unit_rows, "wide", axis=1, tiled=True)
        unit_vec = unit_vec.reshape(32, steps, UNITS).transpose(1, 0, 2)
        down = lax.all_gather(down_weight, "wide", axis=0, tiled=True)
        down = down.reshape(steps, UNITS, width)
    results = layer(
        staged,
        tokens,
        cotangent,
        lengths,
        attn,
        up,
        down,
        unit_vec,
        head_scale,
        down_bias,
    )
    heads = head_scale.shape[0]
    pairs = width // 128
    if staged:
        mixed, tokens_grad, down_total, up_total, shares = results
        up_total = up_total.astype(F32).reshape(width, UNITS)
        down_total = down_total.astype(F32).reshape(UNITS, width)
        unit_totals = [shares[8, index] for index in range(3)]
        down_sum = jnp.concatenate([shares[8, 3], shares[8, 4]])
        scale_sum = shares[8, 5:9, :4].reshape(heads) / head_scale.astype(F32)
        offset = share * lax.rem(lax.axis_index("wide"), 128 // share)
        own = lax.dynamic_slice(shares, (8, 16, offset), (1, len(columns), share))[0]
        vec_totals = [own[index] for index in range(len(columns))]
        in_total = shares[:pairs, :, :384].reshape(pairs, share, 3, 128)
        in_total = in_total.transpose(1, 2, 0, 3).reshape(share, 3 * width)
        out_total = shares[:pairs, :, 384:].transpose(1, 0, 2).reshape(share, width)
    else:
        (mixed, tokens_grad, chunks, up_grad, down_grad, vec_grads, unit_grads) = results[:7]
        down_sum, scale_sum = results[7:]

        def scatter(value, axis=0, over=every):
            return lax.psum_scatter(value, over, scatter_dimension=axis, tiled=True)

        def both_ways(value, axis):
            part = scatter(value.astype(BF), axis, "wide")
            return lax.psum(part, "dp").astype(F32)

        up_total = both_ways(up_grad.transpose(1, 0, 2).reshape(width, units), 1)
        down_total = both_ways(down_grad.reshape(units, width), 0)
        unit_totals = [
            lax.psum(scatter(item.reshape(units), 0, "wide"), "dp") for item in unit_grads
        ]
        down_sum, scale_sum = lax.psum((down_sum, scale_sum), every)
        vec_totals = [scatter(item) for item in vec_grads]
        natural = chunks.transpose(0, 2, 1, 3, 4).reshape(pairs, width, 512)
        in_total = natural[:, :, :384].reshape(pairs, width, 3, 128)
        in_total = scatter(in_total.transpose(1, 2, 0, 3).reshape(width, 3 * width).astype(F32))
        out_total = scatter(
            natural[:, :, 384:].transpose(1, 0, 2).reshape(width, width).astype(F32)
        )
    return (
        mixed,
        tokens_grad,
        in_total,
        vec_totals[0],
        vec_totals[1],
        out_total,
        vec_totals[2],
        scale_sum,
        vec_totals[3],
        vec_totals[4],
        vec_totals[5],
        vec_totals[6],
        vec_totals[7],
        vec_totals[8],
        up_total,
        unit_totals[0],
        unit_totals[1],
        unit_totals[2],
        down_total,
        down_sum,
    )


def solution(mesh):
    by_all = P(("dp", "wide"))
    rows_all = P(("dp", "wide"), None)
    axes = (mesh.shape["dp"], mesh.shape["wide"])
    return jax.shard_map(
        functools.partial(body, axes),
        mesh=mesh,
        in_specs=(
            rows_all,
            rows_all,
            rows_all,
            rows_all,
            by_all,
            by_all,
            rows_all,
            by_all,
            P(),
            by_all,
            by_all,
            by_all,
            by_all,
            by_all,
            by_all,
            P(None, "wide"),
            P("wide"),
            P("wide"),
            P("wide"),
            P("wide", None),
            P(),
        ),
        out_specs=(
            rows_all,
            rows_all,
            rows_all,
            by_all,
            by_all,
            rows_all,
            by_all,
            P(),
            by_all,
            by_all,
            by_all,
            by_all,
            by_all,
            by_all,
            P(None, "wide"),
            P("wide"),
            P("wide"),
            P("wide"),
            P("wide", None),
            P(),
        ),
        check_vma=False,
    )
```

```python
import functools

import jax
import jax.numpy as jnp
from jax import lax
from jax.experimental import pallas as pl
from jax.experimental.pallas import tpu as pltpu
from jax.sharding import PartitionSpec as P

EPS = 1e-05
ROOT_HALF = 0.7071067811865476
INV_ROOT_TAU = 0.3989422804014327
LOG2E = 1.4426950408889634
MASKED = -1e30
BF = jnp.bfloat16
F32 = jnp.float32
TILE = 256
UNITS = 512
SLIM = 64
MESH = pl.DeviceIdType.MESH
VMEM_LIMIT = 62 * 1024 * 1024
ANY = pl.BlockSpec(memory_space=pl.ANY)


def dot_nn(left, right):
    return lax.dot_general(left, right, (((1,), (0,)), ((), ())), preferred_element_type=F32)


def dot_nt(left, right):
    return lax.dot_general(left, right, (((1,), (1,)), ((), ())), preferred_element_type=F32)


def dot_tn(left, right):
    return lax.dot_general(left, right, (((0,), (0,)), ((), ())), preferred_element_type=F32)


def params(**more):
    return pltpu.CompilerParams(
        dimension_semantics=("arbitrary",), vmem_limit_bytes=VMEM_LIMIT, **more
    )


def whole(shape):
    zeros = (0,) * len(shape)
    return pl.BlockSpec(shape, lambda *_: zeros, pipeline_mode=pl.Buffered(1))


def row_norm(values):
    center = values - jnp.mean(values, axis=-1, keepdims=True)
    inv = lax.rsqrt(jnp.mean(center * center, axis=-1, keepdims=True) + EPS)
    return center * inv, inv


def norm_back(grad, gain, normed, inv):
    scaled = grad * gain
    first = jnp.mean(scaled, axis=-1, keepdims=True)
    cross = jnp.mean(scaled * normed, axis=-1, keepdims=True)
    return inv * (scaled - first - normed * cross)


def column_sum(values):
    return jnp.sum(values, axis=0, keepdims=True)


def lane_fold(values):
    total = values[:, :128]
    for start in range(128, values.shape[1], 128):
        total = total + values[:, start : start + 128]
    return total


def cross_flag(lengths_ref, rows_ref):
    return jnp.where(lengths_ref[0, 0] == rows_ref.shape[0], 0.0, MASKED)


def stacked(value, low_lanes):
    zero = jnp.zeros_like(value)
    return jnp.concatenate(
        [jnp.where(low_lanes, value, zero), jnp.where(low_lanes, zero, value)], axis=0
    )


def attention_pair(cross, q_ref, k_ref, v_ref, scale, scaled_ref, out_ref, lse_ref, vext_ref):
    rows = q_ref.shape[0]
    half = rows // 2
    factor = LOG2E * 64 ** (-0.5)
    low_lanes = lax.broadcasted_iota(jnp.int32, (1, 128), 1) < 64
    below = lax.broadcasted_iota(jnp.int32, (TILE, TILE), 1) <= lax.broadcasted_iota(
        jnp.int32, (TILE, TILE), 0
    )
    vext_ref[:, :128] = v_ref[...]
    vext_ref[:, 128:] = jnp.ones((rows, 128), BF)
    for start in range(0, rows, TILE):
        stop = start + TILE
        both = dot_nt(stacked(q_ref[start:stop], low_lanes), k_ref[:stop])
        peaks, weights = [], []
        for head in range(2):
            raw = both[head * TILE : (head + 1) * TILE]
            parts = []
            if start >= half:
                parts.append((raw[:, :half], cross))
                if start > half:
                    parts.append((raw[:, half:start], None))
            elif start > 0:
                parts.append((raw[:, :start], None))
            parts.append((jnp.where(below, raw[:, start:stop], MASKED), None))
            peak = None
            for piece, shift in parts:
                top = jnp.max(piece, axis=-1, keepdims=True)
                if shift is not None:
                    top = top + shift
                peak = top if peak is None else jnp.maximum(peak, top)
            peaks.append(peak)
            pieces = []
            for piece, shift in parts:
                level = peak if shift is None else peak - shift
                pieces.append(jnp.exp2((piece - level) * factor).astype(BF))
            weights.append(pieces[0] if len(pieces) == 1 else jnp.concatenate(pieces, axis=1))
        both = dot_nn(jnp.concatenate(weights, axis=0), vext_ref[:stop])
        total = jnp.where(low_lanes, both[:TILE, 128:], both[TILE:, 128:])
        peak = jnp.where(low_lanes, peaks[0], peaks[1])
        mixed = jnp.where(low_lanes, both[:TILE, :128], both[TILE:, :128]) / total
        out_ref[start:stop] = mixed
        scaled_ref[start:stop] = (mixed * scale).astype(BF)
        lse = (peak * factor + jnp.log2(total)).T
        lse_ref[0, 0:1, start:stop] = lse[0:1]
        lse_ref[0, 1:2, start:stop] = lse[64:65]


def project_pair(first_ref, weights, bias, proj_ref):
    proj_ref[0] = (dot_nn(first_ref[...], weights) + bias).astype(BF)


def three(proj_ref):
    return [proj_ref.at[0, :, pl.ds(part * 128, 128)] for part in range(3)]


def plain_first_kernel(
    lengths_ref,
    tokens_ref,
    wq_ref,
    wk_ref,
    wv_ref,
    vectors_ref,
    bq_ref,
    bv_ref,
    hs_ref,
    first_ref,
    proj_ref,
    scaled_ref,
    attended_ref,
    lse_ref,
    vext_ref,
):
    @pl.when(pl.program_id(0) == 0)
    def _():
        for start in range(0, tokens_ref.shape[0], TILE):
            rows = pl.ds(start, TILE)
            normed, _ = row_norm(tokens_ref[rows].astype(F32))
            first_ref[rows] = (normed * vectors_ref[3:4] + vectors_ref[4:5]).astype(BF)

    weights = jnp.concatenate([wq_ref[...], wk_ref[...], wv_ref[...]], axis=1)
    bias = jnp.concatenate([bq_ref[0:1], jnp.zeros((1, 128), F32), bv_ref[1:2]], axis=1)
    project_pair(first_ref, weights, bias, proj_ref)
    attention_pair(
        cross_flag(lengths_ref, tokens_ref), *three(proj_ref), hs_ref[...], scaled_ref, attended_ref, lse_ref, vext_ref
    )


def plain_first(lengths, tokens, weights, vectors, head_lanes):
    rows, width = tokens.shape
    pairs = width // 128
    column = pl.BlockSpec((rows, 128), lambda p: (0, p))
    bias = pl.BlockSpec((16, 128), lambda p: (0, p))
    return pl.pallas_call(
        plain_first_kernel,
        grid=(pairs,),
        in_specs=[
            pl.BlockSpec(memory_space=pltpu.SMEM),
            whole((rows, width)),
            pl.BlockSpec((width, 128), lambda p: (0, p)),
            pl.BlockSpec((width, 128), lambda p: (0, pairs + p)),
            pl.BlockSpec((width, 128), lambda p: (0, 2 * pairs + p)),
            whole(vectors.shape),
            bias,
            bias,
            pl.BlockSpec((1, 128), lambda p: (0, p)),
        ],
        out_specs=[
            whole((rows, width)),
            pl.BlockSpec((1, rows, 384), lambda p: (p, 0, 0)),
            column,
            column,
            pl.BlockSpec((1, 8, rows), lambda p: (p, 0, 0)),
        ],
        out_shape=[
            jax.ShapeDtypeStruct((rows, width), BF),
            jax.ShapeDtypeStruct((pairs, rows, 384), BF),
            jax.ShapeDtypeStruct((rows, width), BF),
            jax.ShapeDtypeStruct((rows, width), F32),
            jax.ShapeDtypeStruct((pairs, 8, rows), F32),
        ],
        scratch_shapes=[pltpu.VMEM((rows, 256), BF)],
        compiler_params=params(),
        name="plain_first",
    )(lengths, tokens, weights, weights, weights, vectors, vectors, vectors, head_lanes)


def out_proj_rows(scaled_ref, weight_ref, vec_ref, tokens_ref, branch_ref, middle_ref):
    branch = dot_nn(scaled_ref[...], weight_ref[...]) + vec_ref[2:3]
    normed, _ = row_norm(branch)
    middle = tokens_ref[...].astype(F32) + (normed * vec_ref[5:6] + vec_ref[6:7])
    again, _ = row_norm(middle)
    branch_ref[...] = branch
    middle_ref[...] = middle
    return (again * vec_ref[7:8] + vec_ref[8:9]).astype(BF)


def out_proj_kernel(scaled_ref, weight_ref, vec_ref, tokens_ref, branch_ref, middle_ref, feed_ref):
    feed_ref[...] = out_proj_rows(
        scaled_ref, weight_ref, vec_ref, tokens_ref, branch_ref, middle_ref
    )


def out_proj(scaled, weights, vectors, tokens):
    rows, width = tokens.shape
    by_row = pl.BlockSpec((TILE, width), lambda i: (i, 0))
    return pl.pallas_call(
        out_proj_kernel,
        grid=(rows // TILE,),
        in_specs=[
            by_row,
            whole((width, width)),
            whole(vectors.shape),
            by_row,
        ],
        out_specs=[by_row, by_row, by_row],
        out_shape=[
            jax.ShapeDtypeStruct((rows, width), F32),
            jax.ShapeDtypeStruct((rows, width), F32),
            jax.ShapeDtypeStruct((rows, width), BF),
        ],
        compiler_params=params(),
        name="out_proj",
    )(scaled, weights, vectors, tokens)


def phi_and_slope(value):
    bell = jnp.exp2(value * value * (-0.5 * LOG2E))
    t = 1.0 / (1.0 + (0.3275911 * ROOT_HALF) * jnp.abs(value))
    series = t * (
        0.5 * 0.254829592
        + t
        * (
            0.5 * -0.284496736
            + t * (0.5 * 1.421413741 + t * (0.5 * -1.453152027 + t * (0.5 * 1.061405429)))
        )
    )
    tail = series * bell
    area = jnp.where(value < 0.0, tail, 1.0 - tail)
    return value * area, area + value * bell * INV_ROOT_TAU


def up_step(feed_ref, up_ref, vec_ref, act_ref, slope_ref, sums_ref):
    for left in range(0, UNITS, TILE):
        columns = slice(left, left + TILE)
        pre = dot_nn(feed_ref[...], up_ref[0, :, columns])
        bias = vec_ref[0, 0:1, columns].astype(F32)
        for start in range(0, feed_ref.shape[0], SLIM):
            rows = slice(start, start + SLIM)
            act, slope = phi_and_slope(pre[rows] + bias)
            act_ref[0, rows, columns] = act.astype(BF)
            slope_ref[0, rows, columns] = slope.astype(BF)
            sums_ref[0, rows] += lane_fold(act)
            sums_ref[1, rows] += lane_fold(act * act)


def side_by_side(*columns):
    lane = lax.broadcasted_iota(jnp.int32, (1, 128), 1)
    result = jnp.broadcast_to(columns[-1], (columns[-1].shape[0], 128))
    for index in range(len(columns) - 2, -1, -1):
        result = jnp.where(lane == index, columns[index], result)
    return result


def up_stats(units, stats_ref, sums_ref):
    for start in range(0, stats_ref.shape[0], TILE):
        rows = pl.ds(start, TILE)
        mean = jnp.sum(sums_ref[0, rows], axis=1, keepdims=True) / units
        square = jnp.sum(sums_ref[1, rows], axis=1, keepdims=True) / units
        inv = lax.rsqrt(square - mean * mean + EPS)
        stats_ref[rows] = side_by_side(mean, inv)


def up_kernel(units, feed_ref, up_ref, vec_ref, act_ref, slope_ref, stats_ref, sums_ref):
    step = pl.program_id(0)

    @pl.when(step == 0)
    def _():
        sums_ref[...] = jnp.zeros_like(sums_ref)

    up_step(feed_ref, up_ref, vec_ref, act_ref, slope_ref, sums_ref)

    @pl.when(step == pl.num_programs(0) - 1)
    def _():
        up_stats(units, stats_ref, sums_ref)


def up_pass(feed, up, vec):
    rows, width = feed.shape
    steps = up.shape[0]
    block = pl.BlockSpec((1, rows, UNITS), lambda j: (j, 0, 0))
    return pl.pallas_call(
        functools.partial(up_kernel, steps * UNITS),
        grid=(steps,),
        in_specs=[
            whole((rows, width)),
            pl.BlockSpec((1, width, UNITS), lambda j: (j, 0, 0)),
            pl.BlockSpec((1, vec.shape[1], UNITS), lambda j: (j, 0, 0)),
        ],
        out_specs=[block, block, whole((rows, 128))],
        out_shape=[
            jax.ShapeDtypeStruct((steps, rows, UNITS), BF),
            jax.ShapeDtypeStruct((steps, rows, UNITS), BF),
            jax.ShapeDtypeStruct((rows, 128), F32),
        ],
        scratch_shapes=[pltpu.VMEM((2, rows, 128), F32)],
        compiler_params=params(),
        name="up_pass",
    )(feed, up, vec)


def down_kernel(
    units,
    act_ref,
    stats_ref,
    vec_ref,
    down_ref,
    cot_ref,
    middle_ref,
    shift_ref,
    mixed_ref,
    down_grad_ref,
    e_ref,
    all_stats_ref,
    vec_grad_ref,
    total_ref,
    sums_ref,
    low_ref,
):
    step = pl.program_id(0)
    last = pl.num_programs(0) - 1
    rows_all = cot_ref.shape[0]

    @pl.when(step == 0)
    def _():
        total_ref[...] = jnp.zeros_like(total_ref)
        sums_ref[...] = jnp.zeros_like(sums_ref)

    gain = vec_ref[0, 1:2].astype(F32)
    shift = vec_ref[0, 2:3].astype(F32)
    slims = [slice(start, start + SLIM) for start in range(0, rows_all, SLIM)]

    def normalized(rows, columns):
        value = act_ref[0, rows, columns].astype(F32)
        return (value - stats_ref[rows, 0:1]) * stats_ref[rows, 1:2]

    for rows in slims:
        low_ref[rows] = (normalized(rows, slice(0, UNITS)) * gain + shift).astype(BF)
    for left in range(0, UNITS, TILE):
        columns = slice(left, left + TILE)
        grads = dot_nt(cot_ref[...], down_ref[0, columns])
        gain_grad = jnp.zeros((SLIM, TILE), F32)
        bias_grad = jnp.zeros((SLIM, TILE), F32)
        for rows in slims:
            normed = normalized(rows, columns)
            grad = grads[rows]
            gain_grad = gain_grad + grad * normed
            bias_grad = bias_grad + grad
            e = grad * gain[:, columns]
            e_ref[0, rows, columns] = e.astype(BF)
            sums_ref[0, rows] += lane_fold(e)
            sums_ref[1, rows] += lane_fold(e * normed)
        vec_grad_ref[0, 0:1, columns] = column_sum(gain_grad)
        vec_grad_ref[0, 1:2, columns] = column_sum(bias_grad)
    for left in range(0, total_ref.shape[1], TILE):
        columns = slice(left, left + TILE)
        total_ref[:, columns] += dot_nn(low_ref[...], down_ref[0, :, columns])
    for left in range(0, UNITS, TILE):
        columns = slice(left, left + TILE)
        down_grad_ref[0, columns] = dot_tn(low_ref[:, columns], cot_ref[...]).astype(BF)

    @pl.when(step == last)
    def _():
        for start in range(0, rows_all, TILE):
            rows = pl.ds(start, TILE)
            mixed_ref[rows] = (
                middle_ref[rows] + total_ref[rows] + shift_ref[...].astype(F32)
            ).astype(BF)
            first = jnp.sum(sums_ref[0, rows], axis=1, keepdims=True) / units
            cross = jnp.sum(sums_ref[1, rows], axis=1, keepdims=True) / units
            all_stats_ref[rows] = side_by_side(
                stats_ref[rows, 0:1], stats_ref[rows, 1:2], first, cross
            )


def down_pass(act, stats, vec, down, cotangent, middle, shift):
    rows, width = cotangent.shape
    steps = act.shape[0]
    block = pl.BlockSpec((1, rows, UNITS), lambda j: (j, 0, 0))
    return pl.pallas_call(
        functools.partial(down_kernel, steps * UNITS),
        grid=(steps,),
        in_specs=[
            block,
            whole((rows, 128)),
            pl.BlockSpec((1, vec.shape[1], UNITS), lambda j: (j, 0, 0)),
            pl.BlockSpec((1, UNITS, width), lambda j: (j, 0, 0)),
            whole((rows, width)),
            whole((rows, width)),
            whole((1, width)),
        ],
        out_specs=[
            whole((rows, width)),
            pl.BlockSpec((1, UNITS, width), lambda j: (j, 0, 0)),
            block,
            whole((rows, 128)),
            pl.BlockSpec((1, 8, UNITS), lambda j: (j, 0, 0)),
        ],
        out_shape=[
            jax.ShapeDtypeStruct((rows, width), BF),
            jax.ShapeDtypeStruct((steps, UNITS, width), BF),
            jax.ShapeDtypeStruct((steps, rows, UNITS), BF),
            jax.ShapeDtypeStruct((rows, 128), F32),
            jax.ShapeDtypeStruct((steps, 8, UNITS), F32),
        ],
        scratch_shapes=[
            pltpu.VMEM((rows, width), F32),
            pltpu.VMEM((2, rows, 128), F32),
            pltpu.VMEM((rows, UNITS), BF),
        ],
        compiler_params=params(),
        name="down_pass",
    )(act, stats, vec, down, cotangent, middle, shift)


def up_back_step(act, slope, e, stats_ref, up, low_ref, total_ref):
    bias_grad = jnp.zeros((SLIM, UNITS), F32)
    for start in range(0, total_ref.shape[0], SLIM):
        rows = slice(start, start + SLIM)
        inv = stats_ref[rows, 1:2]
        normed = (act[rows].astype(F32) - stats_ref[rows, 0:1]) * inv
        grad_act = inv * (
            e[rows].astype(F32) - stats_ref[rows, 2:3] - normed * stats_ref[rows, 3:4]
        )
        low = (grad_act * slope[rows].astype(F32)).astype(BF)
        bias_grad = bias_grad + low.astype(F32)
        low_ref[rows, 0:UNITS] = low
    for left in range(0, total_ref.shape[1], TILE):
        columns = slice(left, left + TILE)
        total_ref[:, columns] += dot_nt(low_ref[:, 0:UNITS], up[columns])
    return column_sum(bias_grad)


def up_back_kernel(
    act_ref,
    slope_ref,
    e_ref,
    stats_ref,
    up_ref,
    feed_ref,
    up_grad_ref,
    bias_grad_ref,
    total_ref,
    turned_ref,
    low_ref,
):
    @pl.when(pl.program_id(0) == 0)
    def _():
        total_ref[...] = jnp.zeros_like(total_ref)
        turned_ref[...] = feed_ref[...].T

    bias_grad_ref[0, 0:1] = up_back_step(
        act_ref.at[0],
        slope_ref.at[0],
        e_ref.at[0],
        stats_ref,
        up_ref.at[0],
        low_ref,
        total_ref,
    )
    up_grad_ref[0] = dot_nn(turned_ref[...], low_ref[...]).astype(BF)


def up_back(act, slope, e, stats, up, feed):
    rows, width = feed.shape
    steps = act.shape[0]
    block = pl.BlockSpec((1, rows, UNITS), lambda j: (j, 0, 0))
    narrow = whole((rows, 128))
    return pl.pallas_call(
        up_back_kernel,
        grid=(steps,),
        in_specs=[
            block,
            block,
            block,
            narrow,
            pl.BlockSpec((1, width, UNITS), lambda j: (j, 0, 0)),
            whole((rows, width)),
        ],
        out_specs=[
            pl.BlockSpec((1, width, UNITS), lambda j: (j, 0, 0)),
            pl.BlockSpec((1, 8, UNITS), lambda j: (j, 0, 0)),
            whole((rows, width)),
        ],
        out_shape=[
            jax.ShapeDtypeStruct((steps, width, UNITS), BF),
            jax.ShapeDtypeStruct((steps, 8, UNITS), F32),
            jax.ShapeDtypeStruct((rows, width), F32),
        ],
        scratch_shapes=[pltpu.VMEM((width, rows), BF), pltpu.VMEM((rows, UNITS), BF)],
        compiler_params=params(),
        name="up_back",
    )(act, slope, e, stats, up, feed)


def norms_back(grad_feed, cot_ref, middle_ref, branch_ref, vec_ref, sums_ref):
    normed, inv = row_norm(middle_ref[...])
    cot = cot_ref[...].astype(F32)
    grad_middle = cot + norm_back(grad_feed, vec_ref[7:8], normed, inv)
    sums_ref[7:8] += column_sum(grad_feed * normed)
    sums_ref[8:9] += column_sum(grad_feed)
    sums_ref[9:10] += column_sum(cot)
    normed, inv = row_norm(branch_ref[...])
    low = norm_back(grad_middle, vec_ref[5:6], normed, inv).astype(BF)
    sums_ref[5:6] += column_sum(grad_middle * normed)
    sums_ref[6:7] += column_sum(grad_middle)
    sums_ref[2:3] += column_sum(low.astype(F32))
    return grad_middle, low


def heads_back(low, weights, scale, attended):
    grad_out = (dot_nt(low, weights) * scale).astype(BF)
    product = grad_out.astype(F32) * attended
    high = product.astype(BF)
    rest = (product - high.astype(F32)).astype(BF)
    heads = (
        lax.broadcasted_iota(jnp.int32, (product.shape[1], 128), 0) // 64
        == lax.broadcasted_iota(jnp.int32, (product.shape[1], 128), 1)
    ).astype(BF)
    return grad_out, dot_nn(high, heads) + dot_nn(rest, heads)


def out_back_kernel(
    grad_feed_ref,
    cot_ref,
    middle_ref,
    branch_ref,
    scaled_ref,
    attended_ref,
    weight_ref,
    vec_ref,
    hs_ref,
    grad_middle_ref,
    ga_ref,
    out_grad_ref,
    delta_ref,
    sums_ref,
    total_ref,
):
    step = pl.program_id(0)

    @pl.when(step == 0)
    def _():
        total_ref[...] = jnp.zeros_like(total_ref)
        sums_ref[...] = jnp.zeros_like(sums_ref)

    grad_middle, low = norms_back(
        grad_feed_ref[...], cot_ref, middle_ref, branch_ref, vec_ref, sums_ref
    )
    grad_middle_ref[...] = grad_middle
    ga_ref[...], delta = heads_back(low, weight_ref[...], hs_ref[...], attended_ref[...])
    total_ref[...] += dot_tn(scaled_ref[...], low)
    delta_ref[...] = delta.T[: delta_ref.shape[0]]

    @pl.when(step == pl.num_programs(0) - 1)
    def _():
        out_grad_ref[...] = total_ref[...].astype(BF)


def out_back(
    grad_feed, cotangent, middle, branch, scaled, attended, weights, vectors, head_lanes
):
    rows, width = cotangent.shape
    heads = 2 * width // 128
    by_row = pl.BlockSpec((TILE, width), lambda i: (i, 0))
    return pl.pallas_call(
        out_back_kernel,
        grid=(rows // TILE,),
        in_specs=[
            by_row,
            by_row,
            by_row,
            by_row,
            by_row,
            by_row,
            whole((width, width)),
            whole(vectors.shape),
            whole((1, width)),
        ],
        out_specs=[
            by_row,
            by_row,
            whole((width, width)),
            pl.BlockSpec((heads, TILE), lambda i: (0, i)),
            whole((16, width)),
        ],
        out_shape=[
            jax.ShapeDtypeStruct((rows, width), F32),
            jax.ShapeDtypeStruct((rows, width), BF),
            jax.ShapeDtypeStruct((width, width), BF),
            jax.ShapeDtypeStruct((heads, rows), F32),
            jax.ShapeDtypeStruct((16, width), F32),
        ],
        scratch_shapes=[pltpu.VMEM((width, width), F32)],
        compiler_params=params(),
        name="out_back",
    )(
        grad_feed,
        cotangent,
        middle,
        branch,
        scaled,
        attended,
        weights,
        vectors,
        head_lanes,
    )


def attention_back_keys(
    starts, cross, q_ref, k_ref, v_ref, ga_ref, lse_ref, deltas, dq_ref, dk_ref, dv_ref
):
    rows = q_ref.shape[0]
    half = rows // 2
    factor = LOG2E * 64 ** (-0.5)
    low_lanes = lax.broadcasted_iota(jnp.int32, (1, 128), 1) < 64
    above = lax.broadcasted_iota(jnp.int32, (TILE, TILE), 0) <= lax.broadcasted_iota(
        jnp.int32, (TILE, TILE), 1
    )

    def pick(both):
        return jnp.where(low_lanes, both[:TILE], both[TILE:])

    for start in starts:
        stop = start + TILE
        keys = k_ref[start:stop]
        keys_apart = stacked(keys, low_lanes)
        values_apart = stacked(v_ref[start:stop], low_lanes)
        dk = jnp.zeros((TILE, 128), F32)
        dv = jnp.zeros((TILE, 128), F32)
        for left, right in ((start, half), (half, rows)) if start < half else ((start, rows),):
            raw = dot_nt(keys_apart, q_ref[left:right])
            grad_weights = dot_nt(values_apart, ga_ref[left:right])
            weights, grad_scores = [], []
            for head in range(2):
                mine = slice(head * TILE, (head + 1) * TILE)
                level = lse_ref[0, head : head + 1, left:right]
                if start < half <= left:
                    level = level - cross
                exponent = raw[mine] * factor - level
                if left == start:
                    first = jnp.where(above, exponent[:, :TILE], MASKED)
                    exponent = (
                        first
                        if right - left == TILE
                        else jnp.concatenate([first, exponent[:, TILE:]], axis=1)
                    )
                weight = jnp.exp2(exponent)
                weights.append(weight.astype(BF))
                delta = deltas[head][:, left:right]
                grad_scores.append((weight * (grad_weights[mine] - delta)).astype(BF))
            dv = dv + pick(dot_nn(jnp.concatenate(weights, axis=0), ga_ref[left:right]))
            dk = dk + pick(dot_nn(jnp.concatenate(grad_scores, axis=0), q_ref[left:right]))
            dq = jnp.where(low_lanes, dot_tn(grad_scores[0], keys), dot_tn(grad_scores[1], keys))
            if start == 0:
                dq_ref[left:right] = dq
            else:
                dq_ref[left:right] += dq
        dk_ref[start:stop] = dk
        dv_ref[start:stop] = dv


def in_back_pair(dq_ref, dk_ref, dv_ref, weights, turned_ref, out_grad_ref, chunk_ref, total_ref):
    factor = 64 ** (-0.5)
    dq = (dq_ref[...] * factor).astype(BF)
    dk = (dk_ref[...] * factor).astype(BF)
    dv = dv_ref[...].astype(BF)
    grads = jnp.concatenate([dq, dk, dv], axis=1)
    shares = dot_nn(turned_ref[...], grads).astype(BF)
    for start in range(0, total_ref.shape[0], TILE):
        part = jnp.concatenate(
            [shares[start : start + TILE], out_grad_ref[start : start + TILE]], axis=1
        )
        chunk_ref[:, start // TILE] = part.reshape(8, 32, 512)
        columns = slice(start, start + TILE)
        total_ref[:, columns] += dot_nt(grads, weights[columns])
    return column_sum(dq.astype(F32)), column_sum(dv.astype(F32))


def tokens_back(tokens, grad, grad_middle, gain):
    normed, inv = row_norm(tokens.astype(F32))
    back = norm_back(grad, gain, normed, inv)
    return (grad_middle + back).astype(BF), column_sum(grad * normed), column_sum(grad)


def in_back_kernel(
    lengths_ref,
    proj_ref,
    ga_ref,
    lse_ref,
    delta_ref,
    wq_ref,
    wk_ref,
    wv_ref,
    first_ref,
    out_grad_ref,
    tokens_ref,
    gain_ref,
    grad_middle_ref,
    chunk_ref,
    bias_ref,
    tokens_grad_ref,
    sums_ref,
    dq_ref,
    dk_ref,
    dv_ref,
    turned_ref,
    total_ref,
):
    step = pl.program_id(0)
    q_ref, k_ref, v_ref = three(proj_ref)
    rows_all = tokens_ref.shape[0]

    @pl.when(step == 0)
    def _():
        turned_ref[...] = first_ref[...].T
        total_ref[...] = jnp.zeros_like(total_ref)

    deltas = [delta_ref[0, head : head + 1] for head in range(2)]
    attention_back_keys(
        range(0, rows_all, TILE),
        cross_flag(lengths_ref, tokens_ref),
        q_ref,
        k_ref,
        v_ref,
        ga_ref,
        lse_ref,
        deltas,
        dq_ref,
        dk_ref,
        dv_ref,
    )
    weights = jnp.concatenate([wq_ref[...], wk_ref[...], wv_ref[...]], axis=1)
    query_sum, value_sum = in_back_pair(
        dq_ref, dk_ref, dv_ref, weights, turned_ref, out_grad_ref, chunk_ref.at[0], total_ref
    )
    bias_ref[0, 0:1] = query_sum
    bias_ref[0, 1:2] = value_sum

    @pl.when(step == pl.num_programs(0) - 1)
    def _():
        gain_grad = jnp.zeros((1, total_ref.shape[1]), F32)
        shift_grad = jnp.zeros((1, total_ref.shape[1]), F32)
        for start in range(0, rows_all, TILE):
            rows = pl.ds(start, TILE)
            tokens_grad_ref[rows], gain_part, shift_part = tokens_back(
                tokens_ref[rows], total_ref[rows], grad_middle_ref[rows], gain_ref[...]
            )
            gain_grad = gain_grad + gain_part
            shift_grad = shift_grad + shift_part
        sums_ref[0:1] = gain_grad
        sums_ref[1:2] = shift_grad


def in_back(lengths, projected, ga, lse, delta, weights, first, out_grad, tokens, gain, grad_middle):
    rows, width = tokens.shape
    pairs = width // 128
    column = pl.BlockSpec((rows, 128), lambda p: (0, p))
    square = whole((rows, width))
    return pl.pallas_call(
        in_back_kernel,
        grid=(pairs,),
        in_specs=[
            pl.BlockSpec(memory_space=pltpu.SMEM),
            pl.BlockSpec((1, rows, 384), lambda p: (p, 0, 0)),
            column,
            pl.BlockSpec((1, 8, rows), lambda p: (p, 0, 0)),
            pl.BlockSpec((1, 2, rows), lambda p: (p, 0, 0)),
            pl.BlockSpec((width, 128), lambda p: (0, p)),
            pl.BlockSpec((width, 128), lambda p: (0, pairs + p)),
            pl.BlockSpec((width, 128), lambda p: (0, 2 * pairs + p)),
            square,
            column,
            square,
            whole((1, width)),
            square,
        ],
        out_specs=[
            pl.BlockSpec((1, 8, width // TILE, 32, 512), lambda p: (p, 0, 0, 0, 0)),
            pl.BlockSpec((1, 8, 128), lambda p: (p, 0, 0)),
            square,
            whole((8, width)),
        ],
        out_shape=[
            jax.ShapeDtypeStruct((pairs, 8, width // TILE, 32, 512), BF),
            jax.ShapeDtypeStruct((pairs, 8, 128), F32),
            jax.ShapeDtypeStruct((rows, width), BF),
            jax.ShapeDtypeStruct((8, width), F32),
        ],
        scratch_shapes=[
            pltpu.VMEM((rows, 128), F32),
            pltpu.VMEM((rows, 128), F32),
            pltpu.VMEM((rows, 128), F32),
            pltpu.VMEM((width, rows), BF),
            pltpu.VMEM((rows, width), F32),
        ],
        compiler_params=params(),
        name="in_back",
    )(
        lengths,
        projected,
        ga,
        lse,
        delta,
        weights,
        weights,
        weights,
        first,
        out_grad,
        tokens,
        gain,
        grad_middle,
    )


class Place:
    def __init__(self):
        self.z = lax.axis_index("dp")
        wide = lax.axis_index("wide")
        self.y = wide // 4
        self.x = (wide // 2) % 2
        self.c = wide % 2
        self.core = (self.z, wide + 1 - 2 * self.c)
        self.side = (self.z, wide + 2 - 4 * self.x)
        self.over = (self.z, wide + 4 - 8 * self.y)
        self.ranks = (self.z + 1 - 2 * (self.z % 2), (self.z + 2) % 4, 3 - self.z)
        self.planes = tuple((rank, wide) for rank in self.ranks)

    def greet(self, planes=True):
        barrier = pltpu.get_barrier_semaphore()
        peers = (self.core, self.side, self.over) + (self.planes if planes else ())
        for peer in peers:
            pl.semaphore_signal(barrier, inc=1, device_id=peer, device_id_type=MESH)
        pl.semaphore_wait(barrier, len(peers))


class WideGather:
    copies = 10

    def __init__(self, place, source, target, send, recv, first, last, rows=None):
        start, count = (0, target.shape[-2]) if rows is None else rows
        y, x, c = place.y, place.x, place.c
        here, side, over, far = (y, x, c), (y, 1 - x, c), (1 - y, x, c), (1 - y, 1 - x, c)
        upper, lower, both = (
            pl.ds(start, count // 2),
            pl.ds(start + count // 2, count // 2),
            pl.ds(start, count),
        )

        def copy(index, slot, part, peer):
            destination = target.at[(*slot, part)]
            return pltpu.make_async_remote_copy(
                src_ref=source.at[part] if source is not None and slot is here else destination,
                dst_ref=destination,
                send_sem=send.at[first + index],
                recv_sem=recv.at[first + index],
                device_id=peer,
                device_id_type=MESH,
            )

        self.all = (
            copy(0, here, upper, place.side),
            copy(1, here, lower, place.over),
            copy(2, here, upper, place.over),
            copy(3, here, lower, place.side),
            copy(4, here, both, place.core),
            copy(5, side, upper, place.over),
            copy(6, over, lower, place.side),
            copy(7, side, both, place.core),
            copy(8, over, both, place.core),
            copy(9, far, both, place.core),
        )
        self.own = None
        if source is not None and last is not None:
            self.own = pltpu.make_async_copy(source, target.at[here], last)

    def start(self):
        if self.own is not None:
            self.own.start()
        for index in range(5):
            self.all[index].start()

    def relay(self, stage):
        waits, starts = (((0, 1), (5, 6)), ((2, 3), (7, 8)), ((5, 6), (9,)))[stage]
        for index in waits:
            self.all[index].wait_recv()
        for index in starts:
            self.all[index].start()

    def finish(self):
        for index in (4, 7, 8, 9):
            self.all[index].wait_recv()
        for copy in self.all:
            copy.wait_send()
        if self.own is not None:
            self.own.wait()


LAG = 2


class Reduction:
    slots = 2 * LAG
    keep = 3 * LAG + 2

    @classmethod
    def scratch(cls):
        n, k = cls.slots, cls.keep
        return [
            pltpu.VMEM((3 * LAG, 2, 2, 4, 32, 512), BF),
            pltpu.VMEM((n, 2, 2, 4, 32, 512), BF),
            pltpu.VMEM((n, 2, 4, 16, 512), BF),
            pltpu.VMEM((n, 2, 4, 16, 512), BF),
            pltpu.VMEM((n, 4, 16, 512), BF),
            pltpu.VMEM((n, 4, 16, 512), BF),
            pltpu.VMEM((n, 4, 32, 512), BF),
            pltpu.VMEM((n, 3, 32, 512), BF),
            pltpu.VMEM((n, 32, 512), BF),
            pltpu.VMEM((k, 3, 32, 512), BF),
            pltpu.SemaphoreType.DMA((11, k)),
            pltpu.SemaphoreType.DMA((11, k)),
            pltpu.SemaphoreType.DMA((3 * LAG,)),
        ]

    def __init__(self, place, refs):
        self.place = place
        (
            self.chip,
            self.partner,
            self.from_x,
            self.from_y,
            self.then_y,
            self.then_x,
            self.plane,
            self.from_z,
            self.sums,
            self.shared,
            self.send,
            self.recv,
            self.local,
        ) = refs

    def copy(self, index, slot, source, target, peer):
        return pltpu.make_async_remote_copy(
            src_ref=source,
            dst_ref=target,
            send_sem=self.send.at[index, slot],
            recv_sem=self.recv.at[index, slot],
            device_id=peer,
            device_id_type=MESH,
        )

    def to_core(self, slot, source):
        return self.copy(0, slot, source, self.partner.at[slot], self.place.core)

    def load(self, chunk, source):
        slot = chunk % (3 * LAG)
        return pltpu.make_async_copy(source, self.chip.at[slot], self.local.at[slot])

    def first_hop(self, chunk):
        p, slot, chip = self.place, chunk % self.slots, self.chip.at[chunk % (3 * LAG)]
        return (
            self.copy(1, slot, chip.at[:, 1 - p.x, :, pl.ds(0, 16)], self.from_x.at[slot], p.side),
            self.copy(2, slot, chip.at[1 - p.y, :, :, pl.ds(16, 16)], self.from_y.at[slot], p.over),
        )

    def second_hop(self, chunk):
        p, slot, chip = self.place, chunk % self.slots, self.chip.at[chunk % (3 * LAG)]
        return (
            self.copy(
                3, slot, chip.at[1 - p.y, p.x, :, pl.ds(0, 16)], self.then_y.at[slot], p.over
            ),
            self.copy(
                4, slot, chip.at[p.y, 1 - p.x, :, pl.ds(16, 16)], self.then_x.at[slot], p.side
            ),
        )

    def to_planes(self, slot):
        p = self.place
        return [
            self.copy(
                5 + k, slot, self.plane.at[slot, p.ranks[k]], self.from_z.at[slot, k], p.planes[k]
            )
            for k in range(3)
        ]

    def share(self, chunk):
        p, slot, place = self.place, chunk % self.slots, chunk % self.keep
        return self.copy(8, place, self.sums.at[slot], self.shared.at[place, 0], p.planes[1])

    def share_on(self, chunk):
        p, slot, place = self.place, chunk % self.slots, chunk % self.keep
        return (
            self.copy(9, place, self.sums.at[slot], self.shared.at[place, 1], p.planes[0]),
            self.copy(10, place, self.shared.at[place, 0], self.shared.at[place, 2], p.planes[0]),
        )

    def stage0(self, chunk, view):
        slot, c = chunk % self.slots, self.place.c
        self.to_core(slot, view.at[:, :, 1 - c]).start()
        self.load(chunk, view.at[:, :, c]).start()

    def stage1(self, chunk):
        slot, index = chunk % self.slots, chunk % (3 * LAG)
        self.load(chunk, self.partner.at[slot]).wait()
        self.to_core(slot, self.chip.at[index]).wait()
        self.chip[index] += self.partner[slot]
        for copy in self.first_hop(chunk):
            copy.start()

    def stage2(self, chunk):
        p, slot, index = self.place, chunk % self.slots, chunk % (3 * LAG)
        for copy in self.first_hop(chunk):
            copy.wait()
        for k in range(2):
            self.chip[index, k, p.x, :, 0:16] += self.from_x[slot, k]
            self.chip[index, p.y, k, :, 16:32] += self.from_y[slot, k]
        for copy in self.second_hop(chunk):
            copy.start()

    def stage3(self, chunk):
        p, slot = self.place, chunk % self.slots
        for copy in self.second_hop(chunk):
            copy.wait()
        mine = self.chip.at[chunk % (3 * LAG), p.y, p.x]
        self.plane[slot, :, 0:16] = mine[:, 0:16] + self.then_y[slot]
        self.plane[slot, :, 16:32] = mine[:, 16:32] + self.then_x[slot]
        for copy in self.to_planes(slot):
            copy.start()

    def stage4(self, chunk):
        slot = chunk % self.slots
        for copy in self.to_planes(slot):
            copy.wait()
        total = self.plane[slot, self.place.z].astype(F32)
        for k in range(3):
            total = total + self.from_z[slot, k].astype(F32)
        return total

    def spread(self, chunk, total):
        self.sums[chunk % self.slots] = total.astype(BF)
        self.share(chunk).start()

    def stage5(self, chunk):
        self.share(chunk).wait()
        for copy in self.share_on(chunk):
            copy.start()

    def stage6(self, chunk):
        slot, place, ranks = chunk % self.slots, chunk % self.keep, self.place.ranks
        for copy in self.share_on(chunk):
            copy.wait()
        return [
            (self.place.z, self.sums[slot]),
            (ranks[1], self.shared[place, 0]),
            (ranks[0], self.shared[place, 1]),
            (ranks[2], self.shared[place, 2]),
        ]


def dma_sems(count):
    return [pltpu.SemaphoreType.DMA((count,)), pltpu.SemaphoreType.DMA((count,))]


class PlanesFirst:
    copies = 3 + 4 * WideGather.copies

    def __init__(self, place, target, send, recv, first):
        mine = target.at[place.z, place.y, place.x, place.c]
        self.across = [
            pltpu.make_async_remote_copy(
                src_ref=mine,
                dst_ref=mine,
                send_sem=send.at[first + index],
                recv_sem=recv.at[first + index],
                device_id=peer,
                device_id_type=MESH,
            )
            for index, peer in enumerate(place.planes)
        ]
        self.parts = [
            WideGather(
                place, None, target.at[rank], send, recv, first + 3 + index * WideGather.copies, None
            )
            for index, rank in enumerate((place.z, *place.ranks))
        ]

    def start(self):
        for copy in self.across:
            copy.start()

    def relay(self, stage):
        for part in self.parts:
            part.relay(stage)

    def finish(self):
        for copy in self.across:
            copy.wait_send()
        for part in self.parts:
            part.finish()


class PlanesLast:
    copies = WideGather.copies + 6

    def __init__(self, place, source, target, send, recv, last):
        self.wide = WideGather(place, source, target.at[place.z], send, recv, 0, last)

        def copy(index, rank, peer):
            blocks = target.at[rank, :, :, place.c]
            return pltpu.make_async_remote_copy(
                src_ref=blocks,
                dst_ref=blocks,
                send_sem=send.at[WideGather.copies + index],
                recv_sem=recv.at[WideGather.copies + index],
                device_id=peer,
                device_id_type=MESH,
            )

        self.across = [copy(k, place.z, place.planes[k]) for k in range(3)]
        self.over = [copy(3 + k, place.ranks[k], place.core) for k in range(3)]

    def start_across(self):
        self.wide.own.wait()
        for copy in self.across:
            copy.start()

    def start_over(self):
        for arrived, copy in zip(self.across, self.over):
            arrived.wait_recv()
            copy.start()

    def finish(self):
        self.wide.own = None
        self.wide.finish()
        for copy in self.across:
            copy.wait_send()
        for copy in self.over:
            copy.wait()


def first_kernel(
    lengths_ref,
    tokens_ref,
    in_ref,
    vec_ref,
    out_ref,
    up_ref,
    unit_ref,
    hs_ref,
    turned_ref,
    proj_ref,
    scaled_ref,
    scaled_turned_ref,
    attended_ref,
    lse_ref,
    vectors_ref,
    scale_ref,
    in_all,
    out_all,
    up_all,
    unit_all,
    held_ref,
    normed_ref,
    first_ref,
    vext_ref,
    send_in,
    recv_in,
    send_out,
    recv_out,
    send_ff,
    recv_ff,
    local,
):
    step = pl.program_id(0)
    place = Place()
    width = tokens_ref.shape[1]
    count = WideGather.copies
    lanes = (3 * width // 2 + 128, 3 * width // 2)
    into = [
        PlanesFirst(
            place,
            held_ref.at[group, :, :, :, :, :, pl.ds(0, lanes[group])],
            send_in,
            recv_in,
            group * PlanesFirst.copies,
        )
        for group in range(2)
    ]
    out = PlanesLast(place, out_ref, out_all, send_out, recv_out, local.at[2])
    up = WideGather(place, up_ref, up_all, send_ff, recv_ff, 0, local.at[3])
    unit = WideGather(place, unit_ref, unit_all, send_ff, recv_ff, count, local.at[4])
    keep = [
        pltpu.make_async_copy(
            held_ref.at[group, :, :, :, :, :, pl.ds(0, lanes[group])],
            in_all.at[group, :, :, :, :, :, pl.ds(0, lanes[group])],
            local.at[(1, 5)[group]],
        )
        for group in range(2)
    ]

    @pl.when(step == 0)
    def _():
        place.greet()
        half = width // 2
        for group in range(2):
            mine = held_ref.at[group, place.z, place.y, place.x, place.c]
            fills = [
                pltpu.make_async_copy(
                    in_ref.at[:, pl.ds(part * width + group * half, half)],
                    mine.at[:, pl.ds(part * half, half)],
                    local.at[6 + 3 * group + part],
                )
                for part in range(3)
            ]
            for copy in fills:
                copy.start()
            if group == 0:
                mine[:, 3 * half : 3 * half + 128] = jnp.zeros((32, 128), BF)
                mine[:, 3 * half : 3 * half + 32] = vec_ref[...]
            for copy in fills:
                copy.wait()
            into[group].start()
            if group == 0:
                into[0].parts[0].start()
        scale = hs_ref[...].astype(F32)
        for pair in range(width // 128):
            own = slice(pair * 128, (pair + 1) * 128)
            low_lanes = lax.broadcasted_iota(jnp.int32, (1, 128), 1) < 64
            scale_ref[0:1, own] = jnp.where(
                low_lanes, scale[:, 2 * pair : 2 * pair + 1], scale[:, 2 * pair + 1 : 2 * pair + 2]
            )
        for start in range(0, tokens_ref.shape[0], TILE):
            rows = pl.ds(start, TILE)
            normed, _ = row_norm(tokens_ref[rows].astype(F32))
            normed_ref[rows] = normed
        early = into[0]
        for index in range(3):
            early.parts[index].relay(0)
            early.across[index].wait_recv()
            early.parts[index + 1].start()
            early.parts[index].relay(1)
            early.parts[index].relay(2)
        for stage in range(3):
            early.parts[3].relay(stage)
        into[1].parts[0].start()
        for index in range(3):
            into[1].across[index].wait_recv()
            into[1].parts[index + 1].start()
        out.wide.start()
        unit.start()
        early.finish()
        for z in range(4):
            for y in range(2):
                tile = jnp.zeros((16, 128), F32)
                for x in range(2):
                    for c in range(2):
                        piece = held_ref[
                            0, z, y, x, c, 0:16, 3 * half : 3 * half + 128
                        ].astype(F32)
                        spot = 32 * (2 * x + c)
                        tile = tile + (piece if spot == 0 else pltpu.roll(piece, spot, 1))
                vectors_ref[:, (2 * z + y) * 128 : (2 * z + y + 1) * 128] = tile
        for start in range(0, tokens_ref.shape[0], TILE):
            rows = pl.ds(start, TILE)
            first_ref[rows] = (normed_ref[rows] * vectors_ref[3:4] + vectors_ref[4:5]).astype(BF)

    @pl.when((step >= 2) & (step <= 4))
    def _():
        for stage in range(3):

            @pl.when(step == 2 + stage)
            def _():
                into[1].relay(stage)
                out.wide.relay(stage)
                unit.relay(stage)

    @pl.when(step == 2)
    def _():
        up.start()

    @pl.when(step == 4)
    def _():
        out.start_across()

    @pl.when(step == 5)
    def _():
        into[1].finish()
        for copy in keep:
            copy.start()

    for stage, at in enumerate((5, 7, 8)):

        @pl.when(step == at)
        def _():
            up.relay(stage)

    @pl.when(step == 7)
    def _():
        out.start_over()

    @pl.when(step > 0)
    def _():
        pair = step - 1
        columns = [
            pl.ds(pl.multiple_of(part * (width // 2) + pair % 4 * 128, 128), 128)
            for part in range(3)
        ]
        weights = jnp.concatenate(
            [held_ref[pair // 4, :, :, :, :, :, cols].reshape(width, 128) for cols in columns],
            axis=1,
        )
        own = pl.ds(pl.multiple_of(pair * 128, 128), 128)
        bias = jnp.concatenate(
            [vectors_ref[0:1, own], jnp.zeros((1, 128), F32), vectors_ref[1:2, own]], axis=1
        )
        project_pair(first_ref, weights, bias, proj_ref)
        attention_pair(
            cross_flag(lengths_ref, tokens_ref),
            *three(proj_ref),
            scale_ref[0:1, own],
            scaled_ref,
            attended_ref,
            lse_ref,
            vext_ref,
        )
        scaled_turned_ref[...] = scaled_ref[...].T

    @pl.when(step == pl.num_programs(0) - 1)
    def _():
        turned_ref[...] = first_ref[...].T
        for copy in keep:
            copy.wait()
        out.finish()
        unit.finish()
        up.finish()


def first_part(lengths, tokens, in_weight, vec, out_weight, up_weight, unit_rows, head_scale):
    rows, width = tokens.shape
    pairs = width // 128

    def at(step):
        return jnp.maximum(step - 1, 0)

    column = pl.BlockSpec((rows, 128), lambda s: (0, at(s)))
    held = (2, 4, 2, 2, 2, 32, 3 * width // 2 + 128)
    return pl.pallas_call(
        first_kernel,
        grid=(pairs + 1,),
        in_specs=[
            pl.BlockSpec(memory_space=pltpu.SMEM),
            whole((rows, width)),
            ANY,
            whole(vec.shape),
            ANY,
            ANY,
            ANY,
            whole(head_scale.shape),
        ],
        out_specs=[
            whole((width, rows)),
            pl.BlockSpec((1, rows, 384), lambda s: (at(s), 0, 0)),
            column,
            pl.BlockSpec((128, rows), lambda s: (at(s), 0)),
            column,
            pl.BlockSpec((1, 8, rows), lambda s: (at(s), 0, 0)),
            whole((16, width)),
            whole((8, width)),
            ANY,
            ANY,
            ANY,
            ANY,
        ],
        out_shape=[
            jax.ShapeDtypeStruct((width, rows), BF),
            jax.ShapeDtypeStruct((pairs, rows, 384), BF),
            jax.ShapeDtypeStruct((rows, width), BF),
            jax.ShapeDtypeStruct((width, rows), BF),
            jax.ShapeDtypeStruct((rows, width), F32),
            jax.ShapeDtypeStruct((pairs, 8, rows), F32),
            jax.ShapeDtypeStruct((16, width), F32),
            jax.ShapeDtypeStruct((8, width), F32),
            jax.ShapeDtypeStruct(held, BF),
            jax.ShapeDtypeStruct((4, 2, 2, 2, *out_weight.shape), BF),
            jax.ShapeDtypeStruct((2, 2, 2, *up_weight.shape), BF),
            jax.ShapeDtypeStruct((2, 2, 2, *unit_rows.shape), BF),
        ],
        scratch_shapes=[
            pltpu.VMEM(held, BF),
            pltpu.VMEM((rows, width), F32),
            pltpu.VMEM((rows, width), BF),
            pltpu.VMEM((rows, 256), BF),
            *dma_sems(2 * PlanesFirst.copies),
            *dma_sems(PlanesLast.copies),
            *dma_sems(2 * WideGather.copies),
            pltpu.SemaphoreType.DMA((12,)),
        ],
        compiler_params=params(collective_id=0, has_side_effects=True),
        name="first_part",
    )(lengths, tokens, in_weight, vec, out_weight, up_weight, unit_rows, head_scale)


def second_kernel(
    units,
    scaled_ref,
    weight_ref,
    vec_ref,
    tokens_ref,
    up_ref,
    unit_ref,
    down_ref,
    branch_ref,
    middle_ref,
    turned_ref,
    act_ref,
    slope_ref,
    stats_ref,
    down_all,
    feed_ref,
    sums_ref,
    send,
    recv,
    local,
):
    step = pl.program_id(0)
    lead = feed_ref.shape[0] // TILE
    place = Place()
    down = WideGather(place, down_ref, down_all, send, recv, 0, local.at[0])

    @pl.when(step == 0)
    def _():
        place.greet(planes=False)
        down.start()
        sums_ref[...] = jnp.zeros_like(sums_ref)

    for stage, at in enumerate((5, 8, 11)):

        @pl.when(step == at)
        def _():
            down.relay(stage)

    @pl.when(step < lead)
    def _():
        rows = pl.ds(pl.multiple_of(step * TILE, TILE), TILE)
        feed_ref[rows] = out_proj_rows(
            scaled_ref, weight_ref, vec_ref, tokens_ref, branch_ref, middle_ref
        )

    @pl.when(step >= lead)
    def _():
        up_step(feed_ref, up_ref, unit_ref, act_ref, slope_ref, sums_ref)

    @pl.when(step == pl.num_programs(0) - 1)
    def _():
        up_stats(units, stats_ref, sums_ref)
        turned_ref[...] = feed_ref[...].T
        down.finish()


def second_part(scaled, out_weights, vectors, tokens, up, unit_vec, down_weight):
    rows, width = tokens.shape
    steps = up.shape[0]
    lead = rows // TILE

    def early(step):
        return jnp.minimum(step, lead - 1)

    def late(step):
        return jnp.maximum(step - lead, 0)

    by_row = pl.BlockSpec((TILE, width), lambda s: (early(s), 0))
    block = pl.BlockSpec((1, rows, UNITS), lambda s: (late(s), 0, 0))
    return pl.pallas_call(
        functools.partial(second_kernel, steps * UNITS),
        grid=(lead + steps,),
        in_specs=[
            by_row,
            whole((width, width)),
            whole(vectors.shape),
            by_row,
            pl.BlockSpec((1, width, UNITS), lambda s: (late(s), 0, 0)),
            pl.BlockSpec((1, unit_vec.shape[1], UNITS), lambda s: (late(s), 0, 0)),
            ANY,
        ],
        out_specs=[
            by_row,
            by_row,
            whole((width, rows)),
            block,
            block,
            whole((rows, 128)),
            ANY,
        ],
        out_shape=[
            jax.ShapeDtypeStruct((rows, width), F32),
            jax.ShapeDtypeStruct((rows, width), F32),
            jax.ShapeDtypeStruct((width, rows), BF),
            jax.ShapeDtypeStruct((steps, rows, UNITS), BF),
            jax.ShapeDtypeStruct((steps, rows, UNITS), BF),
            jax.ShapeDtypeStruct((rows, 128), F32),
            jax.ShapeDtypeStruct((2, 2, 2, *down_weight.shape), BF),
        ],
        scratch_shapes=[
            pltpu.VMEM((rows, width), BF),
            pltpu.VMEM((2, rows, 128), F32),
            *dma_sems(WideGather.copies),
            pltpu.SemaphoreType.DMA((1,)),
        ],
        compiler_params=params(collective_id=2, has_side_effects=True),
        name="second_part",
    )(scaled, out_weights, vectors, tokens, up, unit_vec, down_weight)


NORMS_AT, COLUMNS_AT, HEADS_AT, TOKENS_AT, LAST_CHUNK_AT = 8, 16, 20, 36, 40
BACK_STEPS = LAST_CHUNK_AT + 4 * LAG + 1
OUT_TILE = 128


def chunk_at(time):
    even = time % 2 == 0
    chunk = jnp.where(time < 8, time, (time + 24) // 4)
    chunk = jnp.where(time >= 16, (time + 4) // 2, chunk)
    chunk = jnp.where(time >= 20, time - 8, chunk)
    chunk = jnp.where(time >= 26, (time + 10) // 2, chunk)
    chunk = jnp.where(time == LAST_CHUNK_AT, 24, chunk)
    there = (time >= 0) & (
        (time < 8)
        | ((time < 16) & (time % 4 == 0))
        | ((time >= 16) & (time < 37) & even)
        | ((time >= 20) & (time < 26))
    )
    return chunk, there | (time == LAST_CHUNK_AT)


def back_kernel(
    lengths_ref,
    act_ref,
    slope_ref,
    e_ref,
    stats_ref,
    up_ref,
    feed_turned_ref,
    unit_grad_ref,
    down_grad_all,
    cot_ref,
    middle_ref,
    branch_ref,
    scaled_turned_ref,
    attended_ref,
    out_weight_ref,
    vec_ref,
    hs_ref,
    proj_ref,
    lse_ref,
    wq_ref,
    wk_ref,
    wv_ref,
    turned_ref,
    tokens_ref,
    tokens_grad_ref,
    down_out,
    up_out,
    attn_out,
    up_grad_all,
    staged_ref,
    total_ref,
    low_ref,
    out_grad_ref,
    ga_ref,
    grad_middle_ref,
    delta_ref,
    delta_sum_ref,
    sums_ref,
    units_ref,
    dq_ref,
    dk_ref,
    dv_ref,
    chunk_ref,
    store_sems,
    *scratch,
):
    step = pl.program_id(0)
    place = Place()
    engine = Reduction(place, scratch)

    @pl.when(step == 0)
    def _():
        place.greet()
        total_ref[...] = jnp.zeros_like(total_ref)
        sums_ref[...] = jnp.zeros_like(sums_ref)
        units_ref[...] = jnp.zeros_like(units_ref)

    def store(block):
        view = up_grad_all.at[block // 4, block // 2 % 2, block % 2]
        return pltpu.make_async_copy(staged_ref, view, store_sems.at[0])

    @pl.when((step >= 1) & (step <= NORMS_AT))
    def _():
        store(step - 1).wait()


    def stage(number, kind, action):
        chunk, there = chunk_at(step - number * LAG)
        up = ((chunk >= 8) & (chunk < 14)) | (chunk == 15) | (chunk == 17)
        wanted = {"all": there, "down": there & (chunk < 8), "up": there & up}
        wanted["shared"] = there & ((chunk < 8) | up)
        wanted["own"] = there & (chunk >= 8) & ~up

        @pl.when(wanted[kind])
        def _():
            action(chunk)

    def up_index(chunk):
        return jnp.where(chunk < 14, chunk - 8, (chunk - 3) // 2)

    def attn_index(chunk):
        return jnp.where(chunk < 18, (chunk - 14) // 2, chunk - 16)

    def put_down(chunk):
        for rank, block in engine.stage6(chunk):
            for half in range(2):

                @pl.when(chunk % 2 == half)
                def _():
                    down_out[chunk // 2, rank, :, half * 512 : half * 512 + 512] = block

    def put_up(chunk):
        for rank, block in engine.stage6(chunk):
            up_out[up_index(chunk), rank] = block

    def put_own(chunk):
        attn_out[attn_index(chunk)] = engine.stage4(chunk)

    def take_down(chunk):
        lanes = pl.ds(pl.multiple_of(chunk % 2 * 512, 512), 512)
        engine.stage0(chunk, down_grad_all.at[:, :, :, chunk // 2, :, :, lanes])

    def take_up(chunk):
        engine.stage0(chunk, up_grad_all.at[:, :, :, up_index(chunk)])

    def take_own(chunk):
        engine.stage0(chunk, chunk_ref.at[attn_index(chunk) % 2])

    stage(6, "down", put_down)
    stage(6, "up", put_up)
    stage(5, "shared", engine.stage5)
    stage(4, "shared", lambda chunk: engine.spread(chunk, engine.stage4(chunk)))
    stage(4, "own", put_own)
    stage(3, "all", engine.stage3)
    stage(2, "all", engine.stage2)
    stage(1, "all", engine.stage1)
    stage(0, "down", take_down)
    stage(0, "up", take_up)


    @pl.when(step < NORMS_AT)
    def _():
        units_ref[step, 0:1] = up_back_step(
            act_ref.at[0],
            slope_ref.at[0],
            e_ref.at[0],
            stats_ref,
            up_ref.at[0],
            low_ref,
            total_ref,
        )
        units_ref[step, 1:3] = unit_grad_ref[step, 0:2]
        for left in range(0, UNITS, TILE):
            columns = slice(left, left + TILE)
            grad = dot_nn(feed_turned_ref[...], low_ref[:, columns]).astype(BF)
            staged_ref[:, :, :, columns] = grad.reshape(8, 4, 32, TILE)
        store(step).start()


    @pl.when((step >= NORMS_AT) & (step < COLUMNS_AT))
    def _():
        rows = pl.ds(pl.multiple_of((step - NORMS_AT) * OUT_TILE, OUT_TILE), OUT_TILE)
        grad_middle, low = norms_back(
            total_ref[rows], cot_ref, middle_ref, branch_ref, vec_ref, sums_ref
        )
        grad_middle_ref[rows] = grad_middle
        low_ref[rows] = low

    @pl.when((step >= COLUMNS_AT) & (step < HEADS_AT))
    def _():
        block = step - COLUMNS_AT
        columns = pl.ds(pl.multiple_of(block * TILE, TILE), TILE)
        grad_out, delta = heads_back(
            low_ref[...], out_weight_ref[columns], hs_ref[0:1, columns], attended_ref[...]
        )
        ga_ref[:, columns] = grad_out
        delta_sum_ref[block, 0:1] = column_sum(delta)
        turned = delta.T
        for head in range(4):
            delta_ref[4 * block + head] = turned[head : head + 1]
        out_grad_ref[:, columns] = dot_nn(scaled_turned_ref[...], low_ref[:, columns]).astype(BF)

    @pl.when(step == HEADS_AT - 1)
    def _():
        total_ref[...] = jnp.zeros_like(total_ref)


    @pl.when((step >= HEADS_AT) & (step < TOKENS_AT))
    def _():
        index = step - HEADS_AT
        pair = index // 2
        columns = pl.ds(pl.multiple_of(pair * 128, 128), 128)
        for part, starts in enumerate(((0, 3 * TILE), (TILE, 2 * TILE))):

            @pl.when(index % 2 == part)
            def _():
                attention_back_keys(
                    starts,
                    cross_flag(lengths_ref, total_ref),
                    *three(proj_ref),
                    ga_ref.at[:, columns],
                    lse_ref,
                    [delta_ref[2 * pair], delta_ref[2 * pair + 1]],
                    dq_ref,
                    dk_ref,
                    dv_ref,
                )

        @pl.when(index % 2 == 1)
        def _():
            weights = jnp.concatenate([wq_ref[...], wk_ref[...], wv_ref[...]], axis=1)
            query_sum, value_sum = in_back_pair(
                dq_ref,
                dk_ref,
                dv_ref,
                weights,
                turned_ref,
                out_grad_ref.at[:, columns],
                chunk_ref.at[pair % 2].reshape(8, 4, 32, 512),
                total_ref,
            )
            sums_ref[0:1, columns] = query_sum
            sums_ref[1:2, columns] = value_sum

    @pl.when((step >= TOKENS_AT) & (step < TOKENS_AT + 4))
    def _():
        rows = pl.ds(pl.multiple_of((step - TOKENS_AT) * TILE, TILE), TILE)
        tokens_grad_ref[...], gain_grad, shift_grad = tokens_back(
            tokens_ref[...], total_ref[rows], grad_middle_ref[rows], vec_ref[3:4]
        )
        sums_ref[3:4] += gain_grad
        sums_ref[4:5] += shift_grad

    @pl.when(step == LAST_CHUNK_AT)
    def _():
        for y in range(2):
            for x in range(2):
                for c in range(2):
                    unit = 4 * y + 2 * x + c
                    units_ref[unit, 3:4] = sums_ref[9:10, 0:UNITS]
                    units_ref[unit, 4:5] = sums_ref[9:10, UNITS : 2 * UNITS]
                    for block in range(4):
                        units_ref[unit, 5 + block : 6 + block, 0:128] = delta_sum_ref[block, 0:1]
                    top = units_ref[unit].astype(BF)
                    for z in range(4):
                        start = (2 * z + y) * 128
                        chunk_ref[0, y, x, c, z, 0:16] = top
                        chunk_ref[0, y, x, c, z, 16:32, 0:128] = sums_ref[
                            :, start : start + 128
                        ].astype(BF)

    stage(0, "own", take_own)


def back_part(
    lengths,
    act,
    slope,
    e,
    stats,
    up,
    feed_turned,
    unit_grad,
    down_grad,
    cotangent,
    middle,
    branch,
    scaled_turned,
    attended,
    out_weights,
    vectors,
    head_lanes,
    projected,
    lse,
    weights,
    turned,
    tokens,
):
    rows, width = tokens.shape
    pairs = width // 128

    def clamp(value, high):
        return jnp.minimum(jnp.maximum(value, 0), high)

    def unit(s):
        return clamp(s, 7)

    def pair(s):
        return clamp((s - HEADS_AT) // 2, pairs - 1)

    def tail(s):
        return clamp(s - TOKENS_AT, 3)

    def columns_of(part):
        return lambda s: (pair(s) // 4, 0, 4 * part + pair(s) % 4)

    block = pl.BlockSpec((1, rows, UNITS), lambda s: (unit(s), 0, 0))
    narrow = whole((rows, 128))
    by_row = pl.BlockSpec((OUT_TILE, width), lambda s: (clamp(s - NORMS_AT, 7), 0))
    square = whole((width, width))
    return pl.pallas_call(
        back_kernel,
        grid=(BACK_STEPS,),
        in_specs=[
            pl.BlockSpec(memory_space=pltpu.SMEM),
            block,
            block,
            block,
            narrow,
            pl.BlockSpec((1, width, UNITS), lambda s: (unit(s), 0, 0)),
            square,
            whole(unit_grad.shape),
            ANY,
            by_row,
            by_row,
            by_row,
            square,
            pl.BlockSpec((rows, TILE), lambda s: (0, clamp(s - COLUMNS_AT, 3))),
            square,
            whole(vectors.shape),
            whole(head_lanes.shape),
            pl.BlockSpec((1, rows, 384), lambda s: (pair(s), 0, 0)),
            pl.BlockSpec((1, 8, rows), lambda s: (pair(s), 0, 0)),
            *[pl.BlockSpec((None, width, 128), columns_of(part)) for part in range(3)],
            square,
            pl.BlockSpec((TILE, width), lambda s: (tail(s), 0)),
        ],
        out_specs=[
            pl.BlockSpec((TILE, width), lambda s: (tail(s), 0)),
            whole((4, 4, 32, 1024)),
            whole((8, 4, 32, 512)),
            whole((9, 32, 512)),
            ANY,
        ],
        out_shape=[
            jax.ShapeDtypeStruct((rows, width), BF),
            jax.ShapeDtypeStruct((4, 4, 32, 1024), BF),
            jax.ShapeDtypeStruct((8, 4, 32, 512), BF),
            jax.ShapeDtypeStruct((9, 32, 512), F32),
            jax.ShapeDtypeStruct((2, 2, 2, 8, 4, 32, UNITS), BF),
        ],
        scratch_shapes=[
            pltpu.VMEM((8, 4, 32, UNITS), BF),
            pltpu.VMEM((rows, width), F32),
            pltpu.VMEM((rows, width), BF),
            pltpu.VMEM((width, width), BF),
            pltpu.VMEM((rows, width), BF),
            pltpu.VMEM((rows, width), F32),
            pltpu.VMEM((2 * pairs, 1, rows), F32),
            pltpu.VMEM((4, 8, 128), F32),
            pltpu.VMEM((16, width), F32),
            pltpu.VMEM((8, 16, UNITS), F32),
            pltpu.VMEM((rows, 128), F32),
            pltpu.VMEM((rows, 128), F32),
            pltpu.VMEM((rows, 128), F32),
            pltpu.VMEM((2, 2, 2, 2, 4, 32, 512), BF),
            pltpu.SemaphoreType.DMA((1,)),
            *Reduction.scratch(),
        ],
        compiler_params=params(collective_id=1, has_side_effects=True),
        name="back_part",
    )(
        lengths,
        act,
        slope,
        e,
        stats,
        up,
        feed_turned,
        unit_grad,
        down_grad.reshape(2, 2, 2, 4, 4, 32, width),
        cotangent,
        middle,
        branch,
        scaled_turned,
        attended,
        out_weights,
        vectors,
        head_lanes,
        projected,
        lse,
        weights,
        weights,
        weights,
        turned,
        tokens,
    )


def layer(staged, tokens, cotangent, lengths, attn, up, down, unit_vec, head_scale, down_bias):
    rows, width = tokens.shape
    heads = head_scale.shape[0]
    pairs = width // 128
    if staged:
        in_weight, out_weight, vec_block = attn
        (
            turned,
            projected,
            scaled,
            scaled_turned,
            attended,
            lse,
            vectors,
            head_lanes,
            weights,
            out_weights,
            up,
            unit_vec,
        ) = first_part(
            lengths, tokens, in_weight, vec_block, out_weight, up, unit_vec, head_scale[None, :]
        )
        weights = weights.reshape(2, width, -1)
        out_weights = out_weights.reshape(width, width)
        up = up.reshape(-1, width, UNITS)
        unit_vec = unit_vec.reshape(-1, unit_vec.shape[-2], UNITS)
        branch, middle, feed_turned, act, slope, stats, down = second_part(
            scaled, out_weights, vectors, tokens, up, unit_vec, down
        )
        down = down.reshape(-1, UNITS, width)
    else:
        weights, out_weights, vectors = attn
        scale = head_scale.astype(F32)
        head_lanes = jnp.repeat(scale, width // heads)[None, :]
        first, projected, scaled, attended, lse = plain_first(
            lengths, tokens, weights, vectors, head_lanes
        )
        branch, middle, feed = out_proj(scaled, out_weights, vectors, tokens)
        act, slope, stats = up_pass(feed, up, unit_vec)
    mixed, down_grad, e, stats, unit_grad = down_pass(
        act, stats, unit_vec, down, cotangent, middle, down_bias[None, :]
    )
    if staged:
        tokens_grad, down_total, up_total, shares, _ = back_part(
            lengths,
            act,
            slope,
            e,
            stats,
            up,
            feed_turned,
            unit_grad,
            down_grad,
            cotangent,
            middle,
            branch,
            scaled_turned,
            attended,
            out_weights,
            vectors,
            head_lanes,
            projected,
            lse,
            weights,
            turned,
            tokens,
        )
        return mixed, tokens_grad, down_total, up_total, shares
    up_grad, up_bias_grad, grad_feed = up_back(
        act, slope, e, stats, up, feed
    )
    grad_middle, ga, out_grad, delta, sums = out_back(
        grad_feed,
        cotangent,
        middle,
        branch,
        scaled,
        attended,
        out_weights,
        vectors,
        head_lanes,
    )
    chunks, proj_bias, tokens_grad, pre_sums = in_back(
        lengths,
        projected,
        ga,
        lse,
        delta.reshape(pairs, 2, rows),
        weights,
        first,
        out_grad,
        tokens,
        vectors[3:4],
        grad_middle,
    )
    scale_grad = jnp.sum(delta, axis=1) / scale
    vec_grads = [
        proj_bias[:, 0].reshape(width),
        proj_bias[:, 1].reshape(width),
        sums[2],
        pre_sums[0],
        pre_sums[1],
        sums[5],
        sums[6],
        sums[7],
        sums[8],
    ]
    unit_grads = [up_bias_grad[:, 0], unit_grad[:, 0], unit_grad[:, 1]]
    return mixed, tokens_grad, chunks, up_grad, down_grad, vec_grads, unit_grads, sums[9], scale_grad


def body(
    axes,
    tokens,
    cotangent,
    lengths,
    in_weight,
    query_bias,
    value_bias,
    out_weight,
    out_bias,
    head_scale,
    pre_gain,
    pre_bias,
    post_gain,
    post_bias,
    feed_gain,
    feed_bias,
    up_weight,
    up_bias,
    mid_gain,
    mid_bias,
    down_weight,
    down_bias,
):
    planes, wide = axes
    every = ("dp", "wide")
    staged = (planes, wide) == (4, 8)
    rows, width = tokens.shape
    units = down_weight.shape[0] * wide
    steps = units // UNITS
    share = in_weight.shape[0]
    columns = [
        query_bias,
        value_bias,
        out_bias,
        pre_gain,
        pre_bias,
        post_gain,
        post_bias,
        feed_gain,
        feed_bias,
    ]
    index = lax.broadcasted_iota(jnp.int32, (32, up_bias.shape[0]), 0)
    unit_rows = jnp.where(index == 0, up_bias[None, :], jnp.zeros((), BF))
    unit_rows = jnp.where(index == 1, mid_gain[None, :], unit_rows)
    unit_rows = jnp.where(index == 2, mid_bias[None, :], unit_rows)
    if staged:
        index = lax.broadcasted_iota(jnp.int32, (32, share), 0)
        vec_block = jnp.zeros((32, share), BF)
        for row, column in enumerate(columns):
            vec_block = jnp.where(index == row, column[None, :], vec_block)
        attn = (in_weight, out_weight, vec_block)
        up, unit_vec, down = up_weight, unit_rows, down_weight
    else:
        flat = jnp.concatenate(columns).reshape(len(columns), share)
        attn = (
            lax.all_gather(in_weight, every, axis=0, tiled=True),
            lax.all_gather(out_weight, every, axis=0, tiled=True),
            jnp.pad(
                lax.all_gather(flat, every, axis=1, tiled=True), ((0, 16 - len(columns)), (0, 0))
            ).astype(F32),
        )
        up = lax.all_gather(up_weight, "wide", axis=1, tiled=True)
        up = up.reshape(width, steps, UNITS).transpose(1, 0, 2)
        unit_vec = lax.all_gather(unit_rows, "wide", axis=1, tiled=True)
        unit_vec = unit_vec.reshape(32, steps, UNITS).transpose(1, 0, 2)
        down = lax.all_gather(down_weight, "wide", axis=0, tiled=True)
        down = down.reshape(steps, UNITS, width)
    results = layer(
        staged,
        tokens,
        cotangent,
        lengths,
        attn,
        up,
        down,
        unit_vec,
        head_scale,
        down_bias,
    )
    heads = head_scale.shape[0]
    pairs = width // 128
    if staged:
        mixed, tokens_grad, down_total, up_total, shares = results
        up_total = up_total.astype(F32).reshape(width, UNITS)
        down_total = down_total.astype(F32).reshape(UNITS, width)
        unit_totals = [shares[8, index] for index in range(3)]
        down_sum = jnp.concatenate([shares[8, 3], shares[8, 4]])
        scale_sum = shares[8, 5:9, :4].reshape(heads) / head_scale.astype(F32)
        offset = share * lax.rem(lax.axis_index("wide"), 128 // share)
        own = lax.dynamic_slice(shares, (8, 16, offset), (1, len(columns), share))[0]
        vec_totals = [own[index] for index in range(len(columns))]
        in_total = shares[:pairs, :, :384].reshape(pairs, share, 3, 128)
        in_total = in_total.transpose(1, 2, 0, 3).reshape(share, 3 * width)
        out_total = shares[:pairs, :, 384:].transpose(1, 0, 2).reshape(share, width)
    else:
        (mixed, tokens_grad, chunks, up_grad, down_grad, vec_grads, unit_grads) = results[:7]
        down_sum, scale_sum = results[7:]

        def scatter(value, axis=0, over=every):
            return lax.psum_scatter(value, over, scatter_dimension=axis, tiled=True)

        def both_ways(value, axis):
            part = scatter(value.astype(BF), axis, "wide")
            return lax.psum(part, "dp").astype(F32)

        up_total = both_ways(up_grad.transpose(1, 0, 2).reshape(width, units), 1)
        down_total = both_ways(down_grad.reshape(units, width), 0)
        unit_totals = [
            lax.psum(scatter(item.reshape(units), 0, "wide"), "dp") for item in unit_grads
        ]
        down_sum, scale_sum = lax.psum((down_sum, scale_sum), every)
        vec_totals = [scatter(item) for item in vec_grads]
        natural = chunks.transpose(0, 2, 1, 3, 4).reshape(pairs, width, 512)
        in_total = natural[:, :, :384].reshape(pairs, width, 3, 128)
        in_total = scatter(in_total.transpose(1, 2, 0, 3).reshape(width, 3 * width).astype(F32))
        out_total = scatter(
            natural[:, :, 384:].transpose(1, 0, 2).reshape(width, width).astype(F32)
        )
    return (
        mixed,
        tokens_grad,
        in_total,
        vec_totals[0],
        vec_totals[1],
        out_total,
        vec_totals[2],
        scale_sum,
        vec_totals[3],
        vec_totals[4],
        vec_totals[5],
        vec_totals[6],
        vec_totals[7],
        vec_totals[8],
        up_total,
        unit_totals[0],
        unit_totals[1],
        unit_totals[2],
        down_total,
        down_sum,
    )


def solution(mesh):
    by_all = P(("dp", "wide"))
    rows_all = P(("dp", "wide"), None)
    axes = (mesh.shape["dp"], mesh.shape["wide"])
    return jax.shard_map(
        functools.partial(body, axes),
        mesh=mesh,
        in_specs=(
            rows_all,
            rows_all,
            rows_all,
            rows_all,
            by_all,
            by_all,
            rows_all,
            by_all,
            P(),
            by_all,
            by_all,
            by_all,
            by_all,
            by_all,
            by_all,
            P(None, "wide"),
            P("wide"),
            P("wide"),
            P("wide"),
            P("wide", None),
            P(),
        ),
        out_specs=(
            rows_all,
            rows_all,
            rows_all,
            by_all,
            by_all,
            rows_all,
            by_all,
            P(),
            by_all,
            by_all,
            by_all,
            by_all,
            by_all,
            by_all,
            P(None, "wide"),
            P("wide"),
            P("wide"),
            P("wide"),
            P("wide", None),
            P(),
        ),
        check_vma=False,
    )
```

```python
import functools

import jax
import jax.numpy as jnp
from jax import lax
from jax.experimental import pallas as pl
from jax.experimental.pallas import tpu as pltpu
from jax.sharding import PartitionSpec as P

EPS = 1e-05
ROOT_HALF = 0.7071067811865476
INV_ROOT_TAU = 0.3989422804014327
LOG2E = 1.4426950408889634
MASKED = -1e30
BF = jnp.bfloat16
F32 = jnp.float32
TILE = 256
UNITS = 512
SLIM = 64
MESH = pl.DeviceIdType.MESH
VMEM_LIMIT = 62 * 1024 * 1024
ANY = pl.BlockSpec(memory_space=pl.ANY)


def dot_nn(left, right):
    return lax.dot_general(left, right, (((1,), (0,)), ((), ())), preferred_element_type=F32)


def dot_nt(left, right):
    return lax.dot_general(left, right, (((1,), (1,)), ((), ())), preferred_element_type=F32)


def dot_tn(left, right):
    return lax.dot_general(left, right, (((0,), (0,)), ((), ())), preferred_element_type=F32)


def params(**more):
    return pltpu.CompilerParams(
        dimension_semantics=("arbitrary",), vmem_limit_bytes=VMEM_LIMIT, **more
    )


def whole(shape):
    zeros = (0,) * len(shape)
    return pl.BlockSpec(shape, lambda *_: zeros, pipeline_mode=pl.Buffered(1))


def row_norm(values):
    center = values - jnp.mean(values, axis=-1, keepdims=True)
    inv = lax.rsqrt(jnp.mean(center * center, axis=-1, keepdims=True) + EPS)
    return center * inv, inv


def norm_back(grad, gain, normed, inv):
    scaled = grad * gain
    first = jnp.mean(scaled, axis=-1, keepdims=True)
    cross = jnp.mean(scaled * normed, axis=-1, keepdims=True)
    return inv * (scaled - first - normed * cross)


def column_sum(values):
    return jnp.sum(values, axis=0, keepdims=True)


def lane_fold(values):
    total = values[:, :128]
    for start in range(128, values.shape[1], 128):
        total = total + values[:, start : start + 128]
    return total


def cross_flag(lengths_ref, rows_ref):
    return jnp.where(lengths_ref[0, 0] == rows_ref.shape[0], 0.0, MASKED)


def stacked(value, low_lanes):
    zero = jnp.zeros_like(value)
    return jnp.concatenate(
        [jnp.where(low_lanes, value, zero), jnp.where(low_lanes, zero, value)], axis=0
    )


def attention_pair(cross, q_ref, k_ref, v_ref, scale, scaled_ref, out_ref, lse_ref, vext_ref):
    rows = q_ref.shape[0]
    half = rows // 2
    factor = LOG2E * 64 ** (-0.5)
    low_lanes = lax.broadcasted_iota(jnp.int32, (1, 128), 1) < 64
    below = lax.broadcasted_iota(jnp.int32, (TILE, TILE), 1) <= lax.broadcasted_iota(
        jnp.int32, (TILE, TILE), 0
    )
    vext_ref[:, :128] = v_ref[...]
    vext_ref[:, 128:] = jnp.ones((rows, 128), BF)
    for start in range(0, rows, TILE):
        stop = start + TILE
        both = dot_nt(stacked(q_ref[start:stop], low_lanes), k_ref[:stop])
        peaks, weights = [], []
        for head in range(2):
            raw = both[head * TILE : (head + 1) * TILE]
            parts = []
            if start >= half:
                parts.append((raw[:, :half], cross))
                if start > half:
                    parts.append((raw[:, half:start], None))
            elif start > 0:
                parts.append((raw[:, :start], None))
            parts.append((jnp.where(below, raw[:, start:stop], MASKED), None))
            peak = None
            for piece, shift in parts:
                top = jnp.max(piece, axis=-1, keepdims=True)
                if shift is not None:
                    top = top + shift
                peak = top if peak is None else jnp.maximum(peak, top)
            peaks.append(peak)
            pieces = []
            for piece, shift in parts:
                level = peak if shift is None else peak - shift
                pieces.append(jnp.exp2((piece - level) * factor).astype(BF))
            weights.append(pieces[0] if len(pieces) == 1 else jnp.concatenate(pieces, axis=1))
        both = dot_nn(jnp.concatenate(weights, axis=0), vext_ref[:stop])
        total = jnp.where(low_lanes, both[:TILE, 128:], both[TILE:, 128:])
        peak = jnp.where(low_lanes, peaks[0], peaks[1])
        mixed = jnp.where(low_lanes, both[:TILE, :128], both[TILE:, :128]) / total
        out_ref[start:stop] = mixed
        scaled_ref[start:stop] = (mixed * scale).astype(BF)
        lse = (peak * factor + jnp.log2(total)).T
        lse_ref[0, 0:1, start:stop] = lse[0:1]
        lse_ref[0, 1:2, start:stop] = lse[64:65]


def project_pair(first_ref, weights, bias, proj_ref):
    proj_ref[0] = (dot_nn(first_ref[...], weights) + bias).astype(BF)


def three(proj_ref):
    return [proj_ref.at[0, :, pl.ds(part * 128, 128)] for part in range(3)]


def plain_first_kernel(
    lengths_ref,
    tokens_ref,
    wq_ref,
    wk_ref,
    wv_ref,
    vectors_ref,
    bq_ref,
    bv_ref,
    hs_ref,
    first_ref,
    proj_ref,
    scaled_ref,
    attended_ref,
    lse_ref,
    vext_ref,
):
    @pl.when(pl.program_id(0) == 0)
    def _():
        for start in range(0, tokens_ref.shape[0], TILE):
            rows = pl.ds(start, TILE)
            normed, _ = row_norm(tokens_ref[rows].astype(F32))
            first_ref[rows] = (normed * vectors_ref[3:4] + vectors_ref[4:5]).astype(BF)

    weights = jnp.concatenate([wq_ref[...], wk_ref[...], wv_ref[...]], axis=1)
    bias = jnp.concatenate([bq_ref[0:1], jnp.zeros((1, 128), F32), bv_ref[1:2]], axis=1)
    project_pair(first_ref, weights, bias, proj_ref)
    attention_pair(
        cross_flag(lengths_ref, tokens_ref), *three(proj_ref), hs_ref[...], scaled_ref, attended_ref, lse_ref, vext_ref
    )


def plain_first(lengths, tokens, weights, vectors, head_lanes):
    rows, width = tokens.shape
    pairs = width // 128
    column = pl.BlockSpec((rows, 128), lambda p: (0, p))
    bias = pl.BlockSpec((16, 128), lambda p: (0, p))
    return pl.pallas_call(
        plain_first_kernel,
        grid=(pairs,),
        in_specs=[
            pl.BlockSpec(memory_space=pltpu.SMEM),
            whole((rows, width)),
            pl.BlockSpec((width, 128), lambda p: (0, p)),
            pl.BlockSpec((width, 128), lambda p: (0, pairs + p)),
            pl.BlockSpec((width, 128), lambda p: (0, 2 * pairs + p)),
            whole(vectors.shape),
            bias,
            bias,
            pl.BlockSpec((1, 128), lambda p: (0, p)),
        ],
        out_specs=[
            whole((rows, width)),
            pl.BlockSpec((1, rows, 384), lambda p: (p, 0, 0)),
            column,
            column,
            pl.BlockSpec((1, 8, rows), lambda p: (p, 0, 0)),
        ],
        out_shape=[
            jax.ShapeDtypeStruct((rows, width), BF),
            jax.ShapeDtypeStruct((pairs, rows, 384), BF),
            jax.ShapeDtypeStruct((rows, width), BF),
            jax.ShapeDtypeStruct((rows, width), F32),
            jax.ShapeDtypeStruct((pairs, 8, rows), F32),
        ],
        scratch_shapes=[pltpu.VMEM((rows, 256), BF)],
        compiler_params=params(),
        name="plain_first",
    )(lengths, tokens, weights, weights, weights, vectors, vectors, vectors, head_lanes)


def out_proj_rows(scaled_ref, weight_ref, vec_ref, tokens_ref, branch_ref, middle_ref):
    branch = dot_nn(scaled_ref[...], weight_ref[...]) + vec_ref[2:3]
    normed, _ = row_norm(branch)
    middle = tokens_ref[...].astype(F32) + (normed * vec_ref[5:6] + vec_ref[6:7])
    again, _ = row_norm(middle)
    branch_ref[...] = branch
    middle_ref[...] = middle
    return (again * vec_ref[7:8] + vec_ref[8:9]).astype(BF)


def out_proj_kernel(scaled_ref, weight_ref, vec_ref, tokens_ref, branch_ref, middle_ref, feed_ref):
    feed_ref[...] = out_proj_rows(
        scaled_ref, weight_ref, vec_ref, tokens_ref, branch_ref, middle_ref
    )


def out_proj(scaled, weights, vectors, tokens):
    rows, width = tokens.shape
    by_row = pl.BlockSpec((TILE, width), lambda i: (i, 0))
    return pl.pallas_call(
        out_proj_kernel,
        grid=(rows // TILE,),
        in_specs=[
            by_row,
            whole((width, width)),
            whole(vectors.shape),
            by_row,
        ],
        out_specs=[by_row, by_row, by_row],
        out_shape=[
            jax.ShapeDtypeStruct((rows, width), F32),
            jax.ShapeDtypeStruct((rows, width), F32),
            jax.ShapeDtypeStruct((rows, width), BF),
        ],
        compiler_params=params(),
        name="out_proj",
    )(scaled, weights, vectors, tokens)


def phi_and_slope(value):
    bell = jnp.exp2(value * value * (-0.5 * LOG2E))
    t = 1.0 / (1.0 + (0.3275911 * ROOT_HALF) * jnp.abs(value))
    series = t * (
        0.5 * 0.254829592
        + t
        * (
            0.5 * -0.284496736
            + t * (0.5 * 1.421413741 + t * (0.5 * -1.453152027 + t * (0.5 * 1.061405429)))
        )
    )
    tail = series * bell
    area = jnp.where(value < 0.0, tail, 1.0 - tail)
    return value * area, area + value * bell * INV_ROOT_TAU


def up_step(feed_ref, up_ref, vec_ref, act_ref, slope_ref, sums_ref):
    for left in range(0, UNITS, TILE):
        columns = slice(left, left + TILE)
        pre = dot_nn(feed_ref[...], up_ref[0, :, columns])
        bias = vec_ref[0, 0:1, columns].astype(F32)
        for start in range(0, feed_ref.shape[0], SLIM):
            rows = slice(start, start + SLIM)
            act, slope = phi_and_slope(pre[rows] + bias)
            act_ref[0, rows, columns] = act.astype(BF)
            slope_ref[0, rows, columns] = slope.astype(BF)
            sums_ref[0, rows] += lane_fold(act)
            sums_ref[1, rows] += lane_fold(act * act)


def side_by_side(*columns):
    lane = lax.broadcasted_iota(jnp.int32, (1, 128), 1)
    result = jnp.broadcast_to(columns[-1], (columns[-1].shape[0], 128))
    for index in range(len(columns) - 2, -1, -1):
        result = jnp.where(lane == index, columns[index], result)
    return result


def up_stats(units, stats_ref, sums_ref):
    for start in range(0, stats_ref.shape[0], TILE):
        rows = pl.ds(start, TILE)
        mean = jnp.sum(sums_ref[0, rows], axis=1, keepdims=True) / units
        square = jnp.sum(sums_ref[1, rows], axis=1, keepdims=True) / units
        inv = lax.rsqrt(square - mean * mean + EPS)
        stats_ref[rows] = side_by_side(mean, inv)


def up_kernel(units, feed_ref, up_ref, vec_ref, act_ref, slope_ref, stats_ref, sums_ref):
    step = pl.program_id(0)

    @pl.when(step == 0)
    def _():
        sums_ref[...] = jnp.zeros_like(sums_ref)

    up_step(feed_ref, up_ref, vec_ref, act_ref, slope_ref, sums_ref)

    @pl.when(step == pl.num_programs(0) - 1)
    def _():
        up_stats(units, stats_ref, sums_ref)


def up_pass(feed, up, vec):
    rows, width = feed.shape
    steps = up.shape[0]
    block = pl.BlockSpec((1, rows, UNITS), lambda j: (j, 0, 0))
    return pl.pallas_call(
        functools.partial(up_kernel, steps * UNITS),
        grid=(steps,),
        in_specs=[
            whole((rows, width)),
            pl.BlockSpec((1, width, UNITS), lambda j: (j, 0, 0)),
            pl.BlockSpec((1, vec.shape[1], UNITS), lambda j: (j, 0, 0)),
        ],
        out_specs=[block, block, whole((rows, 128))],
        out_shape=[
            jax.ShapeDtypeStruct((steps, rows, UNITS), BF),
            jax.ShapeDtypeStruct((steps, rows, UNITS), BF),
            jax.ShapeDtypeStruct((rows, 128), F32),
        ],
        scratch_shapes=[pltpu.VMEM((2, rows, 128), F32)],
        compiler_params=params(),
        name="up_pass",
    )(feed, up, vec)


def down_kernel(
    units,
    act_ref,
    stats_ref,
    vec_ref,
    down_ref,
    cot_ref,
    middle_ref,
    shift_ref,
    mixed_ref,
    down_grad_ref,
    e_ref,
    all_stats_ref,
    vec_grad_ref,
    total_ref,
    sums_ref,
    low_ref,
):
    step = pl.program_id(0)
    last = pl.num_programs(0) - 1
    rows_all = cot_ref.shape[0]

    @pl.when(step == 0)
    def _():
        total_ref[...] = jnp.zeros_like(total_ref)
        sums_ref[...] = jnp.zeros_like(sums_ref)

    gain = vec_ref[0, 1:2].astype(F32)
    shift = vec_ref[0, 2:3].astype(F32)
    slims = [slice(start, start + SLIM) for start in range(0, rows_all, SLIM)]

    def normalized(rows, columns):
        value = act_ref[0, rows, columns].astype(F32)
        return (value - stats_ref[rows, 0:1]) * stats_ref[rows, 1:2]

    for rows in slims:
        low_ref[rows] = (normalized(rows, slice(0, UNITS)) * gain + shift).astype(BF)
    for left in range(0, UNITS, TILE):
        columns = slice(left, left + TILE)
        grads = dot_nt(cot_ref[...], down_ref[0, columns])
        gain_grad = jnp.zeros((SLIM, TILE), F32)
        bias_grad = jnp.zeros((SLIM, TILE), F32)
        for rows in slims:
            normed = normalized(rows, columns)
            grad = grads[rows]
            gain_grad = gain_grad + grad * normed
            bias_grad = bias_grad + grad
            e = grad * gain[:, columns]
            e_ref[0, rows, columns] = e.astype(BF)
            sums_ref[0, rows] += lane_fold(e)
            sums_ref[1, rows] += lane_fold(e * normed)
        vec_grad_ref[0, 0:1, columns] = column_sum(gain_grad)
        vec_grad_ref[0, 1:2, columns] = column_sum(bias_grad)
    for left in range(0, total_ref.shape[1], TILE):
        columns = slice(left, left + TILE)
        total_ref[:, columns] += dot_nn(low_ref[...], down_ref[0, :, columns])
    for left in range(0, UNITS, TILE):
        columns = slice(left, left + TILE)
        down_grad_ref[0, columns] = dot_tn(low_ref[:, columns], cot_ref[...]).astype(BF)

    @pl.when(step == last)
    def _():
        for start in range(0, rows_all, TILE):
            rows = pl.ds(start, TILE)
            mixed_ref[rows] = (
                middle_ref[rows] + total_ref[rows] + shift_ref[...].astype(F32)
            ).astype(BF)
            first = jnp.sum(sums_ref[0, rows], axis=1, keepdims=True) / units
            cross = jnp.sum(sums_ref[1, rows], axis=1, keepdims=True) / units
            all_stats_ref[rows] = side_by_side(
                stats_ref[rows, 0:1], stats_ref[rows, 1:2], first, cross
            )


def down_pass(act, stats, vec, down, cotangent, middle, shift):
    rows, width = cotangent.shape
    steps = act.shape[0]
    block = pl.BlockSpec((1, rows, UNITS), lambda j: (j, 0, 0))
    return pl.pallas_call(
        functools.partial(down_kernel, steps * UNITS),
        grid=(steps,),
        in_specs=[
            block,
            whole((rows, 128)),
            pl.BlockSpec((1, vec.shape[1], UNITS), lambda j: (j, 0, 0)),
            pl.BlockSpec((1, UNITS, width), lambda j: (j, 0, 0)),
            whole((rows, width)),
            whole((rows, width)),
            whole((1, width)),
        ],
        out_specs=[
            whole((rows, width)),
            pl.BlockSpec((1, UNITS, width), lambda j: (j, 0, 0)),
            block,
            whole((rows, 128)),
            pl.BlockSpec((1, 8, UNITS), lambda j: (j, 0, 0)),
        ],
        out_shape=[
            jax.ShapeDtypeStruct((rows, width), BF),
            jax.ShapeDtypeStruct((steps, UNITS, width), BF),
            jax.ShapeDtypeStruct((steps, rows, UNITS), BF),
            jax.ShapeDtypeStruct((rows, 128), F32),
            jax.ShapeDtypeStruct((steps, 8, UNITS), F32),
        ],
        scratch_shapes=[
            pltpu.VMEM((rows, width), F32),
            pltpu.VMEM((2, rows, 128), F32),
            pltpu.VMEM((rows, UNITS), BF),
        ],
        compiler_params=params(),
        name="down_pass",
    )(act, stats, vec, down, cotangent, middle, shift)


def up_back_step(act, slope, e, stats_ref, up, low_ref, total_ref):
    bias_grad = jnp.zeros((SLIM, UNITS), F32)
    for start in range(0, total_ref.shape[0], SLIM):
        rows = slice(start, start + SLIM)
        inv = stats_ref[rows, 1:2]
        normed = (act[rows].astype(F32) - stats_ref[rows, 0:1]) * inv
        grad_act = inv * (
            e[rows].astype(F32) - stats_ref[rows, 2:3] - normed * stats_ref[rows, 3:4]
        )
        low = (grad_act * slope[rows].astype(F32)).astype(BF)
        bias_grad = bias_grad + low.astype(F32)
        low_ref[rows, 0:UNITS] = low
    for left in range(0, total_ref.shape[1], TILE):
        columns = slice(left, left + TILE)
        total_ref[:, columns] += dot_nt(low_ref[:, 0:UNITS], up[columns])
    return column_sum(bias_grad)


def up_back_kernel(
    act_ref,
    slope_ref,
    e_ref,
    stats_ref,
    up_ref,
    feed_ref,
    up_grad_ref,
    bias_grad_ref,
    total_ref,
    turned_ref,
    low_ref,
):
    @pl.when(pl.program_id(0) == 0)
    def _():
        total_ref[...] = jnp.zeros_like(total_ref)
        turned_ref[...] = feed_ref[...].T

    bias_grad_ref[0, 0:1] = up_back_step(
        act_ref.at[0],
        slope_ref.at[0],
        e_ref.at[0],
        stats_ref,
        up_ref.at[0],
        low_ref,
        total_ref,
    )
    up_grad_ref[0] = dot_nn(turned_ref[...], low_ref[...]).astype(BF)


def up_back(act, slope, e, stats, up, feed):
    rows, width = feed.shape
    steps = act.shape[0]
    block = pl.BlockSpec((1, rows, UNITS), lambda j: (j, 0, 0))
    narrow = whole((rows, 128))
    return pl.pallas_call(
        up_back_kernel,
        grid=(steps,),
        in_specs=[
            block,
            block,
            block,
            narrow,
            pl.BlockSpec((1, width, UNITS), lambda j: (j, 0, 0)),
            whole((rows, width)),
        ],
        out_specs=[
            pl.BlockSpec((1, width, UNITS), lambda j: (j, 0, 0)),
            pl.BlockSpec((1, 8, UNITS), lambda j: (j, 0, 0)),
            whole((rows, width)),
        ],
        out_shape=[
            jax.ShapeDtypeStruct((steps, width, UNITS), BF),
            jax.ShapeDtypeStruct((steps, 8, UNITS), F32),
            jax.ShapeDtypeStruct((rows, width), F32),
        ],
        scratch_shapes=[pltpu.VMEM((width, rows), BF), pltpu.VMEM((rows, UNITS), BF)],
        compiler_params=params(),
        name="up_back",
    )(act, slope, e, stats, up, feed)


def norms_back(grad_feed, cot_ref, middle_ref, branch_ref, vec_ref, sums_ref):
    normed, inv = row_norm(middle_ref[...])
    cot = cot_ref[...].astype(F32)
    grad_middle = cot + norm_back(grad_feed, vec_ref[7:8], normed, inv)
    sums_ref[7:8] += column_sum(grad_feed * normed)
    sums_ref[8:9] += column_sum(grad_feed)
    sums_ref[9:10] += column_sum(cot)
    normed, inv = row_norm(branch_ref[...])
    low = norm_back(grad_middle, vec_ref[5:6], normed, inv).astype(BF)
    sums_ref[5:6] += column_sum(grad_middle * normed)
    sums_ref[6:7] += column_sum(grad_middle)
    sums_ref[2:3] += column_sum(low.astype(F32))
    return grad_middle, low


def heads_back(low, weights, scale, attended):
    grad_out = (dot_nt(low, weights) * scale).astype(BF)
    product = grad_out.astype(F32) * attended
    high = product.astype(BF)
    rest = (product - high.astype(F32)).astype(BF)
    heads = (
        lax.broadcasted_iota(jnp.int32, (product.shape[1], 128), 0) // 64
        == lax.broadcasted_iota(jnp.int32, (product.shape[1], 128), 1)
    ).astype(BF)
    return grad_out, dot_nn(high, heads) + dot_nn(rest, heads)


def out_back_kernel(
    grad_feed_ref,
    cot_ref,
    middle_ref,
    branch_ref,
    scaled_ref,
    attended_ref,
    weight_ref,
    vec_ref,
    hs_ref,
    grad_middle_ref,
    ga_ref,
    out_grad_ref,
    delta_ref,
    sums_ref,
    total_ref,
):
    step = pl.program_id(0)

    @pl.when(step == 0)
    def _():
        total_ref[...] = jnp.zeros_like(total_ref)
        sums_ref[...] = jnp.zeros_like(sums_ref)

    grad_middle, low = norms_back(
        grad_feed_ref[...], cot_ref, middle_ref, branch_ref, vec_ref, sums_ref
    )
    grad_middle_ref[...] = grad_middle
    ga_ref[...], delta = heads_back(low, weight_ref[...], hs_ref[...], attended_ref[...])
    total_ref[...] += dot_tn(scaled_ref[...], low)
    delta_ref[...] = delta.T[: delta_ref.shape[0]]

    @pl.when(step == pl.num_programs(0) - 1)
    def _():
        out_grad_ref[...] = total_ref[...].astype(BF)


def out_back(
    grad_feed, cotangent, middle, branch, scaled, attended, weights, vectors, head_lanes
):
    rows, width = cotangent.shape
    heads = 2 * width // 128
    by_row = pl.BlockSpec((TILE, width), lambda i: (i, 0))
    return pl.pallas_call(
        out_back_kernel,
        grid=(rows // TILE,),
        in_specs=[
            by_row,
            by_row,
            by_row,
            by_row,
            by_row,
            by_row,
            whole((width, width)),
            whole(vectors.shape),
            whole((1, width)),
        ],
        out_specs=[
            by_row,
            by_row,
            whole((width, width)),
            pl.BlockSpec((heads, TILE), lambda i: (0, i)),
            whole((16, width)),
        ],
        out_shape=[
            jax.ShapeDtypeStruct((rows, width), F32),
            jax.ShapeDtypeStruct((rows, width), BF),
            jax.ShapeDtypeStruct((width, width), BF),
            jax.ShapeDtypeStruct((heads, rows), F32),
            jax.ShapeDtypeStruct((16, width), F32),
        ],
        scratch_shapes=[pltpu.VMEM((width, width), F32)],
        compiler_params=params(),
        name="out_back",
    )(
        grad_feed,
        cotangent,
        middle,
        branch,
        scaled,
        attended,
        weights,
        vectors,
        head_lanes,
    )


def attention_back_keys(
    starts, cross, q_ref, k_ref, v_ref, ga_ref, lse_ref, deltas, dq_ref, dk_ref, dv_ref
):
    rows = q_ref.shape[0]
    half = rows // 2
    factor = LOG2E * 64 ** (-0.5)
    low_lanes = lax.broadcasted_iota(jnp.int32, (1, 128), 1) < 64
    above = lax.broadcasted_iota(jnp.int32, (TILE, TILE), 0) <= lax.broadcasted_iota(
        jnp.int32, (TILE, TILE), 1
    )

    def pick(both):
        return jnp.where(low_lanes, both[:TILE], both[TILE:])

    for start in starts:
        stop = start + TILE
        keys = k_ref[start:stop]
        keys_apart = stacked(keys, low_lanes)
        values_apart = stacked(v_ref[start:stop], low_lanes)
        dk = jnp.zeros((TILE, 128), F32)
        dv = jnp.zeros((TILE, 128), F32)
        for left, right in ((start, half), (half, rows)) if start < half else ((start, rows),):
            raw = dot_nt(keys_apart, q_ref[left:right])
            grad_weights = dot_nt(values_apart, ga_ref[left:right])
            weights, grad_scores = [], []
            for head in range(2):
                mine = slice(head * TILE, (head + 1) * TILE)
                level = lse_ref[0, head : head + 1, left:right]
                if start < half <= left:
                    level = level - cross
                exponent = raw[mine] * factor - level
                if left == start:
                    first = jnp.where(above, exponent[:, :TILE], MASKED)
                    exponent = (
                        first
                        if right - left == TILE
                        else jnp.concatenate([first, exponent[:, TILE:]], axis=1)
                    )
                weight = jnp.exp2(exponent)
                weights.append(weight.astype(BF))
                delta = deltas[head][:, left:right]
                grad_scores.append((weight * (grad_weights[mine] - delta)).astype(BF))
            dv = dv + pick(dot_nn(jnp.concatenate(weights, axis=0), ga_ref[left:right]))
            dk = dk + pick(dot_nn(jnp.concatenate(grad_scores, axis=0), q_ref[left:right]))
            dq = jnp.where(low_lanes, dot_tn(grad_scores[0], keys), dot_tn(grad_scores[1], keys))
            if start == 0:
                dq_ref[left:right] = dq
            else:
                dq_ref[left:right] += dq
        dk_ref[start:stop] = dk
        dv_ref[start:stop] = dv


def in_back_pair(dq_ref, dk_ref, dv_ref, weights, turned_ref, out_grad_ref, chunk_ref, total_ref):
    factor = 64 ** (-0.5)
    dq = (dq_ref[...] * factor).astype(BF)
    dk = (dk_ref[...] * factor).astype(BF)
    dv = dv_ref[...].astype(BF)
    grads = jnp.concatenate([dq, dk, dv], axis=1)
    shares = dot_nn(turned_ref[...], grads).astype(BF)
    for start in range(0, total_ref.shape[0], TILE):
        part = jnp.concatenate(
            [shares[start : start + TILE], out_grad_ref[start : start + TILE]], axis=1
        )
        chunk_ref[:, start // TILE] = part.reshape(8, 32, 512)
        columns = slice(start, start + TILE)
        total_ref[:, columns] += dot_nt(grads, weights[columns])
    return column_sum(dq.astype(F32)), column_sum(dv.astype(F32))


def tokens_back(tokens, grad, grad_middle, gain):
    normed, inv = row_norm(tokens.astype(F32))
    back = norm_back(grad, gain, normed, inv)
    return (grad_middle + back).astype(BF), column_sum(grad * normed), column_sum(grad)


def in_back_kernel(
    lengths_ref,
    proj_ref,
    ga_ref,
    lse_ref,
    delta_ref,
    wq_ref,
    wk_ref,
    wv_ref,
    first_ref,
    out_grad_ref,
    tokens_ref,
    gain_ref,
    grad_middle_ref,
    chunk_ref,
    bias_ref,
    tokens_grad_ref,
    sums_ref,
    dq_ref,
    dk_ref,
    dv_ref,
    turned_ref,
    total_ref,
):
    step = pl.program_id(0)
    q_ref, k_ref, v_ref = three(proj_ref)
    rows_all = tokens_ref.shape[0]

    @pl.when(step == 0)
    def _():
        turned_ref[...] = first_ref[...].T
        total_ref[...] = jnp.zeros_like(total_ref)

    deltas = [delta_ref[0, head : head + 1] for head in range(2)]
    attention_back_keys(
        range(0, rows_all, TILE),
        cross_flag(lengths_ref, tokens_ref),
        q_ref,
        k_ref,
        v_ref,
        ga_ref,
        lse_ref,
        deltas,
        dq_ref,
        dk_ref,
        dv_ref,
    )
    weights = jnp.concatenate([wq_ref[...], wk_ref[...], wv_ref[...]], axis=1)
    query_sum, value_sum = in_back_pair(
        dq_ref, dk_ref, dv_ref, weights, turned_ref, out_grad_ref, chunk_ref.at[0], total_ref
    )
    bias_ref[0, 0:1] = query_sum
    bias_ref[0, 1:2] = value_sum

    @pl.when(step == pl.num_programs(0) - 1)
    def _():
        gain_grad = jnp.zeros((1, total_ref.shape[1]), F32)
        shift_grad = jnp.zeros((1, total_ref.shape[1]), F32)
        for start in range(0, rows_all, TILE):
            rows = pl.ds(start, TILE)
            tokens_grad_ref[rows], gain_part, shift_part = tokens_back(
                tokens_ref[rows], total_ref[rows], grad_middle_ref[rows], gain_ref[...]
            )
            gain_grad = gain_grad + gain_part
            shift_grad = shift_grad + shift_part
        sums_ref[0:1] = gain_grad
        sums_ref[1:2] = shift_grad


def in_back(lengths, projected, ga, lse, delta, weights, first, out_grad, tokens, gain, grad_middle):
    rows, width = tokens.shape
    pairs = width // 128
    column = pl.BlockSpec((rows, 128), lambda p: (0, p))
    square = whole((rows, width))
    return pl.pallas_call(
        in_back_kernel,
        grid=(pairs,),
        in_specs=[
            pl.BlockSpec(memory_space=pltpu.SMEM),
            pl.BlockSpec((1, rows, 384), lambda p: (p, 0, 0)),
            column,
            pl.BlockSpec((1, 8, rows), lambda p: (p, 0, 0)),
            pl.BlockSpec((1, 2, rows), lambda p: (p, 0, 0)),
            pl.BlockSpec((width, 128), lambda p: (0, p)),
            pl.BlockSpec((width, 128), lambda p: (0, pairs + p)),
            pl.BlockSpec((width, 128), lambda p: (0, 2 * pairs + p)),
            square,
            column,
            square,
            whole((1, width)),
            square,
        ],
        out_specs=[
            pl.BlockSpec((1, 8, width // TILE, 32, 512), lambda p: (p, 0, 0, 0, 0)),
            pl.BlockSpec((1, 8, 128), lambda p: (p, 0, 0)),
            square,
            whole((8, width)),
        ],
        out_shape=[
            jax.ShapeDtypeStruct((pairs, 8, width // TILE, 32, 512), BF),
            jax.ShapeDtypeStruct((pairs, 8, 128), F32),
            jax.ShapeDtypeStruct((rows, width), BF),
            jax.ShapeDtypeStruct((8, width), F32),
        ],
        scratch_shapes=[
            pltpu.VMEM((rows, 128), F32),
            pltpu.VMEM((rows, 128), F32),
            pltpu.VMEM((rows, 128), F32),
            pltpu.VMEM((width, rows), BF),
            pltpu.VMEM((rows, width), F32),
        ],
        compiler_params=params(),
        name="in_back",
    )(
        lengths,
        projected,
        ga,
        lse,
        delta,
        weights,
        weights,
        weights,
        first,
        out_grad,
        tokens,
        gain,
        grad_middle,
    )


class Place:
    def __init__(self):
        self.z = lax.axis_index("dp")
        wide = lax.axis_index("wide")
        self.y = wide // 4
        self.x = (wide // 2) % 2
        self.c = wide % 2
        self.core = (self.z, wide + 1 - 2 * self.c)
        self.side = (self.z, wide + 2 - 4 * self.x)
        self.over = (self.z, wide + 4 - 8 * self.y)
        self.ranks = (self.z + 1 - 2 * (self.z % 2), (self.z + 2) % 4, 3 - self.z)
        self.planes = tuple((rank, wide) for rank in self.ranks)

    def greet(self, planes=True):
        barrier = pltpu.get_barrier_semaphore()
        peers = (self.core, self.side, self.over) + (self.planes if planes else ())
        for peer in peers:
            pl.semaphore_signal(barrier, inc=1, device_id=peer, device_id_type=MESH)
        pl.semaphore_wait(barrier, len(peers))


class WideGather:
    copies = 10

    def __init__(self, place, view, count, send, recv, first, source=None, last=None):
        y, x, c = place.y, place.x, place.c
        here, side, over, far = (y, x, c), (y, 1 - x, c), (1 - y, x, c), (1 - y, 1 - x, c)
        upper, lower = pl.ds(0, count // 2), pl.ds(count // 2, count // 2)
        both = pl.ds(0, count)

        def copy(index, slot, part, peer):
            destination = view(*slot, part)
            return pltpu.make_async_remote_copy(
                src_ref=source.at[part] if source is not None and slot is here else destination,
                dst_ref=destination,
                send_sem=send.at[first + index],
                recv_sem=recv.at[first + index],
                device_id=peer,
                device_id_type=MESH,
            )

        self.all = (
            copy(0, here, upper, place.side),
            copy(1, here, lower, place.over),
            copy(2, here, upper, place.over),
            copy(3, here, lower, place.side),
            copy(4, here, both, place.core),
            copy(5, side, upper, place.over),
            copy(6, over, lower, place.side),
            copy(7, side, both, place.core),
            copy(8, over, both, place.core),
            copy(9, far, both, place.core),
        )
        self.own = None
        if source is not None and last is not None:
            self.own = pltpu.make_async_copy(source, view(*here, both), last)

    def start(self):
        if self.own is not None:
            self.own.start()
        for index in range(5):
            self.all[index].start()

    def relay(self, stage):
        waits, starts = (((0, 1), (5, 6)), ((2, 3), (7, 8)), ((5, 6), (9,)))[stage]
        for index in waits:
            self.all[index].wait_recv()
        for index in starts:
            self.all[index].start()

    def finish(self):
        for index in (4, 7, 8, 9):
            self.all[index].wait_recv()
        for copy in self.all:
            copy.wait_send()
        if self.own is not None:
            self.own.wait()


def blocks_of(target):
    return lambda y, x, c, rows: target.at[y, x, c, rows]


LAG = 2


class Reduction:
    slots = 2
    deep = 3
    keep = 4

    @classmethod
    def scratch(cls):
        n, k = cls.slots, cls.keep
        return [
            pltpu.VMEM((cls.deep, 2, 2, 4, 64, 512), BF),
            pltpu.VMEM((n, 2, 2, 4, 64, 512), BF),
            pltpu.VMEM((n, 2, 2, 4, 32, 512), BF),
            pltpu.VMEM((n, 2, 4, 32, 512), BF),
            pltpu.VMEM((n, 4, 64, 512), BF),
            pltpu.VMEM((n, 3, 64, 512), BF),
            pltpu.VMEM((n, 64, 512), BF),
            pltpu.VMEM((k, 3, 64, 512), BF),
            pltpu.SemaphoreType.DMA((6, k)),
            pltpu.SemaphoreType.DMA((6, k)),
            pltpu.SemaphoreType.DMA((cls.deep,)),
        ]

    def __init__(self, place, refs):
        self.place = place
        (
            self.chip,
            self.partner,
            self.first,
            self.second,
            self.plane,
            self.from_z,
            self.sums,
            self.shared,
            self.send,
            self.recv,
            self.local,
        ) = refs

    def copy(self, index, slot, source, target, peer):
        return pltpu.make_async_remote_copy(
            src_ref=source,
            dst_ref=target,
            send_sem=self.send.at[index, slot],
            recv_sem=self.recv.at[index, slot],
            device_id=peer,
            device_id_type=MESH,
        )

    def wait(self, index, slot, arrived):
        self.copy(index, slot, arrived, arrived, self.place.core).wait()

    def load(self, chunk, source):
        slot = chunk % self.deep
        return pltpu.make_async_copy(source, self.chip.at[slot], self.local.at[slot])

    def stage0(self, chunk, view):
        slot, c = chunk % self.slots, self.place.c
        self.copy(
            0, slot, view.at[:, :, 1 - c], self.partner.at[slot], self.place.core
        ).start()
        self.load(chunk, view.at[:, :, c]).start()

    def stage1(self, chunk):
        p, slot, index = self.place, chunk % self.slots, chunk % self.deep
        partner, chip, target = self.partner.at[slot], self.chip.at[index], self.first.at[slot]
        self.load(chunk, partner).wait()
        self.wait(0, slot, partner)
        chip[...] += partner[...]
        self.copy(1, slot, chip.at[:, 1 - p.x, :, pl.ds(0, 32)], target.at[0], p.side).start()
        self.copy(1, slot, chip.at[1 - p.y, :, :, pl.ds(32, 32)], target.at[1], p.over).start()

    def stage2(self, chunk):
        p, slot, index = self.place, chunk % self.slots, chunk % self.deep
        chip, arrived, target = self.chip.at[index], self.first.at[slot], self.second.at[slot]
        self.wait(1, slot, arrived)
        for k in range(2):
            chip[k, p.x, :, 0:32] += arrived[0, k]
            chip[p.y, k, :, 32:64] += arrived[1, k]
        self.copy(2, slot, chip.at[1 - p.y, p.x, :, pl.ds(0, 32)], target.at[0], p.over).start()
        self.copy(2, slot, chip.at[p.y, 1 - p.x, :, pl.ds(32, 32)], target.at[1], p.side).start()

    def stage3(self, chunk):
        p, slot, index = self.place, chunk % self.slots, chunk % self.deep
        arrived, mine, plane = self.second.at[slot], self.chip.at[index, p.y, p.x], self.plane
        self.wait(2, slot, arrived)
        plane[slot, :, 0:32] = mine[:, 0:32] + arrived[0]
        plane[slot, :, 32:64] = mine[:, 32:64] + arrived[1]
        for k in range(3):
            target = self.from_z.at[slot, k]
            self.copy(3, slot, plane.at[slot, p.ranks[k]], target, p.planes[k]).start()

    def stage4(self, chunk):
        slot = chunk % self.slots
        self.wait(3, slot, self.from_z.at[slot])
        total = self.plane[slot, self.place.z].astype(F32)
        for k in range(3):
            total = total + self.from_z[slot, k].astype(F32)
        return total

    def spread(self, chunk, total):
        slot, place = chunk % self.slots, chunk % self.keep
        self.sums[slot] = total.astype(BF)
        peer = self.place.planes[1]
        self.copy(4, place, self.sums.at[slot], self.shared.at[place, 0], peer).start()

    def stage5(self, chunk):
        slot, place, peer = chunk % self.slots, chunk % self.keep, self.place.planes[0]
        shared = self.shared.at[place]
        self.wait(4, place, shared.at[0])
        self.copy(5, place, self.sums.at[slot], shared.at[1], peer).start()
        self.copy(5, place, shared.at[0], shared.at[2], peer).start()

    def stage6(self, chunk):
        slot, place, ranks = chunk % self.slots, chunk % self.keep, self.place.ranks
        self.wait(5, place, self.shared.at[place, pl.ds(1, 2)])
        return [
            (self.place.z, self.sums[slot]),
            (ranks[1], self.shared[place, 0]),
            (ranks[0], self.shared[place, 1]),
            (ranks[2], self.shared[place, 2]),
        ]


class SmallReduction:
    @staticmethod
    def scratch():
        return [
            pltpu.VMEM((2, 2, 2, 4, 16, 512), BF),
            pltpu.VMEM((2, 2, 4, 16, 512), BF),
            pltpu.VMEM((2, 2, 4, 16, 512), BF),
            pltpu.VMEM((2, 4, 16, 512), BF),
            pltpu.VMEM((4, 16, 512), BF),
            pltpu.VMEM((3, 16, 512), BF),
            pltpu.SemaphoreType.DMA((4,)),
            pltpu.SemaphoreType.DMA((4,)),
        ]

    def __init__(self, place, refs):
        self.place = place
        self.source, self.chip, self.partner, self.first, self.second, self.from_z = refs[:6]
        self.send, self.recv = refs[6:]

    def copy(self, index, source, target, peer):
        return pltpu.make_async_remote_copy(
            src_ref=source,
            dst_ref=target,
            send_sem=self.send.at[index],
            recv_sem=self.recv.at[index],
            device_id=peer,
            device_id_type=MESH,
        )

    def wait(self, index, arrived):
        self.copy(index, arrived, arrived, self.place.core).wait()

    def stage0(self):
        p = self.place
        self.copy(0, self.source.at[:, :, 1 - p.c], self.partner, p.core).start()

    def stage1(self):
        p = self.place
        self.wait(0, self.partner)
        self.chip[...] = self.source[:, :, p.c] + self.partner[...]
        self.copy(1, self.chip.at[:, 1 - p.x], self.first, p.side).start()

    def stage2(self):
        p = self.place
        self.wait(1, self.first)
        for k in range(2):
            self.chip[k, p.x] += self.first[k]
        self.copy(2, self.chip.at[1 - p.y, p.x], self.second, p.over).start()

    def stage3(self):
        p = self.place
        self.wait(2, self.second)
        self.chip[p.y, p.x] += self.second[...]
        for k in range(3):
            block = self.chip.at[p.y, p.x, p.ranks[k]]
            self.copy(3, block, self.from_z.at[k], p.planes[k]).start()

    def stage4(self):
        p = self.place
        self.wait(3, self.from_z)
        total = self.chip[p.y, p.x, p.z].astype(F32)
        for k in range(3):
            total = total + self.from_z[k].astype(F32)
        return total


def dma_sems(count):
    return [pltpu.SemaphoreType.DMA((count,)), pltpu.SemaphoreType.DMA((count,))]


def to_planes(place, mine, landing, send, recv, first):
    return [
        pltpu.make_async_remote_copy(
            src_ref=mine,
            dst_ref=landing(k),
            send_sem=send.at[first + k],
            recv_sem=recv.at[first + k],
            device_id=place.planes[k],
            device_id_type=MESH,
        )
        for k in range(3)
    ]


class PlanesLast:
    copies = WideGather.copies + 6

    def __init__(self, place, source, target, send, recv, last):
        view = blocks_of(target.at[place.z])
        self.wide = WideGather(place, view, source.shape[0], send, recv, 0, source, last)

        def copy(index, rank, peer):
            blocks = target.at[rank, :, :, place.c]
            return pltpu.make_async_remote_copy(
                src_ref=blocks,
                dst_ref=blocks,
                send_sem=send.at[WideGather.copies + index],
                recv_sem=recv.at[WideGather.copies + index],
                device_id=peer,
                device_id_type=MESH,
            )

        self.across = [copy(k, place.z, place.planes[k]) for k in range(3)]
        self.over = [copy(3 + k, place.ranks[k], place.core) for k in range(3)]

    def start_across(self):
        self.wide.own.wait()
        for copy in self.across:
            copy.start()

    def start_over(self):
        for arrived, copy in zip(self.across, self.over):
            arrived.wait_recv()
            copy.start()

    def finish(self):
        self.wide.own = None
        self.wide.finish()
        for copy in self.across:
            copy.wait_send()
        for copy in self.over:
            copy.wait()


def first_kernel(
    lengths_ref,
    tokens_ref,
    in_ref,
    vec_ref,
    out_ref,
    up_ref,
    unit_ref,
    hs_ref,
    turned_ref,
    proj_ref,
    scaled_ref,
    scaled_turned_ref,
    attended_ref,
    lse_ref,
    vectors_ref,
    scale_ref,
    in_all,
    out_all,
    up_all,
    unit_all,
    held_ref,
    normed_ref,
    first_ref,
    vext_ref,
    send_in,
    recv_in,
    send_out,
    recv_out,
    send_ff,
    recv_ff,
    local,
):
    step = pl.program_id(0)
    place = Place()
    width = tokens_ref.shape[1]
    count = WideGather.copies
    lanes = (3 * width // 2 + 128, 3 * width // 2)
    across, early, late = [], [], None
    for group in range(2):
        held = held_ref.at[group, :, :, :, :, :, pl.ds(0, lanes[group])]
        first = group * (3 + 2 * count)

        def blocks(planes, held=held):
            return lambda y, x, c, rows: held.at[planes, y, x, c, rows]

        mine = held.at[0, place.y, place.x, place.c]
        across.append(
            to_planes(
                place,
                mine,
                lambda k, held=held: held.at[k + 1, place.y, place.x, place.c],
                send_in,
                recv_in,
                first,
            )
        )
        if group == 0:
            for part, planes in enumerate((pl.ds(0, 1), pl.ds(1, 3))):
                start = first + 3 + part * count
                early.append(WideGather(place, blocks(planes), 32, send_in, recv_in, start))
        else:
            late = WideGather(place, blocks(pl.ds(0, 4)), 32, send_in, recv_in, first + 3)
    orders = (place.z, *place.ranks)
    out = PlanesLast(place, out_ref, out_all, send_out, recv_out, local.at[2])
    up = WideGather(
        place, blocks_of(up_all), width, send_ff, recv_ff, 0, up_ref, local.at[3]
    )
    unit = WideGather(
        place, blocks_of(unit_all), 32, send_ff, recv_ff, count, unit_ref, local.at[4]
    )
    keep = [
        pltpu.make_async_copy(
            held_ref.at[group, index, :, :, :, :, pl.ds(0, lanes[group])],
            in_all.at[group, rank, :, :, :, :, pl.ds(0, lanes[group])],
            local.at[12 + 4 * group + index],
        )
        for group in range(2)
        for index, rank in enumerate(orders)
    ]

    @pl.when(step == 0)
    def _():
        place.greet()
        half = width // 2
        for group in range(2):
            mine = held_ref.at[group, 0, place.y, place.x, place.c]
            fills = [
                pltpu.make_async_copy(
                    in_ref.at[:, pl.ds(part * width + group * half, half)],
                    mine.at[:, pl.ds(part * half, half)],
                    local.at[6 + 3 * group + part],
                )
                for part in range(3)
            ]
            for copy in fills:
                copy.start()
            if group == 0:
                mine[:, 3 * half : 3 * half + 128] = jnp.zeros((32, 128), BF)
                mine[:, 3 * half : 3 * half + 32] = vec_ref[...]
            for copy in fills:
                copy.wait()
            for copy in across[group]:
                copy.start()
            if group == 0:
                early[0].start()
        scale = hs_ref[...].astype(F32)
        for pair in range(width // 128):
            own = slice(pair * 128, (pair + 1) * 128)
            low_lanes = lax.broadcasted_iota(jnp.int32, (1, 128), 1) < 64
            scale_ref[0:1, own] = jnp.where(
                low_lanes, scale[:, 2 * pair : 2 * pair + 1], scale[:, 2 * pair + 1 : 2 * pair + 2]
            )
        for start in range(0, tokens_ref.shape[0], TILE):
            rows = pl.ds(start, TILE)
            normed, _ = row_norm(tokens_ref[rows].astype(F32))
            normed_ref[rows] = normed
        early[0].relay(0)
        for copy in across[0]:
            copy.wait_recv()
        early[1].start()
        early[0].relay(1)
        early[0].relay(2)
        early[1].relay(0)
        early[1].relay(1)
        for copy in across[1]:
            copy.wait_recv()
        late.start()
        early[1].relay(2)
        out.wide.start()
        unit.start()
        for part in early:
            part.finish()
        for z in range(4):
            for y in range(2):
                tile = jnp.zeros((16, 128), F32)
                for x in range(2):
                    for c in range(2):
                        piece = held_ref[
                            0, orders[z], y, x, c, 0:16, 3 * half : 3 * half + 128
                        ].astype(F32)
                        spot = 32 * (2 * x + c)
                        tile = tile + (piece if spot == 0 else pltpu.roll(piece, spot, 1))
                vectors_ref[:, (2 * z + y) * 128 : (2 * z + y + 1) * 128] = tile
        for start in range(0, tokens_ref.shape[0], TILE):
            rows = pl.ds(start, TILE)
            first_ref[rows] = (normed_ref[rows] * vectors_ref[3:4] + vectors_ref[4:5]).astype(BF)

    @pl.when((step >= 2) & (step <= 4))
    def _():
        for stage in range(3):

            @pl.when(step == 2 + stage)
            def _():
                late.relay(stage)
                out.wide.relay(stage)
                unit.relay(stage)

    @pl.when(step == 2)
    def _():
        up.start()

    @pl.when(step == 4)
    def _():
        out.start_across()

    @pl.when(step == 5)
    def _():
        late.finish()
        for copy in keep:
            copy.start()

    for stage, at in enumerate((5, 7, 8)):

        @pl.when(step == at)
        def _():
            up.relay(stage)

    @pl.when(step == 7)
    def _():
        out.start_over()

    @pl.when(step > 0)
    def _():
        pair = step - 1
        columns = [
            pl.ds(pl.multiple_of(part * (width // 2) + pair % 4 * 128, 128), 128)
            for part in range(3)
        ]
        weights = jnp.concatenate(
            [
                jnp.concatenate(
                    [held_ref[pair // 4, order, :, :, :, :, cols].reshape(TILE, 128) for order in orders]
                )
                for cols in columns
            ],
            axis=1,
        )
        own = pl.ds(pl.multiple_of(pair * 128, 128), 128)
        bias = jnp.concatenate(
            [vectors_ref[0:1, own], jnp.zeros((1, 128), F32), vectors_ref[1:2, own]], axis=1
        )
        project_pair(first_ref, weights, bias, proj_ref)
        attention_pair(
            cross_flag(lengths_ref, tokens_ref),
            *three(proj_ref),
            scale_ref[0:1, own],
            scaled_ref,
            attended_ref,
            lse_ref,
            vext_ref,
        )
        scaled_turned_ref[...] = scaled_ref[...].T

    @pl.when(step == pl.num_programs(0) - 1)
    def _():
        turned_ref[...] = first_ref[...].T
        for copy in (*across[0], *across[1]):
            copy.wait_send()
        for copy in keep:
            copy.wait()
        out.finish()
        unit.finish()
        up.finish()


def first_part(lengths, tokens, in_weight, vec, out_weight, up_weight, unit_rows, head_scale):
    rows, width = tokens.shape
    pairs = width // 128

    def at(step):
        return jnp.maximum(step - 1, 0)

    column = pl.BlockSpec((rows, 128), lambda s: (0, at(s)))
    held = (2, 4, 2, 2, 2, 32, 3 * width // 2 + 128)
    return pl.pallas_call(
        first_kernel,
        grid=(pairs + 1,),
        in_specs=[
            pl.BlockSpec(memory_space=pltpu.SMEM),
            whole((rows, width)),
            ANY,
            whole(vec.shape),
            ANY,
            ANY,
            ANY,
            whole(head_scale.shape),
        ],
        out_specs=[
            whole((width, rows)),
            pl.BlockSpec((1, rows, 384), lambda s: (at(s), 0, 0)),
            column,
            pl.BlockSpec((128, rows), lambda s: (at(s), 0)),
            column,
            pl.BlockSpec((1, 8, rows), lambda s: (at(s), 0, 0)),
            whole((16, width)),
            whole((8, width)),
            ANY,
            ANY,
            ANY,
            ANY,
        ],
        out_shape=[
            jax.ShapeDtypeStruct((width, rows), BF),
            jax.ShapeDtypeStruct((pairs, rows, 384), BF),
            jax.ShapeDtypeStruct((rows, width), BF),
            jax.ShapeDtypeStruct((width, rows), BF),
            jax.ShapeDtypeStruct((rows, width), F32),
            jax.ShapeDtypeStruct((pairs, 8, rows), F32),
            jax.ShapeDtypeStruct((16, width), F32),
            jax.ShapeDtypeStruct((8, width), F32),
            jax.ShapeDtypeStruct(held, BF),
            jax.ShapeDtypeStruct((4, 2, 2, 2, *out_weight.shape), BF),
            jax.ShapeDtypeStruct((2, 2, 2, *up_weight.shape), BF),
            jax.ShapeDtypeStruct((2, 2, 2, *unit_rows.shape), BF),
        ],
        scratch_shapes=[
            pltpu.VMEM(held, BF),
            pltpu.VMEM((rows, width), F32),
            pltpu.VMEM((rows, width), BF),
            pltpu.VMEM((rows, 256), BF),
            *dma_sems(6 + 3 * WideGather.copies),
            *dma_sems(PlanesLast.copies),
            *dma_sems(2 * WideGather.copies),
            pltpu.SemaphoreType.DMA((20,)),
        ],
        compiler_params=params(collective_id=0, has_side_effects=True),
        name="first_part",
    )(lengths, tokens, in_weight, vec, out_weight, up_weight, unit_rows, head_scale)


def second_kernel(
    units,
    scaled_ref,
    weight_ref,
    vec_ref,
    tokens_ref,
    up_ref,
    unit_ref,
    down_ref,
    branch_ref,
    middle_ref,
    turned_ref,
    act_ref,
    slope_ref,
    stats_ref,
    down_all,
    feed_ref,
    sums_ref,
    send,
    recv,
    local,
):
    step = pl.program_id(0)
    lead = feed_ref.shape[0] // TILE
    place = Place()
    down = WideGather(
        place, blocks_of(down_all), UNITS, send, recv, 0, down_ref, local.at[0]
    )

    @pl.when(step == 0)
    def _():
        place.greet(planes=False)
        down.start()
        sums_ref[...] = jnp.zeros_like(sums_ref)

    for stage, at in enumerate((5, 8, 11)):

        @pl.when(step == at)
        def _():
            down.relay(stage)

    @pl.when(step < lead)
    def _():
        rows = pl.ds(pl.multiple_of(step * TILE, TILE), TILE)
        feed_ref[rows] = out_proj_rows(
            scaled_ref, weight_ref, vec_ref, tokens_ref, branch_ref, middle_ref
        )

    @pl.when(step >= lead)
    def _():
        up_step(feed_ref, up_ref, unit_ref, act_ref, slope_ref, sums_ref)

    @pl.when(step == pl.num_programs(0) - 1)
    def _():
        up_stats(units, stats_ref, sums_ref)
        turned_ref[...] = feed_ref[...].T
        down.finish()


def second_part(scaled, out_weights, vectors, tokens, up, unit_vec, down_weight):
    rows, width = tokens.shape
    steps = up.shape[0]
    lead = rows // TILE

    def early(step):
        return jnp.minimum(step, lead - 1)

    def late(step):
        return jnp.maximum(step - lead, 0)

    by_row = pl.BlockSpec((TILE, width), lambda s: (early(s), 0))
    block = pl.BlockSpec((1, rows, UNITS), lambda s: (late(s), 0, 0))
    return pl.pallas_call(
        functools.partial(second_kernel, steps * UNITS),
        grid=(lead + steps,),
        in_specs=[
            by_row,
            whole((width, width)),
            whole(vectors.shape),
            by_row,
            pl.BlockSpec((1, width, UNITS), lambda s: (late(s), 0, 0)),
            pl.BlockSpec((1, unit_vec.shape[1], UNITS), lambda s: (late(s), 0, 0)),
            ANY,
        ],
        out_specs=[
            by_row,
            by_row,
            whole((width, rows)),
            block,
            block,
            whole((rows, 128)),
            ANY,
        ],
        out_shape=[
            jax.ShapeDtypeStruct((rows, width), F32),
            jax.ShapeDtypeStruct((rows, width), F32),
            jax.ShapeDtypeStruct((width, rows), BF),
            jax.ShapeDtypeStruct((steps, rows, UNITS), BF),
            jax.ShapeDtypeStruct((steps, rows, UNITS), BF),
            jax.ShapeDtypeStruct((rows, 128), F32),
            jax.ShapeDtypeStruct((2, 2, 2, *down_weight.shape), BF),
        ],
        scratch_shapes=[
            pltpu.VMEM((rows, width), BF),
            pltpu.VMEM((2, rows, 128), F32),
            *dma_sems(WideGather.copies),
            pltpu.SemaphoreType.DMA((1,)),
        ],
        compiler_params=params(collective_id=2, has_side_effects=True),
        name="second_part",
    )(scaled, out_weights, vectors, tokens, up, unit_vec, down_weight)


NORMS_AT, COLUMNS_AT, HEADS_AT, TOKENS_AT, VECTORS_AT = 8, 16, 20, 36, 40
BACK_STEPS = VECTORS_AT + 5
OUT_TILE = 128


def chunk_at(time):
    chunk = jnp.where(time < 8, time // 2, (time + 8) // 4)
    chunk = jnp.where(time >= 23, (time + 9) // 4, chunk)
    there = ((time < 8) & (time % 2 == 0)) | ((time >= 8) & (time <= 20) & (time % 4 == 0))
    there = there | ((time >= 23) & (time < 36) & (time % 4 == 3))
    return chunk, there & (time >= 0)


def back_kernel(
    lengths_ref,
    act_ref,
    slope_ref,
    e_ref,
    stats_ref,
    up_ref,
    feed_turned_ref,
    unit_grad_ref,
    down_grad_all,
    cot_ref,
    middle_ref,
    branch_ref,
    scaled_turned_ref,
    attended_ref,
    out_weight_ref,
    vec_ref,
    hs_ref,
    proj_ref,
    lse_ref,
    wq_ref,
    wk_ref,
    wv_ref,
    turned_ref,
    tokens_ref,
    tokens_grad_ref,
    down_out,
    up_out,
    attn_out,
    vec_out,
    up_grad_all,
    staged_ref,
    total_ref,
    low_ref,
    out_grad_ref,
    ga_ref,
    grad_middle_ref,
    delta_ref,
    delta_sum_ref,
    sums_ref,
    units_ref,
    dq_ref,
    dk_ref,
    dv_ref,
    chunk_ref,
    store_sems,
    *scratch,
):
    step = pl.program_id(0)
    place = Place()
    engine = Reduction(place, scratch[:11])
    small = SmallReduction(place, scratch[11:])

    @pl.when(step == 0)
    def _():
        place.greet()
        total_ref[...] = jnp.zeros_like(total_ref)
        sums_ref[...] = jnp.zeros_like(sums_ref)
        units_ref[...] = jnp.zeros_like(units_ref)

    def store(block):
        view = up_grad_all.at[block // 4, block // 2 % 2, block % 2]
        return pltpu.make_async_copy(staged_ref, view, store_sems.at[0])

    @pl.when((step >= 1) & (step <= NORMS_AT))
    def _():
        store(step - 1).wait()


    def stage(number, low, high, action):
        chunk, there = chunk_at(step - number * LAG)

        @pl.when(there & (chunk >= low) & (chunk < high))
        def _():
            action(chunk)

    def put_down(chunk):
        for rank, block in engine.stage6(chunk):
            for half in range(2):

                @pl.when(chunk % 2 == half)
                def _():
                    down_out[chunk // 2, rank, :, half * 512 : half * 512 + 512] = block

    def put_up(chunk):
        for rank, block in engine.stage6(chunk):
            up_out[chunk - 4, rank] = block

    def put_own(chunk):
        attn_out[chunk - 8] = engine.stage4(chunk)

    def take_down(chunk):
        lanes = pl.ds(pl.multiple_of(chunk % 2 * 512, 512), 512)
        engine.stage0(chunk, down_grad_all.at[:, :, :, chunk // 2, :, :, lanes])

    def take_up(chunk):
        engine.stage0(chunk, up_grad_all.at[:, :, :, chunk - 4])

    def take_own(chunk):
        engine.stage0(chunk, chunk_ref)

    stage(6, 0, 4, put_down)
    stage(6, 4, 8, put_up)
    stage(5, 0, 8, engine.stage5)
    stage(4, 0, 8, lambda chunk: engine.spread(chunk, engine.stage4(chunk)))
    stage(4, 8, 12, put_own)
    stage(3, 0, 12, engine.stage3)
    stage(2, 0, 12, engine.stage2)
    stage(1, 0, 12, engine.stage1)
    stage(0, 0, 4, take_down)
    stage(0, 4, 8, take_up)


    @pl.when(step < NORMS_AT)
    def _():
        units_ref[step, 0:1] = up_back_step(
            act_ref.at[0],
            slope_ref.at[0],
            e_ref.at[0],
            stats_ref,
            up_ref.at[0],
            low_ref,
            total_ref,
        )
        units_ref[step, 1:3] = unit_grad_ref[step, 0:2]
        for left in range(0, UNITS, TILE):
            columns = slice(left, left + TILE)
            grad = dot_nn(feed_turned_ref[...], low_ref[:, columns]).astype(BF)
            staged_ref[:, :, :, columns] = grad.reshape(4, 4, 64, TILE)
        store(step).start()


    @pl.when((step >= NORMS_AT) & (step < COLUMNS_AT))
    def _():
        rows = pl.ds(pl.multiple_of((step - NORMS_AT) * OUT_TILE, OUT_TILE), OUT_TILE)
        grad_middle, low = norms_back(
            total_ref[rows], cot_ref, middle_ref, branch_ref, vec_ref, sums_ref
        )
        grad_middle_ref[rows] = grad_middle
        low_ref[rows] = low

    @pl.when((step >= COLUMNS_AT) & (step < HEADS_AT))
    def _():
        block = step - COLUMNS_AT
        columns = pl.ds(pl.multiple_of(block * TILE, TILE), TILE)
        grad_out, delta = heads_back(
            low_ref[...], out_weight_ref[columns], hs_ref[0:1, columns], attended_ref[...]
        )
        ga_ref[:, columns] = grad_out
        delta_sum_ref[block, 0:1] = column_sum(delta)
        turned = delta.T
        for head in range(4):
            delta_ref[4 * block + head] = turned[head : head + 1]
        out_grad_ref[:, columns] = dot_nn(scaled_turned_ref[...], low_ref[:, columns]).astype(BF)

    @pl.when(step == HEADS_AT - 1)
    def _():
        total_ref[...] = jnp.zeros_like(total_ref)


    @pl.when((step >= HEADS_AT) & (step < TOKENS_AT))
    def _():
        index = step - HEADS_AT
        pair = index // 2
        columns = pl.ds(pl.multiple_of(pair * 128, 128), 128)
        for part, starts in enumerate(((0, 3 * TILE), (TILE, 2 * TILE))):

            @pl.when(index % 2 == part)
            def _():
                attention_back_keys(
                    starts,
                    cross_flag(lengths_ref, total_ref),
                    *three(proj_ref),
                    ga_ref.at[:, columns],
                    lse_ref,
                    [delta_ref[2 * pair], delta_ref[2 * pair + 1]],
                    dq_ref,
                    dk_ref,
                    dv_ref,
                )

        @pl.when(index % 2 == 1)
        def _():
            weights = jnp.concatenate([wq_ref[...], wk_ref[...], wv_ref[...]], axis=1)
            query_sum, value_sum = in_back_pair(
                dq_ref,
                dk_ref,
                dv_ref,
                weights,
                turned_ref,
                out_grad_ref.at[:, columns],
                chunk_ref.reshape(8, 4, 64, 512).at[
                    :, :, pl.ds(pl.multiple_of(pair % 2 * 32, 32), 32)
                ],
                total_ref,
            )
            sums_ref[0:1, columns] = query_sum
            sums_ref[1:2, columns] = value_sum

    @pl.when((step >= TOKENS_AT) & (step < TOKENS_AT + 4))
    def _():
        rows = pl.ds(pl.multiple_of((step - TOKENS_AT) * TILE, TILE), TILE)
        tokens_grad_ref[...], gain_grad, shift_grad = tokens_back(
            tokens_ref[...], total_ref[rows], grad_middle_ref[rows], vec_ref[3:4]
        )
        sums_ref[3:4] += gain_grad
        sums_ref[4:5] += shift_grad

    stage(0, 8, 12, take_own)


    @pl.when(step == VECTORS_AT)
    def _():
        for y in range(2):
            for z in range(4):
                own = slice((2 * z + y) * 128, (2 * z + y + 1) * 128)
                for index in range(9):
                    lanes = slice(index % 4 * 128, index % 4 * 128 + 128)
                    row = 6 + index // 4
                    units_ref[8, row : row + 1, lanes] = sums_ref[index : index + 1, own]
                for x in range(2):
                    for c in range(2):
                        unit = 4 * y + 2 * x + c
                        units_ref[8, 0:3] = units_ref[unit, 0:3]
                        if (y, z, x, c) == (0, 0, 0, 0):
                            units_ref[8, 3:4] = sums_ref[9:10, 0:UNITS]
                            units_ref[8, 4:5] = sums_ref[9:10, UNITS : 2 * UNITS]
                            for block in range(4):
                                lanes = slice(block * 128, block * 128 + 128)
                                units_ref[8, 5:6, lanes] = delta_sum_ref[block, 0:1]
                        small.source[y, x, c, z] = units_ref[8].astype(BF)
        small.stage0()

    for index, action in enumerate((small.stage1, small.stage2, small.stage3)):

        @pl.when(step == VECTORS_AT + 1 + index)
        def _():
            action()

    @pl.when(step == VECTORS_AT + 4)
    def _():
        vec_out[...] = small.stage4()


def back_part(
    lengths,
    act,
    slope,
    e,
    stats,
    up,
    feed_turned,
    unit_grad,
    down_grad,
    cotangent,
    middle,
    branch,
    scaled_turned,
    attended,
    out_weights,
    vectors,
    head_lanes,
    projected,
    lse,
    weights,
    turned,
    tokens,
):
    rows, width = tokens.shape
    pairs = width // 128

    def clamp(value, high):
        return jnp.minimum(jnp.maximum(value, 0), high)

    def unit(s):
        return clamp(s, 7)

    def pair(s):
        return clamp((s - HEADS_AT) // 2, pairs - 1)

    def tail(s):
        return clamp(s - TOKENS_AT, 3)

    def columns_of(part):
        return lambda s: (pair(s) // 4, 0, 4 * part + pair(s) % 4)

    block = pl.BlockSpec((1, rows, UNITS), lambda s: (unit(s), 0, 0))
    narrow = whole((rows, 128))
    by_row = pl.BlockSpec((OUT_TILE, width), lambda s: (clamp(s - NORMS_AT, 7), 0))
    square = whole((width, width))
    return pl.pallas_call(
        back_kernel,
        grid=(BACK_STEPS,),
        in_specs=[
            pl.BlockSpec(memory_space=pltpu.SMEM),
            block,
            block,
            block,
            narrow,
            pl.BlockSpec((1, width, UNITS), lambda s: (unit(s), 0, 0)),
            square,
            whole(unit_grad.shape),
            ANY,
            by_row,
            by_row,
            by_row,
            square,
            pl.BlockSpec((rows, TILE), lambda s: (0, clamp(s - COLUMNS_AT, 3))),
            square,
            whole(vectors.shape),
            whole(head_lanes.shape),
            pl.BlockSpec((1, rows, 384), lambda s: (pair(s), 0, 0)),
            pl.BlockSpec((1, 8, rows), lambda s: (pair(s), 0, 0)),
            *[pl.BlockSpec((None, width, 128), columns_of(part)) for part in range(3)],
            square,
            pl.BlockSpec((TILE, width), lambda s: (tail(s), 0)),
        ],
        out_specs=[
            pl.BlockSpec((TILE, width), lambda s: (tail(s), 0)),
            whole((2, 4, 64, 1024)),
            whole((4, 4, 64, 512)),
            whole((4, 64, 512)),
            whole((16, 512)),
            ANY,
        ],
        out_shape=[
            jax.ShapeDtypeStruct((rows, width), BF),
            jax.ShapeDtypeStruct((2, 4, 64, 1024), BF),
            jax.ShapeDtypeStruct((4, 4, 64, 512), BF),
            jax.ShapeDtypeStruct((4, 64, 512), F32),
            jax.ShapeDtypeStruct((16, 512), F32),
            jax.ShapeDtypeStruct((2, 2, 2, 4, 4, 64, UNITS), BF),
        ],
        scratch_shapes=[
            pltpu.VMEM((4, 4, 64, UNITS), BF),
            pltpu.VMEM((rows, width), F32),
            pltpu.VMEM((rows, width), BF),
            pltpu.VMEM((width, width), BF),
            pltpu.VMEM((rows, width), BF),
            pltpu.VMEM((rows, width), F32),
            pltpu.VMEM((2 * pairs, 1, rows), F32),
            pltpu.VMEM((4, 8, 128), F32),
            pltpu.VMEM((16, width), F32),
            pltpu.VMEM((9, 16, UNITS), F32),
            pltpu.VMEM((rows, 128), F32),
            pltpu.VMEM((rows, 128), F32),
            pltpu.VMEM((rows, 128), F32),
            pltpu.VMEM((2, 2, 2, 4, 64, 512), BF),
            pltpu.SemaphoreType.DMA((1,)),
            *Reduction.scratch(),
            *SmallReduction.scratch(),
        ],
        compiler_params=params(collective_id=1, has_side_effects=True),
        name="back_part",
    )(
        lengths,
        act,
        slope,
        e,
        stats,
        up,
        feed_turned,
        unit_grad,
        down_grad.reshape(2, 2, 2, 2, 4, 64, width),
        cotangent,
        middle,
        branch,
        scaled_turned,
        attended,
        out_weights,
        vectors,
        head_lanes,
        projected,
        lse,
        weights,
        weights,
        weights,
        turned,
        tokens,
    )


def layer(staged, tokens, cotangent, lengths, attn, up, down, unit_vec, head_scale, down_bias):
    rows, width = tokens.shape
    heads = head_scale.shape[0]
    pairs = width // 128
    if staged:
        in_weight, out_weight, vec_block = attn
        (
            turned,
            projected,
            scaled,
            scaled_turned,
            attended,
            lse,
            vectors,
            head_lanes,
            weights,
            out_weights,
            up,
            unit_vec,
        ) = first_part(
            lengths, tokens, in_weight, vec_block, out_weight, up, unit_vec, head_scale[None, :]
        )
        weights = weights.reshape(2, width, -1)
        out_weights = out_weights.reshape(width, width)
        up = up.reshape(-1, width, UNITS)
        unit_vec = unit_vec.reshape(-1, unit_vec.shape[-2], UNITS)
        branch, middle, feed_turned, act, slope, stats, down = second_part(
            scaled, out_weights, vectors, tokens, up, unit_vec, down
        )
        down = down.reshape(-1, UNITS, width)
    else:
        weights, out_weights, vectors = attn
        scale = head_scale.astype(F32)
        head_lanes = jnp.repeat(scale, width // heads)[None, :]
        first, projected, scaled, attended, lse = plain_first(
            lengths, tokens, weights, vectors, head_lanes
        )
        branch, middle, feed = out_proj(scaled, out_weights, vectors, tokens)
        act, slope, stats = up_pass(feed, up, unit_vec)
    mixed, down_grad, e, stats, unit_grad = down_pass(
        act, stats, unit_vec, down, cotangent, middle, down_bias[None, :]
    )
    if staged:
        tokens_grad, down_total, up_total, shares, vec_shares, _ = back_part(
            lengths,
            act,
            slope,
            e,
            stats,
            up,
            feed_turned,
            unit_grad,
            down_grad,
            cotangent,
            middle,
            branch,
            scaled_turned,
            attended,
            out_weights,
            vectors,
            head_lanes,
            projected,
            lse,
            weights,
            turned,
            tokens,
        )
        return mixed, tokens_grad, down_total, up_total, shares, vec_shares
    up_grad, up_bias_grad, grad_feed = up_back(
        act, slope, e, stats, up, feed
    )
    grad_middle, ga, out_grad, delta, sums = out_back(
        grad_feed,
        cotangent,
        middle,
        branch,
        scaled,
        attended,
        out_weights,
        vectors,
        head_lanes,
    )
    chunks, proj_bias, tokens_grad, pre_sums = in_back(
        lengths,
        projected,
        ga,
        lse,
        delta.reshape(pairs, 2, rows),
        weights,
        first,
        out_grad,
        tokens,
        vectors[3:4],
        grad_middle,
    )
    scale_grad = jnp.sum(delta, axis=1) / scale
    vec_grads = [
        proj_bias[:, 0].reshape(width),
        proj_bias[:, 1].reshape(width),
        sums[2],
        pre_sums[0],
        pre_sums[1],
        sums[5],
        sums[6],
        sums[7],
        sums[8],
    ]
    unit_grads = [up_bias_grad[:, 0], unit_grad[:, 0], unit_grad[:, 1]]
    return mixed, tokens_grad, chunks, up_grad, down_grad, vec_grads, unit_grads, sums[9], scale_grad


def body(
    axes,
    tokens,
    cotangent,
    lengths,
    in_weight,
    query_bias,
    value_bias,
    out_weight,
    out_bias,
    head_scale,
    pre_gain,
    pre_bias,
    post_gain,
    post_bias,
    feed_gain,
    feed_bias,
    up_weight,
    up_bias,
    mid_gain,
    mid_bias,
    down_weight,
    down_bias,
):
    planes, wide = axes
    every = ("dp", "wide")
    staged = (planes, wide) == (4, 8)
    rows, width = tokens.shape
    units = down_weight.shape[0] * wide
    steps = units // UNITS
    share = in_weight.shape[0]
    columns = [
        query_bias,
        value_bias,
        out_bias,
        pre_gain,
        pre_bias,
        post_gain,
        post_bias,
        feed_gain,
        feed_bias,
    ]
    index = lax.broadcasted_iota(jnp.int32, (32, up_bias.shape[0]), 0)
    unit_rows = jnp.where(index == 0, up_bias[None, :], jnp.zeros((), BF))
    unit_rows = jnp.where(index == 1, mid_gain[None, :], unit_rows)
    unit_rows = jnp.where(index == 2, mid_bias[None, :], unit_rows)
    if staged:
        index = lax.broadcasted_iota(jnp.int32, (32, share), 0)
        vec_block = jnp.zeros((32, share), BF)
        for row, column in enumerate(columns):
            vec_block = jnp.where(index == row, column[None, :], vec_block)
        attn = (in_weight, out_weight, vec_block)
        up, unit_vec, down = up_weight, unit_rows, down_weight
    else:
        flat = jnp.concatenate(columns).reshape(len(columns), share)
        attn = (
            lax.all_gather(in_weight, every, axis=0, tiled=True),
            lax.all_gather(out_weight, every, axis=0, tiled=True),
            jnp.pad(
                lax.all_gather(flat, every, axis=1, tiled=True), ((0, 16 - len(columns)), (0, 0))
            ).astype(F32),
        )
        up = lax.all_gather(up_weight, "wide", axis=1, tiled=True)
        up = up.reshape(width, steps, UNITS).transpose(1, 0, 2)
        unit_vec = lax.all_gather(unit_rows, "wide", axis=1, tiled=True)
        unit_vec = unit_vec.reshape(32, steps, UNITS).transpose(1, 0, 2)
        down = lax.all_gather(down_weight, "wide", axis=0, tiled=True)
        down = down.reshape(steps, UNITS, width)
    results = layer(
        staged,
        tokens,
        cotangent,
        lengths,
        attn,
        up,
        down,
        unit_vec,
        head_scale,
        down_bias,
    )
    heads = head_scale.shape[0]
    pairs = width // 128
    if staged:
        mixed, tokens_grad, down_total, up_total, shares, vec_shares = results
        up_total = up_total.astype(F32).reshape(width, UNITS)
        down_total = down_total.astype(F32).reshape(UNITS, width)
        unit_totals = [vec_shares[index] for index in range(3)]
        down_sum = vec_shares[3:5].reshape(width)
        scale_sum = vec_shares[5].reshape(4, 128)[:, :4].reshape(heads) / head_scale.astype(F32)
        offset = share * lax.rem(lax.axis_index("wide"), 128 // share)
        own = vec_shares[6:9].reshape(12, 128)
        own = lax.dynamic_slice(own, (0, offset), (len(columns), share))
        vec_totals = [own[index] for index in range(len(columns))]
        shares = shares.reshape(pairs, share, 512)
        in_total = shares[:, :, :384].reshape(pairs, share, 3, 128)
        in_total = in_total.transpose(1, 2, 0, 3).reshape(share, 3 * width)
        out_total = shares[:, :, 384:].transpose(1, 0, 2).reshape(share, width)
    else:
        (mixed, tokens_grad, chunks, up_grad, down_grad, vec_grads, unit_grads) = results[:7]
        down_sum, scale_sum = results[7:]

        def scatter(value, axis=0, over=every):
            return lax.psum_scatter(value, over, scatter_dimension=axis, tiled=True)

        def both_ways(value, axis):
            part = scatter(value.astype(BF), axis, "wide")
            return lax.psum(part, "dp").astype(F32)

        up_total = both_ways(up_grad.transpose(1, 0, 2).reshape(width, units), 1)
        down_total = both_ways(down_grad.reshape(units, width), 0)
        unit_totals = [
            lax.psum(scatter(item.reshape(units), 0, "wide"), "dp") for item in unit_grads
        ]
        down_sum, scale_sum = lax.psum((down_sum, scale_sum), every)
        vec_totals = [scatter(item) for item in vec_grads]
        natural = chunks.transpose(0, 2, 1, 3, 4).reshape(pairs, width, 512)
        in_total = natural[:, :, :384].reshape(pairs, width, 3, 128)
        in_total = scatter(in_total.transpose(1, 2, 0, 3).reshape(width, 3 * width).astype(F32))
        out_total = scatter(
            natural[:, :, 384:].transpose(1, 0, 2).reshape(width, width).astype(F32)
        )
    return (
        mixed,
        tokens_grad,
        in_total,
        vec_totals[0],
        vec_totals[1],
        out_total,
        vec_totals[2],
        scale_sum,
        vec_totals[3],
        vec_totals[4],
        vec_totals[5],
        vec_totals[6],
        vec_totals[7],
        vec_totals[8],
        up_total,
        unit_totals[0],
        unit_totals[1],
        unit_totals[2],
        down_total,
        down_sum,
    )


def solution(mesh):
    by_all = P(("dp", "wide"))
    rows_all = P(("dp", "wide"), None)
    axes = (mesh.shape["dp"], mesh.shape["wide"])
    return jax.shard_map(
        functools.partial(body, axes),
        mesh=mesh,
        in_specs=(
            rows_all,
            rows_all,
            rows_all,
            rows_all,
            by_all,
            by_all,
            rows_all,
            by_all,
            P(),
            by_all,
            by_all,
            by_all,
            by_all,
            by_all,
            by_all,
            P(None, "wide"),
            P("wide"),
            P("wide"),
            P("wide"),
            P("wide", None),
            P(),
        ),
        out_specs=(
            rows_all,
            rows_all,
            rows_all,
            by_all,
            by_all,
            rows_all,
            by_all,
            P(),
            by_all,
            by_all,
            by_all,
            by_all,
            by_all,
            by_all,
            P(None, "wide"),
            P("wide"),
            P("wide"),
            P("wide"),
            P("wide", None),
            P(),
        ),
        check_vma=False,
    )
```

```python
import functools

import jax
import jax.numpy as jnp
from jax import lax
from jax.experimental import pallas as pl
from jax.experimental.pallas import tpu as pltpu
from jax.sharding import PartitionSpec as P

EPS = 1e-05
ROOT_HALF = 0.7071067811865476
INV_ROOT_TAU = 0.3989422804014327
LOG2E = 1.4426950408889634
MASKED = -1e30
BF = jnp.bfloat16
F32 = jnp.float32
TILE = 256
UNITS = 512
SLIM = 64
MESH = pl.DeviceIdType.MESH
VMEM_LIMIT = 62 * 1024 * 1024
ANY = pl.BlockSpec(memory_space=pl.ANY)


def dot_nn(left, right):
    return lax.dot_general(left, right, (((1,), (0,)), ((), ())), preferred_element_type=F32)


def dot_nt(left, right):
    return lax.dot_general(left, right, (((1,), (1,)), ((), ())), preferred_element_type=F32)


def dot_tn(left, right):
    return lax.dot_general(left, right, (((0,), (0,)), ((), ())), preferred_element_type=F32)


def params(**more):
    return pltpu.CompilerParams(
        dimension_semantics=("arbitrary",), vmem_limit_bytes=VMEM_LIMIT, **more
    )


def whole(shape):
    zeros = (0,) * len(shape)
    return pl.BlockSpec(shape, lambda *_: zeros, pipeline_mode=pl.Buffered(1))


def row_norm(values):
    center = values - jnp.mean(values, axis=-1, keepdims=True)
    inv = lax.rsqrt(jnp.mean(center * center, axis=-1, keepdims=True) + EPS)
    return center * inv, inv


def norm_back(grad, gain, normed, inv):
    scaled = grad * gain
    first = jnp.mean(scaled, axis=-1, keepdims=True)
    cross = jnp.mean(scaled * normed, axis=-1, keepdims=True)
    return inv * (scaled - first - normed * cross)


def column_sum(values):
    return jnp.sum(values, axis=0, keepdims=True)


def lane_fold(values):
    total = values[:, :128]
    for start in range(128, values.shape[1], 128):
        total = total + values[:, start : start + 128]
    return total


def cross_flag(lengths_ref, rows_ref):
    return jnp.where(lengths_ref[0, 0] == rows_ref.shape[0], 0.0, MASKED)


def stacked(value, low_lanes):
    zero = jnp.zeros_like(value)
    return jnp.concatenate(
        [jnp.where(low_lanes, value, zero), jnp.where(low_lanes, zero, value)], axis=0
    )


def attention_pair(cross, q_ref, k_ref, v_ref, scale, scaled_ref, out_ref, lse_ref, vext_ref):
    rows = q_ref.shape[0]
    half = rows // 2
    factor = LOG2E * 64 ** (-0.5)
    low_lanes = lax.broadcasted_iota(jnp.int32, (1, 128), 1) < 64
    below = lax.broadcasted_iota(jnp.int32, (TILE, TILE), 1) <= lax.broadcasted_iota(
        jnp.int32, (TILE, TILE), 0
    )
    vext_ref[:, :128] = v_ref[...]
    vext_ref[:, 128:] = jnp.ones((rows, 128), BF)
    for start in range(0, rows, TILE):
        stop = start + TILE
        both = dot_nt(stacked(q_ref[start:stop], low_lanes), k_ref[:stop])
        peaks, weights = [], []
        for head in range(2):
            raw = both[head * TILE : (head + 1) * TILE]
            parts = []
            if start >= half:
                parts.append((raw[:, :half], cross))
                if start > half:
                    parts.append((raw[:, half:start], None))
            elif start > 0:
                parts.append((raw[:, :start], None))
            parts.append((jnp.where(below, raw[:, start:stop], MASKED), None))
            peak = None
            for piece, shift in parts:
                top = jnp.max(piece, axis=-1, keepdims=True)
                if shift is not None:
                    top = top + shift
                peak = top if peak is None else jnp.maximum(peak, top)
            peaks.append(peak)
            pieces = []
            for piece, shift in parts:
                level = peak if shift is None else peak - shift
                pieces.append(jnp.exp2((piece - level) * factor).astype(BF))
            weights.append(pieces[0] if len(pieces) == 1 else jnp.concatenate(pieces, axis=1))
        both = dot_nn(jnp.concatenate(weights, axis=0), vext_ref[:stop])
        total = jnp.where(low_lanes, both[:TILE, 128:], both[TILE:, 128:])
        peak = jnp.where(low_lanes, peaks[0], peaks[1])
        mixed = jnp.where(low_lanes, both[:TILE, :128], both[TILE:, :128]) / total
        out_ref[start:stop] = mixed
        scaled_ref[start:stop] = (mixed * scale).astype(BF)
        lse = (peak * factor + jnp.log2(total)).T
        lse_ref[0, 0:1, start:stop] = lse[0:1]
        lse_ref[0, 1:2, start:stop] = lse[64:65]


def project_pair(first_ref, weights, bias, proj_ref):
    proj_ref[0] = (dot_nn(first_ref[...], weights) + bias).astype(BF)


def three(proj_ref):
    return [proj_ref.at[0, :, pl.ds(part * 128, 128)] for part in range(3)]


def plain_first_kernel(
    lengths_ref,
    tokens_ref,
    wq_ref,
    wk_ref,
    wv_ref,
    vectors_ref,
    bq_ref,
    bv_ref,
    hs_ref,
    first_ref,
    proj_ref,
    scaled_ref,
    attended_ref,
    lse_ref,
    vext_ref,
):
    @pl.when(pl.program_id(0) == 0)
    def _():
        for start in range(0, tokens_ref.shape[0], TILE):
            rows = pl.ds(start, TILE)
            normed, _ = row_norm(tokens_ref[rows].astype(F32))
            first_ref[rows] = (normed * vectors_ref[3:4] + vectors_ref[4:5]).astype(BF)

    weights = jnp.concatenate([wq_ref[...], wk_ref[...], wv_ref[...]], axis=1)
    bias = jnp.concatenate([bq_ref[0:1], jnp.zeros((1, 128), F32), bv_ref[1:2]], axis=1)
    project_pair(first_ref, weights, bias, proj_ref)
    attention_pair(
        cross_flag(lengths_ref, tokens_ref), *three(proj_ref), hs_ref[...], scaled_ref, attended_ref, lse_ref, vext_ref
    )


def plain_first(lengths, tokens, weights, vectors, head_lanes):
    rows, width = tokens.shape
    pairs = width // 128
    column = pl.BlockSpec((rows, 128), lambda p: (0, p))
    bias = pl.BlockSpec((16, 128), lambda p: (0, p))
    return pl.pallas_call(
        plain_first_kernel,
        grid=(pairs,),
        in_specs=[
            pl.BlockSpec(memory_space=pltpu.SMEM),
            whole((rows, width)),
            pl.BlockSpec((width, 128), lambda p: (0, p)),
            pl.BlockSpec((width, 128), lambda p: (0, pairs + p)),
            pl.BlockSpec((width, 128), lambda p: (0, 2 * pairs + p)),
            whole(vectors.shape),
            bias,
            bias,
            pl.BlockSpec((1, 128), lambda p: (0, p)),
        ],
        out_specs=[
            whole((rows, width)),
            pl.BlockSpec((1, rows, 384), lambda p: (p, 0, 0)),
            column,
            column,
            pl.BlockSpec((1, 8, rows), lambda p: (p, 0, 0)),
        ],
        out_shape=[
            jax.ShapeDtypeStruct((rows, width), BF),
            jax.ShapeDtypeStruct((pairs, rows, 384), BF),
            jax.ShapeDtypeStruct((rows, width), BF),
            jax.ShapeDtypeStruct((rows, width), F32),
            jax.ShapeDtypeStruct((pairs, 8, rows), F32),
        ],
        scratch_shapes=[pltpu.VMEM((rows, 256), BF)],
        compiler_params=params(),
        name="plain_first",
    )(lengths, tokens, weights, weights, weights, vectors, vectors, vectors, head_lanes)


def out_proj_rows(scaled_ref, weight_ref, vec_ref, tokens_ref, branch_ref, middle_ref):
    branch = dot_nn(scaled_ref[...], weight_ref[...]) + vec_ref[2:3]
    normed, _ = row_norm(branch)
    middle = tokens_ref[...].astype(F32) + (normed * vec_ref[5:6] + vec_ref[6:7])
    again, _ = row_norm(middle)
    branch_ref[...] = branch
    middle_ref[...] = middle
    return (again * vec_ref[7:8] + vec_ref[8:9]).astype(BF)


def out_proj_kernel(scaled_ref, weight_ref, vec_ref, tokens_ref, branch_ref, middle_ref, feed_ref):
    feed_ref[...] = out_proj_rows(
        scaled_ref, weight_ref, vec_ref, tokens_ref, branch_ref, middle_ref
    )


def out_proj(scaled, weights, vectors, tokens):
    rows, width = tokens.shape
    by_row = pl.BlockSpec((TILE, width), lambda i: (i, 0))
    return pl.pallas_call(
        out_proj_kernel,
        grid=(rows // TILE,),
        in_specs=[
            by_row,
            whole((width, width)),
            whole(vectors.shape),
            by_row,
        ],
        out_specs=[by_row, by_row, by_row],
        out_shape=[
            jax.ShapeDtypeStruct((rows, width), F32),
            jax.ShapeDtypeStruct((rows, width), F32),
            jax.ShapeDtypeStruct((rows, width), BF),
        ],
        compiler_params=params(),
        name="out_proj",
    )(scaled, weights, vectors, tokens)


def phi_and_slope(value):
    bell = jnp.exp2(value * value * (-0.5 * LOG2E))
    t = 1.0 / (1.0 + (0.3275911 * ROOT_HALF) * jnp.abs(value))
    series = t * (
        0.5 * 0.254829592
        + t
        * (
            0.5 * -0.284496736
            + t * (0.5 * 1.421413741 + t * (0.5 * -1.453152027 + t * (0.5 * 1.061405429)))
        )
    )
    tail = series * bell
    area = jnp.where(value < 0.0, tail, 1.0 - tail)
    return value * area, area + value * bell * INV_ROOT_TAU


def up_step(feed_ref, up_ref, vec_ref, act_ref, slope_ref, sums_ref):
    for left in range(0, UNITS, TILE):
        columns = slice(left, left + TILE)
        pre = dot_nn(feed_ref[...], up_ref[0, :, columns])
        bias = vec_ref[0, 0:1, columns].astype(F32)
        for start in range(0, feed_ref.shape[0], SLIM):
            rows = slice(start, start + SLIM)
            act, slope = phi_and_slope(pre[rows] + bias)
            act_ref[0, rows, columns] = act.astype(BF)
            slope_ref[0, rows, columns] = slope.astype(BF)
            sums_ref[0, rows] += lane_fold(act)
            sums_ref[1, rows] += lane_fold(act * act)


def side_by_side(*columns):
    lane = lax.broadcasted_iota(jnp.int32, (1, 128), 1)
    result = jnp.broadcast_to(columns[-1], (columns[-1].shape[0], 128))
    for index in range(len(columns) - 2, -1, -1):
        result = jnp.where(lane == index, columns[index], result)
    return result


def up_stats(units, stats_ref, sums_ref):
    for start in range(0, stats_ref.shape[0], TILE):
        rows = pl.ds(start, TILE)
        mean = jnp.sum(sums_ref[0, rows], axis=1, keepdims=True) / units
        square = jnp.sum(sums_ref[1, rows], axis=1, keepdims=True) / units
        inv = lax.rsqrt(square - mean * mean + EPS)
        stats_ref[rows] = side_by_side(mean, inv)


def up_kernel(units, feed_ref, up_ref, vec_ref, act_ref, slope_ref, stats_ref, sums_ref):
    step = pl.program_id(0)

    @pl.when(step == 0)
    def _():
        sums_ref[...] = jnp.zeros_like(sums_ref)

    up_step(feed_ref, up_ref, vec_ref, act_ref, slope_ref, sums_ref)

    @pl.when(step == pl.num_programs(0) - 1)
    def _():
        up_stats(units, stats_ref, sums_ref)


def up_pass(feed, up, vec):
    rows, width = feed.shape
    steps = up.shape[0]
    block = pl.BlockSpec((1, rows, UNITS), lambda j: (j, 0, 0))
    return pl.pallas_call(
        functools.partial(up_kernel, steps * UNITS),
        grid=(steps,),
        in_specs=[
            whole((rows, width)),
            pl.BlockSpec((1, width, UNITS), lambda j: (j, 0, 0)),
            pl.BlockSpec((1, vec.shape[1], UNITS), lambda j: (j, 0, 0)),
        ],
        out_specs=[block, block, whole((rows, 128))],
        out_shape=[
            jax.ShapeDtypeStruct((steps, rows, UNITS), BF),
            jax.ShapeDtypeStruct((steps, rows, UNITS), BF),
            jax.ShapeDtypeStruct((rows, 128), F32),
        ],
        scratch_shapes=[pltpu.VMEM((2, rows, 128), F32)],
        compiler_params=params(),
        name="up_pass",
    )(feed, up, vec)


def down_kernel(
    units,
    act_ref,
    stats_ref,
    vec_ref,
    down_ref,
    cot_ref,
    middle_ref,
    shift_ref,
    mixed_ref,
    down_grad_ref,
    e_ref,
    all_stats_ref,
    vec_grad_ref,
    total_ref,
    sums_ref,
    low_ref,
):
    step = pl.program_id(0)
    last = pl.num_programs(0) - 1
    rows_all = cot_ref.shape[0]

    @pl.when(step == 0)
    def _():
        total_ref[...] = jnp.zeros_like(total_ref)
        sums_ref[...] = jnp.zeros_like(sums_ref)

    gain = vec_ref[0, 1:2].astype(F32)
    shift = vec_ref[0, 2:3].astype(F32)
    slims = [slice(start, start + SLIM) for start in range(0, rows_all, SLIM)]

    def normalized(rows, columns):
        value = act_ref[0, rows, columns].astype(F32)
        return (value - stats_ref[rows, 0:1]) * stats_ref[rows, 1:2]

    for rows in slims:
        low_ref[rows] = (normalized(rows, slice(0, UNITS)) * gain + shift).astype(BF)
    for left in range(0, UNITS, TILE):
        columns = slice(left, left + TILE)
        grads = dot_nt(cot_ref[...], down_ref[0, columns])
        gain_grad = jnp.zeros((SLIM, TILE), F32)
        bias_grad = jnp.zeros((SLIM, TILE), F32)
        for rows in slims:
            normed = normalized(rows, columns)
            grad = grads[rows]
            gain_grad = gain_grad + grad * normed
            bias_grad = bias_grad + grad
            e = grad * gain[:, columns]
            e_ref[0, rows, columns] = e.astype(BF)
            sums_ref[0, rows] += lane_fold(e)
            sums_ref[1, rows] += lane_fold(e * normed)
        vec_grad_ref[0, 0:1, columns] = column_sum(gain_grad)
        vec_grad_ref[0, 1:2, columns] = column_sum(bias_grad)
    for left in range(0, total_ref.shape[1], TILE):
        columns = slice(left, left + TILE)
        total_ref[:, columns] += dot_nn(low_ref[...], down_ref[0, :, columns])
    for left in range(0, UNITS, TILE):
        columns = slice(left, left + TILE)
        down_grad_ref[0, columns] = dot_tn(low_ref[:, columns], cot_ref[...]).astype(BF)

    @pl.when(step == last)
    def _():
        for start in range(0, rows_all, TILE):
            rows = pl.ds(start, TILE)
            mixed_ref[rows] = (
                middle_ref[rows] + total_ref[rows] + shift_ref[...].astype(F32)
            ).astype(BF)
            first = jnp.sum(sums_ref[0, rows], axis=1, keepdims=True) / units
            cross = jnp.sum(sums_ref[1, rows], axis=1, keepdims=True) / units
            all_stats_ref[rows] = side_by_side(
                stats_ref[rows, 0:1], stats_ref[rows, 1:2], first, cross
            )


def down_pass(act, stats, vec, down, cotangent, middle, shift):
    rows, width = cotangent.shape
    steps = act.shape[0]
    block = pl.BlockSpec((1, rows, UNITS), lambda j: (j, 0, 0))
    return pl.pallas_call(
        functools.partial(down_kernel, steps * UNITS),
        grid=(steps,),
        in_specs=[
            block,
            whole((rows, 128)),
            pl.BlockSpec((1, vec.shape[1], UNITS), lambda j: (j, 0, 0)),
            pl.BlockSpec((1, UNITS, width), lambda j: (j, 0, 0)),
            whole((rows, width)),
            whole((rows, width)),
            whole((1, width)),
        ],
        out_specs=[
            whole((rows, width)),
            pl.BlockSpec((1, UNITS, width), lambda j: (j, 0, 0)),
            block,
            whole((rows, 128)),
            pl.BlockSpec((1, 8, UNITS), lambda j: (j, 0, 0)),
        ],
        out_shape=[
            jax.ShapeDtypeStruct((rows, width), BF),
            jax.ShapeDtypeStruct((steps, UNITS, width), BF),
            jax.ShapeDtypeStruct((steps, rows, UNITS), BF),
            jax.ShapeDtypeStruct((rows, 128), F32),
            jax.ShapeDtypeStruct((steps, 8, UNITS), F32),
        ],
        scratch_shapes=[
            pltpu.VMEM((rows, width), F32),
            pltpu.VMEM((2, rows, 128), F32),
            pltpu.VMEM((rows, UNITS), BF),
        ],
        compiler_params=params(),
        name="down_pass",
    )(act, stats, vec, down, cotangent, middle, shift)


def up_back_step(act, slope, e, stats_ref, up, low_ref, total_ref):
    bias_grad = jnp.zeros((SLIM, UNITS), F32)
    for start in range(0, total_ref.shape[0], SLIM):
        rows = slice(start, start + SLIM)
        inv = stats_ref[rows, 1:2]
        normed = (act[rows].astype(F32) - stats_ref[rows, 0:1]) * inv
        grad_act = inv * (
            e[rows].astype(F32) - stats_ref[rows, 2:3] - normed * stats_ref[rows, 3:4]
        )
        low = (grad_act * slope[rows].astype(F32)).astype(BF)
        bias_grad = bias_grad + low.astype(F32)
        low_ref[rows, 0:UNITS] = low
    for left in range(0, total_ref.shape[1], TILE):
        columns = slice(left, left + TILE)
        total_ref[:, columns] += dot_nt(low_ref[:, 0:UNITS], up[columns])
    return column_sum(bias_grad)


def up_back_kernel(
    act_ref,
    slope_ref,
    e_ref,
    stats_ref,
    up_ref,
    feed_ref,
    up_grad_ref,
    bias_grad_ref,
    total_ref,
    turned_ref,
    low_ref,
):
    @pl.when(pl.program_id(0) == 0)
    def _():
        total_ref[...] = jnp.zeros_like(total_ref)
        turned_ref[...] = feed_ref[...].T

    bias_grad_ref[0, 0:1] = up_back_step(
        act_ref.at[0],
        slope_ref.at[0],
        e_ref.at[0],
        stats_ref,
        up_ref.at[0],
        low_ref,
        total_ref,
    )
    up_grad_ref[0] = dot_nn(turned_ref[...], low_ref[...]).astype(BF)


def up_back(act, slope, e, stats, up, feed):
    rows, width = feed.shape
    steps = act.shape[0]
    block = pl.BlockSpec((1, rows, UNITS), lambda j: (j, 0, 0))
    narrow = whole((rows, 128))
    return pl.pallas_call(
        up_back_kernel,
        grid=(steps,),
        in_specs=[
            block,
            block,
            block,
            narrow,
            pl.BlockSpec((1, width, UNITS), lambda j: (j, 0, 0)),
            whole((rows, width)),
        ],
        out_specs=[
            pl.BlockSpec((1, width, UNITS), lambda j: (j, 0, 0)),
            pl.BlockSpec((1, 8, UNITS), lambda j: (j, 0, 0)),
            whole((rows, width)),
        ],
        out_shape=[
            jax.ShapeDtypeStruct((steps, width, UNITS), BF),
            jax.ShapeDtypeStruct((steps, 8, UNITS), F32),
            jax.ShapeDtypeStruct((rows, width), F32),
        ],
        scratch_shapes=[pltpu.VMEM((width, rows), BF), pltpu.VMEM((rows, UNITS), BF)],
        compiler_params=params(),
        name="up_back",
    )(act, slope, e, stats, up, feed)


def norms_back(grad_feed, cot_ref, middle_ref, branch_ref, vec_ref, sums_ref):
    normed, inv = row_norm(middle_ref[...])
    cot = cot_ref[...].astype(F32)
    grad_middle = cot + norm_back(grad_feed, vec_ref[7:8], normed, inv)
    sums_ref[7:8] += column_sum(grad_feed * normed)
    sums_ref[8:9] += column_sum(grad_feed)
    sums_ref[9:10] += column_sum(cot)
    normed, inv = row_norm(branch_ref[...])
    low = norm_back(grad_middle, vec_ref[5:6], normed, inv).astype(BF)
    sums_ref[5:6] += column_sum(grad_middle * normed)
    sums_ref[6:7] += column_sum(grad_middle)
    sums_ref[2:3] += column_sum(low.astype(F32))
    return grad_middle, low


def heads_back(low, weights, scale, attended):
    grad_out = (dot_nt(low, weights) * scale).astype(BF)
    product = grad_out.astype(F32) * attended
    high = product.astype(BF)
    rest = (product - high.astype(F32)).astype(BF)
    heads = (
        lax.broadcasted_iota(jnp.int32, (product.shape[1], 128), 0) // 64
        == lax.broadcasted_iota(jnp.int32, (product.shape[1], 128), 1)
    ).astype(BF)
    return grad_out, dot_nn(high, heads) + dot_nn(rest, heads)


def out_back_kernel(
    grad_feed_ref,
    cot_ref,
    middle_ref,
    branch_ref,
    scaled_ref,
    attended_ref,
    weight_ref,
    vec_ref,
    hs_ref,
    grad_middle_ref,
    ga_ref,
    out_grad_ref,
    delta_ref,
    sums_ref,
    total_ref,
):
    step = pl.program_id(0)

    @pl.when(step == 0)
    def _():
        total_ref[...] = jnp.zeros_like(total_ref)
        sums_ref[...] = jnp.zeros_like(sums_ref)

    grad_middle, low = norms_back(
        grad_feed_ref[...], cot_ref, middle_ref, branch_ref, vec_ref, sums_ref
    )
    grad_middle_ref[...] = grad_middle
    ga_ref[...], delta = heads_back(low, weight_ref[...], hs_ref[...], attended_ref[...])
    total_ref[...] += dot_tn(scaled_ref[...], low)
    delta_ref[...] = delta.T[: delta_ref.shape[0]]

    @pl.when(step == pl.num_programs(0) - 1)
    def _():
        out_grad_ref[...] = total_ref[...].astype(BF)


def out_back(
    grad_feed, cotangent, middle, branch, scaled, attended, weights, vectors, head_lanes
):
    rows, width = cotangent.shape
    heads = 2 * width // 128
    by_row = pl.BlockSpec((TILE, width), lambda i: (i, 0))
    return pl.pallas_call(
        out_back_kernel,
        grid=(rows // TILE,),
        in_specs=[
            by_row,
            by_row,
            by_row,
            by_row,
            by_row,
            by_row,
            whole((width, width)),
            whole(vectors.shape),
            whole((1, width)),
        ],
        out_specs=[
            by_row,
            by_row,
            whole((width, width)),
            pl.BlockSpec((heads, TILE), lambda i: (0, i)),
            whole((16, width)),
        ],
        out_shape=[
            jax.ShapeDtypeStruct((rows, width), F32),
            jax.ShapeDtypeStruct((rows, width), BF),
            jax.ShapeDtypeStruct((width, width), BF),
            jax.ShapeDtypeStruct((heads, rows), F32),
            jax.ShapeDtypeStruct((16, width), F32),
        ],
        scratch_shapes=[pltpu.VMEM((width, width), F32)],
        compiler_params=params(),
        name="out_back",
    )(
        grad_feed,
        cotangent,
        middle,
        branch,
        scaled,
        attended,
        weights,
        vectors,
        head_lanes,
    )


def attention_back_keys(
    starts, cross, q_ref, k_ref, v_ref, ga_ref, lse_ref, deltas, dq_ref, dk_ref, dv_ref
):
    rows = q_ref.shape[0]
    half = rows // 2
    factor = LOG2E * 64 ** (-0.5)
    low_lanes = lax.broadcasted_iota(jnp.int32, (1, 128), 1) < 64
    above = lax.broadcasted_iota(jnp.int32, (TILE, TILE), 0) <= lax.broadcasted_iota(
        jnp.int32, (TILE, TILE), 1
    )

    def pick(both):
        return jnp.where(low_lanes, both[:TILE], both[TILE:])

    for start in starts:
        stop = start + TILE
        keys = k_ref[start:stop]
        keys_apart = stacked(keys, low_lanes)
        values_apart = stacked(v_ref[start:stop], low_lanes)
        dk = jnp.zeros((TILE, 128), F32)
        dv = jnp.zeros((TILE, 128), F32)
        for left, right in ((start, half), (half, rows)) if start < half else ((start, rows),):
            raw = dot_nt(keys_apart, q_ref[left:right])
            grad_weights = dot_nt(values_apart, ga_ref[left:right])
            weights, grad_scores = [], []
            for head in range(2):
                mine = slice(head * TILE, (head + 1) * TILE)
                level = lse_ref[head : head + 1, left:right]
                if start < half <= left:
                    level = level - cross
                exponent = raw[mine] * factor - level
                if left == start:
                    first = jnp.where(above, exponent[:, :TILE], MASKED)
                    exponent = (
                        first
                        if right - left == TILE
                        else jnp.concatenate([first, exponent[:, TILE:]], axis=1)
                    )
                weight = jnp.exp2(exponent)
                weights.append(weight.astype(BF))
                delta = deltas[head][:, left:right]
                grad_scores.append((weight * (grad_weights[mine] - delta)).astype(BF))
            dv = dv + pick(dot_nn(jnp.concatenate(weights, axis=0), ga_ref[left:right]))
            dk = dk + pick(dot_nn(jnp.concatenate(grad_scores, axis=0), q_ref[left:right]))
            dq = jnp.where(low_lanes, dot_tn(grad_scores[0], keys), dot_tn(grad_scores[1], keys))
            if start == 0:
                dq_ref[left:right] = dq
            else:
                dq_ref[left:right] += dq
        dk_ref[start:stop] = dk
        dv_ref[start:stop] = dv


def in_back_pair(dq_ref, dk_ref, dv_ref, weights, turned_ref, out_grad_ref, chunk_ref, total_ref):
    factor = 64 ** (-0.5)
    dq = (dq_ref[...] * factor).astype(BF)
    dk = (dk_ref[...] * factor).astype(BF)
    dv = dv_ref[...].astype(BF)
    grads = jnp.concatenate([dq, dk, dv], axis=1)
    shares = dot_nn(turned_ref[...], grads).astype(BF)
    for start in range(0, total_ref.shape[0], TILE):
        part = jnp.concatenate(
            [shares[start : start + TILE], out_grad_ref[start : start + TILE]], axis=1
        )
        chunk_ref[:, start // TILE] = part.reshape(8, 32, 512)
        columns = slice(start, start + TILE)
        total_ref[:, columns] += dot_nt(grads, weights[columns])
    return column_sum(dq.astype(F32)), column_sum(dv.astype(F32))


def tokens_back(tokens, grad, grad_middle, gain):
    normed, inv = row_norm(tokens.astype(F32))
    back = norm_back(grad, gain, normed, inv)
    return (grad_middle + back).astype(BF), column_sum(grad * normed), column_sum(grad)


def in_back_kernel(
    lengths_ref,
    proj_ref,
    ga_ref,
    lse_ref,
    delta_ref,
    wq_ref,
    wk_ref,
    wv_ref,
    first_ref,
    out_grad_ref,
    tokens_ref,
    gain_ref,
    grad_middle_ref,
    chunk_ref,
    bias_ref,
    tokens_grad_ref,
    sums_ref,
    dq_ref,
    dk_ref,
    dv_ref,
    turned_ref,
    total_ref,
):
    step = pl.program_id(0)
    q_ref, k_ref, v_ref = three(proj_ref)
    rows_all = tokens_ref.shape[0]

    @pl.when(step == 0)
    def _():
        turned_ref[...] = first_ref[...].T
        total_ref[...] = jnp.zeros_like(total_ref)

    deltas = [delta_ref[0, head : head + 1] for head in range(2)]
    attention_back_keys(
        range(0, rows_all, TILE),
        cross_flag(lengths_ref, tokens_ref),
        q_ref,
        k_ref,
        v_ref,
        ga_ref,
        lse_ref.at[0],
        deltas,
        dq_ref,
        dk_ref,
        dv_ref,
    )
    weights = jnp.concatenate([wq_ref[...], wk_ref[...], wv_ref[...]], axis=1)
    query_sum, value_sum = in_back_pair(
        dq_ref, dk_ref, dv_ref, weights, turned_ref, out_grad_ref, chunk_ref.at[0], total_ref
    )
    bias_ref[0, 0:1] = query_sum
    bias_ref[0, 1:2] = value_sum

    @pl.when(step == pl.num_programs(0) - 1)
    def _():
        gain_grad = jnp.zeros((1, total_ref.shape[1]), F32)
        shift_grad = jnp.zeros((1, total_ref.shape[1]), F32)
        for start in range(0, rows_all, TILE):
            rows = pl.ds(start, TILE)
            tokens_grad_ref[rows], gain_part, shift_part = tokens_back(
                tokens_ref[rows], total_ref[rows], grad_middle_ref[rows], gain_ref[...]
            )
            gain_grad = gain_grad + gain_part
            shift_grad = shift_grad + shift_part
        sums_ref[0:1] = gain_grad
        sums_ref[1:2] = shift_grad


def in_back(lengths, projected, ga, lse, delta, weights, first, out_grad, tokens, gain, grad_middle):
    rows, width = tokens.shape
    pairs = width // 128
    column = pl.BlockSpec((rows, 128), lambda p: (0, p))
    square = whole((rows, width))
    return pl.pallas_call(
        in_back_kernel,
        grid=(pairs,),
        in_specs=[
            pl.BlockSpec(memory_space=pltpu.SMEM),
            pl.BlockSpec((1, rows, 384), lambda p: (p, 0, 0)),
            column,
            pl.BlockSpec((1, 8, rows), lambda p: (p, 0, 0)),
            pl.BlockSpec((1, 2, rows), lambda p: (p, 0, 0)),
            pl.BlockSpec((width, 128), lambda p: (0, p)),
            pl.BlockSpec((width, 128), lambda p: (0, pairs + p)),
            pl.BlockSpec((width, 128), lambda p: (0, 2 * pairs + p)),
            square,
            column,
            square,
            whole((1, width)),
            square,
        ],
        out_specs=[
            pl.BlockSpec((1, 8, width // TILE, 32, 512), lambda p: (p, 0, 0, 0, 0)),
            pl.BlockSpec((1, 8, 128), lambda p: (p, 0, 0)),
            square,
            whole((8, width)),
        ],
        out_shape=[
            jax.ShapeDtypeStruct((pairs, 8, width // TILE, 32, 512), BF),
            jax.ShapeDtypeStruct((pairs, 8, 128), F32),
            jax.ShapeDtypeStruct((rows, width), BF),
            jax.ShapeDtypeStruct((8, width), F32),
        ],
        scratch_shapes=[
            pltpu.VMEM((rows, 128), F32),
            pltpu.VMEM((rows, 128), F32),
            pltpu.VMEM((rows, 128), F32),
            pltpu.VMEM((width, rows), BF),
            pltpu.VMEM((rows, width), F32),
        ],
        compiler_params=params(),
        name="in_back",
    )(
        lengths,
        projected,
        ga,
        lse,
        delta,
        weights,
        weights,
        weights,
        first,
        out_grad,
        tokens,
        gain,
        grad_middle,
    )


class Place:
    def __init__(self):
        self.z = lax.axis_index("dp")
        wide = lax.axis_index("wide")
        self.y = wide // 4
        self.x = (wide // 2) % 2
        self.c = wide % 2
        self.core = (self.z, wide + 1 - 2 * self.c)
        self.side = (self.z, wide + 2 - 4 * self.x)
        self.over = (self.z, wide + 4 - 8 * self.y)
        self.ranks = (self.z + 1 - 2 * (self.z % 2), (self.z + 2) % 4, 3 - self.z)
        self.planes = tuple((rank, wide) for rank in self.ranks)

    def greet(self, planes=True):
        barrier = pltpu.get_barrier_semaphore()
        peers = (self.core, self.side, self.over) + (self.planes if planes else ())
        for peer in peers:
            pl.semaphore_signal(barrier, inc=1, device_id=peer, device_id_type=MESH)
        pl.semaphore_wait(barrier, len(peers))


class WideGather:
    copies = 10

    def __init__(self, place, view, count, send, recv, first, source=None, last=None):
        y, x, c = place.y, place.x, place.c
        here, side, over, far = (y, x, c), (y, 1 - x, c), (1 - y, x, c), (1 - y, 1 - x, c)
        upper, lower = pl.ds(0, count // 2), pl.ds(count // 2, count // 2)
        both = pl.ds(0, count)

        def copy(index, slot, part, peer):
            destination = view(*slot, part)
            return pltpu.make_async_remote_copy(
                src_ref=source.at[part] if source is not None and slot is here else destination,
                dst_ref=destination,
                send_sem=send.at[first + index],
                recv_sem=recv.at[first + index],
                device_id=peer,
                device_id_type=MESH,
            )

        self.all = (
            copy(0, here, upper, place.side),
            copy(1, here, lower, place.over),
            copy(2, here, upper, place.over),
            copy(3, here, lower, place.side),
            copy(4, here, both, place.core),
            copy(5, side, upper, place.over),
            copy(6, over, lower, place.side),
            copy(7, side, both, place.core),
            copy(8, over, both, place.core),
            copy(9, far, both, place.core),
        )
        self.own = None
        if source is not None and last is not None:
            self.own = pltpu.make_async_copy(source, view(*here, both), last)

    def start(self):
        if self.own is not None:
            self.own.start()
        for index in range(5):
            self.all[index].start()

    def relay(self, stage):
        waits, starts = (((0, 1), (5, 6)), ((2, 3), (7, 8)), ((5, 6), (9,)))[stage]
        for index in waits:
            self.all[index].wait_recv()
        for index in starts:
            self.all[index].start()

    def finish(self):
        for index in (4, 7, 8, 9):
            self.all[index].wait_recv()
        for copy in self.all:
            copy.wait_send()
        if self.own is not None:
            self.own.wait()


def blocks_of(target):
    return lambda y, x, c, rows: target.at[y, x, c, rows]


LAG = 2


class Reduction:
    slots = 2
    deep = 3
    keep = 4

    @classmethod
    def scratch(cls):
        n, k = cls.slots, cls.keep
        return [
            pltpu.VMEM((cls.deep, 2, 2, 4, 64, 512), BF),
            pltpu.VMEM((n, 2, 2, 4, 64, 512), BF),
            pltpu.VMEM((n, 2, 2, 4, 32, 512), BF),
            pltpu.VMEM((n, 2, 4, 32, 512), BF),
            pltpu.VMEM((n, 4, 64, 512), BF),
            pltpu.VMEM((n, 3, 64, 512), BF),
            pltpu.VMEM((n, 64, 512), BF),
            pltpu.VMEM((k, 3, 64, 512), BF),
            pltpu.SemaphoreType.DMA((6, k)),
            pltpu.SemaphoreType.DMA((6, k)),
            pltpu.SemaphoreType.DMA((cls.deep,)),
        ]

    def __init__(self, place, refs):
        self.place = place
        (
            self.chip,
            self.partner,
            self.first,
            self.second,
            self.plane,
            self.from_z,
            self.sums,
            self.shared,
            self.send,
            self.recv,
            self.local,
        ) = refs

    def copy(self, index, slot, source, target, peer):
        return pltpu.make_async_remote_copy(
            src_ref=source,
            dst_ref=target,
            send_sem=self.send.at[index, slot],
            recv_sem=self.recv.at[index, slot],
            device_id=peer,
            device_id_type=MESH,
        )

    def wait(self, index, slot, arrived):
        self.copy(index, slot, arrived, arrived, self.place.core).wait()

    def load(self, chunk, source):
        slot = chunk % self.deep
        return pltpu.make_async_copy(source, self.chip.at[slot], self.local.at[slot])

    def stage0(self, chunk, view):
        slot, c = chunk % self.slots, self.place.c
        self.copy(
            0, slot, view.at[:, :, 1 - c], self.partner.at[slot], self.place.core
        ).start()
        self.load(chunk, view.at[:, :, c]).start()

    def stage1(self, chunk):
        p, slot, index = self.place, chunk % self.slots, chunk % self.deep
        partner, chip, target = self.partner.at[slot], self.chip.at[index], self.first.at[slot]
        self.load(chunk, partner).wait()
        self.wait(0, slot, partner)
        chip[...] += partner[...]
        self.copy(1, slot, chip.at[:, 1 - p.x, :, pl.ds(0, 32)], target.at[0], p.side).start()
        self.copy(1, slot, chip.at[1 - p.y, :, :, pl.ds(32, 32)], target.at[1], p.over).start()

    def stage2(self, chunk):
        p, slot, index = self.place, chunk % self.slots, chunk % self.deep
        chip, arrived, target = self.chip.at[index], self.first.at[slot], self.second.at[slot]
        self.wait(1, slot, arrived)
        for k in range(2):
            chip[k, p.x, :, 0:32] += arrived[0, k]
            chip[p.y, k, :, 32:64] += arrived[1, k]
        self.copy(2, slot, chip.at[1 - p.y, p.x, :, pl.ds(0, 32)], target.at[0], p.over).start()
        self.copy(2, slot, chip.at[p.y, 1 - p.x, :, pl.ds(32, 32)], target.at[1], p.side).start()

    def stage3(self, chunk):
        p, slot, index = self.place, chunk % self.slots, chunk % self.deep
        arrived, mine, plane = self.second.at[slot], self.chip.at[index, p.y, p.x], self.plane
        self.wait(2, slot, arrived)
        plane[slot, :, 0:32] = mine[:, 0:32] + arrived[0]
        plane[slot, :, 32:64] = mine[:, 32:64] + arrived[1]
        for k in range(3):
            target = self.from_z.at[slot, k]
            self.copy(3, slot, plane.at[slot, p.ranks[k]], target, p.planes[k]).start()

    def stage4(self, chunk):
        slot = chunk % self.slots
        self.wait(3, slot, self.from_z.at[slot])
        total = self.plane[slot, self.place.z].astype(F32)
        for k in range(3):
            total = total + self.from_z[slot, k].astype(F32)
        return total

    def spread(self, chunk, total):
        slot, place = chunk % self.slots, chunk % self.keep
        self.sums[slot] = total.astype(BF)
        peer = self.place.planes[1]
        self.copy(4, place, self.sums.at[slot], self.shared.at[place, 0], peer).start()

    def stage5(self, chunk):
        slot, place, peer = chunk % self.slots, chunk % self.keep, self.place.planes[0]
        shared = self.shared.at[place]
        self.wait(4, place, shared.at[0])
        self.copy(5, place, self.sums.at[slot], shared.at[1], peer).start()
        self.copy(5, place, shared.at[0], shared.at[2], peer).start()

    def stage6(self, chunk):
        slot, place, ranks = chunk % self.slots, chunk % self.keep, self.place.ranks
        self.wait(5, place, self.shared.at[place, pl.ds(1, 2)])
        return [
            (self.place.z, self.sums[slot]),
            (ranks[1], self.shared[place, 0]),
            (ranks[0], self.shared[place, 1]),
            (ranks[2], self.shared[place, 2]),
        ]


class SmallReduction:
    @staticmethod
    def scratch():
        return [
            pltpu.VMEM((2, 2, 2, 4, 16, 512), BF),
            pltpu.VMEM((2, 2, 4, 16, 512), BF),
            pltpu.VMEM((2, 2, 4, 16, 512), BF),
            pltpu.VMEM((2, 4, 16, 512), BF),
            pltpu.VMEM((4, 16, 512), BF),
            pltpu.VMEM((3, 16, 512), BF),
            pltpu.SemaphoreType.DMA((4,)),
            pltpu.SemaphoreType.DMA((4,)),
        ]

    def __init__(self, place, refs):
        self.place = place
        self.source, self.chip, self.partner, self.first, self.second, self.from_z = refs[:6]
        self.send, self.recv = refs[6:]

    def copy(self, index, source, target, peer):
        return pltpu.make_async_remote_copy(
            src_ref=source,
            dst_ref=target,
            send_sem=self.send.at[index],
            recv_sem=self.recv.at[index],
            device_id=peer,
            device_id_type=MESH,
        )

    def wait(self, index, arrived):
        self.copy(index, arrived, arrived, self.place.core).wait()

    def stage0(self):
        p = self.place
        self.copy(0, self.source.at[:, :, 1 - p.c], self.partner, p.core).start()

    def stage1(self):
        p = self.place
        self.wait(0, self.partner)
        self.chip[...] = self.source[:, :, p.c] + self.partner[...]
        self.copy(1, self.chip.at[:, 1 - p.x], self.first, p.side).start()

    def stage2(self):
        p = self.place
        self.wait(1, self.first)
        for k in range(2):
            self.chip[k, p.x] += self.first[k]
        self.copy(2, self.chip.at[1 - p.y, p.x], self.second, p.over).start()

    def stage3(self):
        p = self.place
        self.wait(2, self.second)
        self.chip[p.y, p.x] += self.second[...]
        for k in range(3):
            block = self.chip.at[p.y, p.x, p.ranks[k]]
            self.copy(3, block, self.from_z.at[k], p.planes[k]).start()

    def stage4(self):
        p = self.place
        self.wait(3, self.from_z)
        total = self.chip[p.y, p.x, p.z].astype(F32)
        for k in range(3):
            total = total + self.from_z[k].astype(F32)
        return total


def dma_sems(count):
    return [pltpu.SemaphoreType.DMA((count,)), pltpu.SemaphoreType.DMA((count,))]


def to_planes(place, mine, landing, send, recv, first):
    return [
        pltpu.make_async_remote_copy(
            src_ref=mine,
            dst_ref=landing(k),
            send_sem=send.at[first + k],
            recv_sem=recv.at[first + k],
            device_id=place.planes[k],
            device_id_type=MESH,
        )
        for k in range(3)
    ]


class PlanesLast:
    copies = WideGather.copies + 6

    def __init__(self, place, source, target, send, recv, last):
        view = blocks_of(target.at[place.z])
        self.wide = WideGather(place, view, source.shape[0], send, recv, 0, source, last)

        def copy(index, rank, peer):
            blocks = target.at[rank, :, :, place.c]
            return pltpu.make_async_remote_copy(
                src_ref=blocks,
                dst_ref=blocks,
                send_sem=send.at[WideGather.copies + index],
                recv_sem=recv.at[WideGather.copies + index],
                device_id=peer,
                device_id_type=MESH,
            )

        self.across = [copy(k, place.z, place.planes[k]) for k in range(3)]
        self.over = [copy(3 + k, place.ranks[k], place.core) for k in range(3)]

    def start_across(self):
        self.wide.own.wait()
        for copy in self.across:
            copy.start()

    def start_over(self):
        for arrived, copy in zip(self.across, self.over):
            arrived.wait_recv()
            copy.start()

    def finish(self):
        self.wide.own = None
        self.wide.finish()
        for copy in self.across:
            copy.wait_send()
        for copy in self.over:
            copy.wait()


def first_kernel(
    lengths_ref,
    tokens_ref,
    in_ref,
    vec_ref,
    out_ref,
    up_ref,
    unit_ref,
    hs_ref,
    turned_ref,
    proj_ref,
    scaled_ref,
    scaled_turned_ref,
    attended_ref,
    lse_ref,
    vectors_ref,
    scale_ref,
    in_all,
    out_all,
    up_all,
    unit_all,
    held_ref,
    normed_ref,
    first_ref,
    vext_ref,
    send_in,
    recv_in,
    send_out,
    recv_out,
    send_ff,
    recv_ff,
    local,
):
    step = pl.program_id(0)
    place = Place()
    width = tokens_ref.shape[1]
    count = WideGather.copies
    lanes = (3 * width // 2 + 128, 3 * width // 2)
    across, early, late = [], [], None
    for group in range(2):
        held = held_ref.at[group, :, :, :, :, :, pl.ds(0, lanes[group])]
        first = group * (3 + 2 * count)

        def blocks(planes, held=held):
            return lambda y, x, c, rows: held.at[planes, y, x, c, rows]

        mine = held.at[0, place.y, place.x, place.c]
        across.append(
            to_planes(
                place,
                mine,
                lambda k, held=held: held.at[k + 1, place.y, place.x, place.c],
                send_in,
                recv_in,
                first,
            )
        )
        if group == 0:
            for part, planes in enumerate((pl.ds(0, 1), pl.ds(1, 3))):
                start = first + 3 + part * count
                early.append(WideGather(place, blocks(planes), 32, send_in, recv_in, start))
        else:
            late = WideGather(place, blocks(pl.ds(0, 4)), 32, send_in, recv_in, first + 3)
    orders = (place.z, *place.ranks)
    out = PlanesLast(place, out_ref, out_all, send_out, recv_out, local.at[2])
    up = WideGather(
        place, blocks_of(up_all), width, send_ff, recv_ff, 0, up_ref, local.at[3]
    )
    unit = WideGather(
        place, blocks_of(unit_all), 32, send_ff, recv_ff, count, unit_ref, local.at[4]
    )
    keep = [
        pltpu.make_async_copy(
            held_ref.at[group, index, :, :, :, :, pl.ds(0, lanes[1])],
            in_all.at[rank, :, :, :, :, pl.ds(group * lanes[1], lanes[1])],
            local.at[12 + 4 * group + index],
        )
        for group in range(2)
        for index, rank in enumerate(orders)
    ]

    @pl.when(step == 0)
    def _():
        place.greet()
        half = width // 2
        for group in range(2):
            mine = held_ref.at[group, 0, place.y, place.x, place.c]
            own = pl.ds(group * 3 * half, 3 * half)
            fill = pltpu.make_async_copy(
                in_ref.at[:, own], mine.at[:, pl.ds(0, 3 * half)], local.at[6 + group]
            )
            fill.start()
            if group == 0:
                mine[:, 3 * half : 3 * half + 128] = jnp.zeros((32, 128), BF)
                mine[:, 3 * half : 3 * half + 32] = vec_ref[...]
            fill.wait()
            for copy in across[group]:
                copy.start()
            if group == 0:
                early[0].start()
        scale = hs_ref[...].astype(F32)
        for pair in range(width // 128):
            own = slice(pair * 128, (pair + 1) * 128)
            low_lanes = lax.broadcasted_iota(jnp.int32, (1, 128), 1) < 64
            scale_ref[0:1, own] = jnp.where(
                low_lanes, scale[:, 2 * pair : 2 * pair + 1], scale[:, 2 * pair + 1 : 2 * pair + 2]
            )
        for start in range(0, tokens_ref.shape[0], TILE):
            rows = pl.ds(start, TILE)
            normed, _ = row_norm(tokens_ref[rows].astype(F32))
            normed_ref[rows] = normed
        early[0].relay(0)
        for copy in across[0]:
            copy.wait_recv()
        early[1].start()
        early[0].relay(1)
        early[0].relay(2)
        early[1].relay(0)
        early[1].relay(1)
        for copy in across[1]:
            copy.wait_recv()
        late.start()
        early[1].relay(2)
        out.wide.start()
        unit.start()
        for part in early:
            part.finish()
        for z in range(4):
            for y in range(2):
                tile = jnp.zeros((16, 128), F32)
                for x in range(2):
                    for c in range(2):
                        piece = held_ref[
                            0, orders[z], y, x, c, 0:16, 3 * half : 3 * half + 128
                        ].astype(F32)
                        spot = 32 * (2 * x + c)
                        tile = tile + (piece if spot == 0 else pltpu.roll(piece, spot, 1))
                vectors_ref[:, (2 * z + y) * 128 : (2 * z + y + 1) * 128] = tile
        for start in range(0, tokens_ref.shape[0], TILE):
            rows = pl.ds(start, TILE)
            first_ref[rows] = (normed_ref[rows] * vectors_ref[3:4] + vectors_ref[4:5]).astype(BF)

    @pl.when((step >= 2) & (step <= 4))
    def _():
        for stage in range(3):

            @pl.when(step == 2 + stage)
            def _():
                late.relay(stage)
                out.wide.relay(stage)
                unit.relay(stage)

    @pl.when(step == 2)
    def _():
        up.start()

    @pl.when(step == 4)
    def _():
        out.start_across()

    @pl.when(step == 5)
    def _():
        late.finish()
        for copy in keep:
            copy.start()

    for stage, at in enumerate((5, 7, 8)):

        @pl.when(step == at)
        def _():
            up.relay(stage)

    @pl.when(step == 7)
    def _():
        out.start_over()

    @pl.when(step > 0)
    def _():
        pair = step - 1
        columns = pl.ds(pl.multiple_of(pair % 4 * 384, 128), 384)
        weights = jnp.concatenate(
            [held_ref[pair // 4, order, :, :, :, :, columns].reshape(TILE, 384) for order in orders]
        )
        own = pl.ds(pl.multiple_of(pair * 128, 128), 128)
        bias = jnp.concatenate(
            [vectors_ref[0:1, own], jnp.zeros((1, 128), F32), vectors_ref[1:2, own]], axis=1
        )
        project_pair(first_ref, weights, bias, proj_ref)
        attention_pair(
            cross_flag(lengths_ref, tokens_ref),
            *three(proj_ref),
            scale_ref[0:1, own],
            scaled_ref,
            attended_ref,
            lse_ref,
            vext_ref,
        )
        scaled_turned_ref[...] = scaled_ref[...].T

    @pl.when(step == pl.num_programs(0) - 1)
    def _():
        turned_ref[...] = first_ref[...].T
        for copy in (*across[0], *across[1]):
            copy.wait_send()
        for copy in keep:
            copy.wait()
        out.finish()
        unit.finish()
        up.finish()


def first_part(lengths, tokens, in_weight, vec, out_weight, up_weight, unit_rows, head_scale):
    rows, width = tokens.shape
    pairs = width // 128

    def at(step):
        return jnp.maximum(step - 1, 0)

    column = pl.BlockSpec((rows, 128), lambda s: (0, at(s)))
    held = (2, 4, 2, 2, 2, 32, 3 * width // 2 + 128)
    return pl.pallas_call(
        first_kernel,
        grid=(pairs + 1,),
        in_specs=[
            pl.BlockSpec(memory_space=pltpu.SMEM),
            whole((rows, width)),
            ANY,
            whole(vec.shape),
            ANY,
            ANY,
            ANY,
            whole(head_scale.shape),
        ],
        out_specs=[
            whole((width, rows)),
            pl.BlockSpec((1, rows, 384), lambda s: (at(s), 0, 0)),
            column,
            pl.BlockSpec((128, rows), lambda s: (at(s), 0)),
            column,
            pl.BlockSpec((1, 8, rows), lambda s: (at(s), 0, 0)),
            whole((16, width)),
            whole((8, width)),
            ANY,
            ANY,
            ANY,
            ANY,
        ],
        out_shape=[
            jax.ShapeDtypeStruct((width, rows), BF),
            jax.ShapeDtypeStruct((pairs, rows, 384), BF),
            jax.ShapeDtypeStruct((rows, width), BF),
            jax.ShapeDtypeStruct((width, rows), BF),
            jax.ShapeDtypeStruct((rows, width), F32),
            jax.ShapeDtypeStruct((pairs, 8, rows), F32),
            jax.ShapeDtypeStruct((16, width), F32),
            jax.ShapeDtypeStruct((8, width), F32),
            jax.ShapeDtypeStruct((4, 2, 2, 2, 32, 3 * width), BF),
            jax.ShapeDtypeStruct((4, 2, 2, 2, *out_weight.shape), BF),
            jax.ShapeDtypeStruct((2, 2, 2, *up_weight.shape), BF),
            jax.ShapeDtypeStruct((2, 2, 2, *unit_rows.shape), BF),
        ],
        scratch_shapes=[
            pltpu.VMEM(held, BF),
            pltpu.VMEM((rows, width), F32),
            pltpu.VMEM((rows, width), BF),
            pltpu.VMEM((rows, 256), BF),
            *dma_sems(6 + 3 * WideGather.copies),
            *dma_sems(PlanesLast.copies),
            *dma_sems(2 * WideGather.copies),
            pltpu.SemaphoreType.DMA((20,)),
        ],
        compiler_params=params(collective_id=0, has_side_effects=True),
        name="first_part",
    )(lengths, tokens, in_weight, vec, out_weight, up_weight, unit_rows, head_scale)


def second_kernel(
    units,
    scaled_ref,
    weight_ref,
    vec_ref,
    tokens_ref,
    up_ref,
    unit_ref,
    down_ref,
    branch_ref,
    middle_ref,
    turned_ref,
    act_ref,
    slope_ref,
    stats_ref,
    down_all,
    feed_ref,
    sums_ref,
    send,
    recv,
    local,
):
    step = pl.program_id(0)
    lead = feed_ref.shape[0] // TILE
    place = Place()
    down = WideGather(
        place, blocks_of(down_all), UNITS, send, recv, 0, down_ref, local.at[0]
    )

    @pl.when(step == 0)
    def _():
        place.greet(planes=False)
        down.start()
        sums_ref[...] = jnp.zeros_like(sums_ref)

    for stage, at in enumerate((5, 8, 11)):

        @pl.when(step == at)
        def _():
            down.relay(stage)

    @pl.when(step < lead)
    def _():
        rows = pl.ds(pl.multiple_of(step * TILE, TILE), TILE)
        feed_ref[rows] = out_proj_rows(
            scaled_ref, weight_ref, vec_ref, tokens_ref, branch_ref, middle_ref
        )

    @pl.when(step >= lead)
    def _():
        up_step(feed_ref, up_ref, unit_ref, act_ref, slope_ref, sums_ref)

    @pl.when(step == pl.num_programs(0) - 1)
    def _():
        up_stats(units, stats_ref, sums_ref)
        turned_ref[...] = feed_ref[...].T
        down.finish()


def second_part(scaled, out_weights, vectors, tokens, up, unit_vec, down_weight):
    rows, width = tokens.shape
    steps = up.shape[0]
    lead = rows // TILE

    def early(step):
        return jnp.minimum(step, lead - 1)

    def late(step):
        return jnp.maximum(step - lead, 0)

    by_row = pl.BlockSpec((TILE, width), lambda s: (early(s), 0))
    block = pl.BlockSpec((1, rows, UNITS), lambda s: (late(s), 0, 0))
    return pl.pallas_call(
        functools.partial(second_kernel, steps * UNITS),
        grid=(lead + steps,),
        in_specs=[
            by_row,
            whole((width, width)),
            whole(vectors.shape),
            by_row,
            pl.BlockSpec((1, width, UNITS), lambda s: (late(s), 0, 0)),
            pl.BlockSpec((1, unit_vec.shape[1], UNITS), lambda s: (late(s), 0, 0)),
            ANY,
        ],
        out_specs=[
            by_row,
            by_row,
            whole((width, rows)),
            block,
            block,
            whole((rows, 128)),
            ANY,
        ],
        out_shape=[
            jax.ShapeDtypeStruct((rows, width), F32),
            jax.ShapeDtypeStruct((rows, width), F32),
            jax.ShapeDtypeStruct((width, rows), BF),
            jax.ShapeDtypeStruct((steps, rows, UNITS), BF),
            jax.ShapeDtypeStruct((steps, rows, UNITS), BF),
            jax.ShapeDtypeStruct((rows, 128), F32),
            jax.ShapeDtypeStruct((2, 2, 2, *down_weight.shape), BF),
        ],
        scratch_shapes=[
            pltpu.VMEM((rows, width), BF),
            pltpu.VMEM((2, rows, 128), F32),
            *dma_sems(WideGather.copies),
            pltpu.SemaphoreType.DMA((1,)),
        ],
        compiler_params=params(collective_id=2, has_side_effects=True),
        name="second_part",
    )(scaled, out_weights, vectors, tokens, up, unit_vec, down_weight)


NORMS_AT, COLUMNS_AT, HEADS_AT, TOKENS_AT, VECTORS_AT = 8, 16, 20, 28, 32
BACK_STEPS = VECTORS_AT + 5
OUT_TILE = 128


class Stream:
    def __init__(self, view, buffers, sems):
        self.view, self.buffers, self.sems = view, buffers, sems

    def copy(self, index):
        slot = index % 2
        return pltpu.make_async_copy(self.view(index), self.buffers.at[slot], self.sems.at[slot])

    def block(self, index):
        return self.buffers.at[index % 2]


def advance(streams, index, count):
    @pl.when(index + 1 < count)
    def _():
        for stream in streams:
            stream.copy(index + 1).start()

    for stream in streams:
        stream.copy(index).wait()


def chunk_at(time):
    chunk = jnp.where(time < 8, time // 2, (time + 8) // 4)
    chunk = jnp.where(time >= 23, (time + 9) // 4, chunk)
    there = ((time < 8) & (time % 2 == 0)) | ((time >= 8) & (time <= 20) & (time % 4 == 0))
    there = there | ((time >= 23) & (time < 36) & (time % 4 == 3))
    return chunk, there & (time >= 0)


def back_kernel(
    lengths_ref,
    unit_grad_ref,
    vec_ref,
    hs_ref,
    act_all,
    slope_all,
    e_all,
    stats_all,
    up_all,
    feed_turned_all,
    down_grad_all,
    cot_all,
    middle_all,
    branch_all,
    scaled_turned_all,
    attended_all,
    out_weight_all,
    proj_all,
    lse_all,
    in_weight_all,
    turned_all,
    tokens_all,
    down_out,
    up_out,
    attn_out,
    vec_out,
    tokens_grad_all,
    up_grad_all,
    units_in_ref,
    up_ref,
    stats_ref,
    feed_turned_ref,
    cot_ref,
    norms_in_ref,
    scaled_turned_ref,
    attended_ref,
    out_weight_ref,
    proj_ref,
    lse_ref,
    in_weight_ref,
    turned_ref,
    tokens_ref,
    tokens_grad_ref,
    staged_ref,
    total_ref,
    low_ref,
    out_grad_ref,
    ga_ref,
    grad_middle_ref,
    delta_ref,
    delta_sum_ref,
    sums_ref,
    units_ref,
    dq_ref,
    dk_ref,
    dv_ref,
    chunk_ref,
    stream_sems,
    fetch_sems,
    *scratch,
):
    step = pl.program_id(0)
    place = Place()
    engine = Reduction(place, scratch[:11])
    small = SmallReduction(place, scratch[11:])
    pairs = proj_all.shape[0]

    def rows_of(array, size):
        return lambda i: array.at[pl.ds(pl.multiple_of(i * size, size), size)]

    def columns_of(array, size):
        return lambda i: array.at[:, pl.ds(pl.multiple_of(i * size, size), size)]

    def stream(number, view, buffers):
        return Stream(view, buffers, stream_sems.at[number])

    act, slope, e = (
        stream(k, lambda i, array=array: array.at[i], units_in_ref.at[k])
        for k, array in enumerate((act_all, slope_all, e_all))
    )
    up = stream(3, lambda i: up_all.at[i], up_ref)
    cot = stream(4, rows_of(cot_all, OUT_TILE), cot_ref)
    middle = stream(5, rows_of(middle_all, OUT_TILE), norms_in_ref.at[0])
    branch = stream(6, rows_of(branch_all, OUT_TILE), norms_in_ref.at[1])
    attended = stream(7, columns_of(attended_all, TILE), attended_ref)
    proj = stream(8, lambda i: proj_all.at[i], proj_ref)
    lse = stream(9, lambda i: lse_all.at[i], lse_ref)
    in_weight = stream(10, columns_of(in_weight_all, 384), in_weight_ref)
    tokens = stream(11, rows_of(tokens_all, TILE), tokens_ref)
    put = rows_of(tokens_grad_all, TILE)

    def put_tokens(i):
        return pltpu.make_async_copy(
            tokens_grad_ref.at[i % 2], put(i), stream_sems.at[12, i % 2]
        )

    fetches = [
        pltpu.make_async_copy(source, target, fetch_sems.at[index])
        for index, (source, target) in enumerate(
            (
                (stats_all, stats_ref),
                (feed_turned_all, feed_turned_ref),
                (scaled_turned_all, scaled_turned_ref),
                (out_weight_all, out_weight_ref),
                (turned_all, turned_ref),
            )
        )
    ]

    @pl.when(step == 0)
    def _():
        for item in (act, slope, e, up):
            item.copy(0).start()
        for copy in fetches:
            copy.start()
        for item in (cot, middle, branch, attended, proj, lse, in_weight, tokens):
            item.copy(0).start()
        total_ref[...] = jnp.zeros_like(total_ref)
        sums_ref[...] = jnp.zeros_like(sums_ref)
        units_ref[...] = jnp.zeros_like(units_ref)
        place.greet()

    def store(block):
        view = up_grad_all.at[block // 4, block // 2 % 2, block % 2]
        return pltpu.make_async_copy(staged_ref, view, fetch_sems.at[5])

    @pl.when((step >= 1) & (step <= NORMS_AT))
    def _():
        store(step - 1).wait()


    def stage(number, low, high, action, tick):
        chunk, there = chunk_at(tick - number * LAG)

        @pl.when(there & (chunk >= low) & (chunk < high))
        def _():
            action(chunk)

    def put_down(chunk):
        for rank, block in engine.stage6(chunk):
            for half in range(2):

                @pl.when(chunk % 2 == half)
                def _():
                    down_out[chunk // 2, rank, :, half * 512 : half * 512 + 512] = block

    def put_up(chunk):
        for rank, block in engine.stage6(chunk):
            up_out[chunk - 4, rank] = block

    def put_own(chunk):
        attn_out[chunk - 8] = engine.stage4(chunk)

    def take_down(chunk):
        lanes = pl.ds(pl.multiple_of(chunk % 2 * 512, 512), 512)
        engine.stage0(chunk, down_grad_all.at[:, :, :, chunk // 2, :, :, lanes])

    def take_up(chunk):
        engine.stage0(chunk, up_grad_all.at[:, :, :, chunk - 4])

    def take_own(chunk):
        engine.stage0(chunk, chunk_ref)

    def reduce_step(tick):
        stage(6, 0, 4, put_down, tick)
        stage(6, 4, 8, put_up, tick)
        stage(5, 0, 8, engine.stage5, tick)
        stage(4, 0, 8, lambda chunk: engine.spread(chunk, engine.stage4(chunk)), tick)
        stage(4, 8, 12, put_own, tick)
        stage(3, 0, 12, engine.stage3, tick)
        stage(2, 0, 12, engine.stage2, tick)
        stage(1, 0, 12, engine.stage1, tick)
        stage(0, 0, 4, take_down, tick)
        stage(0, 4, 8, take_up, tick)

    tick = jnp.where(step < HEADS_AT, step, 2 * step - HEADS_AT)
    tick = jnp.where(step < TOKENS_AT, tick, step + TOKENS_AT - HEADS_AT)
    reduce_step(tick)


    @pl.when(step < NORMS_AT)
    def _():
        advance((act, slope, e, up), step, NORMS_AT)

        @pl.when(step == 0)
        def _():
            fetches[0].wait()

        units_ref[step, 0:1] = up_back_step(
            act.block(step),
            slope.block(step),
            e.block(step),
            stats_ref,
            up.block(step),
            low_ref,
            total_ref,
        )
        units_ref[step, 1:3] = unit_grad_ref[step, 0:2]

        @pl.when(step == 0)
        def _():
            fetches[1].wait()

        for left in range(0, UNITS, TILE):
            columns = slice(left, left + TILE)
            grad = dot_nn(feed_turned_ref[...], low_ref[:, columns]).astype(BF)
            staged_ref[:, :, :, columns] = grad.reshape(4, 4, 64, TILE)
        store(step).start()


    @pl.when((step >= NORMS_AT) & (step < COLUMNS_AT))
    def _():
        block = step - NORMS_AT
        rows = pl.ds(pl.multiple_of(block * OUT_TILE, OUT_TILE), OUT_TILE)
        advance((cot, middle, branch), block, COLUMNS_AT - NORMS_AT)
        grad_middle, low = norms_back(
            total_ref[rows],
            cot.block(block),
            middle.block(block),
            branch.block(block),
            vec_ref,
            sums_ref,
        )
        grad_middle_ref[rows] = grad_middle
        low_ref[rows] = low

    @pl.when((step >= COLUMNS_AT) & (step < HEADS_AT))
    def _():
        block = step - COLUMNS_AT
        columns = pl.ds(pl.multiple_of(block * TILE, TILE), TILE)
        advance((attended,), block, HEADS_AT - COLUMNS_AT)

        @pl.when(block == 0)
        def _():
            fetches[2].wait()
            fetches[3].wait()

        grad_out, delta = heads_back(
            low_ref[...],
            out_weight_ref[columns],
            hs_ref[0:1, columns],
            attended.block(block)[...],
        )
        ga_ref[:, columns] = grad_out
        delta_sum_ref[block, 0:1] = column_sum(delta)
        turned = delta.T
        for head in range(4):
            delta_ref[4 * block + head] = turned[head : head + 1]
        out_grad_ref[:, columns] = dot_nn(scaled_turned_ref[...], low_ref[:, columns]).astype(BF)

    @pl.when(step == HEADS_AT - 1)
    def _():
        total_ref[...] = jnp.zeros_like(total_ref)


    @pl.when((step >= HEADS_AT) & (step < TOKENS_AT))
    def _():
        pair = step - HEADS_AT
        columns = pl.ds(pl.multiple_of(pair * 128, 128), 128)
        advance((proj, lse, in_weight), pair, pairs)

        @pl.when(pair == 0)
        def _():
            fetches[4].wait()

        for part, starts in enumerate(((0, 3 * TILE), (TILE, 2 * TILE))):
            if part == 1:
                reduce_step(tick + 1)
            attention_back_keys(
                starts,
                cross_flag(lengths_ref, total_ref),
                *[proj.block(pair).at[:, pl.ds(index * 128, 128)] for index in range(3)],
                ga_ref.at[:, columns],
                lse.block(pair),
                [delta_ref[2 * pair], delta_ref[2 * pair + 1]],
                dq_ref,
                dk_ref,
                dv_ref,
            )
        query_sum, value_sum = in_back_pair(
            dq_ref,
            dk_ref,
            dv_ref,
            in_weight.block(pair)[...],
            turned_ref,
            out_grad_ref.at[:, columns],
            chunk_ref.reshape(8, 4, 64, 512).at[
                :, :, pl.ds(pl.multiple_of(pair % 2 * 32, 32), 32)
            ],
            total_ref,
        )
        sums_ref[0:1, columns] = query_sum
        sums_ref[1:2, columns] = value_sum
        stage(0, 8, 12, take_own, tick + 1)

    @pl.when((step >= TOKENS_AT) & (step < TOKENS_AT + 4))
    def _():
        block = step - TOKENS_AT
        rows = pl.ds(pl.multiple_of(block * TILE, TILE), TILE)
        advance((tokens,), block, 4)

        @pl.when(block >= 2)
        def _():
            put_tokens(block - 2).wait()

        result, gain_grad, shift_grad = tokens_back(
            tokens.block(block)[...], total_ref[rows], grad_middle_ref[rows], vec_ref[3:4]
        )
        tokens_grad_ref[block % 2] = result
        put_tokens(block).start()
        sums_ref[3:4] += gain_grad
        sums_ref[4:5] += shift_grad


    @pl.when(step == VECTORS_AT)
    def _():
        for y in range(2):
            for z in range(4):
                own = slice((2 * z + y) * 128, (2 * z + y + 1) * 128)
                for index in range(9):
                    lanes = slice(index % 4 * 128, index % 4 * 128 + 128)
                    row = 6 + index // 4
                    units_ref[8, row : row + 1, lanes] = sums_ref[index : index + 1, own]
                for x in range(2):
                    for c in range(2):
                        unit = 4 * y + 2 * x + c
                        units_ref[8, 0:3] = units_ref[unit, 0:3]
                        if (y, z, x, c) == (0, 0, 0, 0):
                            units_ref[8, 3:4] = sums_ref[9:10, 0:UNITS]
                            units_ref[8, 4:5] = sums_ref[9:10, UNITS : 2 * UNITS]
                            for block in range(4):
                                lanes = slice(block * 128, block * 128 + 128)
                                units_ref[8, 5:6, lanes] = delta_sum_ref[block, 0:1]
                        small.source[y, x, c, z] = units_ref[8].astype(BF)
        small.stage0()

    for index, action in enumerate((small.stage1, small.stage2, small.stage3)):

        @pl.when(step == VECTORS_AT + 1 + index)
        def _():
            action()

    @pl.when(step == VECTORS_AT + 4)
    def _():
        vec_out[...] = small.stage4()
        for block in range(2, 4):
            put_tokens(block).wait()


def back_part(
    lengths,
    act,
    slope,
    e,
    stats,
    up,
    feed_turned,
    unit_grad,
    down_grad,
    cotangent,
    middle,
    branch,
    scaled_turned,
    attended,
    out_weights,
    vectors,
    head_lanes,
    projected,
    lse,
    weights,
    turned,
    tokens,
):
    rows, width = tokens.shape
    pairs = width // 128

    return pl.pallas_call(
        back_kernel,
        grid=(BACK_STEPS,),
        in_specs=[
            pl.BlockSpec(memory_space=pltpu.SMEM),
            whole(unit_grad.shape),
            whole(vectors.shape),
            whole(head_lanes.shape),
            *[ANY] * 18,
        ],
        out_specs=[
            whole((2, 4, 64, 1024)),
            whole((4, 4, 64, 512)),
            whole((4, 64, 512)),
            whole((16, 512)),
            ANY,
            ANY,
        ],
        out_shape=[
            jax.ShapeDtypeStruct((2, 4, 64, 1024), BF),
            jax.ShapeDtypeStruct((4, 4, 64, 512), BF),
            jax.ShapeDtypeStruct((4, 64, 512), F32),
            jax.ShapeDtypeStruct((16, 512), F32),
            jax.ShapeDtypeStruct((rows, width), BF),
            jax.ShapeDtypeStruct((2, 2, 2, 4, 4, 64, UNITS), BF),
        ],
        scratch_shapes=[
            pltpu.VMEM((3, 2, rows, UNITS), BF),
            pltpu.VMEM((2, width, UNITS), BF),
            pltpu.VMEM((rows, 128), F32),
            pltpu.VMEM((width, rows), BF),
            pltpu.VMEM((2, OUT_TILE, width), BF),
            pltpu.VMEM((2, 2, OUT_TILE, width), F32),
            pltpu.VMEM((width, rows), BF),
            pltpu.VMEM((2, rows, TILE), F32),
            pltpu.VMEM((width, width), BF),
            pltpu.VMEM((2, rows, 384), BF),
            pltpu.VMEM((2, 8, rows), F32),
            pltpu.VMEM((2, width, 384), BF),
            pltpu.VMEM((width, rows), BF),
            pltpu.VMEM((2, TILE, width), BF),
            pltpu.VMEM((2, TILE, width), BF),
            pltpu.VMEM((4, 4, 64, UNITS), BF),
            pltpu.VMEM((rows, width), F32),
            pltpu.VMEM((rows, width), BF),
            pltpu.VMEM((width, width), BF),
            pltpu.VMEM((rows, width), BF),
            pltpu.VMEM((rows, width), F32),
            pltpu.VMEM((2 * pairs, 1, rows), F32),
            pltpu.VMEM((4, 8, 128), F32),
            pltpu.VMEM((16, width), F32),
            pltpu.VMEM((9, 16, UNITS), F32),
            pltpu.VMEM((rows, 128), F32),
            pltpu.VMEM((rows, 128), F32),
            pltpu.VMEM((rows, 128), F32),
            pltpu.VMEM((2, 2, 2, 4, 64, 512), BF),
            pltpu.SemaphoreType.DMA((13, 2)),
            pltpu.SemaphoreType.DMA((6,)),
            *Reduction.scratch(),
            *SmallReduction.scratch(),
        ],
        compiler_params=params(collective_id=1, has_side_effects=True),
        name="back_part",
    )(
        lengths,
        unit_grad,
        vectors,
        head_lanes,
        act,
        slope,
        e,
        stats,
        up,
        feed_turned,
        down_grad.reshape(2, 2, 2, 2, 4, 64, width),
        cotangent,
        middle,
        branch,
        scaled_turned,
        attended,
        out_weights,
        projected,
        lse,
        weights,
        turned,
        tokens,
    )


def layer(staged, tokens, cotangent, lengths, attn, up, down, unit_vec, head_scale, down_bias):
    rows, width = tokens.shape
    heads = head_scale.shape[0]
    pairs = width // 128
    if staged:
        in_weight, out_weight, vec_block = attn
        (
            turned,
            projected,
            scaled,
            scaled_turned,
            attended,
            lse,
            vectors,
            head_lanes,
            weights,
            out_weights,
            up,
            unit_vec,
        ) = first_part(
            lengths, tokens, in_weight, vec_block, out_weight, up, unit_vec, head_scale[None, :]
        )
        weights = weights.reshape(width, 3 * width)
        out_weights = out_weights.reshape(width, width)
        up = up.reshape(-1, width, UNITS)
        unit_vec = unit_vec.reshape(-1, unit_vec.shape[-2], UNITS)
        branch, middle, feed_turned, act, slope, stats, down = second_part(
            scaled, out_weights, vectors, tokens, up, unit_vec, down
        )
        down = down.reshape(-1, UNITS, width)
    else:
        weights, out_weights, vectors = attn
        scale = head_scale.astype(F32)
        head_lanes = jnp.repeat(scale, width // heads)[None, :]
        first, projected, scaled, attended, lse = plain_first(
            lengths, tokens, weights, vectors, head_lanes
        )
        branch, middle, feed = out_proj(scaled, out_weights, vectors, tokens)
        act, slope, stats = up_pass(feed, up, unit_vec)
    mixed, down_grad, e, stats, unit_grad = down_pass(
        act, stats, unit_vec, down, cotangent, middle, down_bias[None, :]
    )
    if staged:
        down_total, up_total, shares, vec_shares, tokens_grad, _ = back_part(
            lengths,
            act,
            slope,
            e,
            stats,
            up,
            feed_turned,
            unit_grad,
            down_grad,
            cotangent,
            middle,
            branch,
            scaled_turned,
            attended,
            out_weights,
            vectors,
            head_lanes,
            projected,
            lse,
            weights,
            turned,
            tokens,
        )
        return mixed, tokens_grad, down_total, up_total, shares, vec_shares
    up_grad, up_bias_grad, grad_feed = up_back(
        act, slope, e, stats, up, feed
    )
    grad_middle, ga, out_grad, delta, sums = out_back(
        grad_feed,
        cotangent,
        middle,
        branch,
        scaled,
        attended,
        out_weights,
        vectors,
        head_lanes,
    )
    chunks, proj_bias, tokens_grad, pre_sums = in_back(
        lengths,
        projected,
        ga,
        lse,
        delta.reshape(pairs, 2, rows),
        weights,
        first,
        out_grad,
        tokens,
        vectors[3:4],
        grad_middle,
    )
    scale_grad = jnp.sum(delta, axis=1) / scale
    vec_grads = [
        proj_bias[:, 0].reshape(width),
        proj_bias[:, 1].reshape(width),
        sums[2],
        pre_sums[0],
        pre_sums[1],
        sums[5],
        sums[6],
        sums[7],
        sums[8],
    ]
    unit_grads = [up_bias_grad[:, 0], unit_grad[:, 0], unit_grad[:, 1]]
    return mixed, tokens_grad, chunks, up_grad, down_grad, vec_grads, unit_grads, sums[9], scale_grad


def body(
    axes,
    tokens,
    cotangent,
    lengths,
    in_weight,
    query_bias,
    value_bias,
    out_weight,
    out_bias,
    head_scale,
    pre_gain,
    pre_bias,
    post_gain,
    post_bias,
    feed_gain,
    feed_bias,
    up_weight,
    up_bias,
    mid_gain,
    mid_bias,
    down_weight,
    down_bias,
):
    planes, wide = axes
    every = ("dp", "wide")
    staged = (planes, wide) == (4, 8)
    rows, width = tokens.shape
    units = down_weight.shape[0] * wide
    steps = units // UNITS
    share = in_weight.shape[0]
    columns = [
        query_bias,
        value_bias,
        out_bias,
        pre_gain,
        pre_bias,
        post_gain,
        post_bias,
        feed_gain,
        feed_bias,
    ]
    index = lax.broadcasted_iota(jnp.int32, (32, up_bias.shape[0]), 0)
    unit_rows = jnp.where(index == 0, up_bias[None, :], jnp.zeros((), BF))
    unit_rows = jnp.where(index == 1, mid_gain[None, :], unit_rows)
    unit_rows = jnp.where(index == 2, mid_bias[None, :], unit_rows)
    if staged:
        index = lax.broadcasted_iota(jnp.int32, (32, share), 0)
        vec_block = jnp.zeros((32, share), BF)
        for row, column in enumerate(columns):
            vec_block = jnp.where(index == row, column[None, :], vec_block)
        by_pair = in_weight.reshape(share, 3, width // 128, 128).transpose(0, 2, 1, 3)
        attn = (by_pair.reshape(share, 3 * width), out_weight, vec_block)
        up, unit_vec, down = up_weight, unit_rows, down_weight
    else:
        flat = jnp.concatenate(columns).reshape(len(columns), share)
        attn = (
            lax.all_gather(in_weight, every, axis=0, tiled=True),
            lax.all_gather(out_weight, every, axis=0, tiled=True),
            jnp.pad(
                lax.all_gather(flat, every, axis=1, tiled=True), ((0, 16 - len(columns)), (0, 0))
            ).astype(F32),
        )
        up = lax.all_gather(up_weight, "wide", axis=1, tiled=True)
        up = up.reshape(width, steps, UNITS).transpose(1, 0, 2)
        unit_vec = lax.all_gather(unit_rows, "wide", axis=1, tiled=True)
        unit_vec = unit_vec.reshape(32, steps, UNITS).transpose(1, 0, 2)
        down = lax.all_gather(down_weight, "wide", axis=0, tiled=True)
        down = down.reshape(steps, UNITS, width)
    results = layer(
        staged,
        tokens,
        cotangent,
        lengths,
        attn,
        up,
        down,
        unit_vec,
        head_scale,
        down_bias,
    )
    heads = head_scale.shape[0]
    pairs = width // 128
    if staged:
        mixed, tokens_grad, down_total, up_total, shares, vec_shares = results
        up_total = up_total.astype(F32).reshape(width, UNITS)
        down_total = down_total.astype(F32).reshape(UNITS, width)
        unit_totals = [vec_shares[index] for index in range(3)]
        down_sum = vec_shares[3:5].reshape(width)
        scale_sum = vec_shares[5].reshape(4, 128)[:, :4].reshape(heads) / head_scale.astype(F32)
        offset = share * lax.rem(lax.axis_index("wide"), 128 // share)
        own = vec_shares[6:9].reshape(12, 128)
        own = lax.dynamic_slice(own, (0, offset), (len(columns), share))
        vec_totals = [own[index] for index in range(len(columns))]
        shares = shares.reshape(pairs, share, 512)
        in_total = shares[:, :, :384].reshape(pairs, share, 3, 128)
        in_total = in_total.transpose(1, 2, 0, 3).reshape(share, 3 * width)
        out_total = shares[:, :, 384:].transpose(1, 0, 2).reshape(share, width)
    else:
        (mixed, tokens_grad, chunks, up_grad, down_grad, vec_grads, unit_grads) = results[:7]
        down_sum, scale_sum = results[7:]

        def scatter(value, axis=0, over=every):
            return lax.psum_scatter(value, over, scatter_dimension=axis, tiled=True)

        def both_ways(value, axis):
            part = scatter(value.astype(BF), axis, "wide")
            return lax.psum(part, "dp").astype(F32)

        up_total = both_ways(up_grad.transpose(1, 0, 2).reshape(width, units), 1)
        down_total = both_ways(down_grad.reshape(units, width), 0)
        unit_totals = [
            lax.psum(scatter(item.reshape(units), 0, "wide"), "dp") for item in unit_grads
        ]
        down_sum, scale_sum = lax.psum((down_sum, scale_sum), every)
        vec_totals = [scatter(item) for item in vec_grads]
        natural = chunks.transpose(0, 2, 1, 3, 4).reshape(pairs, width, 512)
        in_total = natural[:, :, :384].reshape(pairs, width, 3, 128)
        in_total = scatter(in_total.transpose(1, 2, 0, 3).reshape(width, 3 * width).astype(F32))
        out_total = scatter(
            natural[:, :, 384:].transpose(1, 0, 2).reshape(width, width).astype(F32)
        )
    return (
        mixed,
        tokens_grad,
        in_total,
        vec_totals[0],
        vec_totals[1],
        out_total,
        vec_totals[2],
        scale_sum,
        vec_totals[3],
        vec_totals[4],
        vec_totals[5],
        vec_totals[6],
        vec_totals[7],
        vec_totals[8],
        up_total,
        unit_totals[0],
        unit_totals[1],
        unit_totals[2],
        down_total,
        down_sum,
    )


def solution(mesh):
    by_all = P(("dp", "wide"))
    rows_all = P(("dp", "wide"), None)
    axes = (mesh.shape["dp"], mesh.shape["wide"])
    return jax.shard_map(
        functools.partial(body, axes),
        mesh=mesh,
        in_specs=(
            rows_all,
            rows_all,
            rows_all,
            rows_all,
            by_all,
            by_all,
            rows_all,
            by_all,
            P(),
            by_all,
            by_all,
            by_all,
            by_all,
            by_all,
            by_all,
            P(None, "wide"),
            P("wide"),
            P("wide"),
            P("wide"),
            P("wide", None),
            P(),
        ),
        out_specs=(
            rows_all,
            rows_all,
            rows_all,
            by_all,
            by_all,
            rows_all,
            by_all,
            P(),
            by_all,
            by_all,
            by_all,
            by_all,
            by_all,
            by_all,
            P(None, "wide"),
            P("wide"),
            P("wide"),
            P("wide"),
            P("wide", None),
            P(),
        ),
        check_vma=False,
    )
```

```python
import functools

import jax
import jax.numpy as jnp
from jax import lax
from jax.experimental import pallas as pl
from jax.experimental.pallas import tpu as pltpu
from jax.sharding import PartitionSpec as P

EPS = 1e-05
ROOT_HALF = 0.7071067811865476
INV_ROOT_TAU = 0.3989422804014327
LOG2E = 1.4426950408889634
MASKED = -1e30
BF = jnp.bfloat16
F32 = jnp.float32
TILE = 256
UNITS = 512
SLIM = 64
MESH = pl.DeviceIdType.MESH
VMEM_LIMIT = 62 * 1024 * 1024
ANY = pl.BlockSpec(memory_space=pl.ANY)


def dot_nn(left, right):
    return lax.dot_general(left, right, (((1,), (0,)), ((), ())), preferred_element_type=F32)


def dot_nt(left, right):
    return lax.dot_general(left, right, (((1,), (1,)), ((), ())), preferred_element_type=F32)


def dot_tn(left, right):
    return lax.dot_general(left, right, (((0,), (0,)), ((), ())), preferred_element_type=F32)


def params(**more):
    return pltpu.CompilerParams(
        dimension_semantics=("arbitrary",), vmem_limit_bytes=VMEM_LIMIT, **more
    )


def whole(shape):
    zeros = (0,) * len(shape)
    return pl.BlockSpec(shape, lambda *_: zeros, pipeline_mode=pl.Buffered(1))


def row_norm(values):
    center = values - jnp.mean(values, axis=-1, keepdims=True)
    inv = lax.rsqrt(jnp.mean(center * center, axis=-1, keepdims=True) + EPS)
    return center * inv, inv


def norm_back(grad, gain, normed, inv):
    scaled = grad * gain
    first = jnp.mean(scaled, axis=-1, keepdims=True)
    cross = jnp.mean(scaled * normed, axis=-1, keepdims=True)
    return inv * (scaled - first - normed * cross)


def column_sum(values):
    return jnp.sum(values, axis=0, keepdims=True)


def lane_fold(values):
    total = values[:, :128]
    for start in range(128, values.shape[1], 128):
        total = total + values[:, start : start + 128]
    return total


def cross_flag(lengths_ref, rows_ref):
    return jnp.where(lengths_ref[0, 0] == rows_ref.shape[0], 0.0, MASKED)


def stacked(value, low_lanes):
    zero = jnp.zeros_like(value)
    return jnp.concatenate(
        [jnp.where(low_lanes, value, zero), jnp.where(low_lanes, zero, value)], axis=0
    )


def attention_pair(cross, q_ref, k_ref, v_ref, scale, scaled_ref, out_ref, lse_ref, vext_ref):
    rows = q_ref.shape[0]
    half = rows // 2
    factor = LOG2E * 64 ** (-0.5)
    low_lanes = lax.broadcasted_iota(jnp.int32, (1, 128), 1) < 64
    below = lax.broadcasted_iota(jnp.int32, (TILE, TILE), 1) <= lax.broadcasted_iota(
        jnp.int32, (TILE, TILE), 0
    )
    vext_ref[:, :128] = v_ref[...]
    vext_ref[:, 128:] = jnp.ones((rows, 128), BF)
    for start in range(0, rows, TILE):
        stop = start + TILE
        both = dot_nt(stacked(q_ref[start:stop], low_lanes), k_ref[:stop])
        peaks, weights = [], []
        for head in range(2):
            raw = both[head * TILE : (head + 1) * TILE]
            parts = []
            if start >= half:
                parts.append((raw[:, :half], cross))
                if start > half:
                    parts.append((raw[:, half:start], None))
            elif start > 0:
                parts.append((raw[:, :start], None))
            parts.append((jnp.where(below, raw[:, start:stop], MASKED), None))
            peak = None
            for piece, shift in parts:
                top = jnp.max(piece, axis=-1, keepdims=True)
                if shift is not None:
                    top = top + shift
                peak = top if peak is None else jnp.maximum(peak, top)
            peaks.append(peak)
            pieces = []
            for piece, shift in parts:
                level = peak if shift is None else peak - shift
                pieces.append(jnp.exp2((piece - level) * factor).astype(BF))
            weights.append(pieces[0] if len(pieces) == 1 else jnp.concatenate(pieces, axis=1))
        both = dot_nn(jnp.concatenate(weights, axis=0), vext_ref[:stop])
        total = jnp.where(low_lanes, both[:TILE, 128:], both[TILE:, 128:])
        peak = jnp.where(low_lanes, peaks[0], peaks[1])
        mixed = jnp.where(low_lanes, both[:TILE, :128], both[TILE:, :128]) / total
        out_ref[start:stop] = mixed
        scaled_ref[start:stop] = (mixed * scale).astype(BF)
        lse = (peak * factor + jnp.log2(total)).T
        lse_ref[0, 0:1, start:stop] = lse[0:1]
        lse_ref[0, 1:2, start:stop] = lse[64:65]


def project_pair(first_ref, weights, bias, proj_ref):
    proj_ref[0] = (dot_nn(first_ref[...], weights) + bias).astype(BF)


def three(proj_ref):
    return [proj_ref.at[0, :, pl.ds(part * 128, 128)] for part in range(3)]


def plain_first_kernel(
    lengths_ref,
    tokens_ref,
    wq_ref,
    wk_ref,
    wv_ref,
    vectors_ref,
    bq_ref,
    bv_ref,
    hs_ref,
    first_ref,
    proj_ref,
    scaled_ref,
    attended_ref,
    lse_ref,
    vext_ref,
):
    @pl.when(pl.program_id(0) == 0)
    def _():
        for start in range(0, tokens_ref.shape[0], TILE):
            rows = pl.ds(start, TILE)
            normed, _ = row_norm(tokens_ref[rows].astype(F32))
            first_ref[rows] = (normed * vectors_ref[3:4] + vectors_ref[4:5]).astype(BF)

    weights = jnp.concatenate([wq_ref[...], wk_ref[...], wv_ref[...]], axis=1)
    bias = jnp.concatenate([bq_ref[0:1], jnp.zeros((1, 128), F32), bv_ref[1:2]], axis=1)
    project_pair(first_ref, weights, bias, proj_ref)
    attention_pair(
        cross_flag(lengths_ref, tokens_ref), *three(proj_ref), hs_ref[...], scaled_ref, attended_ref, lse_ref, vext_ref
    )


def plain_first(lengths, tokens, weights, vectors, head_lanes):
    rows, width = tokens.shape
    pairs = width // 128
    column = pl.BlockSpec((rows, 128), lambda p: (0, p))
    bias = pl.BlockSpec((16, 128), lambda p: (0, p))
    return pl.pallas_call(
        plain_first_kernel,
        grid=(pairs,),
        in_specs=[
            pl.BlockSpec(memory_space=pltpu.SMEM),
            whole((rows, width)),
            pl.BlockSpec((width, 128), lambda p: (0, p)),
            pl.BlockSpec((width, 128), lambda p: (0, pairs + p)),
            pl.BlockSpec((width, 128), lambda p: (0, 2 * pairs + p)),
            whole(vectors.shape),
            bias,
            bias,
            pl.BlockSpec((1, 128), lambda p: (0, p)),
        ],
        out_specs=[
            whole((rows, width)),
            pl.BlockSpec((1, rows, 384), lambda p: (p, 0, 0)),
            column,
            column,
            pl.BlockSpec((1, 8, rows), lambda p: (p, 0, 0)),
        ],
        out_shape=[
            jax.ShapeDtypeStruct((rows, width), BF),
            jax.ShapeDtypeStruct((pairs, rows, 384), BF),
            jax.ShapeDtypeStruct((rows, width), BF),
            jax.ShapeDtypeStruct((rows, width), F32),
            jax.ShapeDtypeStruct((pairs, 8, rows), F32),
        ],
        scratch_shapes=[pltpu.VMEM((rows, 256), BF)],
        compiler_params=params(),
        name="plain_first",
    )(lengths, tokens, weights, weights, weights, vectors, vectors, vectors, head_lanes)


def out_proj_rows(scaled_ref, weight_ref, vec_ref, tokens_ref, branch_ref, middle_ref):
    branch = dot_nn(scaled_ref[...], weight_ref[...]) + vec_ref[2:3]
    normed, _ = row_norm(branch)
    middle = tokens_ref[...].astype(F32) + (normed * vec_ref[5:6] + vec_ref[6:7])
    again, _ = row_norm(middle)
    branch_ref[...] = branch
    middle_ref[...] = middle
    return (again * vec_ref[7:8] + vec_ref[8:9]).astype(BF)


def out_proj_kernel(scaled_ref, weight_ref, vec_ref, tokens_ref, branch_ref, middle_ref, feed_ref):
    feed_ref[...] = out_proj_rows(
        scaled_ref, weight_ref, vec_ref, tokens_ref, branch_ref, middle_ref
    )


def out_proj(scaled, weights, vectors, tokens):
    rows, width = tokens.shape
    by_row = pl.BlockSpec((TILE, width), lambda i: (i, 0))
    return pl.pallas_call(
        out_proj_kernel,
        grid=(rows // TILE,),
        in_specs=[
            by_row,
            whole((width, width)),
            whole(vectors.shape),
            by_row,
        ],
        out_specs=[by_row, by_row, by_row],
        out_shape=[
            jax.ShapeDtypeStruct((rows, width), F32),
            jax.ShapeDtypeStruct((rows, width), F32),
            jax.ShapeDtypeStruct((rows, width), BF),
        ],
        compiler_params=params(),
        name="out_proj",
    )(scaled, weights, vectors, tokens)


def phi_and_slope(value):
    bell = jnp.exp2(value * value * (-0.5 * LOG2E))
    t = 1.0 / (1.0 + (0.3275911 * ROOT_HALF) * jnp.abs(value))
    series = t * (
        0.5 * 0.254829592
        + t
        * (
            0.5 * -0.284496736
            + t * (0.5 * 1.421413741 + t * (0.5 * -1.453152027 + t * (0.5 * 1.061405429)))
        )
    )
    tail = series * bell
    area = jnp.where(value < 0.0, tail, 1.0 - tail)
    return value * area, area + value * bell * INV_ROOT_TAU


def up_step(feed_ref, up_ref, vec_ref, act_ref, slope_ref, sums_ref):
    for left in range(0, UNITS, TILE):
        columns = slice(left, left + TILE)
        pre = dot_nn(feed_ref[...], up_ref[0, :, columns])
        bias = vec_ref[0, 0:1, columns].astype(F32)
        for start in range(0, feed_ref.shape[0], SLIM):
            rows = slice(start, start + SLIM)
            act, slope = phi_and_slope(pre[rows] + bias)
            act_ref[0, rows, columns] = act.astype(BF)
            slope_ref[0, rows, columns] = slope.astype(BF)
            sums_ref[0, rows] += lane_fold(act)
            sums_ref[1, rows] += lane_fold(act * act)


def side_by_side(*columns):
    lane = lax.broadcasted_iota(jnp.int32, (1, 128), 1)
    result = jnp.broadcast_to(columns[-1], (columns[-1].shape[0], 128))
    for index in range(len(columns) - 2, -1, -1):
        result = jnp.where(lane == index, columns[index], result)
    return result


def up_stats(units, stats_ref, sums_ref):
    for start in range(0, stats_ref.shape[0], TILE):
        rows = pl.ds(start, TILE)
        mean = jnp.sum(sums_ref[0, rows], axis=1, keepdims=True) / units
        square = jnp.sum(sums_ref[1, rows], axis=1, keepdims=True) / units
        inv = lax.rsqrt(square - mean * mean + EPS)
        stats_ref[rows] = side_by_side(mean, inv)


def up_kernel(units, feed_ref, up_ref, vec_ref, act_ref, slope_ref, stats_ref, sums_ref):
    step = pl.program_id(0)

    @pl.when(step == 0)
    def _():
        sums_ref[...] = jnp.zeros_like(sums_ref)

    up_step(feed_ref, up_ref, vec_ref, act_ref, slope_ref, sums_ref)

    @pl.when(step == pl.num_programs(0) - 1)
    def _():
        up_stats(units, stats_ref, sums_ref)


def up_pass(feed, up, vec):
    rows, width = feed.shape
    steps = up.shape[0]
    block = pl.BlockSpec((1, rows, UNITS), lambda j: (j, 0, 0))
    return pl.pallas_call(
        functools.partial(up_kernel, steps * UNITS),
        grid=(steps,),
        in_specs=[
            whole((rows, width)),
            pl.BlockSpec((1, width, UNITS), lambda j: (j, 0, 0)),
            pl.BlockSpec((1, vec.shape[1], UNITS), lambda j: (j, 0, 0)),
        ],
        out_specs=[block, block, whole((rows, 128))],
        out_shape=[
            jax.ShapeDtypeStruct((steps, rows, UNITS), BF),
            jax.ShapeDtypeStruct((steps, rows, UNITS), BF),
            jax.ShapeDtypeStruct((rows, 128), F32),
        ],
        scratch_shapes=[pltpu.VMEM((2, rows, 128), F32)],
        compiler_params=params(),
        name="up_pass",
    )(feed, up, vec)


def down_kernel(
    units,
    act_ref,
    stats_ref,
    vec_ref,
    down_ref,
    cot_ref,
    middle_ref,
    shift_ref,
    mixed_ref,
    down_grad_ref,
    e_ref,
    all_stats_ref,
    vec_grad_ref,
    total_ref,
    sums_ref,
    low_ref,
):
    step = pl.program_id(0)
    last = pl.num_programs(0) - 1
    rows_all = cot_ref.shape[0]

    @pl.when(step == 0)
    def _():
        total_ref[...] = jnp.zeros_like(total_ref)
        sums_ref[...] = jnp.zeros_like(sums_ref)

    gain = vec_ref[0, 1:2].astype(F32)
    shift = vec_ref[0, 2:3].astype(F32)
    slims = [slice(start, start + SLIM) for start in range(0, rows_all, SLIM)]

    def normalized(rows, columns):
        value = act_ref[0, rows, columns].astype(F32)
        return (value - stats_ref[rows, 0:1]) * stats_ref[rows, 1:2]

    for rows in slims:
        low_ref[rows] = (normalized(rows, slice(0, UNITS)) * gain + shift).astype(BF)
    for left in range(0, UNITS, TILE):
        columns = slice(left, left + TILE)
        grads = dot_nt(cot_ref[...], down_ref[0, columns])
        gain_grad = jnp.zeros((SLIM, TILE), F32)
        bias_grad = jnp.zeros((SLIM, TILE), F32)
        for rows in slims:
            normed = normalized(rows, columns)
            grad = grads[rows]
            gain_grad = gain_grad + grad * normed
            bias_grad = bias_grad + grad
            e = grad * gain[:, columns]
            e_ref[0, rows, columns] = e.astype(BF)
            sums_ref[0, rows] += lane_fold(e)
            sums_ref[1, rows] += lane_fold(e * normed)
        vec_grad_ref[0, 0:1, columns] = column_sum(gain_grad)
        vec_grad_ref[0, 1:2, columns] = column_sum(bias_grad)
    for left in range(0, total_ref.shape[1], TILE):
        columns = slice(left, left + TILE)
        total_ref[:, columns] += dot_nn(low_ref[...], down_ref[0, :, columns])
    for left in range(0, UNITS, TILE):
        columns = slice(left, left + TILE)
        down_grad_ref[0, columns] = dot_tn(low_ref[:, columns], cot_ref[...]).astype(BF)

    @pl.when(step == last)
    def _():
        for start in range(0, rows_all, TILE):
            rows = pl.ds(start, TILE)
            mixed_ref[rows] = (
                middle_ref[rows] + total_ref[rows] + shift_ref[...].astype(F32)
            ).astype(BF)
            first = jnp.sum(sums_ref[0, rows], axis=1, keepdims=True) / units
            cross = jnp.sum(sums_ref[1, rows], axis=1, keepdims=True) / units
            all_stats_ref[rows] = side_by_side(
                stats_ref[rows, 0:1], stats_ref[rows, 1:2], first, cross
            )


def down_pass(act, stats, vec, down, cotangent, middle, shift):
    rows, width = cotangent.shape
    steps = act.shape[0]
    block = pl.BlockSpec((1, rows, UNITS), lambda j: (j, 0, 0))
    return pl.pallas_call(
        functools.partial(down_kernel, steps * UNITS),
        grid=(steps,),
        in_specs=[
            block,
            whole((rows, 128)),
            pl.BlockSpec((1, vec.shape[1], UNITS), lambda j: (j, 0, 0)),
            pl.BlockSpec((1, UNITS, width), lambda j: (j, 0, 0)),
            whole((rows, width)),
            whole((rows, width)),
            whole((1, width)),
        ],
        out_specs=[
            whole((rows, width)),
            pl.BlockSpec((1, UNITS, width), lambda j: (j, 0, 0)),
            block,
            whole((rows, 128)),
            pl.BlockSpec((1, 8, UNITS), lambda j: (j, 0, 0)),
        ],
        out_shape=[
            jax.ShapeDtypeStruct((rows, width), BF),
            jax.ShapeDtypeStruct((steps, UNITS, width), BF),
            jax.ShapeDtypeStruct((steps, rows, UNITS), BF),
            jax.ShapeDtypeStruct((rows, 128), F32),
            jax.ShapeDtypeStruct((steps, 8, UNITS), F32),
        ],
        scratch_shapes=[
            pltpu.VMEM((rows, width), F32),
            pltpu.VMEM((2, rows, 128), F32),
            pltpu.VMEM((rows, UNITS), BF),
        ],
        compiler_params=params(),
        name="down_pass",
    )(act, stats, vec, down, cotangent, middle, shift)


def up_back_step(act, slope, e, stats_ref, up, low_ref, total_ref):
    bias_grad = jnp.zeros((SLIM, UNITS), F32)
    for start in range(0, total_ref.shape[0], SLIM):
        rows = slice(start, start + SLIM)
        inv = stats_ref[rows, 1:2]
        normed = (act[rows].astype(F32) - stats_ref[rows, 0:1]) * inv
        grad_act = inv * (
            e[rows].astype(F32) - stats_ref[rows, 2:3] - normed * stats_ref[rows, 3:4]
        )
        low = (grad_act * slope[rows].astype(F32)).astype(BF)
        bias_grad = bias_grad + low.astype(F32)
        low_ref[rows, 0:UNITS] = low
    for left in range(0, total_ref.shape[1], TILE):
        columns = slice(left, left + TILE)
        total_ref[:, columns] += dot_nt(low_ref[:, 0:UNITS], up[columns])
    return column_sum(bias_grad)


def up_back_kernel(
    act_ref,
    slope_ref,
    e_ref,
    stats_ref,
    up_ref,
    feed_ref,
    up_grad_ref,
    bias_grad_ref,
    total_ref,
    turned_ref,
    low_ref,
):
    @pl.when(pl.program_id(0) == 0)
    def _():
        total_ref[...] = jnp.zeros_like(total_ref)
        turned_ref[...] = feed_ref[...].T

    bias_grad_ref[0, 0:1] = up_back_step(
        act_ref.at[0],
        slope_ref.at[0],
        e_ref.at[0],
        stats_ref,
        up_ref.at[0],
        low_ref,
        total_ref,
    )
    up_grad_ref[0] = dot_nn(turned_ref[...], low_ref[...]).astype(BF)


def up_back(act, slope, e, stats, up, feed):
    rows, width = feed.shape
    steps = act.shape[0]
    block = pl.BlockSpec((1, rows, UNITS), lambda j: (j, 0, 0))
    narrow = whole((rows, 128))
    return pl.pallas_call(
        up_back_kernel,
        grid=(steps,),
        in_specs=[
            block,
            block,
            block,
            narrow,
            pl.BlockSpec((1, width, UNITS), lambda j: (j, 0, 0)),
            whole((rows, width)),
        ],
        out_specs=[
            pl.BlockSpec((1, width, UNITS), lambda j: (j, 0, 0)),
            pl.BlockSpec((1, 8, UNITS), lambda j: (j, 0, 0)),
            whole((rows, width)),
        ],
        out_shape=[
            jax.ShapeDtypeStruct((steps, width, UNITS), BF),
            jax.ShapeDtypeStruct((steps, 8, UNITS), F32),
            jax.ShapeDtypeStruct((rows, width), F32),
        ],
        scratch_shapes=[pltpu.VMEM((width, rows), BF), pltpu.VMEM((rows, UNITS), BF)],
        compiler_params=params(),
        name="up_back",
    )(act, slope, e, stats, up, feed)


def norms_back(grad_feed, cot_ref, middle_ref, branch_ref, vec_ref, sums_ref):
    normed, inv = row_norm(middle_ref[...])
    cot = cot_ref[...].astype(F32)
    grad_middle = cot + norm_back(grad_feed, vec_ref[7:8], normed, inv)
    sums_ref[7:8] += column_sum(grad_feed * normed)
    sums_ref[8:9] += column_sum(grad_feed)
    sums_ref[9:10] += column_sum(cot)
    normed, inv = row_norm(branch_ref[...])
    low = norm_back(grad_middle, vec_ref[5:6], normed, inv).astype(BF)
    sums_ref[5:6] += column_sum(grad_middle * normed)
    sums_ref[6:7] += column_sum(grad_middle)
    sums_ref[2:3] += column_sum(low.astype(F32))
    return grad_middle, low


def heads_back(low, weights, scale, attended):
    grad_out = (dot_nt(low, weights) * scale).astype(BF)
    product = grad_out.astype(F32) * attended
    high = product.astype(BF)
    rest = (product - high.astype(F32)).astype(BF)
    heads = (
        lax.broadcasted_iota(jnp.int32, (product.shape[1], 128), 0) // 64
        == lax.broadcasted_iota(jnp.int32, (product.shape[1], 128), 1)
    ).astype(BF)
    return grad_out, dot_nn(high, heads) + dot_nn(rest, heads)


def out_back_kernel(
    grad_feed_ref,
    cot_ref,
    middle_ref,
    branch_ref,
    scaled_ref,
    attended_ref,
    weight_ref,
    vec_ref,
    hs_ref,
    grad_middle_ref,
    ga_ref,
    out_grad_ref,
    delta_ref,
    sums_ref,
    total_ref,
):
    step = pl.program_id(0)

    @pl.when(step == 0)
    def _():
        total_ref[...] = jnp.zeros_like(total_ref)
        sums_ref[...] = jnp.zeros_like(sums_ref)

    grad_middle, low = norms_back(
        grad_feed_ref[...], cot_ref, middle_ref, branch_ref, vec_ref, sums_ref
    )
    grad_middle_ref[...] = grad_middle
    ga_ref[...], delta = heads_back(low, weight_ref[...], hs_ref[...], attended_ref[...])
    total_ref[...] += dot_tn(scaled_ref[...], low)
    delta_ref[...] = delta.T[: delta_ref.shape[0]]

    @pl.when(step == pl.num_programs(0) - 1)
    def _():
        out_grad_ref[...] = total_ref[...].astype(BF)


def out_back(
    grad_feed, cotangent, middle, branch, scaled, attended, weights, vectors, head_lanes
):
    rows, width = cotangent.shape
    heads = 2 * width // 128
    by_row = pl.BlockSpec((TILE, width), lambda i: (i, 0))
    return pl.pallas_call(
        out_back_kernel,
        grid=(rows // TILE,),
        in_specs=[
            by_row,
            by_row,
            by_row,
            by_row,
            by_row,
            by_row,
            whole((width, width)),
            whole(vectors.shape),
            whole((1, width)),
        ],
        out_specs=[
            by_row,
            by_row,
            whole((width, width)),
            pl.BlockSpec((heads, TILE), lambda i: (0, i)),
            whole((16, width)),
        ],
        out_shape=[
            jax.ShapeDtypeStruct((rows, width), F32),
            jax.ShapeDtypeStruct((rows, width), BF),
            jax.ShapeDtypeStruct((width, width), BF),
            jax.ShapeDtypeStruct((heads, rows), F32),
            jax.ShapeDtypeStruct((16, width), F32),
        ],
        scratch_shapes=[pltpu.VMEM((width, width), F32)],
        compiler_params=params(),
        name="out_back",
    )(
        grad_feed,
        cotangent,
        middle,
        branch,
        scaled,
        attended,
        weights,
        vectors,
        head_lanes,
    )


def attention_back_keys(
    starts, cross, q_ref, k_ref, v_ref, ga_ref, lse_ref, deltas, dq_ref, dk_ref, dv_ref
):
    rows = q_ref.shape[0]
    half = rows // 2
    factor = LOG2E * 64 ** (-0.5)
    low_lanes = lax.broadcasted_iota(jnp.int32, (1, 128), 1) < 64
    above = lax.broadcasted_iota(jnp.int32, (TILE, TILE), 0) <= lax.broadcasted_iota(
        jnp.int32, (TILE, TILE), 1
    )

    def pick(both):
        return jnp.where(low_lanes, both[:TILE], both[TILE:])

    for start in starts:
        stop = start + TILE
        keys = k_ref[start:stop]
        keys_apart = stacked(keys, low_lanes)
        values_apart = stacked(v_ref[start:stop], low_lanes)
        dk = jnp.zeros((TILE, 128), F32)
        dv = jnp.zeros((TILE, 128), F32)
        for left, right in ((start, half), (half, rows)) if start < half else ((start, rows),):
            raw = dot_nt(keys_apart, q_ref[left:right])
            grad_weights = dot_nt(values_apart, ga_ref[left:right])
            weights, grad_scores = [], []
            for head in range(2):
                mine = slice(head * TILE, (head + 1) * TILE)
                level = lse_ref[head : head + 1, left:right]
                if start < half <= left:
                    level = level - cross
                exponent = raw[mine] * factor - level
                if left == start:
                    first = jnp.where(above, exponent[:, :TILE], MASKED)
                    exponent = (
                        first
                        if right - left == TILE
                        else jnp.concatenate([first, exponent[:, TILE:]], axis=1)
                    )
                weight = jnp.exp2(exponent)
                weights.append(weight.astype(BF))
                delta = deltas[head][:, left:right]
                grad_scores.append((weight * (grad_weights[mine] - delta)).astype(BF))
            dv = dv + pick(dot_nn(jnp.concatenate(weights, axis=0), ga_ref[left:right]))
            dk = dk + pick(dot_nn(jnp.concatenate(grad_scores, axis=0), q_ref[left:right]))
            dq = jnp.where(low_lanes, dot_tn(grad_scores[0], keys), dot_tn(grad_scores[1], keys))
            if start == 0:
                dq_ref[left:right] = dq
            else:
                dq_ref[left:right] += dq
        dk_ref[start:stop] = dk
        dv_ref[start:stop] = dv


def in_back_pair(dq_ref, dk_ref, dv_ref, weights, turned_ref, out_grad_ref, chunk_ref, total_ref):
    factor = 64 ** (-0.5)
    dq = (dq_ref[...] * factor).astype(BF)
    dk = (dk_ref[...] * factor).astype(BF)
    dv = dv_ref[...].astype(BF)
    grads = jnp.concatenate([dq, dk, dv], axis=1)
    shares = dot_nn(turned_ref[...], grads).astype(BF)
    for start in range(0, total_ref.shape[0], TILE):
        part = jnp.concatenate(
            [shares[start : start + TILE], out_grad_ref[start : start + TILE]], axis=1
        )
        chunk_ref[:, start // TILE] = part.reshape(8, 32, 512)
        columns = slice(start, start + TILE)
        total_ref[:, columns] += dot_nt(grads, weights[columns])
    return column_sum(dq.astype(F32)), column_sum(dv.astype(F32))


def tokens_back(tokens, grad, grad_middle, gain):
    normed, inv = row_norm(tokens.astype(F32))
    back = norm_back(grad, gain, normed, inv)
    return (grad_middle + back).astype(BF), column_sum(grad * normed), column_sum(grad)


def in_back_kernel(
    lengths_ref,
    proj_ref,
    ga_ref,
    lse_ref,
    delta_ref,
    wq_ref,
    wk_ref,
    wv_ref,
    first_ref,
    out_grad_ref,
    tokens_ref,
    gain_ref,
    grad_middle_ref,
    chunk_ref,
    bias_ref,
    tokens_grad_ref,
    sums_ref,
    dq_ref,
    dk_ref,
    dv_ref,
    turned_ref,
    total_ref,
):
    step = pl.program_id(0)
    q_ref, k_ref, v_ref = three(proj_ref)
    rows_all = tokens_ref.shape[0]

    @pl.when(step == 0)
    def _():
        turned_ref[...] = first_ref[...].T
        total_ref[...] = jnp.zeros_like(total_ref)

    deltas = [delta_ref[0, head : head + 1] for head in range(2)]
    attention_back_keys(
        range(0, rows_all, TILE),
        cross_flag(lengths_ref, tokens_ref),
        q_ref,
        k_ref,
        v_ref,
        ga_ref,
        lse_ref.at[0],
        deltas,
        dq_ref,
        dk_ref,
        dv_ref,
    )
    weights = jnp.concatenate([wq_ref[...], wk_ref[...], wv_ref[...]], axis=1)
    query_sum, value_sum = in_back_pair(
        dq_ref, dk_ref, dv_ref, weights, turned_ref, out_grad_ref, chunk_ref.at[0], total_ref
    )
    bias_ref[0, 0:1] = query_sum
    bias_ref[0, 1:2] = value_sum

    @pl.when(step == pl.num_programs(0) - 1)
    def _():
        gain_grad = jnp.zeros((1, total_ref.shape[1]), F32)
        shift_grad = jnp.zeros((1, total_ref.shape[1]), F32)
        for start in range(0, rows_all, TILE):
            rows = pl.ds(start, TILE)
            tokens_grad_ref[rows], gain_part, shift_part = tokens_back(
                tokens_ref[rows], total_ref[rows], grad_middle_ref[rows], gain_ref[...]
            )
            gain_grad = gain_grad + gain_part
            shift_grad = shift_grad + shift_part
        sums_ref[0:1] = gain_grad
        sums_ref[1:2] = shift_grad


def in_back(lengths, projected, ga, lse, delta, weights, first, out_grad, tokens, gain, grad_middle):
    rows, width = tokens.shape
    pairs = width // 128
    column = pl.BlockSpec((rows, 128), lambda p: (0, p))
    square = whole((rows, width))
    return pl.pallas_call(
        in_back_kernel,
        grid=(pairs,),
        in_specs=[
            pl.BlockSpec(memory_space=pltpu.SMEM),
            pl.BlockSpec((1, rows, 384), lambda p: (p, 0, 0)),
            column,
            pl.BlockSpec((1, 8, rows), lambda p: (p, 0, 0)),
            pl.BlockSpec((1, 2, rows), lambda p: (p, 0, 0)),
            pl.BlockSpec((width, 128), lambda p: (0, p)),
            pl.BlockSpec((width, 128), lambda p: (0, pairs + p)),
            pl.BlockSpec((width, 128), lambda p: (0, 2 * pairs + p)),
            square,
            column,
            square,
            whole((1, width)),
            square,
        ],
        out_specs=[
            pl.BlockSpec((1, 8, width // TILE, 32, 512), lambda p: (p, 0, 0, 0, 0)),
            pl.BlockSpec((1, 8, 128), lambda p: (p, 0, 0)),
            square,
            whole((8, width)),
        ],
        out_shape=[
            jax.ShapeDtypeStruct((pairs, 8, width // TILE, 32, 512), BF),
            jax.ShapeDtypeStruct((pairs, 8, 128), F32),
            jax.ShapeDtypeStruct((rows, width), BF),
            jax.ShapeDtypeStruct((8, width), F32),
        ],
        scratch_shapes=[
            pltpu.VMEM((rows, 128), F32),
            pltpu.VMEM((rows, 128), F32),
            pltpu.VMEM((rows, 128), F32),
            pltpu.VMEM((width, rows), BF),
            pltpu.VMEM((rows, width), F32),
        ],
        compiler_params=params(),
        name="in_back",
    )(
        lengths,
        projected,
        ga,
        lse,
        delta,
        weights,
        weights,
        weights,
        first,
        out_grad,
        tokens,
        gain,
        grad_middle,
    )


class Place:
    def __init__(self):
        self.z = lax.axis_index("dp")
        wide = lax.axis_index("wide")
        self.y = wide // 4
        self.x = (wide // 2) % 2
        self.c = wide % 2
        self.core = (self.z, wide + 1 - 2 * self.c)
        self.side = (self.z, wide + 2 - 4 * self.x)
        self.over = (self.z, wide + 4 - 8 * self.y)
        self.ranks = (self.z + 1 - 2 * (self.z % 2), (self.z + 2) % 4, 3 - self.z)
        self.planes = tuple((rank, wide) for rank in self.ranks)

    def greet(self, planes=True):
        barrier = pltpu.get_barrier_semaphore()
        peers = (self.core, self.side, self.over) + (self.planes if planes else ())
        for peer in peers:
            pl.semaphore_signal(barrier, inc=1, device_id=peer, device_id_type=MESH)
        pl.semaphore_wait(barrier, len(peers))


class WideGather:
    copies = 10

    def __init__(
        self, place, view, count, send, recv, first, source=None, last=None, offset=0, total=None
    ):
        y, x, c = place.y, place.x, place.c
        here, side, over, far = (y, x, c), (y, 1 - x, c), (1 - y, x, c), (1 - y, 1 - x, c)
        upper, lower = pl.ds(offset, count // 2), pl.ds(offset + count // 2, count // 2)
        both = pl.ds(offset, count)
        everything = both if total is None else pl.ds(0, total)

        def copy(index, slot, part, peer):
            destination = view(*slot, part)
            return pltpu.make_async_remote_copy(
                src_ref=source.at[part] if source is not None and slot is here else destination,
                dst_ref=destination,
                send_sem=send.at[first + index],
                recv_sem=recv.at[first + index],
                device_id=peer,
                device_id_type=MESH,
            )

        self.all = (
            copy(0, here, upper, place.side),
            copy(1, here, lower, place.over),
            copy(2, here, upper, place.over),
            copy(3, here, lower, place.side),
            None if total == 0 else copy(4, here, everything, place.core),
            copy(5, side, upper, place.over),
            copy(6, over, lower, place.side),
            copy(7, side, both, place.core),
            copy(8, over, both, place.core),
            copy(9, far, both, place.core),
        )
        self.own = None
        if source is not None and last is not None:
            self.own = pltpu.make_async_copy(source, view(*here, everything), last)

    def start(self):
        if self.own is not None:
            self.own.start()
        for copy in self.all[:5]:
            if copy is not None:
                copy.start()

    def relay(self, stage):
        waits, starts = (((0, 1), (5, 6)), ((2, 3), (7, 8)), ((5, 6), (9,)))[stage]
        for index in waits:
            self.all[index].wait_recv()
        for index in starts:
            self.all[index].start()

    def finish(self):
        for index in (4, 7, 8, 9):
            if self.all[index] is not None:
                self.all[index].wait_recv()
        for copy in self.all:
            if copy is not None:
                copy.wait_send()
        if self.own is not None:
            self.own.wait()


def blocks_of(target):
    return lambda y, x, c, rows: target.at[y, x, c, rows]


class PairGather:
    copies = 2 * WideGather.copies + 6

    def __init__(self, place, target, send, recv, first, source, last):
        count = target.shape[-2]
        shared = count * 5 // 16
        alone = count - 2 * shared
        view = blocks_of(target)
        y, x, c = place.y, place.x, place.c
        odd = place.z % 2
        mine = pl.multiple_of(alone + shared * odd, 32)
        other = pl.multiple_of(alone + shared * (1 - odd), 32)
        start = first + WideGather.copies
        self.parts = (
            WideGather(place, view, alone, send, recv, first, source, last, 0, count),
            WideGather(place, view, shared, send, recv, start, source, None, mine, 0),
        )
        slots = ((y, 1 - x, c), (1 - y, x, c), (1 - y, 1 - x, c))

        def copy(index, slot, begin, peer):
            block = view(*slot, pl.ds(begin, shared))
            return pltpu.make_async_remote_copy(
                src_ref=block,
                dst_ref=block,
                send_sem=send.at[start + WideGather.copies + index],
                recv_sem=recv.at[start + WideGather.copies + index],
                device_id=peer,
                device_id_type=MESH,
            )

        self.along = [copy(k, slot, mine, place.planes[0]) for k, slot in enumerate(slots)]
        self.over = [copy(3 + k, slot, other, place.core) for k, slot in enumerate(slots)]

    def start(self):
        for part in self.parts:
            part.start()

    def relay(self, stage):
        if stage < 3:
            for part in self.parts:
                part.relay(stage)
        if stage == 1:
            self.along[0].start()
            self.along[1].start()
        if stage == 2:
            self.along[2].start()
        for k in ((), (), (), (0, 1), (2,))[stage]:
            self.along[k].wait_recv()
            self.over[k].start()

    def finish(self):
        for part in self.parts:
            part.finish()
        for copy in self.along:
            copy.wait_send()
        for copy in self.over:
            copy.wait()


LAG = 2


class Reduction:
    slots = 2 * LAG
    deep = 3 * LAG
    keep = 3 * LAG + 2

    @classmethod
    def scratch(cls):
        n, k = cls.slots, cls.keep
        return [
            pltpu.VMEM((cls.deep, 2, 2, 4, 32, 512), BF),
            pltpu.VMEM((n, 2, 2, 4, 32, 512), BF),
            pltpu.VMEM((n, 2, 2, 4, 16, 512), BF),
            pltpu.VMEM((n, 2, 4, 16, 512), BF),
            pltpu.VMEM((n, 4, 32, 512), BF),
            pltpu.VMEM((n, 3, 32, 512), BF),
            pltpu.VMEM((n, 32, 512), BF),
            pltpu.VMEM((k, 3, 32, 512), BF),
            pltpu.SemaphoreType.DMA((6, k)),
            pltpu.SemaphoreType.DMA((6, k)),
            pltpu.SemaphoreType.DMA((cls.deep,)),
        ]

    def __init__(self, place, refs):
        self.place = place
        (
            self.chip,
            self.partner,
            self.first,
            self.second,
            self.plane,
            self.from_z,
            self.sums,
            self.shared,
            self.send,
            self.recv,
            self.local,
        ) = refs

    def copy(self, index, slot, source, target, peer):
        return pltpu.make_async_remote_copy(
            src_ref=source,
            dst_ref=target,
            send_sem=self.send.at[index, slot],
            recv_sem=self.recv.at[index, slot],
            device_id=peer,
            device_id_type=MESH,
        )

    def wait(self, index, slot, arrived):
        self.copy(index, slot, arrived, arrived, self.place.core).wait()

    def load(self, chunk, source):
        slot = chunk % self.deep
        return pltpu.make_async_copy(source, self.chip.at[slot], self.local.at[slot])

    def stage0(self, chunk, view):
        slot, c = chunk % self.slots, self.place.c
        self.copy(
            0, slot, view.at[:, :, 1 - c], self.partner.at[slot], self.place.core
        ).start()
        self.load(chunk, view.at[:, :, c]).start()

    def stage1(self, chunk):
        p, slot, index = self.place, chunk % self.slots, chunk % self.deep
        partner, chip, target = self.partner.at[slot], self.chip.at[index], self.first.at[slot]
        self.load(chunk, partner).wait()
        self.wait(0, slot, partner)
        chip[...] += partner[...]
        self.copy(1, slot, chip.at[:, 1 - p.x, :, pl.ds(0, 16)], target.at[0], p.side).start()
        self.copy(1, slot, chip.at[1 - p.y, :, :, pl.ds(16, 16)], target.at[1], p.over).start()

    def stage2(self, chunk):
        p, slot, index = self.place, chunk % self.slots, chunk % self.deep
        chip, arrived, target = self.chip.at[index], self.first.at[slot], self.second.at[slot]
        self.wait(1, slot, arrived)
        for k in range(2):
            chip[k, p.x, :, 0:16] += arrived[0, k]
            chip[p.y, k, :, 16:32] += arrived[1, k]
        self.copy(2, slot, chip.at[1 - p.y, p.x, :, pl.ds(0, 16)], target.at[0], p.over).start()
        self.copy(2, slot, chip.at[p.y, 1 - p.x, :, pl.ds(16, 16)], target.at[1], p.side).start()

    def stage3(self, chunk):
        p, slot, index = self.place, chunk % self.slots, chunk % self.deep
        arrived, mine, plane = self.second.at[slot], self.chip.at[index, p.y, p.x], self.plane
        self.wait(2, slot, arrived)
        plane[slot, :, 0:16] = mine[:, 0:16] + arrived[0]
        plane[slot, :, 16:32] = mine[:, 16:32] + arrived[1]
        for k in range(3):
            target = self.from_z.at[slot, k]
            self.copy(3, slot, plane.at[slot, p.ranks[k]], target, p.planes[k]).start()

    def stage4(self, chunk):
        slot = chunk % self.slots
        self.wait(3, slot, self.from_z.at[slot])
        total = self.plane[slot, self.place.z].astype(F32)
        for k in range(3):
            total = total + self.from_z[slot, k].astype(F32)
        return total

    def spread(self, chunk, total):
        slot, place = chunk % self.slots, chunk % self.keep
        self.sums[slot] = total.astype(BF)
        peer = self.place.planes[1]
        self.copy(4, place, self.sums.at[slot], self.shared.at[place, 0], peer).start()

    def stage5(self, chunk):
        slot, place, peer = chunk % self.slots, chunk % self.keep, self.place.planes[0]
        shared = self.shared.at[place]
        self.wait(4, place, shared.at[0])
        self.copy(5, place, self.sums.at[slot], shared.at[1], peer).start()
        self.copy(5, place, shared.at[0], shared.at[2], peer).start()

    def stage6(self, chunk):
        slot, place, ranks = chunk % self.slots, chunk % self.keep, self.place.ranks
        self.wait(5, place, self.shared.at[place, pl.ds(1, 2)])
        return [
            (self.place.z, self.sums[slot]),
            (ranks[1], self.shared[place, 0]),
            (ranks[0], self.shared[place, 1]),
            (ranks[2], self.shared[place, 2]),
        ]


class SmallReduction:
    @staticmethod
    def scratch():
        return [
            pltpu.VMEM((2, 2, 2, 4, 16, 512), BF),
            pltpu.VMEM((2, 2, 4, 16, 512), BF),
            pltpu.VMEM((2, 2, 4, 16, 512), BF),
            pltpu.VMEM((2, 4, 16, 512), BF),
            pltpu.VMEM((4, 16, 512), BF),
            pltpu.VMEM((3, 16, 512), BF),
            pltpu.SemaphoreType.DMA((4,)),
            pltpu.SemaphoreType.DMA((4,)),
        ]

    def __init__(self, place, refs):
        self.place = place
        self.source, self.chip, self.partner, self.first, self.second, self.from_z = refs[:6]
        self.send, self.recv = refs[6:]

    def copy(self, index, source, target, peer):
        return pltpu.make_async_remote_copy(
            src_ref=source,
            dst_ref=target,
            send_sem=self.send.at[index],
            recv_sem=self.recv.at[index],
            device_id=peer,
            device_id_type=MESH,
        )

    def wait(self, index, arrived):
        self.copy(index, arrived, arrived, self.place.core).wait()

    def stage0(self):
        p = self.place
        self.copy(0, self.source.at[:, :, 1 - p.c], self.partner, p.core).start()

    def stage1(self):
        p = self.place
        self.wait(0, self.partner)
        self.chip[...] = self.source[:, :, p.c] + self.partner[...]
        self.copy(1, self.chip.at[:, 1 - p.x], self.first, p.side).start()

    def stage2(self):
        p = self.place
        self.wait(1, self.first)
        for k in range(2):
            self.chip[k, p.x] += self.first[k]
        self.copy(2, self.chip.at[1 - p.y, p.x], self.second, p.over).start()

    def stage3(self):
        p = self.place
        self.wait(2, self.second)
        self.chip[p.y, p.x] += self.second[...]
        for k in range(3):
            block = self.chip.at[p.y, p.x, p.ranks[k]]
            self.copy(3, block, self.from_z.at[k], p.planes[k]).start()

    def stage4(self):
        p = self.place
        self.wait(3, self.from_z)
        total = self.chip[p.y, p.x, p.z].astype(F32)
        for k in range(3):
            total = total + self.from_z[k].astype(F32)
        return total


def dma_sems(count):
    return [pltpu.SemaphoreType.DMA((count,)), pltpu.SemaphoreType.DMA((count,))]


def to_planes(place, mine, landing, send, recv, first):
    return [
        pltpu.make_async_remote_copy(
            src_ref=mine,
            dst_ref=landing(k),
            send_sem=send.at[first + k],
            recv_sem=recv.at[first + k],
            device_id=place.planes[k],
            device_id_type=MESH,
        )
        for k in range(3)
    ]


class PlanesLast:
    copies = WideGather.copies + 6

    def __init__(self, place, source, target, send, recv, last):
        view = blocks_of(target.at[place.z])
        self.wide = WideGather(place, view, source.shape[0], send, recv, 0, source, last)

        def copy(index, rank, peer):
            blocks = target.at[rank, :, :, place.c]
            return pltpu.make_async_remote_copy(
                src_ref=blocks,
                dst_ref=blocks,
                send_sem=send.at[WideGather.copies + index],
                recv_sem=recv.at[WideGather.copies + index],
                device_id=peer,
                device_id_type=MESH,
            )

        self.across = [copy(k, place.z, place.planes[k]) for k in range(3)]
        self.over = [copy(3 + k, place.ranks[k], place.core) for k in range(3)]

    def start_across(self):
        self.wide.own.wait()
        for copy in self.across:
            copy.start()

    def start_over(self):
        for arrived, copy in zip(self.across, self.over):
            arrived.wait_recv()
            copy.start()

    def finish(self):
        self.wide.own = None
        self.wide.finish()
        for copy in self.across:
            copy.wait_send()
        for copy in self.over:
            copy.wait()


def first_kernel(
    lengths_ref,
    tokens_ref,
    in_ref,
    vec_ref,
    out_ref,
    up_ref,
    unit_ref,
    hs_ref,
    turned_ref,
    proj_ref,
    scaled_ref,
    scaled_turned_ref,
    attended_ref,
    lse_ref,
    vectors_ref,
    scale_ref,
    in_all,
    out_all,
    up_all,
    unit_all,
    held_ref,
    normed_ref,
    first_ref,
    vext_ref,
    send_in,
    recv_in,
    send_out,
    recv_out,
    send_ff,
    recv_ff,
    local,
):
    step = pl.program_id(0)
    place = Place()
    width = tokens_ref.shape[1]
    count = WideGather.copies
    lanes = (3 * width // 2 + 128, 3 * width // 2)
    across, early, late = [], [], None
    for group in range(2):
        held = held_ref.at[group, :, :, :, :, :, pl.ds(0, lanes[group])]
        first = group * (3 + 2 * count)

        def blocks(planes, held=held):
            return lambda y, x, c, rows: held.at[planes, y, x, c, rows]

        mine = held.at[0, place.y, place.x, place.c]
        across.append(
            to_planes(
                place,
                mine,
                lambda k, held=held: held.at[k + 1, place.y, place.x, place.c],
                send_in,
                recv_in,
                first,
            )
        )
        if group == 0:
            for part, planes in enumerate((pl.ds(0, 1), pl.ds(1, 3))):
                start = first + 3 + part * count
                early.append(WideGather(place, blocks(planes), 32, send_in, recv_in, start))
        else:
            late = WideGather(place, blocks(pl.ds(0, 4)), 32, send_in, recv_in, first + 3)
    orders = (place.z, *place.ranks)
    out = PlanesLast(place, out_ref, out_all, send_out, recv_out, local.at[2])
    up = PairGather(place, up_all, send_ff, recv_ff, 0, up_ref, local.at[3])
    unit = WideGather(
        place, blocks_of(unit_all), 32, send_ff, recv_ff, PairGather.copies, unit_ref, local.at[4]
    )
    keep = [
        pltpu.make_async_copy(
            held_ref.at[group, index, :, :, :, :, pl.ds(0, lanes[1])],
            in_all.at[rank, :, :, :, :, pl.ds(group * lanes[1], lanes[1])],
            local.at[12 + 4 * group + index],
        )
        for group in range(2)
        for index, rank in enumerate(orders)
    ]

    @pl.when(step == 0)
    def _():
        place.greet()
        half = width // 2
        for group in range(2):
            mine = held_ref.at[group, 0, place.y, place.x, place.c]
            own = pl.ds(group * 3 * half, 3 * half)
            fill = pltpu.make_async_copy(
                in_ref.at[:, own], mine.at[:, pl.ds(0, 3 * half)], local.at[6 + group]
            )
            fill.start()
            if group == 0:
                mine[:, 3 * half : 3 * half + 128] = jnp.zeros((32, 128), BF)
                mine[:, 3 * half : 3 * half + 32] = vec_ref[...]
            fill.wait()
            for copy in across[group]:
                copy.start()
            if group == 0:
                early[0].start()
        scale = hs_ref[...].astype(F32)
        for pair in range(width // 128):
            own = slice(pair * 128, (pair + 1) * 128)
            low_lanes = lax.broadcasted_iota(jnp.int32, (1, 128), 1) < 64
            scale_ref[0:1, own] = jnp.where(
                low_lanes, scale[:, 2 * pair : 2 * pair + 1], scale[:, 2 * pair + 1 : 2 * pair + 2]
            )
        for start in range(0, tokens_ref.shape[0], TILE):
            rows = pl.ds(start, TILE)
            normed, _ = row_norm(tokens_ref[rows].astype(F32))
            normed_ref[rows] = normed
        early[0].relay(0)
        for copy in across[0]:
            copy.wait_recv()
        early[1].start()
        early[0].relay(1)
        early[0].relay(2)
        early[1].relay(0)
        early[1].relay(1)
        for copy in across[1]:
            copy.wait_recv()
        late.start()
        early[1].relay(2)
        out.wide.start()
        unit.start()
        for part in early:
            part.finish()
        for z in range(4):
            for y in range(2):
                tile = jnp.zeros((16, 128), F32)
                for x in range(2):
                    for c in range(2):
                        piece = held_ref[
                            0, orders[z], y, x, c, 0:16, 3 * half : 3 * half + 128
                        ].astype(F32)
                        spot = 32 * (2 * x + c)
                        tile = tile + (piece if spot == 0 else pltpu.roll(piece, spot, 1))
                vectors_ref[:, (2 * z + y) * 128 : (2 * z + y + 1) * 128] = tile
        for start in range(0, tokens_ref.shape[0], TILE):
            rows = pl.ds(start, TILE)
            first_ref[rows] = (normed_ref[rows] * vectors_ref[3:4] + vectors_ref[4:5]).astype(BF)

    @pl.when((step >= 2) & (step <= 4))
    def _():
        for stage in range(3):

            @pl.when(step == 2 + stage)
            def _():
                late.relay(stage)
                out.wide.relay(stage)
                unit.relay(stage)

    @pl.when(step == 2)
    def _():
        up.start()

    @pl.when(step == 4)
    def _():
        out.start_across()

    @pl.when(step == 5)
    def _():
        late.finish()
        for copy in keep:
            copy.start()

    for stage, at in enumerate((4, 5, 7, 8)):

        @pl.when(step == at)
        def _():
            up.relay(stage)

    @pl.when(step == 7)
    def _():
        out.start_over()

    @pl.when(step > 0)
    def _():
        pair = step - 1
        columns = pl.ds(pl.multiple_of(pair % 4 * 384, 128), 384)
        weights = jnp.concatenate(
            [held_ref[pair // 4, order, :, :, :, :, columns].reshape(TILE, 384) for order in orders]
        )
        own = pl.ds(pl.multiple_of(pair * 128, 128), 128)
        bias = jnp.concatenate(
            [vectors_ref[0:1, own], jnp.zeros((1, 128), F32), vectors_ref[1:2, own]], axis=1
        )
        project_pair(first_ref, weights, bias, proj_ref)
        attention_pair(
            cross_flag(lengths_ref, tokens_ref),
            *three(proj_ref),
            scale_ref[0:1, own],
            scaled_ref,
            attended_ref,
            lse_ref,
            vext_ref,
        )
        scaled_turned_ref[...] = scaled_ref[...].T

    @pl.when(step == pl.num_programs(0) - 1)
    def _():
        turned_ref[...] = first_ref[...].T
        up.relay(4)
        for copy in (*across[0], *across[1]):
            copy.wait_send()
        for copy in keep:
            copy.wait()
        out.finish()
        unit.finish()
        up.finish()


def first_part(lengths, tokens, in_weight, vec, out_weight, up_weight, unit_rows, head_scale):
    rows, width = tokens.shape
    pairs = width // 128

    def at(step):
        return jnp.maximum(step - 1, 0)

    column = pl.BlockSpec((rows, 128), lambda s: (0, at(s)))
    held = (2, 4, 2, 2, 2, 32, 3 * width // 2 + 128)
    return pl.pallas_call(
        first_kernel,
        grid=(pairs + 1,),
        in_specs=[
            pl.BlockSpec(memory_space=pltpu.SMEM),
            whole((rows, width)),
            ANY,
            whole(vec.shape),
            ANY,
            ANY,
            ANY,
            whole(head_scale.shape),
        ],
        out_specs=[
            whole((width, rows)),
            pl.BlockSpec((1, rows, 384), lambda s: (at(s), 0, 0)),
            column,
            pl.BlockSpec((128, rows), lambda s: (at(s), 0)),
            column,
            pl.BlockSpec((1, 8, rows), lambda s: (at(s), 0, 0)),
            whole((16, width)),
            whole((8, width)),
            ANY,
            ANY,
            ANY,
            ANY,
        ],
        out_shape=[
            jax.ShapeDtypeStruct((width, rows), BF),
            jax.ShapeDtypeStruct((pairs, rows, 384), BF),
            jax.ShapeDtypeStruct((rows, width), BF),
            jax.ShapeDtypeStruct((width, rows), BF),
            jax.ShapeDtypeStruct((rows, width), F32),
            jax.ShapeDtypeStruct((pairs, 8, rows), F32),
            jax.ShapeDtypeStruct((16, width), F32),
            jax.ShapeDtypeStruct((8, width), F32),
            jax.ShapeDtypeStruct((4, 2, 2, 2, 32, 3 * width), BF),
            jax.ShapeDtypeStruct((4, 2, 2, 2, *out_weight.shape), BF),
            jax.ShapeDtypeStruct((2, 2, 2, *up_weight.shape), BF),
            jax.ShapeDtypeStruct((2, 2, 2, *unit_rows.shape), BF),
        ],
        scratch_shapes=[
            pltpu.VMEM(held, BF),
            pltpu.VMEM((rows, width), F32),
            pltpu.VMEM((rows, width), BF),
            pltpu.VMEM((rows, 256), BF),
            *dma_sems(6 + 3 * WideGather.copies),
            *dma_sems(PlanesLast.copies),
            *dma_sems(PairGather.copies + WideGather.copies),
            pltpu.SemaphoreType.DMA((20,)),
        ],
        compiler_params=params(collective_id=0, has_side_effects=True),
        name="first_part",
    )(lengths, tokens, in_weight, vec, out_weight, up_weight, unit_rows, head_scale)


def second_kernel(
    units,
    scaled_ref,
    weight_ref,
    vec_ref,
    tokens_ref,
    up_ref,
    unit_ref,
    down_ref,
    branch_ref,
    middle_ref,
    turned_ref,
    act_ref,
    slope_ref,
    stats_ref,
    down_all,
    feed_ref,
    sums_ref,
    send,
    recv,
    local,
):
    step = pl.program_id(0)
    lead = feed_ref.shape[0] // TILE
    place = Place()
    down = PairGather(place, down_all, send, recv, 0, down_ref, local.at[0])

    @pl.when(step == 0)
    def _():
        place.greet()
        down.start()
        sums_ref[...] = jnp.zeros_like(sums_ref)

    for stage, at in enumerate((4, 6, 8, 10, 11)):

        @pl.when(step == at)
        def _():
            down.relay(stage)

    @pl.when(step < lead)
    def _():
        rows = pl.ds(pl.multiple_of(step * TILE, TILE), TILE)
        feed_ref[rows] = out_proj_rows(
            scaled_ref, weight_ref, vec_ref, tokens_ref, branch_ref, middle_ref
        )

    @pl.when(step >= lead)
    def _():
        up_step(feed_ref, up_ref, unit_ref, act_ref, slope_ref, sums_ref)

    @pl.when(step == pl.num_programs(0) - 1)
    def _():
        up_stats(units, stats_ref, sums_ref)
        turned_ref[...] = feed_ref[...].T
        down.finish()


def second_part(scaled, out_weights, vectors, tokens, up, unit_vec, down_weight):
    rows, width = tokens.shape
    steps = up.shape[0]
    lead = rows // TILE

    def early(step):
        return jnp.minimum(step, lead - 1)

    def late(step):
        return jnp.maximum(step - lead, 0)

    by_row = pl.BlockSpec((TILE, width), lambda s: (early(s), 0))
    block = pl.BlockSpec((1, rows, UNITS), lambda s: (late(s), 0, 0))
    return pl.pallas_call(
        functools.partial(second_kernel, steps * UNITS),
        grid=(lead + steps,),
        in_specs=[
            by_row,
            whole((width, width)),
            whole(vectors.shape),
            by_row,
            pl.BlockSpec((1, width, UNITS), lambda s: (late(s), 0, 0)),
            pl.BlockSpec((1, unit_vec.shape[1], UNITS), lambda s: (late(s), 0, 0)),
            ANY,
        ],
        out_specs=[
            by_row,
            by_row,
            whole((width, rows)),
            block,
            block,
            whole((rows, 128)),
            ANY,
        ],
        out_shape=[
            jax.ShapeDtypeStruct((rows, width), F32),
            jax.ShapeDtypeStruct((rows, width), F32),
            jax.ShapeDtypeStruct((width, rows), BF),
            jax.ShapeDtypeStruct((steps, rows, UNITS), BF),
            jax.ShapeDtypeStruct((steps, rows, UNITS), BF),
            jax.ShapeDtypeStruct((rows, 128), F32),
            jax.ShapeDtypeStruct((2, 2, 2, *down_weight.shape), BF),
        ],
        scratch_shapes=[
            pltpu.VMEM((rows, width), BF),
            pltpu.VMEM((2, rows, 128), F32),
            *dma_sems(PairGather.copies),
            pltpu.SemaphoreType.DMA((1,)),
        ],
        compiler_params=params(collective_id=2, has_side_effects=True),
        name="second_part",
    )(scaled, out_weights, vectors, tokens, up, unit_vec, down_weight)


NORMS_AT, COLUMNS_AT, HEADS_AT, TOKENS_AT, VECTORS_AT = 8, 16, 20, 28, 32
BACK_STEPS = VECTORS_AT + 7
OUT_TILE = 128


class Stream:
    def __init__(self, view, buffers, sems):
        self.view, self.buffers, self.sems = view, buffers, sems

    def copy(self, index):
        slot = index % 2
        return pltpu.make_async_copy(self.view(index), self.buffers.at[slot], self.sems.at[slot])

    def block(self, index):
        return self.buffers.at[index % 2]


def advance(streams, index, count):
    @pl.when(index + 1 < count)
    def _():
        for stream in streams:
            stream.copy(index + 1).start()

    for stream in streams:
        stream.copy(index).wait()


def chunk_at(time):
    chunk = jnp.where(time < 13, time, time - 1)
    chunk = jnp.where(time >= 20, (time + 17) // 2, chunk)
    return chunk, (time >= 0) & ((time < 13) | ((time >= 14) & (time < 20)) | ((time >= 20) & (time < 30) & (time % 2 == 1)))


def back_kernel(
    lengths_ref,
    unit_grad_ref,
    vec_ref,
    hs_ref,
    act_all,
    slope_all,
    e_all,
    stats_all,
    up_all,
    feed_turned_all,
    down_grad_all,
    cot_all,
    middle_all,
    branch_all,
    scaled_turned_all,
    attended_all,
    out_weight_all,
    proj_all,
    lse_all,
    in_weight_all,
    turned_all,
    tokens_all,
    down_out,
    up_out,
    attn_out,
    vec_out,
    tokens_grad_all,
    up_grad_all,
    units_in_ref,
    up_ref,
    stats_ref,
    feed_turned_ref,
    cot_ref,
    norms_in_ref,
    scaled_turned_ref,
    attended_ref,
    out_weight_ref,
    proj_ref,
    lse_ref,
    in_weight_ref,
    turned_ref,
    tokens_ref,
    tokens_grad_ref,
    staged_ref,
    total_ref,
    low_ref,
    out_grad_ref,
    ga_ref,
    grad_middle_ref,
    delta_ref,
    delta_sum_ref,
    sums_ref,
    units_ref,
    dq_ref,
    dk_ref,
    dv_ref,
    chunk_ref,
    stream_sems,
    fetch_sems,
    *scratch,
):
    step = pl.program_id(0)
    place = Place()
    engine = Reduction(place, scratch[:11])
    small = SmallReduction(place, scratch[11:])
    pairs = proj_all.shape[0]

    def rows_of(array, size):
        return lambda i: array.at[pl.ds(pl.multiple_of(i * size, size), size)]

    def columns_of(array, size):
        return lambda i: array.at[:, pl.ds(pl.multiple_of(i * size, size), size)]

    def stream(number, view, buffers):
        return Stream(view, buffers, stream_sems.at[number])

    act, slope, e = (
        stream(k, lambda i, array=array: array.at[i], units_in_ref.at[k])
        for k, array in enumerate((act_all, slope_all, e_all))
    )
    up = stream(3, lambda i: up_all.at[i], up_ref)
    cot = stream(4, rows_of(cot_all, OUT_TILE), cot_ref)
    middle = stream(5, rows_of(middle_all, OUT_TILE), norms_in_ref.at[0])
    branch = stream(6, rows_of(branch_all, OUT_TILE), norms_in_ref.at[1])
    attended = stream(7, columns_of(attended_all, TILE), attended_ref)
    proj = stream(8, lambda i: proj_all.at[i], proj_ref)
    lse = stream(9, lambda i: lse_all.at[i], lse_ref)
    in_weight = stream(10, columns_of(in_weight_all, 384), in_weight_ref)
    tokens = stream(11, rows_of(tokens_all, TILE), tokens_ref)
    put = rows_of(tokens_grad_all, TILE)

    def put_tokens(i):
        return pltpu.make_async_copy(
            tokens_grad_ref.at[i % 2], put(i), stream_sems.at[12, i % 2]
        )

    fetches = [
        pltpu.make_async_copy(source, target, fetch_sems.at[index])
        for index, (source, target) in enumerate(
            (
                (stats_all, stats_ref),
                (feed_turned_all, feed_turned_ref),
                (scaled_turned_all, scaled_turned_ref),
                (out_weight_all, out_weight_ref),
                (turned_all, turned_ref),
            )
        )
    ]

    @pl.when(step == 0)
    def _():
        for item in (act, slope, e, up):
            item.copy(0).start()
        for copy in fetches:
            copy.start()
        for item in (cot, middle, branch, attended, proj, lse, in_weight, tokens):
            item.copy(0).start()
        total_ref[...] = jnp.zeros_like(total_ref)
        sums_ref[...] = jnp.zeros_like(sums_ref)
        units_ref[...] = jnp.zeros_like(units_ref)
        place.greet()

    def store(block):
        view = up_grad_all.at[block // 4, block // 2 % 2, block % 2]
        return pltpu.make_async_copy(staged_ref, view, fetch_sems.at[5])

    @pl.when((step >= 1) & (step <= NORMS_AT))
    def _():
        store(step - 1).wait()


    def stage(number, kind, action, tick):
        chunk, there = chunk_at(tick - number * LAG)
        up = ((chunk >= 8) & (chunk < 14)) | (chunk == 15) | (chunk == 17)
        wanted = {
            "all": there,
            "down": there & (chunk < 8),
            "up": there & up,
            "shared": there & ((chunk < 8) | up),
            "own": there & (chunk >= 8) & ~up,
        }

        @pl.when(wanted[kind])
        def _():
            action(chunk)

    def up_index(chunk):
        return jnp.where(chunk < 14, chunk - 8, (chunk - 3) // 2)

    def pair_index(chunk):
        return jnp.where(chunk < 18, (chunk - 14) // 2, chunk - 16)

    def put_down(chunk):
        for rank, block in engine.stage6(chunk):
            for half in range(2):

                @pl.when(chunk % 2 == half)
                def _():
                    down_out[chunk // 2, rank, :, half * 512 : half * 512 + 512] = block

    def put_up(chunk):
        for rank, block in engine.stage6(chunk):
            up_out[up_index(chunk), rank] = block

    def put_own(chunk):
        attn_out[pair_index(chunk)] = engine.stage4(chunk)

    def take_down(chunk):
        lanes = pl.ds(pl.multiple_of(chunk % 2 * 512, 512), 512)
        engine.stage0(chunk, down_grad_all.at[:, :, :, chunk // 2, :, :, lanes])

    def take_up(chunk):
        engine.stage0(chunk, up_grad_all.at[:, :, :, up_index(chunk)])

    def take_own(chunk):
        engine.stage0(chunk, chunk_ref.at[pair_index(chunk) % 2])

    def reduce_step(tick):
        stage(6, "down", put_down, tick)
        stage(6, "up", put_up, tick)
        stage(5, "shared", engine.stage5, tick)
        stage(4, "shared", lambda chunk: engine.spread(chunk, engine.stage4(chunk)), tick)
        stage(4, "own", put_own, tick)
        stage(3, "all", engine.stage3, tick)
        stage(2, "all", engine.stage2, tick)
        stage(1, "all", engine.stage1, tick)
        stage(0, "down", take_down, tick)
        stage(0, "up", take_up, tick)

    tick = jnp.where(step < NORMS_AT, step, NORMS_AT + (step - NORMS_AT) // 4)
    tick = jnp.where(step < COLUMNS_AT, tick, step - 6)
    tick = jnp.where(step < HEADS_AT, tick, 2 * step - 26)
    tick = jnp.where(step < TOKENS_AT, tick, 30)
    tick = jnp.where(step < VECTORS_AT, tick, step - 1)
    within = (step > NORMS_AT) & (step < COLUMNS_AT) & (step % 4 != 0)
    within = within | ((step > TOKENS_AT) & (step < VECTORS_AT))

    @pl.when(~within)
    def _():
        reduce_step(tick)


    @pl.when(step < NORMS_AT)
    def _():
        advance((act, slope, e, up), step, NORMS_AT)

        @pl.when(step == 0)
        def _():
            fetches[0].wait()

        units_ref[step, 0:1] = up_back_step(
            act.block(step),
            slope.block(step),
            e.block(step),
            stats_ref,
            up.block(step),
            low_ref,
            total_ref,
        )
        units_ref[step, 1:3] = unit_grad_ref[step, 0:2]

        @pl.when(step == 0)
        def _():
            fetches[1].wait()

        for left in range(0, UNITS, TILE):
            columns = slice(left, left + TILE)
            grad = dot_nn(feed_turned_ref[...], low_ref[:, columns]).astype(BF)
            staged_ref[:, :, :, columns] = grad.reshape(8, 4, 32, TILE)
        store(step).start()


    @pl.when((step >= NORMS_AT) & (step < COLUMNS_AT))
    def _():
        block = step - NORMS_AT
        rows = pl.ds(pl.multiple_of(block * OUT_TILE, OUT_TILE), OUT_TILE)
        advance((cot, middle, branch), block, COLUMNS_AT - NORMS_AT)
        grad_middle, low = norms_back(
            total_ref[rows],
            cot.block(block),
            middle.block(block),
            branch.block(block),
            vec_ref,
            sums_ref,
        )
        grad_middle_ref[rows] = grad_middle
        low_ref[rows] = low

    @pl.when((step >= COLUMNS_AT) & (step < HEADS_AT))
    def _():
        block = step - COLUMNS_AT
        columns = pl.ds(pl.multiple_of(block * TILE, TILE), TILE)
        advance((attended,), block, HEADS_AT - COLUMNS_AT)

        @pl.when(block == 0)
        def _():
            fetches[2].wait()
            fetches[3].wait()

        grad_out, delta = heads_back(
            low_ref[...],
            out_weight_ref[columns],
            hs_ref[0:1, columns],
            attended.block(block)[...],
        )
        ga_ref[:, columns] = grad_out
        delta_sum_ref[block, 0:1] = column_sum(delta)
        turned = delta.T
        for head in range(4):
            delta_ref[4 * block + head] = turned[head : head + 1]
        out_grad_ref[:, columns] = dot_nn(scaled_turned_ref[...], low_ref[:, columns]).astype(BF)

    @pl.when(step == HEADS_AT - 1)
    def _():
        total_ref[...] = jnp.zeros_like(total_ref)


    @pl.when((step >= HEADS_AT) & (step < TOKENS_AT))
    def _():
        pair = step - HEADS_AT
        columns = pl.ds(pl.multiple_of(pair * 128, 128), 128)
        advance((proj, lse, in_weight), pair, pairs)

        @pl.when(pair == 0)
        def _():
            fetches[4].wait()

        for part, starts in enumerate(((0, 3 * TILE), (TILE, 2 * TILE))):
            if part == 1:
                reduce_step(tick + 1)
            attention_back_keys(
                starts,
                cross_flag(lengths_ref, total_ref),
                *[proj.block(pair).at[:, pl.ds(index * 128, 128)] for index in range(3)],
                ga_ref.at[:, columns],
                lse.block(pair),
                [delta_ref[2 * pair], delta_ref[2 * pair + 1]],
                dq_ref,
                dk_ref,
                dv_ref,
            )
        query_sum, value_sum = in_back_pair(
            dq_ref,
            dk_ref,
            dv_ref,
            in_weight.block(pair)[...],
            turned_ref,
            out_grad_ref.at[:, columns],
            chunk_ref.at[pair % 2].reshape(8, 4, 32, 512),
            total_ref,
        )
        sums_ref[0:1, columns] = query_sum
        sums_ref[1:2, columns] = value_sum
        stage(0, "own", take_own, tick + 1)

    @pl.when((step >= TOKENS_AT) & (step < TOKENS_AT + 4))
    def _():
        block = step - TOKENS_AT
        rows = pl.ds(pl.multiple_of(block * TILE, TILE), TILE)
        advance((tokens,), block, 4)

        @pl.when(block >= 2)
        def _():
            put_tokens(block - 2).wait()

        result, gain_grad, shift_grad = tokens_back(
            tokens.block(block)[...], total_ref[rows], grad_middle_ref[rows], vec_ref[3:4]
        )
        tokens_grad_ref[block % 2] = result
        put_tokens(block).start()
        sums_ref[3:4] += gain_grad
        sums_ref[4:5] += shift_grad


    @pl.when(step == VECTORS_AT)
    def _():
        for y in range(2):
            for z in range(4):
                own = slice((2 * z + y) * 128, (2 * z + y + 1) * 128)
                for index in range(9):
                    lanes = slice(index % 4 * 128, index % 4 * 128 + 128)
                    row = 6 + index // 4
                    units_ref[8, row : row + 1, lanes] = sums_ref[index : index + 1, own]
                for x in range(2):
                    for c in range(2):
                        unit = 4 * y + 2 * x + c
                        units_ref[8, 0:3] = units_ref[unit, 0:3]
                        if (y, z, x, c) == (0, 0, 0, 0):
                            units_ref[8, 3:4] = sums_ref[9:10, 0:UNITS]
                            units_ref[8, 4:5] = sums_ref[9:10, UNITS : 2 * UNITS]
                            for block in range(4):
                                lanes = slice(block * 128, block * 128 + 128)
                                units_ref[8, 5:6, lanes] = delta_sum_ref[block, 0:1]
                        small.source[y, x, c, z] = units_ref[8].astype(BF)
        small.stage0()

    for index, action in enumerate((small.stage1, small.stage2, small.stage3)):

        @pl.when(step == VECTORS_AT + 1 + index)
        def _():
            action()

    @pl.when(step == VECTORS_AT + 4)
    def _():
        vec_out[...] = small.stage4()
        for block in range(2, 4):
            put_tokens(block).wait()


def back_part(
    lengths,
    act,
    slope,
    e,
    stats,
    up,
    feed_turned,
    unit_grad,
    down_grad,
    cotangent,
    middle,
    branch,
    scaled_turned,
    attended,
    out_weights,
    vectors,
    head_lanes,
    projected,
    lse,
    weights,
    turned,
    tokens,
):
    rows, width = tokens.shape
    pairs = width // 128

    return pl.pallas_call(
        back_kernel,
        grid=(BACK_STEPS,),
        in_specs=[
            pl.BlockSpec(memory_space=pltpu.SMEM),
            whole(unit_grad.shape),
            whole(vectors.shape),
            whole(head_lanes.shape),
            *[ANY] * 18,
        ],
        out_specs=[
            whole((4, 4, 32, 1024)),
            whole((8, 4, 32, 512)),
            whole((8, 32, 512)),
            whole((16, 512)),
            ANY,
            ANY,
        ],
        out_shape=[
            jax.ShapeDtypeStruct((4, 4, 32, 1024), BF),
            jax.ShapeDtypeStruct((8, 4, 32, 512), BF),
            jax.ShapeDtypeStruct((8, 32, 512), F32),
            jax.ShapeDtypeStruct((16, 512), F32),
            jax.ShapeDtypeStruct((rows, width), BF),
            jax.ShapeDtypeStruct((2, 2, 2, 8, 4, 32, UNITS), BF),
        ],
        scratch_shapes=[
            pltpu.VMEM((3, 2, rows, UNITS), BF),
            pltpu.VMEM((2, width, UNITS), BF),
            pltpu.VMEM((rows, 128), F32),
            pltpu.VMEM((width, rows), BF),
            pltpu.VMEM((2, OUT_TILE, width), BF),
            pltpu.VMEM((2, 2, OUT_TILE, width), F32),
            pltpu.VMEM((width, rows), BF),
            pltpu.VMEM((2, rows, TILE), F32),
            pltpu.VMEM((width, width), BF),
            pltpu.VMEM((2, rows, 384), BF),
            pltpu.VMEM((2, 8, rows), F32),
            pltpu.VMEM((2, width, 384), BF),
            pltpu.VMEM((width, rows), BF),
            pltpu.VMEM((2, TILE, width), BF),
            pltpu.VMEM((2, TILE, width), BF),
            pltpu.VMEM((8, 4, 32, UNITS), BF),
            pltpu.VMEM((rows, width), F32),
            pltpu.VMEM((rows, width), BF),
            pltpu.VMEM((width, width), BF),
            pltpu.VMEM((rows, width), BF),
            pltpu.VMEM((rows, width), F32),
            pltpu.VMEM((2 * pairs, 1, rows), F32),
            pltpu.VMEM((4, 8, 128), F32),
            pltpu.VMEM((16, width), F32),
            pltpu.VMEM((9, 16, UNITS), F32),
            pltpu.VMEM((rows, 128), F32),
            pltpu.VMEM((rows, 128), F32),
            pltpu.VMEM((rows, 128), F32),
            pltpu.VMEM((2, 2, 2, 2, 4, 32, 512), BF),
            pltpu.SemaphoreType.DMA((13, 2)),
            pltpu.SemaphoreType.DMA((6,)),
            *Reduction.scratch(),
            *SmallReduction.scratch(),
        ],
        compiler_params=params(collective_id=1, has_side_effects=True),
        name="back_part",
    )(
        lengths,
        unit_grad,
        vectors,
        head_lanes,
        act,
        slope,
        e,
        stats,
        up,
        feed_turned,
        down_grad.reshape(2, 2, 2, 4, 4, 32, width),
        cotangent,
        middle,
        branch,
        scaled_turned,
        attended,
        out_weights,
        projected,
        lse,
        weights,
        turned,
        tokens,
    )


def layer(staged, tokens, cotangent, lengths, attn, up, down, unit_vec, head_scale, down_bias):
    rows, width = tokens.shape
    heads = head_scale.shape[0]
    pairs = width // 128
    if staged:
        in_weight, out_weight, vec_block = attn
        (
            turned,
            projected,
            scaled,
            scaled_turned,
            attended,
            lse,
            vectors,
            head_lanes,
            weights,
            out_weights,
            up,
            unit_vec,
        ) = first_part(
            lengths, tokens, in_weight, vec_block, out_weight, up, unit_vec, head_scale[None, :]
        )
        weights = weights.reshape(width, 3 * width)
        out_weights = out_weights.reshape(width, width)
        up = up.reshape(-1, width, UNITS)
        unit_vec = unit_vec.reshape(-1, unit_vec.shape[-2], UNITS)
        branch, middle, feed_turned, act, slope, stats, down = second_part(
            scaled, out_weights, vectors, tokens, up, unit_vec, down
        )
        down = down.reshape(-1, UNITS, width)
    else:
        weights, out_weights, vectors = attn
        scale = head_scale.astype(F32)
        head_lanes = jnp.repeat(scale, width // heads)[None, :]
        first, projected, scaled, attended, lse = plain_first(
            lengths, tokens, weights, vectors, head_lanes
        )
        branch, middle, feed = out_proj(scaled, out_weights, vectors, tokens)
        act, slope, stats = up_pass(feed, up, unit_vec)
    mixed, down_grad, e, stats, unit_grad = down_pass(
        act, stats, unit_vec, down, cotangent, middle, down_bias[None, :]
    )
    if staged:
        down_total, up_total, shares, vec_shares, tokens_grad, _ = back_part(
            lengths,
            act,
            slope,
            e,
            stats,
            up,
            feed_turned,
            unit_grad,
            down_grad,
            cotangent,
            middle,
            branch,
            scaled_turned,
            attended,
            out_weights,
            vectors,
            head_lanes,
            projected,
            lse,
            weights,
            turned,
            tokens,
        )
        return mixed, tokens_grad, down_total, up_total, shares, vec_shares
    up_grad, up_bias_grad, grad_feed = up_back(
        act, slope, e, stats, up, feed
    )
    grad_middle, ga, out_grad, delta, sums = out_back(
        grad_feed,
        cotangent,
        middle,
        branch,
        scaled,
        attended,
        out_weights,
        vectors,
        head_lanes,
    )
    chunks, proj_bias, tokens_grad, pre_sums = in_back(
        lengths,
        projected,
        ga,
        lse,
        delta.reshape(pairs, 2, rows),
        weights,
        first,
        out_grad,
        tokens,
        vectors[3:4],
        grad_middle,
    )
    scale_grad = jnp.sum(delta, axis=1) / scale
    vec_grads = [
        proj_bias[:, 0].reshape(width),
        proj_bias[:, 1].reshape(width),
        sums[2],
        pre_sums[0],
        pre_sums[1],
        sums[5],
        sums[6],
        sums[7],
        sums[8],
    ]
    unit_grads = [up_bias_grad[:, 0], unit_grad[:, 0], unit_grad[:, 1]]
    return mixed, tokens_grad, chunks, up_grad, down_grad, vec_grads, unit_grads, sums[9], scale_grad


def body(
    axes,
    tokens,
    cotangent,
    lengths,
    in_weight,
    query_bias,
    value_bias,
    out_weight,
    out_bias,
    head_scale,
    pre_gain,
    pre_bias,
    post_gain,
    post_bias,
    feed_gain,
    feed_bias,
    up_weight,
    up_bias,
    mid_gain,
    mid_bias,
    down_weight,
    down_bias,
):
    planes, wide = axes
    every = ("dp", "wide")
    staged = (planes, wide) == (4, 8)
    rows, width = tokens.shape
    units = down_weight.shape[0] * wide
    steps = units // UNITS
    share = in_weight.shape[0]
    columns = [
        query_bias,
        value_bias,
        out_bias,
        pre_gain,
        pre_bias,
        post_gain,
        post_bias,
        feed_gain,
        feed_bias,
    ]
    index = lax.broadcasted_iota(jnp.int32, (32, up_bias.shape[0]), 0)
    unit_rows = jnp.where(index == 0, up_bias[None, :], jnp.zeros((), BF))
    unit_rows = jnp.where(index == 1, mid_gain[None, :], unit_rows)
    unit_rows = jnp.where(index == 2, mid_bias[None, :], unit_rows)
    if staged:
        index = lax.broadcasted_iota(jnp.int32, (32, share), 0)
        vec_block = jnp.zeros((32, share), BF)
        for row, column in enumerate(columns):
            vec_block = jnp.where(index == row, column[None, :], vec_block)
        by_pair = in_weight.reshape(share, 3, width // 128, 128).transpose(0, 2, 1, 3)
        attn = (by_pair.reshape(share, 3 * width), out_weight, vec_block)
        up, unit_vec, down = up_weight, unit_rows, down_weight
    else:
        flat = jnp.concatenate(columns).reshape(len(columns), share)
        attn = (
            lax.all_gather(in_weight, every, axis=0, tiled=True),
            lax.all_gather(out_weight, every, axis=0, tiled=True),
            jnp.pad(
                lax.all_gather(flat, every, axis=1, tiled=True), ((0, 16 - len(columns)), (0, 0))
            ).astype(F32),
        )
        up = lax.all_gather(up_weight, "wide", axis=1, tiled=True)
        up = up.reshape(width, steps, UNITS).transpose(1, 0, 2)
        unit_vec = lax.all_gather(unit_rows, "wide", axis=1, tiled=True)
        unit_vec = unit_vec.reshape(32, steps, UNITS).transpose(1, 0, 2)
        down = lax.all_gather(down_weight, "wide", axis=0, tiled=True)
        down = down.reshape(steps, UNITS, width)
    results = layer(
        staged,
        tokens,
        cotangent,
        lengths,
        attn,
        up,
        down,
        unit_vec,
        head_scale,
        down_bias,
    )
    heads = head_scale.shape[0]
    pairs = width // 128
    if staged:
        mixed, tokens_grad, down_total, up_total, shares, vec_shares = results
        up_total = up_total.astype(F32).reshape(width, UNITS)
        down_total = down_total.astype(F32).reshape(UNITS, width)
        unit_totals = [vec_shares[index] for index in range(3)]
        down_sum = vec_shares[3:5].reshape(width)
        scale_sum = vec_shares[5].reshape(4, 128)[:, :4].reshape(heads) / head_scale.astype(F32)
        offset = share * lax.rem(lax.axis_index("wide"), 128 // share)
        own = vec_shares[6:9].reshape(12, 128)
        own = lax.dynamic_slice(own, (0, offset), (len(columns), share))
        vec_totals = [own[index] for index in range(len(columns))]
        shares = shares.reshape(pairs, share, 512)
        in_total = shares[:, :, :384].reshape(pairs, share, 3, 128)
        in_total = in_total.transpose(1, 2, 0, 3).reshape(share, 3 * width)
        out_total = shares[:, :, 384:].transpose(1, 0, 2).reshape(share, width)
    else:
        (mixed, tokens_grad, chunks, up_grad, down_grad, vec_grads, unit_grads) = results[:7]
        down_sum, scale_sum = results[7:]

        def scatter(value, axis=0, over=every):
            return lax.psum_scatter(value, over, scatter_dimension=axis, tiled=True)

        def both_ways(value, axis):
            part = scatter(value.astype(BF), axis, "wide")
            return lax.psum(part, "dp").astype(F32)

        up_total = both_ways(up_grad.transpose(1, 0, 2).reshape(width, units), 1)
        down_total = both_ways(down_grad.reshape(units, width), 0)
        unit_totals = [
            lax.psum(scatter(item.reshape(units), 0, "wide"), "dp") for item in unit_grads
        ]
        down_sum, scale_sum = lax.psum((down_sum, scale_sum), every)
        vec_totals = [scatter(item) for item in vec_grads]
        natural = chunks.transpose(0, 2, 1, 3, 4).reshape(pairs, width, 512)
        in_total = natural[:, :, :384].reshape(pairs, width, 3, 128)
        in_total = scatter(in_total.transpose(1, 2, 0, 3).reshape(width, 3 * width).astype(F32))
        out_total = scatter(
            natural[:, :, 384:].transpose(1, 0, 2).reshape(width, width).astype(F32)
        )
    return (
        mixed,
        tokens_grad,
        in_total,
        vec_totals[0],
        vec_totals[1],
        out_total,
        vec_totals[2],
        scale_sum,
        vec_totals[3],
        vec_totals[4],
        vec_totals[5],
        vec_totals[6],
        vec_totals[7],
        vec_totals[8],
        up_total,
        unit_totals[0],
        unit_totals[1],
        unit_totals[2],
        down_total,
        down_sum,
    )


def solution(mesh):
    by_all = P(("dp", "wide"))
    rows_all = P(("dp", "wide"), None)
    axes = (mesh.shape["dp"], mesh.shape["wide"])
    return jax.shard_map(
        functools.partial(body, axes),
        mesh=mesh,
        in_specs=(
            rows_all,
            rows_all,
            rows_all,
            rows_all,
            by_all,
            by_all,
            rows_all,
            by_all,
            P(),
            by_all,
            by_all,
            by_all,
            by_all,
            by_all,
            by_all,
            P(None, "wide"),
            P("wide"),
            P("wide"),
            P("wide"),
            P("wide", None),
            P(),
        ),
        out_specs=(
            rows_all,
            rows_all,
            rows_all,
            by_all,
            by_all,
            rows_all,
            by_all,
            P(),
            by_all,
            by_all,
            by_all,
            by_all,
            by_all,
            by_all,
            P(None, "wide"),
            P("wide"),
            P("wide"),
            P("wide"),
            P("wide", None),
            P(),
        ),
        check_vma=False,
    )
```

```python
import functools

import jax
import jax.numpy as jnp
from jax import lax
from jax.experimental import pallas as pl
from jax.experimental.pallas import tpu as pltpu
from jax.sharding import PartitionSpec as P

EPS = 1e-05
ROOT_HALF = 0.7071067811865476
INV_ROOT_TAU = 0.3989422804014327
LOG2E = 1.4426950408889634
MASKED = -1e30
BF = jnp.bfloat16
F32 = jnp.float32
TILE = 256
UNITS = 512
SLIM = 64
MESH = pl.DeviceIdType.MESH
VMEM_LIMIT = 62 * 1024 * 1024
ANY = pl.BlockSpec(memory_space=pl.ANY)


def dot_nn(left, right):
    return lax.dot_general(left, right, (((1,), (0,)), ((), ())), preferred_element_type=F32)


def dot_nt(left, right):
    return lax.dot_general(left, right, (((1,), (1,)), ((), ())), preferred_element_type=F32)


def dot_tn(left, right):
    return lax.dot_general(left, right, (((0,), (0,)), ((), ())), preferred_element_type=F32)


def params(**more):
    return pltpu.CompilerParams(
        dimension_semantics=("arbitrary",), vmem_limit_bytes=VMEM_LIMIT, **more
    )


def whole(shape):
    zeros = (0,) * len(shape)
    return pl.BlockSpec(shape, lambda *_: zeros, pipeline_mode=pl.Buffered(1))


def row_norm(values):
    center = values - jnp.mean(values, axis=-1, keepdims=True)
    inv = lax.rsqrt(jnp.mean(center * center, axis=-1, keepdims=True) + EPS)
    return center * inv, inv


def norm_back(grad, gain, normed, inv):
    scaled = grad * gain
    first = jnp.mean(scaled, axis=-1, keepdims=True)
    cross = jnp.mean(scaled * normed, axis=-1, keepdims=True)
    return inv * (scaled - first - normed * cross)


def column_sum(values):
    return jnp.sum(values, axis=0, keepdims=True)


def lane_fold(values):
    total = values[:, :128]
    for start in range(128, values.shape[1], 128):
        total = total + values[:, start : start + 128]
    return total


def cross_flag(lengths_ref, rows_ref):
    return jnp.where(lengths_ref[0, 0] == rows_ref.shape[0], 0.0, MASKED)


def stacked(value, low_lanes):
    zero = jnp.zeros_like(value)
    return jnp.concatenate(
        [jnp.where(low_lanes, value, zero), jnp.where(low_lanes, zero, value)], axis=0
    )


def attention_pair(cross, q_ref, k_ref, v_ref, scale, scaled_ref, out_ref, lse_ref, vext_ref):
    rows = q_ref.shape[0]
    half = rows // 2
    factor = LOG2E * 64 ** (-0.5)
    low_lanes = lax.broadcasted_iota(jnp.int32, (1, 128), 1) < 64
    below = lax.broadcasted_iota(jnp.int32, (TILE, TILE), 1) <= lax.broadcasted_iota(
        jnp.int32, (TILE, TILE), 0
    )
    vext_ref[:, :128] = v_ref[...]
    vext_ref[:, 128:] = jnp.ones((rows, 128), BF)
    for start in range(0, rows, TILE):
        stop = start + TILE
        both = dot_nt(stacked(q_ref[start:stop], low_lanes), k_ref[:stop])
        peaks, weights = [], []
        for head in range(2):
            raw = both[head * TILE : (head + 1) * TILE]
            parts = []
            if start >= half:
                parts.append((raw[:, :half], cross))
                if start > half:
                    parts.append((raw[:, half:start], None))
            elif start > 0:
                parts.append((raw[:, :start], None))
            parts.append((jnp.where(below, raw[:, start:stop], MASKED), None))
            peak = None
            for piece, shift in parts:
                top = jnp.max(piece, axis=-1, keepdims=True)
                if shift is not None:
                    top = top + shift
                peak = top if peak is None else jnp.maximum(peak, top)
            peaks.append(peak)
            pieces = []
            for piece, shift in parts:
                level = peak if shift is None else peak - shift
                pieces.append(jnp.exp2((piece - level) * factor).astype(BF))
            weights.append(pieces[0] if len(pieces) == 1 else jnp.concatenate(pieces, axis=1))
        both = dot_nn(jnp.concatenate(weights, axis=0), vext_ref[:stop])
        total = jnp.where(low_lanes, both[:TILE, 128:], both[TILE:, 128:])
        peak = jnp.where(low_lanes, peaks[0], peaks[1])
        mixed = jnp.where(low_lanes, both[:TILE, :128], both[TILE:, :128]) / total
        out_ref[start:stop] = mixed
        scaled_ref[start:stop] = (mixed * scale).astype(BF)
        lse = (peak * factor + jnp.log2(total)).T
        lse_ref[0, 0:1, start:stop] = lse[0:1]
        lse_ref[0, 1:2, start:stop] = lse[64:65]


def project_pair(first_ref, weights, bias, proj_ref):
    proj_ref[0] = (dot_nn(first_ref[...], weights) + bias).astype(BF)


def three(proj_ref):
    return [proj_ref.at[0, :, pl.ds(part * 128, 128)] for part in range(3)]


def plain_first_kernel(
    lengths_ref,
    tokens_ref,
    wq_ref,
    wk_ref,
    wv_ref,
    vectors_ref,
    bq_ref,
    bv_ref,
    hs_ref,
    first_ref,
    proj_ref,
    scaled_ref,
    attended_ref,
    lse_ref,
    vext_ref,
):
    @pl.when(pl.program_id(0) == 0)
    def _():
        for start in range(0, tokens_ref.shape[0], TILE):
            rows = pl.ds(start, TILE)
            normed, _ = row_norm(tokens_ref[rows].astype(F32))
            first_ref[rows] = (normed * vectors_ref[3:4] + vectors_ref[4:5]).astype(BF)

    weights = jnp.concatenate([wq_ref[...], wk_ref[...], wv_ref[...]], axis=1)
    bias = jnp.concatenate([bq_ref[0:1], jnp.zeros((1, 128), F32), bv_ref[1:2]], axis=1)
    project_pair(first_ref, weights, bias, proj_ref)
    attention_pair(
        cross_flag(lengths_ref, tokens_ref), *three(proj_ref), hs_ref[...], scaled_ref, attended_ref, lse_ref, vext_ref
    )


def plain_first(lengths, tokens, weights, vectors, head_lanes):
    rows, width = tokens.shape
    pairs = width // 128
    column = pl.BlockSpec((rows, 128), lambda p: (0, p))
    bias = pl.BlockSpec((16, 128), lambda p: (0, p))
    return pl.pallas_call(
        plain_first_kernel,
        grid=(pairs,),
        in_specs=[
            pl.BlockSpec(memory_space=pltpu.SMEM),
            whole((rows, width)),
            pl.BlockSpec((width, 128), lambda p: (0, p)),
            pl.BlockSpec((width, 128), lambda p: (0, pairs + p)),
            pl.BlockSpec((width, 128), lambda p: (0, 2 * pairs + p)),
            whole(vectors.shape),
            bias,
            bias,
            pl.BlockSpec((1, 128), lambda p: (0, p)),
        ],
        out_specs=[
            whole((rows, width)),
            pl.BlockSpec((1, rows, 384), lambda p: (p, 0, 0)),
            column,
            column,
            pl.BlockSpec((1, 8, rows), lambda p: (p, 0, 0)),
        ],
        out_shape=[
            jax.ShapeDtypeStruct((rows, width), BF),
            jax.ShapeDtypeStruct((pairs, rows, 384), BF),
            jax.ShapeDtypeStruct((rows, width), BF),
            jax.ShapeDtypeStruct((rows, width), F32),
            jax.ShapeDtypeStruct((pairs, 8, rows), F32),
        ],
        scratch_shapes=[pltpu.VMEM((rows, 256), BF)],
        compiler_params=params(),
        name="plain_first",
    )(lengths, tokens, weights, weights, weights, vectors, vectors, vectors, head_lanes)


def out_proj_rows(scaled_ref, weight_ref, vec_ref, tokens_ref, branch_ref, middle_ref):
    branch = dot_nn(scaled_ref[...], weight_ref[...]) + vec_ref[2:3]
    normed, _ = row_norm(branch)
    middle = tokens_ref[...].astype(F32) + (normed * vec_ref[5:6] + vec_ref[6:7])
    again, _ = row_norm(middle)
    branch_ref[...] = branch
    middle_ref[...] = middle
    return (again * vec_ref[7:8] + vec_ref[8:9]).astype(BF)


def out_proj_kernel(scaled_ref, weight_ref, vec_ref, tokens_ref, branch_ref, middle_ref, feed_ref):
    feed_ref[...] = out_proj_rows(
        scaled_ref, weight_ref, vec_ref, tokens_ref, branch_ref, middle_ref
    )


def out_proj(scaled, weights, vectors, tokens):
    rows, width = tokens.shape
    by_row = pl.BlockSpec((TILE, width), lambda i: (i, 0))
    return pl.pallas_call(
        out_proj_kernel,
        grid=(rows // TILE,),
        in_specs=[
            by_row,
            whole((width, width)),
            whole(vectors.shape),
            by_row,
        ],
        out_specs=[by_row, by_row, by_row],
        out_shape=[
            jax.ShapeDtypeStruct((rows, width), F32),
            jax.ShapeDtypeStruct((rows, width), F32),
            jax.ShapeDtypeStruct((rows, width), BF),
        ],
        compiler_params=params(),
        name="out_proj",
    )(scaled, weights, vectors, tokens)


def phi_and_slope(value):
    bell = jnp.exp2(value * value * (-0.5 * LOG2E))
    t = 1.0 / (1.0 + (0.3275911 * ROOT_HALF) * jnp.abs(value))
    series = t * (
        0.5 * 0.254829592
        + t
        * (
            0.5 * -0.284496736
            + t * (0.5 * 1.421413741 + t * (0.5 * -1.453152027 + t * (0.5 * 1.061405429)))
        )
    )
    tail = series * bell
    area = jnp.where(value < 0.0, tail, 1.0 - tail)
    return value * area, area + value * bell * INV_ROOT_TAU


def up_step(feed_ref, up_ref, vec_ref, act_ref, slope_ref, sums_ref):
    for left in range(0, UNITS, TILE):
        columns = slice(left, left + TILE)
        pre = dot_nn(feed_ref[...], up_ref[0, :, columns])
        bias = vec_ref[0, 0:1, columns].astype(F32)
        for start in range(0, feed_ref.shape[0], SLIM):
            rows = slice(start, start + SLIM)
            act, slope = phi_and_slope(pre[rows] + bias)
            act_ref[0, rows, columns] = act.astype(BF)
            slope_ref[0, rows, columns] = slope.astype(BF)
            sums_ref[0, rows] += lane_fold(act)
            sums_ref[1, rows] += lane_fold(act * act)


def side_by_side(*columns):
    lane = lax.broadcasted_iota(jnp.int32, (1, 128), 1)
    result = jnp.broadcast_to(columns[-1], (columns[-1].shape[0], 128))
    for index in range(len(columns) - 2, -1, -1):
        result = jnp.where(lane == index, columns[index], result)
    return result


def up_stats(units, stats_ref, sums_ref):
    for start in range(0, stats_ref.shape[0], TILE):
        rows = pl.ds(start, TILE)
        mean = jnp.sum(sums_ref[0, rows], axis=1, keepdims=True) / units
        square = jnp.sum(sums_ref[1, rows], axis=1, keepdims=True) / units
        inv = lax.rsqrt(square - mean * mean + EPS)
        stats_ref[rows] = side_by_side(mean, inv)


def up_kernel(units, feed_ref, up_ref, vec_ref, act_ref, slope_ref, stats_ref, sums_ref):
    step = pl.program_id(0)

    @pl.when(step == 0)
    def _():
        sums_ref[...] = jnp.zeros_like(sums_ref)

    up_step(feed_ref, up_ref, vec_ref, act_ref, slope_ref, sums_ref)

    @pl.when(step == pl.num_programs(0) - 1)
    def _():
        up_stats(units, stats_ref, sums_ref)


def up_pass(feed, up, vec):
    rows, width = feed.shape
    steps = up.shape[0]
    block = pl.BlockSpec((1, rows, UNITS), lambda j: (j, 0, 0))
    return pl.pallas_call(
        functools.partial(up_kernel, steps * UNITS),
        grid=(steps,),
        in_specs=[
            whole((rows, width)),
            pl.BlockSpec((1, width, UNITS), lambda j: (j, 0, 0)),
            pl.BlockSpec((1, vec.shape[1], UNITS), lambda j: (j, 0, 0)),
        ],
        out_specs=[block, block, whole((rows, 128))],
        out_shape=[
            jax.ShapeDtypeStruct((steps, rows, UNITS), BF),
            jax.ShapeDtypeStruct((steps, rows, UNITS), BF),
            jax.ShapeDtypeStruct((rows, 128), F32),
        ],
        scratch_shapes=[pltpu.VMEM((2, rows, 128), F32)],
        compiler_params=params(),
        name="up_pass",
    )(feed, up, vec)


def down_kernel(
    units,
    act_ref,
    stats_ref,
    vec_ref,
    down_ref,
    cot_ref,
    middle_ref,
    shift_ref,
    mixed_ref,
    down_grad_ref,
    e_ref,
    all_stats_ref,
    vec_grad_ref,
    total_ref,
    sums_ref,
    low_ref,
):
    step = pl.program_id(0)
    last = pl.num_programs(0) - 1
    rows_all = cot_ref.shape[0]

    @pl.when(step == 0)
    def _():
        total_ref[...] = jnp.zeros_like(total_ref)
        sums_ref[...] = jnp.zeros_like(sums_ref)

    gain = vec_ref[0, 1:2].astype(F32)
    shift = vec_ref[0, 2:3].astype(F32)
    slims = [slice(start, start + SLIM) for start in range(0, rows_all, SLIM)]

    def normalized(rows, columns):
        value = act_ref[0, rows, columns].astype(F32)
        return (value - stats_ref[rows, 0:1]) * stats_ref[rows, 1:2]

    for rows in slims:
        low_ref[rows] = (normalized(rows, slice(0, UNITS)) * gain + shift).astype(BF)
    for left in range(0, UNITS, TILE):
        columns = slice(left, left + TILE)
        grads = dot_nt(cot_ref[...], down_ref[0, columns])
        gain_grad = jnp.zeros((SLIM, TILE), F32)
        bias_grad = jnp.zeros((SLIM, TILE), F32)
        for rows in slims:
            normed = normalized(rows, columns)
            grad = grads[rows]
            gain_grad = gain_grad + grad * normed
            bias_grad = bias_grad + grad
            e = grad * gain[:, columns]
            e_ref[0, rows, columns] = e.astype(BF)
            sums_ref[0, rows] += lane_fold(e)
            sums_ref[1, rows] += lane_fold(e * normed)
        vec_grad_ref[0, 0:1, columns] = column_sum(gain_grad)
        vec_grad_ref[0, 1:2, columns] = column_sum(bias_grad)
    for left in range(0, total_ref.shape[1], TILE):
        columns = slice(left, left + TILE)
        total_ref[:, columns] += dot_nn(low_ref[...], down_ref[0, :, columns])
    for left in range(0, UNITS, TILE):
        columns = slice(left, left + TILE)
        down_grad_ref[0, columns] = dot_tn(low_ref[:, columns], cot_ref[...]).astype(BF)

    @pl.when(step == last)
    def _():
        for start in range(0, rows_all, TILE):
            rows = pl.ds(start, TILE)
            mixed_ref[rows] = (
                middle_ref[rows] + total_ref[rows] + shift_ref[...].astype(F32)
            ).astype(BF)
            first = jnp.sum(sums_ref[0, rows], axis=1, keepdims=True) / units
            cross = jnp.sum(sums_ref[1, rows], axis=1, keepdims=True) / units
            all_stats_ref[rows] = side_by_side(
                stats_ref[rows, 0:1], stats_ref[rows, 1:2], first, cross
            )


def down_pass(act, stats, vec, down, cotangent, middle, shift):
    rows, width = cotangent.shape
    steps = act.shape[0]
    block = pl.BlockSpec((1, rows, UNITS), lambda j: (j, 0, 0))
    return pl.pallas_call(
        functools.partial(down_kernel, steps * UNITS),
        grid=(steps,),
        in_specs=[
            block,
            whole((rows, 128)),
            pl.BlockSpec((1, vec.shape[1], UNITS), lambda j: (j, 0, 0)),
            pl.BlockSpec((1, UNITS, width), lambda j: (j, 0, 0)),
            whole((rows, width)),
            whole((rows, width)),
            whole((1, width)),
        ],
        out_specs=[
            whole((rows, width)),
            pl.BlockSpec((1, UNITS, width), lambda j: (j, 0, 0)),
            block,
            whole((rows, 128)),
            pl.BlockSpec((1, 8, UNITS), lambda j: (j, 0, 0)),
        ],
        out_shape=[
            jax.ShapeDtypeStruct((rows, width), BF),
            jax.ShapeDtypeStruct((steps, UNITS, width), BF),
            jax.ShapeDtypeStruct((steps, rows, UNITS), BF),
            jax.ShapeDtypeStruct((rows, 128), F32),
            jax.ShapeDtypeStruct((steps, 8, UNITS), F32),
        ],
        scratch_shapes=[
            pltpu.VMEM((rows, width), F32),
            pltpu.VMEM((2, rows, 128), F32),
            pltpu.VMEM((rows, UNITS), BF),
        ],
        compiler_params=params(),
        name="down_pass",
    )(act, stats, vec, down, cotangent, middle, shift)


def up_back_step(act, slope, e, stats_ref, up, low_ref, total_ref):
    bias_grad = jnp.zeros((SLIM, UNITS), F32)
    for start in range(0, total_ref.shape[0], SLIM):
        rows = slice(start, start + SLIM)
        inv = stats_ref[rows, 1:2]
        normed = (act[rows].astype(F32) - stats_ref[rows, 0:1]) * inv
        grad_act = inv * (
            e[rows].astype(F32) - stats_ref[rows, 2:3] - normed * stats_ref[rows, 3:4]
        )
        low = (grad_act * slope[rows].astype(F32)).astype(BF)
        bias_grad = bias_grad + low.astype(F32)
        low_ref[rows, 0:UNITS] = low
    for left in range(0, total_ref.shape[1], TILE):
        columns = slice(left, left + TILE)
        total_ref[:, columns] += dot_nt(low_ref[:, 0:UNITS], up[columns])
    return column_sum(bias_grad)


def up_back_kernel(
    act_ref,
    slope_ref,
    e_ref,
    stats_ref,
    up_ref,
    feed_ref,
    up_grad_ref,
    bias_grad_ref,
    total_ref,
    turned_ref,
    low_ref,
):
    @pl.when(pl.program_id(0) == 0)
    def _():
        total_ref[...] = jnp.zeros_like(total_ref)
        turned_ref[...] = feed_ref[...].T

    bias_grad_ref[0, 0:1] = up_back_step(
        act_ref.at[0],
        slope_ref.at[0],
        e_ref.at[0],
        stats_ref,
        up_ref.at[0],
        low_ref,
        total_ref,
    )
    up_grad_ref[0] = dot_nn(turned_ref[...], low_ref[...]).astype(BF)


def up_back(act, slope, e, stats, up, feed):
    rows, width = feed.shape
    steps = act.shape[0]
    block = pl.BlockSpec((1, rows, UNITS), lambda j: (j, 0, 0))
    narrow = whole((rows, 128))
    return pl.pallas_call(
        up_back_kernel,
        grid=(steps,),
        in_specs=[
            block,
            block,
            block,
            narrow,
            pl.BlockSpec((1, width, UNITS), lambda j: (j, 0, 0)),
            whole((rows, width)),
        ],
        out_specs=[
            pl.BlockSpec((1, width, UNITS), lambda j: (j, 0, 0)),
            pl.BlockSpec((1, 8, UNITS), lambda j: (j, 0, 0)),
            whole((rows, width)),
        ],
        out_shape=[
            jax.ShapeDtypeStruct((steps, width, UNITS), BF),
            jax.ShapeDtypeStruct((steps, 8, UNITS), F32),
            jax.ShapeDtypeStruct((rows, width), F32),
        ],
        scratch_shapes=[pltpu.VMEM((width, rows), BF), pltpu.VMEM((rows, UNITS), BF)],
        compiler_params=params(),
        name="up_back",
    )(act, slope, e, stats, up, feed)


def norms_back(grad_feed, cot_ref, middle_ref, branch_ref, vec_ref, sums_ref):
    normed, inv = row_norm(middle_ref[...])
    cot = cot_ref[...].astype(F32)
    grad_middle = cot + norm_back(grad_feed, vec_ref[7:8], normed, inv)
    sums_ref[7:8] += column_sum(grad_feed * normed)
    sums_ref[8:9] += column_sum(grad_feed)
    sums_ref[9:10] += column_sum(cot)
    normed, inv = row_norm(branch_ref[...])
    low = norm_back(grad_middle, vec_ref[5:6], normed, inv).astype(BF)
    sums_ref[5:6] += column_sum(grad_middle * normed)
    sums_ref[6:7] += column_sum(grad_middle)
    sums_ref[2:3] += column_sum(low.astype(F32))
    return grad_middle, low


def heads_back(low, weights, scale, attended):
    grad_out = (dot_nt(low, weights) * scale).astype(BF)
    product = grad_out.astype(F32) * attended
    high = product.astype(BF)
    rest = (product - high.astype(F32)).astype(BF)
    heads = (
        lax.broadcasted_iota(jnp.int32, (product.shape[1], 128), 0) // 64
        == lax.broadcasted_iota(jnp.int32, (product.shape[1], 128), 1)
    ).astype(BF)
    return grad_out, dot_nn(high, heads) + dot_nn(rest, heads)


def out_back_kernel(
    grad_feed_ref,
    cot_ref,
    middle_ref,
    branch_ref,
    scaled_ref,
    attended_ref,
    weight_ref,
    vec_ref,
    hs_ref,
    grad_middle_ref,
    ga_ref,
    out_grad_ref,
    delta_ref,
    sums_ref,
    total_ref,
):
    step = pl.program_id(0)

    @pl.when(step == 0)
    def _():
        total_ref[...] = jnp.zeros_like(total_ref)
        sums_ref[...] = jnp.zeros_like(sums_ref)

    grad_middle, low = norms_back(
        grad_feed_ref[...], cot_ref, middle_ref, branch_ref, vec_ref, sums_ref
    )
    grad_middle_ref[...] = grad_middle
    ga_ref[...], delta = heads_back(low, weight_ref[...], hs_ref[...], attended_ref[...])
    total_ref[...] += dot_tn(scaled_ref[...], low)
    delta_ref[...] = delta.T[: delta_ref.shape[0]]

    @pl.when(step == pl.num_programs(0) - 1)
    def _():
        out_grad_ref[...] = total_ref[...].astype(BF)


def out_back(
    grad_feed, cotangent, middle, branch, scaled, attended, weights, vectors, head_lanes
):
    rows, width = cotangent.shape
    heads = 2 * width // 128
    by_row = pl.BlockSpec((TILE, width), lambda i: (i, 0))
    return pl.pallas_call(
        out_back_kernel,
        grid=(rows // TILE,),
        in_specs=[
            by_row,
            by_row,
            by_row,
            by_row,
            by_row,
            by_row,
            whole((width, width)),
            whole(vectors.shape),
            whole((1, width)),
        ],
        out_specs=[
            by_row,
            by_row,
            whole((width, width)),
            pl.BlockSpec((heads, TILE), lambda i: (0, i)),
            whole((16, width)),
        ],
        out_shape=[
            jax.ShapeDtypeStruct((rows, width), F32),
            jax.ShapeDtypeStruct((rows, width), BF),
            jax.ShapeDtypeStruct((width, width), BF),
            jax.ShapeDtypeStruct((heads, rows), F32),
            jax.ShapeDtypeStruct((16, width), F32),
        ],
        scratch_shapes=[pltpu.VMEM((width, width), F32)],
        compiler_params=params(),
        name="out_back",
    )(
        grad_feed,
        cotangent,
        middle,
        branch,
        scaled,
        attended,
        weights,
        vectors,
        head_lanes,
    )


def attention_back_keys(
    starts, cross, q_ref, k_ref, v_ref, ga_ref, lse_ref, deltas, dq_ref, dk_ref, dv_ref
):
    rows = q_ref.shape[0]
    half = rows // 2
    factor = LOG2E * 64 ** (-0.5)
    low_lanes = lax.broadcasted_iota(jnp.int32, (1, 128), 1) < 64
    above = lax.broadcasted_iota(jnp.int32, (TILE, TILE), 0) <= lax.broadcasted_iota(
        jnp.int32, (TILE, TILE), 1
    )

    def pick(both):
        return jnp.where(low_lanes, both[:TILE], both[TILE:])

    for start in starts:
        stop = start + TILE
        keys = k_ref[start:stop]
        keys_apart = stacked(keys, low_lanes)
        values_apart = stacked(v_ref[start:stop], low_lanes)
        dk = jnp.zeros((TILE, 128), F32)
        dv = jnp.zeros((TILE, 128), F32)
        for left, right in ((start, half), (half, rows)) if start < half else ((start, rows),):
            raw = dot_nt(keys_apart, q_ref[left:right])
            grad_weights = dot_nt(values_apart, ga_ref[left:right])
            weights, grad_scores = [], []
            for head in range(2):
                mine = slice(head * TILE, (head + 1) * TILE)
                level = lse_ref[head : head + 1, left:right]
                if start < half <= left:
                    level = level - cross
                exponent = raw[mine] * factor - level
                if left == start:
                    first = jnp.where(above, exponent[:, :TILE], MASKED)
                    exponent = (
                        first
                        if right - left == TILE
                        else jnp.concatenate([first, exponent[:, TILE:]], axis=1)
                    )
                weight = jnp.exp2(exponent)
                weights.append(weight.astype(BF))
                delta = deltas[head][:, left:right]
                grad_scores.append((weight * (grad_weights[mine] - delta)).astype(BF))
            dv = dv + pick(dot_nn(jnp.concatenate(weights, axis=0), ga_ref[left:right]))
            dk = dk + pick(dot_nn(jnp.concatenate(grad_scores, axis=0), q_ref[left:right]))
            dq = jnp.where(low_lanes, dot_tn(grad_scores[0], keys), dot_tn(grad_scores[1], keys))
            if start == 0:
                dq_ref[left:right] = dq
            else:
                dq_ref[left:right] += dq
        dk_ref[start:stop] = dk
        dv_ref[start:stop] = dv


def in_back_pair(dq_ref, dk_ref, dv_ref, weights, turned_ref, out_grad_ref, chunk_ref, total_ref):
    factor = 64 ** (-0.5)
    dq = (dq_ref[...] * factor).astype(BF)
    dk = (dk_ref[...] * factor).astype(BF)
    dv = dv_ref[...].astype(BF)
    grads = jnp.concatenate([dq, dk, dv], axis=1)
    shares = dot_nn(turned_ref[...], grads).astype(BF)
    for start in range(0, total_ref.shape[0], TILE):
        part = jnp.concatenate(
            [shares[start : start + TILE], out_grad_ref[start : start + TILE]], axis=1
        )
        chunk_ref[:, start // TILE] = part.reshape(8, 32, 512)
        columns = slice(start, start + TILE)
        total_ref[:, columns] += dot_nt(grads, weights[columns])
    return column_sum(dq.astype(F32)), column_sum(dv.astype(F32))


def tokens_back(tokens, grad, grad_middle, gain):
    normed, inv = row_norm(tokens.astype(F32))
    back = norm_back(grad, gain, normed, inv)
    return (grad_middle + back).astype(BF), column_sum(grad * normed), column_sum(grad)


def in_back_kernel(
    lengths_ref,
    proj_ref,
    ga_ref,
    lse_ref,
    delta_ref,
    wq_ref,
    wk_ref,
    wv_ref,
    first_ref,
    out_grad_ref,
    tokens_ref,
    gain_ref,
    grad_middle_ref,
    chunk_ref,
    bias_ref,
    tokens_grad_ref,
    sums_ref,
    dq_ref,
    dk_ref,
    dv_ref,
    turned_ref,
    total_ref,
):
    step = pl.program_id(0)
    q_ref, k_ref, v_ref = three(proj_ref)
    rows_all = tokens_ref.shape[0]

    @pl.when(step == 0)
    def _():
        turned_ref[...] = first_ref[...].T
        total_ref[...] = jnp.zeros_like(total_ref)

    deltas = [delta_ref[0, head : head + 1] for head in range(2)]
    attention_back_keys(
        range(0, rows_all, TILE),
        cross_flag(lengths_ref, tokens_ref),
        q_ref,
        k_ref,
        v_ref,
        ga_ref,
        lse_ref.at[0],
        deltas,
        dq_ref,
        dk_ref,
        dv_ref,
    )
    weights = jnp.concatenate([wq_ref[...], wk_ref[...], wv_ref[...]], axis=1)
    query_sum, value_sum = in_back_pair(
        dq_ref, dk_ref, dv_ref, weights, turned_ref, out_grad_ref, chunk_ref.at[0], total_ref
    )
    bias_ref[0, 0:1] = query_sum
    bias_ref[0, 1:2] = value_sum

    @pl.when(step == pl.num_programs(0) - 1)
    def _():
        gain_grad = jnp.zeros((1, total_ref.shape[1]), F32)
        shift_grad = jnp.zeros((1, total_ref.shape[1]), F32)
        for start in range(0, rows_all, TILE):
            rows = pl.ds(start, TILE)
            tokens_grad_ref[rows], gain_part, shift_part = tokens_back(
                tokens_ref[rows], total_ref[rows], grad_middle_ref[rows], gain_ref[...]
            )
            gain_grad = gain_grad + gain_part
            shift_grad = shift_grad + shift_part
        sums_ref[0:1] = gain_grad
        sums_ref[1:2] = shift_grad


def in_back(lengths, projected, ga, lse, delta, weights, first, out_grad, tokens, gain, grad_middle):
    rows, width = tokens.shape
    pairs = width // 128
    column = pl.BlockSpec((rows, 128), lambda p: (0, p))
    square = whole((rows, width))
    return pl.pallas_call(
        in_back_kernel,
        grid=(pairs,),
        in_specs=[
            pl.BlockSpec(memory_space=pltpu.SMEM),
            pl.BlockSpec((1, rows, 384), lambda p: (p, 0, 0)),
            column,
            pl.BlockSpec((1, 8, rows), lambda p: (p, 0, 0)),
            pl.BlockSpec((1, 2, rows), lambda p: (p, 0, 0)),
            pl.BlockSpec((width, 128), lambda p: (0, p)),
            pl.BlockSpec((width, 128), lambda p: (0, pairs + p)),
            pl.BlockSpec((width, 128), lambda p: (0, 2 * pairs + p)),
            square,
            column,
            square,
            whole((1, width)),
            square,
        ],
        out_specs=[
            pl.BlockSpec((1, 8, width // TILE, 32, 512), lambda p: (p, 0, 0, 0, 0)),
            pl.BlockSpec((1, 8, 128), lambda p: (p, 0, 0)),
            square,
            whole((8, width)),
        ],
        out_shape=[
            jax.ShapeDtypeStruct((pairs, 8, width // TILE, 32, 512), BF),
            jax.ShapeDtypeStruct((pairs, 8, 128), F32),
            jax.ShapeDtypeStruct((rows, width), BF),
            jax.ShapeDtypeStruct((8, width), F32),
        ],
        scratch_shapes=[
            pltpu.VMEM((rows, 128), F32),
            pltpu.VMEM((rows, 128), F32),
            pltpu.VMEM((rows, 128), F32),
            pltpu.VMEM((width, rows), BF),
            pltpu.VMEM((rows, width), F32),
        ],
        compiler_params=params(),
        name="in_back",
    )(
        lengths,
        projected,
        ga,
        lse,
        delta,
        weights,
        weights,
        weights,
        first,
        out_grad,
        tokens,
        gain,
        grad_middle,
    )


class Place:
    def __init__(self):
        self.z = lax.axis_index("dp")
        wide = lax.axis_index("wide")
        self.y = wide // 4
        self.x = (wide // 2) % 2
        self.c = wide % 2
        self.core = (self.z, wide + 1 - 2 * self.c)
        self.side = (self.z, wide + 2 - 4 * self.x)
        self.over = (self.z, wide + 4 - 8 * self.y)
        self.ranks = (self.z + 1 - 2 * (self.z % 2), (self.z + 2) % 4, 3 - self.z)
        self.planes = tuple((rank, wide) for rank in self.ranks)

    def greet(self, planes=True):
        barrier = pltpu.get_barrier_semaphore()
        peers = (self.core, self.side, self.over) + (self.planes if planes else ())
        for peer in peers:
            pl.semaphore_signal(barrier, inc=1, device_id=peer, device_id_type=MESH)
        pl.semaphore_wait(barrier, len(peers))


class WideGather:
    copies = 10

    def __init__(
        self, place, view, count, send, recv, first, source=None, last=None, offset=0, total=None
    ):
        y, x, c = place.y, place.x, place.c
        here, side, over, far = (y, x, c), (y, 1 - x, c), (1 - y, x, c), (1 - y, 1 - x, c)
        upper, lower = pl.ds(offset, count // 2), pl.ds(offset + count // 2, count // 2)
        both = pl.ds(offset, count)
        everything = both if total is None else pl.ds(0, total)

        def copy(index, slot, part, peer):
            destination = view(*slot, part)
            return pltpu.make_async_remote_copy(
                src_ref=source.at[part] if source is not None and slot is here else destination,
                dst_ref=destination,
                send_sem=send.at[first + index],
                recv_sem=recv.at[first + index],
                device_id=peer,
                device_id_type=MESH,
            )

        self.all = (
            copy(0, here, upper, place.side),
            copy(1, here, lower, place.over),
            copy(2, here, upper, place.over),
            copy(3, here, lower, place.side),
            None if total == 0 else copy(4, here, everything, place.core),
            copy(5, side, upper, place.over),
            copy(6, over, lower, place.side),
            copy(7, side, both, place.core),
            copy(8, over, both, place.core),
            copy(9, far, both, place.core),
        )
        self.own = None
        if source is not None and last is not None:
            self.own = pltpu.make_async_copy(source, view(*here, everything), last)

    def start(self):
        if self.own is not None:
            self.own.start()
        for copy in self.all[:5]:
            if copy is not None:
                copy.start()

    def relay(self, stage):
        waits, starts = (((0, 1), (5, 6)), ((2, 3), (7, 8)), ((5, 6), (9,)))[stage]
        for index in waits:
            self.all[index].wait_recv()
        for index in starts:
            self.all[index].start()

    def finish(self):
        for index in (4, 7, 8, 9):
            if self.all[index] is not None:
                self.all[index].wait_recv()
        for copy in self.all:
            if copy is not None:
                copy.wait_send()
        if self.own is not None:
            self.own.wait()


def blocks_of(target):
    return lambda y, x, c, rows: target.at[y, x, c, rows]


LAG = 2


class Reduction:
    slots = 2 * LAG
    deep = 3 * LAG
    keep = 3 * LAG + 2

    @classmethod
    def scratch(cls):
        n, k = cls.slots, cls.keep
        return [
            pltpu.VMEM((cls.deep, 2, 2, 4, 32, 512), BF),
            pltpu.VMEM((n, 2, 2, 4, 32, 512), BF),
            pltpu.VMEM((n, 2, 2, 4, 16, 512), BF),
            pltpu.VMEM((n, 2, 4, 16, 512), BF),
            pltpu.VMEM((n, 4, 32, 512), BF),
            pltpu.VMEM((n, 3, 32, 512), BF),
            pltpu.VMEM((n, 32, 512), BF),
            pltpu.VMEM((k, 3, 32, 512), BF),
            pltpu.SemaphoreType.DMA((6, k)),
            pltpu.SemaphoreType.DMA((6, k)),
            pltpu.SemaphoreType.DMA((cls.deep,)),
        ]

    def __init__(self, place, refs):
        self.place = place
        (
            self.chip,
            self.partner,
            self.first,
            self.second,
            self.plane,
            self.from_z,
            self.sums,
            self.shared,
            self.send,
            self.recv,
            self.local,
        ) = refs

    def copy(self, index, slot, source, target, peer):
        return pltpu.make_async_remote_copy(
            src_ref=source,
            dst_ref=target,
            send_sem=self.send.at[index, slot],
            recv_sem=self.recv.at[index, slot],
            device_id=peer,
            device_id_type=MESH,
        )

    def wait(self, index, slot, arrived):
        self.copy(index, slot, arrived, arrived, self.place.core).wait()

    def load(self, chunk, source):
        slot = chunk % self.deep
        return pltpu.make_async_copy(source, self.chip.at[slot], self.local.at[slot])

    def stage0(self, chunk, view):
        slot, c = chunk % self.slots, self.place.c
        self.copy(
            0, slot, view.at[:, :, 1 - c], self.partner.at[slot], self.place.core
        ).start()
        self.load(chunk, view.at[:, :, c]).start()

    def stage1(self, chunk):
        p, slot, index = self.place, chunk % self.slots, chunk % self.deep
        partner, chip, target = self.partner.at[slot], self.chip.at[index], self.first.at[slot]
        self.load(chunk, partner).wait()
        self.wait(0, slot, partner)
        chip[...] += partner[...]
        self.copy(1, slot, chip.at[:, 1 - p.x, :, pl.ds(0, 16)], target.at[0], p.side).start()
        self.copy(1, slot, chip.at[1 - p.y, :, :, pl.ds(16, 16)], target.at[1], p.over).start()

    def stage2(self, chunk):
        p, slot, index = self.place, chunk % self.slots, chunk % self.deep
        chip, arrived, target = self.chip.at[index], self.first.at[slot], self.second.at[slot]
        self.wait(1, slot, arrived)
        for k in range(2):
            chip[k, p.x, :, 0:16] += arrived[0, k]
            chip[p.y, k, :, 16:32] += arrived[1, k]
        self.copy(2, slot, chip.at[1 - p.y, p.x, :, pl.ds(0, 16)], target.at[0], p.over).start()
        self.copy(2, slot, chip.at[p.y, 1 - p.x, :, pl.ds(16, 16)], target.at[1], p.side).start()

    def stage3(self, chunk):
        p, slot, index = self.place, chunk % self.slots, chunk % self.deep
        arrived, mine, plane = self.second.at[slot], self.chip.at[index, p.y, p.x], self.plane
        self.wait(2, slot, arrived)
        plane[slot, :, 0:16] = mine[:, 0:16] + arrived[0]
        plane[slot, :, 16:32] = mine[:, 16:32] + arrived[1]
        for k in range(3):
            target = self.from_z.at[slot, k]
            self.copy(3, slot, plane.at[slot, p.ranks[k]], target, p.planes[k]).start()

    def stage4(self, chunk):
        slot = chunk % self.slots
        self.wait(3, slot, self.from_z.at[slot])
        total = self.plane[slot, self.place.z].astype(F32)
        for k in range(3):
            total = total + self.from_z[slot, k].astype(F32)
        return total

    def spread(self, chunk, total):
        slot, place = chunk % self.slots, chunk % self.keep
        self.sums[slot] = total.astype(BF)
        peer = self.place.planes[1]
        self.copy(4, place, self.sums.at[slot], self.shared.at[place, 0], peer).start()

    def stage5(self, chunk):
        slot, place, peer = chunk % self.slots, chunk % self.keep, self.place.planes[0]
        shared = self.shared.at[place]
        self.wait(4, place, shared.at[0])
        self.copy(5, place, self.sums.at[slot], shared.at[1], peer).start()
        self.copy(5, place, shared.at[0], shared.at[2], peer).start()

    def stage6(self, chunk):
        slot, place, ranks = chunk % self.slots, chunk % self.keep, self.place.ranks
        self.wait(5, place, self.shared.at[place, pl.ds(1, 2)])
        return [
            (self.place.z, self.sums[slot]),
            (ranks[1], self.shared[place, 0]),
            (ranks[0], self.shared[place, 1]),
            (ranks[2], self.shared[place, 2]),
        ]


class SmallReduction:
    @staticmethod
    def scratch():
        return [
            pltpu.VMEM((2, 2, 2, 4, 16, 512), BF),
            pltpu.VMEM((2, 2, 4, 16, 512), BF),
            pltpu.VMEM((2, 2, 4, 16, 512), BF),
            pltpu.VMEM((2, 4, 16, 512), BF),
            pltpu.VMEM((4, 16, 512), BF),
            pltpu.VMEM((3, 16, 512), BF),
            pltpu.SemaphoreType.DMA((4,)),
            pltpu.SemaphoreType.DMA((4,)),
        ]

    def __init__(self, place, refs):
        self.place = place
        self.source, self.chip, self.partner, self.first, self.second, self.from_z = refs[:6]
        self.send, self.recv = refs[6:]

    def copy(self, index, source, target, peer):
        return pltpu.make_async_remote_copy(
            src_ref=source,
            dst_ref=target,
            send_sem=self.send.at[index],
            recv_sem=self.recv.at[index],
            device_id=peer,
            device_id_type=MESH,
        )

    def wait(self, index, arrived):
        self.copy(index, arrived, arrived, self.place.core).wait()

    def stage0(self):
        p = self.place
        self.copy(0, self.source.at[:, :, 1 - p.c], self.partner, p.core).start()

    def stage1(self):
        p = self.place
        self.wait(0, self.partner)
        self.chip[...] = self.source[:, :, p.c] + self.partner[...]
        self.copy(1, self.chip.at[:, 1 - p.x], self.first, p.side).start()

    def stage2(self):
        p = self.place
        self.wait(1, self.first)
        for k in range(2):
            self.chip[k, p.x] += self.first[k]
        self.copy(2, self.chip.at[1 - p.y, p.x], self.second, p.over).start()

    def stage3(self):
        p = self.place
        self.wait(2, self.second)
        self.chip[p.y, p.x] += self.second[...]
        for k in range(3):
            block = self.chip.at[p.y, p.x, p.ranks[k]]
            self.copy(3, block, self.from_z.at[k], p.planes[k]).start()

    def stage4(self):
        p = self.place
        self.wait(3, self.from_z)
        total = self.chip[p.y, p.x, p.z].astype(F32)
        for k in range(3):
            total = total + self.from_z[k].astype(F32)
        return total


def dma_sems(count):
    return [pltpu.SemaphoreType.DMA((count,)), pltpu.SemaphoreType.DMA((count,))]


def to_planes(place, mine, landing, send, recv, first):
    return [
        pltpu.make_async_remote_copy(
            src_ref=mine,
            dst_ref=landing(k),
            send_sem=send.at[first + k],
            recv_sem=recv.at[first + k],
            device_id=place.planes[k],
            device_id_type=MESH,
        )
        for k in range(3)
    ]


class PlanesLast:
    copies = WideGather.copies + 6

    def __init__(self, place, source, target, send, recv, last):
        view = blocks_of(target.at[place.z])
        self.wide = WideGather(place, view, source.shape[0], send, recv, 0, source, last)

        def copy(index, rank, peer):
            blocks = target.at[rank, :, :, place.c]
            return pltpu.make_async_remote_copy(
                src_ref=blocks,
                dst_ref=blocks,
                send_sem=send.at[WideGather.copies + index],
                recv_sem=recv.at[WideGather.copies + index],
                device_id=peer,
                device_id_type=MESH,
            )

        self.across = [copy(k, place.z, place.planes[k]) for k in range(3)]
        self.over = [copy(3 + k, place.ranks[k], place.core) for k in range(3)]

    def start_across(self):
        self.wide.own.wait()
        for copy in self.across:
            copy.start()

    def start_over(self):
        for arrived, copy in zip(self.across, self.over):
            arrived.wait_recv()
            copy.start()

    def finish(self):
        self.wide.own = None
        self.wide.finish()
        for copy in self.across:
            copy.wait_send()
        for copy in self.over:
            copy.wait()


def first_kernel(
    lengths_ref,
    tokens_ref,
    in_ref,
    vec_ref,
    out_ref,
    up_ref,
    unit_ref,
    hs_ref,
    turned_ref,
    proj_ref,
    scaled_ref,
    scaled_turned_ref,
    attended_ref,
    lse_ref,
    vectors_ref,
    scale_ref,
    in_all,
    out_all,
    up_all,
    unit_all,
    held_ref,
    normed_ref,
    first_ref,
    vext_ref,
    send_in,
    recv_in,
    send_out,
    recv_out,
    send_ff,
    recv_ff,
    local,
):
    step = pl.program_id(0)
    place = Place()
    width = tokens_ref.shape[1]
    count = WideGather.copies
    lanes = (3 * width // 2 + 128, 3 * width // 2)
    across, early, late = [], [], None
    for group in range(2):
        held = held_ref.at[group, :, :, :, :, :, pl.ds(0, lanes[group])]
        first = group * (3 + 2 * count)

        def blocks(planes, held=held):
            return lambda y, x, c, rows: held.at[planes, y, x, c, rows]

        mine = held.at[0, place.y, place.x, place.c]
        across.append(
            to_planes(
                place,
                mine,
                lambda k, held=held: held.at[k + 1, place.y, place.x, place.c],
                send_in,
                recv_in,
                first,
            )
        )
        if group == 0:
            for part, planes in enumerate((pl.ds(0, 1), pl.ds(1, 3))):
                start = first + 3 + part * count
                early.append(WideGather(place, blocks(planes), 32, send_in, recv_in, start))
        else:
            late = WideGather(place, blocks(pl.ds(0, 4)), 32, send_in, recv_in, first + 3)
    orders = (place.z, *place.ranks)
    out = PlanesLast(place, out_ref, out_all, send_out, recv_out, local.at[2])
    half_rows = width // 2
    ups = [
        WideGather(
            place,
            blocks_of(up_all),
            half_rows,
            send_ff,
            recv_ff,
            (1 + part) * count,
            up_ref,
            None,
            part * half_rows,
        )
        for part in range(2)
    ]
    keep_up = pltpu.make_async_copy(
        up_ref, up_all.at[place.y, place.x, place.c], local.at[3]
    )
    unit = WideGather(
        place, blocks_of(unit_all), 32, send_ff, recv_ff, 0, unit_ref, local.at[4]
    )
    keep = [
        pltpu.make_async_copy(
            held_ref.at[group, index, :, :, :, :, pl.ds(0, lanes[1])],
            in_all.at[rank, :, :, :, :, pl.ds(group * lanes[1], lanes[1])],
            local.at[12 + 4 * group + index],
        )
        for group in range(2)
        for index, rank in enumerate(orders)
    ]

    @pl.when(step == 0)
    def _():
        place.greet()
        half = width // 2
        for group in range(2):
            mine = held_ref.at[group, 0, place.y, place.x, place.c]
            fills = []
            for pair in range(4):
                for part in range(3):
                    column = part * width + (4 * group + pair) * 128
                    fills.append(
                        pltpu.make_async_copy(
                            in_ref.at[:, pl.ds(column, 128)],
                            mine.at[:, pl.ds(pair * 384 + part * 128, 128)],
                            local.at[20 + group * 12 + pair * 3 + part],
                        )
                    )
            for copy in fills:
                copy.start()
            if group == 0:
                mine[:, 3 * half : 3 * half + 128] = jnp.zeros((32, 128), BF)
                mine[:, 3 * half : 3 * half + 32] = vec_ref[...]
            for copy in fills:
                copy.wait()
            for copy in across[group]:
                copy.start()
            if group == 0:
                early[0].start()
        keep_up.start()
        ups[0].start()
        scale = hs_ref[...].astype(F32)
        for pair in range(width // 128):
            own = slice(pair * 128, (pair + 1) * 128)
            low_lanes = lax.broadcasted_iota(jnp.int32, (1, 128), 1) < 64
            scale_ref[0:1, own] = jnp.where(
                low_lanes, scale[:, 2 * pair : 2 * pair + 1], scale[:, 2 * pair + 1 : 2 * pair + 2]
            )
        for start in range(0, tokens_ref.shape[0], TILE):
            rows = pl.ds(start, TILE)
            normed, _ = row_norm(tokens_ref[rows].astype(F32))
            normed_ref[rows] = normed
        early[0].relay(0)
        for copy in across[0]:
            copy.wait_recv()
        early[1].start()
        early[0].relay(1)
        early[0].relay(2)
        early[1].relay(0)
        early[1].relay(1)
        for copy in across[1]:
            copy.wait_recv()
        late.start()
        early[1].relay(2)
        out.wide.start()
        unit.start()
        for part in early:
            part.finish()
        for z in range(4):
            for y in range(2):
                tile = jnp.zeros((16, 128), F32)
                for x in range(2):
                    for c in range(2):
                        piece = held_ref[
                            0, orders[z], y, x, c, 0:16, 3 * half : 3 * half + 128
                        ].astype(F32)
                        spot = 32 * (2 * x + c)
                        tile = tile + (piece if spot == 0 else pltpu.roll(piece, spot, 1))
                vectors_ref[:, (2 * z + y) * 128 : (2 * z + y + 1) * 128] = tile
        for start in range(0, tokens_ref.shape[0], TILE):
            rows = pl.ds(start, TILE)
            first_ref[rows] = (normed_ref[rows] * vectors_ref[3:4] + vectors_ref[4:5]).astype(BF)

    @pl.when((step >= 2) & (step <= 4))
    def _():
        for stage in range(3):

            @pl.when(step == 2 + stage)
            def _():
                late.relay(stage)
                out.wide.relay(stage)
                unit.relay(stage)

    @pl.when(step == 2)
    def _():
        ups[1].start()

    @pl.when(step == 4)
    def _():
        out.start_across()

    @pl.when(step == 5)
    def _():
        late.finish()
        for copy in keep:
            copy.start()

    for part, steps in enumerate(((1, 2, 3), (4, 6, 8))):
        for stage, at in enumerate(steps):

            @pl.when(step == at)
            def _():
                ups[part].relay(stage)

    @pl.when(step == 7)
    def _():
        out.start_over()

    @pl.when(step > 0)
    def _():
        pair = step - 1
        columns = pl.ds(pl.multiple_of(pair % 4 * 384, 128), 384)
        weights = jnp.concatenate(
            [held_ref[pair // 4, order, :, :, :, :, columns].reshape(TILE, 384) for order in orders]
        )
        own = pl.ds(pl.multiple_of(pair * 128, 128), 128)
        bias = jnp.concatenate(
            [vectors_ref[0:1, own], jnp.zeros((1, 128), F32), vectors_ref[1:2, own]], axis=1
        )
        project_pair(first_ref, weights, bias, proj_ref)
        attention_pair(
            cross_flag(lengths_ref, tokens_ref),
            *three(proj_ref),
            scale_ref[0:1, own],
            scaled_ref,
            attended_ref,
            lse_ref,
            vext_ref,
        )
        scaled_turned_ref[...] = scaled_ref[...].T

    @pl.when(step == pl.num_programs(0) - 1)
    def _():
        turned_ref[...] = first_ref[...].T
        for copy in (*across[0], *across[1]):
            copy.wait_send()
        for copy in keep:
            copy.wait()
        out.finish()
        unit.finish()
        keep_up.wait()
        for part in ups:
            part.finish()


def first_part(lengths, tokens, in_weight, vec, out_weight, up_weight, unit_rows, head_scale):
    rows, width = tokens.shape
    pairs = width // 128

    def at(step):
        return jnp.maximum(step - 1, 0)

    column = pl.BlockSpec((rows, 128), lambda s: (0, at(s)))
    held = (2, 4, 2, 2, 2, 32, 3 * width // 2 + 128)
    return pl.pallas_call(
        first_kernel,
        grid=(pairs + 1,),
        in_specs=[
            pl.BlockSpec(memory_space=pltpu.SMEM),
            whole((rows, width)),
            ANY,
            whole(vec.shape),
            ANY,
            ANY,
            ANY,
            whole(head_scale.shape),
        ],
        out_specs=[
            whole((width, rows)),
            pl.BlockSpec((1, rows, 384), lambda s: (at(s), 0, 0)),
            column,
            pl.BlockSpec((128, rows), lambda s: (at(s), 0)),
            column,
            pl.BlockSpec((1, 8, rows), lambda s: (at(s), 0, 0)),
            whole((16, width)),
            whole((8, width)),
            ANY,
            ANY,
            ANY,
            ANY,
        ],
        out_shape=[
            jax.ShapeDtypeStruct((width, rows), BF),
            jax.ShapeDtypeStruct((pairs, rows, 384), BF),
            jax.ShapeDtypeStruct((rows, width), BF),
            jax.ShapeDtypeStruct((width, rows), BF),
            jax.ShapeDtypeStruct((rows, width), F32),
            jax.ShapeDtypeStruct((pairs, 8, rows), F32),
            jax.ShapeDtypeStruct((16, width), F32),
            jax.ShapeDtypeStruct((8, width), F32),
            jax.ShapeDtypeStruct((4, 2, 2, 2, 32, 3 * width), BF),
            jax.ShapeDtypeStruct((4, 2, 2, 2, *out_weight.shape), BF),
            jax.ShapeDtypeStruct((2, 2, 2, *up_weight.shape), BF),
            jax.ShapeDtypeStruct((2, 2, 2, *unit_rows.shape), BF),
        ],
        scratch_shapes=[
            pltpu.VMEM(held, BF),
            pltpu.VMEM((rows, width), F32),
            pltpu.VMEM((rows, width), BF),
            pltpu.VMEM((rows, 256), BF),
            *dma_sems(6 + 3 * WideGather.copies),
            *dma_sems(PlanesLast.copies),
            *dma_sems(3 * WideGather.copies),
            pltpu.SemaphoreType.DMA((44,)),
        ],
        compiler_params=params(collective_id=0, has_side_effects=True),
        name="first_part",
    )(lengths, tokens, in_weight, vec, out_weight, up_weight, unit_rows, head_scale)


def second_kernel(
    units,
    scaled_ref,
    weight_ref,
    vec_ref,
    tokens_ref,
    up_ref,
    unit_ref,
    down_ref,
    branch_ref,
    middle_ref,
    turned_ref,
    act_ref,
    slope_ref,
    stats_ref,
    down_all,
    feed_ref,
    sums_ref,
    send,
    recv,
    local,
):
    step = pl.program_id(0)
    lead = feed_ref.shape[0] // TILE
    place = Place()
    down = WideGather(
        place, blocks_of(down_all), UNITS, send, recv, 0, down_ref, local.at[0]
    )

    @pl.when(step == 0)
    def _():
        place.greet()
        down.start()
        sums_ref[...] = jnp.zeros_like(sums_ref)

    for stage, at in enumerate((4, 8, 11)):

        @pl.when(step == at)
        def _():
            down.relay(stage)

    @pl.when(step < lead)
    def _():
        rows = pl.ds(pl.multiple_of(step * TILE, TILE), TILE)
        feed_ref[rows] = out_proj_rows(
            scaled_ref, weight_ref, vec_ref, tokens_ref, branch_ref, middle_ref
        )

    @pl.when(step >= lead)
    def _():
        up_step(feed_ref, up_ref, unit_ref, act_ref, slope_ref, sums_ref)

    @pl.when(step == pl.num_programs(0) - 1)
    def _():
        up_stats(units, stats_ref, sums_ref)
        turned_ref[...] = feed_ref[...].T
        down.finish()


def second_part(scaled, out_weights, vectors, tokens, up, unit_vec, down_weight):
    rows, width = tokens.shape
    steps = up.shape[0]
    lead = rows // TILE

    def early(step):
        return jnp.minimum(step, lead - 1)

    def late(step):
        return jnp.maximum(step - lead, 0)

    by_row = pl.BlockSpec((TILE, width), lambda s: (early(s), 0))
    block = pl.BlockSpec((1, rows, UNITS), lambda s: (late(s), 0, 0))
    return pl.pallas_call(
        functools.partial(second_kernel, steps * UNITS),
        grid=(lead + steps,),
        in_specs=[
            by_row,
            whole((width, width)),
            whole(vectors.shape),
            by_row,
            pl.BlockSpec((1, width, UNITS), lambda s: (late(s), 0, 0)),
            pl.BlockSpec((1, unit_vec.shape[1], UNITS), lambda s: (late(s), 0, 0)),
            ANY,
        ],
        out_specs=[
            by_row,
            by_row,
            whole((width, rows)),
            block,
            block,
            whole((rows, 128)),
            ANY,
        ],
        out_shape=[
            jax.ShapeDtypeStruct((rows, width), F32),
            jax.ShapeDtypeStruct((rows, width), F32),
            jax.ShapeDtypeStruct((width, rows), BF),
            jax.ShapeDtypeStruct((steps, rows, UNITS), BF),
            jax.ShapeDtypeStruct((steps, rows, UNITS), BF),
            jax.ShapeDtypeStruct((rows, 128), F32),
            jax.ShapeDtypeStruct((2, 2, 2, *down_weight.shape), BF),
        ],
        scratch_shapes=[
            pltpu.VMEM((rows, width), BF),
            pltpu.VMEM((2, rows, 128), F32),
            *dma_sems(WideGather.copies),
            pltpu.SemaphoreType.DMA((1,)),
        ],
        compiler_params=params(collective_id=2, has_side_effects=True),
        name="second_part",
    )(scaled, out_weights, vectors, tokens, up, unit_vec, down_weight)


NORMS_AT, COLUMNS_AT, HEADS_AT, TOKENS_AT, VECTORS_AT = 8, 16, 20, 28, 32
BACK_STEPS = VECTORS_AT + 7
OUT_TILE = 128


class Stream:
    def __init__(self, view, buffers, sems):
        self.view, self.buffers, self.sems = view, buffers, sems

    def copy(self, index):
        slot = index % 2
        return pltpu.make_async_copy(self.view(index), self.buffers.at[slot], self.sems.at[slot])

    def block(self, index):
        return self.buffers.at[index % 2]


def advance(streams, index, count):
    @pl.when(index + 1 < count)
    def _():
        for stream in streams:
            stream.copy(index + 1).start()

    for stream in streams:
        stream.copy(index).wait()


def chunk_at(time):
    chunk = jnp.where(time < 13, time, time - 1)
    chunk = jnp.where(time >= 20, (time + 17) // 2, chunk)
    return chunk, (time >= 0) & ((time < 13) | ((time >= 14) & (time < 20)) | ((time >= 20) & (time < 30) & (time % 2 == 1)))


def back_kernel(
    lengths_ref,
    unit_grad_ref,
    vec_ref,
    hs_ref,
    act_all,
    slope_all,
    e_all,
    stats_all,
    up_all,
    feed_turned_all,
    down_grad_all,
    cot_all,
    middle_all,
    branch_all,
    scaled_turned_all,
    attended_all,
    out_weight_all,
    proj_all,
    lse_all,
    in_weight_all,
    turned_all,
    tokens_all,
    down_out,
    up_out,
    in_out,
    out_out,
    vec_out,
    tokens_grad_all,
    up_grad_all,
    units_in_ref,
    up_ref,
    stats_ref,
    feed_turned_ref,
    cot_ref,
    norms_in_ref,
    scaled_turned_ref,
    attended_ref,
    out_weight_ref,
    proj_ref,
    lse_ref,
    in_weight_ref,
    turned_ref,
    tokens_ref,
    tokens_grad_ref,
    staged_ref,
    total_ref,
    low_ref,
    out_grad_ref,
    ga_ref,
    grad_middle_ref,
    delta_ref,
    delta_sum_ref,
    sums_ref,
    units_ref,
    dq_ref,
    dk_ref,
    dv_ref,
    chunk_ref,
    stream_sems,
    fetch_sems,
    *scratch,
):
    step = pl.program_id(0)
    place = Place()
    engine = Reduction(place, scratch[:11])
    small = SmallReduction(place, scratch[11:])
    pairs = proj_all.shape[0]

    def rows_of(array, size):
        return lambda i: array.at[pl.ds(pl.multiple_of(i * size, size), size)]

    def columns_of(array, size):
        return lambda i: array.at[:, pl.ds(pl.multiple_of(i * size, size), size)]

    def stream(number, view, buffers):
        return Stream(view, buffers, stream_sems.at[number])

    act, slope, e = (
        stream(k, lambda i, array=array: array.at[i], units_in_ref.at[k])
        for k, array in enumerate((act_all, slope_all, e_all))
    )
    up = stream(3, lambda i: up_all.at[i], up_ref)
    cot = stream(4, rows_of(cot_all, OUT_TILE), cot_ref)
    middle = stream(5, rows_of(middle_all, OUT_TILE), norms_in_ref.at[0])
    branch = stream(6, rows_of(branch_all, OUT_TILE), norms_in_ref.at[1])
    attended = stream(7, columns_of(attended_all, TILE), attended_ref)
    proj = stream(8, lambda i: proj_all.at[i], proj_ref)
    lse = stream(9, lambda i: lse_all.at[i], lse_ref)
    in_weight = stream(10, columns_of(in_weight_all, 384), in_weight_ref)
    tokens = stream(11, rows_of(tokens_all, TILE), tokens_ref)
    put = rows_of(tokens_grad_all, TILE)

    def put_tokens(i):
        return pltpu.make_async_copy(
            tokens_grad_ref.at[i % 2], put(i), stream_sems.at[12, i % 2]
        )

    fetches = [
        pltpu.make_async_copy(source, target, fetch_sems.at[index])
        for index, (source, target) in enumerate(
            (
                (stats_all, stats_ref),
                (feed_turned_all, feed_turned_ref),
                (scaled_turned_all, scaled_turned_ref),
                (out_weight_all, out_weight_ref),
                (turned_all, turned_ref),
            )
        )
    ]

    @pl.when(step == 0)
    def _():
        for item in (act, slope, e, up):
            item.copy(0).start()
        for copy in fetches:
            copy.start()
        for item in (cot, middle, branch, attended, proj, lse, in_weight, tokens):
            item.copy(0).start()
        total_ref[...] = jnp.zeros_like(total_ref)
        sums_ref[...] = jnp.zeros_like(sums_ref)
        units_ref[...] = jnp.zeros_like(units_ref)
        place.greet()

    def store(block):
        view = up_grad_all.at[block // 4, block // 2 % 2, block % 2]
        return pltpu.make_async_copy(staged_ref, view, fetch_sems.at[5])

    @pl.when((step >= 1) & (step <= NORMS_AT))
    def _():
        store(step - 1).wait()


    def stage(number, kind, action, tick):
        chunk, there = chunk_at(tick - number * LAG)
        up = ((chunk >= 8) & (chunk < 14)) | (chunk == 15) | (chunk == 17)
        wanted = {
            "all": there,
            "down": there & (chunk < 8),
            "up": there & up,
            "shared": there & ((chunk < 8) | up),
            "own": there & (chunk >= 8) & ~up,
        }

        @pl.when(wanted[kind])
        def _():
            action(chunk)

    def up_index(chunk):
        return jnp.where(chunk < 14, chunk - 8, (chunk - 3) // 2)

    def pair_index(chunk):
        return jnp.where(chunk < 18, (chunk - 14) // 2, chunk - 16)

    def put_down(chunk):
        for rank, block in engine.stage6(chunk):
            for half in range(2):

                @pl.when(chunk % 2 == half)
                def _():
                    down_out[chunk // 2, rank, :, half * 512 : half * 512 + 512] = block

    def put_up(chunk):
        for rank, block in engine.stage6(chunk):
            up_out[up_index(chunk), rank] = block

    def put_own(chunk):
        total = engine.stage4(chunk)
        first = pair_index(chunk) * 128
        for part in range(3):
            lanes = pl.ds(pl.multiple_of(part * 1024 + first, 128), 128)
            in_out[:, lanes] = total[:, part * 128 : part * 128 + 128]
        out_out[:, pl.ds(pl.multiple_of(first, 128), 128)] = total[:, 384:512]

    def take_down(chunk):
        lanes = pl.ds(pl.multiple_of(chunk % 2 * 512, 512), 512)
        engine.stage0(chunk, down_grad_all.at[:, :, :, chunk // 2, :, :, lanes])

    def take_up(chunk):
        engine.stage0(chunk, up_grad_all.at[:, :, :, up_index(chunk)])

    def take_own(chunk):
        engine.stage0(chunk, chunk_ref.at[pair_index(chunk) % 2])

    def reduce_step(tick):
        stage(6, "down", put_down, tick)
        stage(6, "up", put_up, tick)
        stage(5, "shared", engine.stage5, tick)
        stage(4, "shared", lambda chunk: engine.spread(chunk, engine.stage4(chunk)), tick)
        stage(4, "own", put_own, tick)
        stage(3, "all", engine.stage3, tick)
        stage(2, "all", engine.stage2, tick)
        stage(1, "all", engine.stage1, tick)
        stage(0, "down", take_down, tick)
        stage(0, "up", take_up, tick)

    tick = jnp.where(step < NORMS_AT, step, NORMS_AT + (step - NORMS_AT) // 4)
    tick = jnp.where(step < COLUMNS_AT, tick, step - 6)
    tick = jnp.where(step < HEADS_AT, tick, 2 * step - 26)
    tick = jnp.where(step < TOKENS_AT, tick, 30)
    tick = jnp.where(step < VECTORS_AT, tick, step - 1)
    within = (step > NORMS_AT) & (step < COLUMNS_AT) & (step % 4 != 0)
    within = within | ((step > TOKENS_AT) & (step < VECTORS_AT))

    @pl.when(~within)
    def _():
        reduce_step(tick)


    @pl.when(step < NORMS_AT)
    def _():
        advance((act, slope, e, up), step, NORMS_AT)

        @pl.when(step == 0)
        def _():
            fetches[0].wait()

        units_ref[step, 0:1] = up_back_step(
            act.block(step),
            slope.block(step),
            e.block(step),
            stats_ref,
            up.block(step),
            low_ref,
            total_ref,
        )
        units_ref[step, 1:3] = unit_grad_ref[step, 0:2]

        @pl.when(step == 0)
        def _():
            fetches[1].wait()

        for left in range(0, UNITS, TILE):
            columns = slice(left, left + TILE)
            grad = dot_nn(feed_turned_ref[...], low_ref[:, columns]).astype(BF)
            staged_ref[:, :, :, columns] = grad.reshape(8, 4, 32, TILE)
        store(step).start()


    @pl.when((step >= NORMS_AT) & (step < COLUMNS_AT))
    def _():
        block = step - NORMS_AT
        rows = pl.ds(pl.multiple_of(block * OUT_TILE, OUT_TILE), OUT_TILE)
        advance((cot, middle, branch), block, COLUMNS_AT - NORMS_AT)
        grad_middle, low = norms_back(
            total_ref[rows],
            cot.block(block),
            middle.block(block),
            branch.block(block),
            vec_ref,
            sums_ref,
        )
        grad_middle_ref[rows] = grad_middle
        low_ref[rows] = low

    @pl.when((step >= COLUMNS_AT) & (step < HEADS_AT))
    def _():
        block = step - COLUMNS_AT
        columns = pl.ds(pl.multiple_of(block * TILE, TILE), TILE)
        advance((attended,), block, HEADS_AT - COLUMNS_AT)

        @pl.when(block == 0)
        def _():
            fetches[2].wait()
            fetches[3].wait()

        grad_out, delta = heads_back(
            low_ref[...],
            out_weight_ref[columns],
            hs_ref[0:1, columns],
            attended.block(block)[...],
        )
        ga_ref[:, columns] = grad_out
        delta_sum_ref[block, 0:1] = column_sum(delta)
        turned = delta.T
        for head in range(4):
            delta_ref[4 * block + head] = turned[head : head + 1]
        out_grad_ref[:, columns] = dot_nn(scaled_turned_ref[...], low_ref[:, columns]).astype(BF)

    @pl.when(step == HEADS_AT - 1)
    def _():
        total_ref[...] = jnp.zeros_like(total_ref)


    @pl.when((step >= HEADS_AT) & (step < TOKENS_AT))
    def _():
        pair = step - HEADS_AT
        columns = pl.ds(pl.multiple_of(pair * 128, 128), 128)
        advance((proj, lse, in_weight), pair, pairs)

        @pl.when(pair == 0)
        def _():
            fetches[4].wait()

        for part, starts in enumerate(((0, 3 * TILE), (TILE, 2 * TILE))):
            if part == 1:
                reduce_step(tick + 1)
            attention_back_keys(
                starts,
                cross_flag(lengths_ref, total_ref),
                *[proj.block(pair).at[:, pl.ds(index * 128, 128)] for index in range(3)],
                ga_ref.at[:, columns],
                lse.block(pair),
                [delta_ref[2 * pair], delta_ref[2 * pair + 1]],
                dq_ref,
                dk_ref,
                dv_ref,
            )
        query_sum, value_sum = in_back_pair(
            dq_ref,
            dk_ref,
            dv_ref,
            in_weight.block(pair)[...],
            turned_ref,
            out_grad_ref.at[:, columns],
            chunk_ref.at[pair % 2].reshape(8, 4, 32, 512),
            total_ref,
        )
        sums_ref[0:1, columns] = query_sum
        sums_ref[1:2, columns] = value_sum
        stage(0, "own", take_own, tick + 1)

    @pl.when((step >= TOKENS_AT) & (step < TOKENS_AT + 4))
    def _():
        block = step - TOKENS_AT
        rows = pl.ds(pl.multiple_of(block * TILE, TILE), TILE)
        advance((tokens,), block, 4)

        @pl.when(block >= 2)
        def _():
            put_tokens(block - 2).wait()

        result, gain_grad, shift_grad = tokens_back(
            tokens.block(block)[...], total_ref[rows], grad_middle_ref[rows], vec_ref[3:4]
        )
        tokens_grad_ref[block % 2] = result
        put_tokens(block).start()
        sums_ref[3:4] += gain_grad
        sums_ref[4:5] += shift_grad


    @pl.when(step == VECTORS_AT)
    def _():
        for y in range(2):
            for z in range(4):
                own = slice((2 * z + y) * 128, (2 * z + y + 1) * 128)
                for index in range(9):
                    lanes = slice(index % 4 * 128, index % 4 * 128 + 128)
                    row = 6 + index // 4
                    units_ref[8, row : row + 1, lanes] = sums_ref[index : index + 1, own]
                for x in range(2):
                    for c in range(2):
                        unit = 4 * y + 2 * x + c
                        units_ref[8, 0:3] = units_ref[unit, 0:3]
                        if (y, z, x, c) == (0, 0, 0, 0):
                            units_ref[8, 3:4] = sums_ref[9:10, 0:UNITS]
                            units_ref[8, 4:5] = sums_ref[9:10, UNITS : 2 * UNITS]
                            for block in range(4):
                                lanes = slice(block * 128, block * 128 + 128)
                                units_ref[8, 5:6, lanes] = delta_sum_ref[block, 0:1]
                        small.source[y, x, c, z] = units_ref[8].astype(BF)
        small.stage0()

    for index, action in enumerate((small.stage1, small.stage2, small.stage3)):

        @pl.when(step == VECTORS_AT + 1 + index)
        def _():
            action()

    @pl.when(step == VECTORS_AT + 4)
    def _():
        vec_out[...] = small.stage4()
        for block in range(2, 4):
            put_tokens(block).wait()


def back_part(
    lengths,
    act,
    slope,
    e,
    stats,
    up,
    feed_turned,
    unit_grad,
    down_grad,
    cotangent,
    middle,
    branch,
    scaled_turned,
    attended,
    out_weights,
    vectors,
    head_lanes,
    projected,
    lse,
    weights,
    turned,
    tokens,
):
    rows, width = tokens.shape
    pairs = width // 128

    return pl.pallas_call(
        back_kernel,
        grid=(BACK_STEPS,),
        in_specs=[
            pl.BlockSpec(memory_space=pltpu.SMEM),
            whole(unit_grad.shape),
            whole(vectors.shape),
            whole(head_lanes.shape),
            *[ANY] * 18,
        ],
        out_specs=[
            whole((4, 4, 32, 1024)),
            whole((8, 4, 32, 512)),
            whole((32, 3 * width)),
            whole((32, width)),
            whole((16, 512)),
            ANY,
            ANY,
        ],
        out_shape=[
            jax.ShapeDtypeStruct((4, 4, 32, 1024), BF),
            jax.ShapeDtypeStruct((8, 4, 32, 512), BF),
            jax.ShapeDtypeStruct((32, 3 * width), F32),
            jax.ShapeDtypeStruct((32, width), F32),
            jax.ShapeDtypeStruct((16, 512), F32),
            jax.ShapeDtypeStruct((rows, width), BF),
            jax.ShapeDtypeStruct((2, 2, 2, 8, 4, 32, UNITS), BF),
        ],
        scratch_shapes=[
            pltpu.VMEM((3, 2, rows, UNITS), BF),
            pltpu.VMEM((2, width, UNITS), BF),
            pltpu.VMEM((rows, 128), F32),
            pltpu.VMEM((width, rows), BF),
            pltpu.VMEM((2, OUT_TILE, width), BF),
            pltpu.VMEM((2, 2, OUT_TILE, width), F32),
            pltpu.VMEM((width, rows), BF),
            pltpu.VMEM((2, rows, TILE), F32),
            pltpu.VMEM((width, width), BF),
            pltpu.VMEM((2, rows, 384), BF),
            pltpu.VMEM((2, 8, rows), F32),
            pltpu.VMEM((2, width, 384), BF),
            pltpu.VMEM((width, rows), BF),
            pltpu.VMEM((2, TILE, width), BF),
            pltpu.VMEM((2, TILE, width), BF),
            pltpu.VMEM((8, 4, 32, UNITS), BF),
            pltpu.VMEM((rows, width), F32),
            pltpu.VMEM((rows, width), BF),
            pltpu.VMEM((width, width), BF),
            pltpu.VMEM((rows, width), BF),
            pltpu.VMEM((rows, width), F32),
            pltpu.VMEM((2 * pairs, 1, rows), F32),
            pltpu.VMEM((4, 8, 128), F32),
            pltpu.VMEM((16, width), F32),
            pltpu.VMEM((9, 16, UNITS), F32),
            pltpu.VMEM((rows, 128), F32),
            pltpu.VMEM((rows, 128), F32),
            pltpu.VMEM((rows, 128), F32),
            pltpu.VMEM((2, 2, 2, 2, 4, 32, 512), BF),
            pltpu.SemaphoreType.DMA((13, 2)),
            pltpu.SemaphoreType.DMA((6,)),
            *Reduction.scratch(),
            *SmallReduction.scratch(),
        ],
        compiler_params=params(collective_id=1, has_side_effects=True),
        name="back_part",
    )(
        lengths,
        unit_grad,
        vectors,
        head_lanes,
        act,
        slope,
        e,
        stats,
        up,
        feed_turned,
        down_grad.reshape(2, 2, 2, 4, 4, 32, width),
        cotangent,
        middle,
        branch,
        scaled_turned,
        attended,
        out_weights,
        projected,
        lse,
        weights,
        turned,
        tokens,
    )


def layer(staged, tokens, cotangent, lengths, attn, up, down, unit_vec, head_scale, down_bias):
    rows, width = tokens.shape
    heads = head_scale.shape[0]
    pairs = width // 128
    if staged:
        in_weight, out_weight, vec_block = attn
        (
            turned,
            projected,
            scaled,
            scaled_turned,
            attended,
            lse,
            vectors,
            head_lanes,
            weights,
            out_weights,
            up,
            unit_vec,
        ) = first_part(
            lengths, tokens, in_weight, vec_block, out_weight, up, unit_vec, head_scale[None, :]
        )
        weights = weights.reshape(width, 3 * width)
        out_weights = out_weights.reshape(width, width)
        up = up.reshape(-1, width, UNITS)
        unit_vec = unit_vec.reshape(-1, unit_vec.shape[-2], UNITS)
        branch, middle, feed_turned, act, slope, stats, down = second_part(
            scaled, out_weights, vectors, tokens, up, unit_vec, down
        )
        down = down.reshape(-1, UNITS, width)
    else:
        weights, out_weights, vectors = attn
        scale = head_scale.astype(F32)
        head_lanes = jnp.repeat(scale, width // heads)[None, :]
        first, projected, scaled, attended, lse = plain_first(
            lengths, tokens, weights, vectors, head_lanes
        )
        branch, middle, feed = out_proj(scaled, out_weights, vectors, tokens)
        act, slope, stats = up_pass(feed, up, unit_vec)
    mixed, down_grad, e, stats, unit_grad = down_pass(
        act, stats, unit_vec, down, cotangent, middle, down_bias[None, :]
    )
    if staged:
        down_total, up_total, in_total, out_total, vec_shares, tokens_grad, _ = back_part(
            lengths,
            act,
            slope,
            e,
            stats,
            up,
            feed_turned,
            unit_grad,
            down_grad,
            cotangent,
            middle,
            branch,
            scaled_turned,
            attended,
            out_weights,
            vectors,
            head_lanes,
            projected,
            lse,
            weights,
            turned,
            tokens,
        )
        return mixed, tokens_grad, down_total, up_total, in_total, out_total, vec_shares
    up_grad, up_bias_grad, grad_feed = up_back(
        act, slope, e, stats, up, feed
    )
    grad_middle, ga, out_grad, delta, sums = out_back(
        grad_feed,
        cotangent,
        middle,
        branch,
        scaled,
        attended,
        out_weights,
        vectors,
        head_lanes,
    )
    chunks, proj_bias, tokens_grad, pre_sums = in_back(
        lengths,
        projected,
        ga,
        lse,
        delta.reshape(pairs, 2, rows),
        weights,
        first,
        out_grad,
        tokens,
        vectors[3:4],
        grad_middle,
    )
    scale_grad = jnp.sum(delta, axis=1) / scale
    vec_grads = [
        proj_bias[:, 0].reshape(width),
        proj_bias[:, 1].reshape(width),
        sums[2],
        pre_sums[0],
        pre_sums[1],
        sums[5],
        sums[6],
        sums[7],
        sums[8],
    ]
    unit_grads = [up_bias_grad[:, 0], unit_grad[:, 0], unit_grad[:, 1]]
    return mixed, tokens_grad, chunks, up_grad, down_grad, vec_grads, unit_grads, sums[9], scale_grad


def body(
    axes,
    tokens,
    cotangent,
    lengths,
    in_weight,
    query_bias,
    value_bias,
    out_weight,
    out_bias,
    head_scale,
    pre_gain,
    pre_bias,
    post_gain,
    post_bias,
    feed_gain,
    feed_bias,
    up_weight,
    up_bias,
    mid_gain,
    mid_bias,
    down_weight,
    down_bias,
):
    planes, wide = axes
    every = ("dp", "wide")
    staged = (planes, wide) == (4, 8)
    rows, width = tokens.shape
    units = down_weight.shape[0] * wide
    steps = units // UNITS
    share = in_weight.shape[0]
    columns = [
        query_bias,
        value_bias,
        out_bias,
        pre_gain,
        pre_bias,
        post_gain,
        post_bias,
        feed_gain,
        feed_bias,
    ]
    index = lax.broadcasted_iota(jnp.int32, (32, up_bias.shape[0]), 0)
    unit_rows = jnp.where(index == 0, up_bias[None, :], jnp.zeros((), BF))
    unit_rows = jnp.where(index == 1, mid_gain[None, :], unit_rows)
    unit_rows = jnp.where(index == 2, mid_bias[None, :], unit_rows)
    if staged:
        index = lax.broadcasted_iota(jnp.int32, (32, share), 0)
        vec_block = jnp.zeros((32, share), BF)
        for row, column in enumerate(columns):
            vec_block = jnp.where(index == row, column[None, :], vec_block)
        attn = (in_weight, out_weight, vec_block)
        up, unit_vec, down = up_weight, unit_rows, down_weight
    else:
        flat = jnp.concatenate(columns).reshape(len(columns), share)
        attn = (
            lax.all_gather(in_weight, every, axis=0, tiled=True),
            lax.all_gather(out_weight, every, axis=0, tiled=True),
            jnp.pad(
                lax.all_gather(flat, every, axis=1, tiled=True), ((0, 16 - len(columns)), (0, 0))
            ).astype(F32),
        )
        up = lax.all_gather(up_weight, "wide", axis=1, tiled=True)
        up = up.reshape(width, steps, UNITS).transpose(1, 0, 2)
        unit_vec = lax.all_gather(unit_rows, "wide", axis=1, tiled=True)
        unit_vec = unit_vec.reshape(32, steps, UNITS).transpose(1, 0, 2)
        down = lax.all_gather(down_weight, "wide", axis=0, tiled=True)
        down = down.reshape(steps, UNITS, width)
    results = layer(
        staged,
        tokens,
        cotangent,
        lengths,
        attn,
        up,
        down,
        unit_vec,
        head_scale,
        down_bias,
    )
    heads = head_scale.shape[0]
    pairs = width // 128
    if staged:
        mixed, tokens_grad, down_total, up_total, in_total, out_total, vec_shares = results
        up_total = up_total.astype(F32).reshape(width, UNITS)
        down_total = down_total.astype(F32).reshape(UNITS, width)
        unit_totals = [vec_shares[index] for index in range(3)]
        down_sum = vec_shares[3:5].reshape(width)
        scale_sum = vec_shares[5].reshape(4, 128)[:, :4].reshape(heads) / head_scale.astype(F32)
        offset = share * lax.rem(lax.axis_index("wide"), 128 // share)
        own = vec_shares[6:9].reshape(12, 128)
        own = lax.dynamic_slice(own, (0, offset), (len(columns), share))
        vec_totals = [own[index] for index in range(len(columns))]
    else:
        (mixed, tokens_grad, chunks, up_grad, down_grad, vec_grads, unit_grads) = results[:7]
        down_sum, scale_sum = results[7:]

        def scatter(value, axis=0, over=every):
            return lax.psum_scatter(value, over, scatter_dimension=axis, tiled=True)

        def both_ways(value, axis):
            part = scatter(value.astype(BF), axis, "wide")
            return lax.psum(part, "dp").astype(F32)

        up_total = both_ways(up_grad.transpose(1, 0, 2).reshape(width, units), 1)
        down_total = both_ways(down_grad.reshape(units, width), 0)
        unit_totals = [
            lax.psum(scatter(item.reshape(units), 0, "wide"), "dp") for item in unit_grads
        ]
        down_sum, scale_sum = lax.psum((down_sum, scale_sum), every)
        vec_totals = [scatter(item) for item in vec_grads]
        natural = chunks.transpose(0, 2, 1, 3, 4).reshape(pairs, width, 512)
        in_total = natural[:, :, :384].reshape(pairs, width, 3, 128)
        in_total = scatter(in_total.transpose(1, 2, 0, 3).reshape(width, 3 * width).astype(F32))
        out_total = scatter(
            natural[:, :, 384:].transpose(1, 0, 2).reshape(width, width).astype(F32)
        )
    return (
        mixed,
        tokens_grad,
        in_total,
        vec_totals[0],
        vec_totals[1],
        out_total,
        vec_totals[2],
        scale_sum,
        vec_totals[3],
        vec_totals[4],
        vec_totals[5],
        vec_totals[6],
        vec_totals[7],
        vec_totals[8],
        up_total,
        unit_totals[0],
        unit_totals[1],
        unit_totals[2],
        down_total,
        down_sum,
    )


def solution(mesh):
    by_all = P(("dp", "wide"))
    rows_all = P(("dp", "wide"), None)
    axes = (mesh.shape["dp"], mesh.shape["wide"])
    return jax.shard_map(
        functools.partial(body, axes),
        mesh=mesh,
        in_specs=(
            rows_all,
            rows_all,
            rows_all,
            rows_all,
            by_all,
            by_all,
            rows_all,
            by_all,
            P(),
            by_all,
            by_all,
            by_all,
            by_all,
            by_all,
            by_all,
            P(None, "wide"),
            P("wide"),
            P("wide"),
            P("wide"),
            P("wide", None),
            P(),
        ),
        out_specs=(
            rows_all,
            rows_all,
            rows_all,
            by_all,
            by_all,
            rows_all,
            by_all,
            P(),
            by_all,
            by_all,
            by_all,
            by_all,
            by_all,
            by_all,
            P(None, "wide"),
            P("wide"),
            P("wide"),
            P("wide"),
            P("wide", None),
            P(),
        ),
        check_vma=False,
    )
```

```python
import functools

import jax
import jax.numpy as jnp
from jax import lax
from jax.experimental import pallas as pl
from jax.experimental.pallas import tpu as pltpu
from jax.sharding import PartitionSpec as P

EPS = 1e-05
ROOT_HALF = 0.7071067811865476
INV_ROOT_TAU = 0.3989422804014327
LOG2E = 1.4426950408889634
MASKED = -1e30
BF = jnp.bfloat16
F32 = jnp.float32
TILE = 256
UNITS = 512
SLIM = 64
MESH = pl.DeviceIdType.MESH
VMEM_LIMIT = 62 * 1024 * 1024
ANY = pl.BlockSpec(memory_space=pl.ANY)


def dot_nn(left, right):
    return lax.dot_general(left, right, (((1,), (0,)), ((), ())), preferred_element_type=F32)


def dot_nt(left, right):
    return lax.dot_general(left, right, (((1,), (1,)), ((), ())), preferred_element_type=F32)


def dot_tn(left, right):
    return lax.dot_general(left, right, (((0,), (0,)), ((), ())), preferred_element_type=F32)


def params(**more):
    return pltpu.CompilerParams(
        dimension_semantics=("arbitrary",), vmem_limit_bytes=VMEM_LIMIT, **more
    )


def whole(shape):
    zeros = (0,) * len(shape)
    return pl.BlockSpec(shape, lambda *_: zeros, pipeline_mode=pl.Buffered(1))


def row_norm(values):
    center = values - jnp.mean(values, axis=-1, keepdims=True)
    inv = lax.rsqrt(jnp.mean(center * center, axis=-1, keepdims=True) + EPS)
    return center * inv, inv


def norm_back(grad, gain, normed, inv):
    scaled = grad * gain
    first = jnp.mean(scaled, axis=-1, keepdims=True)
    cross = jnp.mean(scaled * normed, axis=-1, keepdims=True)
    return inv * (scaled - first - normed * cross)


def column_sum(values):
    return jnp.sum(values, axis=0, keepdims=True)


def lane_fold(values):
    total = values[:, :128]
    for start in range(128, values.shape[1], 128):
        total = total + values[:, start : start + 128]
    return total


def cross_flag(lengths_ref, rows_ref):
    return jnp.where(lengths_ref[0, 0] == rows_ref.shape[0], 0.0, MASKED)


def stacked(value, low_lanes):
    zero = jnp.zeros_like(value)
    return jnp.concatenate(
        [jnp.where(low_lanes, value, zero), jnp.where(low_lanes, zero, value)], axis=0
    )


def attention_pair(cross, q_ref, k_ref, v_ref, scale, scaled_ref, out_ref, lse_ref, vext_ref):
    rows = q_ref.shape[0]
    half = rows // 2
    factor = LOG2E * 64 ** (-0.5)
    low_lanes = lax.broadcasted_iota(jnp.int32, (1, 128), 1) < 64
    below = lax.broadcasted_iota(jnp.int32, (TILE, TILE), 1) <= lax.broadcasted_iota(
        jnp.int32, (TILE, TILE), 0
    )
    vext_ref[:, :128] = v_ref[...]
    vext_ref[:, 128:] = jnp.ones((rows, 128), BF)
    for start in range(0, rows, TILE):
        stop = start + TILE
        both = dot_nt(stacked(q_ref[start:stop], low_lanes), k_ref[:stop])
        peaks, weights = [], []
        for head in range(2):
            raw = both[head * TILE : (head + 1) * TILE]
            parts = []
            if start >= half:
                parts.append((raw[:, :half], cross))
                if start > half:
                    parts.append((raw[:, half:start], None))
            elif start > 0:
                parts.append((raw[:, :start], None))
            parts.append((jnp.where(below, raw[:, start:stop], MASKED), None))
            peak = None
            for piece, shift in parts:
                top = jnp.max(piece, axis=-1, keepdims=True)
                if shift is not None:
                    top = top + shift
                peak = top if peak is None else jnp.maximum(peak, top)
            peaks.append(peak)
            pieces = []
            for piece, shift in parts:
                level = peak if shift is None else peak - shift
                pieces.append(jnp.exp2((piece - level) * factor).astype(BF))
            weights.append(pieces[0] if len(pieces) == 1 else jnp.concatenate(pieces, axis=1))
        both = dot_nn(jnp.concatenate(weights, axis=0), vext_ref[:stop])
        total = jnp.where(low_lanes, both[:TILE, 128:], both[TILE:, 128:])
        peak = jnp.where(low_lanes, peaks[0], peaks[1])
        mixed = jnp.where(low_lanes, both[:TILE, :128], both[TILE:, :128]) / total
        out_ref[start:stop] = mixed
        scaled_ref[start:stop] = (mixed * scale).astype(BF)
        lse = (peak * factor + jnp.log2(total)).T
        lse_ref[0, 0:1, start:stop] = lse[0:1]
        lse_ref[0, 1:2, start:stop] = lse[64:65]


def project_pair(first_ref, weights, bias, proj_ref):
    proj_ref[0] = (dot_nn(first_ref[...], weights) + bias).astype(BF)


def three(proj_ref):
    return [proj_ref.at[0, :, pl.ds(part * 128, 128)] for part in range(3)]


def plain_first_kernel(
    lengths_ref,
    tokens_ref,
    wq_ref,
    wk_ref,
    wv_ref,
    vectors_ref,
    bq_ref,
    bv_ref,
    hs_ref,
    first_ref,
    proj_ref,
    scaled_ref,
    attended_ref,
    lse_ref,
    vext_ref,
):
    @pl.when(pl.program_id(0) == 0)
    def _():
        for start in range(0, tokens_ref.shape[0], TILE):
            rows = pl.ds(start, TILE)
            normed, _ = row_norm(tokens_ref[rows].astype(F32))
            first_ref[rows] = (normed * vectors_ref[3:4] + vectors_ref[4:5]).astype(BF)

    weights = jnp.concatenate([wq_ref[...], wk_ref[...], wv_ref[...]], axis=1)
    bias = jnp.concatenate([bq_ref[0:1], jnp.zeros((1, 128), F32), bv_ref[1:2]], axis=1)
    project_pair(first_ref, weights, bias, proj_ref)
    attention_pair(
        cross_flag(lengths_ref, tokens_ref), *three(proj_ref), hs_ref[...], scaled_ref, attended_ref, lse_ref, vext_ref
    )


def plain_first(lengths, tokens, weights, vectors, head_lanes):
    rows, width = tokens.shape
    pairs = width // 128
    column = pl.BlockSpec((rows, 128), lambda p: (0, p))
    bias = pl.BlockSpec((16, 128), lambda p: (0, p))
    return pl.pallas_call(
        plain_first_kernel,
        grid=(pairs,),
        in_specs=[
            pl.BlockSpec(memory_space=pltpu.SMEM),
            whole((rows, width)),
            pl.BlockSpec((width, 128), lambda p: (0, p)),
            pl.BlockSpec((width, 128), lambda p: (0, pairs + p)),
            pl.BlockSpec((width, 128), lambda p: (0, 2 * pairs + p)),
            whole(vectors.shape),
            bias,
            bias,
            pl.BlockSpec((1, 128), lambda p: (0, p)),
        ],
        out_specs=[
            whole((rows, width)),
            pl.BlockSpec((1, rows, 384), lambda p: (p, 0, 0)),
            column,
            column,
            pl.BlockSpec((1, 8, rows), lambda p: (p, 0, 0)),
        ],
        out_shape=[
            jax.ShapeDtypeStruct((rows, width), BF),
            jax.ShapeDtypeStruct((pairs, rows, 384), BF),
            jax.ShapeDtypeStruct((rows, width), BF),
            jax.ShapeDtypeStruct((rows, width), F32),
            jax.ShapeDtypeStruct((pairs, 8, rows), F32),
        ],
        scratch_shapes=[pltpu.VMEM((rows, 256), BF)],
        compiler_params=params(),
        name="plain_first",
    )(lengths, tokens, weights, weights, weights, vectors, vectors, vectors, head_lanes)


def out_proj_rows(scaled, weights, vec_ref, tokens, branch_ref, middle_ref):
    branch = dot_nn(scaled, weights) + vec_ref[2:3]
    normed, _ = row_norm(branch)
    middle = tokens.astype(F32) + (normed * vec_ref[5:6] + vec_ref[6:7])
    again, _ = row_norm(middle)
    branch_ref[...] = branch
    middle_ref[...] = middle
    return (again * vec_ref[7:8] + vec_ref[8:9]).astype(BF)


def out_proj_kernel(scaled_ref, weight_ref, vec_ref, tokens_ref, branch_ref, middle_ref, feed_ref):
    feed_ref[...] = out_proj_rows(
        scaled_ref[...], weight_ref[...], vec_ref, tokens_ref[...], branch_ref, middle_ref
    )


def out_proj(scaled, weights, vectors, tokens):
    rows, width = tokens.shape
    by_row = pl.BlockSpec((TILE, width), lambda i: (i, 0))
    return pl.pallas_call(
        out_proj_kernel,
        grid=(rows // TILE,),
        in_specs=[
            by_row,
            whole((width, width)),
            whole(vectors.shape),
            by_row,
        ],
        out_specs=[by_row, by_row, by_row],
        out_shape=[
            jax.ShapeDtypeStruct((rows, width), F32),
            jax.ShapeDtypeStruct((rows, width), F32),
            jax.ShapeDtypeStruct((rows, width), BF),
        ],
        compiler_params=params(),
        name="out_proj",
    )(scaled, weights, vectors, tokens)


def phi_and_slope(value):
    bell = jnp.exp2(value * value * (-0.5 * LOG2E))
    t = 1.0 / (1.0 + (0.3275911 * ROOT_HALF) * jnp.abs(value))
    series = t * (
        0.5 * 0.254829592
        + t
        * (
            0.5 * -0.284496736
            + t * (0.5 * 1.421413741 + t * (0.5 * -1.453152027 + t * (0.5 * 1.061405429)))
        )
    )
    tail = series * bell
    area = jnp.where(value < 0.0, tail, 1.0 - tail)
    return value * area, area + value * bell * INV_ROOT_TAU


def up_step(feed_ref, up, vec, act_ref, slope_ref, sums_ref):
    for left in range(0, UNITS, TILE):
        columns = slice(left, left + TILE)
        pre = dot_nn(feed_ref[...], up[:, columns])
        bias = vec[0:1, columns].astype(F32)
        for start in range(0, feed_ref.shape[0], SLIM):
            rows = slice(start, start + SLIM)
            act, slope = phi_and_slope(pre[rows] + bias)
            act_ref[0, rows, columns] = act.astype(BF)
            slope_ref[0, rows, columns] = slope.astype(BF)
            sums_ref[0, rows] += lane_fold(act)
            sums_ref[1, rows] += lane_fold(act * act)


def side_by_side(*columns):
    lane = lax.broadcasted_iota(jnp.int32, (1, 128), 1)
    result = jnp.broadcast_to(columns[-1], (columns[-1].shape[0], 128))
    for index in range(len(columns) - 2, -1, -1):
        result = jnp.where(lane == index, columns[index], result)
    return result


def up_stats(units, stats_ref, sums_ref):
    for start in range(0, stats_ref.shape[0], TILE):
        rows = pl.ds(start, TILE)
        mean = jnp.sum(sums_ref[0, rows], axis=1, keepdims=True) / units
        square = jnp.sum(sums_ref[1, rows], axis=1, keepdims=True) / units
        inv = lax.rsqrt(square - mean * mean + EPS)
        stats_ref[rows] = side_by_side(mean, inv)


def up_kernel(units, feed_ref, up_ref, vec_ref, act_ref, slope_ref, stats_ref, sums_ref):
    step = pl.program_id(0)

    @pl.when(step == 0)
    def _():
        sums_ref[...] = jnp.zeros_like(sums_ref)

    up_step(feed_ref, up_ref.at[0], vec_ref.at[0], act_ref, slope_ref, sums_ref)

    @pl.when(step == pl.num_programs(0) - 1)
    def _():
        up_stats(units, stats_ref, sums_ref)


def up_pass(feed, up, vec):
    rows, width = feed.shape
    steps = up.shape[0]
    block = pl.BlockSpec((1, rows, UNITS), lambda j: (j, 0, 0))
    return pl.pallas_call(
        functools.partial(up_kernel, steps * UNITS),
        grid=(steps,),
        in_specs=[
            whole((rows, width)),
            pl.BlockSpec((1, width, UNITS), lambda j: (j, 0, 0)),
            pl.BlockSpec((1, vec.shape[1], UNITS), lambda j: (j, 0, 0)),
        ],
        out_specs=[block, block, whole((rows, 128))],
        out_shape=[
            jax.ShapeDtypeStruct((steps, rows, UNITS), BF),
            jax.ShapeDtypeStruct((steps, rows, UNITS), BF),
            jax.ShapeDtypeStruct((rows, 128), F32),
        ],
        scratch_shapes=[pltpu.VMEM((2, rows, 128), F32)],
        compiler_params=params(),
        name="up_pass",
    )(feed, up, vec)


def down_kernel(
    units,
    act_ref,
    stats_ref,
    vec_ref,
    down_ref,
    cot_ref,
    middle_ref,
    shift_ref,
    mixed_ref,
    down_grad_ref,
    e_ref,
    all_stats_ref,
    vec_grad_ref,
    total_ref,
    sums_ref,
    low_ref,
):
    step = pl.program_id(0)
    last = pl.num_programs(0) - 1
    rows_all = cot_ref.shape[0]

    @pl.when(step == 0)
    def _():
        total_ref[...] = jnp.zeros_like(total_ref)
        sums_ref[...] = jnp.zeros_like(sums_ref)

    gain = vec_ref[0, 1:2].astype(F32)
    shift = vec_ref[0, 2:3].astype(F32)
    slims = [slice(start, start + SLIM) for start in range(0, rows_all, SLIM)]

    def normalized(rows, columns):
        value = act_ref[0, rows, columns].astype(F32)
        return (value - stats_ref[rows, 0:1]) * stats_ref[rows, 1:2]

    for rows in slims:
        low_ref[rows] = (normalized(rows, slice(0, UNITS)) * gain + shift).astype(BF)
    for left in range(0, UNITS, TILE):
        columns = slice(left, left + TILE)
        grads = dot_nt(cot_ref[...], down_ref[0, columns])
        gain_grad = jnp.zeros((SLIM, TILE), F32)
        bias_grad = jnp.zeros((SLIM, TILE), F32)
        for rows in slims:
            normed = normalized(rows, columns)
            grad = grads[rows]
            gain_grad = gain_grad + grad * normed
            bias_grad = bias_grad + grad
            e = grad * gain[:, columns]
            e_ref[0, rows, columns] = e.astype(BF)
            sums_ref[0, rows] += lane_fold(e)
            sums_ref[1, rows] += lane_fold(e * normed)
        vec_grad_ref[0, 0:1, columns] = column_sum(gain_grad)
        vec_grad_ref[0, 1:2, columns] = column_sum(bias_grad)
    for left in range(0, total_ref.shape[1], TILE):
        columns = slice(left, left + TILE)
        total_ref[:, columns] += dot_nn(low_ref[...], down_ref[0, :, columns])
    for left in range(0, UNITS, TILE):
        columns = slice(left, left + TILE)
        down_grad_ref[0, columns] = dot_tn(low_ref[:, columns], cot_ref[...]).astype(BF)

    @pl.when(step == last)
    def _():
        for start in range(0, rows_all, TILE):
            rows = pl.ds(start, TILE)
            mixed_ref[rows] = (
                middle_ref[rows] + total_ref[rows] + shift_ref[...].astype(F32)
            ).astype(BF)
            first = jnp.sum(sums_ref[0, rows], axis=1, keepdims=True) / units
            cross = jnp.sum(sums_ref[1, rows], axis=1, keepdims=True) / units
            all_stats_ref[rows] = side_by_side(
                stats_ref[rows, 0:1], stats_ref[rows, 1:2], first, cross
            )


def down_pass(act, stats, vec, down, cotangent, middle, shift):
    rows, width = cotangent.shape
    steps = act.shape[0]
    block = pl.BlockSpec((1, rows, UNITS), lambda j: (j, 0, 0))
    return pl.pallas_call(
        functools.partial(down_kernel, steps * UNITS),
        grid=(steps,),
        in_specs=[
            block,
            whole((rows, 128)),
            pl.BlockSpec((1, vec.shape[1], UNITS), lambda j: (j, 0, 0)),
            pl.BlockSpec((1, UNITS, width), lambda j: (j, 0, 0)),
            whole((rows, width)),
            whole((rows, width)),
            whole((1, width)),
        ],
        out_specs=[
            whole((rows, width)),
            pl.BlockSpec((1, UNITS, width), lambda j: (j, 0, 0)),
            block,
            whole((rows, 128)),
            pl.BlockSpec((1, 8, UNITS), lambda j: (j, 0, 0)),
        ],
        out_shape=[
            jax.ShapeDtypeStruct((rows, width), BF),
            jax.ShapeDtypeStruct((steps, UNITS, width), BF),
            jax.ShapeDtypeStruct((steps, rows, UNITS), BF),
            jax.ShapeDtypeStruct((rows, 128), F32),
            jax.ShapeDtypeStruct((steps, 8, UNITS), F32),
        ],
        scratch_shapes=[
            pltpu.VMEM((rows, width), F32),
            pltpu.VMEM((2, rows, 128), F32),
            pltpu.VMEM((rows, UNITS), BF),
        ],
        compiler_params=params(),
        name="down_pass",
    )(act, stats, vec, down, cotangent, middle, shift)


def up_back_step(act, slope, e, stats_ref, up, low_ref, total_ref):
    bias_grad = jnp.zeros((SLIM, UNITS), F32)
    for start in range(0, total_ref.shape[0], SLIM):
        rows = slice(start, start + SLIM)
        inv = stats_ref[rows, 1:2]
        normed = (act[rows].astype(F32) - stats_ref[rows, 0:1]) * inv
        grad_act = inv * (
            e[rows].astype(F32) - stats_ref[rows, 2:3] - normed * stats_ref[rows, 3:4]
        )
        low = (grad_act * slope[rows].astype(F32)).astype(BF)
        bias_grad = bias_grad + low.astype(F32)
        low_ref[rows, 0:UNITS] = low
    for left in range(0, total_ref.shape[1], TILE):
        columns = slice(left, left + TILE)
        total_ref[:, columns] += dot_nt(low_ref[:, 0:UNITS], up[columns])
    return column_sum(bias_grad)


def up_back_kernel(
    act_ref,
    slope_ref,
    e_ref,
    stats_ref,
    up_ref,
    feed_ref,
    up_grad_ref,
    bias_grad_ref,
    total_ref,
    turned_ref,
    low_ref,
):
    @pl.when(pl.program_id(0) == 0)
    def _():
        total_ref[...] = jnp.zeros_like(total_ref)
        turned_ref[...] = feed_ref[...].T

    bias_grad_ref[0, 0:1] = up_back_step(
        act_ref.at[0],
        slope_ref.at[0],
        e_ref.at[0],
        stats_ref,
        up_ref.at[0],
        low_ref,
        total_ref,
    )
    up_grad_ref[0] = dot_nn(turned_ref[...], low_ref[...]).astype(BF)


def up_back(act, slope, e, stats, up, feed):
    rows, width = feed.shape
    steps = act.shape[0]
    block = pl.BlockSpec((1, rows, UNITS), lambda j: (j, 0, 0))
    narrow = whole((rows, 128))
    return pl.pallas_call(
        up_back_kernel,
        grid=(steps,),
        in_specs=[
            block,
            block,
            block,
            narrow,
            pl.BlockSpec((1, width, UNITS), lambda j: (j, 0, 0)),
            whole((rows, width)),
        ],
        out_specs=[
            pl.BlockSpec((1, width, UNITS), lambda j: (j, 0, 0)),
            pl.BlockSpec((1, 8, UNITS), lambda j: (j, 0, 0)),
            whole((rows, width)),
        ],
        out_shape=[
            jax.ShapeDtypeStruct((steps, width, UNITS), BF),
            jax.ShapeDtypeStruct((steps, 8, UNITS), F32),
            jax.ShapeDtypeStruct((rows, width), F32),
        ],
        scratch_shapes=[pltpu.VMEM((width, rows), BF), pltpu.VMEM((rows, UNITS), BF)],
        compiler_params=params(),
        name="up_back",
    )(act, slope, e, stats, up, feed)


def norms_back(grad_feed, cot_ref, middle_ref, branch_ref, vec_ref, sums_ref):
    normed, inv = row_norm(middle_ref[...])
    cot = cot_ref[...].astype(F32)
    grad_middle = cot + norm_back(grad_feed, vec_ref[7:8], normed, inv)
    sums_ref[7:8] += column_sum(grad_feed * normed)
    sums_ref[8:9] += column_sum(grad_feed)
    sums_ref[9:10] += column_sum(cot)
    normed, inv = row_norm(branch_ref[...])
    low = norm_back(grad_middle, vec_ref[5:6], normed, inv).astype(BF)
    sums_ref[5:6] += column_sum(grad_middle * normed)
    sums_ref[6:7] += column_sum(grad_middle)
    sums_ref[2:3] += column_sum(low.astype(F32))
    return grad_middle, low


def heads_back(low, weights, scale, attended):
    grad_out = (dot_nt(low, weights) * scale).astype(BF)
    product = grad_out.astype(F32) * attended
    high = product.astype(BF)
    rest = (product - high.astype(F32)).astype(BF)
    heads = (
        lax.broadcasted_iota(jnp.int32, (product.shape[1], 128), 0) // 64
        == lax.broadcasted_iota(jnp.int32, (product.shape[1], 128), 1)
    ).astype(BF)
    return grad_out, dot_nn(high, heads) + dot_nn(rest, heads)


def out_back_kernel(
    grad_feed_ref,
    cot_ref,
    middle_ref,
    branch_ref,
    scaled_ref,
    attended_ref,
    weight_ref,
    vec_ref,
    hs_ref,
    grad_middle_ref,
    ga_ref,
    out_grad_ref,
    delta_ref,
    sums_ref,
    total_ref,
):
    step = pl.program_id(0)

    @pl.when(step == 0)
    def _():
        total_ref[...] = jnp.zeros_like(total_ref)
        sums_ref[...] = jnp.zeros_like(sums_ref)

    grad_middle, low = norms_back(
        grad_feed_ref[...], cot_ref, middle_ref, branch_ref, vec_ref, sums_ref
    )
    grad_middle_ref[...] = grad_middle
    ga_ref[...], delta = heads_back(low, weight_ref[...], hs_ref[...], attended_ref[...])
    total_ref[...] += dot_tn(scaled_ref[...], low)
    delta_ref[...] = delta.T[: delta_ref.shape[0]]

    @pl.when(step == pl.num_programs(0) - 1)
    def _():
        out_grad_ref[...] = total_ref[...].astype(BF)


def out_back(
    grad_feed, cotangent, middle, branch, scaled, attended, weights, vectors, head_lanes
):
    rows, width = cotangent.shape
    heads = 2 * width // 128
    by_row = pl.BlockSpec((TILE, width), lambda i: (i, 0))
    return pl.pallas_call(
        out_back_kernel,
        grid=(rows // TILE,),
        in_specs=[
            by_row,
            by_row,
            by_row,
            by_row,
            by_row,
            by_row,
            whole((width, width)),
            whole(vectors.shape),
            whole((1, width)),
        ],
        out_specs=[
            by_row,
            by_row,
            whole((width, width)),
            pl.BlockSpec((heads, TILE), lambda i: (0, i)),
            whole((16, width)),
        ],
        out_shape=[
            jax.ShapeDtypeStruct((rows, width), F32),
            jax.ShapeDtypeStruct((rows, width), BF),
            jax.ShapeDtypeStruct((width, width), BF),
            jax.ShapeDtypeStruct((heads, rows), F32),
            jax.ShapeDtypeStruct((16, width), F32),
        ],
        scratch_shapes=[pltpu.VMEM((width, width), F32)],
        compiler_params=params(),
        name="out_back",
    )(
        grad_feed,
        cotangent,
        middle,
        branch,
        scaled,
        attended,
        weights,
        vectors,
        head_lanes,
    )


def attention_back_keys(
    starts, cross, q_ref, k_ref, v_ref, ga_ref, lse_ref, deltas, dq_ref, dk_ref, dv_ref
):
    rows = q_ref.shape[0]
    half = rows // 2
    factor = LOG2E * 64 ** (-0.5)
    low_lanes = lax.broadcasted_iota(jnp.int32, (1, 128), 1) < 64
    above = lax.broadcasted_iota(jnp.int32, (TILE, TILE), 0) <= lax.broadcasted_iota(
        jnp.int32, (TILE, TILE), 1
    )

    def pick(both):
        return jnp.where(low_lanes, both[:TILE], both[TILE:])

    for start in starts:
        stop = start + TILE
        keys = k_ref[start:stop]
        keys_apart = stacked(keys, low_lanes)
        values_apart = stacked(v_ref[start:stop], low_lanes)
        dk = jnp.zeros((TILE, 128), F32)
        dv = jnp.zeros((TILE, 128), F32)
        for left, right in ((start, half), (half, rows)) if start < half else ((start, rows),):
            raw = dot_nt(keys_apart, q_ref[left:right])
            grad_weights = dot_nt(values_apart, ga_ref[left:right])
            weights, grad_scores = [], []
            for head in range(2):
                mine = slice(head * TILE, (head + 1) * TILE)
                level = lse_ref[head : head + 1, left:right]
                if start < half <= left:
                    level = level - cross
                exponent = raw[mine] * factor - level
                if left == start:
                    first = jnp.where(above, exponent[:, :TILE], MASKED)
                    exponent = (
                        first
                        if right - left == TILE
                        else jnp.concatenate([first, exponent[:, TILE:]], axis=1)
                    )
                weight = jnp.exp2(exponent)
                weights.append(weight.astype(BF))
                delta = deltas[head][:, left:right]
                grad_scores.append((weight * (grad_weights[mine] - delta)).astype(BF))
            dv = dv + pick(dot_nn(jnp.concatenate(weights, axis=0), ga_ref[left:right]))
            dk = dk + pick(dot_nn(jnp.concatenate(grad_scores, axis=0), q_ref[left:right]))
            dq = jnp.where(low_lanes, dot_tn(grad_scores[0], keys), dot_tn(grad_scores[1], keys))
            if start == 0:
                dq_ref[left:right] = dq
            else:
                dq_ref[left:right] += dq
        dk_ref[start:stop] = dk
        dv_ref[start:stop] = dv


def in_back_pair(dq_ref, dk_ref, dv_ref, weights, turned_ref, out_grad_ref, chunk_ref, total_ref):
    factor = 64 ** (-0.5)
    dq = (dq_ref[...] * factor).astype(BF)
    dk = (dk_ref[...] * factor).astype(BF)
    dv = dv_ref[...].astype(BF)
    grads = jnp.concatenate([dq, dk, dv], axis=1)
    shares = dot_nn(turned_ref[...], grads).astype(BF)
    for start in range(0, total_ref.shape[0], TILE):
        part = jnp.concatenate(
            [shares[start : start + TILE], out_grad_ref[start : start + TILE]], axis=1
        )
        chunk_ref[:, start // TILE] = part.reshape(8, 32, 512)
        columns = slice(start, start + TILE)
        total_ref[:, columns] += dot_nt(grads, weights[columns])
    return column_sum(dq.astype(F32)), column_sum(dv.astype(F32))


def tokens_back(tokens, grad, grad_middle, gain):
    normed, inv = row_norm(tokens.astype(F32))
    back = norm_back(grad, gain, normed, inv)
    return (grad_middle + back).astype(BF), column_sum(grad * normed), column_sum(grad)


def in_back_kernel(
    lengths_ref,
    proj_ref,
    ga_ref,
    lse_ref,
    delta_ref,
    wq_ref,
    wk_ref,
    wv_ref,
    first_ref,
    out_grad_ref,
    tokens_ref,
    gain_ref,
    grad_middle_ref,
    chunk_ref,
    bias_ref,
    tokens_grad_ref,
    sums_ref,
    dq_ref,
    dk_ref,
    dv_ref,
    turned_ref,
    total_ref,
):
    step = pl.program_id(0)
    q_ref, k_ref, v_ref = three(proj_ref)
    rows_all = tokens_ref.shape[0]

    @pl.when(step == 0)
    def _():
        turned_ref[...] = first_ref[...].T
        total_ref[...] = jnp.zeros_like(total_ref)

    deltas = [delta_ref[0, head : head + 1] for head in range(2)]
    attention_back_keys(
        range(0, rows_all, TILE),
        cross_flag(lengths_ref, tokens_ref),
        q_ref,
        k_ref,
        v_ref,
        ga_ref,
        lse_ref.at[0],
        deltas,
        dq_ref,
        dk_ref,
        dv_ref,
    )
    weights = jnp.concatenate([wq_ref[...], wk_ref[...], wv_ref[...]], axis=1)
    query_sum, value_sum = in_back_pair(
        dq_ref, dk_ref, dv_ref, weights, turned_ref, out_grad_ref, chunk_ref.at[0], total_ref
    )
    bias_ref[0, 0:1] = query_sum
    bias_ref[0, 1:2] = value_sum

    @pl.when(step == pl.num_programs(0) - 1)
    def _():
        gain_grad = jnp.zeros((1, total_ref.shape[1]), F32)
        shift_grad = jnp.zeros((1, total_ref.shape[1]), F32)
        for start in range(0, rows_all, TILE):
            rows = pl.ds(start, TILE)
            tokens_grad_ref[rows], gain_part, shift_part = tokens_back(
                tokens_ref[rows], total_ref[rows], grad_middle_ref[rows], gain_ref[...]
            )
            gain_grad = gain_grad + gain_part
            shift_grad = shift_grad + shift_part
        sums_ref[0:1] = gain_grad
        sums_ref[1:2] = shift_grad


def in_back(lengths, projected, ga, lse, delta, weights, first, out_grad, tokens, gain, grad_middle):
    rows, width = tokens.shape
    pairs = width // 128
    column = pl.BlockSpec((rows, 128), lambda p: (0, p))
    square = whole((rows, width))
    return pl.pallas_call(
        in_back_kernel,
        grid=(pairs,),
        in_specs=[
            pl.BlockSpec(memory_space=pltpu.SMEM),
            pl.BlockSpec((1, rows, 384), lambda p: (p, 0, 0)),
            column,
            pl.BlockSpec((1, 8, rows), lambda p: (p, 0, 0)),
            pl.BlockSpec((1, 2, rows), lambda p: (p, 0, 0)),
            pl.BlockSpec((width, 128), lambda p: (0, p)),
            pl.BlockSpec((width, 128), lambda p: (0, pairs + p)),
            pl.BlockSpec((width, 128), lambda p: (0, 2 * pairs + p)),
            square,
            column,
            square,
            whole((1, width)),
            square,
        ],
        out_specs=[
            pl.BlockSpec((1, 8, width // TILE, 32, 512), lambda p: (p, 0, 0, 0, 0)),
            pl.BlockSpec((1, 8, 128), lambda p: (p, 0, 0)),
            square,
            whole((8, width)),
        ],
        out_shape=[
            jax.ShapeDtypeStruct((pairs, 8, width // TILE, 32, 512), BF),
            jax.ShapeDtypeStruct((pairs, 8, 128), F32),
            jax.ShapeDtypeStruct((rows, width), BF),
            jax.ShapeDtypeStruct((8, width), F32),
        ],
        scratch_shapes=[
            pltpu.VMEM((rows, 128), F32),
            pltpu.VMEM((rows, 128), F32),
            pltpu.VMEM((rows, 128), F32),
            pltpu.VMEM((width, rows), BF),
            pltpu.VMEM((rows, width), F32),
        ],
        compiler_params=params(),
        name="in_back",
    )(
        lengths,
        projected,
        ga,
        lse,
        delta,
        weights,
        weights,
        weights,
        first,
        out_grad,
        tokens,
        gain,
        grad_middle,
    )


class Place:
    def __init__(self):
        self.z = lax.axis_index("dp")
        wide = lax.axis_index("wide")
        self.y = wide // 4
        self.x = (wide // 2) % 2
        self.c = wide % 2
        self.core = (self.z, wide + 1 - 2 * self.c)
        self.side = (self.z, wide + 2 - 4 * self.x)
        self.over = (self.z, wide + 4 - 8 * self.y)
        self.ranks = (self.z + 1 - 2 * (self.z % 2), (self.z + 2) % 4, 3 - self.z)
        self.planes = tuple((rank, wide) for rank in self.ranks)

    def greet(self, planes=True):
        barrier = pltpu.get_barrier_semaphore()
        peers = (self.core, self.side, self.over) + (self.planes if planes else ())
        for peer in peers:
            pl.semaphore_signal(barrier, inc=1, device_id=peer, device_id_type=MESH)
        pl.semaphore_wait(barrier, len(peers))


class WideGather:
    copies = 10

    def __init__(
        self, place, view, count, send, recv, first, source=None, last=None, offset=0, total=None
    ):
        y, x, c = place.y, place.x, place.c
        here, side, over, far = (y, x, c), (y, 1 - x, c), (1 - y, x, c), (1 - y, 1 - x, c)
        upper, lower = pl.ds(offset, count // 2), pl.ds(offset + count // 2, count // 2)
        both = pl.ds(offset, count)
        everything = both if total is None else pl.ds(0, total)

        def copy(index, slot, part, peer):
            destination = view(*slot, part)
            return pltpu.make_async_remote_copy(
                src_ref=source.at[part] if source is not None and slot is here else destination,
                dst_ref=destination,
                send_sem=send.at[first + index],
                recv_sem=recv.at[first + index],
                device_id=peer,
                device_id_type=MESH,
            )

        self.all = (
            copy(0, here, upper, place.side),
            copy(1, here, lower, place.over),
            copy(2, here, upper, place.over),
            copy(3, here, lower, place.side),
            None if total == 0 else copy(4, here, everything, place.core),
            copy(5, side, upper, place.over),
            copy(6, over, lower, place.side),
            copy(7, side, both, place.core),
            copy(8, over, both, place.core),
            copy(9, far, both, place.core),
        )
        self.own = None
        if source is not None and last is not None:
            self.own = pltpu.make_async_copy(source, view(*here, everything), last)

    def start(self):
        if self.own is not None:
            self.own.start()
        for copy in self.all[:5]:
            if copy is not None:
                copy.start()

    def relay(self, stage):
        waits, starts = (((0, 1), (5, 6)), ((2, 3), (7, 8)), ((5, 6), (9,)))[stage]
        for index in waits:
            self.all[index].wait_recv()
        for index in starts:
            self.all[index].start()

    def finish(self):
        for index in (4, 7, 8, 9):
            if self.all[index] is not None:
                self.all[index].wait_recv()
        for copy in self.all:
            if copy is not None:
                copy.wait_send()
        if self.own is not None:
            self.own.wait()


def blocks_of(target):
    return lambda y, x, c, rows: target.at[y, x, c, rows]


LAG = 2


class Reduction:
    slots = 2 * LAG
    deep = 3 * LAG
    keep = 3 * LAG + 2

    @classmethod
    def scratch(cls):
        n, k = cls.slots, cls.keep
        return [
            pltpu.VMEM((cls.deep, 2, 2, 4, 32, 512), BF),
            pltpu.VMEM((n, 2, 2, 4, 32, 512), BF),
            pltpu.VMEM((n, 2, 2, 4, 16, 512), BF),
            pltpu.VMEM((n, 2, 4, 16, 512), BF),
            pltpu.VMEM((n, 4, 32, 512), BF),
            pltpu.VMEM((n, 3, 32, 512), BF),
            pltpu.VMEM((n, 32, 512), BF),
            pltpu.VMEM((k, 3, 32, 512), BF),
            pltpu.SemaphoreType.DMA((6, k)),
            pltpu.SemaphoreType.DMA((6, k)),
            pltpu.SemaphoreType.DMA((cls.deep,)),
        ]

    def __init__(self, place, refs):
        self.place = place
        (
            self.chip,
            self.partner,
            self.first,
            self.second,
            self.plane,
            self.from_z,
            self.sums,
            self.shared,
            self.send,
            self.recv,
            self.local,
        ) = refs

    def copy(self, index, slot, source, target, peer):
        return pltpu.make_async_remote_copy(
            src_ref=source,
            dst_ref=target,
            send_sem=self.send.at[index, slot],
            recv_sem=self.recv.at[index, slot],
            device_id=peer,
            device_id_type=MESH,
        )

    def wait(self, index, slot, arrived):
        self.copy(index, slot, arrived, arrived, self.place.core).wait()

    def load(self, chunk, source):
        slot = chunk % self.deep
        return pltpu.make_async_copy(source, self.chip.at[slot], self.local.at[slot])

    def stage0(self, chunk, view):
        slot, c = chunk % self.slots, self.place.c
        self.copy(
            0, slot, view.at[:, :, 1 - c], self.partner.at[slot], self.place.core
        ).start()
        self.load(chunk, view.at[:, :, c]).start()

    def stage1(self, chunk):
        p, slot, index = self.place, chunk % self.slots, chunk % self.deep
        partner, chip, target = self.partner.at[slot], self.chip.at[index], self.first.at[slot]
        self.load(chunk, partner).wait()
        self.wait(0, slot, partner)
        chip[...] += partner[...]
        self.copy(1, slot, chip.at[:, 1 - p.x, :, pl.ds(0, 16)], target.at[0], p.side).start()
        self.copy(1, slot, chip.at[1 - p.y, :, :, pl.ds(16, 16)], target.at[1], p.over).start()

    def stage2(self, chunk):
        p, slot, index = self.place, chunk % self.slots, chunk % self.deep
        chip, arrived, target = self.chip.at[index], self.first.at[slot], self.second.at[slot]
        self.wait(1, slot, arrived)
        for k in range(2):
            chip[k, p.x, :, 0:16] += arrived[0, k]
            chip[p.y, k, :, 16:32] += arrived[1, k]
        self.copy(2, slot, chip.at[1 - p.y, p.x, :, pl.ds(0, 16)], target.at[0], p.over).start()
        self.copy(2, slot, chip.at[p.y, 1 - p.x, :, pl.ds(16, 16)], target.at[1], p.side).start()

    def stage3(self, chunk):
        p, slot, index = self.place, chunk % self.slots, chunk % self.deep
        arrived, mine, plane = self.second.at[slot], self.chip.at[index, p.y, p.x], self.plane
        self.wait(2, slot, arrived)
        plane[slot, :, 0:16] = mine[:, 0:16] + arrived[0]
        plane[slot, :, 16:32] = mine[:, 16:32] + arrived[1]
        for k in range(3):
            target = self.from_z.at[slot, k]
            self.copy(3, slot, plane.at[slot, p.ranks[k]], target, p.planes[k]).start()

    def stage4(self, chunk):
        slot = chunk % self.slots
        self.wait(3, slot, self.from_z.at[slot])
        total = self.plane[slot, self.place.z].astype(F32)
        for k in range(3):
            total = total + self.from_z[slot, k].astype(F32)
        return total

    def spread(self, chunk, total):
        slot, place = chunk % self.slots, chunk % self.keep
        self.sums[slot] = total.astype(BF)
        peer = self.place.planes[1]
        self.copy(4, place, self.sums.at[slot], self.shared.at[place, 0], peer).start()

    def stage5(self, chunk):
        slot, place, peer = chunk % self.slots, chunk % self.keep, self.place.planes[0]
        shared = self.shared.at[place]
        self.wait(4, place, shared.at[0])
        self.copy(5, place, self.sums.at[slot], shared.at[1], peer).start()
        self.copy(5, place, shared.at[0], shared.at[2], peer).start()

    def stage6(self, chunk):
        slot, place, ranks = chunk % self.slots, chunk % self.keep, self.place.ranks
        self.wait(5, place, self.shared.at[place, pl.ds(1, 2)])
        return [
            (self.place.z, self.sums[slot]),
            (ranks[1], self.shared[place, 0]),
            (ranks[0], self.shared[place, 1]),
            (ranks[2], self.shared[place, 2]),
        ]


class SmallReduction:
    @staticmethod
    def scratch():
        return [
            pltpu.VMEM((2, 2, 2, 4, 16, 512), BF),
            pltpu.VMEM((2, 2, 4, 16, 512), BF),
            pltpu.VMEM((2, 2, 4, 16, 512), BF),
            pltpu.VMEM((2, 4, 16, 512), BF),
            pltpu.VMEM((4, 16, 512), BF),
            pltpu.VMEM((3, 16, 512), BF),
            pltpu.SemaphoreType.DMA((4,)),
            pltpu.SemaphoreType.DMA((4,)),
        ]

    def __init__(self, place, refs):
        self.place = place
        self.source, self.chip, self.partner, self.first, self.second, self.from_z = refs[:6]
        self.send, self.recv = refs[6:]

    def copy(self, index, source, target, peer):
        return pltpu.make_async_remote_copy(
            src_ref=source,
            dst_ref=target,
            send_sem=self.send.at[index],
            recv_sem=self.recv.at[index],
            device_id=peer,
            device_id_type=MESH,
        )

    def wait(self, index, arrived):
        self.copy(index, arrived, arrived, self.place.core).wait()

    def stage0(self):
        p = self.place
        self.copy(0, self.source.at[:, :, 1 - p.c], self.partner, p.core).start()

    def stage1(self):
        p = self.place
        self.wait(0, self.partner)
        self.chip[...] = self.source[:, :, p.c] + self.partner[...]
        self.copy(1, self.chip.at[:, 1 - p.x], self.first, p.side).start()

    def stage2(self):
        p = self.place
        self.wait(1, self.first)
        for k in range(2):
            self.chip[k, p.x] += self.first[k]
        self.copy(2, self.chip.at[1 - p.y, p.x], self.second, p.over).start()

    def stage3(self):
        p = self.place
        self.wait(2, self.second)
        self.chip[p.y, p.x] += self.second[...]
        for k in range(3):
            block = self.chip.at[p.y, p.x, p.ranks[k]]
            self.copy(3, block, self.from_z.at[k], p.planes[k]).start()

    def stage4(self):
        p = self.place
        self.wait(3, self.from_z)
        total = self.chip[p.y, p.x, p.z].astype(F32)
        for k in range(3):
            total = total + self.from_z[k].astype(F32)
        return total


class Stream:
    def __init__(self, view, buffers, sems):
        self.view, self.buffers, self.sems = view, buffers, sems

    def copy(self, index):
        slot = index % 2
        return pltpu.make_async_copy(self.view(index), self.buffers.at[slot], self.sems.at[slot])

    def block(self, index):
        return self.buffers.at[index % 2]


def advance(streams, index, count):
    @pl.when(index + 1 < count)
    def _():
        for stream in streams:
            stream.copy(index + 1).start()

    for stream in streams:
        stream.copy(index).wait()


def dma_sems(count):
    return [pltpu.SemaphoreType.DMA((count,)), pltpu.SemaphoreType.DMA((count,))]


def to_planes(place, mine, landing, send, recv, first):
    return [
        pltpu.make_async_remote_copy(
            src_ref=mine,
            dst_ref=landing(k),
            send_sem=send.at[first + k],
            recv_sem=recv.at[first + k],
            device_id=place.planes[k],
            device_id_type=MESH,
        )
        for k in range(3)
    ]


class PlanesLast:
    copies = WideGather.copies + 6

    def __init__(self, place, source, target, send, recv, last):
        view = blocks_of(target.at[place.z])
        self.wide = WideGather(place, view, source.shape[0], send, recv, 0, source, last)

        def copy(index, rank, peer):
            blocks = target.at[rank, :, :, place.c]
            return pltpu.make_async_remote_copy(
                src_ref=blocks,
                dst_ref=blocks,
                send_sem=send.at[WideGather.copies + index],
                recv_sem=recv.at[WideGather.copies + index],
                device_id=peer,
                device_id_type=MESH,
            )

        self.across = [copy(k, place.z, place.planes[k]) for k in range(3)]
        self.over = [copy(3 + k, place.ranks[k], place.core) for k in range(3)]

    def start_across(self):
        self.wide.own.wait()
        for copy in self.across:
            copy.start()

    def start_over(self):
        for arrived, copy in zip(self.across, self.over):
            arrived.wait_recv()
            copy.start()

    def finish(self):
        self.wide.own = None
        self.wide.finish()
        for copy in self.across:
            copy.wait_send()
        for copy in self.over:
            copy.wait()


OUT_PROJ_AT, UP_AT, FORWARD_STEPS = 9, 13, 21


def forward_kernel(
    units,
    lengths_ref,
    tokens_ref,
    in_ref,
    vec_ref,
    out_ref,
    up_ref,
    unit_ref,
    down_ref,
    hs_ref,
    turned_ref,
    proj_ref,
    scaled_turned_ref,
    attended_ref,
    lse_ref,
    vectors_ref,
    scale_ref,
    branch_ref,
    middle_ref,
    feed_turned_ref,
    act_ref,
    slope_ref,
    stats_ref,
    in_all,
    out_all,
    up_all,
    unit_all,
    down_all,
    scaled_ref,
    out_held_ref,
    feed_ref,
    up_held_ref,
    unit_held_ref,
    sums_ref,
    held_ref,
    normed_ref,
    first_ref,
    vext_ref,
    send_in,
    recv_in,
    send_out,
    recv_out,
    send_ff,
    recv_ff,
    local,
    stream_sems,
):
    step = pl.program_id(0)
    place = Place()
    width = tokens_ref.shape[1]
    count = WideGather.copies
    lanes = (3 * width // 2 + 128, 3 * width // 2)
    across, early, late = [], [], None
    for group in range(2):
        held = held_ref.at[group, :, :, :, :, :, pl.ds(0, lanes[group])]
        first = group * (3 + 2 * count)

        def blocks(planes, held=held):
            return lambda y, x, c, rows: held.at[planes, y, x, c, rows]

        mine = held.at[0, place.y, place.x, place.c]
        across.append(
            to_planes(
                place,
                mine,
                lambda k, held=held: held.at[k + 1, place.y, place.x, place.c],
                send_in,
                recv_in,
                first,
            )
        )
        if group == 0:
            for part, planes in enumerate((pl.ds(0, 1), pl.ds(1, 3))):
                start = first + 3 + part * count
                early.append(WideGather(place, blocks(planes), 32, send_in, recv_in, start))
        else:
            late = WideGather(place, blocks(pl.ds(0, 4)), 32, send_in, recv_in, first + 3)
    orders = (place.z, *place.ranks)
    out = PlanesLast(place, out_ref, out_all, send_out, recv_out, local.at[2])

    def halves(source, target, first):
        size = source.shape[0] // 2
        return [
            WideGather(
                place,
                blocks_of(target),
                size,
                send_ff,
                recv_ff,
                first + part * count,
                source,
                None,
                part * size,
            )
            for part in range(2)
        ]

    ups = halves(up_ref, up_all, count)
    downs = halves(down_ref, down_all, 3 * count)
    keep_own = [
        pltpu.make_async_copy(source, target.at[place.y, place.x, place.c], local.at[sem])
        for source, target, sem in ((up_ref, up_all, 3), (down_ref, down_all, 6))
    ]
    fetch_out = pltpu.make_async_copy(out_all, out_held_ref, local.at[0])
    fetch_unit = pltpu.make_async_copy(unit_all, unit_held_ref, local.at[7])
    up_stream = Stream(
        lambda i: up_all.at[i // 4, i // 2 % 2, i % 2], up_held_ref, stream_sems
    )
    unit = WideGather(
        place, blocks_of(unit_all), 32, send_ff, recv_ff, 0, unit_ref, local.at[4]
    )
    keep = [
        pltpu.make_async_copy(
            held_ref.at[group, index, :, :, :, :, pl.ds(0, lanes[1])],
            in_all.at[rank, :, :, :, :, pl.ds(group * lanes[1], lanes[1])],
            local.at[12 + 4 * group + index],
        )
        for group in range(2)
        for index, rank in enumerate(orders)
    ]

    @pl.when(step == 0)
    def _():
        place.greet()
        half = width // 2
        for group in range(2):
            mine = held_ref.at[group, 0, place.y, place.x, place.c]
            fills = []
            for pair in range(4):
                for part in range(3):
                    column = part * width + (4 * group + pair) * 128
                    fills.append(
                        pltpu.make_async_copy(
                            in_ref.at[:, pl.ds(column, 128)],
                            mine.at[:, pl.ds(pair * 384 + part * 128, 128)],
                            local.at[20 + group * 12 + pair * 3 + part],
                        )
                    )
            for copy in fills:
                copy.start()
            if group == 0:
                mine[:, 3 * half : 3 * half + 128] = jnp.zeros((32, 128), BF)
                mine[:, 3 * half : 3 * half + 32] = vec_ref[...]
            for copy in fills:
                copy.wait()
            for copy in across[group]:
                copy.start()
            if group == 0:
                early[0].start()
        for copy in keep_own:
            copy.start()
        ups[0].start()
        scale = hs_ref[...].astype(F32)
        for pair in range(width // 128):
            own = slice(pair * 128, (pair + 1) * 128)
            low_lanes = lax.broadcasted_iota(jnp.int32, (1, 128), 1) < 64
            scale_ref[0:1, own] = jnp.where(
                low_lanes, scale[:, 2 * pair : 2 * pair + 1], scale[:, 2 * pair + 1 : 2 * pair + 2]
            )
        for start in range(0, tokens_ref.shape[0], TILE):
            rows = pl.ds(start, TILE)
            normed, _ = row_norm(tokens_ref[rows].astype(F32))
            normed_ref[rows] = normed
        early[0].relay(0)
        for copy in across[0]:
            copy.wait_recv()
        early[1].start()
        early[0].relay(1)
        early[0].relay(2)
        early[1].relay(0)
        early[1].relay(1)
        for copy in across[1]:
            copy.wait_recv()
        late.start()
        early[1].relay(2)
        out.wide.start()
        unit.start()
        for part in early:
            part.finish()
        for z in range(4):
            for y in range(2):
                tile = jnp.zeros((16, 128), F32)
                for x in range(2):
                    for c in range(2):
                        piece = held_ref[
                            0, orders[z], y, x, c, 0:16, 3 * half : 3 * half + 128
                        ].astype(F32)
                        spot = 32 * (2 * x + c)
                        tile = tile + (piece if spot == 0 else pltpu.roll(piece, spot, 1))
                vectors_ref[:, (2 * z + y) * 128 : (2 * z + y + 1) * 128] = tile
        for start in range(0, tokens_ref.shape[0], TILE):
            rows = pl.ds(start, TILE)
            first_ref[rows] = (normed_ref[rows] * vectors_ref[3:4] + vectors_ref[4:5]).astype(BF)

    def at(index, *actions):
        @pl.when(step == index)
        def _():
            for action in actions:
                action()

    def relay(index, stage, *items):
        at(index, *[functools.partial(item.relay, stage) for item in items])

    relay(2, 0, late, out.wide, unit)
    relay(3, 1, late, out.wide, unit)
    relay(3, 0, ups[0])
    relay(4, 2, late, out.wide, unit)
    at(4, out.start_across, ups[1].start)
    relay(5, 1, ups[0])
    at(5, late.finish, unit.finish, fetch_unit.start, *[copy.start for copy in keep])
    relay(6, 2, ups[0])
    relay(6, 0, ups[1])
    at(7, out.start_over)
    relay(8, 1, ups[1])
    at(8, out.finish, fetch_out.start)
    at(9, fetch_out.wait, fetch_unit.wait, downs[0].start)
    relay(10, 2, ups[1])
    at(11, downs[1].start)
    relay(12, 0, downs[0])
    at(UP_AT, keep_own[0].wait, ups[0].finish, ups[1].finish, up_stream.copy(0).start)
    relay(14, 1, downs[0])
    relay(15, 2, downs[0])
    relay(15, 0, downs[1])
    relay(17, 1, downs[1])
    relay(19, 2, downs[1])

    @pl.when((step > 0) & (step < OUT_PROJ_AT))
    def _():
        pair = step - 1
        columns = pl.ds(pl.multiple_of(pair % 4 * 384, 128), 384)
        weights = jnp.concatenate(
            [held_ref[pair // 4, order, :, :, :, :, columns].reshape(TILE, 384) for order in orders]
        )
        own = pl.ds(pl.multiple_of(pair * 128, 128), 128)
        bias = jnp.concatenate(
            [vectors_ref[0:1, own], jnp.zeros((1, 128), F32), vectors_ref[1:2, own]], axis=1
        )
        project_pair(first_ref, weights, bias, proj_ref)
        attention_pair(
            cross_flag(lengths_ref, tokens_ref),
            *three(proj_ref),
            scale_ref[0:1, own],
            scaled_ref.at[:, own],
            attended_ref,
            lse_ref,
            vext_ref,
        )
        scaled_turned_ref[...] = scaled_ref[:, own].T

    @pl.when(step == OUT_PROJ_AT)
    def _():
        turned_ref[...] = first_ref[...].T
        sums_ref[...] = jnp.zeros_like(sums_ref)

    @pl.when((step >= OUT_PROJ_AT) & (step < UP_AT))
    def _():
        rows = pl.ds(pl.multiple_of((step - OUT_PROJ_AT) * TILE, TILE), TILE)
        feed_ref[rows] = out_proj_rows(
            scaled_ref[rows],
            out_held_ref[...].reshape(width, width),
            vectors_ref,
            tokens_ref[rows],
            branch_ref,
            middle_ref,
        )

    @pl.when(step >= UP_AT)
    def _():
        block = step - UP_AT
        advance((up_stream,), block, FORWARD_STEPS - UP_AT)
        up_step(
            feed_ref,
            up_stream.block(block),
            unit_held_ref.at[block // 4, block // 2 % 2, block % 2],
            act_ref,
            slope_ref,
            sums_ref,
        )

    @pl.when(step == FORWARD_STEPS - 1)
    def _():
        up_stats(units, stats_ref, sums_ref)
        feed_turned_ref[...] = feed_ref[...].T
        for copy in (*across[0], *across[1]):
            copy.wait_send()
        for copy in (*keep, keep_own[1]):
            copy.wait()
        for part in downs:
            part.finish()


def forward_part(
    lengths, tokens, in_weight, vec, out_weight, up_weight, unit_rows, down_weight, head_scale
):
    rows, width = tokens.shape
    pairs = width // 128
    steps = 8

    def between(low, high):
        return lambda s: jnp.minimum(jnp.maximum(s - low, 0), high - low - 1)

    pair, row, unit = between(1, OUT_PROJ_AT), between(OUT_PROJ_AT, UP_AT), between(UP_AT, FORWARD_STEPS)
    by_row = pl.BlockSpec((TILE, width), lambda s: (row(s), 0))
    block = pl.BlockSpec((1, rows, UNITS), lambda s: (unit(s), 0, 0))
    held = (2, 4, 2, 2, 2, 32, 3 * width // 2 + 128)
    return pl.pallas_call(
        functools.partial(forward_kernel, steps * UNITS),
        grid=(FORWARD_STEPS,),
        in_specs=[
            pl.BlockSpec(memory_space=pltpu.SMEM),
            whole((rows, width)),
            ANY,
            whole(vec.shape),
            ANY,
            ANY,
            ANY,
            ANY,
            whole(head_scale.shape),
        ],
        out_specs=[
            whole((width, rows)),
            pl.BlockSpec((1, rows, 384), lambda s: (pair(s), 0, 0)),
            pl.BlockSpec((128, rows), lambda s: (pair(s), 0)),
            pl.BlockSpec((rows, 128), lambda s: (0, pair(s))),
            pl.BlockSpec((1, 8, rows), lambda s: (pair(s), 0, 0)),
            whole((16, width)),
            whole((8, width)),
            by_row,
            by_row,
            whole((width, rows)),
            block,
            block,
            whole((rows, 128)),
            *[ANY] * 5,
        ],
        out_shape=[
            jax.ShapeDtypeStruct((width, rows), BF),
            jax.ShapeDtypeStruct((pairs, rows, 384), BF),
            jax.ShapeDtypeStruct((width, rows), BF),
            jax.ShapeDtypeStruct((rows, width), F32),
            jax.ShapeDtypeStruct((pairs, 8, rows), F32),
            jax.ShapeDtypeStruct((16, width), F32),
            jax.ShapeDtypeStruct((8, width), F32),
            jax.ShapeDtypeStruct((rows, width), F32),
            jax.ShapeDtypeStruct((rows, width), F32),
            jax.ShapeDtypeStruct((width, rows), BF),
            jax.ShapeDtypeStruct((steps, rows, UNITS), BF),
            jax.ShapeDtypeStruct((steps, rows, UNITS), BF),
            jax.ShapeDtypeStruct((rows, 128), F32),
            jax.ShapeDtypeStruct((4, 2, 2, 2, 32, 3 * width), BF),
            jax.ShapeDtypeStruct((4, 2, 2, 2, *out_weight.shape), BF),
            jax.ShapeDtypeStruct((2, 2, 2, *up_weight.shape), BF),
            jax.ShapeDtypeStruct((2, 2, 2, *unit_rows.shape), BF),
            jax.ShapeDtypeStruct((2, 2, 2, *down_weight.shape), BF),
        ],
        scratch_shapes=[
            pltpu.VMEM((rows, width), BF),
            pltpu.VMEM((4, 2, 2, 2, *out_weight.shape), BF),
            pltpu.VMEM((rows, width), BF),
            pltpu.VMEM((2, *up_weight.shape), BF),
            pltpu.VMEM((2, 2, 2, *unit_rows.shape), BF),
            pltpu.VMEM((2, rows, 128), F32),
            pltpu.VMEM(held, BF),
            pltpu.VMEM((rows, width), F32),
            pltpu.VMEM((rows, width), BF),
            pltpu.VMEM((rows, 256), BF),
            *dma_sems(6 + 3 * WideGather.copies),
            *dma_sems(PlanesLast.copies),
            *dma_sems(5 * WideGather.copies),
            pltpu.SemaphoreType.DMA((44,)),
            pltpu.SemaphoreType.DMA((2,)),
        ],
        compiler_params=params(collective_id=0, has_side_effects=True),
        name="forward_part",
    )(lengths, tokens, in_weight, vec, out_weight, up_weight, unit_rows, down_weight, head_scale)


NORMS_AT, COLUMNS_AT, HEADS_AT, TOKENS_AT, VECTORS_AT = 8, 16, 20, 28, 32
BACK_STEPS = VECTORS_AT + 7
OUT_TILE = 128


def chunk_at(time):
    chunk = jnp.where(time < 13, time, time - 1)
    chunk = jnp.where(time >= 20, (time + 17) // 2, chunk)
    return chunk, (time >= 0) & ((time < 13) | ((time >= 14) & (time < 20)) | ((time >= 20) & (time < 30) & (time % 2 == 1)))


def back_kernel(
    lengths_ref,
    unit_grad_ref,
    vec_ref,
    hs_ref,
    act_all,
    slope_all,
    e_all,
    stats_all,
    up_all,
    feed_turned_all,
    down_grad_all,
    cot_all,
    middle_all,
    branch_all,
    scaled_turned_all,
    attended_all,
    out_weight_all,
    proj_all,
    lse_all,
    in_weight_all,
    turned_all,
    tokens_all,
    down_out,
    up_out,
    in_out,
    out_out,
    vec_out,
    tokens_grad_all,
    up_grad_all,
    units_in_ref,
    up_ref,
    stats_ref,
    feed_turned_ref,
    cot_ref,
    norms_in_ref,
    scaled_turned_ref,
    attended_ref,
    out_weight_ref,
    proj_ref,
    lse_ref,
    in_weight_ref,
    turned_ref,
    tokens_ref,
    tokens_grad_ref,
    staged_ref,
    total_ref,
    low_ref,
    out_grad_ref,
    ga_ref,
    grad_middle_ref,
    delta_ref,
    delta_sum_ref,
    sums_ref,
    units_ref,
    dq_ref,
    dk_ref,
    dv_ref,
    chunk_ref,
    stream_sems,
    fetch_sems,
    *scratch,
):
    step = pl.program_id(0)
    place = Place()
    engine = Reduction(place, scratch[:11])
    small = SmallReduction(place, scratch[11:])
    pairs = proj_all.shape[0]

    def rows_of(array, size):
        return lambda i: array.at[pl.ds(pl.multiple_of(i * size, size), size)]

    def columns_of(array, size):
        return lambda i: array.at[:, pl.ds(pl.multiple_of(i * size, size), size)]

    def stream(number, view, buffers):
        return Stream(view, buffers, stream_sems.at[number])

    act, slope, e = (
        stream(k, lambda i, array=array: array.at[i], units_in_ref.at[k])
        for k, array in enumerate((act_all, slope_all, e_all))
    )
    up = stream(3, lambda i: up_all.at[i], up_ref)
    cot = stream(4, rows_of(cot_all, OUT_TILE), cot_ref)
    middle = stream(5, rows_of(middle_all, OUT_TILE), norms_in_ref.at[0])
    branch = stream(6, rows_of(branch_all, OUT_TILE), norms_in_ref.at[1])
    attended = stream(7, columns_of(attended_all, TILE), attended_ref)
    proj = stream(8, lambda i: proj_all.at[i], proj_ref)
    lse = stream(9, lambda i: lse_all.at[i], lse_ref)
    in_weight = stream(10, columns_of(in_weight_all, 384), in_weight_ref)
    tokens = stream(11, rows_of(tokens_all, TILE), tokens_ref)
    put = rows_of(tokens_grad_all, TILE)

    def put_tokens(i):
        return pltpu.make_async_copy(
            tokens_grad_ref.at[i % 2], put(i), stream_sems.at[12, i % 2]
        )

    fetches = [
        pltpu.make_async_copy(source, target, fetch_sems.at[index])
        for index, (source, target) in enumerate(
            (
                (stats_all, stats_ref),
                (feed_turned_all, feed_turned_ref),
                (scaled_turned_all, scaled_turned_ref),
                (out_weight_all, out_weight_ref),
                (turned_all, turned_ref),
            )
        )
    ]

    @pl.when(step == 0)
    def _():
        for item in (act, slope, e, up):
            item.copy(0).start()
        for copy in fetches:
            copy.start()
        for item in (cot, middle, branch, attended, proj, lse, in_weight, tokens):
            item.copy(0).start()
        total_ref[...] = jnp.zeros_like(total_ref)
        sums_ref[...] = jnp.zeros_like(sums_ref)
        units_ref[...] = jnp.zeros_like(units_ref)
        place.greet()

    def store(block):
        view = up_grad_all.at[block // 4, block // 2 % 2, block % 2]
        return pltpu.make_async_copy(staged_ref, view, fetch_sems.at[5])

    @pl.when((step >= 1) & (step <= NORMS_AT))
    def _():
        store(step - 1).wait()


    def stage(number, kind, action, tick):
        chunk, there = chunk_at(tick - number * LAG)
        up = ((chunk >= 8) & (chunk < 14)) | (chunk == 15) | (chunk == 17)
        wanted = {
            "all": there,
            "down": there & (chunk < 8),
            "up": there & up,
            "shared": there & ((chunk < 8) | up),
            "own": there & (chunk >= 8) & ~up,
        }

        @pl.when(wanted[kind])
        def _():
            action(chunk)

    def up_index(chunk):
        return jnp.where(chunk < 14, chunk - 8, (chunk - 3) // 2)

    def pair_index(chunk):
        return jnp.where(chunk < 18, (chunk - 14) // 2, chunk - 16)

    def put_down(chunk):
        for rank, block in engine.stage6(chunk):
            for half in range(2):

                @pl.when(chunk % 2 == half)
                def _():
                    down_out[chunk // 2, rank, :, half * 512 : half * 512 + 512] = block

    def put_up(chunk):
        for rank, block in engine.stage6(chunk):
            up_out[up_index(chunk), rank] = block

    def put_own(chunk):
        total = engine.stage4(chunk)
        first = pair_index(chunk) * 128
        for part in range(3):
            lanes = pl.ds(pl.multiple_of(part * 1024 + first, 128), 128)
            in_out[:, lanes] = total[:, part * 128 : part * 128 + 128]
        out_out[:, pl.ds(pl.multiple_of(first, 128), 128)] = total[:, 384:512]

    def take_down(chunk):
        lanes = pl.ds(pl.multiple_of(chunk % 2 * 512, 512), 512)
        engine.stage0(chunk, down_grad_all.at[:, :, :, chunk // 2, :, :, lanes])

    def take_up(chunk):
        engine.stage0(chunk, up_grad_all.at[:, :, :, up_index(chunk)])

    def take_own(chunk):
        engine.stage0(chunk, chunk_ref.at[pair_index(chunk) % 2])

    def reduce_step(tick):
        stage(6, "down", put_down, tick)
        stage(6, "up", put_up, tick)
        stage(5, "shared", engine.stage5, tick)
        stage(4, "shared", lambda chunk: engine.spread(chunk, engine.stage4(chunk)), tick)
        stage(4, "own", put_own, tick)
        stage(3, "all", engine.stage3, tick)
        stage(2, "all", engine.stage2, tick)
        stage(1, "all", engine.stage1, tick)
        stage(0, "down", take_down, tick)
        stage(0, "up", take_up, tick)

    tick = jnp.where(step < NORMS_AT, step, NORMS_AT + (step - NORMS_AT) // 4)
    tick = jnp.where(step < COLUMNS_AT, tick, step - 6)
    tick = jnp.where(step < HEADS_AT, tick, 2 * step - 26)
    tick = jnp.where(step < TOKENS_AT, tick, 30)
    tick = jnp.where(step < VECTORS_AT, tick, step - 1)
    within = (step > NORMS_AT) & (step < COLUMNS_AT) & (step % 4 != 0)
    within = within | ((step > TOKENS_AT) & (step < VECTORS_AT))

    @pl.when(~within)
    def _():
        reduce_step(tick)


    @pl.when(step < NORMS_AT)
    def _():
        advance((act, slope, e, up), step, NORMS_AT)

        @pl.when(step == 0)
        def _():
            fetches[0].wait()

        units_ref[step, 0:1] = up_back_step(
            act.block(step),
            slope.block(step),
            e.block(step),
            stats_ref,
            up.block(step),
            low_ref,
            total_ref,
        )
        units_ref[step, 1:3] = unit_grad_ref[step, 0:2]

        @pl.when(step == 0)
        def _():
            fetches[1].wait()

        for left in range(0, UNITS, TILE):
            columns = slice(left, left + TILE)
            grad = dot_nn(feed_turned_ref[...], low_ref[:, columns]).astype(BF)
            staged_ref[:, :, :, columns] = grad.reshape(8, 4, 32, TILE)
        store(step).start()


    @pl.when((step >= NORMS_AT) & (step < COLUMNS_AT))
    def _():
        block = step - NORMS_AT
        rows = pl.ds(pl.multiple_of(block * OUT_TILE, OUT_TILE), OUT_TILE)
        advance((cot, middle, branch), block, COLUMNS_AT - NORMS_AT)
        grad_middle, low = norms_back(
            total_ref[rows],
            cot.block(block),
            middle.block(block),
            branch.block(block),
            vec_ref,
            sums_ref,
        )
        grad_middle_ref[rows] = grad_middle
        low_ref[rows] = low

    @pl.when((step >= COLUMNS_AT) & (step < HEADS_AT))
    def _():
        block = step - COLUMNS_AT
        columns = pl.ds(pl.multiple_of(block * TILE, TILE), TILE)
        advance((attended,), block, HEADS_AT - COLUMNS_AT)

        @pl.when(block == 0)
        def _():
            fetches[2].wait()
            fetches[3].wait()

        grad_out, delta = heads_back(
            low_ref[...],
            out_weight_ref[columns],
            hs_ref[0:1, columns],
            attended.block(block)[...],
        )
        ga_ref[:, columns] = grad_out
        delta_sum_ref[block, 0:1] = column_sum(delta)
        turned = delta.T
        for head in range(4):
            delta_ref[4 * block + head] = turned[head : head + 1]
        out_grad_ref[:, columns] = dot_nn(scaled_turned_ref[...], low_ref[:, columns]).astype(BF)

    @pl.when(step == HEADS_AT - 1)
    def _():
        total_ref[...] = jnp.zeros_like(total_ref)


    @pl.when((step >= HEADS_AT) & (step < TOKENS_AT))
    def _():
        pair = step - HEADS_AT
        columns = pl.ds(pl.multiple_of(pair * 128, 128), 128)
        advance((proj, lse, in_weight), pair, pairs)

        @pl.when(pair == 0)
        def _():
            fetches[4].wait()

        for part, starts in enumerate(((0, 3 * TILE), (TILE, 2 * TILE))):
            if part == 1:
                reduce_step(tick + 1)
            attention_back_keys(
                starts,
                cross_flag(lengths_ref, total_ref),
                *[proj.block(pair).at[:, pl.ds(index * 128, 128)] for index in range(3)],
                ga_ref.at[:, columns],
                lse.block(pair),
                [delta_ref[2 * pair], delta_ref[2 * pair + 1]],
                dq_ref,
                dk_ref,
                dv_ref,
            )
        query_sum, value_sum = in_back_pair(
            dq_ref,
            dk_ref,
            dv_ref,
            in_weight.block(pair)[...],
            turned_ref,
            out_grad_ref.at[:, columns],
            chunk_ref.at[pair % 2].reshape(8, 4, 32, 512),
            total_ref,
        )
        sums_ref[0:1, columns] = query_sum
        sums_ref[1:2, columns] = value_sum
        stage(0, "own", take_own, tick + 1)

    @pl.when((step >= TOKENS_AT) & (step < TOKENS_AT + 4))
    def _():
        block = step - TOKENS_AT
        rows = pl.ds(pl.multiple_of(block * TILE, TILE), TILE)
        advance((tokens,), block, 4)

        @pl.when(block >= 2)
        def _():
            put_tokens(block - 2).wait()

        result, gain_grad, shift_grad = tokens_back(
            tokens.block(block)[...], total_ref[rows], grad_middle_ref[rows], vec_ref[3:4]
        )
        tokens_grad_ref[block % 2] = result
        put_tokens(block).start()
        sums_ref[3:4] += gain_grad
        sums_ref[4:5] += shift_grad


    @pl.when(step == VECTORS_AT)
    def _():
        for y in range(2):
            for z in range(4):
                own = slice((2 * z + y) * 128, (2 * z + y + 1) * 128)
                for index in range(9):
                    lanes = slice(index % 4 * 128, index % 4 * 128 + 128)
                    row = 6 + index // 4
                    units_ref[8, row : row + 1, lanes] = sums_ref[index : index + 1, own]
                for x in range(2):
                    for c in range(2):
                        unit = 4 * y + 2 * x + c
                        units_ref[8, 0:3] = units_ref[unit, 0:3]
                        if (y, z, x, c) == (0, 0, 0, 0):
                            units_ref[8, 3:4] = sums_ref[9:10, 0:UNITS]
                            units_ref[8, 4:5] = sums_ref[9:10, UNITS : 2 * UNITS]
                            for block in range(4):
                                lanes = slice(block * 128, block * 128 + 128)
                                units_ref[8, 5:6, lanes] = delta_sum_ref[block, 0:1]
                        small.source[y, x, c, z] = units_ref[8].astype(BF)
        small.stage0()

    for index, action in enumerate((small.stage1, small.stage2, small.stage3)):

        @pl.when(step == VECTORS_AT + 1 + index)
        def _():
            action()

    @pl.when(step == VECTORS_AT + 4)
    def _():
        vec_out[...] = small.stage4()
        for block in range(2, 4):
            put_tokens(block).wait()


def back_part(
    lengths,
    act,
    slope,
    e,
    stats,
    up,
    feed_turned,
    unit_grad,
    down_grad,
    cotangent,
    middle,
    branch,
    scaled_turned,
    attended,
    out_weights,
    vectors,
    head_lanes,
    projected,
    lse,
    weights,
    turned,
    tokens,
):
    rows, width = tokens.shape
    pairs = width // 128

    return pl.pallas_call(
        back_kernel,
        grid=(BACK_STEPS,),
        in_specs=[
            pl.BlockSpec(memory_space=pltpu.SMEM),
            whole(unit_grad.shape),
            whole(vectors.shape),
            whole(head_lanes.shape),
            *[ANY] * 18,
        ],
        out_specs=[
            whole((4, 4, 32, 1024)),
            whole((8, 4, 32, 512)),
            whole((32, 3 * width)),
            whole((32, width)),
            whole((16, 512)),
            ANY,
            ANY,
        ],
        out_shape=[
            jax.ShapeDtypeStruct((4, 4, 32, 1024), BF),
            jax.ShapeDtypeStruct((8, 4, 32, 512), BF),
            jax.ShapeDtypeStruct((32, 3 * width), F32),
            jax.ShapeDtypeStruct((32, width), F32),
            jax.ShapeDtypeStruct((16, 512), F32),
            jax.ShapeDtypeStruct((rows, width), BF),
            jax.ShapeDtypeStruct((2, 2, 2, 8, 4, 32, UNITS), BF),
        ],
        scratch_shapes=[
            pltpu.VMEM((3, 2, rows, UNITS), BF),
            pltpu.VMEM((2, width, UNITS), BF),
            pltpu.VMEM((rows, 128), F32),
            pltpu.VMEM((width, rows), BF),
            pltpu.VMEM((2, OUT_TILE, width), BF),
            pltpu.VMEM((2, 2, OUT_TILE, width), F32),
            pltpu.VMEM((width, rows), BF),
            pltpu.VMEM((2, rows, TILE), F32),
            pltpu.VMEM((width, width), BF),
            pltpu.VMEM((2, rows, 384), BF),
            pltpu.VMEM((2, 8, rows), F32),
            pltpu.VMEM((2, width, 384), BF),
            pltpu.VMEM((width, rows), BF),
            pltpu.VMEM((2, TILE, width), BF),
            pltpu.VMEM((2, TILE, width), BF),
            pltpu.VMEM((8, 4, 32, UNITS), BF),
            pltpu.VMEM((rows, width), F32),
            pltpu.VMEM((rows, width), BF),
            pltpu.VMEM((width, width), BF),
            pltpu.VMEM((rows, width), BF),
            pltpu.VMEM((rows, width), F32),
            pltpu.VMEM((2 * pairs, 1, rows), F32),
            pltpu.VMEM((4, 8, 128), F32),
            pltpu.VMEM((16, width), F32),
            pltpu.VMEM((9, 16, UNITS), F32),
            pltpu.VMEM((rows, 128), F32),
            pltpu.VMEM((rows, 128), F32),
            pltpu.VMEM((rows, 128), F32),
            pltpu.VMEM((2, 2, 2, 2, 4, 32, 512), BF),
            pltpu.SemaphoreType.DMA((13, 2)),
            pltpu.SemaphoreType.DMA((6,)),
            *Reduction.scratch(),
            *SmallReduction.scratch(),
        ],
        compiler_params=params(collective_id=1, has_side_effects=True),
        name="back_part",
    )(
        lengths,
        unit_grad,
        vectors,
        head_lanes,
        act,
        slope,
        e,
        stats,
        up,
        feed_turned,
        down_grad.reshape(2, 2, 2, 4, 4, 32, width),
        cotangent,
        middle,
        branch,
        scaled_turned,
        attended,
        out_weights,
        projected,
        lse,
        weights,
        turned,
        tokens,
    )


def layer(staged, tokens, cotangent, lengths, attn, up, down, unit_vec, head_scale, down_bias):
    rows, width = tokens.shape
    heads = head_scale.shape[0]
    pairs = width // 128
    if staged:
        in_weight, out_weight, vec_block = attn
        (
            turned,
            projected,
            scaled_turned,
            attended,
            lse,
            vectors,
            head_lanes,
            branch,
            middle,
            feed_turned,
            act,
            slope,
            stats,
            weights,
            out_weights,
            up,
            unit_vec,
            down,
        ) = forward_part(
            lengths,
            tokens,
            in_weight,
            vec_block,
            out_weight,
            up,
            unit_vec,
            down,
            head_scale[None, :],
        )
        weights = weights.reshape(width, 3 * width)
        out_weights = out_weights.reshape(width, width)
        up = up.reshape(-1, width, UNITS)
        unit_vec = unit_vec.reshape(-1, unit_vec.shape[-2], UNITS)
        down = down.reshape(-1, UNITS, width)
    else:
        weights, out_weights, vectors = attn
        scale = head_scale.astype(F32)
        head_lanes = jnp.repeat(scale, width // heads)[None, :]
        first, projected, scaled, attended, lse = plain_first(
            lengths, tokens, weights, vectors, head_lanes
        )
        branch, middle, feed = out_proj(scaled, out_weights, vectors, tokens)
        act, slope, stats = up_pass(feed, up, unit_vec)
    mixed, down_grad, e, stats, unit_grad = down_pass(
        act, stats, unit_vec, down, cotangent, middle, down_bias[None, :]
    )
    if staged:
        down_total, up_total, in_total, out_total, vec_shares, tokens_grad, _ = back_part(
            lengths,
            act,
            slope,
            e,
            stats,
            up,
            feed_turned,
            unit_grad,
            down_grad,
            cotangent,
            middle,
            branch,
            scaled_turned,
            attended,
            out_weights,
            vectors,
            head_lanes,
            projected,
            lse,
            weights,
            turned,
            tokens,
        )
        return mixed, tokens_grad, down_total, up_total, in_total, out_total, vec_shares
    up_grad, up_bias_grad, grad_feed = up_back(
        act, slope, e, stats, up, feed
    )
    grad_middle, ga, out_grad, delta, sums = out_back(
        grad_feed,
        cotangent,
        middle,
        branch,
        scaled,
        attended,
        out_weights,
        vectors,
        head_lanes,
    )
    chunks, proj_bias, tokens_grad, pre_sums = in_back(
        lengths,
        projected,
        ga,
        lse,
        delta.reshape(pairs, 2, rows),
        weights,
        first,
        out_grad,
        tokens,
        vectors[3:4],
        grad_middle,
    )
    scale_grad = jnp.sum(delta, axis=1) / scale
    vec_grads = [
        proj_bias[:, 0].reshape(width),
        proj_bias[:, 1].reshape(width),
        sums[2],
        pre_sums[0],
        pre_sums[1],
        sums[5],
        sums[6],
        sums[7],
        sums[8],
    ]
    unit_grads = [up_bias_grad[:, 0], unit_grad[:, 0], unit_grad[:, 1]]
    return mixed, tokens_grad, chunks, up_grad, down_grad, vec_grads, unit_grads, sums[9], scale_grad


def body(
    axes,
    tokens,
    cotangent,
    lengths,
    in_weight,
    query_bias,
    value_bias,
    out_weight,
    out_bias,
    head_scale,
    pre_gain,
    pre_bias,
    post_gain,
    post_bias,
    feed_gain,
    feed_bias,
    up_weight,
    up_bias,
    mid_gain,
    mid_bias,
    down_weight,
    down_bias,
):
    planes, wide = axes
    every = ("dp", "wide")
    staged = (planes, wide) == (4, 8)
    rows, width = tokens.shape
    units = down_weight.shape[0] * wide
    steps = units // UNITS
    share = in_weight.shape[0]
    columns = [
        query_bias,
        value_bias,
        out_bias,
        pre_gain,
        pre_bias,
        post_gain,
        post_bias,
        feed_gain,
        feed_bias,
    ]
    index = lax.broadcasted_iota(jnp.int32, (32, up_bias.shape[0]), 0)
    unit_rows = jnp.where(index == 0, up_bias[None, :], jnp.zeros((), BF))
    unit_rows = jnp.where(index == 1, mid_gain[None, :], unit_rows)
    unit_rows = jnp.where(index == 2, mid_bias[None, :], unit_rows)
    if staged:
        index = lax.broadcasted_iota(jnp.int32, (32, share), 0)
        vec_block = jnp.zeros((32, share), BF)
        for row, column in enumerate(columns):
            vec_block = jnp.where(index == row, column[None, :], vec_block)
        attn = (in_weight, out_weight, vec_block)
        up, unit_vec, down = up_weight, unit_rows, down_weight
    else:
        flat = jnp.concatenate(columns).reshape(len(columns), share)
        attn = (
            lax.all_gather(in_weight, every, axis=0, tiled=True),
            lax.all_gather(out_weight, every, axis=0, tiled=True),
            jnp.pad(
                lax.all_gather(flat, every, axis=1, tiled=True), ((0, 16 - len(columns)), (0, 0))
            ).astype(F32),
        )
        up = lax.all_gather(up_weight, "wide", axis=1, tiled=True)
        up = up.reshape(width, steps, UNITS).transpose(1, 0, 2)
        unit_vec = lax.all_gather(unit_rows, "wide", axis=1, tiled=True)
        unit_vec = unit_vec.reshape(32, steps, UNITS).transpose(1, 0, 2)
        down = lax.all_gather(down_weight, "wide", axis=0, tiled=True)
        down = down.reshape(steps, UNITS, width)
    results = layer(
        staged,
        tokens,
        cotangent,
        lengths,
        attn,
        up,
        down,
        unit_vec,
        head_scale,
        down_bias,
    )
    heads = head_scale.shape[0]
    pairs = width // 128
    if staged:
        mixed, tokens_grad, down_total, up_total, in_total, out_total, vec_shares = results
        up_total = up_total.astype(F32).reshape(width, UNITS)
        down_total = down_total.astype(F32).reshape(UNITS, width)
        unit_totals = [vec_shares[index] for index in range(3)]
        down_sum = vec_shares[3:5].reshape(width)
        scale_sum = vec_shares[5].reshape(4, 128)[:, :4].reshape(heads) / head_scale.astype(F32)
        offset = share * lax.rem(lax.axis_index("wide"), 128 // share)
        own = vec_shares[6:9].reshape(12, 128)
        own = lax.dynamic_slice(own, (0, offset), (len(columns), share))
        vec_totals = [own[index] for index in range(len(columns))]
    else:
        (mixed, tokens_grad, chunks, up_grad, down_grad, vec_grads, unit_grads) = results[:7]
        down_sum, scale_sum = results[7:]

        def scatter(value, axis=0, over=every):
            return lax.psum_scatter(value, over, scatter_dimension=axis, tiled=True)

        def both_ways(value, axis):
            part = scatter(value.astype(BF), axis, "wide")
            return lax.psum(part, "dp").astype(F32)

        up_total = both_ways(up_grad.transpose(1, 0, 2).reshape(width, units), 1)
        down_total = both_ways(down_grad.reshape(units, width), 0)
        unit_totals = [
            lax.psum(scatter(item.reshape(units), 0, "wide"), "dp") for item in unit_grads
        ]
        down_sum, scale_sum = lax.psum((down_sum, scale_sum), every)
        vec_totals = [scatter(item) for item in vec_grads]
        natural = chunks.transpose(0, 2, 1, 3, 4).reshape(pairs, width, 512)
        in_total = natural[:, :, :384].reshape(pairs, width, 3, 128)
        in_total = scatter(in_total.transpose(1, 2, 0, 3).reshape(width, 3 * width).astype(F32))
        out_total = scatter(
            natural[:, :, 384:].transpose(1, 0, 2).reshape(width, width).astype(F32)
        )
    return (
        mixed,
        tokens_grad,
        in_total,
        vec_totals[0],
        vec_totals[1],
        out_total,
        vec_totals[2],
        scale_sum,
        vec_totals[3],
        vec_totals[4],
        vec_totals[5],
        vec_totals[6],
        vec_totals[7],
        vec_totals[8],
        up_total,
        unit_totals[0],
        unit_totals[1],
        unit_totals[2],
        down_total,
        down_sum,
    )


def solution(mesh):
    by_all = P(("dp", "wide"))
    rows_all = P(("dp", "wide"), None)
    axes = (mesh.shape["dp"], mesh.shape["wide"])
    return jax.shard_map(
        functools.partial(body, axes),
        mesh=mesh,
        in_specs=(
            rows_all,
            rows_all,
            rows_all,
            rows_all,
            by_all,
            by_all,
            rows_all,
            by_all,
            P(),
            by_all,
            by_all,
            by_all,
            by_all,
            by_all,
            by_all,
            P(None, "wide"),
            P("wide"),
            P("wide"),
            P("wide"),
            P("wide", None),
            P(),
        ),
        out_specs=(
            rows_all,
            rows_all,
            rows_all,
            by_all,
            by_all,
            rows_all,
            by_all,
            P(),
            by_all,
            by_all,
            by_all,
            by_all,
            by_all,
            by_all,
            P(None, "wide"),
            P("wide"),
            P("wide"),
            P("wide"),
            P("wide", None),
            P(),
        ),
        check_vma=False,
    )
```

```python
import functools

import jax
import jax.numpy as jnp
from jax import lax
from jax.experimental import pallas as pl
from jax.experimental.pallas import tpu as pltpu
from jax.sharding import PartitionSpec as P

EPS = 1e-05
ROOT_HALF = 0.7071067811865476
INV_ROOT_TAU = 0.3989422804014327
LOG2E = 1.4426950408889634
MASKED = -1e30
BF = jnp.bfloat16
F32 = jnp.float32
TILE = 256
UNITS = 512
SLIM = 64
MESH = pl.DeviceIdType.MESH
VMEM_LIMIT = 62 * 1024 * 1024
ANY = pl.BlockSpec(memory_space=pl.ANY)


def dot_nn(left, right):
    return lax.dot_general(left, right, (((1,), (0,)), ((), ())), preferred_element_type=F32)


def dot_nt(left, right):
    return lax.dot_general(left, right, (((1,), (1,)), ((), ())), preferred_element_type=F32)


def dot_tn(left, right):
    return lax.dot_general(left, right, (((0,), (0,)), ((), ())), preferred_element_type=F32)


def params(**more):
    return pltpu.CompilerParams(
        dimension_semantics=("arbitrary",), vmem_limit_bytes=VMEM_LIMIT, **more
    )


def whole(shape):
    zeros = (0,) * len(shape)
    return pl.BlockSpec(shape, lambda *_: zeros, pipeline_mode=pl.Buffered(1))


def row_norm(values):
    center = values - jnp.mean(values, axis=-1, keepdims=True)
    inv = lax.rsqrt(jnp.mean(center * center, axis=-1, keepdims=True) + EPS)
    return center * inv, inv


def norm_back(grad, gain, normed, inv):
    scaled = grad * gain
    first = jnp.mean(scaled, axis=-1, keepdims=True)
    cross = jnp.mean(scaled * normed, axis=-1, keepdims=True)
    return inv * (scaled - first - normed * cross)


def column_sum(values):
    return jnp.sum(values, axis=0, keepdims=True)


def lane_fold(values):
    total = values[:, :128]
    for start in range(128, values.shape[1], 128):
        total = total + values[:, start : start + 128]
    return total


def cross_flag(lengths_ref, rows_ref):
    return jnp.where(lengths_ref[0, 0] == rows_ref.shape[0], 0.0, MASKED)


def stacked(value, low_lanes):
    zero = jnp.zeros_like(value)
    return jnp.concatenate(
        [jnp.where(low_lanes, value, zero), jnp.where(low_lanes, zero, value)], axis=0
    )


def attention_pair(cross, q_ref, k_ref, v_ref, scale, scaled_ref, out_ref, lse_ref, vext_ref):
    rows = q_ref.shape[0]
    half = rows // 2
    factor = LOG2E * 64 ** (-0.5)
    low_lanes = lax.broadcasted_iota(jnp.int32, (1, 128), 1) < 64
    below = lax.broadcasted_iota(jnp.int32, (TILE, TILE), 1) <= lax.broadcasted_iota(
        jnp.int32, (TILE, TILE), 0
    )
    vext_ref[:, :128] = v_ref[...]
    vext_ref[:, 128:] = jnp.ones((rows, 128), BF)
    for start in range(0, rows, TILE):
        stop = start + TILE
        both = dot_nt(stacked(q_ref[start:stop], low_lanes), k_ref[:stop])
        peaks, weights = [], []
        for head in range(2):
            raw = both[head * TILE : (head + 1) * TILE]
            parts = []
            if start >= half:
                parts.append((raw[:, :half], cross))
                if start > half:
                    parts.append((raw[:, half:start], None))
            elif start > 0:
                parts.append((raw[:, :start], None))
            parts.append((jnp.where(below, raw[:, start:stop], MASKED), None))
            peak = None
            for piece, shift in parts:
                top = jnp.max(piece, axis=-1, keepdims=True)
                if shift is not None:
                    top = top + shift
                peak = top if peak is None else jnp.maximum(peak, top)
            peaks.append(peak)
            pieces = []
            for piece, shift in parts:
                level = peak if shift is None else peak - shift
                pieces.append(jnp.exp2((piece - level) * factor).astype(BF))
            weights.append(pieces[0] if len(pieces) == 1 else jnp.concatenate(pieces, axis=1))
        both = dot_nn(jnp.concatenate(weights, axis=0), vext_ref[:stop])
        total = jnp.where(low_lanes, both[:TILE, 128:], both[TILE:, 128:])
        peak = jnp.where(low_lanes, peaks[0], peaks[1])
        mixed = jnp.where(low_lanes, both[:TILE, :128], both[TILE:, :128]) / total
        out_ref[start:stop] = mixed
        scaled_ref[start:stop] = (mixed * scale).astype(BF)
        lse = (peak * factor + jnp.log2(total)).T
        lse_ref[0, 0:1, start:stop] = lse[0:1]
        lse_ref[0, 1:2, start:stop] = lse[64:65]


def project_pair(first_ref, weights, bias, proj_ref):
    proj_ref[0] = (dot_nn(first_ref[...], weights) + bias).astype(BF)


def three(proj_ref):
    return [proj_ref.at[0, :, pl.ds(part * 128, 128)] for part in range(3)]


def plain_first_kernel(
    lengths_ref,
    tokens_ref,
    wq_ref,
    wk_ref,
    wv_ref,
    vectors_ref,
    bq_ref,
    bv_ref,
    hs_ref,
    first_ref,
    proj_ref,
    scaled_ref,
    attended_ref,
    lse_ref,
    vext_ref,
):
    @pl.when(pl.program_id(0) == 0)
    def _():
        for start in range(0, tokens_ref.shape[0], TILE):
            rows = pl.ds(start, TILE)
            normed, _ = row_norm(tokens_ref[rows].astype(F32))
            first_ref[rows] = (normed * vectors_ref[3:4] + vectors_ref[4:5]).astype(BF)

    weights = jnp.concatenate([wq_ref[...], wk_ref[...], wv_ref[...]], axis=1)
    bias = jnp.concatenate([bq_ref[0:1], jnp.zeros((1, 128), F32), bv_ref[1:2]], axis=1)
    project_pair(first_ref, weights, bias, proj_ref)
    attention_pair(
        cross_flag(lengths_ref, tokens_ref), *three(proj_ref), hs_ref[...], scaled_ref, attended_ref, lse_ref, vext_ref
    )


def plain_first(lengths, tokens, weights, vectors, head_lanes):
    rows, width = tokens.shape
    pairs = width // 128
    column = pl.BlockSpec((rows, 128), lambda p: (0, p))
    bias = pl.BlockSpec((16, 128), lambda p: (0, p))
    return pl.pallas_call(
        plain_first_kernel,
        grid=(pairs,),
        in_specs=[
            pl.BlockSpec(memory_space=pltpu.SMEM),
            whole((rows, width)),
            pl.BlockSpec((width, 128), lambda p: (0, p)),
            pl.BlockSpec((width, 128), lambda p: (0, pairs + p)),
            pl.BlockSpec((width, 128), lambda p: (0, 2 * pairs + p)),
            whole(vectors.shape),
            bias,
            bias,
            pl.BlockSpec((1, 128), lambda p: (0, p)),
        ],
        out_specs=[
            whole((rows, width)),
            pl.BlockSpec((1, rows, 384), lambda p: (p, 0, 0)),
            column,
            column,
            pl.BlockSpec((1, 8, rows), lambda p: (p, 0, 0)),
        ],
        out_shape=[
            jax.ShapeDtypeStruct((rows, width), BF),
            jax.ShapeDtypeStruct((pairs, rows, 384), BF),
            jax.ShapeDtypeStruct((rows, width), BF),
            jax.ShapeDtypeStruct((rows, width), F32),
            jax.ShapeDtypeStruct((pairs, 8, rows), F32),
        ],
        scratch_shapes=[pltpu.VMEM((rows, 256), BF)],
        compiler_params=params(),
        name="plain_first",
    )(lengths, tokens, weights, weights, weights, vectors, vectors, vectors, head_lanes)


def out_proj_rows(scaled_ref, weight_ref, vec_ref, tokens_ref, branch_ref, middle_ref):
    branch = dot_nn(scaled_ref[...], weight_ref[...]) + vec_ref[2:3]
    normed, _ = row_norm(branch)
    middle = tokens_ref[...].astype(F32) + (normed * vec_ref[5:6] + vec_ref[6:7])
    again, _ = row_norm(middle)
    branch_ref[...] = branch
    middle_ref[...] = middle
    return (again * vec_ref[7:8] + vec_ref[8:9]).astype(BF)


def out_proj_kernel(scaled_ref, weight_ref, vec_ref, tokens_ref, branch_ref, middle_ref, feed_ref):
    feed_ref[...] = out_proj_rows(
        scaled_ref, weight_ref, vec_ref, tokens_ref, branch_ref, middle_ref
    )


def out_proj(scaled, weights, vectors, tokens):
    rows, width = tokens.shape
    by_row = pl.BlockSpec((TILE, width), lambda i: (i, 0))
    return pl.pallas_call(
        out_proj_kernel,
        grid=(rows // TILE,),
        in_specs=[
            by_row,
            whole((width, width)),
            whole(vectors.shape),
            by_row,
        ],
        out_specs=[by_row, by_row, by_row],
        out_shape=[
            jax.ShapeDtypeStruct((rows, width), F32),
            jax.ShapeDtypeStruct((rows, width), F32),
            jax.ShapeDtypeStruct((rows, width), BF),
        ],
        compiler_params=params(),
        name="out_proj",
    )(scaled, weights, vectors, tokens)


def phi_and_slope(value):
    bell = jnp.exp2(value * value * (-0.5 * LOG2E))
    t = 1.0 / (1.0 + (0.3275911 * ROOT_HALF) * jnp.abs(value))
    series = t * (
        0.5 * 0.254829592
        + t
        * (
            0.5 * -0.284496736
            + t * (0.5 * 1.421413741 + t * (0.5 * -1.453152027 + t * (0.5 * 1.061405429)))
        )
    )
    tail = series * bell
    area = jnp.where(value < 0.0, tail, 1.0 - tail)
    return value * area, area + value * bell * INV_ROOT_TAU


def up_step(feed_ref, up_ref, vec_ref, act_ref, slope_ref, sums_ref):
    for left in range(0, UNITS, TILE):
        columns = slice(left, left + TILE)
        pre = dot_nn(feed_ref[...], up_ref[0, :, columns])
        bias = vec_ref[0, 0:1, columns].astype(F32)
        for start in range(0, feed_ref.shape[0], SLIM):
            rows = slice(start, start + SLIM)
            act, slope = phi_and_slope(pre[rows] + bias)
            act_ref[0, rows, columns] = act.astype(BF)
            slope_ref[0, rows, columns] = slope.astype(BF)
            sums_ref[0, rows] += lane_fold(act)
            sums_ref[1, rows] += lane_fold(act * act)


def side_by_side(*columns):
    lane = lax.broadcasted_iota(jnp.int32, (1, 128), 1)
    result = jnp.broadcast_to(columns[-1], (columns[-1].shape[0], 128))
    for index in range(len(columns) - 2, -1, -1):
        result = jnp.where(lane == index, columns[index], result)
    return result


def up_stats(units, stats_ref, sums_ref):
    for start in range(0, stats_ref.shape[0], TILE):
        rows = pl.ds(start, TILE)
        mean = jnp.sum(sums_ref[0, rows], axis=1, keepdims=True) / units
        square = jnp.sum(sums_ref[1, rows], axis=1, keepdims=True) / units
        inv = lax.rsqrt(square - mean * mean + EPS)
        stats_ref[rows] = side_by_side(mean, inv)


def up_kernel(units, feed_ref, up_ref, vec_ref, act_ref, slope_ref, stats_ref, sums_ref):
    step = pl.program_id(0)

    @pl.when(step == 0)
    def _():
        sums_ref[...] = jnp.zeros_like(sums_ref)

    up_step(feed_ref, up_ref, vec_ref, act_ref, slope_ref, sums_ref)

    @pl.when(step == pl.num_programs(0) - 1)
    def _():
        up_stats(units, stats_ref, sums_ref)


def up_pass(feed, up, vec):
    rows, width = feed.shape
    steps = up.shape[0]
    block = pl.BlockSpec((1, rows, UNITS), lambda j: (j, 0, 0))
    return pl.pallas_call(
        functools.partial(up_kernel, steps * UNITS),
        grid=(steps,),
        in_specs=[
            whole((rows, width)),
            pl.BlockSpec((1, width, UNITS), lambda j: (j, 0, 0)),
            pl.BlockSpec((1, vec.shape[1], UNITS), lambda j: (j, 0, 0)),
        ],
        out_specs=[block, block, whole((rows, 128))],
        out_shape=[
            jax.ShapeDtypeStruct((steps, rows, UNITS), BF),
            jax.ShapeDtypeStruct((steps, rows, UNITS), BF),
            jax.ShapeDtypeStruct((rows, 128), F32),
        ],
        scratch_shapes=[pltpu.VMEM((2, rows, 128), F32)],
        compiler_params=params(),
        name="up_pass",
    )(feed, up, vec)


def down_kernel(
    units,
    act_ref,
    stats_ref,
    vec_ref,
    down_ref,
    cot_ref,
    middle_ref,
    shift_ref,
    mixed_ref,
    down_grad_ref,
    e_ref,
    all_stats_ref,
    vec_grad_ref,
    total_ref,
    sums_ref,
    low_ref,
):
    step = pl.program_id(0)
    last = pl.num_programs(0) - 1
    rows_all = cot_ref.shape[0]

    @pl.when(step == 0)
    def _():
        total_ref[...] = jnp.zeros_like(total_ref)
        sums_ref[...] = jnp.zeros_like(sums_ref)

    gain = vec_ref[0, 1:2].astype(F32)
    shift = vec_ref[0, 2:3].astype(F32)
    slims = [slice(start, start + SLIM) for start in range(0, rows_all, SLIM)]

    def normalized(rows, columns):
        value = act_ref[0, rows, columns].astype(F32)
        return (value - stats_ref[rows, 0:1]) * stats_ref[rows, 1:2]

    for rows in slims:
        low_ref[rows] = (normalized(rows, slice(0, UNITS)) * gain + shift).astype(BF)
    for left in range(0, UNITS, TILE):
        columns = slice(left, left + TILE)
        grads = dot_nt(cot_ref[...], down_ref[0, columns])
        gain_grad = jnp.zeros((SLIM, TILE), F32)
        bias_grad = jnp.zeros((SLIM, TILE), F32)
        for rows in slims:
            normed = normalized(rows, columns)
            grad = grads[rows]
            gain_grad = gain_grad + grad * normed
            bias_grad = bias_grad + grad
            e = grad * gain[:, columns]
            e_ref[0, rows, columns] = e.astype(BF)
            sums_ref[0, rows] += lane_fold(e)
            sums_ref[1, rows] += lane_fold(e * normed)
        vec_grad_ref[0, 0:1, columns] = column_sum(gain_grad)
        vec_grad_ref[0, 1:2, columns] = column_sum(bias_grad)
    for left in range(0, total_ref.shape[1], TILE):
        columns = slice(left, left + TILE)
        total_ref[:, columns] += dot_nn(low_ref[...], down_ref[0, :, columns])
    for left in range(0, UNITS, TILE):
        columns = slice(left, left + TILE)
        down_grad_ref[0, columns] = dot_tn(low_ref[:, columns], cot_ref[...]).astype(BF)

    @pl.when(step == last)
    def _():
        for start in range(0, rows_all, TILE):
            rows = pl.ds(start, TILE)
            mixed_ref[rows] = (
                middle_ref[rows] + total_ref[rows] + shift_ref[...].astype(F32)
            ).astype(BF)
            first = jnp.sum(sums_ref[0, rows], axis=1, keepdims=True) / units
            cross = jnp.sum(sums_ref[1, rows], axis=1, keepdims=True) / units
            all_stats_ref[rows] = side_by_side(
                stats_ref[rows, 0:1], stats_ref[rows, 1:2], first, cross
            )


def down_pass(act, stats, vec, down, cotangent, middle, shift):
    rows, width = cotangent.shape
    steps = act.shape[0]
    block = pl.BlockSpec((1, rows, UNITS), lambda j: (j, 0, 0))
    return pl.pallas_call(
        functools.partial(down_kernel, steps * UNITS),
        grid=(steps,),
        in_specs=[
            block,
            whole((rows, 128)),
            pl.BlockSpec((1, vec.shape[1], UNITS), lambda j: (j, 0, 0)),
            pl.BlockSpec((1, UNITS, width), lambda j: (j, 0, 0)),
            whole((rows, width)),
            whole((rows, width)),
            whole((1, width)),
        ],
        out_specs=[
            whole((rows, width)),
            pl.BlockSpec((1, UNITS, width), lambda j: (j, 0, 0)),
            block,
            whole((rows, 128)),
            pl.BlockSpec((1, 8, UNITS), lambda j: (j, 0, 0)),
        ],
        out_shape=[
            jax.ShapeDtypeStruct((rows, width), BF),
            jax.ShapeDtypeStruct((steps, UNITS, width), BF),
            jax.ShapeDtypeStruct((steps, rows, UNITS), BF),
            jax.ShapeDtypeStruct((rows, 128), F32),
            jax.ShapeDtypeStruct((steps, 8, UNITS), F32),
        ],
        scratch_shapes=[
            pltpu.VMEM((rows, width), F32),
            pltpu.VMEM((2, rows, 128), F32),
            pltpu.VMEM((rows, UNITS), BF),
        ],
        compiler_params=params(),
        name="down_pass",
    )(act, stats, vec, down, cotangent, middle, shift)


def up_back_step(act, slope, e, stats_ref, up, low_ref, total_ref):
    bias_grad = jnp.zeros((SLIM, UNITS), F32)
    for start in range(0, total_ref.shape[0], SLIM):
        rows = slice(start, start + SLIM)
        inv = stats_ref[rows, 1:2]
        normed = (act[rows].astype(F32) - stats_ref[rows, 0:1]) * inv
        grad_act = inv * (
            e[rows].astype(F32) - stats_ref[rows, 2:3] - normed * stats_ref[rows, 3:4]
        )
        low = (grad_act * slope[rows].astype(F32)).astype(BF)
        bias_grad = bias_grad + low.astype(F32)
        low_ref[rows, 0:UNITS] = low
    for left in range(0, total_ref.shape[1], TILE):
        columns = slice(left, left + TILE)
        total_ref[:, columns] += dot_nt(low_ref[:, 0:UNITS], up[columns])
    return column_sum(bias_grad)


def up_back_kernel(
    act_ref,
    slope_ref,
    e_ref,
    stats_ref,
    up_ref,
    feed_ref,
    up_grad_ref,
    bias_grad_ref,
    total_ref,
    turned_ref,
    low_ref,
):
    @pl.when(pl.program_id(0) == 0)
    def _():
        total_ref[...] = jnp.zeros_like(total_ref)
        turned_ref[...] = feed_ref[...].T

    bias_grad_ref[0, 0:1] = up_back_step(
        act_ref.at[0],
        slope_ref.at[0],
        e_ref.at[0],
        stats_ref,
        up_ref.at[0],
        low_ref,
        total_ref,
    )
    up_grad_ref[0] = dot_nn(turned_ref[...], low_ref[...]).astype(BF)


def up_back(act, slope, e, stats, up, feed):
    rows, width = feed.shape
    steps = act.shape[0]
    block = pl.BlockSpec((1, rows, UNITS), lambda j: (j, 0, 0))
    narrow = whole((rows, 128))
    return pl.pallas_call(
        up_back_kernel,
        grid=(steps,),
        in_specs=[
            block,
            block,
            block,
            narrow,
            pl.BlockSpec((1, width, UNITS), lambda j: (j, 0, 0)),
            whole((rows, width)),
        ],
        out_specs=[
            pl.BlockSpec((1, width, UNITS), lambda j: (j, 0, 0)),
            pl.BlockSpec((1, 8, UNITS), lambda j: (j, 0, 0)),
            whole((rows, width)),
        ],
        out_shape=[
            jax.ShapeDtypeStruct((steps, width, UNITS), BF),
            jax.ShapeDtypeStruct((steps, 8, UNITS), F32),
            jax.ShapeDtypeStruct((rows, width), F32),
        ],
        scratch_shapes=[pltpu.VMEM((width, rows), BF), pltpu.VMEM((rows, UNITS), BF)],
        compiler_params=params(),
        name="up_back",
    )(act, slope, e, stats, up, feed)


def norms_back(grad_feed, cot_ref, middle_ref, branch_ref, vec_ref, sums_ref):
    normed, inv = row_norm(middle_ref[...])
    cot = cot_ref[...].astype(F32)
    grad_middle = cot + norm_back(grad_feed, vec_ref[7:8], normed, inv)
    sums_ref[7:8] += column_sum(grad_feed * normed)
    sums_ref[8:9] += column_sum(grad_feed)
    sums_ref[9:10] += column_sum(cot)
    normed, inv = row_norm(branch_ref[...])
    low = norm_back(grad_middle, vec_ref[5:6], normed, inv).astype(BF)
    sums_ref[5:6] += column_sum(grad_middle * normed)
    sums_ref[6:7] += column_sum(grad_middle)
    sums_ref[2:3] += column_sum(low.astype(F32))
    return grad_middle, low


def heads_back(low, weights, scale, attended):
    grad_out = (dot_nt(low, weights) * scale).astype(BF)
    product = grad_out.astype(F32) * attended
    high = product.astype(BF)
    rest = (product - high.astype(F32)).astype(BF)
    heads = (
        lax.broadcasted_iota(jnp.int32, (product.shape[1], 128), 0) // 64
        == lax.broadcasted_iota(jnp.int32, (product.shape[1], 128), 1)
    ).astype(BF)
    return grad_out, dot_nn(high, heads) + dot_nn(rest, heads)


def out_back_kernel(
    grad_feed_ref,
    cot_ref,
    middle_ref,
    branch_ref,
    scaled_ref,
    attended_ref,
    weight_ref,
    vec_ref,
    hs_ref,
    grad_middle_ref,
    ga_ref,
    out_grad_ref,
    delta_ref,
    sums_ref,
    total_ref,
):
    step = pl.program_id(0)

    @pl.when(step == 0)
    def _():
        total_ref[...] = jnp.zeros_like(total_ref)
        sums_ref[...] = jnp.zeros_like(sums_ref)

    grad_middle, low = norms_back(
        grad_feed_ref[...], cot_ref, middle_ref, branch_ref, vec_ref, sums_ref
    )
    grad_middle_ref[...] = grad_middle
    ga_ref[...], delta = heads_back(low, weight_ref[...], hs_ref[...], attended_ref[...])
    total_ref[...] += dot_tn(scaled_ref[...], low)
    delta_ref[...] = delta.T[: delta_ref.shape[0]]

    @pl.when(step == pl.num_programs(0) - 1)
    def _():
        out_grad_ref[...] = total_ref[...].astype(BF)


def out_back(
    grad_feed, cotangent, middle, branch, scaled, attended, weights, vectors, head_lanes
):
    rows, width = cotangent.shape
    heads = 2 * width // 128
    by_row = pl.BlockSpec((TILE, width), lambda i: (i, 0))
    return pl.pallas_call(
        out_back_kernel,
        grid=(rows // TILE,),
        in_specs=[
            by_row,
            by_row,
            by_row,
            by_row,
            by_row,
            by_row,
            whole((width, width)),
            whole(vectors.shape),
            whole((1, width)),
        ],
        out_specs=[
            by_row,
            by_row,
            whole((width, width)),
            pl.BlockSpec((heads, TILE), lambda i: (0, i)),
            whole((16, width)),
        ],
        out_shape=[
            jax.ShapeDtypeStruct((rows, width), F32),
            jax.ShapeDtypeStruct((rows, width), BF),
            jax.ShapeDtypeStruct((width, width), BF),
            jax.ShapeDtypeStruct((heads, rows), F32),
            jax.ShapeDtypeStruct((16, width), F32),
        ],
        scratch_shapes=[pltpu.VMEM((width, width), F32)],
        compiler_params=params(),
        name="out_back",
    )(
        grad_feed,
        cotangent,
        middle,
        branch,
        scaled,
        attended,
        weights,
        vectors,
        head_lanes,
    )


def attention_back_keys(
    starts, cross, q_ref, k_ref, v_ref, ga_ref, lse_ref, deltas, dq_ref, dk_ref, dv_ref
):
    rows = q_ref.shape[0]
    half = rows // 2
    factor = LOG2E * 64 ** (-0.5)
    low_lanes = lax.broadcasted_iota(jnp.int32, (1, 128), 1) < 64
    above = lax.broadcasted_iota(jnp.int32, (TILE, TILE), 0) <= lax.broadcasted_iota(
        jnp.int32, (TILE, TILE), 1
    )

    def pick(both):
        return jnp.where(low_lanes, both[:TILE], both[TILE:])

    for start in starts:
        stop = start + TILE
        keys = k_ref[start:stop]
        keys_apart = stacked(keys, low_lanes)
        values_apart = stacked(v_ref[start:stop], low_lanes)
        dk = jnp.zeros((TILE, 128), F32)
        dv = jnp.zeros((TILE, 128), F32)
        for left, right in ((start, half), (half, rows)) if start < half else ((start, rows),):
            raw = dot_nt(keys_apart, q_ref[left:right])
            grad_weights = dot_nt(values_apart, ga_ref[left:right])
            weights, grad_scores = [], []
            for head in range(2):
                mine = slice(head * TILE, (head + 1) * TILE)
                level = lse_ref[head : head + 1, left:right]
                if start < half <= left:
                    level = level - cross
                exponent = raw[mine] * factor - level
                if left == start:
                    first = jnp.where(above, exponent[:, :TILE], MASKED)
                    exponent = (
                        first
                        if right - left == TILE
                        else jnp.concatenate([first, exponent[:, TILE:]], axis=1)
                    )
                weight = jnp.exp2(exponent)
                weights.append(weight.astype(BF))
                delta = deltas[head][:, left:right]
                grad_scores.append((weight * (grad_weights[mine] - delta)).astype(BF))
            dv = dv + pick(dot_nn(jnp.concatenate(weights, axis=0), ga_ref[left:right]))
            dk = dk + pick(dot_nn(jnp.concatenate(grad_scores, axis=0), q_ref[left:right]))
            dq = jnp.where(low_lanes, dot_tn(grad_scores[0], keys), dot_tn(grad_scores[1], keys))
            if start == 0:
                dq_ref[left:right] = dq
            else:
                dq_ref[left:right] += dq
        dk_ref[start:stop] = dk
        dv_ref[start:stop] = dv


def in_back_pair(dq_ref, dk_ref, dv_ref, weights, turned_ref, out_grad_ref, chunk_ref, total_ref):
    factor = 64 ** (-0.5)
    dq = (dq_ref[...] * factor).astype(BF)
    dk = (dk_ref[...] * factor).astype(BF)
    dv = dv_ref[...].astype(BF)
    grads = jnp.concatenate([dq, dk, dv], axis=1)
    shares = dot_nn(turned_ref[...], grads).astype(BF)
    for start in range(0, total_ref.shape[0], TILE):
        part = jnp.concatenate(
            [shares[start : start + TILE], out_grad_ref[start : start + TILE]], axis=1
        )
        chunk_ref[:, start // TILE] = part.reshape(8, 32, 512)
        columns = slice(start, start + TILE)
        total_ref[:, columns] += dot_nt(grads, weights[columns])
    return column_sum(dq.astype(F32)), column_sum(dv.astype(F32))


def tokens_back(tokens, grad, grad_middle, gain):
    normed, inv = row_norm(tokens.astype(F32))
    back = norm_back(grad, gain, normed, inv)
    return (grad_middle + back).astype(BF), column_sum(grad * normed), column_sum(grad)


def in_back_kernel(
    lengths_ref,
    proj_ref,
    ga_ref,
    lse_ref,
    delta_ref,
    wq_ref,
    wk_ref,
    wv_ref,
    first_ref,
    out_grad_ref,
    tokens_ref,
    gain_ref,
    grad_middle_ref,
    chunk_ref,
    bias_ref,
    tokens_grad_ref,
    sums_ref,
    dq_ref,
    dk_ref,
    dv_ref,
    turned_ref,
    total_ref,
):
    step = pl.program_id(0)
    q_ref, k_ref, v_ref = three(proj_ref)
    rows_all = tokens_ref.shape[0]

    @pl.when(step == 0)
    def _():
        turned_ref[...] = first_ref[...].T
        total_ref[...] = jnp.zeros_like(total_ref)

    deltas = [delta_ref[0, head : head + 1] for head in range(2)]
    attention_back_keys(
        range(0, rows_all, TILE),
        cross_flag(lengths_ref, tokens_ref),
        q_ref,
        k_ref,
        v_ref,
        ga_ref,
        lse_ref.at[0],
        deltas,
        dq_ref,
        dk_ref,
        dv_ref,
    )
    weights = jnp.concatenate([wq_ref[...], wk_ref[...], wv_ref[...]], axis=1)
    query_sum, value_sum = in_back_pair(
        dq_ref, dk_ref, dv_ref, weights, turned_ref, out_grad_ref, chunk_ref.at[0], total_ref
    )
    bias_ref[0, 0:1] = query_sum
    bias_ref[0, 1:2] = value_sum

    @pl.when(step == pl.num_programs(0) - 1)
    def _():
        gain_grad = jnp.zeros((1, total_ref.shape[1]), F32)
        shift_grad = jnp.zeros((1, total_ref.shape[1]), F32)
        for start in range(0, rows_all, TILE):
            rows = pl.ds(start, TILE)
            tokens_grad_ref[rows], gain_part, shift_part = tokens_back(
                tokens_ref[rows], total_ref[rows], grad_middle_ref[rows], gain_ref[...]
            )
            gain_grad = gain_grad + gain_part
            shift_grad = shift_grad + shift_part
        sums_ref[0:1] = gain_grad
        sums_ref[1:2] = shift_grad


def in_back(lengths, projected, ga, lse, delta, weights, first, out_grad, tokens, gain, grad_middle):
    rows, width = tokens.shape
    pairs = width // 128
    column = pl.BlockSpec((rows, 128), lambda p: (0, p))
    square = whole((rows, width))
    return pl.pallas_call(
        in_back_kernel,
        grid=(pairs,),
        in_specs=[
            pl.BlockSpec(memory_space=pltpu.SMEM),
            pl.BlockSpec((1, rows, 384), lambda p: (p, 0, 0)),
            column,
            pl.BlockSpec((1, 8, rows), lambda p: (p, 0, 0)),
            pl.BlockSpec((1, 2, rows), lambda p: (p, 0, 0)),
            pl.BlockSpec((width, 128), lambda p: (0, p)),
            pl.BlockSpec((width, 128), lambda p: (0, pairs + p)),
            pl.BlockSpec((width, 128), lambda p: (0, 2 * pairs + p)),
            square,
            column,
            square,
            whole((1, width)),
            square,
        ],
        out_specs=[
            pl.BlockSpec((1, 8, width // TILE, 32, 512), lambda p: (p, 0, 0, 0, 0)),
            pl.BlockSpec((1, 8, 128), lambda p: (p, 0, 0)),
            square,
            whole((8, width)),
        ],
        out_shape=[
            jax.ShapeDtypeStruct((pairs, 8, width // TILE, 32, 512), BF),
            jax.ShapeDtypeStruct((pairs, 8, 128), F32),
            jax.ShapeDtypeStruct((rows, width), BF),
            jax.ShapeDtypeStruct((8, width), F32),
        ],
        scratch_shapes=[
            pltpu.VMEM((rows, 128), F32),
            pltpu.VMEM((rows, 128), F32),
            pltpu.VMEM((rows, 128), F32),
            pltpu.VMEM((width, rows), BF),
            pltpu.VMEM((rows, width), F32),
        ],
        compiler_params=params(),
        name="in_back",
    )(
        lengths,
        projected,
        ga,
        lse,
        delta,
        weights,
        weights,
        weights,
        first,
        out_grad,
        tokens,
        gain,
        grad_middle,
    )


class Place:
    def __init__(self):
        self.z = lax.axis_index("dp")
        wide = lax.axis_index("wide")
        self.y = wide // 4
        self.x = (wide // 2) % 2
        self.c = wide % 2
        self.core = (self.z, wide + 1 - 2 * self.c)
        self.side = (self.z, wide + 2 - 4 * self.x)
        self.over = (self.z, wide + 4 - 8 * self.y)
        self.ranks = (self.z + 1 - 2 * (self.z % 2), (self.z + 2) % 4, 3 - self.z)
        self.planes = tuple((rank, wide) for rank in self.ranks)

    def greet(self, planes=True):
        barrier = pltpu.get_barrier_semaphore()
        peers = (self.core, self.side, self.over) + (self.planes if planes else ())
        for peer in peers:
            pl.semaphore_signal(barrier, inc=1, device_id=peer, device_id_type=MESH)
        pl.semaphore_wait(barrier, len(peers))


class WideGather:
    copies = 22

    def __init__(
        self, place, view, count, send, recv, first, source=None, last=None, offset=0
    ):
        y, x, c = place.y, place.x, place.c
        here, side, over, far = (y, x, c), (y, 1 - x, c), (1 - y, x, c), (1 - y, 1 - x, c)
        upper, lower = pl.ds(offset, count // 2), pl.ds(offset + count // 2, count // 2)
        both = pl.ds(offset, count)
        parts = 4 if count % 64 == 0 else 2 if count % 32 == 0 else 1
        slices = [pl.ds(offset + k * (count // parts), count // parts) for k in range(parts)]

        def copy(index, slot, part, peer):
            destination = view(*slot, part)
            return pltpu.make_async_remote_copy(
                src_ref=source.at[part] if source is not None and slot is here else destination,
                dst_ref=destination,
                send_sem=send.at[first + index],
                recv_sem=recv.at[first + index],
                device_id=peer,
                device_id_type=MESH,
            )

        self.all = (
            copy(0, here, upper, place.side),
            copy(1, here, lower, place.over),
            copy(2, here, upper, place.over),
            copy(3, here, lower, place.side),
            copy(4, side, upper, place.over),
            copy(5, over, lower, place.side),
        )
        self.core = [
            [copy(6 + 4 * k + part, slot, rows, place.core) for part, rows in enumerate(slices)]
            for k, slot in enumerate((here, side, over, far))
        ]
        self.own = None
        if source is not None and last is not None:
            self.own = pltpu.make_async_copy(source, view(*here, both), last)

    def start(self):
        if self.own is not None:
            self.own.start()
        for copy in (*self.all[:4], *self.core[0]):
            copy.start()

    def relay(self, stage):
        waits, starts, blocks = (((0, 1), (4, 5), ()), ((2, 3), (), (1, 2)), ((4, 5), (), (3,)))[stage]
        for index in waits:
            self.all[index].wait_recv()
        for index in starts:
            self.all[index].start()
        for block in blocks:
            for copy in self.core[block]:
                copy.start()

    def finish(self):
        for copy in self.all:
            copy.wait_send()
        for copies in self.core:
            for copy in copies:
                copy.wait()
        if self.own is not None:
            self.own.wait()


def blocks_of(target):
    return lambda y, x, c, rows: target.at[y, x, c, rows]


LAG = 2


class Reduction:
    slots = 2 * LAG
    deep = 3 * LAG
    keep = 3 * LAG + 2

    @classmethod
    def scratch(cls):
        n, k = cls.slots, cls.keep
        return [
            pltpu.VMEM((cls.deep, 2, 2, 4, 32, 512), BF),
            pltpu.VMEM((n, 2, 2, 4, 32, 512), BF),
            pltpu.VMEM((n, 2, 2, 4, 16, 512), BF),
            pltpu.VMEM((n, 2, 4, 16, 512), BF),
            pltpu.VMEM((n, 4, 32, 512), BF),
            pltpu.VMEM((n, 3, 32, 512), BF),
            pltpu.VMEM((n, 32, 512), BF),
            pltpu.VMEM((k, 3, 32, 512), BF),
            pltpu.SemaphoreType.DMA((6, k)),
            pltpu.SemaphoreType.DMA((6, k)),
            pltpu.SemaphoreType.DMA((cls.deep,)),
        ]

    def __init__(self, place, refs):
        self.place = place
        (
            self.chip,
            self.partner,
            self.first,
            self.second,
            self.plane,
            self.from_z,
            self.sums,
            self.shared,
            self.send,
            self.recv,
            self.local,
        ) = refs

    def copy(self, index, slot, source, target, peer):
        return pltpu.make_async_remote_copy(
            src_ref=source,
            dst_ref=target,
            send_sem=self.send.at[index, slot],
            recv_sem=self.recv.at[index, slot],
            device_id=peer,
            device_id_type=MESH,
        )

    def wait(self, index, slot, arrived):
        self.copy(index, slot, arrived, arrived, self.place.core).wait()

    def load(self, chunk, source):
        slot = chunk % self.deep
        return pltpu.make_async_copy(source, self.chip.at[slot], self.local.at[slot])

    def stage0(self, chunk, view):
        slot, c = chunk % self.slots, self.place.c
        for y in range(2):
            for x in range(2):
                target = self.partner.at[slot, y, x]
                self.copy(0, slot, view.at[y, x, 1 - c], target, self.place.core).start()
        self.load(chunk, view.at[:, :, c]).start()

    def stage1(self, chunk):
        p, slot, index = self.place, chunk % self.slots, chunk % self.deep
        partner, chip, target = self.partner.at[slot], self.chip.at[index], self.first.at[slot]
        self.load(chunk, partner).wait()
        self.wait(0, slot, partner)
        chip[...] += partner[...]
        self.copy(1, slot, chip.at[:, 1 - p.x, :, pl.ds(0, 16)], target.at[0], p.side).start()
        self.copy(1, slot, chip.at[1 - p.y, :, :, pl.ds(16, 16)], target.at[1], p.over).start()

    def stage2(self, chunk):
        p, slot, index = self.place, chunk % self.slots, chunk % self.deep
        chip, arrived, target = self.chip.at[index], self.first.at[slot], self.second.at[slot]
        self.wait(1, slot, arrived)
        for k in range(2):
            chip[k, p.x, :, 0:16] += arrived[0, k]
            chip[p.y, k, :, 16:32] += arrived[1, k]
        self.copy(2, slot, chip.at[1 - p.y, p.x, :, pl.ds(0, 16)], target.at[0], p.over).start()
        self.copy(2, slot, chip.at[p.y, 1 - p.x, :, pl.ds(16, 16)], target.at[1], p.side).start()

    def stage3(self, chunk):
        p, slot, index = self.place, chunk % self.slots, chunk % self.deep
        arrived, mine, plane = self.second.at[slot], self.chip.at[index, p.y, p.x], self.plane
        self.wait(2, slot, arrived)
        plane[slot, :, 0:16] = mine[:, 0:16] + arrived[0]
        plane[slot, :, 16:32] = mine[:, 16:32] + arrived[1]
        for k in range(3):
            target = self.from_z.at[slot, k]
            self.copy(3, slot, plane.at[slot, p.ranks[k]], target, p.planes[k]).start()

    def stage4(self, chunk):
        slot = chunk % self.slots
        self.wait(3, slot, self.from_z.at[slot])
        total = self.plane[slot, self.place.z].astype(F32)
        for k in range(3):
            total = total + self.from_z[slot, k].astype(F32)
        return total

    def spread(self, chunk, total):
        slot, place = chunk % self.slots, chunk % self.keep
        self.sums[slot] = total.astype(BF)
        peer = self.place.planes[1]
        self.copy(4, place, self.sums.at[slot], self.shared.at[place, 0], peer).start()

    def stage5(self, chunk):
        slot, place, peer = chunk % self.slots, chunk % self.keep, self.place.planes[0]
        shared = self.shared.at[place]
        self.wait(4, place, shared.at[0])
        self.copy(5, place, self.sums.at[slot], shared.at[1], peer).start()
        self.copy(5, place, shared.at[0], shared.at[2], peer).start()

    def stage6(self, chunk):
        slot, place, ranks = chunk % self.slots, chunk % self.keep, self.place.ranks
        self.wait(5, place, self.shared.at[place, pl.ds(1, 2)])
        return [
            (self.place.z, self.sums[slot]),
            (ranks[1], self.shared[place, 0]),
            (ranks[0], self.shared[place, 1]),
            (ranks[2], self.shared[place, 2]),
        ]


class SmallReduction:
    @staticmethod
    def scratch():
        return [
            pltpu.VMEM((2, 2, 2, 4, 16, 512), BF),
            pltpu.VMEM((2, 2, 4, 16, 512), BF),
            pltpu.VMEM((2, 2, 4, 16, 512), BF),
            pltpu.VMEM((2, 4, 16, 512), BF),
            pltpu.VMEM((4, 16, 512), BF),
            pltpu.VMEM((3, 16, 512), BF),
            pltpu.SemaphoreType.DMA((4,)),
            pltpu.SemaphoreType.DMA((4,)),
        ]

    def __init__(self, place, refs):
        self.place = place
        self.source, self.chip, self.partner, self.first, self.second, self.from_z = refs[:6]
        self.send, self.recv = refs[6:]

    def copy(self, index, source, target, peer):
        return pltpu.make_async_remote_copy(
            src_ref=source,
            dst_ref=target,
            send_sem=self.send.at[index],
            recv_sem=self.recv.at[index],
            device_id=peer,
            device_id_type=MESH,
        )

    def wait(self, index, arrived):
        self.copy(index, arrived, arrived, self.place.core).wait()

    def stage0(self):
        p = self.place
        self.copy(0, self.source.at[:, :, 1 - p.c], self.partner, p.core).start()

    def stage1(self):
        p = self.place
        self.wait(0, self.partner)
        self.chip[...] = self.source[:, :, p.c] + self.partner[...]
        self.copy(1, self.chip.at[:, 1 - p.x], self.first, p.side).start()

    def stage2(self):
        p = self.place
        self.wait(1, self.first)
        for k in range(2):
            self.chip[k, p.x] += self.first[k]
        self.copy(2, self.chip.at[1 - p.y, p.x], self.second, p.over).start()

    def stage3(self):
        p = self.place
        self.wait(2, self.second)
        self.chip[p.y, p.x] += self.second[...]
        for k in range(3):
            block = self.chip.at[p.y, p.x, p.ranks[k]]
            self.copy(3, block, self.from_z.at[k], p.planes[k]).start()

    def stage4(self):
        p = self.place
        self.wait(3, self.from_z)
        total = self.chip[p.y, p.x, p.z].astype(F32)
        for k in range(3):
            total = total + self.from_z[k].astype(F32)
        return total


def dma_sems(count):
    return [pltpu.SemaphoreType.DMA((count,)), pltpu.SemaphoreType.DMA((count,))]


def to_planes(place, mine, landing, send, recv, first):
    return [
        pltpu.make_async_remote_copy(
            src_ref=mine,
            dst_ref=landing(k),
            send_sem=send.at[first + k],
            recv_sem=recv.at[first + k],
            device_id=place.planes[k],
            device_id_type=MESH,
        )
        for k in range(3)
    ]


class PlanesLast:
    copies = WideGather.copies + 6

    def __init__(self, place, source, target, send, recv, last):
        view = blocks_of(target.at[place.z])
        self.wide = WideGather(place, view, source.shape[0], send, recv, 0, source, last)

        def copy(index, rank, peer):
            blocks = target.at[rank, :, :, place.c]
            return pltpu.make_async_remote_copy(
                src_ref=blocks,
                dst_ref=blocks,
                send_sem=send.at[WideGather.copies + index],
                recv_sem=recv.at[WideGather.copies + index],
                device_id=peer,
                device_id_type=MESH,
            )

        self.across = [copy(k, place.z, place.planes[k]) for k in range(3)]
        self.over = [copy(3 + k, place.ranks[k], place.core) for k in range(3)]

    def start_across(self):
        self.wide.own.wait()
        for copy in self.across:
            copy.start()

    def start_over(self):
        for arrived, copy in zip(self.across, self.over):
            arrived.wait_recv()
            copy.start()

    def finish(self):
        self.wide.own = None
        self.wide.finish()
        for copy in self.across:
            copy.wait_send()
        for copy in self.over:
            copy.wait()


def first_kernel(
    lengths_ref,
    tokens_ref,
    in_ref,
    vec_ref,
    out_ref,
    up_ref,
    unit_ref,
    hs_ref,
    turned_ref,
    proj_ref,
    scaled_ref,
    scaled_turned_ref,
    attended_ref,
    lse_ref,
    vectors_ref,
    scale_ref,
    in_all,
    out_all,
    up_all,
    unit_all,
    held_ref,
    normed_ref,
    first_ref,
    vext_ref,
    send_in,
    recv_in,
    send_out,
    recv_out,
    send_ff,
    recv_ff,
    local,
):
    step = pl.program_id(0)
    place = Place()
    width = tokens_ref.shape[1]
    count = WideGather.copies
    lanes = (3 * width // 2 + 128, 3 * width // 2)
    across, early, late = [], [], None
    for group in range(2):
        held = held_ref.at[group, :, :, :, :, :, pl.ds(0, lanes[group])]
        first = group * (3 + 2 * count)

        def blocks(planes, held=held):
            return lambda y, x, c, rows: held.at[planes, y, x, c, rows]

        mine = held.at[0, place.y, place.x, place.c]
        across.append(
            to_planes(
                place,
                mine,
                lambda k, held=held: held.at[k + 1, place.y, place.x, place.c],
                send_in,
                recv_in,
                first,
            )
        )
        if group == 0:
            for part, planes in enumerate((pl.ds(0, 1), pl.ds(1, 3))):
                start = first + 3 + part * count
                early.append(WideGather(place, blocks(planes), 32, send_in, recv_in, start))
        else:
            late = WideGather(place, blocks(pl.ds(0, 4)), 32, send_in, recv_in, first + 3)
    orders = (place.z, *place.ranks)
    out = PlanesLast(place, out_ref, out_all, send_out, recv_out, local.at[2])
    half_rows = width // 2
    ups = [
        WideGather(
            place,
            blocks_of(up_all),
            half_rows,
            send_ff,
            recv_ff,
            (1 + part) * count,
            up_ref,
            None,
            part * half_rows,
        )
        for part in range(2)
    ]
    keep_up = pltpu.make_async_copy(
        up_ref, up_all.at[place.y, place.x, place.c], local.at[3]
    )
    unit = WideGather(
        place, blocks_of(unit_all), 32, send_ff, recv_ff, 0, unit_ref, local.at[4]
    )
    keep = [
        pltpu.make_async_copy(
            held_ref.at[group, index, :, :, :, :, pl.ds(0, lanes[1])],
            in_all.at[rank, :, :, :, :, pl.ds(group * lanes[1], lanes[1])],
            local.at[12 + 4 * group + index],
        )
        for group in range(2)
        for index, rank in enumerate(orders)
    ]

    @pl.when(step == 0)
    def _():
        place.greet()
        half = width // 2
        for group in range(2):
            mine = held_ref.at[group, 0, place.y, place.x, place.c]
            fills = []
            for pair in range(4):
                for part in range(3):
                    column = part * width + (4 * group + pair) * 128
                    fills.append(
                        pltpu.make_async_copy(
                            in_ref.at[:, pl.ds(column, 128)],
                            mine.at[:, pl.ds(pair * 384 + part * 128, 128)],
                            local.at[20 + group * 12 + pair * 3 + part],
                        )
                    )
            for copy in fills:
                copy.start()
            if group == 0:
                mine[:, 3 * half : 3 * half + 128] = jnp.zeros((32, 128), BF)
                mine[:, 3 * half : 3 * half + 32] = vec_ref[...]
            for copy in fills:
                copy.wait()
            for copy in across[group]:
                copy.start()
            if group == 0:
                early[0].start()
        keep_up.start()
        ups[0].start()
        scale = hs_ref[...].astype(F32)
        for pair in range(width // 128):
            own = slice(pair * 128, (pair + 1) * 128)
            low_lanes = lax.broadcasted_iota(jnp.int32, (1, 128), 1) < 64
            scale_ref[0:1, own] = jnp.where(
                low_lanes, scale[:, 2 * pair : 2 * pair + 1], scale[:, 2 * pair + 1 : 2 * pair + 2]
            )
        for start in range(0, tokens_ref.shape[0], TILE):
            rows = pl.ds(start, TILE)
            normed, _ = row_norm(tokens_ref[rows].astype(F32))
            normed_ref[rows] = normed
        early[0].relay(0)
        for copy in across[0]:
            copy.wait_recv()
        early[1].start()
        early[0].relay(1)
        early[0].relay(2)
        early[1].relay(0)
        early[1].relay(1)
        for copy in across[1]:
            copy.wait_recv()
        late.start()
        early[1].relay(2)
        out.wide.start()
        unit.start()
        for part in early:
            part.finish()
        for z in range(4):
            for y in range(2):
                tile = jnp.zeros((16, 128), F32)
                for x in range(2):
                    for c in range(2):
                        piece = held_ref[
                            0, orders[z], y, x, c, 0:16, 3 * half : 3 * half + 128
                        ].astype(F32)
                        spot = 32 * (2 * x + c)
                        tile = tile + (piece if spot == 0 else pltpu.roll(piece, spot, 1))
                vectors_ref[:, (2 * z + y) * 128 : (2 * z + y + 1) * 128] = tile
        for start in range(0, tokens_ref.shape[0], TILE):
            rows = pl.ds(start, TILE)
            first_ref[rows] = (normed_ref[rows] * vectors_ref[3:4] + vectors_ref[4:5]).astype(BF)

    @pl.when((step >= 2) & (step <= 4))
    def _():
        for stage in range(3):

            @pl.when(step == 2 + stage)
            def _():
                late.relay(stage)
                out.wide.relay(stage)
                unit.relay(stage)

    @pl.when(step == 2)
    def _():
        ups[1].start()

    @pl.when(step == 4)
    def _():
        out.start_across()

    @pl.when(step == 5)
    def _():
        late.finish()
        for copy in keep:
            copy.start()

    for part, steps in enumerate(((1, 2, 3), (4, 6, 8))):
        for stage, at in enumerate(steps):

            @pl.when(step == at)
            def _():
                ups[part].relay(stage)

    @pl.when(step == 7)
    def _():
        out.start_over()

    @pl.when(step > 0)
    def _():
        pair = step - 1
        columns = pl.ds(pl.multiple_of(pair % 4 * 384, 128), 384)
        weights = jnp.concatenate(
            [held_ref[pair // 4, order, :, :, :, :, columns].reshape(TILE, 384) for order in orders]
        )
        own = pl.ds(pl.multiple_of(pair * 128, 128), 128)
        bias = jnp.concatenate(
            [vectors_ref[0:1, own], jnp.zeros((1, 128), F32), vectors_ref[1:2, own]], axis=1
        )
        project_pair(first_ref, weights, bias, proj_ref)
        attention_pair(
            cross_flag(lengths_ref, tokens_ref),
            *three(proj_ref),
            scale_ref[0:1, own],
            scaled_ref,
            attended_ref,
            lse_ref,
            vext_ref,
        )
        scaled_turned_ref[...] = scaled_ref[...].T

    @pl.when(step == pl.num_programs(0) - 1)
    def _():
        turned_ref[...] = first_ref[...].T
        for copy in (*across[0], *across[1]):
            copy.wait_send()
        for copy in keep:
            copy.wait()
        out.finish()
        unit.finish()
        keep_up.wait()
        for part in ups:
            part.finish()


def first_part(lengths, tokens, in_weight, vec, out_weight, up_weight, unit_rows, head_scale):
    rows, width = tokens.shape
    pairs = width // 128

    def at(step):
        return jnp.maximum(step - 1, 0)

    column = pl.BlockSpec((rows, 128), lambda s: (0, at(s)))
    held = (2, 4, 2, 2, 2, 32, 3 * width // 2 + 128)
    return pl.pallas_call(
        first_kernel,
        grid=(pairs + 1,),
        in_specs=[
            pl.BlockSpec(memory_space=pltpu.SMEM),
            whole((rows, width)),
            ANY,
            whole(vec.shape),
            ANY,
            ANY,
            ANY,
            whole(head_scale.shape),
        ],
        out_specs=[
            whole((width, rows)),
            pl.BlockSpec((1, rows, 384), lambda s: (at(s), 0, 0)),
            column,
            pl.BlockSpec((128, rows), lambda s: (at(s), 0)),
            column,
            pl.BlockSpec((1, 8, rows), lambda s: (at(s), 0, 0)),
            whole((16, width)),
            whole((8, width)),
            ANY,
            ANY,
            ANY,
            ANY,
        ],
        out_shape=[
            jax.ShapeDtypeStruct((width, rows), BF),
            jax.ShapeDtypeStruct((pairs, rows, 384), BF),
            jax.ShapeDtypeStruct((rows, width), BF),
            jax.ShapeDtypeStruct((width, rows), BF),
            jax.ShapeDtypeStruct((rows, width), F32),
            jax.ShapeDtypeStruct((pairs, 8, rows), F32),
            jax.ShapeDtypeStruct((16, width), F32),
            jax.ShapeDtypeStruct((8, width), F32),
            jax.ShapeDtypeStruct((4, 2, 2, 2, 32, 3 * width), BF),
            jax.ShapeDtypeStruct((4, 2, 2, 2, *out_weight.shape), BF),
            jax.ShapeDtypeStruct((2, 2, 2, *up_weight.shape), BF),
            jax.ShapeDtypeStruct((2, 2, 2, *unit_rows.shape), BF),
        ],
        scratch_shapes=[
            pltpu.VMEM(held, BF),
            pltpu.VMEM((rows, width), F32),
            pltpu.VMEM((rows, width), BF),
            pltpu.VMEM((rows, 256), BF),
            *dma_sems(6 + 3 * WideGather.copies),
            *dma_sems(PlanesLast.copies),
            *dma_sems(3 * WideGather.copies),
            pltpu.SemaphoreType.DMA((44,)),
        ],
        compiler_params=params(collective_id=0, has_side_effects=True),
        name="first_part",
    )(lengths, tokens, in_weight, vec, out_weight, up_weight, unit_rows, head_scale)


def second_kernel(
    units,
    scaled_ref,
    weight_ref,
    vec_ref,
    tokens_ref,
    up_ref,
    unit_ref,
    down_ref,
    branch_ref,
    middle_ref,
    turned_ref,
    act_ref,
    slope_ref,
    stats_ref,
    down_all,
    feed_ref,
    sums_ref,
    send,
    recv,
    local,
):
    step = pl.program_id(0)
    lead = feed_ref.shape[0] // TILE
    place = Place()
    down = WideGather(
        place, blocks_of(down_all), UNITS, send, recv, 0, down_ref, local.at[0]
    )

    @pl.when(step == 0)
    def _():
        place.greet()
        down.start()
        sums_ref[...] = jnp.zeros_like(sums_ref)

    for stage, at in enumerate((4, 8, 11)):

        @pl.when(step == at)
        def _():
            down.relay(stage)

    @pl.when(step < lead)
    def _():
        rows = pl.ds(pl.multiple_of(step * TILE, TILE), TILE)
        feed_ref[rows] = out_proj_rows(
            scaled_ref, weight_ref, vec_ref, tokens_ref, branch_ref, middle_ref
        )

    @pl.when(step >= lead)
    def _():
        up_step(feed_ref, up_ref, unit_ref, act_ref, slope_ref, sums_ref)

    @pl.when(step == pl.num_programs(0) - 1)
    def _():
        up_stats(units, stats_ref, sums_ref)
        turned_ref[...] = feed_ref[...].T
        down.finish()


def second_part(scaled, out_weights, vectors, tokens, up, unit_vec, down_weight):
    rows, width = tokens.shape
    steps = up.shape[0]
    lead = rows // TILE

    def early(step):
        return jnp.minimum(step, lead - 1)

    def late(step):
        return jnp.maximum(step - lead, 0)

    by_row = pl.BlockSpec((TILE, width), lambda s: (early(s), 0))
    block = pl.BlockSpec((1, rows, UNITS), lambda s: (late(s), 0, 0))
    return pl.pallas_call(
        functools.partial(second_kernel, steps * UNITS),
        grid=(lead + steps,),
        in_specs=[
            by_row,
            whole((width, width)),
            whole(vectors.shape),
            by_row,
            pl.BlockSpec((1, width, UNITS), lambda s: (late(s), 0, 0)),
            pl.BlockSpec((1, unit_vec.shape[1], UNITS), lambda s: (late(s), 0, 0)),
            ANY,
        ],
        out_specs=[
            by_row,
            by_row,
            whole((width, rows)),
            block,
            block,
            whole((rows, 128)),
            ANY,
        ],
        out_shape=[
            jax.ShapeDtypeStruct((rows, width), F32),
            jax.ShapeDtypeStruct((rows, width), F32),
            jax.ShapeDtypeStruct((width, rows), BF),
            jax.ShapeDtypeStruct((steps, rows, UNITS), BF),
            jax.ShapeDtypeStruct((steps, rows, UNITS), BF),
            jax.ShapeDtypeStruct((rows, 128), F32),
            jax.ShapeDtypeStruct((2, 2, 2, *down_weight.shape), BF),
        ],
        scratch_shapes=[
            pltpu.VMEM((rows, width), BF),
            pltpu.VMEM((2, rows, 128), F32),
            *dma_sems(WideGather.copies),
            pltpu.SemaphoreType.DMA((1,)),
        ],
        compiler_params=params(collective_id=2, has_side_effects=True),
        name="second_part",
    )(scaled, out_weights, vectors, tokens, up, unit_vec, down_weight)


NORMS_AT, COLUMNS_AT, HEADS_AT, TOKENS_AT, VECTORS_AT = 8, 16, 20, 28, 32
BACK_STEPS = VECTORS_AT + 7
OUT_TILE = 128


class Stream:
    def __init__(self, view, buffers, sems):
        self.view, self.buffers, self.sems = view, buffers, sems

    def copy(self, index):
        slot = index % 2
        return pltpu.make_async_copy(self.view(index), self.buffers.at[slot], self.sems.at[slot])

    def block(self, index):
        return self.buffers.at[index % 2]


def advance(streams, index, count):
    @pl.when(index + 1 < count)
    def _():
        for stream in streams:
            stream.copy(index + 1).start()

    for stream in streams:
        stream.copy(index).wait()


def chunk_at(time):
    chunk = jnp.where(time < 13, time, time - 1)
    chunk = jnp.where(time >= 20, (time + 17) // 2, chunk)
    return chunk, (time >= 0) & ((time < 13) | ((time >= 14) & (time < 20)) | ((time >= 20) & (time < 30) & (time % 2 == 1)))


def back_kernel(
    lengths_ref,
    unit_grad_ref,
    vec_ref,
    hs_ref,
    act_all,
    slope_all,
    e_all,
    stats_all,
    up_all,
    feed_turned_all,
    down_grad_all,
    cot_all,
    middle_all,
    branch_all,
    scaled_turned_all,
    attended_all,
    out_weight_all,
    proj_all,
    lse_all,
    in_weight_all,
    turned_all,
    tokens_all,
    down_out,
    up_out,
    in_out,
    out_out,
    vec_out,
    tokens_grad_all,
    up_grad_all,
    units_in_ref,
    up_ref,
    stats_ref,
    feed_turned_ref,
    cot_ref,
    norms_in_ref,
    scaled_turned_ref,
    attended_ref,
    out_weight_ref,
    proj_ref,
    lse_ref,
    in_weight_ref,
    turned_ref,
    tokens_ref,
    tokens_grad_ref,
    staged_ref,
    total_ref,
    low_ref,
    out_grad_ref,
    ga_ref,
    grad_middle_ref,
    delta_ref,
    delta_sum_ref,
    sums_ref,
    units_ref,
    dq_ref,
    dk_ref,
    dv_ref,
    chunk_ref,
    stream_sems,
    fetch_sems,
    *scratch,
):
    step = pl.program_id(0)
    place = Place()
    engine = Reduction(place, scratch[:11])
    small = SmallReduction(place, scratch[11:])
    pairs = proj_all.shape[0]

    def rows_of(array, size):
        return lambda i: array.at[pl.ds(pl.multiple_of(i * size, size), size)]

    def columns_of(array, size):
        return lambda i: array.at[:, pl.ds(pl.multiple_of(i * size, size), size)]

    def stream(number, view, buffers):
        return Stream(view, buffers, stream_sems.at[number])

    act, slope, e = (
        stream(k, lambda i, array=array: array.at[i], units_in_ref.at[k])
        for k, array in enumerate((act_all, slope_all, e_all))
    )
    up = stream(3, lambda i: up_all.at[i], up_ref)
    cot = stream(4, rows_of(cot_all, OUT_TILE), cot_ref)
    middle = stream(5, rows_of(middle_all, OUT_TILE), norms_in_ref.at[0])
    branch = stream(6, rows_of(branch_all, OUT_TILE), norms_in_ref.at[1])
    attended = stream(7, columns_of(attended_all, TILE), attended_ref)
    proj = stream(8, lambda i: proj_all.at[i], proj_ref)
    lse = stream(9, lambda i: lse_all.at[i], lse_ref)
    in_weight = stream(10, columns_of(in_weight_all, 384), in_weight_ref)
    tokens = stream(11, rows_of(tokens_all, TILE), tokens_ref)
    put = rows_of(tokens_grad_all, TILE)

    def put_tokens(i):
        return pltpu.make_async_copy(
            tokens_grad_ref.at[i % 2], put(i), stream_sems.at[12, i % 2]
        )

    fetches = [
        pltpu.make_async_copy(source, target, fetch_sems.at[index])
        for index, (source, target) in enumerate(
            (
                (stats_all, stats_ref),
                (feed_turned_all, feed_turned_ref),
                (scaled_turned_all, scaled_turned_ref),
                (out_weight_all, out_weight_ref),
                (turned_all, turned_ref),
            )
        )
    ]

    @pl.when(step == 0)
    def _():
        for item in (act, slope, e, up):
            item.copy(0).start()
        for copy in fetches:
            copy.start()
        for item in (cot, middle, branch, attended, proj, lse, in_weight, tokens):
            item.copy(0).start()
        total_ref[...] = jnp.zeros_like(total_ref)
        sums_ref[...] = jnp.zeros_like(sums_ref)
        units_ref[...] = jnp.zeros_like(units_ref)
        place.greet()

    def store(block):
        view = up_grad_all.at[block // 4, block // 2 % 2, block % 2]
        return pltpu.make_async_copy(staged_ref, view, fetch_sems.at[5])

    @pl.when((step >= 1) & (step <= NORMS_AT))
    def _():
        store(step - 1).wait()


    def stage(number, kind, action, tick):
        chunk, there = chunk_at(tick - number * LAG)
        up = ((chunk >= 8) & (chunk < 14)) | (chunk == 15) | (chunk == 17)
        wanted = {
            "all": there,
            "down": there & (chunk < 8),
            "up": there & up,
            "shared": there & ((chunk < 8) | up),
            "own": there & (chunk >= 8) & ~up,
        }

        @pl.when(wanted[kind])
        def _():
            action(chunk)

    def up_index(chunk):
        return jnp.where(chunk < 14, chunk - 8, (chunk - 3) // 2)

    def pair_index(chunk):
        return jnp.where(chunk < 18, (chunk - 14) // 2, chunk - 16)

    def put_down(chunk):
        for rank, block in engine.stage6(chunk):
            for half in range(2):

                @pl.when(chunk % 2 == half)
                def _():
                    down_out[chunk // 2, rank, :, half * 512 : half * 512 + 512] = block

    def put_up(chunk):
        for rank, block in engine.stage6(chunk):
            up_out[up_index(chunk), rank] = block

    def put_own(chunk):
        total = engine.stage4(chunk)
        first = pair_index(chunk) * 128
        for part in range(3):
            lanes = pl.ds(pl.multiple_of(part * 1024 + first, 128), 128)
            in_out[:, lanes] = total[:, part * 128 : part * 128 + 128]
        out_out[:, pl.ds(pl.multiple_of(first, 128), 128)] = total[:, 384:512]

    def take_down(chunk):
        lanes = pl.ds(pl.multiple_of(chunk % 2 * 512, 512), 512)
        engine.stage0(chunk, down_grad_all.at[:, :, :, chunk // 2, :, :, lanes])

    def take_up(chunk):
        engine.stage0(chunk, up_grad_all.at[:, :, :, up_index(chunk)])

    def take_own(chunk):
        engine.stage0(chunk, chunk_ref.at[pair_index(chunk) % 2])

    def reduce_step(tick):
        stage(6, "down", put_down, tick)
        stage(6, "up", put_up, tick)
        stage(5, "shared", engine.stage5, tick)
        stage(4, "shared", lambda chunk: engine.spread(chunk, engine.stage4(chunk)), tick)
        stage(4, "own", put_own, tick)
        stage(3, "all", engine.stage3, tick)
        stage(2, "all", engine.stage2, tick)
        stage(1, "all", engine.stage1, tick)
        stage(0, "down", take_down, tick)
        stage(0, "up", take_up, tick)

    tick = jnp.where(step < NORMS_AT, step, NORMS_AT + (step - NORMS_AT) // 4)
    tick = jnp.where(step < COLUMNS_AT, tick, step - 6)
    tick = jnp.where(step < HEADS_AT, tick, 2 * step - 26)
    tick = jnp.where(step < TOKENS_AT, tick, 30)
    tick = jnp.where(step < VECTORS_AT, tick, step - 1)
    within = (step > NORMS_AT) & (step < COLUMNS_AT) & (step % 4 != 0)
    within = within | ((step > TOKENS_AT) & (step < VECTORS_AT))

    @pl.when(~within)
    def _():
        reduce_step(tick)


    @pl.when(step < NORMS_AT)
    def _():
        advance((act, slope, e, up), step, NORMS_AT)

        @pl.when(step == 0)
        def _():
            fetches[0].wait()

        units_ref[step, 0:1] = up_back_step(
            act.block(step),
            slope.block(step),
            e.block(step),
            stats_ref,
            up.block(step),
            low_ref,
            total_ref,
        )
        units_ref[step, 1:3] = unit_grad_ref[step, 0:2]

        @pl.when(step == 0)
        def _():
            fetches[1].wait()

        for left in range(0, UNITS, TILE):
            columns = slice(left, left + TILE)
            grad = dot_nn(feed_turned_ref[...], low_ref[:, columns]).astype(BF)
            staged_ref[:, :, :, columns] = grad.reshape(8, 4, 32, TILE)
        store(step).start()


    @pl.when((step >= NORMS_AT) & (step < COLUMNS_AT))
    def _():
        block = step - NORMS_AT
        rows = pl.ds(pl.multiple_of(block * OUT_TILE, OUT_TILE), OUT_TILE)
        advance((cot, middle, branch), block, COLUMNS_AT - NORMS_AT)
        grad_middle, low = norms_back(
            total_ref[rows],
            cot.block(block),
            middle.block(block),
            branch.block(block),
            vec_ref,
            sums_ref,
        )
        grad_middle_ref[rows] = grad_middle
        low_ref[rows] = low

    @pl.when((step >= COLUMNS_AT) & (step < HEADS_AT))
    def _():
        block = step - COLUMNS_AT
        columns = pl.ds(pl.multiple_of(block * TILE, TILE), TILE)
        advance((attended,), block, HEADS_AT - COLUMNS_AT)

        @pl.when(block == 0)
        def _():
            fetches[2].wait()
            fetches[3].wait()

        grad_out, delta = heads_back(
            low_ref[...],
            out_weight_ref[columns],
            hs_ref[0:1, columns],
            attended.block(block)[...],
        )
        ga_ref[:, columns] = grad_out
        delta_sum_ref[block, 0:1] = column_sum(delta)
        turned = delta.T
        for head in range(4):
            delta_ref[4 * block + head] = turned[head : head + 1]
        out_grad_ref[:, columns] = dot_nn(scaled_turned_ref[...], low_ref[:, columns]).astype(BF)

    @pl.when(step == HEADS_AT - 1)
    def _():
        total_ref[...] = jnp.zeros_like(total_ref)


    @pl.when((step >= HEADS_AT) & (step < TOKENS_AT))
    def _():
        pair = step - HEADS_AT
        columns = pl.ds(pl.multiple_of(pair * 128, 128), 128)
        advance((proj, lse, in_weight), pair, pairs)

        @pl.when(pair == 0)
        def _():
            fetches[4].wait()

        for part, starts in enumerate(((0, 3 * TILE), (TILE, 2 * TILE))):
            if part == 1:
                reduce_step(tick + 1)
            attention_back_keys(
                starts,
                cross_flag(lengths_ref, total_ref),
                *[proj.block(pair).at[:, pl.ds(index * 128, 128)] for index in range(3)],
                ga_ref.at[:, columns],
                lse.block(pair),
                [delta_ref[2 * pair], delta_ref[2 * pair + 1]],
                dq_ref,
                dk_ref,
                dv_ref,
            )
        query_sum, value_sum = in_back_pair(
            dq_ref,
            dk_ref,
            dv_ref,
            in_weight.block(pair)[...],
            turned_ref,
            out_grad_ref.at[:, columns],
            chunk_ref.at[pair % 2].reshape(8, 4, 32, 512),
            total_ref,
        )
        sums_ref[0:1, columns] = query_sum
        sums_ref[1:2, columns] = value_sum
        stage(0, "own", take_own, tick + 1)

    @pl.when((step >= TOKENS_AT) & (step < TOKENS_AT + 4))
    def _():
        block = step - TOKENS_AT
        rows = pl.ds(pl.multiple_of(block * TILE, TILE), TILE)
        advance((tokens,), block, 4)

        @pl.when(block >= 2)
        def _():
            put_tokens(block - 2).wait()

        result, gain_grad, shift_grad = tokens_back(
            tokens.block(block)[...], total_ref[rows], grad_middle_ref[rows], vec_ref[3:4]
        )
        tokens_grad_ref[block % 2] = result
        put_tokens(block).start()
        sums_ref[3:4] += gain_grad
        sums_ref[4:5] += shift_grad


    @pl.when(step == VECTORS_AT)
    def _():
        for y in range(2):
            for z in range(4):
                own = slice((2 * z + y) * 128, (2 * z + y + 1) * 128)
                for index in range(9):
                    lanes = slice(index % 4 * 128, index % 4 * 128 + 128)
                    row = 6 + index // 4
                    units_ref[8, row : row + 1, lanes] = sums_ref[index : index + 1, own]
                for x in range(2):
                    for c in range(2):
                        unit = 4 * y + 2 * x + c
                        units_ref[8, 0:3] = units_ref[unit, 0:3]
                        if (y, z, x, c) == (0, 0, 0, 0):
                            units_ref[8, 3:4] = sums_ref[9:10, 0:UNITS]
                            units_ref[8, 4:5] = sums_ref[9:10, UNITS : 2 * UNITS]
                            for block in range(4):
                                lanes = slice(block * 128, block * 128 + 128)
                                units_ref[8, 5:6, lanes] = delta_sum_ref[block, 0:1]
                        small.source[y, x, c, z] = units_ref[8].astype(BF)
        small.stage0()

    for index, action in enumerate((small.stage1, small.stage2, small.stage3)):

        @pl.when(step == VECTORS_AT + 1 + index)
        def _():
            action()

    @pl.when(step == VECTORS_AT + 4)
    def _():
        vec_out[...] = small.stage4()
        for block in range(2, 4):
            put_tokens(block).wait()


def back_part(
    lengths,
    act,
    slope,
    e,
    stats,
    up,
    feed_turned,
    unit_grad,
    down_grad,
    cotangent,
    middle,
    branch,
    scaled_turned,
    attended,
    out_weights,
    vectors,
    head_lanes,
    projected,
    lse,
    weights,
    turned,
    tokens,
):
    rows, width = tokens.shape
    pairs = width // 128

    return pl.pallas_call(
        back_kernel,
        grid=(BACK_STEPS,),
        in_specs=[
            pl.BlockSpec(memory_space=pltpu.SMEM),
            whole(unit_grad.shape),
            whole(vectors.shape),
            whole(head_lanes.shape),
            *[ANY] * 18,
        ],
        out_specs=[
            whole((4, 4, 32, 1024)),
            whole((8, 4, 32, 512)),
            whole((32, 3 * width)),
            whole((32, width)),
            whole((16, 512)),
            ANY,
            ANY,
        ],
        out_shape=[
            jax.ShapeDtypeStruct((4, 4, 32, 1024), BF),
            jax.ShapeDtypeStruct((8, 4, 32, 512), BF),
            jax.ShapeDtypeStruct((32, 3 * width), F32),
            jax.ShapeDtypeStruct((32, width), F32),
            jax.ShapeDtypeStruct((16, 512), F32),
            jax.ShapeDtypeStruct((rows, width), BF),
            jax.ShapeDtypeStruct((2, 2, 2, 8, 4, 32, UNITS), BF),
        ],
        scratch_shapes=[
            pltpu.VMEM((3, 2, rows, UNITS), BF),
            pltpu.VMEM((2, width, UNITS), BF),
            pltpu.VMEM((rows, 128), F32),
            pltpu.VMEM((width, rows), BF),
            pltpu.VMEM((2, OUT_TILE, width), BF),
            pltpu.VMEM((2, 2, OUT_TILE, width), F32),
            pltpu.VMEM((width, rows), BF),
            pltpu.VMEM((2, rows, TILE), F32),
            pltpu.VMEM((width, width), BF),
            pltpu.VMEM((2, rows, 384), BF),
            pltpu.VMEM((2, 8, rows), F32),
            pltpu.VMEM((2, width, 384), BF),
            pltpu.VMEM((width, rows), BF),
            pltpu.VMEM((2, TILE, width), BF),
            pltpu.VMEM((2, TILE, width), BF),
            pltpu.VMEM((8, 4, 32, UNITS), BF),
            pltpu.VMEM((rows, width), F32),
            pltpu.VMEM((rows, width), BF),
            pltpu.VMEM((width, width), BF),
            pltpu.VMEM((rows, width), BF),
            pltpu.VMEM((rows, width), F32),
            pltpu.VMEM((2 * pairs, 1, rows), F32),
            pltpu.VMEM((4, 8, 128), F32),
            pltpu.VMEM((16, width), F32),
            pltpu.VMEM((9, 16, UNITS), F32),
            pltpu.VMEM((rows, 128), F32),
            pltpu.VMEM((rows, 128), F32),
            pltpu.VMEM((rows, 128), F32),
            pltpu.VMEM((2, 2, 2, 2, 4, 32, 512), BF),
            pltpu.SemaphoreType.DMA((13, 2)),
            pltpu.SemaphoreType.DMA((6,)),
            *Reduction.scratch(),
            *SmallReduction.scratch(),
        ],
        compiler_params=params(collective_id=1, has_side_effects=True),
        name="back_part",
    )(
        lengths,
        unit_grad,
        vectors,
        head_lanes,
        act,
        slope,
        e,
        stats,
        up,
        feed_turned,
        down_grad.reshape(2, 2, 2, 4, 4, 32, width),
        cotangent,
        middle,
        branch,
        scaled_turned,
        attended,
        out_weights,
        projected,
        lse,
        weights,
        turned,
        tokens,
    )


def layer(staged, tokens, cotangent, lengths, attn, up, down, unit_vec, head_scale, down_bias):
    rows, width = tokens.shape
    heads = head_scale.shape[0]
    pairs = width // 128
    if staged:
        in_weight, out_weight, vec_block = attn
        (
            turned,
            projected,
            scaled,
            scaled_turned,
            attended,
            lse,
            vectors,
            head_lanes,
            weights,
            out_weights,
            up,
            unit_vec,
        ) = first_part(
            lengths, tokens, in_weight, vec_block, out_weight, up, unit_vec, head_scale[None, :]
        )
        weights = weights.reshape(width, 3 * width)
        out_weights = out_weights.reshape(width, width)
        up = up.reshape(-1, width, UNITS)
        unit_vec = unit_vec.reshape(-1, unit_vec.shape[-2], UNITS)
        branch, middle, feed_turned, act, slope, stats, down = second_part(
            scaled, out_weights, vectors, tokens, up, unit_vec, down
        )
        down = down.reshape(-1, UNITS, width)
    else:
        weights, out_weights, vectors = attn
        scale = head_scale.astype(F32)
        head_lanes = jnp.repeat(scale, width // heads)[None, :]
        first, projected, scaled, attended, lse = plain_first(
            lengths, tokens, weights, vectors, head_lanes
        )
        branch, middle, feed = out_proj(scaled, out_weights, vectors, tokens)
        act, slope, stats = up_pass(feed, up, unit_vec)
    mixed, down_grad, e, stats, unit_grad = down_pass(
        act, stats, unit_vec, down, cotangent, middle, down_bias[None, :]
    )
    if staged:
        down_total, up_total, in_total, out_total, vec_shares, tokens_grad, _ = back_part(
            lengths,
            act,
            slope,
            e,
            stats,
            up,
            feed_turned,
            unit_grad,
            down_grad,
            cotangent,
            middle,
            branch,
            scaled_turned,
            attended,
            out_weights,
            vectors,
            head_lanes,
            projected,
            lse,
            weights,
            turned,
            tokens,
        )
        return mixed, tokens_grad, down_total, up_total, in_total, out_total, vec_shares
    up_grad, up_bias_grad, grad_feed = up_back(
        act, slope, e, stats, up, feed
    )
    grad_middle, ga, out_grad, delta, sums = out_back(
        grad_feed,
        cotangent,
        middle,
        branch,
        scaled,
        attended,
        out_weights,
        vectors,
        head_lanes,
    )
    chunks, proj_bias, tokens_grad, pre_sums = in_back(
        lengths,
        projected,
        ga,
        lse,
        delta.reshape(pairs, 2, rows),
        weights,
        first,
        out_grad,
        tokens,
        vectors[3:4],
        grad_middle,
    )
    scale_grad = jnp.sum(delta, axis=1) / scale
    vec_grads = [
        proj_bias[:, 0].reshape(width),
        proj_bias[:, 1].reshape(width),
        sums[2],
        pre_sums[0],
        pre_sums[1],
        sums[5],
        sums[6],
        sums[7],
        sums[8],
    ]
    unit_grads = [up_bias_grad[:, 0], unit_grad[:, 0], unit_grad[:, 1]]
    return mixed, tokens_grad, chunks, up_grad, down_grad, vec_grads, unit_grads, sums[9], scale_grad


def body(
    axes,
    tokens,
    cotangent,
    lengths,
    in_weight,
    query_bias,
    value_bias,
    out_weight,
    out_bias,
    head_scale,
    pre_gain,
    pre_bias,
    post_gain,
    post_bias,
    feed_gain,
    feed_bias,
    up_weight,
    up_bias,
    mid_gain,
    mid_bias,
    down_weight,
    down_bias,
):
    planes, wide = axes
    every = ("dp", "wide")
    staged = (planes, wide) == (4, 8)
    rows, width = tokens.shape
    units = down_weight.shape[0] * wide
    steps = units // UNITS
    share = in_weight.shape[0]
    columns = [
        query_bias,
        value_bias,
        out_bias,
        pre_gain,
        pre_bias,
        post_gain,
        post_bias,
        feed_gain,
        feed_bias,
    ]
    index = lax.broadcasted_iota(jnp.int32, (32, up_bias.shape[0]), 0)
    unit_rows = jnp.where(index == 0, up_bias[None, :], jnp.zeros((), BF))
    unit_rows = jnp.where(index == 1, mid_gain[None, :], unit_rows)
    unit_rows = jnp.where(index == 2, mid_bias[None, :], unit_rows)
    if staged:
        index = lax.broadcasted_iota(jnp.int32, (32, share), 0)
        vec_block = jnp.zeros((32, share), BF)
        for row, column in enumerate(columns):
            vec_block = jnp.where(index == row, column[None, :], vec_block)
        attn = (in_weight, out_weight, vec_block)
        up, unit_vec, down = up_weight, unit_rows, down_weight
    else:
        flat = jnp.concatenate(columns).reshape(len(columns), share)
        attn = (
            lax.all_gather(in_weight, every, axis=0, tiled=True),
            lax.all_gather(out_weight, every, axis=0, tiled=True),
            jnp.pad(
                lax.all_gather(flat, every, axis=1, tiled=True), ((0, 16 - len(columns)), (0, 0))
            ).astype(F32),
        )
        up = lax.all_gather(up_weight, "wide", axis=1, tiled=True)
        up = up.reshape(width, steps, UNITS).transpose(1, 0, 2)
        unit_vec = lax.all_gather(unit_rows, "wide", axis=1, tiled=True)
        unit_vec = unit_vec.reshape(32, steps, UNITS).transpose(1, 0, 2)
        down = lax.all_gather(down_weight, "wide", axis=0, tiled=True)
        down = down.reshape(steps, UNITS, width)
    results = layer(
        staged,
        tokens,
        cotangent,
        lengths,
        attn,
        up,
        down,
        unit_vec,
        head_scale,
        down_bias,
    )
    heads = head_scale.shape[0]
    pairs = width // 128
    if staged:
        mixed, tokens_grad, down_total, up_total, in_total, out_total, vec_shares = results
        up_total = up_total.astype(F32).reshape(width, UNITS)
        down_total = down_total.astype(F32).reshape(UNITS, width)
        unit_totals = [vec_shares[index] for index in range(3)]
        down_sum = vec_shares[3:5].reshape(width)
        scale_sum = vec_shares[5].reshape(4, 128)[:, :4].reshape(heads) / head_scale.astype(F32)
        offset = share * lax.rem(lax.axis_index("wide"), 128 // share)
        own = vec_shares[6:9].reshape(12, 128)
        own = lax.dynamic_slice(own, (0, offset), (len(columns), share))
        vec_totals = [own[index] for index in range(len(columns))]
    else:
        (mixed, tokens_grad, chunks, up_grad, down_grad, vec_grads, unit_grads) = results[:7]
        down_sum, scale_sum = results[7:]

        def scatter(value, axis=0, over=every):
            return lax.psum_scatter(value, over, scatter_dimension=axis, tiled=True)

        def both_ways(value, axis):
            part = scatter(value.astype(BF), axis, "wide")
            return lax.psum(part, "dp").astype(F32)

        up_total = both_ways(up_grad.transpose(1, 0, 2).reshape(width, units), 1)
        down_total = both_ways(down_grad.reshape(units, width), 0)
        unit_totals = [
            lax.psum(scatter(item.reshape(units), 0, "wide"), "dp") for item in unit_grads
        ]
        down_sum, scale_sum = lax.psum((down_sum, scale_sum), every)
        vec_totals = [scatter(item) for item in vec_grads]
        natural = chunks.transpose(0, 2, 1, 3, 4).reshape(pairs, width, 512)
        in_total = natural[:, :, :384].reshape(pairs, width, 3, 128)
        in_total = scatter(in_total.transpose(1, 2, 0, 3).reshape(width, 3 * width).astype(F32))
        out_total = scatter(
            natural[:, :, 384:].transpose(1, 0, 2).reshape(width, width).astype(F32)
        )
    return (
        mixed,
        tokens_grad,
        in_total,
        vec_totals[0],
        vec_totals[1],
        out_total,
        vec_totals[2],
        scale_sum,
        vec_totals[3],
        vec_totals[4],
        vec_totals[5],
        vec_totals[6],
        vec_totals[7],
        vec_totals[8],
        up_total,
        unit_totals[0],
        unit_totals[1],
        unit_totals[2],
        down_total,
        down_sum,
    )


def solution(mesh):
    by_all = P(("dp", "wide"))
    rows_all = P(("dp", "wide"), None)
    axes = (mesh.shape["dp"], mesh.shape["wide"])
    return jax.shard_map(
        functools.partial(body, axes),
        mesh=mesh,
        in_specs=(
            rows_all,
            rows_all,
            rows_all,
            rows_all,
            by_all,
            by_all,
            rows_all,
            by_all,
            P(),
            by_all,
            by_all,
            by_all,
            by_all,
            by_all,
            by_all,
            P(None, "wide"),
            P("wide"),
            P("wide"),
            P("wide"),
            P("wide", None),
            P(),
        ),
        out_specs=(
            rows_all,
            rows_all,
            rows_all,
            by_all,
            by_all,
            rows_all,
            by_all,
            P(),
            by_all,
            by_all,
            by_all,
            by_all,
            by_all,
            by_all,
            P(None, "wide"),
            P("wide"),
            P("wide"),
            P("wide"),
            P("wide", None),
            P(),
        ),
        check_vma=False,
    )
```

```python
import functools

import jax
import jax.numpy as jnp
from jax import lax
from jax.experimental import pallas as pl
from jax.experimental.pallas import tpu as pltpu
from jax.sharding import PartitionSpec as P

EPS = 1e-05
ROOT_HALF = 0.7071067811865476
INV_ROOT_TAU = 0.3989422804014327
LOG2E = 1.4426950408889634
MASKED = -1e30
BF = jnp.bfloat16
F32 = jnp.float32
TILE = 256
UNITS = 512
SLIM = 64
MESH = pl.DeviceIdType.MESH
VMEM_LIMIT = 62 * 1024 * 1024
ANY = pl.BlockSpec(memory_space=pl.ANY)


def dot_nn(left, right):
    return lax.dot_general(left, right, (((1,), (0,)), ((), ())), preferred_element_type=F32)


def dot_nt(left, right):
    return lax.dot_general(left, right, (((1,), (1,)), ((), ())), preferred_element_type=F32)


def dot_tn(left, right):
    return lax.dot_general(left, right, (((0,), (0,)), ((), ())), preferred_element_type=F32)


def params(**more):
    return pltpu.CompilerParams(
        dimension_semantics=("arbitrary",), vmem_limit_bytes=VMEM_LIMIT, **more
    )


def whole(shape):
    zeros = (0,) * len(shape)
    return pl.BlockSpec(shape, lambda *_: zeros, pipeline_mode=pl.Buffered(1))


def row_norm(values):
    center = values - jnp.mean(values, axis=-1, keepdims=True)
    inv = lax.rsqrt(jnp.mean(center * center, axis=-1, keepdims=True) + EPS)
    return center * inv, inv


def norm_back(grad, gain, normed, inv):
    scaled = grad * gain
    first = jnp.mean(scaled, axis=-1, keepdims=True)
    cross = jnp.mean(scaled * normed, axis=-1, keepdims=True)
    return inv * (scaled - first - normed * cross)


def column_sum(values):
    return jnp.sum(values, axis=0, keepdims=True)


def lane_fold(values):
    total = values[:, :128]
    for start in range(128, values.shape[1], 128):
        total = total + values[:, start : start + 128]
    return total


def cross_flag(lengths_ref, rows_ref):
    return jnp.where(lengths_ref[0, 0] == rows_ref.shape[0], 0.0, MASKED)


def stacked(value, low_lanes):
    zero = jnp.zeros_like(value)
    return jnp.concatenate(
        [jnp.where(low_lanes, value, zero), jnp.where(low_lanes, zero, value)], axis=0
    )


def attention_pair(cross, q_ref, k_ref, v_ref, scale, scaled_ref, out_ref, lse_ref, vext_ref):
    rows = q_ref.shape[0]
    half = rows // 2
    factor = LOG2E * 64 ** (-0.5)
    low_lanes = lax.broadcasted_iota(jnp.int32, (1, 128), 1) < 64
    below = lax.broadcasted_iota(jnp.int32, (TILE, TILE), 1) <= lax.broadcasted_iota(
        jnp.int32, (TILE, TILE), 0
    )
    vext_ref[:, :128] = v_ref[...]
    vext_ref[:, 128:] = jnp.ones((rows, 128), BF)
    for start in range(0, rows, TILE):
        stop = start + TILE
        both = dot_nt(stacked(q_ref[start:stop], low_lanes), k_ref[:stop])
        peaks, weights = [], []
        for head in range(2):
            raw = both[head * TILE : (head + 1) * TILE]
            parts = []
            if start >= half:
                parts.append((raw[:, :half], cross))
                if start > half:
                    parts.append((raw[:, half:start], None))
            elif start > 0:
                parts.append((raw[:, :start], None))
            parts.append((jnp.where(below, raw[:, start:stop], MASKED), None))
            peak = None
            for piece, shift in parts:
                top = jnp.max(piece, axis=-1, keepdims=True)
                if shift is not None:
                    top = top + shift
                peak = top if peak is None else jnp.maximum(peak, top)
            peaks.append(peak)
            pieces = []
            for piece, shift in parts:
                level = peak if shift is None else peak - shift
                pieces.append(jnp.exp2((piece - level) * factor).astype(BF))
            weights.append(pieces[0] if len(pieces) == 1 else jnp.concatenate(pieces, axis=1))
        both = dot_nn(jnp.concatenate(weights, axis=0), vext_ref[:stop])
        total = jnp.where(low_lanes, both[:TILE, 128:], both[TILE:, 128:])
        peak = jnp.where(low_lanes, peaks[0], peaks[1])
        mixed = jnp.where(low_lanes, both[:TILE, :128], both[TILE:, :128]) / total
        out_ref[start:stop] = mixed
        scaled_ref[start:stop] = (mixed * scale).astype(BF)
        lse = (peak * factor + jnp.log2(total)).T
        lse_ref[0, 0:1, start:stop] = lse[0:1]
        lse_ref[0, 1:2, start:stop] = lse[64:65]


def project_pair(first_ref, weights, bias, proj_ref):
    proj_ref[0] = (dot_nn(first_ref[...], weights) + bias).astype(BF)


def three(proj_ref):
    return [proj_ref.at[0, :, pl.ds(part * 128, 128)] for part in range(3)]


def plain_first_kernel(
    lengths_ref,
    tokens_ref,
    wq_ref,
    wk_ref,
    wv_ref,
    vectors_ref,
    bq_ref,
    bv_ref,
    hs_ref,
    first_ref,
    proj_ref,
    scaled_ref,
    attended_ref,
    lse_ref,
    vext_ref,
):
    @pl.when(pl.program_id(0) == 0)
    def _():
        for start in range(0, tokens_ref.shape[0], TILE):
            rows = pl.ds(start, TILE)
            normed, _ = row_norm(tokens_ref[rows].astype(F32))
            first_ref[rows] = (normed * vectors_ref[3:4] + vectors_ref[4:5]).astype(BF)

    weights = jnp.concatenate([wq_ref[...], wk_ref[...], wv_ref[...]], axis=1)
    bias = jnp.concatenate([bq_ref[0:1], jnp.zeros((1, 128), F32), bv_ref[1:2]], axis=1)
    project_pair(first_ref, weights, bias, proj_ref)
    attention_pair(
        cross_flag(lengths_ref, tokens_ref), *three(proj_ref), hs_ref[...], scaled_ref, attended_ref, lse_ref, vext_ref
    )


def plain_first(lengths, tokens, weights, vectors, head_lanes):
    rows, width = tokens.shape
    pairs = width // 128
    column = pl.BlockSpec((rows, 128), lambda p: (0, p))
    bias = pl.BlockSpec((16, 128), lambda p: (0, p))
    return pl.pallas_call(
        plain_first_kernel,
        grid=(pairs,),
        in_specs=[
            pl.BlockSpec(memory_space=pltpu.SMEM),
            whole((rows, width)),
            pl.BlockSpec((width, 128), lambda p: (0, p)),
            pl.BlockSpec((width, 128), lambda p: (0, pairs + p)),
            pl.BlockSpec((width, 128), lambda p: (0, 2 * pairs + p)),
            whole(vectors.shape),
            bias,
            bias,
            pl.BlockSpec((1, 128), lambda p: (0, p)),
        ],
        out_specs=[
            whole((rows, width)),
            pl.BlockSpec((1, rows, 384), lambda p: (p, 0, 0)),
            column,
            column,
            pl.BlockSpec((1, 8, rows), lambda p: (p, 0, 0)),
        ],
        out_shape=[
            jax.ShapeDtypeStruct((rows, width), BF),
            jax.ShapeDtypeStruct((pairs, rows, 384), BF),
            jax.ShapeDtypeStruct((rows, width), BF),
            jax.ShapeDtypeStruct((rows, width), F32),
            jax.ShapeDtypeStruct((pairs, 8, rows), F32),
        ],
        scratch_shapes=[pltpu.VMEM((rows, 256), BF)],
        compiler_params=params(),
        name="plain_first",
    )(lengths, tokens, weights, weights, weights, vectors, vectors, vectors, head_lanes)


def out_proj_rows(scaled_ref, weight_ref, vec_ref, tokens_ref, branch_ref, middle_ref):
    branch = dot_nn(scaled_ref[...], weight_ref[...]) + vec_ref[2:3]
    normed, _ = row_norm(branch)
    middle = tokens_ref[...].astype(F32) + (normed * vec_ref[5:6] + vec_ref[6:7])
    again, _ = row_norm(middle)
    branch_ref[...] = branch
    middle_ref[...] = middle
    return (again * vec_ref[7:8] + vec_ref[8:9]).astype(BF)


def out_proj_kernel(scaled_ref, weight_ref, vec_ref, tokens_ref, branch_ref, middle_ref, feed_ref):
    feed_ref[...] = out_proj_rows(
        scaled_ref, weight_ref, vec_ref, tokens_ref, branch_ref, middle_ref
    )


def out_proj(scaled, weights, vectors, tokens):
    rows, width = tokens.shape
    by_row = pl.BlockSpec((TILE, width), lambda i: (i, 0))
    return pl.pallas_call(
        out_proj_kernel,
        grid=(rows // TILE,),
        in_specs=[
            by_row,
            whole((width, width)),
            whole(vectors.shape),
            by_row,
        ],
        out_specs=[by_row, by_row, by_row],
        out_shape=[
            jax.ShapeDtypeStruct((rows, width), F32),
            jax.ShapeDtypeStruct((rows, width), F32),
            jax.ShapeDtypeStruct((rows, width), BF),
        ],
        compiler_params=params(),
        name="out_proj",
    )(scaled, weights, vectors, tokens)


def phi_and_slope(value):
    bell = jnp.exp2(value * value * (-0.5 * LOG2E))
    t = 1.0 / (1.0 + (0.3275911 * ROOT_HALF) * jnp.abs(value))
    series = t * (
        0.5 * 0.254829592
        + t
        * (
            0.5 * -0.284496736
            + t * (0.5 * 1.421413741 + t * (0.5 * -1.453152027 + t * (0.5 * 1.061405429)))
        )
    )
    tail = series * bell
    area = jnp.where(value < 0.0, tail, 1.0 - tail)
    return value * area, area + value * bell * INV_ROOT_TAU


def up_step(feed_ref, up, vec, act_ref, slope_ref, sums_ref):
    for left in range(0, UNITS, TILE):
        columns = slice(left, left + TILE)
        pre = dot_nn(feed_ref[...], up[:, columns])
        bias = vec[0:1, columns].astype(F32)
        for start in range(0, feed_ref.shape[0], SLIM):
            rows = slice(start, start + SLIM)
            act, slope = phi_and_slope(pre[rows] + bias)
            act_ref[0, rows, columns] = act.astype(BF)
            slope_ref[0, rows, columns] = slope.astype(BF)
            sums_ref[0, rows] += lane_fold(act)
            sums_ref[1, rows] += lane_fold(act * act)


def side_by_side(*columns):
    lane = lax.broadcasted_iota(jnp.int32, (1, 128), 1)
    result = jnp.broadcast_to(columns[-1], (columns[-1].shape[0], 128))
    for index in range(len(columns) - 2, -1, -1):
        result = jnp.where(lane == index, columns[index], result)
    return result


def up_stats(units, stats_ref, sums_ref):
    for start in range(0, stats_ref.shape[0], TILE):
        rows = pl.ds(start, TILE)
        mean = jnp.sum(sums_ref[0, rows], axis=1, keepdims=True) / units
        square = jnp.sum(sums_ref[1, rows], axis=1, keepdims=True) / units
        inv = lax.rsqrt(square - mean * mean + EPS)
        stats_ref[rows] = side_by_side(mean, inv)


def up_kernel(units, feed_ref, up_ref, vec_ref, act_ref, slope_ref, stats_ref, sums_ref):
    step = pl.program_id(0)

    @pl.when(step == 0)
    def _():
        sums_ref[...] = jnp.zeros_like(sums_ref)

    up_step(feed_ref, up_ref.at[0], vec_ref.at[0], act_ref, slope_ref, sums_ref)

    @pl.when(step == pl.num_programs(0) - 1)
    def _():
        up_stats(units, stats_ref, sums_ref)


def up_pass(feed, up, vec):
    rows, width = feed.shape
    steps = up.shape[0]
    block = pl.BlockSpec((1, rows, UNITS), lambda j: (j, 0, 0))
    return pl.pallas_call(
        functools.partial(up_kernel, steps * UNITS),
        grid=(steps,),
        in_specs=[
            whole((rows, width)),
            pl.BlockSpec((1, width, UNITS), lambda j: (j, 0, 0)),
            pl.BlockSpec((1, vec.shape[1], UNITS), lambda j: (j, 0, 0)),
        ],
        out_specs=[block, block, whole((rows, 128))],
        out_shape=[
            jax.ShapeDtypeStruct((steps, rows, UNITS), BF),
            jax.ShapeDtypeStruct((steps, rows, UNITS), BF),
            jax.ShapeDtypeStruct((rows, 128), F32),
        ],
        scratch_shapes=[pltpu.VMEM((2, rows, 128), F32)],
        compiler_params=params(),
        name="up_pass",
    )(feed, up, vec)


def down_step(
    act_ref, stats_ref, vec, down, cot_ref, down_grad_ref, e_ref, vec_grad_ref, total_ref, sums_ref,
    low_ref
):
    gain = vec[1:2].astype(F32)
    shift = vec[2:3].astype(F32)
    slims = [slice(start, start + SLIM) for start in range(0, cot_ref.shape[0], SLIM)]

    def normalized(rows, columns):
        value = act_ref[0, rows, columns].astype(F32)
        return (value - stats_ref[rows, 0:1]) * stats_ref[rows, 1:2]

    for rows in slims:
        low_ref[rows] = (normalized(rows, slice(0, UNITS)) * gain + shift).astype(BF)
    for left in range(0, UNITS, TILE):
        columns = slice(left, left + TILE)
        grads = dot_nt(cot_ref[...], down[columns])
        gain_grad = jnp.zeros((SLIM, TILE), F32)
        bias_grad = jnp.zeros((SLIM, TILE), F32)
        for rows in slims:
            normed = normalized(rows, columns)
            grad = grads[rows]
            gain_grad = gain_grad + grad * normed
            bias_grad = bias_grad + grad
            e = grad * gain[:, columns]
            e_ref[0, rows, columns] = e.astype(BF)
            sums_ref[0, rows] += lane_fold(e)
            sums_ref[1, rows] += lane_fold(e * normed)
        vec_grad_ref[0, 0:1, columns] = column_sum(gain_grad)
        vec_grad_ref[0, 1:2, columns] = column_sum(bias_grad)
    for left in range(0, total_ref.shape[1], TILE):
        columns = slice(left, left + TILE)
        total_ref[:, columns] += dot_nn(low_ref[...], down[:, columns])
    for left in range(0, UNITS, TILE):
        columns = slice(left, left + TILE)
        down_grad_ref[0, columns] = dot_tn(low_ref[:, columns], cot_ref[...]).astype(BF)


def down_end(
    units, stats_ref, middle_ref, shift_ref, mixed_ref, all_stats_ref, total_ref, sums_ref
):
    for start in range(0, total_ref.shape[0], TILE):
        rows = pl.ds(start, TILE)
        mixed_ref[rows] = (
            middle_ref[rows] + total_ref[rows] + shift_ref[...].astype(F32)
        ).astype(BF)
        first = jnp.sum(sums_ref[0, rows], axis=1, keepdims=True) / units
        cross = jnp.sum(sums_ref[1, rows], axis=1, keepdims=True) / units
        all_stats_ref[rows] = side_by_side(stats_ref[rows, 0:1], stats_ref[rows, 1:2], first, cross)


def down_kernel(
    units,
    act_ref,
    stats_ref,
    vec_ref,
    down_ref,
    cot_ref,
    middle_ref,
    shift_ref,
    mixed_ref,
    down_grad_ref,
    e_ref,
    all_stats_ref,
    vec_grad_ref,
    total_ref,
    sums_ref,
    low_ref,
):
    step = pl.program_id(0)

    @pl.when(step == 0)
    def _():
        total_ref[...] = jnp.zeros_like(total_ref)
        sums_ref[...] = jnp.zeros_like(sums_ref)

    down_step(
        act_ref, stats_ref, vec_ref.at[0], down_ref.at[0], cot_ref, down_grad_ref, e_ref, vec_grad_ref,
        total_ref, sums_ref, low_ref
    )

    @pl.when(step == pl.num_programs(0) - 1)
    def _():
        down_end(
            units, stats_ref, middle_ref, shift_ref, mixed_ref, all_stats_ref, total_ref, sums_ref
        )


def down_pass(act, stats, vec, down, cotangent, middle, shift):
    rows, width = cotangent.shape
    steps = act.shape[0]
    block = pl.BlockSpec((1, rows, UNITS), lambda j: (j, 0, 0))
    return pl.pallas_call(
        functools.partial(down_kernel, steps * UNITS),
        grid=(steps,),
        in_specs=[
            block,
            whole((rows, 128)),
            pl.BlockSpec((1, vec.shape[1], UNITS), lambda j: (j, 0, 0)),
            pl.BlockSpec((1, UNITS, width), lambda j: (j, 0, 0)),
            whole((rows, width)),
            whole((rows, width)),
            whole((1, width)),
        ],
        out_specs=[
            whole((rows, width)),
            pl.BlockSpec((1, UNITS, width), lambda j: (j, 0, 0)),
            block,
            whole((rows, 128)),
            pl.BlockSpec((1, 8, UNITS), lambda j: (j, 0, 0)),
        ],
        out_shape=[
            jax.ShapeDtypeStruct((rows, width), BF),
            jax.ShapeDtypeStruct((steps, UNITS, width), BF),
            jax.ShapeDtypeStruct((steps, rows, UNITS), BF),
            jax.ShapeDtypeStruct((rows, 128), F32),
            jax.ShapeDtypeStruct((steps, 8, UNITS), F32),
        ],
        scratch_shapes=[
            pltpu.VMEM((rows, width), F32),
            pltpu.VMEM((2, rows, 128), F32),
            pltpu.VMEM((rows, UNITS), BF),
        ],
        compiler_params=params(),
        name="down_pass",
    )(act, stats, vec, down, cotangent, middle, shift)


def up_back_step(act, slope, e, stats_ref, up, low_ref, total_ref):
    bias_grad = jnp.zeros((SLIM, UNITS), F32)
    for start in range(0, total_ref.shape[0], SLIM):
        rows = slice(start, start + SLIM)
        inv = stats_ref[rows, 1:2]
        normed = (act[rows].astype(F32) - stats_ref[rows, 0:1]) * inv
        grad_act = inv * (
            e[rows].astype(F32) - stats_ref[rows, 2:3] - normed * stats_ref[rows, 3:4]
        )
        low = (grad_act * slope[rows].astype(F32)).astype(BF)
        bias_grad = bias_grad + low.astype(F32)
        low_ref[rows, 0:UNITS] = low
    for left in range(0, total_ref.shape[1], TILE):
        columns = slice(left, left + TILE)
        total_ref[:, columns] += dot_nt(low_ref[:, 0:UNITS], up[columns])
    return column_sum(bias_grad)


def up_back_kernel(
    act_ref,
    slope_ref,
    e_ref,
    stats_ref,
    up_ref,
    feed_ref,
    up_grad_ref,
    bias_grad_ref,
    total_ref,
    turned_ref,
    low_ref,
):
    @pl.when(pl.program_id(0) == 0)
    def _():
        total_ref[...] = jnp.zeros_like(total_ref)
        turned_ref[...] = feed_ref[...].T

    bias_grad_ref[0, 0:1] = up_back_step(
        act_ref.at[0],
        slope_ref.at[0],
        e_ref.at[0],
        stats_ref,
        up_ref.at[0],
        low_ref,
        total_ref,
    )
    up_grad_ref[0] = dot_nn(turned_ref[...], low_ref[...]).astype(BF)


def up_back(act, slope, e, stats, up, feed):
    rows, width = feed.shape
    steps = act.shape[0]
    block = pl.BlockSpec((1, rows, UNITS), lambda j: (j, 0, 0))
    narrow = whole((rows, 128))
    return pl.pallas_call(
        up_back_kernel,
        grid=(steps,),
        in_specs=[
            block,
            block,
            block,
            narrow,
            pl.BlockSpec((1, width, UNITS), lambda j: (j, 0, 0)),
            whole((rows, width)),
        ],
        out_specs=[
            pl.BlockSpec((1, width, UNITS), lambda j: (j, 0, 0)),
            pl.BlockSpec((1, 8, UNITS), lambda j: (j, 0, 0)),
            whole((rows, width)),
        ],
        out_shape=[
            jax.ShapeDtypeStruct((steps, width, UNITS), BF),
            jax.ShapeDtypeStruct((steps, 8, UNITS), F32),
            jax.ShapeDtypeStruct((rows, width), F32),
        ],
        scratch_shapes=[pltpu.VMEM((width, rows), BF), pltpu.VMEM((rows, UNITS), BF)],
        compiler_params=params(),
        name="up_back",
    )(act, slope, e, stats, up, feed)


def norms_back(grad_feed, cot_ref, middle_ref, branch_ref, vec_ref, sums_ref):
    normed, inv = row_norm(middle_ref[...])
    cot = cot_ref[...].astype(F32)
    grad_middle = cot + norm_back(grad_feed, vec_ref[7:8], normed, inv)
    sums_ref[7:8] += column_sum(grad_feed * normed)
    sums_ref[8:9] += column_sum(grad_feed)
    sums_ref[9:10] += column_sum(cot)
    normed, inv = row_norm(branch_ref[...])
    low = norm_back(grad_middle, vec_ref[5:6], normed, inv).astype(BF)
    sums_ref[5:6] += column_sum(grad_middle * normed)
    sums_ref[6:7] += column_sum(grad_middle)
    sums_ref[2:3] += column_sum(low.astype(F32))
    return grad_middle, low


def heads_back(low, weights, scale, attended):
    grad_out = (dot_nt(low, weights) * scale).astype(BF)
    product = grad_out.astype(F32) * attended
    high = product.astype(BF)
    rest = (product - high.astype(F32)).astype(BF)
    heads = (
        lax.broadcasted_iota(jnp.int32, (product.shape[1], 128), 0) // 64
        == lax.broadcasted_iota(jnp.int32, (product.shape[1], 128), 1)
    ).astype(BF)
    return grad_out, dot_nn(high, heads) + dot_nn(rest, heads)


def out_back_kernel(
    grad_feed_ref,
    cot_ref,
    middle_ref,
    branch_ref,
    scaled_ref,
    attended_ref,
    weight_ref,
    vec_ref,
    hs_ref,
    grad_middle_ref,
    ga_ref,
    out_grad_ref,
    delta_ref,
    sums_ref,
    total_ref,
):
    step = pl.program_id(0)

    @pl.when(step == 0)
    def _():
        total_ref[...] = jnp.zeros_like(total_ref)
        sums_ref[...] = jnp.zeros_like(sums_ref)

    grad_middle, low = norms_back(
        grad_feed_ref[...], cot_ref, middle_ref, branch_ref, vec_ref, sums_ref
    )
    grad_middle_ref[...] = grad_middle
    ga_ref[...], delta = heads_back(low, weight_ref[...], hs_ref[...], attended_ref[...])
    total_ref[...] += dot_tn(scaled_ref[...], low)
    delta_ref[...] = delta.T[: delta_ref.shape[0]]

    @pl.when(step == pl.num_programs(0) - 1)
    def _():
        out_grad_ref[...] = total_ref[...].astype(BF)


def out_back(
    grad_feed, cotangent, middle, branch, scaled, attended, weights, vectors, head_lanes
):
    rows, width = cotangent.shape
    heads = 2 * width // 128
    by_row = pl.BlockSpec((TILE, width), lambda i: (i, 0))
    return pl.pallas_call(
        out_back_kernel,
        grid=(rows // TILE,),
        in_specs=[
            by_row,
            by_row,
            by_row,
            by_row,
            by_row,
            by_row,
            whole((width, width)),
            whole(vectors.shape),
            whole((1, width)),
        ],
        out_specs=[
            by_row,
            by_row,
            whole((width, width)),
            pl.BlockSpec((heads, TILE), lambda i: (0, i)),
            whole((16, width)),
        ],
        out_shape=[
            jax.ShapeDtypeStruct((rows, width), F32),
            jax.ShapeDtypeStruct((rows, width), BF),
            jax.ShapeDtypeStruct((width, width), BF),
            jax.ShapeDtypeStruct((heads, rows), F32),
            jax.ShapeDtypeStruct((16, width), F32),
        ],
        scratch_shapes=[pltpu.VMEM((width, width), F32)],
        compiler_params=params(),
        name="out_back",
    )(
        grad_feed,
        cotangent,
        middle,
        branch,
        scaled,
        attended,
        weights,
        vectors,
        head_lanes,
    )


def attention_back_keys(
    starts, cross, q_ref, k_ref, v_ref, ga_ref, lse_ref, deltas, dq_ref, dk_ref, dv_ref
):
    rows = q_ref.shape[0]
    half = rows // 2
    factor = LOG2E * 64 ** (-0.5)
    low_lanes = lax.broadcasted_iota(jnp.int32, (1, 128), 1) < 64
    above = lax.broadcasted_iota(jnp.int32, (TILE, TILE), 0) <= lax.broadcasted_iota(
        jnp.int32, (TILE, TILE), 1
    )

    def pick(both):
        return jnp.where(low_lanes, both[:TILE], both[TILE:])

    for start in starts:
        stop = start + TILE
        keys = k_ref[start:stop]
        keys_apart = stacked(keys, low_lanes)
        values_apart = stacked(v_ref[start:stop], low_lanes)
        dk = jnp.zeros((TILE, 128), F32)
        dv = jnp.zeros((TILE, 128), F32)
        for left, right in ((start, half), (half, rows)) if start < half else ((start, rows),):
            raw = dot_nt(keys_apart, q_ref[left:right])
            grad_weights = dot_nt(values_apart, ga_ref[left:right])
            weights, grad_scores = [], []
            for head in range(2):
                mine = slice(head * TILE, (head + 1) * TILE)
                level = lse_ref[head : head + 1, left:right]
                if start < half <= left:
                    level = level - cross
                exponent = raw[mine] * factor - level
                if left == start:
                    first = jnp.where(above, exponent[:, :TILE], MASKED)
                    exponent = (
                        first
                        if right - left == TILE
                        else jnp.concatenate([first, exponent[:, TILE:]], axis=1)
                    )
                weight = jnp.exp2(exponent)
                weights.append(weight.astype(BF))
                delta = deltas[head][:, left:right]
                grad_scores.append((weight * (grad_weights[mine] - delta)).astype(BF))
            dv = dv + pick(dot_nn(jnp.concatenate(weights, axis=0), ga_ref[left:right]))
            dk = dk + pick(dot_nn(jnp.concatenate(grad_scores, axis=0), q_ref[left:right]))
            dq = jnp.where(low_lanes, dot_tn(grad_scores[0], keys), dot_tn(grad_scores[1], keys))
            if start == 0:
                dq_ref[left:right] = dq
            else:
                dq_ref[left:right] += dq
        dk_ref[start:stop] = dk
        dv_ref[start:stop] = dv


def in_back_pair(dq_ref, dk_ref, dv_ref, weights, turned_ref, out_grad_ref, chunk_ref, total_ref):
    factor = 64 ** (-0.5)
    dq = (dq_ref[...] * factor).astype(BF)
    dk = (dk_ref[...] * factor).astype(BF)
    dv = dv_ref[...].astype(BF)
    grads = jnp.concatenate([dq, dk, dv], axis=1)
    shares = dot_nn(turned_ref[...], grads).astype(BF)
    for start in range(0, total_ref.shape[0], TILE):
        part = jnp.concatenate(
            [shares[start : start + TILE], out_grad_ref[start : start + TILE]], axis=1
        )
        chunk_ref[:, start // TILE] = part.reshape(8, 32, 512)
        columns = slice(start, start + TILE)
        total_ref[:, columns] += dot_nt(grads, weights[columns])
    return column_sum(dq.astype(F32)), column_sum(dv.astype(F32))


def tokens_back(tokens, grad, grad_middle, gain):
    normed, inv = row_norm(tokens.astype(F32))
    back = norm_back(grad, gain, normed, inv)
    return (grad_middle + back).astype(BF), column_sum(grad * normed), column_sum(grad)


def in_back_kernel(
    lengths_ref,
    proj_ref,
    ga_ref,
    lse_ref,
    delta_ref,
    wq_ref,
    wk_ref,
    wv_ref,
    first_ref,
    out_grad_ref,
    tokens_ref,
    gain_ref,
    grad_middle_ref,
    chunk_ref,
    bias_ref,
    tokens_grad_ref,
    sums_ref,
    dq_ref,
    dk_ref,
    dv_ref,
    turned_ref,
    total_ref,
):
    step = pl.program_id(0)
    q_ref, k_ref, v_ref = three(proj_ref)
    rows_all = tokens_ref.shape[0]

    @pl.when(step == 0)
    def _():
        turned_ref[...] = first_ref[...].T
        total_ref[...] = jnp.zeros_like(total_ref)

    deltas = [delta_ref[0, head : head + 1] for head in range(2)]
    attention_back_keys(
        range(0, rows_all, TILE),
        cross_flag(lengths_ref, tokens_ref),
        q_ref,
        k_ref,
        v_ref,
        ga_ref,
        lse_ref.at[0],
        deltas,
        dq_ref,
        dk_ref,
        dv_ref,
    )
    weights = jnp.concatenate([wq_ref[...], wk_ref[...], wv_ref[...]], axis=1)
    query_sum, value_sum = in_back_pair(
        dq_ref, dk_ref, dv_ref, weights, turned_ref, out_grad_ref, chunk_ref.at[0], total_ref
    )
    bias_ref[0, 0:1] = query_sum
    bias_ref[0, 1:2] = value_sum

    @pl.when(step == pl.num_programs(0) - 1)
    def _():
        gain_grad = jnp.zeros((1, total_ref.shape[1]), F32)
        shift_grad = jnp.zeros((1, total_ref.shape[1]), F32)
        for start in range(0, rows_all, TILE):
            rows = pl.ds(start, TILE)
            tokens_grad_ref[rows], gain_part, shift_part = tokens_back(
                tokens_ref[rows], total_ref[rows], grad_middle_ref[rows], gain_ref[...]
            )
            gain_grad = gain_grad + gain_part
            shift_grad = shift_grad + shift_part
        sums_ref[0:1] = gain_grad
        sums_ref[1:2] = shift_grad


def in_back(lengths, projected, ga, lse, delta, weights, first, out_grad, tokens, gain, grad_middle):
    rows, width = tokens.shape
    pairs = width // 128
    column = pl.BlockSpec((rows, 128), lambda p: (0, p))
    square = whole((rows, width))
    return pl.pallas_call(
        in_back_kernel,
        grid=(pairs,),
        in_specs=[
            pl.BlockSpec(memory_space=pltpu.SMEM),
            pl.BlockSpec((1, rows, 384), lambda p: (p, 0, 0)),
            column,
            pl.BlockSpec((1, 8, rows), lambda p: (p, 0, 0)),
            pl.BlockSpec((1, 2, rows), lambda p: (p, 0, 0)),
            pl.BlockSpec((width, 128), lambda p: (0, p)),
            pl.BlockSpec((width, 128), lambda p: (0, pairs + p)),
            pl.BlockSpec((width, 128), lambda p: (0, 2 * pairs + p)),
            square,
            column,
            square,
            whole((1, width)),
            square,
        ],
        out_specs=[
            pl.BlockSpec((1, 8, width // TILE, 32, 512), lambda p: (p, 0, 0, 0, 0)),
            pl.BlockSpec((1, 8, 128), lambda p: (p, 0, 0)),
            square,
            whole((8, width)),
        ],
        out_shape=[
            jax.ShapeDtypeStruct((pairs, 8, width // TILE, 32, 512), BF),
            jax.ShapeDtypeStruct((pairs, 8, 128), F32),
            jax.ShapeDtypeStruct((rows, width), BF),
            jax.ShapeDtypeStruct((8, width), F32),
        ],
        scratch_shapes=[
            pltpu.VMEM((rows, 128), F32),
            pltpu.VMEM((rows, 128), F32),
            pltpu.VMEM((rows, 128), F32),
            pltpu.VMEM((width, rows), BF),
            pltpu.VMEM((rows, width), F32),
        ],
        compiler_params=params(),
        name="in_back",
    )(
        lengths,
        projected,
        ga,
        lse,
        delta,
        weights,
        weights,
        weights,
        first,
        out_grad,
        tokens,
        gain,
        grad_middle,
    )


class Place:
    def __init__(self):
        self.z = lax.axis_index("dp")
        wide = lax.axis_index("wide")
        self.y = wide // 4
        self.x = (wide // 2) % 2
        self.c = wide % 2
        self.core = (self.z, wide + 1 - 2 * self.c)
        self.side = (self.z, wide + 2 - 4 * self.x)
        self.over = (self.z, wide + 4 - 8 * self.y)
        self.ranks = (self.z + 1 - 2 * (self.z % 2), (self.z + 2) % 4, 3 - self.z)
        self.planes = tuple((rank, wide) for rank in self.ranks)

    def greet(self, planes=True):
        barrier = pltpu.get_barrier_semaphore()
        peers = (self.core, self.side, self.over) + (self.planes if planes else ())
        for peer in peers:
            pl.semaphore_signal(barrier, inc=1, device_id=peer, device_id_type=MESH)
        pl.semaphore_wait(barrier, len(peers))


class WideGather:
    copies = 10

    def __init__(
        self, place, view, count, send, recv, first, source=None, last=None, offset=0, total=None
    ):
        y, x, c = place.y, place.x, place.c
        here, side, over, far = (y, x, c), (y, 1 - x, c), (1 - y, x, c), (1 - y, 1 - x, c)
        upper, lower = pl.ds(offset, count // 2), pl.ds(offset + count // 2, count // 2)
        both = pl.ds(offset, count)
        everything = both if total is None else pl.ds(0, total)

        def copy(index, slot, part, peer):
            destination = view(*slot, part)
            return pltpu.make_async_remote_copy(
                src_ref=source.at[part] if source is not None and slot is here else destination,
                dst_ref=destination,
                send_sem=send.at[first + index],
                recv_sem=recv.at[first + index],
                device_id=peer,
                device_id_type=MESH,
            )

        self.all = (
            copy(0, here, upper, place.side),
            copy(1, here, lower, place.over),
            copy(2, here, upper, place.over),
            copy(3, here, lower, place.side),
            None if total == 0 else copy(4, here, everything, place.core),
            copy(5, side, upper, place.over),
            copy(6, over, lower, place.side),
            copy(7, side, both, place.core),
            copy(8, over, both, place.core),
            copy(9, far, both, place.core),
        )
        self.own = None
        if source is not None and last is not None:
            self.own = pltpu.make_async_copy(source, view(*here, everything), last)

    def start(self):
        if self.own is not None:
            self.own.start()
        for copy in self.all[:5]:
            if copy is not None:
                copy.start()

    def relay(self, stage):
        waits, starts = (((0, 1), (5, 6)), ((2, 3), (7, 8)), ((5, 6), (9,)))[stage]
        for index in waits:
            self.all[index].wait_recv()
        for index in starts:
            self.all[index].start()

    def finish(self):
        for index in (4, 7, 8, 9):
            if self.all[index] is not None:
                self.all[index].wait_recv()
        for copy in self.all:
            if copy is not None:
                copy.wait_send()
        if self.own is not None:
            self.own.wait()


def blocks_of(target):
    return lambda y, x, c, rows: target.at[y, x, c, rows]


LAG = 2


class Reduction:
    slots = 2 * LAG
    deep = 3 * LAG
    keep = 3 * LAG + 2

    @classmethod
    def scratch(cls):
        n, k = cls.slots, cls.keep
        return [
            pltpu.VMEM((cls.deep, 2, 2, 4, 32, 512), BF),
            pltpu.VMEM((n, 2, 2, 4, 32, 512), BF),
            pltpu.VMEM((n, 2, 2, 4, 16, 512), BF),
            pltpu.VMEM((n, 2, 4, 16, 512), BF),
            pltpu.VMEM((n, 4, 32, 512), BF),
            pltpu.VMEM((n, 3, 32, 512), BF),
            pltpu.VMEM((n, 32, 512), BF),
            pltpu.VMEM((k, 3, 32, 512), BF),
            pltpu.SemaphoreType.DMA((6, k)),
            pltpu.SemaphoreType.DMA((6, k)),
            pltpu.SemaphoreType.DMA((cls.deep,)),
        ]

    def __init__(self, place, refs):
        self.place = place
        (
            self.chip,
            self.partner,
            self.first,
            self.second,
            self.plane,
            self.from_z,
            self.sums,
            self.shared,
            self.send,
            self.recv,
            self.local,
        ) = refs

    def copy(self, index, slot, source, target, peer):
        return pltpu.make_async_remote_copy(
            src_ref=source,
            dst_ref=target,
            send_sem=self.send.at[index, slot],
            recv_sem=self.recv.at[index, slot],
            device_id=peer,
            device_id_type=MESH,
        )

    def wait(self, index, slot, arrived):
        self.copy(index, slot, arrived, arrived, self.place.core).wait()

    def load(self, chunk, source):
        slot = chunk % self.deep
        return pltpu.make_async_copy(source, self.chip.at[slot], self.local.at[slot])

    def stage0(self, chunk, view):
        slot, c = chunk % self.slots, self.place.c
        self.copy(
            0, slot, view.at[:, :, 1 - c], self.partner.at[slot], self.place.core
        ).start()
        self.load(chunk, view.at[:, :, c]).start()

    def stage1(self, chunk):
        p, slot, index = self.place, chunk % self.slots, chunk % self.deep
        partner, chip, target = self.partner.at[slot], self.chip.at[index], self.first.at[slot]
        self.load(chunk, partner).wait()
        self.wait(0, slot, partner)
        chip[...] += partner[...]
        self.copy(1, slot, chip.at[:, 1 - p.x, :, pl.ds(0, 16)], target.at[0], p.side).start()
        self.copy(1, slot, chip.at[1 - p.y, :, :, pl.ds(16, 16)], target.at[1], p.over).start()

    def stage2(self, chunk):
        p, slot, index = self.place, chunk % self.slots, chunk % self.deep
        chip, arrived, target = self.chip.at[index], self.first.at[slot], self.second.at[slot]
        self.wait(1, slot, arrived)
        for k in range(2):
            chip[k, p.x, :, 0:16] += arrived[0, k]
            chip[p.y, k, :, 16:32] += arrived[1, k]
        self.copy(2, slot, chip.at[1 - p.y, p.x, :, pl.ds(0, 16)], target.at[0], p.over).start()
        self.copy(2, slot, chip.at[p.y, 1 - p.x, :, pl.ds(16, 16)], target.at[1], p.side).start()

    def stage3(self, chunk):
        p, slot, index = self.place, chunk % self.slots, chunk % self.deep
        arrived, mine, plane = self.second.at[slot], self.chip.at[index, p.y, p.x], self.plane
        self.wait(2, slot, arrived)
        plane[slot, :, 0:16] = mine[:, 0:16] + arrived[0]
        plane[slot, :, 16:32] = mine[:, 16:32] + arrived[1]
        for k in range(3):
            target = self.from_z.at[slot, k]
            self.copy(3, slot, plane.at[slot, p.ranks[k]], target, p.planes[k]).start()

    def stage4(self, chunk):
        slot = chunk % self.slots
        self.wait(3, slot, self.from_z.at[slot])
        total = self.plane[slot, self.place.z].astype(F32)
        for k in range(3):
            total = total + self.from_z[slot, k].astype(F32)
        return total

    def spread(self, chunk, total):
        slot, place = chunk % self.slots, chunk % self.keep
        self.sums[slot] = total.astype(BF)
        peer = self.place.planes[1]
        self.copy(4, place, self.sums.at[slot], self.shared.at[place, 0], peer).start()

    def stage5(self, chunk):
        slot, place, peer = chunk % self.slots, chunk % self.keep, self.place.planes[0]
        shared = self.shared.at[place]
        self.wait(4, place, shared.at[0])
        self.copy(5, place, self.sums.at[slot], shared.at[1], peer).start()
        self.copy(5, place, shared.at[0], shared.at[2], peer).start()

    def stage6(self, chunk):
        slot, place, ranks = chunk % self.slots, chunk % self.keep, self.place.ranks
        self.wait(5, place, self.shared.at[place, pl.ds(1, 2)])
        return [
            (self.place.z, self.sums[slot]),
            (ranks[1], self.shared[place, 0]),
            (ranks[0], self.shared[place, 1]),
            (ranks[2], self.shared[place, 2]),
        ]


class SmallReduction:
    @staticmethod
    def scratch():
        return [
            pltpu.VMEM((2, 2, 2, 4, 16, 512), BF),
            pltpu.VMEM((2, 2, 4, 16, 512), BF),
            pltpu.VMEM((2, 2, 4, 16, 512), BF),
            pltpu.VMEM((2, 4, 16, 512), BF),
            pltpu.VMEM((4, 16, 512), BF),
            pltpu.VMEM((3, 16, 512), BF),
            pltpu.SemaphoreType.DMA((4,)),
            pltpu.SemaphoreType.DMA((4,)),
        ]

    def __init__(self, place, refs):
        self.place = place
        self.source, self.chip, self.partner, self.first, self.second, self.from_z = refs[:6]
        self.send, self.recv = refs[6:]

    def copy(self, index, source, target, peer):
        return pltpu.make_async_remote_copy(
            src_ref=source,
            dst_ref=target,
            send_sem=self.send.at[index],
            recv_sem=self.recv.at[index],
            device_id=peer,
            device_id_type=MESH,
        )

    def wait(self, index, arrived):
        self.copy(index, arrived, arrived, self.place.core).wait()

    def stage0(self):
        p = self.place
        self.copy(0, self.source.at[:, :, 1 - p.c], self.partner, p.core).start()

    def stage1(self):
        p = self.place
        self.wait(0, self.partner)
        self.chip[...] = self.source[:, :, p.c] + self.partner[...]
        self.copy(1, self.chip.at[:, 1 - p.x], self.first, p.side).start()

    def stage2(self):
        p = self.place
        self.wait(1, self.first)
        for k in range(2):
            self.chip[k, p.x] += self.first[k]
        self.copy(2, self.chip.at[1 - p.y, p.x], self.second, p.over).start()

    def stage3(self):
        p = self.place
        self.wait(2, self.second)
        self.chip[p.y, p.x] += self.second[...]
        for k in range(3):
            block = self.chip.at[p.y, p.x, p.ranks[k]]
            self.copy(3, block, self.from_z.at[k], p.planes[k]).start()

    def stage4(self):
        p = self.place
        self.wait(3, self.from_z)
        total = self.chip[p.y, p.x, p.z].astype(F32)
        for k in range(3):
            total = total + self.from_z[k].astype(F32)
        return total


class Stream:
    def __init__(self, view, buffers, sems):
        self.view, self.buffers, self.sems = view, buffers, sems

    def copy(self, index):
        slot = index % 2
        return pltpu.make_async_copy(self.view(index), self.buffers.at[slot], self.sems.at[slot])

    def start(self, index):
        self.copy(index).start()

    def block(self, index):
        return self.buffers.at[index % 2]


def advance(streams, index, count):
    @pl.when(index + 1 < count)
    def _():
        for stream in streams:
            stream.start(index + 1)

    for stream in streams:
        stream.copy(index).wait()


def nearness(i):
    over = (i == 3) | (i >= 5)
    side = (i == 2) | (i == 4) | (i >= 6)
    other = (i == 1) | (i == 4) | (i == 5) | (i == 7)
    return over, side, other


def unit_index(i):
    wide = lax.axis_index("wide")
    y, x, c = wide // 4, wide // 2 % 2, wide % 2
    over, side, other = nearness(i)
    y, x, c = (jnp.where(flip, 1 - k, k) for flip, k in zip((over, side, other), (y, x, c)))
    return 4 * y + 2 * x + c


class NearGather:
    copies = 3

    def __init__(self, place, source, target, send, recv, first, last):
        slot = target.at[place.y, place.x, place.c]
        self.all = [
            pltpu.make_async_remote_copy(
                src_ref=source,
                dst_ref=slot,
                send_sem=send.at[first + index],
                recv_sem=recv.at[first + index],
                device_id=peer,
                device_id_type=MESH,
            )
            for index, peer in enumerate((place.side, place.over, place.core))
        ]
        self.own = pltpu.make_async_copy(source, slot, last)

    def start(self):
        self.own.start()
        for copy in self.all:
            copy.start()

    def finish(self):
        self.own.wait()
        for copy in self.all:
            copy.wait()


class LateGather:
    copies = 5

    def __init__(self, place, near, late, send, recv, first):
        rows = near.shape[-2]
        upper, lower = pl.ds(0, rows // 2), pl.ds(rows // 2, rows // 2)
        side, over = near.at[place.y, 1 - place.x, place.c], near.at[1 - place.y, place.x, place.c]

        def copy(index, source, target, peer):
            return pltpu.make_async_remote_copy(
                src_ref=source,
                dst_ref=target,
                send_sem=send.at[first + index],
                recv_sem=recv.at[first + index],
                device_id=peer,
                device_id_type=MESH,
            )

        self.all = (
            copy(0, side.at[upper], late.at[2, upper], place.over),
            copy(1, over.at[lower], late.at[2, lower], place.side),
            copy(2, side, late.at[0], place.core),
            copy(3, over, late.at[1], place.core),
            copy(4, late.at[2], late.at[3], place.core),
        )

    def start(self):
        for copy in self.all[:4]:
            copy.start()

    def relay(self):
        for copy in self.all[:2]:
            copy.wait_recv()
        self.all[4].start()

    def arrived(self, *indices):
        for index in indices:
            self.all[index].wait_recv()

    def finish(self):
        for copy in self.all:
            copy.wait_send()


class WeightStream(Stream):
    def __init__(self, near, late, buffers, sems):
        super().__init__(lambda i: late.at[0], buffers, sems)
        self.near, self.late = near, late

    def start(self, index):
        slot = index % 2
        target, sem = self.buffers.at[slot], self.sems.at[slot]

        @pl.when(index < 4)
        def _():
            block = unit_index(index)
            view = self.near.at[block // 4, block // 2 % 2, block % 2]
            pltpu.make_async_copy(view, target, sem).start()

        @pl.when(index >= 4)
        def _():
            pltpu.make_async_copy(self.late.at[index - 4], target, sem).start()


def dma_sems(count):
    return [pltpu.SemaphoreType.DMA((count,)), pltpu.SemaphoreType.DMA((count,))]


def to_planes(place, mine, landing, send, recv, first):
    return [
        pltpu.make_async_remote_copy(
            src_ref=mine,
            dst_ref=landing(k),
            send_sem=send.at[first + k],
            recv_sem=recv.at[first + k],
            device_id=place.planes[k],
            device_id_type=MESH,
        )
        for k in range(3)
    ]


class PlanesLast:
    copies = WideGather.copies + 6

    def __init__(self, place, source, target, send, recv, last):
        view = blocks_of(target.at[place.z])
        self.wide = WideGather(place, view, source.shape[0], send, recv, 0, source, last)

        def copy(index, rank, peer):
            blocks = target.at[rank, :, :, place.c]
            return pltpu.make_async_remote_copy(
                src_ref=blocks,
                dst_ref=blocks,
                send_sem=send.at[WideGather.copies + index],
                recv_sem=recv.at[WideGather.copies + index],
                device_id=peer,
                device_id_type=MESH,
            )

        self.across = [copy(k, place.z, place.planes[k]) for k in range(3)]
        self.over = [copy(3 + k, place.ranks[k], place.core) for k in range(3)]

    def start_across(self):
        self.wide.own.wait()
        for copy in self.across:
            copy.start()

    def start_over(self):
        for arrived, copy in zip(self.across, self.over):
            arrived.wait_recv()
            copy.start()

    def finish(self):
        self.wide.own = None
        self.wide.finish()
        for copy in self.across:
            copy.wait_send()
        for copy in self.over:
            copy.wait()


def first_kernel(
    lengths_ref,
    tokens_ref,
    in_ref,
    vec_ref,
    out_ref,
    up_ref,
    unit_ref,
    hs_ref,
    turned_ref,
    proj_ref,
    scaled_ref,
    scaled_turned_ref,
    attended_ref,
    lse_ref,
    vectors_ref,
    scale_ref,
    in_all,
    out_all,
    up_all,
    unit_all,
    held_ref,
    normed_ref,
    first_ref,
    vext_ref,
    send_in,
    recv_in,
    send_out,
    recv_out,
    send_ff,
    recv_ff,
    local,
):
    step = pl.program_id(0)
    place = Place()
    width = tokens_ref.shape[1]
    count = WideGather.copies
    lanes = (3 * width // 2 + 128, 3 * width // 2)
    across, early, late = [], [], None
    for group in range(2):
        held = held_ref.at[group, :, :, :, :, :, pl.ds(0, lanes[group])]
        first = group * (3 + 2 * count)

        def blocks(planes, held=held):
            return lambda y, x, c, rows: held.at[planes, y, x, c, rows]

        mine = held.at[0, place.y, place.x, place.c]
        across.append(
            to_planes(
                place,
                mine,
                lambda k, held=held: held.at[k + 1, place.y, place.x, place.c],
                send_in,
                recv_in,
                first,
            )
        )
        if group == 0:
            for part, planes in enumerate((pl.ds(0, 1), pl.ds(1, 3))):
                start = first + 3 + part * count
                early.append(WideGather(place, blocks(planes), 32, send_in, recv_in, start))
        else:
            late = WideGather(place, blocks(pl.ds(0, 4)), 32, send_in, recv_in, first + 3)
    orders = (place.z, *place.ranks)
    out = PlanesLast(place, out_ref, out_all, send_out, recv_out, local.at[2])
    up = NearGather(place, up_ref, up_all, send_ff, recv_ff, count, local.at[3])
    unit = WideGather(
        place, blocks_of(unit_all), 32, send_ff, recv_ff, 0, unit_ref, local.at[4]
    )
    keep = [
        pltpu.make_async_copy(
            held_ref.at[group, index, :, :, :, :, pl.ds(0, lanes[1])],
            in_all.at[rank, :, :, :, :, pl.ds(group * lanes[1], lanes[1])],
            local.at[12 + 4 * group + index],
        )
        for group in range(2)
        for index, rank in enumerate(orders)
    ]

    @pl.when(step == 0)
    def _():
        place.greet()
        half = width // 2
        for group in range(2):
            mine = held_ref.at[group, 0, place.y, place.x, place.c]
            fills = []
            for pair in range(4):
                for part in range(3):
                    column = part * width + (4 * group + pair) * 128
                    fills.append(
                        pltpu.make_async_copy(
                            in_ref.at[:, pl.ds(column, 128)],
                            mine.at[:, pl.ds(pair * 384 + part * 128, 128)],
                            local.at[20 + group * 12 + pair * 3 + part],
                        )
                    )
            for copy in fills:
                copy.start()
            if group == 0:
                mine[:, 3 * half : 3 * half + 128] = jnp.zeros((32, 128), BF)
                mine[:, 3 * half : 3 * half + 32] = vec_ref[...]
            for copy in fills:
                copy.wait()
            for copy in across[group]:
                copy.start()
            if group == 0:
                early[0].start()
        scale = hs_ref[...].astype(F32)
        for pair in range(width // 128):
            own = slice(pair * 128, (pair + 1) * 128)
            low_lanes = lax.broadcasted_iota(jnp.int32, (1, 128), 1) < 64
            scale_ref[0:1, own] = jnp.where(
                low_lanes, scale[:, 2 * pair : 2 * pair + 1], scale[:, 2 * pair + 1 : 2 * pair + 2]
            )
        for start in range(0, tokens_ref.shape[0], TILE):
            rows = pl.ds(start, TILE)
            normed, _ = row_norm(tokens_ref[rows].astype(F32))
            normed_ref[rows] = normed
        early[0].relay(0)
        for copy in across[0]:
            copy.wait_recv()
        early[1].start()
        early[0].relay(1)
        early[0].relay(2)
        early[1].relay(0)
        early[1].relay(1)
        for copy in across[1]:
            copy.wait_recv()
        late.start()
        early[1].relay(2)
        out.wide.start()
        unit.start()
        for part in early:
            part.finish()
        for z in range(4):
            for y in range(2):
                tile = jnp.zeros((16, 128), F32)
                for x in range(2):
                    for c in range(2):
                        piece = held_ref[
                            0, orders[z], y, x, c, 0:16, 3 * half : 3 * half + 128
                        ].astype(F32)
                        spot = 32 * (2 * x + c)
                        tile = tile + (piece if spot == 0 else pltpu.roll(piece, spot, 1))
                vectors_ref[:, (2 * z + y) * 128 : (2 * z + y + 1) * 128] = tile
        for start in range(0, tokens_ref.shape[0], TILE):
            rows = pl.ds(start, TILE)
            first_ref[rows] = (normed_ref[rows] * vectors_ref[3:4] + vectors_ref[4:5]).astype(BF)

    @pl.when((step >= 2) & (step <= 4))
    def _():
        for stage in range(3):

            @pl.when(step == 2 + stage)
            def _():
                late.relay(stage)
                out.wide.relay(stage)
                unit.relay(stage)

    @pl.when(step == 2)
    def _():
        up.start()

    @pl.when(step == 4)
    def _():
        out.start_across()

    @pl.when(step == 5)
    def _():
        late.finish()
        for copy in keep:
            copy.start()

    @pl.when(step == 7)
    def _():
        out.start_over()

    @pl.when(step > 0)
    def _():
        pair = step - 1
        columns = pl.ds(pl.multiple_of(pair % 4 * 384, 128), 384)
        weights = jnp.concatenate(
            [held_ref[pair // 4, order, :, :, :, :, columns].reshape(TILE, 384) for order in orders]
        )
        own = pl.ds(pl.multiple_of(pair * 128, 128), 128)
        bias = jnp.concatenate(
            [vectors_ref[0:1, own], jnp.zeros((1, 128), F32), vectors_ref[1:2, own]], axis=1
        )
        project_pair(first_ref, weights, bias, proj_ref)
        attention_pair(
            cross_flag(lengths_ref, tokens_ref),
            *three(proj_ref),
            scale_ref[0:1, own],
            scaled_ref,
            attended_ref,
            lse_ref,
            vext_ref,
        )
        scaled_turned_ref[...] = scaled_ref[...].T

    @pl.when(step == pl.num_programs(0) - 1)
    def _():
        turned_ref[...] = first_ref[...].T
        for copy in (*across[0], *across[1]):
            copy.wait_send()
        for copy in keep:
            copy.wait()
        out.finish()
        unit.finish()
        up.finish()


def first_part(lengths, tokens, in_weight, vec, out_weight, up_weight, unit_rows, head_scale):
    rows, width = tokens.shape
    pairs = width // 128

    def at(step):
        return jnp.maximum(step - 1, 0)

    column = pl.BlockSpec((rows, 128), lambda s: (0, at(s)))
    held = (2, 4, 2, 2, 2, 32, 3 * width // 2 + 128)
    return pl.pallas_call(
        first_kernel,
        grid=(pairs + 1,),
        in_specs=[
            pl.BlockSpec(memory_space=pltpu.SMEM),
            whole((rows, width)),
            ANY,
            whole(vec.shape),
            ANY,
            ANY,
            ANY,
            whole(head_scale.shape),
        ],
        out_specs=[
            whole((width, rows)),
            pl.BlockSpec((1, rows, 384), lambda s: (at(s), 0, 0)),
            column,
            pl.BlockSpec((128, rows), lambda s: (at(s), 0)),
            column,
            pl.BlockSpec((1, 8, rows), lambda s: (at(s), 0, 0)),
            whole((16, width)),
            whole((8, width)),
            ANY,
            ANY,
            ANY,
            ANY,
        ],
        out_shape=[
            jax.ShapeDtypeStruct((width, rows), BF),
            jax.ShapeDtypeStruct((pairs, rows, 384), BF),
            jax.ShapeDtypeStruct((rows, width), BF),
            jax.ShapeDtypeStruct((width, rows), BF),
            jax.ShapeDtypeStruct((rows, width), F32),
            jax.ShapeDtypeStruct((pairs, 8, rows), F32),
            jax.ShapeDtypeStruct((16, width), F32),
            jax.ShapeDtypeStruct((8, width), F32),
            jax.ShapeDtypeStruct((4, 2, 2, 2, 32, 3 * width), BF),
            jax.ShapeDtypeStruct((4, 2, 2, 2, *out_weight.shape), BF),
            jax.ShapeDtypeStruct((2, 2, 2, *up_weight.shape), BF),
            jax.ShapeDtypeStruct((2, 2, 2, *unit_rows.shape), BF),
        ],
        scratch_shapes=[
            pltpu.VMEM(held, BF),
            pltpu.VMEM((rows, width), F32),
            pltpu.VMEM((rows, width), BF),
            pltpu.VMEM((rows, 256), BF),
            *dma_sems(6 + 3 * WideGather.copies),
            *dma_sems(PlanesLast.copies),
            *dma_sems(WideGather.copies + NearGather.copies),
            pltpu.SemaphoreType.DMA((44,)),
        ],
        compiler_params=params(collective_id=0, has_side_effects=True),
        name="first_part",
    )(lengths, tokens, in_weight, vec, out_weight, up_weight, unit_rows, head_scale)


def second_kernel(
    units,
    scaled_ref,
    weight_ref,
    vec_ref,
    tokens_ref,
    unit_ref,
    up_near,
    down_ref,
    branch_ref,
    middle_ref,
    turned_ref,
    act_ref,
    slope_ref,
    stats_ref,
    up_late,
    down_near,
    feed_ref,
    sums_ref,
    up_ref,
    send,
    recv,
    local,
    stream_sems,
):
    step = pl.program_id(0)
    lead = feed_ref.shape[0] // TILE
    place = Place()
    late = LateGather(place, up_near, up_late, send, recv, 0)
    down = NearGather(place, down_ref, down_near, send, recv, LateGather.copies, local.at[0])
    up = WeightStream(up_near, up_late, up_ref, stream_sems)

    @pl.when(step == 0)
    def _():
        place.greet(planes=False)
        late.start()
        up.start(0)
        sums_ref[...] = jnp.zeros_like(sums_ref)

    @pl.when(step == 2)
    def _():
        down.start()

    @pl.when(step < lead)
    def _():
        rows = pl.ds(pl.multiple_of(step * TILE, TILE), TILE)
        feed_ref[rows] = out_proj_rows(
            scaled_ref, weight_ref, vec_ref, tokens_ref, branch_ref, middle_ref
        )

    @pl.when(step >= lead)
    def _():
        block = step - lead

        @pl.when(block == 2)
        def _():
            late.relay()

        @pl.when(block == 3)
        def _():
            late.arrived(2, 3)

        @pl.when(block == 6)
        def _():
            late.arrived(4)

        advance((up,), block, 8)
        up_step(feed_ref, up.block(block), unit_ref.at[0], act_ref, slope_ref, sums_ref)

    @pl.when(step == pl.num_programs(0) - 1)
    def _():
        up_stats(units, stats_ref, sums_ref)
        turned_ref[...] = feed_ref[...].T
        late.finish()
        down.finish()


def second_part(scaled, out_weights, vectors, tokens, up_near, unit_vec, down_weight):
    rows, width = tokens.shape
    steps = 8
    lead = rows // TILE

    def early(step):
        return jnp.minimum(step, lead - 1)

    def unit(step):
        return unit_index(jnp.maximum(step - lead, 0))

    by_row = pl.BlockSpec((TILE, width), lambda s: (early(s), 0))
    block = pl.BlockSpec((1, rows, UNITS), lambda s: (unit(s), 0, 0))
    return pl.pallas_call(
        functools.partial(second_kernel, steps * UNITS),
        grid=(lead + steps,),
        in_specs=[
            by_row,
            whole((width, width)),
            whole(vectors.shape),
            by_row,
            pl.BlockSpec((1, unit_vec.shape[1], UNITS), lambda s: (unit(s), 0, 0)),
            ANY,
            ANY,
        ],
        out_specs=[
            by_row,
            by_row,
            whole((width, rows)),
            block,
            block,
            whole((rows, 128)),
            ANY,
            ANY,
        ],
        out_shape=[
            jax.ShapeDtypeStruct((rows, width), F32),
            jax.ShapeDtypeStruct((rows, width), F32),
            jax.ShapeDtypeStruct((width, rows), BF),
            jax.ShapeDtypeStruct((steps, rows, UNITS), BF),
            jax.ShapeDtypeStruct((steps, rows, UNITS), BF),
            jax.ShapeDtypeStruct((rows, 128), F32),
            jax.ShapeDtypeStruct((4, *up_near.shape[3:]), BF),
            jax.ShapeDtypeStruct((2, 2, 2, *down_weight.shape), BF),
        ],
        scratch_shapes=[
            pltpu.VMEM((rows, width), BF),
            pltpu.VMEM((2, rows, 128), F32),
            pltpu.VMEM((2, *up_near.shape[3:]), BF),
            *dma_sems(LateGather.copies + NearGather.copies),
            pltpu.SemaphoreType.DMA((1,)),
            pltpu.SemaphoreType.DMA((2,)),
        ],
        compiler_params=params(collective_id=2, has_side_effects=True),
        name="second_part",
    )(scaled, out_weights, vectors, tokens, unit_vec, up_near, down_weight)


def third_kernel(
    units,
    act_ref,
    stats_ref,
    vec_ref,
    cot_ref,
    middle_ref,
    shift_ref,
    down_near,
    mixed_ref,
    down_grad_ref,
    e_ref,
    all_stats_ref,
    vec_grad_ref,
    down_late,
    total_ref,
    sums_ref,
    low_ref,
    down_ref,
    send,
    recv,
    stream_sems,
):
    step = pl.program_id(0)
    place = Place()
    late = LateGather(place, down_near, down_late, send, recv, 0)
    down = WeightStream(down_near, down_late, down_ref, stream_sems)

    @pl.when(step == 0)
    def _():
        place.greet(planes=False)
        late.start()
        down.start(0)
        total_ref[...] = jnp.zeros_like(total_ref)
        sums_ref[...] = jnp.zeros_like(sums_ref)

    @pl.when(step == 3)
    def _():
        late.relay()
        late.arrived(2, 3)

    @pl.when(step == 6)
    def _():
        late.arrived(4)

    advance((down,), step, 8)
    down_step(
        act_ref, stats_ref, vec_ref.at[0], down.block(step), cot_ref, down_grad_ref, e_ref,
        vec_grad_ref, total_ref, sums_ref, low_ref
    )

    @pl.when(step == pl.num_programs(0) - 1)
    def _():
        down_end(
            units, stats_ref, middle_ref, shift_ref, mixed_ref, all_stats_ref, total_ref, sums_ref
        )
        late.finish()


def third_part(act, stats, vec, down_near, cotangent, middle, shift):
    rows, width = cotangent.shape
    steps = 8

    def unit(shape):
        return pl.BlockSpec((1, *shape), lambda s: (unit_index(s), 0, 0))

    block = unit((rows, UNITS))
    return pl.pallas_call(
        functools.partial(third_kernel, steps * UNITS),
        grid=(steps,),
        in_specs=[
            block,
            whole((rows, 128)),
            unit((vec.shape[1], UNITS)),
            whole((rows, width)),
            whole((rows, width)),
            whole((1, width)),
            ANY,
        ],
        out_specs=[
            whole((rows, width)),
            unit((UNITS, width)),
            block,
            whole((rows, 128)),
            unit((8, UNITS)),
            ANY,
        ],
        out_shape=[
            jax.ShapeDtypeStruct((rows, width), BF),
            jax.ShapeDtypeStruct((steps, UNITS, width), BF),
            jax.ShapeDtypeStruct((steps, rows, UNITS), BF),
            jax.ShapeDtypeStruct((rows, 128), F32),
            jax.ShapeDtypeStruct((steps, 8, UNITS), F32),
            jax.ShapeDtypeStruct((4, *down_near.shape[3:]), BF),
        ],
        scratch_shapes=[
            pltpu.VMEM((rows, width), F32),
            pltpu.VMEM((2, rows, 128), F32),
            pltpu.VMEM((rows, UNITS), BF),
            pltpu.VMEM((2, *down_near.shape[3:]), BF),
            *dma_sems(LateGather.copies),
            pltpu.SemaphoreType.DMA((2,)),
        ],
        compiler_params=params(collective_id=3, has_side_effects=True),
        name="third_part",
    )(act, stats, vec, cotangent, middle, shift, down_near)


NORMS_AT, COLUMNS_AT, HEADS_AT, TOKENS_AT, VECTORS_AT = 8, 16, 20, 28, 32
BACK_STEPS = VECTORS_AT + 7
OUT_TILE = 128


def chunk_at(time):
    chunk = jnp.where(time < 13, time, time - 1)
    chunk = jnp.where(time >= 20, (time + 17) // 2, chunk)
    return chunk, (time >= 0) & ((time < 13) | ((time >= 14) & (time < 20)) | ((time >= 20) & (time < 30) & (time % 2 == 1)))


def back_kernel(
    lengths_ref,
    unit_grad_ref,
    vec_ref,
    hs_ref,
    act_all,
    slope_all,
    e_all,
    stats_all,
    up_near,
    up_late,
    feed_turned_all,
    down_grad_all,
    cot_all,
    middle_all,
    branch_all,
    scaled_turned_all,
    attended_all,
    out_weight_all,
    proj_all,
    lse_all,
    in_weight_all,
    turned_all,
    tokens_all,
    down_out,
    up_out,
    in_out,
    out_out,
    vec_out,
    tokens_grad_all,
    up_grad_all,
    units_in_ref,
    up_ref,
    stats_ref,
    feed_turned_ref,
    cot_ref,
    norms_in_ref,
    scaled_turned_ref,
    attended_ref,
    out_weight_ref,
    proj_ref,
    lse_ref,
    in_weight_ref,
    turned_ref,
    tokens_ref,
    tokens_grad_ref,
    staged_ref,
    total_ref,
    low_ref,
    out_grad_ref,
    ga_ref,
    grad_middle_ref,
    delta_ref,
    delta_sum_ref,
    sums_ref,
    units_ref,
    dq_ref,
    dk_ref,
    dv_ref,
    chunk_ref,
    stream_sems,
    fetch_sems,
    *scratch,
):
    step = pl.program_id(0)
    place = Place()
    engine = Reduction(place, scratch[:11])
    small = SmallReduction(place, scratch[11:])
    pairs = proj_all.shape[0]

    def rows_of(array, size):
        return lambda i: array.at[pl.ds(pl.multiple_of(i * size, size), size)]

    def columns_of(array, size):
        return lambda i: array.at[:, pl.ds(pl.multiple_of(i * size, size), size)]

    def stream(number, view, buffers):
        return Stream(view, buffers, stream_sems.at[number])

    act, slope, e = (
        stream(k, lambda i, array=array: array.at[unit_index(i)], units_in_ref.at[k])
        for k, array in enumerate((act_all, slope_all, e_all))
    )
    up = WeightStream(up_near, up_late, up_ref, stream_sems.at[3])
    cot = stream(4, rows_of(cot_all, OUT_TILE), cot_ref)
    middle = stream(5, rows_of(middle_all, OUT_TILE), norms_in_ref.at[0])
    branch = stream(6, rows_of(branch_all, OUT_TILE), norms_in_ref.at[1])
    attended = stream(7, columns_of(attended_all, TILE), attended_ref)
    proj = stream(8, lambda i: proj_all.at[i], proj_ref)
    lse = stream(9, lambda i: lse_all.at[i], lse_ref)
    in_weight = stream(10, columns_of(in_weight_all, 384), in_weight_ref)
    tokens = stream(11, rows_of(tokens_all, TILE), tokens_ref)
    put = rows_of(tokens_grad_all, TILE)

    def put_tokens(i):
        return pltpu.make_async_copy(
            tokens_grad_ref.at[i % 2], put(i), stream_sems.at[12, i % 2]
        )

    fetches = [
        pltpu.make_async_copy(source, target, fetch_sems.at[index])
        for index, (source, target) in enumerate(
            (
                (stats_all, stats_ref),
                (feed_turned_all, feed_turned_ref),
                (scaled_turned_all, scaled_turned_ref),
                (out_weight_all, out_weight_ref),
                (turned_all, turned_ref),
            )
        )
    ]

    @pl.when(step == 0)
    def _():
        for item in (act, slope, e, up):
            item.start(0)
        for copy in fetches:
            copy.start()
        for item in (cot, middle, branch, attended, proj, lse, in_weight, tokens):
            item.copy(0).start()
        total_ref[...] = jnp.zeros_like(total_ref)
        sums_ref[...] = jnp.zeros_like(sums_ref)
        units_ref[...] = jnp.zeros_like(units_ref)
        place.greet()

    def store(index):
        block = unit_index(index)
        view = up_grad_all.at[block // 4, block // 2 % 2, block % 2]
        return pltpu.make_async_copy(staged_ref, view, fetch_sems.at[5])

    @pl.when((step >= 1) & (step <= NORMS_AT))
    def _():
        store(step - 1).wait()


    def stage(number, kind, action, tick):
        chunk, there = chunk_at(tick - number * LAG)
        up = ((chunk >= 8) & (chunk < 14)) | (chunk == 15) | (chunk == 17)
        wanted = {
            "all": there,
            "down": there & (chunk < 8),
            "up": there & up,
            "shared": there & ((chunk < 8) | up),
            "own": there & (chunk >= 8) & ~up,
        }

        @pl.when(wanted[kind])
        def _():
            action(chunk)

    def up_index(chunk):
        return jnp.where(chunk < 14, chunk - 8, (chunk - 3) // 2)

    def pair_index(chunk):
        return jnp.where(chunk < 18, (chunk - 14) // 2, chunk - 16)

    def put_down(chunk):
        for rank, block in engine.stage6(chunk):
            for half in range(2):

                @pl.when(chunk % 2 == half)
                def _():
                    down_out[chunk // 2, rank, :, half * 512 : half * 512 + 512] = block

    def put_up(chunk):
        for rank, block in engine.stage6(chunk):
            up_out[up_index(chunk), rank] = block

    def put_own(chunk):
        total = engine.stage4(chunk)
        first = pair_index(chunk) * 128
        for part in range(3):
            lanes = pl.ds(pl.multiple_of(part * 1024 + first, 128), 128)
            in_out[:, lanes] = total[:, part * 128 : part * 128 + 128]
        out_out[:, pl.ds(pl.multiple_of(first, 128), 128)] = total[:, 384:512]

    def take_down(chunk):
        lanes = pl.ds(pl.multiple_of(chunk % 2 * 512, 512), 512)
        engine.stage0(chunk, down_grad_all.at[:, :, :, chunk // 2, :, :, lanes])

    def take_up(chunk):
        engine.stage0(chunk, up_grad_all.at[:, :, :, up_index(chunk)])

    def take_own(chunk):
        engine.stage0(chunk, chunk_ref.at[pair_index(chunk) % 2])

    def reduce_step(tick):
        stage(6, "down", put_down, tick)
        stage(6, "up", put_up, tick)
        stage(5, "shared", engine.stage5, tick)
        stage(4, "shared", lambda chunk: engine.spread(chunk, engine.stage4(chunk)), tick)
        stage(4, "own", put_own, tick)
        stage(3, "all", engine.stage3, tick)
        stage(2, "all", engine.stage2, tick)
        stage(1, "all", engine.stage1, tick)
        stage(0, "down", take_down, tick)
        stage(0, "up", take_up, tick)

    tick = jnp.where(step < NORMS_AT, step, NORMS_AT + (step - NORMS_AT) // 4)
    tick = jnp.where(step < COLUMNS_AT, tick, step - 6)
    tick = jnp.where(step < HEADS_AT, tick, 2 * step - 26)
    tick = jnp.where(step < TOKENS_AT, tick, 30)
    tick = jnp.where(step < VECTORS_AT, tick, step - 1)
    within = (step > NORMS_AT) & (step < COLUMNS_AT) & (step % 4 != 0)
    within = within | ((step > TOKENS_AT) & (step < VECTORS_AT))

    @pl.when(~within)
    def _():
        reduce_step(tick)


    @pl.when(step < NORMS_AT)
    def _():
        advance((act, slope, e, up), step, NORMS_AT)

        @pl.when(step == 0)
        def _():
            fetches[0].wait()

        unit = unit_index(step)
        units_ref[unit, 0:1] = up_back_step(
            act.block(step),
            slope.block(step),
            e.block(step),
            stats_ref,
            up.block(step),
            low_ref,
            total_ref,
        )
        units_ref[unit, 1:3] = unit_grad_ref[unit, 0:2]

        @pl.when(step == 0)
        def _():
            fetches[1].wait()

        for left in range(0, UNITS, TILE):
            columns = slice(left, left + TILE)
            grad = dot_nn(feed_turned_ref[...], low_ref[:, columns]).astype(BF)
            staged_ref[:, :, :, columns] = grad.reshape(8, 4, 32, TILE)
        store(step).start()


    @pl.when((step >= NORMS_AT) & (step < COLUMNS_AT))
    def _():
        block = step - NORMS_AT
        rows = pl.ds(pl.multiple_of(block * OUT_TILE, OUT_TILE), OUT_TILE)
        advance((cot, middle, branch), block, COLUMNS_AT - NORMS_AT)
        grad_middle, low = norms_back(
            total_ref[rows],
            cot.block(block),
            middle.block(block),
            branch.block(block),
            vec_ref,
            sums_ref,
        )
        grad_middle_ref[rows] = grad_middle
        low_ref[rows] = low

    @pl.when((step >= COLUMNS_AT) & (step < HEADS_AT))
    def _():
        block = step - COLUMNS_AT
        columns = pl.ds(pl.multiple_of(block * TILE, TILE), TILE)
        advance((attended,), block, HEADS_AT - COLUMNS_AT)

        @pl.when(block == 0)
        def _():
            fetches[2].wait()
            fetches[3].wait()

        grad_out, delta = heads_back(
            low_ref[...],
            out_weight_ref[columns],
            hs_ref[0:1, columns],
            attended.block(block)[...],
        )
        ga_ref[:, columns] = grad_out
        delta_sum_ref[block, 0:1] = column_sum(delta)
        turned = delta.T
        for head in range(4):
            delta_ref[4 * block + head] = turned[head : head + 1]
        out_grad_ref[:, columns] = dot_nn(scaled_turned_ref[...], low_ref[:, columns]).astype(BF)

    @pl.when(step == HEADS_AT - 1)
    def _():
        total_ref[...] = jnp.zeros_like(total_ref)


    @pl.when((step >= HEADS_AT) & (step < TOKENS_AT))
    def _():
        pair = step - HEADS_AT
        columns = pl.ds(pl.multiple_of(pair * 128, 128), 128)
        advance((proj, lse, in_weight), pair, pairs)

        @pl.when(pair == 0)
        def _():
            fetches[4].wait()

        for part, starts in enumerate(((0, 3 * TILE), (TILE, 2 * TILE))):
            if part == 1:
                reduce_step(tick + 1)
            attention_back_keys(
                starts,
                cross_flag(lengths_ref, total_ref),
                *[proj.block(pair).at[:, pl.ds(index * 128, 128)] for index in range(3)],
                ga_ref.at[:, columns],
                lse.block(pair),
                [delta_ref[2 * pair], delta_ref[2 * pair + 1]],
                dq_ref,
                dk_ref,
                dv_ref,
            )
        query_sum, value_sum = in_back_pair(
            dq_ref,
            dk_ref,
            dv_ref,
            in_weight.block(pair)[...],
            turned_ref,
            out_grad_ref.at[:, columns],
            chunk_ref.at[pair % 2].reshape(8, 4, 32, 512),
            total_ref,
        )
        sums_ref[0:1, columns] = query_sum
        sums_ref[1:2, columns] = value_sum
        stage(0, "own", take_own, tick + 1)

    @pl.when((step >= TOKENS_AT) & (step < TOKENS_AT + 4))
    def _():
        block = step - TOKENS_AT
        rows = pl.ds(pl.multiple_of(block * TILE, TILE), TILE)
        advance((tokens,), block, 4)

        @pl.when(block >= 2)
        def _():
            put_tokens(block - 2).wait()

        result, gain_grad, shift_grad = tokens_back(
            tokens.block(block)[...], total_ref[rows], grad_middle_ref[rows], vec_ref[3:4]
        )
        tokens_grad_ref[block % 2] = result
        put_tokens(block).start()
        sums_ref[3:4] += gain_grad
        sums_ref[4:5] += shift_grad


    @pl.when(step == VECTORS_AT)
    def _():
        for y in range(2):
            for z in range(4):
                own = slice((2 * z + y) * 128, (2 * z + y + 1) * 128)
                for index in range(9):
                    lanes = slice(index % 4 * 128, index % 4 * 128 + 128)
                    row = 6 + index // 4
                    units_ref[8, row : row + 1, lanes] = sums_ref[index : index + 1, own]
                for x in range(2):
                    for c in range(2):
                        unit = 4 * y + 2 * x + c
                        units_ref[8, 0:3] = units_ref[unit, 0:3]
                        if (y, z, x, c) == (0, 0, 0, 0):
                            units_ref[8, 3:4] = sums_ref[9:10, 0:UNITS]
                            units_ref[8, 4:5] = sums_ref[9:10, UNITS : 2 * UNITS]
                            for block in range(4):
                                lanes = slice(block * 128, block * 128 + 128)
                                units_ref[8, 5:6, lanes] = delta_sum_ref[block, 0:1]
                        small.source[y, x, c, z] = units_ref[8].astype(BF)
        small.stage0()

    for index, action in enumerate((small.stage1, small.stage2, small.stage3)):

        @pl.when(step == VECTORS_AT + 1 + index)
        def _():
            action()

    @pl.when(step == VECTORS_AT + 4)
    def _():
        vec_out[...] = small.stage4()
        for block in range(2, 4):
            put_tokens(block).wait()


def back_part(
    lengths,
    act,
    slope,
    e,
    stats,
    up_near,
    up_late,
    feed_turned,
    unit_grad,
    down_grad,
    cotangent,
    middle,
    branch,
    scaled_turned,
    attended,
    out_weights,
    vectors,
    head_lanes,
    projected,
    lse,
    weights,
    turned,
    tokens,
):
    rows, width = tokens.shape
    pairs = width // 128

    return pl.pallas_call(
        back_kernel,
        grid=(BACK_STEPS,),
        in_specs=[
            pl.BlockSpec(memory_space=pltpu.SMEM),
            whole(unit_grad.shape),
            whole(vectors.shape),
            whole(head_lanes.shape),
            *[ANY] * 19,
        ],
        out_specs=[
            whole((4, 4, 32, 1024)),
            whole((8, 4, 32, 512)),
            whole((32, 3 * width)),
            whole((32, width)),
            whole((16, 512)),
            ANY,
            ANY,
        ],
        out_shape=[
            jax.ShapeDtypeStruct((4, 4, 32, 1024), BF),
            jax.ShapeDtypeStruct((8, 4, 32, 512), BF),
            jax.ShapeDtypeStruct((32, 3 * width), F32),
            jax.ShapeDtypeStruct((32, width), F32),
            jax.ShapeDtypeStruct((16, 512), F32),
            jax.ShapeDtypeStruct((rows, width), BF),
            jax.ShapeDtypeStruct((2, 2, 2, 8, 4, 32, UNITS), BF),
        ],
        scratch_shapes=[
            pltpu.VMEM((3, 2, rows, UNITS), BF),
            pltpu.VMEM((2, width, UNITS), BF),
            pltpu.VMEM((rows, 128), F32),
            pltpu.VMEM((width, rows), BF),
            pltpu.VMEM((2, OUT_TILE, width), BF),
            pltpu.VMEM((2, 2, OUT_TILE, width), F32),
            pltpu.VMEM((width, rows), BF),
            pltpu.VMEM((2, rows, TILE), F32),
            pltpu.VMEM((width, width), BF),
            pltpu.VMEM((2, rows, 384), BF),
            pltpu.VMEM((2, 8, rows), F32),
            pltpu.VMEM((2, width, 384), BF),
            pltpu.VMEM((width, rows), BF),
            pltpu.VMEM((2, TILE, width), BF),
            pltpu.VMEM((2, TILE, width), BF),
            pltpu.VMEM((8, 4, 32, UNITS), BF),
            pltpu.VMEM((rows, width), F32),
            pltpu.VMEM((rows, width), BF),
            pltpu.VMEM((width, width), BF),
            pltpu.VMEM((rows, width), BF),
            pltpu.VMEM((rows, width), F32),
            pltpu.VMEM((2 * pairs, 1, rows), F32),
            pltpu.VMEM((4, 8, 128), F32),
            pltpu.VMEM((16, width), F32),
            pltpu.VMEM((9, 16, UNITS), F32),
            pltpu.VMEM((rows, 128), F32),
            pltpu.VMEM((rows, 128), F32),
            pltpu.VMEM((rows, 128), F32),
            pltpu.VMEM((2, 2, 2, 2, 4, 32, 512), BF),
            pltpu.SemaphoreType.DMA((13, 2)),
            pltpu.SemaphoreType.DMA((6,)),
            *Reduction.scratch(),
            *SmallReduction.scratch(),
        ],
        compiler_params=params(collective_id=1, has_side_effects=True),
        name="back_part",
    )(
        lengths,
        unit_grad,
        vectors,
        head_lanes,
        act,
        slope,
        e,
        stats,
        up_near,
        up_late,
        feed_turned,
        down_grad.reshape(2, 2, 2, 4, 4, 32, width),
        cotangent,
        middle,
        branch,
        scaled_turned,
        attended,
        out_weights,
        projected,
        lse,
        weights,
        turned,
        tokens,
    )


def layer(staged, tokens, cotangent, lengths, attn, up, down, unit_vec, head_scale, down_bias):
    rows, width = tokens.shape
    heads = head_scale.shape[0]
    pairs = width // 128
    if staged:
        in_weight, out_weight, vec_block = attn
        (
            turned,
            projected,
            scaled,
            scaled_turned,
            attended,
            lse,
            vectors,
            head_lanes,
            weights,
            out_weights,
            up,
            unit_vec,
        ) = first_part(
            lengths, tokens, in_weight, vec_block, out_weight, up, unit_vec, head_scale[None, :]
        )
        weights = weights.reshape(width, 3 * width)
        out_weights = out_weights.reshape(width, width)
        unit_vec = unit_vec.reshape(-1, unit_vec.shape[-2], UNITS)
        branch, middle, feed_turned, act, slope, stats, up_late, down_near = second_part(
            scaled, out_weights, vectors, tokens, up, unit_vec, down
        )
        mixed, down_grad, e, stats, unit_grad, _ = third_part(
            act, stats, unit_vec, down_near, cotangent, middle, down_bias[None, :]
        )
    else:
        weights, out_weights, vectors = attn
        scale = head_scale.astype(F32)
        head_lanes = jnp.repeat(scale, width // heads)[None, :]
        first, projected, scaled, attended, lse = plain_first(
            lengths, tokens, weights, vectors, head_lanes
        )
        branch, middle, feed = out_proj(scaled, out_weights, vectors, tokens)
        act, slope, stats = up_pass(feed, up, unit_vec)
        mixed, down_grad, e, stats, unit_grad = down_pass(
            act, stats, unit_vec, down, cotangent, middle, down_bias[None, :]
        )
    if staged:
        down_total, up_total, in_total, out_total, vec_shares, tokens_grad, _ = back_part(
            lengths,
            act,
            slope,
            e,
            stats,
            up,
            up_late,
            feed_turned,
            unit_grad,
            down_grad,
            cotangent,
            middle,
            branch,
            scaled_turned,
            attended,
            out_weights,
            vectors,
            head_lanes,
            projected,
            lse,
            weights,
            turned,
            tokens,
        )
        return mixed, tokens_grad, down_total, up_total, in_total, out_total, vec_shares
    up_grad, up_bias_grad, grad_feed = up_back(
        act, slope, e, stats, up, feed
    )
    grad_middle, ga, out_grad, delta, sums = out_back(
        grad_feed,
        cotangent,
        middle,
        branch,
        scaled,
        attended,
        out_weights,
        vectors,
        head_lanes,
    )
    chunks, proj_bias, tokens_grad, pre_sums = in_back(
        lengths,
        projected,
        ga,
        lse,
        delta.reshape(pairs, 2, rows),
        weights,
        first,
        out_grad,
        tokens,
        vectors[3:4],
        grad_middle,
    )
    scale_grad = jnp.sum(delta, axis=1) / scale
    vec_grads = [
        proj_bias[:, 0].reshape(width),
        proj_bias[:, 1].reshape(width),
        sums[2],
        pre_sums[0],
        pre_sums[1],
        sums[5],
        sums[6],
        sums[7],
        sums[8],
    ]
    unit_grads = [up_bias_grad[:, 0], unit_grad[:, 0], unit_grad[:, 1]]
    return mixed, tokens_grad, chunks, up_grad, down_grad, vec_grads, unit_grads, sums[9], scale_grad


def body(
    axes,
    tokens,
    cotangent,
    lengths,
    in_weight,
    query_bias,
    value_bias,
    out_weight,
    out_bias,
    head_scale,
    pre_gain,
    pre_bias,
    post_gain,
    post_bias,
    feed_gain,
    feed_bias,
    up_weight,
    up_bias,
    mid_gain,
    mid_bias,
    down_weight,
    down_bias,
):
    planes, wide = axes
    every = ("dp", "wide")
    staged = (planes, wide) == (4, 8)
    rows, width = tokens.shape
    units = down_weight.shape[0] * wide
    steps = units // UNITS
    share = in_weight.shape[0]
    columns = [
        query_bias,
        value_bias,
        out_bias,
        pre_gain,
        pre_bias,
        post_gain,
        post_bias,
        feed_gain,
        feed_bias,
    ]
    index = lax.broadcasted_iota(jnp.int32, (32, up_bias.shape[0]), 0)
    unit_rows = jnp.where(index == 0, up_bias[None, :], jnp.zeros((), BF))
    unit_rows = jnp.where(index == 1, mid_gain[None, :], unit_rows)
    unit_rows = jnp.where(index == 2, mid_bias[None, :], unit_rows)
    if staged:
        index = lax.broadcasted_iota(jnp.int32, (32, share), 0)
        vec_block = jnp.zeros((32, share), BF)
        for row, column in enumerate(columns):
            vec_block = jnp.where(index == row, column[None, :], vec_block)
        attn = (in_weight, out_weight, vec_block)
        up, unit_vec, down = up_weight, unit_rows, down_weight
    else:
        flat = jnp.concatenate(columns).reshape(len(columns), share)
        attn = (
            lax.all_gather(in_weight, every, axis=0, tiled=True),
            lax.all_gather(out_weight, every, axis=0, tiled=True),
            jnp.pad(
                lax.all_gather(flat, every, axis=1, tiled=True), ((0, 16 - len(columns)), (0, 0))
            ).astype(F32),
        )
        up = lax.all_gather(up_weight, "wide", axis=1, tiled=True)
        up = up.reshape(width, steps, UNITS).transpose(1, 0, 2)
        unit_vec = lax.all_gather(unit_rows, "wide", axis=1, tiled=True)
        unit_vec = unit_vec.reshape(32, steps, UNITS).transpose(1, 0, 2)
        down = lax.all_gather(down_weight, "wide", axis=0, tiled=True)
        down = down.reshape(steps, UNITS, width)
    results = layer(
        staged,
        tokens,
        cotangent,
        lengths,
        attn,
        up,
        down,
        unit_vec,
        head_scale,
        down_bias,
    )
    heads = head_scale.shape[0]
    pairs = width // 128
    if staged:
        mixed, tokens_grad, down_total, up_total, in_total, out_total, vec_shares = results
        up_total = up_total.astype(F32).reshape(width, UNITS)
        down_total = down_total.astype(F32).reshape(UNITS, width)
        unit_totals = [vec_shares[index] for index in range(3)]
        down_sum = vec_shares[3:5].reshape(width)
        scale_sum = vec_shares[5].reshape(4, 128)[:, :4].reshape(heads) / head_scale.astype(F32)
        offset = share * lax.rem(lax.axis_index("wide"), 128 // share)
        own = vec_shares[6:9].reshape(12, 128)
        own = lax.dynamic_slice(own, (0, offset), (len(columns), share))
        vec_totals = [own[index] for index in range(len(columns))]
    else:
        (mixed, tokens_grad, chunks, up_grad, down_grad, vec_grads, unit_grads) = results[:7]
        down_sum, scale_sum = results[7:]

        def scatter(value, axis=0, over=every):
            return lax.psum_scatter(value, over, scatter_dimension=axis, tiled=True)

        def both_ways(value, axis):
            part = scatter(value.astype(BF), axis, "wide")
            return lax.psum(part, "dp").astype(F32)

        up_total = both_ways(up_grad.transpose(1, 0, 2).reshape(width, units), 1)
        down_total = both_ways(down_grad.reshape(units, width), 0)
        unit_totals = [
            lax.psum(scatter(item.reshape(units), 0, "wide"), "dp") for item in unit_grads
        ]
        down_sum, scale_sum = lax.psum((down_sum, scale_sum), every)
        vec_totals = [scatter(item) for item in vec_grads]
        natural = chunks.transpose(0, 2, 1, 3, 4).reshape(pairs, width, 512)
        in_total = natural[:, :, :384].reshape(pairs, width, 3, 128)
        in_total = scatter(in_total.transpose(1, 2, 0, 3).reshape(width, 3 * width).astype(F32))
        out_total = scatter(
            natural[:, :, 384:].transpose(1, 0, 2).reshape(width, width).astype(F32)
        )
    return (
        mixed,
        tokens_grad,
        in_total,
        vec_totals[0],
        vec_totals[1],
        out_total,
        vec_totals[2],
        scale_sum,
        vec_totals[3],
        vec_totals[4],
        vec_totals[5],
        vec_totals[6],
        vec_totals[7],
        vec_totals[8],
        up_total,
        unit_totals[0],
        unit_totals[1],
        unit_totals[2],
        down_total,
        down_sum,
    )


def solution(mesh):
    by_all = P(("dp", "wide"))
    rows_all = P(("dp", "wide"), None)
    axes = (mesh.shape["dp"], mesh.shape["wide"])
    return jax.shard_map(
        functools.partial(body, axes),
        mesh=mesh,
        in_specs=(
            rows_all,
            rows_all,
            rows_all,
            rows_all,
            by_all,
            by_all,
            rows_all,
            by_all,
            P(),
            by_all,
            by_all,
            by_all,
            by_all,
            by_all,
            by_all,
            P(None, "wide"),
            P("wide"),
            P("wide"),
            P("wide"),
            P("wide", None),
            P(),
        ),
        out_specs=(
            rows_all,
            rows_all,
            rows_all,
            by_all,
            by_all,
            rows_all,
            by_all,
            P(),
            by_all,
            by_all,
            by_all,
            by_all,
            by_all,
            by_all,
            P(None, "wide"),
            P("wide"),
            P("wide"),
            P("wide"),
            P("wide", None),
            P(),
        ),
        check_vma=False,
    )
```

```python
import functools

import jax
import jax.numpy as jnp
from jax import lax
from jax.experimental import pallas as pl
from jax.experimental.pallas import tpu as pltpu
from jax.sharding import PartitionSpec as P

EPS = 1e-05
ROOT_HALF = 0.7071067811865476
INV_ROOT_TAU = 0.3989422804014327
LOG2E = 1.4426950408889634
MASKED = -1e30
BF = jnp.bfloat16
F32 = jnp.float32
TILE = 256
UNITS = 512
SLIM = 64
MESH = pl.DeviceIdType.MESH
VMEM_LIMIT = 62 * 1024 * 1024
ANY = pl.BlockSpec(memory_space=pl.ANY)


def dot_nn(left, right):
    return lax.dot_general(left, right, (((1,), (0,)), ((), ())), preferred_element_type=F32)


def dot_nt(left, right):
    return lax.dot_general(left, right, (((1,), (1,)), ((), ())), preferred_element_type=F32)


def dot_tn(left, right):
    return lax.dot_general(left, right, (((0,), (0,)), ((), ())), preferred_element_type=F32)


def params(**more):
    return pltpu.CompilerParams(
        dimension_semantics=("arbitrary",), vmem_limit_bytes=VMEM_LIMIT, **more
    )


def whole(shape):
    zeros = (0,) * len(shape)
    return pl.BlockSpec(shape, lambda *_: zeros, pipeline_mode=pl.Buffered(1))


def row_norm(values):
    center = values - jnp.mean(values, axis=-1, keepdims=True)
    inv = lax.rsqrt(jnp.mean(center * center, axis=-1, keepdims=True) + EPS)
    return center * inv, inv


def norm_back(grad, gain, normed, inv):
    scaled = grad * gain
    first = jnp.mean(scaled, axis=-1, keepdims=True)
    cross = jnp.mean(scaled * normed, axis=-1, keepdims=True)
    return inv * (scaled - first - normed * cross)


def column_sum(values):
    return jnp.sum(values, axis=0, keepdims=True)


def lane_fold(values):
    total = values[:, :128]
    for start in range(128, values.shape[1], 128):
        total = total + values[:, start : start + 128]
    return total


def cross_flag(lengths_ref, rows_ref):
    return jnp.where(lengths_ref[0, 0] == rows_ref.shape[0], 0.0, MASKED)


def attention_pair(cross, q_ref, k_ref, v_ref, scale, scaled_ref, out_ref, lse_ref, vext_ref):
    rows = q_ref.shape[0]
    half = rows // 2
    factor = LOG2E * 64 ** (-0.5)
    low_lanes = lax.broadcasted_iota(jnp.int32, (1, 128), 1) < 64
    below = lax.broadcasted_iota(jnp.int32, (TILE, TILE), 1) <= lax.broadcasted_iota(
        jnp.int32, (TILE, TILE), 0
    )
    vext_ref[:, :128] = v_ref[...]
    vext_ref[:, 128:] = jnp.ones((rows, 128), BF)
    for start in range(0, rows, TILE):
        stop = start + TILE
        query = q_ref[start:stop]
        results = []
        for head in range(2):
            mine = low_lanes if head == 0 else ~low_lanes
            raw = dot_nt(jnp.where(mine, query, jnp.zeros_like(query)), k_ref[:stop])
            parts = []
            if start >= half:
                parts.append((raw[:, :half], cross))
                if start > half:
                    parts.append((raw[:, half:start], None))
            elif start > 0:
                parts.append((raw[:, :start], None))
            parts.append((jnp.where(below, raw[:, start:stop], MASKED), None))
            peak = None
            for piece, shift in parts:
                top = jnp.max(piece, axis=-1, keepdims=True)
                if shift is not None:
                    top = top + shift
                peak = top if peak is None else jnp.maximum(peak, top)
            weights = []
            for piece, shift in parts:
                level = peak if shift is None else peak - shift
                weights.append(jnp.exp2((piece - level) * factor).astype(BF))
            weights = weights[0] if len(weights) == 1 else jnp.concatenate(weights, axis=1)
            both = dot_nn(weights, vext_ref[:stop])
            total = both[:, 128:]
            results.append((both[:, :128] / total, peak * factor + jnp.log2(total)))
        mixed = jnp.where(low_lanes, results[0][0], results[1][0])
        out_ref[start:stop] = mixed
        scaled_ref[start:stop] = (mixed * scale).astype(BF)
        lse = jnp.where(low_lanes, results[0][1], results[1][1]).T
        lse_ref[0, 0:1, start:stop] = lse[0:1]
        lse_ref[0, 1:2, start:stop] = lse[64:65]


def project_pair(first_ref, weights, bias, proj_ref):
    proj_ref[0] = (dot_nn(first_ref[...], weights) + bias).astype(BF)


def three(proj_ref):
    return [proj_ref.at[0, :, pl.ds(part * 128, 128)] for part in range(3)]


def plain_first_kernel(
    lengths_ref,
    tokens_ref,
    wq_ref,
    wk_ref,
    wv_ref,
    vectors_ref,
    bq_ref,
    bv_ref,
    hs_ref,
    first_ref,
    proj_ref,
    scaled_ref,
    attended_ref,
    lse_ref,
    vext_ref,
):
    @pl.when(pl.program_id(0) == 0)
    def _():
        for start in range(0, tokens_ref.shape[0], TILE):
            rows = pl.ds(start, TILE)
            normed, _ = row_norm(tokens_ref[rows].astype(F32))
            first_ref[rows] = (normed * vectors_ref[3:4] + vectors_ref[4:5]).astype(BF)

    weights = jnp.concatenate([wq_ref[...], wk_ref[...], wv_ref[...]], axis=1)
    bias = jnp.concatenate([bq_ref[0:1], jnp.zeros((1, 128), F32), bv_ref[1:2]], axis=1)
    project_pair(first_ref, weights, bias, proj_ref)
    attention_pair(
        cross_flag(lengths_ref, tokens_ref), *three(proj_ref), hs_ref[...], scaled_ref, attended_ref, lse_ref, vext_ref
    )


def plain_first(lengths, tokens, weights, vectors, head_lanes):
    rows, width = tokens.shape
    pairs = width // 128
    column = pl.BlockSpec((rows, 128), lambda p: (0, p))
    bias = pl.BlockSpec((16, 128), lambda p: (0, p))
    return pl.pallas_call(
        plain_first_kernel,
        grid=(pairs,),
        in_specs=[
            pl.BlockSpec(memory_space=pltpu.SMEM),
            whole((rows, width)),
            pl.BlockSpec((width, 128), lambda p: (0, p)),
            pl.BlockSpec((width, 128), lambda p: (0, pairs + p)),
            pl.BlockSpec((width, 128), lambda p: (0, 2 * pairs + p)),
            whole(vectors.shape),
            bias,
            bias,
            pl.BlockSpec((1, 128), lambda p: (0, p)),
        ],
        out_specs=[
            whole((rows, width)),
            pl.BlockSpec((1, rows, 384), lambda p: (p, 0, 0)),
            column,
            column,
            pl.BlockSpec((1, 8, rows), lambda p: (p, 0, 0)),
        ],
        out_shape=[
            jax.ShapeDtypeStruct((rows, width), BF),
            jax.ShapeDtypeStruct((pairs, rows, 384), BF),
            jax.ShapeDtypeStruct((rows, width), BF),
            jax.ShapeDtypeStruct((rows, width), F32),
            jax.ShapeDtypeStruct((pairs, 8, rows), F32),
        ],
        scratch_shapes=[pltpu.VMEM((rows, 256), BF)],
        compiler_params=params(),
        name="plain_first",
    )(lengths, tokens, weights, weights, weights, vectors, vectors, vectors, head_lanes)


def out_proj_rows(scaled_ref, weight_ref, vec_ref, tokens_ref, branch_ref, middle_ref):
    branch = dot_nn(scaled_ref[...], weight_ref[...]) + vec_ref[2:3]
    normed, _ = row_norm(branch)
    middle = tokens_ref[...].astype(F32) + (normed * vec_ref[5:6] + vec_ref[6:7])
    again, _ = row_norm(middle)
    branch_ref[...] = branch
    middle_ref[...] = middle
    return (again * vec_ref[7:8] + vec_ref[8:9]).astype(BF)


def out_proj_kernel(scaled_ref, weight_ref, vec_ref, tokens_ref, branch_ref, middle_ref, feed_ref):
    feed_ref[...] = out_proj_rows(
        scaled_ref, weight_ref, vec_ref, tokens_ref, branch_ref, middle_ref
    )


def out_proj(scaled, weights, vectors, tokens):
    rows, width = tokens.shape
    by_row = pl.BlockSpec((TILE, width), lambda i: (i, 0))
    return pl.pallas_call(
        out_proj_kernel,
        grid=(rows // TILE,),
        in_specs=[
            by_row,
            whole((width, width)),
            whole(vectors.shape),
            by_row,
        ],
        out_specs=[by_row, by_row, by_row],
        out_shape=[
            jax.ShapeDtypeStruct((rows, width), F32),
            jax.ShapeDtypeStruct((rows, width), F32),
            jax.ShapeDtypeStruct((rows, width), BF),
        ],
        compiler_params=params(),
        name="out_proj",
    )(scaled, weights, vectors, tokens)


def phi_and_slope(value):
    bell = jnp.exp2(value * value * (-0.5 * LOG2E))
    t = 1.0 / (1.0 + (0.3275911 * ROOT_HALF) * jnp.abs(value))
    series = t * (
        0.5 * 0.254829592
        + t
        * (
            0.5 * -0.284496736
            + t * (0.5 * 1.421413741 + t * (0.5 * -1.453152027 + t * (0.5 * 1.061405429)))
        )
    )
    tail = series * bell
    area = jnp.where(value < 0.0, tail, 1.0 - tail)
    return value * area, area + value * bell * INV_ROOT_TAU


def up_step(feed_ref, up, vec, act_ref, slope_ref, sums_ref):
    for left in range(0, UNITS, TILE):
        columns = slice(left, left + TILE)
        pre = dot_nn(feed_ref[...], up[:, columns])
        bias = vec[0:1, columns].astype(F32)
        for start in range(0, feed_ref.shape[0], SLIM):
            rows = slice(start, start + SLIM)
            act, slope = phi_and_slope(pre[rows] + bias)
            act_ref[0, rows, columns] = act.astype(BF)
            slope_ref[0, rows, columns] = slope.astype(BF)
            sums_ref[0, rows] += lane_fold(act)
            sums_ref[1, rows] += lane_fold(act * act)


def side_by_side(*columns):
    lane = lax.broadcasted_iota(jnp.int32, (1, 128), 1)
    result = jnp.broadcast_to(columns[-1], (columns[-1].shape[0], 128))
    for index in range(len(columns) - 2, -1, -1):
        result = jnp.where(lane == index, columns[index], result)
    return result


def up_stats(units, stats_ref, sums_ref):
    for start in range(0, stats_ref.shape[0], TILE):
        rows = pl.ds(start, TILE)
        mean = jnp.sum(sums_ref[0, rows], axis=1, keepdims=True) / units
        square = jnp.sum(sums_ref[1, rows], axis=1, keepdims=True) / units
        inv = lax.rsqrt(square - mean * mean + EPS)
        stats_ref[rows] = side_by_side(mean, inv)


def up_kernel(units, feed_ref, up_ref, vec_ref, act_ref, slope_ref, stats_ref, sums_ref):
    step = pl.program_id(0)

    @pl.when(step == 0)
    def _():
        sums_ref[...] = jnp.zeros_like(sums_ref)

    up_step(feed_ref, up_ref.at[0], vec_ref.at[0], act_ref, slope_ref, sums_ref)

    @pl.when(step == pl.num_programs(0) - 1)
    def _():
        up_stats(units, stats_ref, sums_ref)


def up_pass(feed, up, vec):
    rows, width = feed.shape
    steps = up.shape[0]
    block = pl.BlockSpec((1, rows, UNITS), lambda j: (j, 0, 0))
    return pl.pallas_call(
        functools.partial(up_kernel, steps * UNITS),
        grid=(steps,),
        in_specs=[
            whole((rows, width)),
            pl.BlockSpec((1, width, UNITS), lambda j: (j, 0, 0)),
            pl.BlockSpec((1, vec.shape[1], UNITS), lambda j: (j, 0, 0)),
        ],
        out_specs=[block, block, whole((rows, 128))],
        out_shape=[
            jax.ShapeDtypeStruct((steps, rows, UNITS), BF),
            jax.ShapeDtypeStruct((steps, rows, UNITS), BF),
            jax.ShapeDtypeStruct((rows, 128), F32),
        ],
        scratch_shapes=[pltpu.VMEM((2, rows, 128), F32)],
        compiler_params=params(),
        name="up_pass",
    )(feed, up, vec)


def down_step(
    act_ref, stats_ref, vec, down, cot_ref, down_grad_ref, e_ref, vec_grad_ref, total_ref, sums_ref,
    low_ref
):
    gain = vec[1:2].astype(F32)
    shift = vec[2:3].astype(F32)
    slims = [slice(start, start + SLIM) for start in range(0, cot_ref.shape[0], SLIM)]

    def normalized(rows, columns):
        value = act_ref[0, rows, columns].astype(F32)
        return (value - stats_ref[rows, 0:1]) * stats_ref[rows, 1:2]

    for rows in slims:
        low_ref[rows] = (normalized(rows, slice(0, UNITS)) * gain + shift).astype(BF)
    for left in range(0, UNITS, TILE):
        columns = slice(left, left + TILE)
        grads = dot_nt(cot_ref[...], down[columns])
        gain_grad = jnp.zeros((SLIM, TILE), F32)
        bias_grad = jnp.zeros((SLIM, TILE), F32)
        for rows in slims:
            normed = normalized(rows, columns)
            grad = grads[rows]
            gain_grad = gain_grad + grad * normed
            bias_grad = bias_grad + grad
            e = grad * gain[:, columns]
            e_ref[0, rows, columns] = e.astype(BF)
            sums_ref[0, rows] += lane_fold(e)
            sums_ref[1, rows] += lane_fold(e * normed)
        vec_grad_ref[0, 0:1, columns] = column_sum(gain_grad)
        vec_grad_ref[0, 1:2, columns] = column_sum(bias_grad)
    for left in range(0, total_ref.shape[1], TILE):
        columns = slice(left, left + TILE)
        total_ref[:, columns] += dot_nn(low_ref[...], down[:, columns])
    for left in range(0, UNITS, TILE):
        columns = slice(left, left + TILE)
        down_grad_ref[0, columns] = dot_tn(low_ref[:, columns], cot_ref[...]).astype(BF)


def down_end(
    units, stats_ref, middle_ref, shift_ref, mixed_ref, all_stats_ref, total_ref, sums_ref
):
    for start in range(0, total_ref.shape[0], TILE):
        rows = pl.ds(start, TILE)
        mixed_ref[rows] = (
            middle_ref[rows] + total_ref[rows] + shift_ref[...].astype(F32)
        ).astype(BF)
        first = jnp.sum(sums_ref[0, rows], axis=1, keepdims=True) / units
        cross = jnp.sum(sums_ref[1, rows], axis=1, keepdims=True) / units
        all_stats_ref[rows] = side_by_side(stats_ref[rows, 0:1], stats_ref[rows, 1:2], first, cross)


def down_kernel(
    units,
    act_ref,
    stats_ref,
    vec_ref,
    down_ref,
    cot_ref,
    middle_ref,
    shift_ref,
    mixed_ref,
    down_grad_ref,
    e_ref,
    all_stats_ref,
    vec_grad_ref,
    total_ref,
    sums_ref,
    low_ref,
):
    step = pl.program_id(0)

    @pl.when(step == 0)
    def _():
        total_ref[...] = jnp.zeros_like(total_ref)
        sums_ref[...] = jnp.zeros_like(sums_ref)

    down_step(
        act_ref, stats_ref, vec_ref.at[0], down_ref.at[0], cot_ref, down_grad_ref, e_ref, vec_grad_ref,
        total_ref, sums_ref, low_ref
    )

    @pl.when(step == pl.num_programs(0) - 1)
    def _():
        down_end(
            units, stats_ref, middle_ref, shift_ref, mixed_ref, all_stats_ref, total_ref, sums_ref
        )


def down_pass(act, stats, vec, down, cotangent, middle, shift):
    rows, width = cotangent.shape
    steps = act.shape[0]
    block = pl.BlockSpec((1, rows, UNITS), lambda j: (j, 0, 0))
    return pl.pallas_call(
        functools.partial(down_kernel, steps * UNITS),
        grid=(steps,),
        in_specs=[
            block,
            whole((rows, 128)),
            pl.BlockSpec((1, vec.shape[1], UNITS), lambda j: (j, 0, 0)),
            pl.BlockSpec((1, UNITS, width), lambda j: (j, 0, 0)),
            whole((rows, width)),
            whole((rows, width)),
            whole((1, width)),
        ],
        out_specs=[
            whole((rows, width)),
            pl.BlockSpec((1, UNITS, width), lambda j: (j, 0, 0)),
            block,
            whole((rows, 128)),
            pl.BlockSpec((1, 8, UNITS), lambda j: (j, 0, 0)),
        ],
        out_shape=[
            jax.ShapeDtypeStruct((rows, width), BF),
            jax.ShapeDtypeStruct((steps, UNITS, width), BF),
            jax.ShapeDtypeStruct((steps, rows, UNITS), BF),
            jax.ShapeDtypeStruct((rows, 128), F32),
            jax.ShapeDtypeStruct((steps, 8, UNITS), F32),
        ],
        scratch_shapes=[
            pltpu.VMEM((rows, width), F32),
            pltpu.VMEM((2, rows, 128), F32),
            pltpu.VMEM((rows, UNITS), BF),
        ],
        compiler_params=params(),
        name="down_pass",
    )(act, stats, vec, down, cotangent, middle, shift)


def up_back_step(act, slope, e, stats_ref, up, low_ref, total_ref):
    bias_grad = jnp.zeros((SLIM, UNITS), F32)
    for start in range(0, total_ref.shape[0], SLIM):
        rows = slice(start, start + SLIM)
        inv = stats_ref[rows, 1:2]
        normed = (act[rows].astype(F32) - stats_ref[rows, 0:1]) * inv
        grad_act = inv * (
            e[rows].astype(F32) - stats_ref[rows, 2:3] - normed * stats_ref[rows, 3:4]
        )
        low = (grad_act * slope[rows].astype(F32)).astype(BF)
        bias_grad = bias_grad + low.astype(F32)
        low_ref[rows, 0:UNITS] = low
    for left in range(0, total_ref.shape[1], TILE):
        columns = slice(left, left + TILE)
        total_ref[:, columns] += dot_nt(low_ref[:, 0:UNITS], up[columns])
    return column_sum(bias_grad)


def up_back_kernel(
    act_ref,
    slope_ref,
    e_ref,
    stats_ref,
    up_ref,
    feed_ref,
    up_grad_ref,
    bias_grad_ref,
    total_ref,
    turned_ref,
    low_ref,
):
    @pl.when(pl.program_id(0) == 0)
    def _():
        total_ref[...] = jnp.zeros_like(total_ref)
        turned_ref[...] = feed_ref[...].T

    bias_grad_ref[0, 0:1] = up_back_step(
        act_ref.at[0],
        slope_ref.at[0],
        e_ref.at[0],
        stats_ref,
        up_ref.at[0],
        low_ref,
        total_ref,
    )
    up_grad_ref[0] = dot_nn(turned_ref[...], low_ref[...]).astype(BF)


def up_back(act, slope, e, stats, up, feed):
    rows, width = feed.shape
    steps = act.shape[0]
    block = pl.BlockSpec((1, rows, UNITS), lambda j: (j, 0, 0))
    narrow = whole((rows, 128))
    return pl.pallas_call(
        up_back_kernel,
        grid=(steps,),
        in_specs=[
            block,
            block,
            block,
            narrow,
            pl.BlockSpec((1, width, UNITS), lambda j: (j, 0, 0)),
            whole((rows, width)),
        ],
        out_specs=[
            pl.BlockSpec((1, width, UNITS), lambda j: (j, 0, 0)),
            pl.BlockSpec((1, 8, UNITS), lambda j: (j, 0, 0)),
            whole((rows, width)),
        ],
        out_shape=[
            jax.ShapeDtypeStruct((steps, width, UNITS), BF),
            jax.ShapeDtypeStruct((steps, 8, UNITS), F32),
            jax.ShapeDtypeStruct((rows, width), F32),
        ],
        scratch_shapes=[pltpu.VMEM((width, rows), BF), pltpu.VMEM((rows, UNITS), BF)],
        compiler_params=params(),
        name="up_back",
    )(act, slope, e, stats, up, feed)


def norms_back(grad_feed, cot_ref, middle_ref, branch_ref, vec_ref, sums_ref):
    normed, inv = row_norm(middle_ref[...])
    cot = cot_ref[...].astype(F32)
    grad_middle = cot + norm_back(grad_feed, vec_ref[7:8], normed, inv)
    sums_ref[7:8] += column_sum(grad_feed * normed)
    sums_ref[8:9] += column_sum(grad_feed)
    sums_ref[9:10] += column_sum(cot)
    normed, inv = row_norm(branch_ref[...])
    low = norm_back(grad_middle, vec_ref[5:6], normed, inv).astype(BF)
    sums_ref[5:6] += column_sum(grad_middle * normed)
    sums_ref[6:7] += column_sum(grad_middle)
    sums_ref[2:3] += column_sum(low.astype(F32))
    return grad_middle, low


def heads_back(low, weights, scale, attended):
    grad_out = (dot_nt(low, weights) * scale).astype(BF)
    product = grad_out.astype(F32) * attended
    high = product.astype(BF)
    rest = (product - high.astype(F32)).astype(BF)
    heads = (
        lax.broadcasted_iota(jnp.int32, (product.shape[1], 128), 0) // 64
        == lax.broadcasted_iota(jnp.int32, (product.shape[1], 128), 1)
    ).astype(BF)
    return grad_out, dot_nn(high, heads) + dot_nn(rest, heads)


def out_back_kernel(
    grad_feed_ref,
    cot_ref,
    middle_ref,
    branch_ref,
    scaled_ref,
    attended_ref,
    weight_ref,
    vec_ref,
    hs_ref,
    grad_middle_ref,
    ga_ref,
    out_grad_ref,
    delta_ref,
    sums_ref,
    total_ref,
):
    step = pl.program_id(0)

    @pl.when(step == 0)
    def _():
        total_ref[...] = jnp.zeros_like(total_ref)
        sums_ref[...] = jnp.zeros_like(sums_ref)

    grad_middle, low = norms_back(
        grad_feed_ref[...], cot_ref, middle_ref, branch_ref, vec_ref, sums_ref
    )
    grad_middle_ref[...] = grad_middle
    ga_ref[...], delta = heads_back(low, weight_ref[...], hs_ref[...], attended_ref[...])
    total_ref[...] += dot_tn(scaled_ref[...], low)
    delta_ref[...] = delta.T[: delta_ref.shape[0]]

    @pl.when(step == pl.num_programs(0) - 1)
    def _():
        out_grad_ref[...] = total_ref[...].astype(BF)


def out_back(
    grad_feed, cotangent, middle, branch, scaled, attended, weights, vectors, head_lanes
):
    rows, width = cotangent.shape
    heads = 2 * width // 128
    by_row = pl.BlockSpec((TILE, width), lambda i: (i, 0))
    return pl.pallas_call(
        out_back_kernel,
        grid=(rows // TILE,),
        in_specs=[
            by_row,
            by_row,
            by_row,
            by_row,
            by_row,
            by_row,
            whole((width, width)),
            whole(vectors.shape),
            whole((1, width)),
        ],
        out_specs=[
            by_row,
            by_row,
            whole((width, width)),
            pl.BlockSpec((heads, TILE), lambda i: (0, i)),
            whole((16, width)),
        ],
        out_shape=[
            jax.ShapeDtypeStruct((rows, width), F32),
            jax.ShapeDtypeStruct((rows, width), BF),
            jax.ShapeDtypeStruct((width, width), BF),
            jax.ShapeDtypeStruct((heads, rows), F32),
            jax.ShapeDtypeStruct((16, width), F32),
        ],
        scratch_shapes=[pltpu.VMEM((width, width), F32)],
        compiler_params=params(),
        name="out_back",
    )(
        grad_feed,
        cotangent,
        middle,
        branch,
        scaled,
        attended,
        weights,
        vectors,
        head_lanes,
    )


def attention_back_head(
    head, cross, q_ref, k_ref, v_ref, ga_ref, lse_ref, delta, dq_ref, dk_ref, dv_ref
):
    rows = q_ref.shape[0]
    half = rows // 2
    factor = LOG2E * 64 ** (-0.5)
    low_lanes = lax.broadcasted_iota(jnp.int32, (1, 128), 1) < 64
    mine = low_lanes if head == 0 else ~low_lanes
    above = lax.broadcasted_iota(jnp.int32, (TILE, TILE), 0) <= lax.broadcasted_iota(
        jnp.int32, (TILE, TILE), 1
    )
    zero = jnp.zeros((rows, 128), BF)
    query = jnp.where(mine, q_ref[...], zero)
    grad = jnp.where(mine, ga_ref[...], zero)
    key_own = jnp.where(mine, k_ref[...], zero)
    for start in range(0, rows, TILE):
        stop = start + TILE
        raw = dot_nt(k_ref[start:stop], query[start:])
        level = lse_ref[head : head + 1, start:]
        parts = [jnp.where(above, raw[:, :TILE] * factor - level[:, :TILE], MASKED)]
        if start < half:
            if stop < half:
                parts.append(raw[:, TILE : half - start] * factor - level[:, TILE : half - start])
            parts.append(raw[:, half - start :] * factor - (level[:, half - start :] - cross))
        elif stop < rows:
            parts.append(raw[:, TILE:] * factor - level[:, TILE:])
        exponent = parts[0] if len(parts) == 1 else jnp.concatenate(parts, axis=1)
        weights = jnp.exp2(exponent)
        grad_weights = dot_nt(v_ref[start:stop], grad[start:])
        grad_scores = (weights * (grad_weights - delta[:, start:])).astype(BF)
        dv = dot_nn(weights.astype(BF), grad[start:])
        dk = dot_nn(grad_scores, query[start:])
        dq = dot_tn(grad_scores, key_own[start:stop])
        if head == 0:
            dv_ref[start:stop] = dv
            dk_ref[start:stop] = dk
        else:
            dv_ref[start:stop] += dv
            dk_ref[start:stop] += dk
        if head == 0 and start == 0:
            dq_ref[...] = dq
        else:
            dq_ref[start:] += dq


def in_back_pair(dq_ref, dk_ref, dv_ref, weights, turned_ref, out_grad_ref, chunk_ref, total_ref):
    factor = 64 ** (-0.5)
    dq = (dq_ref[...] * factor).astype(BF)
    dk = (dk_ref[...] * factor).astype(BF)
    dv = dv_ref[...].astype(BF)
    grads = jnp.concatenate([dq, dk, dv], axis=1)
    shares = dot_nn(turned_ref[...], grads).astype(BF)
    for start in range(0, total_ref.shape[0], TILE):
        part = jnp.concatenate(
            [shares[start : start + TILE], out_grad_ref[start : start + TILE]], axis=1
        )
        chunk_ref[:, start // TILE] = part.reshape(8, 32, 512)
        columns = slice(start, start + TILE)
        total_ref[:, columns] += dot_nt(grads, weights[columns])
    return column_sum(dq.astype(F32)), column_sum(dv.astype(F32))


def tokens_back(tokens, grad, grad_middle, gain):
    normed, inv = row_norm(tokens.astype(F32))
    back = norm_back(grad, gain, normed, inv)
    return (grad_middle + back).astype(BF), column_sum(grad * normed), column_sum(grad)


def in_back_kernel(
    lengths_ref,
    proj_ref,
    ga_ref,
    lse_ref,
    delta_ref,
    wq_ref,
    wk_ref,
    wv_ref,
    first_ref,
    out_grad_ref,
    tokens_ref,
    gain_ref,
    grad_middle_ref,
    chunk_ref,
    bias_ref,
    tokens_grad_ref,
    sums_ref,
    dq_ref,
    dk_ref,
    dv_ref,
    turned_ref,
    total_ref,
):
    step = pl.program_id(0)
    q_ref, k_ref, v_ref = three(proj_ref)
    rows_all = tokens_ref.shape[0]

    @pl.when(step == 0)
    def _():
        turned_ref[...] = first_ref[...].T
        total_ref[...] = jnp.zeros_like(total_ref)

    for head in range(2):
        attention_back_head(
            head,
            cross_flag(lengths_ref, tokens_ref),
            q_ref,
            k_ref,
            v_ref,
            ga_ref,
            lse_ref.at[0],
            delta_ref[0, head : head + 1],
            dq_ref,
            dk_ref,
            dv_ref,
        )
    weights = jnp.concatenate([wq_ref[...], wk_ref[...], wv_ref[...]], axis=1)
    query_sum, value_sum = in_back_pair(
        dq_ref, dk_ref, dv_ref, weights, turned_ref, out_grad_ref, chunk_ref.at[0], total_ref
    )
    bias_ref[0, 0:1] = query_sum
    bias_ref[0, 1:2] = value_sum

    @pl.when(step == pl.num_programs(0) - 1)
    def _():
        gain_grad = jnp.zeros((1, total_ref.shape[1]), F32)
        shift_grad = jnp.zeros((1, total_ref.shape[1]), F32)
        for start in range(0, rows_all, TILE):
            rows = pl.ds(start, TILE)
            tokens_grad_ref[rows], gain_part, shift_part = tokens_back(
                tokens_ref[rows], total_ref[rows], grad_middle_ref[rows], gain_ref[...]
            )
            gain_grad = gain_grad + gain_part
            shift_grad = shift_grad + shift_part
        sums_ref[0:1] = gain_grad
        sums_ref[1:2] = shift_grad


def in_back(lengths, projected, ga, lse, delta, weights, first, out_grad, tokens, gain, grad_middle):
    rows, width = tokens.shape
    pairs = width // 128
    column = pl.BlockSpec((rows, 128), lambda p: (0, p))
    square = whole((rows, width))
    return pl.pallas_call(
        in_back_kernel,
        grid=(pairs,),
        in_specs=[
            pl.BlockSpec(memory_space=pltpu.SMEM),
            pl.BlockSpec((1, rows, 384), lambda p: (p, 0, 0)),
            column,
            pl.BlockSpec((1, 8, rows), lambda p: (p, 0, 0)),
            pl.BlockSpec((1, 2, rows), lambda p: (p, 0, 0)),
            pl.BlockSpec((width, 128), lambda p: (0, p)),
            pl.BlockSpec((width, 128), lambda p: (0, pairs + p)),
            pl.BlockSpec((width, 128), lambda p: (0, 2 * pairs + p)),
            square,
            column,
            square,
            whole((1, width)),
            square,
        ],
        out_specs=[
            pl.BlockSpec((1, 8, width // TILE, 32, 512), lambda p: (p, 0, 0, 0, 0)),
            pl.BlockSpec((1, 8, 128), lambda p: (p, 0, 0)),
            square,
            whole((8, width)),
        ],
        out_shape=[
            jax.ShapeDtypeStruct((pairs, 8, width // TILE, 32, 512), BF),
            jax.ShapeDtypeStruct((pairs, 8, 128), F32),
            jax.ShapeDtypeStruct((rows, width), BF),
            jax.ShapeDtypeStruct((8, width), F32),
        ],
        scratch_shapes=[
            pltpu.VMEM((rows, 128), F32),
            pltpu.VMEM((rows, 128), F32),
            pltpu.VMEM((rows, 128), F32),
            pltpu.VMEM((width, rows), BF),
            pltpu.VMEM((rows, width), F32),
        ],
        compiler_params=params(),
        name="in_back",
    )(
        lengths,
        projected,
        ga,
        lse,
        delta,
        weights,
        weights,
        weights,
        first,
        out_grad,
        tokens,
        gain,
        grad_middle,
    )


class Place:
    def __init__(self):
        self.z = lax.axis_index("dp")
        wide = lax.axis_index("wide")
        self.y = wide // 4
        self.x = (wide // 2) % 2
        self.c = wide % 2
        self.core = (self.z, wide + 1 - 2 * self.c)
        self.side = (self.z, wide + 2 - 4 * self.x)
        self.over = (self.z, wide + 4 - 8 * self.y)
        self.ranks = (self.z + 1 - 2 * (self.z % 2), (self.z + 2) % 4, 3 - self.z)
        self.planes = tuple((rank, wide) for rank in self.ranks)

    def greet(self, planes=True):
        barrier = pltpu.get_barrier_semaphore()
        peers = (self.core, self.side, self.over) + (self.planes if planes else ())
        for peer in peers:
            pl.semaphore_signal(barrier, inc=1, device_id=peer, device_id_type=MESH)
        pl.semaphore_wait(barrier, len(peers))


class WideGather:
    copies = 10

    def __init__(
        self, place, view, count, send, recv, first, source=None, last=None, offset=0, total=None
    ):
        y, x, c = place.y, place.x, place.c
        here, side, over, far = (y, x, c), (y, 1 - x, c), (1 - y, x, c), (1 - y, 1 - x, c)
        upper, lower = pl.ds(offset, count // 2), pl.ds(offset + count // 2, count // 2)
        both = pl.ds(offset, count)
        everything = both if total is None else pl.ds(0, total)

        def copy(index, slot, part, peer):
            destination = view(*slot, part)
            return pltpu.make_async_remote_copy(
                src_ref=source.at[part] if source is not None and slot is here else destination,
                dst_ref=destination,
                send_sem=send.at[first + index],
                recv_sem=recv.at[first + index],
                device_id=peer,
                device_id_type=MESH,
            )

        self.all = (
            copy(0, here, upper, place.side),
            copy(1, here, lower, place.over),
            copy(2, here, upper, place.over),
            copy(3, here, lower, place.side),
            None if total == 0 else copy(4, here, everything, place.core),
            copy(5, side, upper, place.over),
            copy(6, over, lower, place.side),
            copy(7, side, both, place.core),
            copy(8, over, both, place.core),
            copy(9, far, both, place.core),
        )
        self.own = None
        if source is not None and last is not None:
            self.own = pltpu.make_async_copy(source, view(*here, everything), last)

    def start(self):
        if self.own is not None:
            self.own.start()
        for copy in self.all[:5]:
            if copy is not None:
                copy.start()

    def relay(self, stage):
        waits, starts = (((0, 1), (5, 6)), ((2, 3), (7, 8)), ((5, 6), (9,)))[stage]
        for index in waits:
            self.all[index].wait_recv()
        for index in starts:
            self.all[index].start()

    def finish(self):
        for index in (4, 7, 8, 9):
            if self.all[index] is not None:
                self.all[index].wait_recv()
        for copy in self.all:
            if copy is not None:
                copy.wait_send()
        if self.own is not None:
            self.own.wait()


def blocks_of(target):
    return lambda y, x, c, rows: target.at[y, x, c, rows]


LAG = 2


class Reduction:
    slots = 2 * LAG
    deep = 3 * LAG
    keep = 3 * LAG + 2

    @classmethod
    def scratch(cls):
        n, k = cls.slots, cls.keep
        return [
            pltpu.VMEM((cls.deep, 2, 2, 4, 32, 512), BF),
            pltpu.VMEM((n, 2, 2, 4, 32, 512), BF),
            pltpu.VMEM((n, 2, 2, 4, 16, 512), BF),
            pltpu.VMEM((n, 2, 4, 16, 512), BF),
            pltpu.VMEM((n, 4, 32, 512), BF),
            pltpu.VMEM((n, 3, 32, 512), BF),
            pltpu.VMEM((n, 32, 512), BF),
            pltpu.VMEM((k, 3, 32, 512), BF),
            pltpu.SemaphoreType.DMA((6, k)),
            pltpu.SemaphoreType.DMA((6, k)),
            pltpu.SemaphoreType.DMA((cls.deep,)),
        ]

    def __init__(self, place, refs):
        self.place = place
        (
            self.chip,
            self.partner,
            self.first,
            self.second,
            self.plane,
            self.from_z,
            self.sums,
            self.shared,
            self.send,
            self.recv,
            self.local,
        ) = refs

    def copy(self, index, slot, source, target, peer):
        return pltpu.make_async_remote_copy(
            src_ref=source,
            dst_ref=target,
            send_sem=self.send.at[index, slot],
            recv_sem=self.recv.at[index, slot],
            device_id=peer,
            device_id_type=MESH,
        )

    def wait(self, index, slot, arrived):
        self.copy(index, slot, arrived, arrived, self.place.core).wait()

    def load(self, chunk, source):
        slot = chunk % self.deep
        return pltpu.make_async_copy(source, self.chip.at[slot], self.local.at[slot])

    def stage0(self, chunk, view):
        slot, c = chunk % self.slots, self.place.c
        self.copy(
            0, slot, view.at[:, :, 1 - c], self.partner.at[slot], self.place.core
        ).start()
        self.load(chunk, view.at[:, :, c]).start()

    def stage1(self, chunk):
        p, slot, index = self.place, chunk % self.slots, chunk % self.deep
        partner, chip, target = self.partner.at[slot], self.chip.at[index], self.first.at[slot]
        self.load(chunk, partner).wait()
        self.wait(0, slot, partner)
        chip[...] += partner[...]
        self.copy(1, slot, chip.at[:, 1 - p.x, :, pl.ds(0, 16)], target.at[0], p.side).start()
        self.copy(1, slot, chip.at[1 - p.y, :, :, pl.ds(16, 16)], target.at[1], p.over).start()

    def stage2(self, chunk):
        p, slot, index = self.place, chunk % self.slots, chunk % self.deep
        chip, arrived, target = self.chip.at[index], self.first.at[slot], self.second.at[slot]
        self.wait(1, slot, arrived)
        for k in range(2):
            chip[k, p.x, :, 0:16] += arrived[0, k]
            chip[p.y, k, :, 16:32] += arrived[1, k]
        self.copy(2, slot, chip.at[1 - p.y, p.x, :, pl.ds(0, 16)], target.at[0], p.over).start()
        self.copy(2, slot, chip.at[p.y, 1 - p.x, :, pl.ds(16, 16)], target.at[1], p.side).start()

    def stage3(self, chunk):
        p, slot, index = self.place, chunk % self.slots, chunk % self.deep
        arrived, mine, plane = self.second.at[slot], self.chip.at[index, p.y, p.x], self.plane
        self.wait(2, slot, arrived)
        plane[slot, :, 0:16] = mine[:, 0:16] + arrived[0]
        plane[slot, :, 16:32] = mine[:, 16:32] + arrived[1]
        for k in range(3):
            target = self.from_z.at[slot, k]
            self.copy(3, slot, plane.at[slot, p.ranks[k]], target, p.planes[k]).start()

    def stage4(self, chunk):
        slot = chunk % self.slots
        self.wait(3, slot, self.from_z.at[slot])
        total = self.plane[slot, self.place.z].astype(F32)
        for k in range(3):
            total = total + self.from_z[slot, k].astype(F32)
        return total

    def spread(self, chunk, total):
        slot, place = chunk % self.slots, chunk % self.keep
        self.sums[slot] = total.astype(BF)
        peer = self.place.planes[1]
        self.copy(4, place, self.sums.at[slot], self.shared.at[place, 0], peer).start()

    def stage5(self, chunk):
        slot, place, peer = chunk % self.slots, chunk % self.keep, self.place.planes[0]
        shared = self.shared.at[place]
        self.wait(4, place, shared.at[0])
        self.copy(5, place, self.sums.at[slot], shared.at[1], peer).start()
        self.copy(5, place, shared.at[0], shared.at[2], peer).start()

    def stage6(self, chunk):
        slot, place, ranks = chunk % self.slots, chunk % self.keep, self.place.ranks
        self.wait(5, place, self.shared.at[place, pl.ds(1, 2)])
        return [
            (self.place.z, self.sums[slot]),
            (ranks[1], self.shared[place, 0]),
            (ranks[0], self.shared[place, 1]),
            (ranks[2], self.shared[place, 2]),
        ]


class SmallReduction:
    @staticmethod
    def scratch():
        return [
            pltpu.VMEM((2, 2, 2, 4, 16, 512), BF),
            pltpu.VMEM((2, 2, 4, 16, 512), BF),
            pltpu.VMEM((2, 2, 4, 16, 512), BF),
            pltpu.VMEM((2, 4, 16, 512), BF),
            pltpu.VMEM((4, 16, 512), BF),
            pltpu.VMEM((3, 16, 512), BF),
            pltpu.SemaphoreType.DMA((4,)),
            pltpu.SemaphoreType.DMA((4,)),
        ]

    def __init__(self, place, refs):
        self.place = place
        self.source, self.chip, self.partner, self.first, self.second, self.from_z = refs[:6]
        self.send, self.recv = refs[6:]

    def copy(self, index, source, target, peer):
        return pltpu.make_async_remote_copy(
            src_ref=source,
            dst_ref=target,
            send_sem=self.send.at[index],
            recv_sem=self.recv.at[index],
            device_id=peer,
            device_id_type=MESH,
        )

    def wait(self, index, arrived):
        self.copy(index, arrived, arrived, self.place.core).wait()

    def stage0(self):
        p = self.place
        self.copy(0, self.source.at[:, :, 1 - p.c], self.partner, p.core).start()

    def stage1(self):
        p = self.place
        self.wait(0, self.partner)
        self.chip[...] = self.source[:, :, p.c] + self.partner[...]
        self.copy(1, self.chip.at[:, 1 - p.x], self.first, p.side).start()

    def stage2(self):
        p = self.place
        self.wait(1, self.first)
        for k in range(2):
            self.chip[k, p.x] += self.first[k]
        self.copy(2, self.chip.at[1 - p.y, p.x], self.second, p.over).start()

    def stage3(self):
        p = self.place
        self.wait(2, self.second)
        self.chip[p.y, p.x] += self.second[...]
        for k in range(3):
            block = self.chip.at[p.y, p.x, p.ranks[k]]
            self.copy(3, block, self.from_z.at[k], p.planes[k]).start()

    def stage4(self):
        p = self.place
        self.wait(3, self.from_z)
        total = self.chip[p.y, p.x, p.z].astype(F32)
        for k in range(3):
            total = total + self.from_z[k].astype(F32)
        return total


class Stream:
    def __init__(self, view, buffers, sems):
        self.view, self.buffers, self.sems = view, buffers, sems

    def copy(self, index):
        slot = index % 2
        return pltpu.make_async_copy(self.view(index), self.buffers.at[slot], self.sems.at[slot])

    def start(self, index):
        self.copy(index).start()

    def block(self, index):
        return self.buffers.at[index % 2]


def advance(streams, index, count):
    @pl.when(index + 1 < count)
    def _():
        for stream in streams:
            stream.start(index + 1)

    for stream in streams:
        stream.copy(index).wait()


def nearness(i):
    over = (i == 3) | (i >= 5)
    side = (i == 2) | (i == 4) | (i >= 6)
    other = (i == 1) | (i == 4) | (i == 5) | (i == 7)
    return over, side, other


def unit_index(i):
    wide = lax.axis_index("wide")
    y, x, c = wide // 4, wide // 2 % 2, wide % 2
    over, side, other = nearness(i)
    y, x, c = (jnp.where(flip, 1 - k, k) for flip, k in zip((over, side, other), (y, x, c)))
    return 4 * y + 2 * x + c


class NearGather:
    copies = 3

    def __init__(self, place, source, target, send, recv, first, last):
        slot = target.at[place.y, place.x, place.c]
        self.all = [
            pltpu.make_async_remote_copy(
                src_ref=source,
                dst_ref=slot,
                send_sem=send.at[first + index],
                recv_sem=recv.at[first + index],
                device_id=peer,
                device_id_type=MESH,
            )
            for index, peer in enumerate((place.side, place.over, place.core))
        ]
        self.own = pltpu.make_async_copy(source, slot, last)

    def start(self):
        self.own.start()
        for copy in self.all:
            copy.start()

    def finish(self):
        self.own.wait()
        for copy in self.all:
            copy.wait()


class LateGather:
    copies = 5

    def __init__(self, place, near, late, send, recv, first):
        rows = near.shape[-2]
        upper, lower = pl.ds(0, rows // 2), pl.ds(rows // 2, rows // 2)
        side, over = near.at[place.y, 1 - place.x, place.c], near.at[1 - place.y, place.x, place.c]

        def copy(index, source, target, peer):
            return pltpu.make_async_remote_copy(
                src_ref=source,
                dst_ref=target,
                send_sem=send.at[first + index],
                recv_sem=recv.at[first + index],
                device_id=peer,
                device_id_type=MESH,
            )

        self.all = (
            copy(0, side.at[upper], late.at[2, upper], place.over),
            copy(1, over.at[lower], late.at[2, lower], place.side),
            copy(2, side, late.at[0], place.core),
            copy(3, over, late.at[1], place.core),
            copy(4, late.at[2], late.at[3], place.core),
        )

    def start(self):
        for copy in self.all[:4]:
            copy.start()

    def relay(self):
        for copy in self.all[:2]:
            copy.wait_recv()
        self.all[4].start()

    def arrived(self, *indices):
        for index in indices:
            self.all[index].wait_recv()

    def finish(self):
        for copy in self.all:
            copy.wait_send()


class WeightStream(Stream):
    def __init__(self, near, late, buffers, sems):
        super().__init__(lambda i: late.at[0], buffers, sems)
        self.near, self.late = near, late

    def start(self, index):
        slot = index % 2
        target, sem = self.buffers.at[slot], self.sems.at[slot]

        @pl.when(index < 4)
        def _():
            block = unit_index(index)
            view = self.near.at[block // 4, block // 2 % 2, block % 2]
            pltpu.make_async_copy(view, target, sem).start()

        @pl.when(index >= 4)
        def _():
            pltpu.make_async_copy(self.late.at[index - 4], target, sem).start()


def dma_sems(count):
    return [pltpu.SemaphoreType.DMA((count,)), pltpu.SemaphoreType.DMA((count,))]


def to_planes(place, mine, landing, send, recv, first):
    return [
        pltpu.make_async_remote_copy(
            src_ref=mine,
            dst_ref=landing(k),
            send_sem=send.at[first + k],
            recv_sem=recv.at[first + k],
            device_id=place.planes[k],
            device_id_type=MESH,
        )
        for k in range(3)
    ]


class PlanesLast:
    copies = WideGather.copies + 6

    def __init__(self, place, source, target, send, recv, last):
        view = blocks_of(target.at[place.z])
        self.wide = WideGather(place, view, source.shape[0], send, recv, 0, source, last)

        def copy(index, rank, peer):
            blocks = target.at[rank, :, :, place.c]
            return pltpu.make_async_remote_copy(
                src_ref=blocks,
                dst_ref=blocks,
                send_sem=send.at[WideGather.copies + index],
                recv_sem=recv.at[WideGather.copies + index],
                device_id=peer,
                device_id_type=MESH,
            )

        self.across = [copy(k, place.z, place.planes[k]) for k in range(3)]
        self.over = [copy(3 + k, place.ranks[k], place.core) for k in range(3)]

    def start_across(self):
        self.wide.own.wait()
        for copy in self.across:
            copy.start()

    def start_over(self):
        for arrived, copy in zip(self.across, self.over):
            arrived.wait_recv()
            copy.start()

    def finish(self):
        self.wide.own = None
        self.wide.finish()
        for copy in self.across:
            copy.wait_send()
        for copy in self.over:
            copy.wait()


def first_kernel(
    lengths_ref,
    tokens_ref,
    in_ref,
    vec_ref,
    out_ref,
    up_ref,
    unit_ref,
    hs_ref,
    turned_ref,
    proj_ref,
    scaled_ref,
    scaled_turned_ref,
    attended_ref,
    lse_ref,
    vectors_ref,
    scale_ref,
    in_all,
    out_all,
    up_all,
    unit_all,
    held_ref,
    normed_ref,
    first_ref,
    vext_ref,
    send_in,
    recv_in,
    send_out,
    recv_out,
    send_ff,
    recv_ff,
    local,
):
    step = pl.program_id(0)
    place = Place()
    width = tokens_ref.shape[1]
    count = WideGather.copies
    lanes = (3 * width // 2 + 128, 3 * width // 2)
    across, early, late = [], [], None
    for group in range(2):
        held = held_ref.at[group, :, :, :, :, :, pl.ds(0, lanes[group])]
        first = group * (3 + 2 * count)

        def blocks(planes, held=held):
            return lambda y, x, c, rows: held.at[planes, y, x, c, rows]

        mine = held.at[0, place.y, place.x, place.c]
        across.append(
            to_planes(
                place,
                mine,
                lambda k, held=held: held.at[k + 1, place.y, place.x, place.c],
                send_in,
                recv_in,
                first,
            )
        )
        if group == 0:
            for part, planes in enumerate((pl.ds(0, 1), pl.ds(1, 3))):
                start = first + 3 + part * count
                early.append(WideGather(place, blocks(planes), 32, send_in, recv_in, start))
        else:
            late = WideGather(place, blocks(pl.ds(0, 4)), 32, send_in, recv_in, first + 3)
    orders = (place.z, *place.ranks)
    out = PlanesLast(place, out_ref, out_all, send_out, recv_out, local.at[2])
    up = NearGather(place, up_ref, up_all, send_ff, recv_ff, count, local.at[3])
    unit = WideGather(
        place, blocks_of(unit_all), 32, send_ff, recv_ff, 0, unit_ref, local.at[4]
    )
    keep = [
        pltpu.make_async_copy(
            held_ref.at[group, index, :, :, :, :, pl.ds(0, lanes[1])],
            in_all.at[rank, :, :, :, :, pl.ds(group * lanes[1], lanes[1])],
            local.at[12 + 4 * group + index],
        )
        for group in range(2)
        for index, rank in enumerate(orders)
    ]

    @pl.when(step == 0)
    def _():
        place.greet()
        half = width // 2
        for group in range(2):
            mine = held_ref.at[group, 0, place.y, place.x, place.c]
            fills = []
            for pair in range(4):
                for part in range(3):
                    column = part * width + (4 * group + pair) * 128
                    fills.append(
                        pltpu.make_async_copy(
                            in_ref.at[:, pl.ds(column, 128)],
                            mine.at[:, pl.ds(pair * 384 + part * 128, 128)],
                            local.at[20 + group * 12 + pair * 3 + part],
                        )
                    )
            for copy in fills:
                copy.start()
            if group == 0:
                mine[:, 3 * half : 3 * half + 128] = jnp.zeros((32, 128), BF)
                mine[:, 3 * half : 3 * half + 32] = vec_ref[...]
            for copy in fills:
                copy.wait()
            for copy in across[group]:
                copy.start()
            if group == 0:
                early[0].start()
        scale = hs_ref[...].astype(F32)
        for pair in range(width // 128):
            own = slice(pair * 128, (pair + 1) * 128)
            low_lanes = lax.broadcasted_iota(jnp.int32, (1, 128), 1) < 64
            scale_ref[0:1, own] = jnp.where(
                low_lanes, scale[:, 2 * pair : 2 * pair + 1], scale[:, 2 * pair + 1 : 2 * pair + 2]
            )
        for start in range(0, tokens_ref.shape[0], TILE):
            rows = pl.ds(start, TILE)
            normed, _ = row_norm(tokens_ref[rows].astype(F32))
            normed_ref[rows] = normed
        early[0].relay(0)
        for copy in across[0]:
            copy.wait_recv()
        early[1].start()
        early[0].relay(1)
        early[0].relay(2)
        early[1].relay(0)
        early[1].relay(1)
        for copy in across[1]:
            copy.wait_recv()
        late.start()
        early[1].relay(2)
        out.wide.start()
        unit.start()
        for part in early:
            part.finish()
        for z in range(4):
            for y in range(2):
                tile = jnp.zeros((16, 128), F32)
                for x in range(2):
                    for c in range(2):
                        piece = held_ref[
                            0, orders[z], y, x, c, 0:16, 3 * half : 3 * half + 128
                        ].astype(F32)
                        spot = 32 * (2 * x + c)
                        tile = tile + (piece if spot == 0 else pltpu.roll(piece, spot, 1))
                vectors_ref[:, (2 * z + y) * 128 : (2 * z + y + 1) * 128] = tile
        for start in range(0, tokens_ref.shape[0], TILE):
            rows = pl.ds(start, TILE)
            first_ref[rows] = (normed_ref[rows] * vectors_ref[3:4] + vectors_ref[4:5]).astype(BF)

    @pl.when((step >= 2) & (step <= 4))
    def _():
        for stage in range(3):

            @pl.when(step == 2 + stage)
            def _():
                late.relay(stage)
                out.wide.relay(stage)
                unit.relay(stage)

    @pl.when(step == 2)
    def _():
        up.start()

    @pl.when(step == 4)
    def _():
        out.start_across()

    @pl.when(step == 5)
    def _():
        late.finish()
        for copy in keep:
            copy.start()

    @pl.when(step == 7)
    def _():
        out.start_over()

    @pl.when(step > 0)
    def _():
        pair = step - 1
        columns = pl.ds(pl.multiple_of(pair % 4 * 384, 128), 384)
        weights = jnp.concatenate(
            [held_ref[pair // 4, order, :, :, :, :, columns].reshape(TILE, 384) for order in orders]
        )
        own = pl.ds(pl.multiple_of(pair * 128, 128), 128)
        bias = jnp.concatenate(
            [vectors_ref[0:1, own], jnp.zeros((1, 128), F32), vectors_ref[1:2, own]], axis=1
        )
        project_pair(first_ref, weights, bias, proj_ref)
        attention_pair(
            cross_flag(lengths_ref, tokens_ref),
            *three(proj_ref),
            scale_ref[0:1, own],
            scaled_ref,
            attended_ref,
            lse_ref,
            vext_ref,
        )
        scaled_turned_ref[...] = scaled_ref[...].T

    @pl.when(step == pl.num_programs(0) - 1)
    def _():
        turned_ref[...] = first_ref[...].T
        for copy in (*across[0], *across[1]):
            copy.wait_send()
        for copy in keep:
            copy.wait()
        out.finish()
        unit.finish()
        up.finish()


def first_part(lengths, tokens, in_weight, vec, out_weight, up_weight, unit_rows, head_scale):
    rows, width = tokens.shape
    pairs = width // 128

    def at(step):
        return jnp.maximum(step - 1, 0)

    column = pl.BlockSpec((rows, 128), lambda s: (0, at(s)))
    held = (2, 4, 2, 2, 2, 32, 3 * width // 2 + 128)
    return pl.pallas_call(
        first_kernel,
        grid=(pairs + 1,),
        in_specs=[
            pl.BlockSpec(memory_space=pltpu.SMEM),
            whole((rows, width)),
            ANY,
            whole(vec.shape),
            ANY,
            ANY,
            ANY,
            whole(head_scale.shape),
        ],
        out_specs=[
            whole((width, rows)),
            pl.BlockSpec((1, rows, 384), lambda s: (at(s), 0, 0)),
            column,
            pl.BlockSpec((128, rows), lambda s: (at(s), 0)),
            column,
            pl.BlockSpec((1, 8, rows), lambda s: (at(s), 0, 0)),
            whole((16, width)),
            whole((8, width)),
            ANY,
            ANY,
            ANY,
            ANY,
        ],
        out_shape=[
            jax.ShapeDtypeStruct((width, rows), BF),
            jax.ShapeDtypeStruct((pairs, rows, 384), BF),
            jax.ShapeDtypeStruct((rows, width), BF),
            jax.ShapeDtypeStruct((width, rows), BF),
            jax.ShapeDtypeStruct((rows, width), F32),
            jax.ShapeDtypeStruct((pairs, 8, rows), F32),
            jax.ShapeDtypeStruct((16, width), F32),
            jax.ShapeDtypeStruct((8, width), F32),
            jax.ShapeDtypeStruct((4, 2, 2, 2, 32, 3 * width), BF),
            jax.ShapeDtypeStruct((4, 2, 2, 2, *out_weight.shape), BF),
            jax.ShapeDtypeStruct((2, 2, 2, *up_weight.shape), BF),
            jax.ShapeDtypeStruct((2, 2, 2, *unit_rows.shape), BF),
        ],
        scratch_shapes=[
            pltpu.VMEM(held, BF),
            pltpu.VMEM((rows, width), F32),
            pltpu.VMEM((rows, width), BF),
            pltpu.VMEM((rows, 256), BF),
            *dma_sems(6 + 3 * WideGather.copies),
            *dma_sems(PlanesLast.copies),
            *dma_sems(WideGather.copies + NearGather.copies),
            pltpu.SemaphoreType.DMA((44,)),
        ],
        compiler_params=params(collective_id=0, has_side_effects=True),
        name="first_part",
    )(lengths, tokens, in_weight, vec, out_weight, up_weight, unit_rows, head_scale)


def second_kernel(
    units,
    scaled_ref,
    weight_ref,
    vec_ref,
    tokens_ref,
    unit_ref,
    up_near,
    down_ref,
    branch_ref,
    middle_ref,
    turned_ref,
    act_ref,
    slope_ref,
    stats_ref,
    up_late,
    down_near,
    feed_ref,
    sums_ref,
    up_ref,
    send,
    recv,
    local,
    stream_sems,
):
    step = pl.program_id(0)
    lead = feed_ref.shape[0] // TILE
    place = Place()
    late = LateGather(place, up_near, up_late, send, recv, 0)
    down = NearGather(place, down_ref, down_near, send, recv, LateGather.copies, local.at[0])
    up = WeightStream(up_near, up_late, up_ref, stream_sems)

    @pl.when(step == 0)
    def _():
        place.greet(planes=False)
        late.start()
        up.start(0)
        sums_ref[...] = jnp.zeros_like(sums_ref)

    @pl.when(step == 2)
    def _():
        down.start()

    @pl.when(step < lead)
    def _():
        rows = pl.ds(pl.multiple_of(step * TILE, TILE), TILE)
        feed_ref[rows] = out_proj_rows(
            scaled_ref, weight_ref, vec_ref, tokens_ref, branch_ref, middle_ref
        )

    @pl.when(step >= lead)
    def _():
        block = step - lead

        @pl.when(block == 2)
        def _():
            late.relay()

        @pl.when(block == 3)
        def _():
            late.arrived(2, 3)

        @pl.when(block == 6)
        def _():
            late.arrived(4)

        advance((up,), block, 8)
        up_step(feed_ref, up.block(block), unit_ref.at[0], act_ref, slope_ref, sums_ref)

    @pl.when(step == pl.num_programs(0) - 1)
    def _():
        up_stats(units, stats_ref, sums_ref)
        turned_ref[...] = feed_ref[...].T
        late.finish()
        down.finish()


def second_part(scaled, out_weights, vectors, tokens, up_near, unit_vec, down_weight):
    rows, width = tokens.shape
    steps = 8
    lead = rows // TILE

    def early(step):
        return jnp.minimum(step, lead - 1)

    def unit(step):
        return unit_index(jnp.maximum(step - lead, 0))

    by_row = pl.BlockSpec((TILE, width), lambda s: (early(s), 0))
    block = pl.BlockSpec((1, rows, UNITS), lambda s: (unit(s), 0, 0))
    return pl.pallas_call(
        functools.partial(second_kernel, steps * UNITS),
        grid=(lead + steps,),
        in_specs=[
            by_row,
            whole((width, width)),
            whole(vectors.shape),
            by_row,
            pl.BlockSpec((1, unit_vec.shape[1], UNITS), lambda s: (unit(s), 0, 0)),
            ANY,
            ANY,
        ],
        out_specs=[
            by_row,
            by_row,
            whole((width, rows)),
            block,
            block,
            whole((rows, 128)),
            ANY,
            ANY,
        ],
        out_shape=[
            jax.ShapeDtypeStruct((rows, width), F32),
            jax.ShapeDtypeStruct((rows, width), F32),
            jax.ShapeDtypeStruct((width, rows), BF),
            jax.ShapeDtypeStruct((steps, rows, UNITS), BF),
            jax.ShapeDtypeStruct((steps, rows, UNITS), BF),
            jax.ShapeDtypeStruct((rows, 128), F32),
            jax.ShapeDtypeStruct((4, *up_near.shape[3:]), BF),
            jax.ShapeDtypeStruct((2, 2, 2, *down_weight.shape), BF),
        ],
        scratch_shapes=[
            pltpu.VMEM((rows, width), BF),
            pltpu.VMEM((2, rows, 128), F32),
            pltpu.VMEM((2, *up_near.shape[3:]), BF),
            *dma_sems(LateGather.copies + NearGather.copies),
            pltpu.SemaphoreType.DMA((1,)),
            pltpu.SemaphoreType.DMA((2,)),
        ],
        compiler_params=params(collective_id=2, has_side_effects=True),
        name="second_part",
    )(scaled, out_weights, vectors, tokens, unit_vec, up_near, down_weight)


def third_kernel(
    units,
    act_ref,
    stats_ref,
    vec_ref,
    cot_ref,
    middle_ref,
    shift_ref,
    down_near,
    mixed_ref,
    down_grad_ref,
    e_ref,
    all_stats_ref,
    vec_grad_ref,
    down_late,
    total_ref,
    sums_ref,
    low_ref,
    down_ref,
    send,
    recv,
    stream_sems,
):
    step = pl.program_id(0)
    place = Place()
    late = LateGather(place, down_near, down_late, send, recv, 0)
    down = WeightStream(down_near, down_late, down_ref, stream_sems)

    @pl.when(step == 0)
    def _():
        place.greet(planes=False)
        late.start()
        down.start(0)
        total_ref[...] = jnp.zeros_like(total_ref)
        sums_ref[...] = jnp.zeros_like(sums_ref)

    @pl.when(step == 3)
    def _():
        late.relay()
        late.arrived(2, 3)

    @pl.when(step == 6)
    def _():
        late.arrived(4)

    advance((down,), step, 8)
    down_step(
        act_ref, stats_ref, vec_ref.at[0], down.block(step), cot_ref, down_grad_ref, e_ref,
        vec_grad_ref, total_ref, sums_ref, low_ref
    )

    @pl.when(step == pl.num_programs(0) - 1)
    def _():
        down_end(
            units, stats_ref, middle_ref, shift_ref, mixed_ref, all_stats_ref, total_ref, sums_ref
        )
        late.finish()


def third_part(act, stats, vec, down_near, cotangent, middle, shift):
    rows, width = cotangent.shape
    steps = 8

    def unit(shape):
        return pl.BlockSpec((1, *shape), lambda s: (unit_index(s), 0, 0))

    block = unit((rows, UNITS))
    return pl.pallas_call(
        functools.partial(third_kernel, steps * UNITS),
        grid=(steps,),
        in_specs=[
            block,
            whole((rows, 128)),
            unit((vec.shape[1], UNITS)),
            whole((rows, width)),
            whole((rows, width)),
            whole((1, width)),
            ANY,
        ],
        out_specs=[
            whole((rows, width)),
            unit((UNITS, width)),
            block,
            whole((rows, 128)),
            unit((8, UNITS)),
            ANY,
        ],
        out_shape=[
            jax.ShapeDtypeStruct((rows, width), BF),
            jax.ShapeDtypeStruct((steps, UNITS, width), BF),
            jax.ShapeDtypeStruct((steps, rows, UNITS), BF),
            jax.ShapeDtypeStruct((rows, 128), F32),
            jax.ShapeDtypeStruct((steps, 8, UNITS), F32),
            jax.ShapeDtypeStruct((4, *down_near.shape[3:]), BF),
        ],
        scratch_shapes=[
            pltpu.VMEM((rows, width), F32),
            pltpu.VMEM((2, rows, 128), F32),
            pltpu.VMEM((rows, UNITS), BF),
            pltpu.VMEM((2, *down_near.shape[3:]), BF),
            *dma_sems(LateGather.copies),
            pltpu.SemaphoreType.DMA((2,)),
        ],
        compiler_params=params(collective_id=3, has_side_effects=True),
        name="third_part",
    )(act, stats, vec, cotangent, middle, shift, down_near)


NORMS_AT, COLUMNS_AT, HEADS_AT, TOKENS_AT, VECTORS_AT = 8, 16, 20, 28, 32
BACK_STEPS = VECTORS_AT + 7
OUT_TILE = 128


def chunk_at(time):
    chunk = jnp.where(time < 13, time, time - 1)
    chunk = jnp.where(time >= 20, (time + 17) // 2, chunk)
    return chunk, (time >= 0) & ((time < 13) | ((time >= 14) & (time < 20)) | ((time >= 20) & (time < 30) & (time % 2 == 1)))


def back_kernel(
    lengths_ref,
    unit_grad_ref,
    vec_ref,
    hs_ref,
    act_all,
    slope_all,
    e_all,
    stats_all,
    up_near,
    up_late,
    feed_turned_all,
    down_grad_all,
    cot_all,
    middle_all,
    branch_all,
    scaled_turned_all,
    attended_all,
    out_weight_all,
    proj_all,
    lse_all,
    in_weight_all,
    turned_all,
    tokens_all,
    down_out,
    up_out,
    in_out,
    out_out,
    vec_out,
    tokens_grad_all,
    up_grad_all,
    units_in_ref,
    up_ref,
    stats_ref,
    feed_turned_ref,
    cot_ref,
    norms_in_ref,
    scaled_turned_ref,
    attended_ref,
    out_weight_ref,
    proj_ref,
    lse_ref,
    in_weight_ref,
    turned_ref,
    tokens_ref,
    tokens_grad_ref,
    staged_ref,
    total_ref,
    low_ref,
    out_grad_ref,
    ga_ref,
    grad_middle_ref,
    delta_ref,
    delta_sum_ref,
    sums_ref,
    units_ref,
    dq_ref,
    dk_ref,
    dv_ref,
    chunk_ref,
    stream_sems,
    fetch_sems,
    *scratch,
):
    step = pl.program_id(0)
    place = Place()
    engine = Reduction(place, scratch[:11])
    small = SmallReduction(place, scratch[11:])
    pairs = proj_all.shape[0]

    def rows_of(array, size):
        return lambda i: array.at[pl.ds(pl.multiple_of(i * size, size), size)]

    def columns_of(array, size):
        return lambda i: array.at[:, pl.ds(pl.multiple_of(i * size, size), size)]

    def stream(number, view, buffers):
        return Stream(view, buffers, stream_sems.at[number])

    act, slope, e = (
        stream(k, lambda i, array=array: array.at[unit_index(i)], units_in_ref.at[k])
        for k, array in enumerate((act_all, slope_all, e_all))
    )
    up = WeightStream(up_near, up_late, up_ref, stream_sems.at[3])
    cot = stream(4, rows_of(cot_all, OUT_TILE), cot_ref)
    middle = stream(5, rows_of(middle_all, OUT_TILE), norms_in_ref.at[0])
    branch = stream(6, rows_of(branch_all, OUT_TILE), norms_in_ref.at[1])
    attended = stream(7, columns_of(attended_all, TILE), attended_ref)
    proj = stream(8, lambda i: proj_all.at[i], proj_ref)
    lse = stream(9, lambda i: lse_all.at[i], lse_ref)
    in_weight = stream(10, columns_of(in_weight_all, 384), in_weight_ref)
    tokens = stream(11, rows_of(tokens_all, TILE), tokens_ref)
    put = rows_of(tokens_grad_all, TILE)

    def put_tokens(i):
        return pltpu.make_async_copy(
            tokens_grad_ref.at[i % 2], put(i), stream_sems.at[12, i % 2]
        )

    fetches = [
        pltpu.make_async_copy(source, target, fetch_sems.at[index])
        for index, (source, target) in enumerate(
            (
                (stats_all, stats_ref),
                (feed_turned_all, feed_turned_ref),
                (scaled_turned_all, scaled_turned_ref),
                (out_weight_all, out_weight_ref),
                (turned_all, turned_ref),
            )
        )
    ]

    @pl.when(step == 0)
    def _():
        for item in (act, slope, e, up):
            item.start(0)
        for copy in fetches:
            copy.start()
        for item in (cot, middle, branch, attended, proj, lse, in_weight, tokens):
            item.copy(0).start()
        total_ref[...] = jnp.zeros_like(total_ref)
        sums_ref[...] = jnp.zeros_like(sums_ref)
        units_ref[...] = jnp.zeros_like(units_ref)
        place.greet()

    def store(index):
        block = unit_index(index)
        view = up_grad_all.at[block // 4, block // 2 % 2, block % 2]
        return pltpu.make_async_copy(staged_ref, view, fetch_sems.at[5])

    @pl.when((step >= 1) & (step <= NORMS_AT))
    def _():
        store(step - 1).wait()


    def stage(number, kind, action, tick):
        chunk, there = chunk_at(tick - number * LAG)
        up = ((chunk >= 8) & (chunk < 14)) | (chunk == 15) | (chunk == 17)
        wanted = {
            "all": there,
            "down": there & (chunk < 8),
            "up": there & up,
            "shared": there & ((chunk < 8) | up),
            "own": there & (chunk >= 8) & ~up,
        }

        @pl.when(wanted[kind])
        def _():
            action(chunk)

    def up_index(chunk):
        return jnp.where(chunk < 14, chunk - 8, (chunk - 3) // 2)

    def pair_index(chunk):
        return jnp.where(chunk < 18, (chunk - 14) // 2, chunk - 16)

    def put_down(chunk):
        for rank, block in engine.stage6(chunk):
            for half in range(2):

                @pl.when(chunk % 2 == half)
                def _():
                    down_out[chunk // 2, rank, :, half * 512 : half * 512 + 512] = block

    def put_up(chunk):
        for rank, block in engine.stage6(chunk):
            up_out[up_index(chunk), rank] = block

    def put_own(chunk):
        total = engine.stage4(chunk)
        first = pair_index(chunk) * 128
        for part in range(3):
            lanes = pl.ds(pl.multiple_of(part * 1024 + first, 128), 128)
            in_out[:, lanes] = total[:, part * 128 : part * 128 + 128]
        out_out[:, pl.ds(pl.multiple_of(first, 128), 128)] = total[:, 384:512]

    def take_down(chunk):
        lanes = pl.ds(pl.multiple_of(chunk % 2 * 512, 512), 512)
        engine.stage0(chunk, down_grad_all.at[:, :, :, chunk // 2, :, :, lanes])

    def take_up(chunk):
        engine.stage0(chunk, up_grad_all.at[:, :, :, up_index(chunk)])

    def take_own(chunk):
        engine.stage0(chunk, chunk_ref.at[pair_index(chunk) % 2])

    def reduce_step(tick):
        stage(6, "down", put_down, tick)
        stage(6, "up", put_up, tick)
        stage(5, "shared", engine.stage5, tick)
        stage(4, "shared", lambda chunk: engine.spread(chunk, engine.stage4(chunk)), tick)
        stage(4, "own", put_own, tick)
        stage(3, "all", engine.stage3, tick)
        stage(2, "all", engine.stage2, tick)
        stage(1, "all", engine.stage1, tick)
        stage(0, "down", take_down, tick)
        stage(0, "up", take_up, tick)

    tick = jnp.where(step < NORMS_AT, step, NORMS_AT + (step - NORMS_AT) // 4)
    tick = jnp.where(step < COLUMNS_AT, tick, step - 6)
    tick = jnp.where(step < HEADS_AT, tick, 2 * step - 26)
    tick = jnp.where(step < TOKENS_AT, tick, 30)
    tick = jnp.where(step < VECTORS_AT, tick, step - 1)
    within = (step > NORMS_AT) & (step < COLUMNS_AT) & (step % 4 != 0)
    within = within | ((step > TOKENS_AT) & (step < VECTORS_AT))

    @pl.when(~within)
    def _():
        reduce_step(tick)


    @pl.when(step < NORMS_AT)
    def _():
        advance((act, slope, e, up), step, NORMS_AT)

        @pl.when(step == 0)
        def _():
            fetches[0].wait()

        unit = unit_index(step)
        units_ref[unit, 0:1] = up_back_step(
            act.block(step),
            slope.block(step),
            e.block(step),
            stats_ref,
            up.block(step),
            low_ref,
            total_ref,
        )
        units_ref[unit, 1:3] = unit_grad_ref[unit, 0:2]

        @pl.when(step == 0)
        def _():
            fetches[1].wait()

        for left in range(0, UNITS, TILE):
            columns = slice(left, left + TILE)
            grad = dot_nn(feed_turned_ref[...], low_ref[:, columns]).astype(BF)
            staged_ref[:, :, :, columns] = grad.reshape(8, 4, 32, TILE)
        store(step).start()


    @pl.when((step >= NORMS_AT) & (step < COLUMNS_AT))
    def _():
        block = step - NORMS_AT
        rows = pl.ds(pl.multiple_of(block * OUT_TILE, OUT_TILE), OUT_TILE)
        advance((cot, middle, branch), block, COLUMNS_AT - NORMS_AT)
        grad_middle, low = norms_back(
            total_ref[rows],
            cot.block(block),
            middle.block(block),
            branch.block(block),
            vec_ref,
            sums_ref,
        )
        grad_middle_ref[rows] = grad_middle
        low_ref[rows] = low

    @pl.when((step >= COLUMNS_AT) & (step < HEADS_AT))
    def _():
        block = step - COLUMNS_AT
        columns = pl.ds(pl.multiple_of(block * TILE, TILE), TILE)
        advance((attended,), block, HEADS_AT - COLUMNS_AT)

        @pl.when(block == 0)
        def _():
            fetches[2].wait()
            fetches[3].wait()

        grad_out, delta = heads_back(
            low_ref[...],
            out_weight_ref[columns],
            hs_ref[0:1, columns],
            attended.block(block)[...],
        )
        ga_ref[:, columns] = grad_out
        delta_sum_ref[block, 0:1] = column_sum(delta)
        turned = delta.T
        for head in range(4):
            delta_ref[4 * block + head] = turned[head : head + 1]
        out_grad_ref[:, columns] = dot_nn(scaled_turned_ref[...], low_ref[:, columns]).astype(BF)

    @pl.when(step == HEADS_AT - 1)
    def _():
        total_ref[...] = jnp.zeros_like(total_ref)


    @pl.when((step >= HEADS_AT) & (step < TOKENS_AT))
    def _():
        pair = step - HEADS_AT
        columns = pl.ds(pl.multiple_of(pair * 128, 128), 128)
        advance((proj, lse, in_weight), pair, pairs)

        @pl.when(pair == 0)
        def _():
            fetches[4].wait()

        for head in range(2):
            if head == 1:
                reduce_step(tick + 1)
            attention_back_head(
                head,
                cross_flag(lengths_ref, total_ref),
                *[proj.block(pair).at[:, pl.ds(index * 128, 128)] for index in range(3)],
                ga_ref.at[:, columns],
                lse.block(pair),
                delta_ref[2 * pair + head],
                dq_ref,
                dk_ref,
                dv_ref,
            )
        query_sum, value_sum = in_back_pair(
            dq_ref,
            dk_ref,
            dv_ref,
            in_weight.block(pair)[...],
            turned_ref,
            out_grad_ref.at[:, columns],
            chunk_ref.at[pair % 2].reshape(8, 4, 32, 512),
            total_ref,
        )
        sums_ref[0:1, columns] = query_sum
        sums_ref[1:2, columns] = value_sum
        stage(0, "own", take_own, tick + 1)

    @pl.when((step >= TOKENS_AT) & (step < TOKENS_AT + 4))
    def _():
        block = step - TOKENS_AT
        rows = pl.ds(pl.multiple_of(block * TILE, TILE), TILE)
        advance((tokens,), block, 4)

        @pl.when(block >= 2)
        def _():
            put_tokens(block - 2).wait()

        result, gain_grad, shift_grad = tokens_back(
            tokens.block(block)[...], total_ref[rows], grad_middle_ref[rows], vec_ref[3:4]
        )
        tokens_grad_ref[block % 2] = result
        put_tokens(block).start()
        sums_ref[3:4] += gain_grad
        sums_ref[4:5] += shift_grad


    @pl.when(step == VECTORS_AT)
    def _():
        for y in range(2):
            for z in range(4):
                own = slice((2 * z + y) * 128, (2 * z + y + 1) * 128)
                for index in range(9):
                    lanes = slice(index % 4 * 128, index % 4 * 128 + 128)
                    row = 6 + index // 4
                    units_ref[8, row : row + 1, lanes] = sums_ref[index : index + 1, own]
                for x in range(2):
                    for c in range(2):
                        unit = 4 * y + 2 * x + c
                        units_ref[8, 0:3] = units_ref[unit, 0:3]
                        if (y, z, x, c) == (0, 0, 0, 0):
                            units_ref[8, 3:4] = sums_ref[9:10, 0:UNITS]
                            units_ref[8, 4:5] = sums_ref[9:10, UNITS : 2 * UNITS]
                            for block in range(4):
                                lanes = slice(block * 128, block * 128 + 128)
                                units_ref[8, 5:6, lanes] = delta_sum_ref[block, 0:1]
                        small.source[y, x, c, z] = units_ref[8].astype(BF)
        small.stage0()

    for index, action in enumerate((small.stage1, small.stage2, small.stage3)):

        @pl.when(step == VECTORS_AT + 1 + index)
        def _():
            action()

    @pl.when(step == VECTORS_AT + 4)
    def _():
        vec_out[...] = small.stage4()
        for block in range(2, 4):
            put_tokens(block).wait()


def back_part(
    lengths,
    act,
    slope,
    e,
    stats,
    up_near,
    up_late,
    feed_turned,
    unit_grad,
    down_grad,
    cotangent,
    middle,
    branch,
    scaled_turned,
    attended,
    out_weights,
    vectors,
    head_lanes,
    projected,
    lse,
    weights,
    turned,
    tokens,
):
    rows, width = tokens.shape
    pairs = width // 128

    return pl.pallas_call(
        back_kernel,
        grid=(BACK_STEPS,),
        in_specs=[
            pl.BlockSpec(memory_space=pltpu.SMEM),
            whole(unit_grad.shape),
            whole(vectors.shape),
            whole(head_lanes.shape),
            *[ANY] * 19,
        ],
        out_specs=[
            whole((4, 4, 32, 1024)),
            whole((8, 4, 32, 512)),
            whole((32, 3 * width)),
            whole((32, width)),
            whole((16, 512)),
            ANY,
            ANY,
        ],
        out_shape=[
            jax.ShapeDtypeStruct((4, 4, 32, 1024), BF),
            jax.ShapeDtypeStruct((8, 4, 32, 512), BF),
            jax.ShapeDtypeStruct((32, 3 * width), F32),
            jax.ShapeDtypeStruct((32, width), F32),
            jax.ShapeDtypeStruct((16, 512), F32),
            jax.ShapeDtypeStruct((rows, width), BF),
            jax.ShapeDtypeStruct((2, 2, 2, 8, 4, 32, UNITS), BF),
        ],
        scratch_shapes=[
            pltpu.VMEM((3, 2, rows, UNITS), BF),
            pltpu.VMEM((2, width, UNITS), BF),
            pltpu.VMEM((rows, 128), F32),
            pltpu.VMEM((width, rows), BF),
            pltpu.VMEM((2, OUT_TILE, width), BF),
            pltpu.VMEM((2, 2, OUT_TILE, width), F32),
            pltpu.VMEM((width, rows), BF),
            pltpu.VMEM((2, rows, TILE), F32),
            pltpu.VMEM((width, width), BF),
            pltpu.VMEM((2, rows, 384), BF),
            pltpu.VMEM((2, 8, rows), F32),
            pltpu.VMEM((2, width, 384), BF),
            pltpu.VMEM((width, rows), BF),
            pltpu.VMEM((2, TILE, width), BF),
            pltpu.VMEM((2, TILE, width), BF),
            pltpu.VMEM((8, 4, 32, UNITS), BF),
            pltpu.VMEM((rows, width), F32),
            pltpu.VMEM((rows, width), BF),
            pltpu.VMEM((width, width), BF),
            pltpu.VMEM((rows, width), BF),
            pltpu.VMEM((rows, width), F32),
            pltpu.VMEM((2 * pairs, 1, rows), F32),
            pltpu.VMEM((4, 8, 128), F32),
            pltpu.VMEM((16, width), F32),
            pltpu.VMEM((9, 16, UNITS), F32),
            pltpu.VMEM((rows, 128), F32),
            pltpu.VMEM((rows, 128), F32),
            pltpu.VMEM((rows, 128), F32),
            pltpu.VMEM((2, 2, 2, 2, 4, 32, 512), BF),
            pltpu.SemaphoreType.DMA((13, 2)),
            pltpu.SemaphoreType.DMA((6,)),
            *Reduction.scratch(),
            *SmallReduction.scratch(),
        ],
        compiler_params=params(collective_id=1, has_side_effects=True),
        name="back_part",
    )(
        lengths,
        unit_grad,
        vectors,
        head_lanes,
        act,
        slope,
        e,
        stats,
        up_near,
        up_late,
        feed_turned,
        down_grad.reshape(2, 2, 2, 4, 4, 32, width),
        cotangent,
        middle,
        branch,
        scaled_turned,
        attended,
        out_weights,
        projected,
        lse,
        weights,
        turned,
        tokens,
    )


def layer(staged, tokens, cotangent, lengths, attn, up, down, unit_vec, head_scale, down_bias):
    rows, width = tokens.shape
    heads = head_scale.shape[0]
    pairs = width // 128
    if staged:
        in_weight, out_weight, vec_block = attn
        (
            turned,
            projected,
            scaled,
            scaled_turned,
            attended,
            lse,
            vectors,
            head_lanes,
            weights,
            out_weights,
            up,
            unit_vec,
        ) = first_part(
            lengths, tokens, in_weight, vec_block, out_weight, up, unit_vec, head_scale[None, :]
        )
        weights = weights.reshape(width, 3 * width)
        out_weights = out_weights.reshape(width, width)
        unit_vec = unit_vec.reshape(-1, unit_vec.shape[-2], UNITS)
        branch, middle, feed_turned, act, slope, stats, up_late, down_near = second_part(
            scaled, out_weights, vectors, tokens, up, unit_vec, down
        )
        mixed, down_grad, e, stats, unit_grad, _ = third_part(
            act, stats, unit_vec, down_near, cotangent, middle, down_bias[None, :]
        )
    else:
        weights, out_weights, vectors = attn
        scale = head_scale.astype(F32)
        head_lanes = jnp.repeat(scale, width // heads)[None, :]
        first, projected, scaled, attended, lse = plain_first(
            lengths, tokens, weights, vectors, head_lanes
        )
        branch, middle, feed = out_proj(scaled, out_weights, vectors, tokens)
        act, slope, stats = up_pass(feed, up, unit_vec)
        mixed, down_grad, e, stats, unit_grad = down_pass(
            act, stats, unit_vec, down, cotangent, middle, down_bias[None, :]
        )
    if staged:
        down_total, up_total, in_total, out_total, vec_shares, tokens_grad, _ = back_part(
            lengths,
            act,
            slope,
            e,
            stats,
            up,
            up_late,
            feed_turned,
            unit_grad,
            down_grad,
            cotangent,
            middle,
            branch,
            scaled_turned,
            attended,
            out_weights,
            vectors,
            head_lanes,
            projected,
            lse,
            weights,
            turned,
            tokens,
        )
        return mixed, tokens_grad, down_total, up_total, in_total, out_total, vec_shares
    up_grad, up_bias_grad, grad_feed = up_back(
        act, slope, e, stats, up, feed
    )
    grad_middle, ga, out_grad, delta, sums = out_back(
        grad_feed,
        cotangent,
        middle,
        branch,
        scaled,
        attended,
        out_weights,
        vectors,
        head_lanes,
    )
    chunks, proj_bias, tokens_grad, pre_sums = in_back(
        lengths,
        projected,
        ga,
        lse,
        delta.reshape(pairs, 2, rows),
        weights,
        first,
        out_grad,
        tokens,
        vectors[3:4],
        grad_middle,
    )
    scale_grad = jnp.sum(delta, axis=1) / scale
    vec_grads = [
        proj_bias[:, 0].reshape(width),
        proj_bias[:, 1].reshape(width),
        sums[2],
        pre_sums[0],
        pre_sums[1],
        sums[5],
        sums[6],
        sums[7],
        sums[8],
    ]
    unit_grads = [up_bias_grad[:, 0], unit_grad[:, 0], unit_grad[:, 1]]
    return mixed, tokens_grad, chunks, up_grad, down_grad, vec_grads, unit_grads, sums[9], scale_grad


def body(
    axes,
    tokens,
    cotangent,
    lengths,
    in_weight,
    query_bias,
    value_bias,
    out_weight,
    out_bias,
    head_scale,
    pre_gain,
    pre_bias,
    post_gain,
    post_bias,
    feed_gain,
    feed_bias,
    up_weight,
    up_bias,
    mid_gain,
    mid_bias,
    down_weight,
    down_bias,
):
    planes, wide = axes
    every = ("dp", "wide")
    staged = (planes, wide) == (4, 8)
    rows, width = tokens.shape
    units = down_weight.shape[0] * wide
    steps = units // UNITS
    share = in_weight.shape[0]
    columns = [
        query_bias,
        value_bias,
        out_bias,
        pre_gain,
        pre_bias,
        post_gain,
        post_bias,
        feed_gain,
        feed_bias,
    ]
    index = lax.broadcasted_iota(jnp.int32, (32, up_bias.shape[0]), 0)
    unit_rows = jnp.where(index == 0, up_bias[None, :], jnp.zeros((), BF))
    unit_rows = jnp.where(index == 1, mid_gain[None, :], unit_rows)
    unit_rows = jnp.where(index == 2, mid_bias[None, :], unit_rows)
    if staged:
        index = lax.broadcasted_iota(jnp.int32, (32, share), 0)
        vec_block = jnp.zeros((32, share), BF)
        for row, column in enumerate(columns):
            vec_block = jnp.where(index == row, column[None, :], vec_block)
        attn = (in_weight, out_weight, vec_block)
        up, unit_vec, down = up_weight, unit_rows, down_weight
    else:
        flat = jnp.concatenate(columns).reshape(len(columns), share)
        attn = (
            lax.all_gather(in_weight, every, axis=0, tiled=True),
            lax.all_gather(out_weight, every, axis=0, tiled=True),
            jnp.pad(
                lax.all_gather(flat, every, axis=1, tiled=True), ((0, 16 - len(columns)), (0, 0))
            ).astype(F32),
        )
        up = lax.all_gather(up_weight, "wide", axis=1, tiled=True)
        up = up.reshape(width, steps, UNITS).transpose(1, 0, 2)
        unit_vec = lax.all_gather(unit_rows, "wide", axis=1, tiled=True)
        unit_vec = unit_vec.reshape(32, steps, UNITS).transpose(1, 0, 2)
        down = lax.all_gather(down_weight, "wide", axis=0, tiled=True)
        down = down.reshape(steps, UNITS, width)
    results = layer(
        staged,
        tokens,
        cotangent,
        lengths,
        attn,
        up,
        down,
        unit_vec,
        head_scale,
        down_bias,
    )
    heads = head_scale.shape[0]
    pairs = width // 128
    if staged:
        mixed, tokens_grad, down_total, up_total, in_total, out_total, vec_shares = results
        up_total = up_total.astype(F32).reshape(width, UNITS)
        down_total = down_total.astype(F32).reshape(UNITS, width)
        unit_totals = [vec_shares[index] for index in range(3)]
        down_sum = vec_shares[3:5].reshape(width)
        scale_sum = vec_shares[5].reshape(4, 128)[:, :4].reshape(heads) / head_scale.astype(F32)
        offset = share * lax.rem(lax.axis_index("wide"), 128 // share)
        own = vec_shares[6:9].reshape(12, 128)
        own = lax.dynamic_slice(own, (0, offset), (len(columns), share))
        vec_totals = [own[index] for index in range(len(columns))]
    else:
        (mixed, tokens_grad, chunks, up_grad, down_grad, vec_grads, unit_grads) = results[:7]
        down_sum, scale_sum = results[7:]

        def scatter(value, axis=0, over=every):
            return lax.psum_scatter(value, over, scatter_dimension=axis, tiled=True)

        def both_ways(value, axis):
            part = scatter(value.astype(BF), axis, "wide")
            return lax.psum(part, "dp").astype(F32)

        up_total = both_ways(up_grad.transpose(1, 0, 2).reshape(width, units), 1)
        down_total = both_ways(down_grad.reshape(units, width), 0)
        unit_totals = [
            lax.psum(scatter(item.reshape(units), 0, "wide"), "dp") for item in unit_grads
        ]
        down_sum, scale_sum = lax.psum((down_sum, scale_sum), every)
        vec_totals = [scatter(item) for item in vec_grads]
        natural = chunks.transpose(0, 2, 1, 3, 4).reshape(pairs, width, 512)
        in_total = natural[:, :, :384].reshape(pairs, width, 3, 128)
        in_total = scatter(in_total.transpose(1, 2, 0, 3).reshape(width, 3 * width).astype(F32))
        out_total = scatter(
            natural[:, :, 384:].transpose(1, 0, 2).reshape(width, width).astype(F32)
        )
    return (
        mixed,
        tokens_grad,
        in_total,
        vec_totals[0],
        vec_totals[1],
        out_total,
        vec_totals[2],
        scale_sum,
        vec_totals[3],
        vec_totals[4],
        vec_totals[5],
        vec_totals[6],
        vec_totals[7],
        vec_totals[8],
        up_total,
        unit_totals[0],
        unit_totals[1],
        unit_totals[2],
        down_total,
        down_sum,
    )


def solution(mesh):
    by_all = P(("dp", "wide"))
    rows_all = P(("dp", "wide"), None)
    axes = (mesh.shape["dp"], mesh.shape["wide"])
    return jax.shard_map(
        functools.partial(body, axes),
        mesh=mesh,
        in_specs=(
            rows_all,
            rows_all,
            rows_all,
            rows_all,
            by_all,
            by_all,
            rows_all,
            by_all,
            P(),
            by_all,
            by_all,
            by_all,
            by_all,
            by_all,
            by_all,
            P(None, "wide"),
            P("wide"),
            P("wide"),
            P("wide"),
            P("wide", None),
            P(),
        ),
        out_specs=(
            rows_all,
            rows_all,
            rows_all,
            by_all,
            by_all,
            rows_all,
            by_all,
            P(),
            by_all,
            by_all,
            by_all,
            by_all,
            by_all,
            by_all,
            P(None, "wide"),
            P("wide"),
            P("wide"),
            P("wide"),
            P("wide", None),
            P(),
        ),
        check_vma=False,
    )
```

```python
import functools

import jax
import jax.numpy as jnp
from jax import lax
from jax.experimental import pallas as pl
from jax.experimental.pallas import tpu as pltpu
from jax.sharding import PartitionSpec as P

EPS = 1e-05
ROOT_HALF = 0.7071067811865476
INV_ROOT_TAU = 0.3989422804014327
LOG2E = 1.4426950408889634
MASKED = -1e30
BF = jnp.bfloat16
F32 = jnp.float32
TILE = 256
UNITS = 512
SLIM = 64
MESH = pl.DeviceIdType.MESH
VMEM_LIMIT = 62 * 1024 * 1024
ANY = pl.BlockSpec(memory_space=pl.ANY)


def dot_nn(left, right):
    return lax.dot_general(left, right, (((1,), (0,)), ((), ())), preferred_element_type=F32)


def dot_nt(left, right):
    return lax.dot_general(left, right, (((1,), (1,)), ((), ())), preferred_element_type=F32)


def dot_tn(left, right):
    return lax.dot_general(left, right, (((0,), (0,)), ((), ())), preferred_element_type=F32)


def params(**more):
    return pltpu.CompilerParams(
        dimension_semantics=("arbitrary",), vmem_limit_bytes=VMEM_LIMIT, **more
    )


def whole(shape):
    zeros = (0,) * len(shape)
    return pl.BlockSpec(shape, lambda *_: zeros, pipeline_mode=pl.Buffered(1))


def row_norm(values):
    center = values - jnp.mean(values, axis=-1, keepdims=True)
    inv = lax.rsqrt(jnp.mean(center * center, axis=-1, keepdims=True) + EPS)
    return center * inv, inv


def norm_back(grad, gain, normed, inv):
    scaled = grad * gain
    first = jnp.mean(scaled, axis=-1, keepdims=True)
    cross = jnp.mean(scaled * normed, axis=-1, keepdims=True)
    return inv * (scaled - first - normed * cross)


def column_sum(values):
    return jnp.sum(values, axis=0, keepdims=True)


def lane_fold(values):
    total = values[:, :128]
    for start in range(128, values.shape[1], 128):
        total = total + values[:, start : start + 128]
    return total


def cross_flag(lengths_ref, rows_ref):
    return jnp.where(lengths_ref[0, 0] == rows_ref.shape[0], 0.0, MASKED)


def attention_pair(cross, q_ref, k_ref, v_ref, scale, scaled_ref, out_ref, lse_ref, vext_ref):
    rows = q_ref.shape[0]
    half = rows // 2
    factor = LOG2E * 64 ** (-0.5)
    low_lanes = lax.broadcasted_iota(jnp.int32, (1, 128), 1) < 64
    below = lax.broadcasted_iota(jnp.int32, (TILE, TILE), 1) <= lax.broadcasted_iota(
        jnp.int32, (TILE, TILE), 0
    )
    vext_ref[:, :128] = v_ref[...]
    vext_ref[:, 128:] = jnp.ones((rows, 128), BF)
    for start in range(0, rows, TILE):
        stop = start + TILE
        query = q_ref[start:stop]
        results = []
        for head in range(2):
            mine = low_lanes if head == 0 else ~low_lanes
            raw = dot_nt(jnp.where(mine, query, jnp.zeros_like(query)), k_ref[:stop])
            parts = []
            if start >= half:
                parts.append((raw[:, :half], cross))
                if start > half:
                    parts.append((raw[:, half:start], None))
            elif start > 0:
                parts.append((raw[:, :start], None))
            parts.append((jnp.where(below, raw[:, start:stop], MASKED), None))
            peak = None
            for piece, shift in parts:
                top = jnp.max(piece, axis=-1, keepdims=True)
                if shift is not None:
                    top = top + shift
                peak = top if peak is None else jnp.maximum(peak, top)
            weights = []
            for piece, shift in parts:
                level = peak if shift is None else peak - shift
                weights.append(jnp.exp2((piece - level) * factor).astype(BF))
            weights = weights[0] if len(weights) == 1 else jnp.concatenate(weights, axis=1)
            both = dot_nn(weights, vext_ref[:stop])
            total = both[:, 128:]
            results.append((both[:, :128] / total, peak * factor + jnp.log2(total)))
        mixed = jnp.where(low_lanes, results[0][0], results[1][0])
        out_ref[start:stop] = mixed
        scaled_ref[start:stop] = (mixed * scale).astype(BF)
        lse = jnp.where(low_lanes, results[0][1], results[1][1]).T
        lse_ref[0, 0:1, start:stop] = lse[0:1]
        lse_ref[0, 1:2, start:stop] = lse[64:65]


def project_pair(first_ref, weights, bias, proj_ref):
    proj_ref[0] = (dot_nn(first_ref[...], weights) + bias).astype(BF)


def three(proj_ref):
    return [proj_ref.at[0, :, pl.ds(part * 128, 128)] for part in range(3)]


def plain_first_kernel(
    lengths_ref,
    tokens_ref,
    wq_ref,
    wk_ref,
    wv_ref,
    vectors_ref,
    bq_ref,
    bv_ref,
    hs_ref,
    first_ref,
    proj_ref,
    scaled_ref,
    attended_ref,
    lse_ref,
    vext_ref,
):
    @pl.when(pl.program_id(0) == 0)
    def _():
        for start in range(0, tokens_ref.shape[0], TILE):
            rows = pl.ds(start, TILE)
            normed, _ = row_norm(tokens_ref[rows].astype(F32))
            first_ref[rows] = (normed * vectors_ref[3:4] + vectors_ref[4:5]).astype(BF)

    weights = jnp.concatenate([wq_ref[...], wk_ref[...], wv_ref[...]], axis=1)
    bias = jnp.concatenate([bq_ref[0:1], jnp.zeros((1, 128), F32), bv_ref[1:2]], axis=1)
    project_pair(first_ref, weights, bias, proj_ref)
    attention_pair(
        cross_flag(lengths_ref, tokens_ref), *three(proj_ref), hs_ref[...], scaled_ref, attended_ref, lse_ref, vext_ref
    )


def plain_first(lengths, tokens, weights, vectors, head_lanes):
    rows, width = tokens.shape
    pairs = width // 128
    column = pl.BlockSpec((rows, 128), lambda p: (0, p))
    bias = pl.BlockSpec((16, 128), lambda p: (0, p))
    return pl.pallas_call(
        plain_first_kernel,
        grid=(pairs,),
        in_specs=[
            pl.BlockSpec(memory_space=pltpu.SMEM),
            whole((rows, width)),
            pl.BlockSpec((width, 128), lambda p: (0, p)),
            pl.BlockSpec((width, 128), lambda p: (0, pairs + p)),
            pl.BlockSpec((width, 128), lambda p: (0, 2 * pairs + p)),
            whole(vectors.shape),
            bias,
            bias,
            pl.BlockSpec((1, 128), lambda p: (0, p)),
        ],
        out_specs=[
            whole((rows, width)),
            pl.BlockSpec((1, rows, 384), lambda p: (p, 0, 0)),
            column,
            column,
            pl.BlockSpec((1, 8, rows), lambda p: (p, 0, 0)),
        ],
        out_shape=[
            jax.ShapeDtypeStruct((rows, width), BF),
            jax.ShapeDtypeStruct((pairs, rows, 384), BF),
            jax.ShapeDtypeStruct((rows, width), BF),
            jax.ShapeDtypeStruct((rows, width), F32),
            jax.ShapeDtypeStruct((pairs, 8, rows), F32),
        ],
        scratch_shapes=[pltpu.VMEM((rows, 256), BF)],
        compiler_params=params(),
        name="plain_first",
    )(lengths, tokens, weights, weights, weights, vectors, vectors, vectors, head_lanes)


def out_proj_rows(scaled_ref, weight_ref, vec_ref, tokens_ref, branch_ref, middle_ref):
    branch = dot_nn(scaled_ref[...], weight_ref[...]) + vec_ref[2:3]
    normed, _ = row_norm(branch)
    middle = tokens_ref[...].astype(F32) + (normed * vec_ref[5:6] + vec_ref[6:7])
    again, _ = row_norm(middle)
    branch_ref[...] = branch
    middle_ref[...] = middle
    return (again * vec_ref[7:8] + vec_ref[8:9]).astype(BF)


def out_proj_kernel(scaled_ref, weight_ref, vec_ref, tokens_ref, branch_ref, middle_ref, feed_ref):
    feed_ref[...] = out_proj_rows(
        scaled_ref, weight_ref, vec_ref, tokens_ref, branch_ref, middle_ref
    )


def out_proj(scaled, weights, vectors, tokens):
    rows, width = tokens.shape
    by_row = pl.BlockSpec((TILE, width), lambda i: (i, 0))
    return pl.pallas_call(
        out_proj_kernel,
        grid=(rows // TILE,),
        in_specs=[
            by_row,
            whole((width, width)),
            whole(vectors.shape),
            by_row,
        ],
        out_specs=[by_row, by_row, by_row],
        out_shape=[
            jax.ShapeDtypeStruct((rows, width), F32),
            jax.ShapeDtypeStruct((rows, width), F32),
            jax.ShapeDtypeStruct((rows, width), BF),
        ],
        compiler_params=params(),
        name="out_proj",
    )(scaled, weights, vectors, tokens)


def phi_and_slope(value):
    bell = jnp.exp2(value * value * (-0.5 * LOG2E))
    t = 1.0 / (1.0 + (0.3275911 * ROOT_HALF) * jnp.abs(value))
    series = t * (
        0.5 * 0.254829592
        + t
        * (
            0.5 * -0.284496736
            + t * (0.5 * 1.421413741 + t * (0.5 * -1.453152027 + t * (0.5 * 1.061405429)))
        )
    )
    tail = series * bell
    area = jnp.where(value < 0.0, tail, 1.0 - tail)
    return value * area, area + value * bell * INV_ROOT_TAU


def up_step(feed_ref, up, vec, act_ref, slope_ref, sums_ref):
    for left in range(0, UNITS, TILE):
        columns = slice(left, left + TILE)
        pre = dot_nn(feed_ref[...], up[:, columns])
        bias = vec[0:1, columns].astype(F32)
        for start in range(0, feed_ref.shape[0], SLIM):
            rows = slice(start, start + SLIM)
            act, slope = phi_and_slope(pre[rows] + bias)
            act_ref[0, rows, columns] = act.astype(BF)
            slope_ref[0, rows, columns] = slope.astype(BF)
            sums_ref[0, rows] += lane_fold(act)
            sums_ref[1, rows] += lane_fold(act * act)


def side_by_side(*columns):
    lane = lax.broadcasted_iota(jnp.int32, (1, 128), 1)
    result = jnp.broadcast_to(columns[-1], (columns[-1].shape[0], 128))
    for index in range(len(columns) - 2, -1, -1):
        result = jnp.where(lane == index, columns[index], result)
    return result


def up_stats(units, stats_ref, sums_ref):
    for start in range(0, stats_ref.shape[0], TILE):
        rows = pl.ds(start, TILE)
        mean = jnp.sum(sums_ref[0, rows], axis=1, keepdims=True) / units
        square = jnp.sum(sums_ref[1, rows], axis=1, keepdims=True) / units
        inv = lax.rsqrt(square - mean * mean + EPS)
        stats_ref[rows] = side_by_side(mean, inv)


def up_kernel(units, feed_ref, up_ref, vec_ref, act_ref, slope_ref, stats_ref, sums_ref):
    step = pl.program_id(0)

    @pl.when(step == 0)
    def _():
        sums_ref[...] = jnp.zeros_like(sums_ref)

    up_step(feed_ref, up_ref.at[0], vec_ref.at[0], act_ref, slope_ref, sums_ref)

    @pl.when(step == pl.num_programs(0) - 1)
    def _():
        up_stats(units, stats_ref, sums_ref)


def up_pass(feed, up, vec):
    rows, width = feed.shape
    steps = up.shape[0]
    block = pl.BlockSpec((1, rows, UNITS), lambda j: (j, 0, 0))
    return pl.pallas_call(
        functools.partial(up_kernel, steps * UNITS),
        grid=(steps,),
        in_specs=[
            whole((rows, width)),
            pl.BlockSpec((1, width, UNITS), lambda j: (j, 0, 0)),
            pl.BlockSpec((1, vec.shape[1], UNITS), lambda j: (j, 0, 0)),
        ],
        out_specs=[block, block, whole((rows, 128))],
        out_shape=[
            jax.ShapeDtypeStruct((steps, rows, UNITS), BF),
            jax.ShapeDtypeStruct((steps, rows, UNITS), BF),
            jax.ShapeDtypeStruct((rows, 128), F32),
        ],
        scratch_shapes=[pltpu.VMEM((2, rows, 128), F32)],
        compiler_params=params(),
        name="up_pass",
    )(feed, up, vec)


def down_step(
    act_ref, stats_ref, vec, down, cot_ref, down_grad_ref, e_ref, vec_grad_ref, total_ref, sums_ref,
    low_ref
):
    gain = vec[1:2].astype(F32)
    shift = vec[2:3].astype(F32)
    slims = [slice(start, start + SLIM) for start in range(0, cot_ref.shape[0], SLIM)]

    def normalized(rows, columns):
        value = act_ref[0, rows, columns].astype(F32)
        return (value - stats_ref[rows, 0:1]) * stats_ref[rows, 1:2]

    for rows in slims:
        low_ref[rows] = (normalized(rows, slice(0, UNITS)) * gain + shift).astype(BF)
    for left in range(0, UNITS, TILE):
        columns = slice(left, left + TILE)
        grads = dot_nt(cot_ref[...], down[columns])
        gain_grad = jnp.zeros((SLIM, TILE), F32)
        bias_grad = jnp.zeros((SLIM, TILE), F32)
        for rows in slims:
            normed = normalized(rows, columns)
            grad = grads[rows]
            gain_grad = gain_grad + grad * normed
            bias_grad = bias_grad + grad
            e = grad * gain[:, columns]
            e_ref[0, rows, columns] = e.astype(BF)
            sums_ref[0, rows] += lane_fold(e)
            sums_ref[1, rows] += lane_fold(e * normed)
        vec_grad_ref[0, 0:1, columns] = column_sum(gain_grad)
        vec_grad_ref[0, 1:2, columns] = column_sum(bias_grad)
    for left in range(0, total_ref.shape[1], TILE):
        columns = slice(left, left + TILE)
        total_ref[:, columns] += dot_nn(low_ref[...], down[:, columns])
    for left in range(0, UNITS, TILE):
        columns = slice(left, left + TILE)
        down_grad_ref[0, columns] = dot_tn(low_ref[:, columns], cot_ref[...]).astype(BF)


def down_end(
    units, stats_ref, middle_ref, shift_ref, mixed_ref, all_stats_ref, total_ref, sums_ref
):
    for start in range(0, total_ref.shape[0], TILE):
        rows = pl.ds(start, TILE)
        mixed_ref[rows] = (
            middle_ref[rows] + total_ref[rows] + shift_ref[...].astype(F32)
        ).astype(BF)
        first = jnp.sum(sums_ref[0, rows], axis=1, keepdims=True) / units
        cross = jnp.sum(sums_ref[1, rows], axis=1, keepdims=True) / units
        all_stats_ref[rows] = side_by_side(stats_ref[rows, 0:1], stats_ref[rows, 1:2], first, cross)


def down_kernel(
    units,
    act_ref,
    stats_ref,
    vec_ref,
    down_ref,
    cot_ref,
    middle_ref,
    shift_ref,
    mixed_ref,
    down_grad_ref,
    e_ref,
    all_stats_ref,
    vec_grad_ref,
    total_ref,
    sums_ref,
    low_ref,
):
    step = pl.program_id(0)

    @pl.when(step == 0)
    def _():
        total_ref[...] = jnp.zeros_like(total_ref)
        sums_ref[...] = jnp.zeros_like(sums_ref)

    down_step(
        act_ref, stats_ref, vec_ref.at[0], down_ref.at[0], cot_ref, down_grad_ref, e_ref, vec_grad_ref,
        total_ref, sums_ref, low_ref
    )

    @pl.when(step == pl.num_programs(0) - 1)
    def _():
        down_end(
            units, stats_ref, middle_ref, shift_ref, mixed_ref, all_stats_ref, total_ref, sums_ref
        )


def down_pass(act, stats, vec, down, cotangent, middle, shift):
    rows, width = cotangent.shape
    steps = act.shape[0]
    block = pl.BlockSpec((1, rows, UNITS), lambda j: (j, 0, 0))
    return pl.pallas_call(
        functools.partial(down_kernel, steps * UNITS),
        grid=(steps,),
        in_specs=[
            block,
            whole((rows, 128)),
            pl.BlockSpec((1, vec.shape[1], UNITS), lambda j: (j, 0, 0)),
            pl.BlockSpec((1, UNITS, width), lambda j: (j, 0, 0)),
            whole((rows, width)),
            whole((rows, width)),
            whole((1, width)),
        ],
        out_specs=[
            whole((rows, width)),
            pl.BlockSpec((1, UNITS, width), lambda j: (j, 0, 0)),
            block,
            whole((rows, 128)),
            pl.BlockSpec((1, 8, UNITS), lambda j: (j, 0, 0)),
        ],
        out_shape=[
            jax.ShapeDtypeStruct((rows, width), BF),
            jax.ShapeDtypeStruct((steps, UNITS, width), BF),
            jax.ShapeDtypeStruct((steps, rows, UNITS), BF),
            jax.ShapeDtypeStruct((rows, 128), F32),
            jax.ShapeDtypeStruct((steps, 8, UNITS), F32),
        ],
        scratch_shapes=[
            pltpu.VMEM((rows, width), F32),
            pltpu.VMEM((2, rows, 128), F32),
            pltpu.VMEM((rows, UNITS), BF),
        ],
        compiler_params=params(),
        name="down_pass",
    )(act, stats, vec, down, cotangent, middle, shift)


def up_back_step(act, slope, e, stats_ref, up, low_ref, total_ref):
    bias_grad = jnp.zeros((SLIM, UNITS), F32)
    for start in range(0, total_ref.shape[0], SLIM):
        rows = slice(start, start + SLIM)
        inv = stats_ref[rows, 1:2]
        normed = (act[rows].astype(F32) - stats_ref[rows, 0:1]) * inv
        grad_act = inv * (
            e[rows].astype(F32) - stats_ref[rows, 2:3] - normed * stats_ref[rows, 3:4]
        )
        low = (grad_act * slope[rows].astype(F32)).astype(BF)
        bias_grad = bias_grad + low.astype(F32)
        low_ref[rows, 0:UNITS] = low
    for left in range(0, total_ref.shape[1], TILE):
        columns = slice(left, left + TILE)
        total_ref[:, columns] += dot_nt(low_ref[:, 0:UNITS], up[columns])
    return column_sum(bias_grad)


def up_back_kernel(
    act_ref,
    slope_ref,
    e_ref,
    stats_ref,
    up_ref,
    feed_ref,
    up_grad_ref,
    bias_grad_ref,
    total_ref,
    turned_ref,
    low_ref,
):
    @pl.when(pl.program_id(0) == 0)
    def _():
        total_ref[...] = jnp.zeros_like(total_ref)
        turned_ref[...] = feed_ref[...].T

    bias_grad_ref[0, 0:1] = up_back_step(
        act_ref.at[0],
        slope_ref.at[0],
        e_ref.at[0],
        stats_ref,
        up_ref.at[0],
        low_ref,
        total_ref,
    )
    up_grad_ref[0] = dot_nn(turned_ref[...], low_ref[...]).astype(BF)


def up_back(act, slope, e, stats, up, feed):
    rows, width = feed.shape
    steps = act.shape[0]
    block = pl.BlockSpec((1, rows, UNITS), lambda j: (j, 0, 0))
    narrow = whole((rows, 128))
    return pl.pallas_call(
        up_back_kernel,
        grid=(steps,),
        in_specs=[
            block,
            block,
            block,
            narrow,
            pl.BlockSpec((1, width, UNITS), lambda j: (j, 0, 0)),
            whole((rows, width)),
        ],
        out_specs=[
            pl.BlockSpec((1, width, UNITS), lambda j: (j, 0, 0)),
            pl.BlockSpec((1, 8, UNITS), lambda j: (j, 0, 0)),
            whole((rows, width)),
        ],
        out_shape=[
            jax.ShapeDtypeStruct((steps, width, UNITS), BF),
            jax.ShapeDtypeStruct((steps, 8, UNITS), F32),
            jax.ShapeDtypeStruct((rows, width), F32),
        ],
        scratch_shapes=[pltpu.VMEM((width, rows), BF), pltpu.VMEM((rows, UNITS), BF)],
        compiler_params=params(),
        name="up_back",
    )(act, slope, e, stats, up, feed)


def norms_back(grad_feed, cot_ref, middle_ref, branch_ref, vec_ref, sums_ref):
    normed, inv = row_norm(middle_ref[...])
    cot = cot_ref[...].astype(F32)
    grad_middle = cot + norm_back(grad_feed, vec_ref[7:8], normed, inv)
    sums_ref[7:8] += column_sum(grad_feed * normed)
    sums_ref[8:9] += column_sum(grad_feed)
    sums_ref[9:10] += column_sum(cot)
    normed, inv = row_norm(branch_ref[...])
    low = norm_back(grad_middle, vec_ref[5:6], normed, inv).astype(BF)
    sums_ref[5:6] += column_sum(grad_middle * normed)
    sums_ref[6:7] += column_sum(grad_middle)
    sums_ref[2:3] += column_sum(low.astype(F32))
    return grad_middle, low


def heads_back(low, weights, scale, attended):
    grad_out = (dot_nt(low, weights) * scale).astype(BF)
    product = grad_out.astype(F32) * attended
    high = product.astype(BF)
    rest = (product - high.astype(F32)).astype(BF)
    heads = (
        lax.broadcasted_iota(jnp.int32, (product.shape[1], 128), 0) // 64
        == lax.broadcasted_iota(jnp.int32, (product.shape[1], 128), 1)
    ).astype(BF)
    return grad_out, dot_nn(high, heads) + dot_nn(rest, heads)


def out_back_kernel(
    grad_feed_ref,
    cot_ref,
    middle_ref,
    branch_ref,
    scaled_ref,
    attended_ref,
    weight_ref,
    vec_ref,
    hs_ref,
    grad_middle_ref,
    ga_ref,
    out_grad_ref,
    delta_ref,
    sums_ref,
    total_ref,
):
    step = pl.program_id(0)

    @pl.when(step == 0)
    def _():
        total_ref[...] = jnp.zeros_like(total_ref)
        sums_ref[...] = jnp.zeros_like(sums_ref)

    grad_middle, low = norms_back(
        grad_feed_ref[...], cot_ref, middle_ref, branch_ref, vec_ref, sums_ref
    )
    grad_middle_ref[...] = grad_middle
    ga_ref[...], delta = heads_back(low, weight_ref[...], hs_ref[...], attended_ref[...])
    total_ref[...] += dot_tn(scaled_ref[...], low)
    delta_ref[...] = delta.T[: delta_ref.shape[0]]

    @pl.when(step == pl.num_programs(0) - 1)
    def _():
        out_grad_ref[...] = total_ref[...].astype(BF)


def out_back(
    grad_feed, cotangent, middle, branch, scaled, attended, weights, vectors, head_lanes
):
    rows, width = cotangent.shape
    heads = 2 * width // 128
    by_row = pl.BlockSpec((TILE, width), lambda i: (i, 0))
    return pl.pallas_call(
        out_back_kernel,
        grid=(rows // TILE,),
        in_specs=[
            by_row,
            by_row,
            by_row,
            by_row,
            by_row,
            by_row,
            whole((width, width)),
            whole(vectors.shape),
            whole((1, width)),
        ],
        out_specs=[
            by_row,
            by_row,
            whole((width, width)),
            pl.BlockSpec((heads, TILE), lambda i: (0, i)),
            whole((16, width)),
        ],
        out_shape=[
            jax.ShapeDtypeStruct((rows, width), F32),
            jax.ShapeDtypeStruct((rows, width), BF),
            jax.ShapeDtypeStruct((width, width), BF),
            jax.ShapeDtypeStruct((heads, rows), F32),
            jax.ShapeDtypeStruct((16, width), F32),
        ],
        scratch_shapes=[pltpu.VMEM((width, width), F32)],
        compiler_params=params(),
        name="out_back",
    )(
        grad_feed,
        cotangent,
        middle,
        branch,
        scaled,
        attended,
        weights,
        vectors,
        head_lanes,
    )


def attention_back_head(
    head, cross, q_ref, k_ref, v_ref, ga_ref, lse_ref, delta, dq_ref, dk_ref, dv_ref
):
    rows = q_ref.shape[0]
    half = rows // 2
    factor = LOG2E * 64 ** (-0.5)
    low_lanes = lax.broadcasted_iota(jnp.int32, (1, 128), 1) < 64
    mine = low_lanes if head == 0 else ~low_lanes
    above = lax.broadcasted_iota(jnp.int32, (TILE, TILE), 0) <= lax.broadcasted_iota(
        jnp.int32, (TILE, TILE), 1
    )
    zero = jnp.zeros((rows, 128), BF)
    query = jnp.where(mine, q_ref[...], zero)
    grad = jnp.where(mine, ga_ref[...], zero)
    key_own = jnp.where(mine, k_ref[...], zero)
    for start in range(0, rows, TILE):
        stop = start + TILE
        raw = dot_nt(k_ref[start:stop], query[start:])
        level = lse_ref[head : head + 1, start:]
        parts = [jnp.where(above, raw[:, :TILE] * factor - level[:, :TILE], MASKED)]
        if start < half:
            if stop < half:
                parts.append(raw[:, TILE : half - start] * factor - level[:, TILE : half - start])
            parts.append(raw[:, half - start :] * factor - (level[:, half - start :] - cross))
        elif stop < rows:
            parts.append(raw[:, TILE:] * factor - level[:, TILE:])
        exponent = parts[0] if len(parts) == 1 else jnp.concatenate(parts, axis=1)
        weights = jnp.exp2(exponent)
        grad_weights = dot_nt(v_ref[start:stop], grad[start:])
        grad_scores = (weights * (grad_weights - delta[:, start:])).astype(BF)
        dv = dot_nn(weights.astype(BF), grad[start:])
        dk = dot_nn(grad_scores, query[start:])
        dq = dot_tn(grad_scores, key_own[start:stop])
        if head == 0:
            dv_ref[start:stop] = dv
            dk_ref[start:stop] = dk
        else:
            dv_ref[start:stop] += dv
            dk_ref[start:stop] += dk
        if head == 0 and start == 0:
            dq_ref[...] = dq
        else:
            dq_ref[start:] += dq


def in_back_pair(dq_ref, dk_ref, dv_ref, weights, turned_ref, out_grad_ref, chunk_ref, total_ref):
    factor = 64 ** (-0.5)
    dq = (dq_ref[...] * factor).astype(BF)
    dk = (dk_ref[...] * factor).astype(BF)
    dv = dv_ref[...].astype(BF)
    grads = jnp.concatenate([dq, dk, dv], axis=1)
    shares = dot_nn(turned_ref[...], grads).astype(BF)
    for start in range(0, total_ref.shape[0], TILE):
        part = jnp.concatenate(
            [shares[start : start + TILE], out_grad_ref[start : start + TILE]], axis=1
        )
        chunk_ref[:, start // TILE] = part.reshape(8, 32, 512)
        columns = slice(start, start + TILE)
        total_ref[:, columns] += dot_nt(grads, weights[columns])
    return column_sum(dq.astype(F32)), column_sum(dv.astype(F32))


def tokens_back(tokens, grad, grad_middle, gain):
    normed, inv = row_norm(tokens.astype(F32))
    back = norm_back(grad, gain, normed, inv)
    return (grad_middle + back).astype(BF), column_sum(grad * normed), column_sum(grad)


def in_back_kernel(
    lengths_ref,
    proj_ref,
    ga_ref,
    lse_ref,
    delta_ref,
    wq_ref,
    wk_ref,
    wv_ref,
    first_ref,
    out_grad_ref,
    tokens_ref,
    gain_ref,
    grad_middle_ref,
    chunk_ref,
    bias_ref,
    tokens_grad_ref,
    sums_ref,
    dq_ref,
    dk_ref,
    dv_ref,
    turned_ref,
    total_ref,
):
    step = pl.program_id(0)
    q_ref, k_ref, v_ref = three(proj_ref)
    rows_all = tokens_ref.shape[0]

    @pl.when(step == 0)
    def _():
        turned_ref[...] = first_ref[...].T
        total_ref[...] = jnp.zeros_like(total_ref)

    for head in range(2):
        attention_back_head(
            head,
            cross_flag(lengths_ref, tokens_ref),
            q_ref,
            k_ref,
            v_ref,
            ga_ref,
            lse_ref.at[0],
            delta_ref[0, head : head + 1],
            dq_ref,
            dk_ref,
            dv_ref,
        )
    weights = jnp.concatenate([wq_ref[...], wk_ref[...], wv_ref[...]], axis=1)
    query_sum, value_sum = in_back_pair(
        dq_ref, dk_ref, dv_ref, weights, turned_ref, out_grad_ref, chunk_ref.at[0], total_ref
    )
    bias_ref[0, 0:1] = query_sum
    bias_ref[0, 1:2] = value_sum

    @pl.when(step == pl.num_programs(0) - 1)
    def _():
        gain_grad = jnp.zeros((1, total_ref.shape[1]), F32)
        shift_grad = jnp.zeros((1, total_ref.shape[1]), F32)
        for start in range(0, rows_all, TILE):
            rows = pl.ds(start, TILE)
            tokens_grad_ref[rows], gain_part, shift_part = tokens_back(
                tokens_ref[rows], total_ref[rows], grad_middle_ref[rows], gain_ref[...]
            )
            gain_grad = gain_grad + gain_part
            shift_grad = shift_grad + shift_part
        sums_ref[0:1] = gain_grad
        sums_ref[1:2] = shift_grad


def in_back(lengths, projected, ga, lse, delta, weights, first, out_grad, tokens, gain, grad_middle):
    rows, width = tokens.shape
    pairs = width // 128
    column = pl.BlockSpec((rows, 128), lambda p: (0, p))
    square = whole((rows, width))
    return pl.pallas_call(
        in_back_kernel,
        grid=(pairs,),
        in_specs=[
            pl.BlockSpec(memory_space=pltpu.SMEM),
            pl.BlockSpec((1, rows, 384), lambda p: (p, 0, 0)),
            column,
            pl.BlockSpec((1, 8, rows), lambda p: (p, 0, 0)),
            pl.BlockSpec((1, 2, rows), lambda p: (p, 0, 0)),
            pl.BlockSpec((width, 128), lambda p: (0, p)),
            pl.BlockSpec((width, 128), lambda p: (0, pairs + p)),
            pl.BlockSpec((width, 128), lambda p: (0, 2 * pairs + p)),
            square,
            column,
            square,
            whole((1, width)),
            square,
        ],
        out_specs=[
            pl.BlockSpec((1, 8, width // TILE, 32, 512), lambda p: (p, 0, 0, 0, 0)),
            pl.BlockSpec((1, 8, 128), lambda p: (p, 0, 0)),
            square,
            whole((8, width)),
        ],
        out_shape=[
            jax.ShapeDtypeStruct((pairs, 8, width // TILE, 32, 512), BF),
            jax.ShapeDtypeStruct((pairs, 8, 128), F32),
            jax.ShapeDtypeStruct((rows, width), BF),
            jax.ShapeDtypeStruct((8, width), F32),
        ],
        scratch_shapes=[
            pltpu.VMEM((rows, 128), F32),
            pltpu.VMEM((rows, 128), F32),
            pltpu.VMEM((rows, 128), F32),
            pltpu.VMEM((width, rows), BF),
            pltpu.VMEM((rows, width), F32),
        ],
        compiler_params=params(),
        name="in_back",
    )(
        lengths,
        projected,
        ga,
        lse,
        delta,
        weights,
        weights,
        weights,
        first,
        out_grad,
        tokens,
        gain,
        grad_middle,
    )


class Place:
    def __init__(self):
        self.z = lax.axis_index("dp")
        wide = lax.axis_index("wide")
        self.y = wide // 4
        self.x = (wide // 2) % 2
        self.c = wide % 2
        self.core = (self.z, wide + 1 - 2 * self.c)
        self.side = (self.z, wide + 2 - 4 * self.x)
        self.over = (self.z, wide + 4 - 8 * self.y)
        self.ranks = (self.z + 1 - 2 * (self.z % 2), (self.z + 2) % 4, 3 - self.z)
        self.planes = tuple((rank, wide) for rank in self.ranks)

    def greet(self, planes=True):
        barrier = pltpu.get_barrier_semaphore()
        peers = (self.core, self.side, self.over) + (self.planes if planes else ())
        for peer in peers:
            pl.semaphore_signal(barrier, inc=1, device_id=peer, device_id_type=MESH)
        pl.semaphore_wait(barrier, len(peers))


class WideGather:
    copies = 10

    def __init__(
        self, place, view, count, send, recv, first, source=None, last=None, offset=0, total=None
    ):
        y, x, c = place.y, place.x, place.c
        here, side, over, far = (y, x, c), (y, 1 - x, c), (1 - y, x, c), (1 - y, 1 - x, c)
        upper, lower = pl.ds(offset, count // 2), pl.ds(offset + count // 2, count // 2)
        both = pl.ds(offset, count)
        everything = both if total is None else pl.ds(0, total)

        def copy(index, slot, part, peer):
            destination = view(*slot, part)
            return pltpu.make_async_remote_copy(
                src_ref=source.at[part] if source is not None and slot is here else destination,
                dst_ref=destination,
                send_sem=send.at[first + index],
                recv_sem=recv.at[first + index],
                device_id=peer,
                device_id_type=MESH,
            )

        self.all = (
            copy(0, here, upper, place.side),
            copy(1, here, lower, place.over),
            copy(2, here, upper, place.over),
            copy(3, here, lower, place.side),
            None if total == 0 else copy(4, here, everything, place.core),
            copy(5, side, upper, place.over),
            copy(6, over, lower, place.side),
            copy(7, side, both, place.core),
            copy(8, over, both, place.core),
            copy(9, far, both, place.core),
        )
        self.own = None
        if source is not None and last is not None:
            self.own = pltpu.make_async_copy(source, view(*here, everything), last)

    def start(self):
        if self.own is not None:
            self.own.start()
        for copy in self.all[:5]:
            if copy is not None:
                copy.start()

    def relay(self, stage):
        waits, starts = (((0, 1), (5, 6)), ((2, 3), (7, 8)), ((5, 6), (9,)))[stage]
        for index in waits:
            self.all[index].wait_recv()
        for index in starts:
            self.all[index].start()

    def finish(self):
        for index in (4, 7, 8, 9):
            if self.all[index] is not None:
                self.all[index].wait_recv()
        for copy in self.all:
            if copy is not None:
                copy.wait_send()
        if self.own is not None:
            self.own.wait()


def blocks_of(target):
    return lambda y, x, c, rows: target.at[y, x, c, rows]


LAG = 2


class Reduction:
    slots = 2 * LAG
    deep = 3 * LAG
    keep = 3 * LAG + 2

    @classmethod
    def scratch(cls):
        n, k = cls.slots, cls.keep
        return [
            pltpu.VMEM((cls.deep, 2, 2, 4, 32, 512), BF),
            pltpu.VMEM((n, 2, 2, 4, 32, 512), BF),
            pltpu.VMEM((n, 2, 2, 4, 16, 512), BF),
            pltpu.VMEM((n, 2, 4, 16, 512), BF),
            pltpu.VMEM((n, 4, 32, 512), BF),
            pltpu.VMEM((n, 3, 32, 512), BF),
            pltpu.VMEM((n, 32, 512), BF),
            pltpu.VMEM((k, 3, 32, 512), BF),
            pltpu.SemaphoreType.DMA((6, k)),
            pltpu.SemaphoreType.DMA((6, k)),
            pltpu.SemaphoreType.DMA((cls.deep,)),
        ]

    def __init__(self, place, refs):
        self.place = place
        (
            self.chip,
            self.partner,
            self.first,
            self.second,
            self.plane,
            self.from_z,
            self.sums,
            self.shared,
            self.send,
            self.recv,
            self.local,
        ) = refs

    def copy(self, index, slot, source, target, peer):
        return pltpu.make_async_remote_copy(
            src_ref=source,
            dst_ref=target,
            send_sem=self.send.at[index, slot],
            recv_sem=self.recv.at[index, slot],
            device_id=peer,
            device_id_type=MESH,
        )

    def wait(self, index, slot, arrived):
        self.copy(index, slot, arrived, arrived, self.place.core).wait()

    def load(self, chunk, source):
        slot = chunk % self.deep
        return pltpu.make_async_copy(source, self.chip.at[slot], self.local.at[slot])

    def stage0(self, chunk, view):
        slot, c = chunk % self.slots, self.place.c
        self.copy(
            0, slot, view.at[:, :, 1 - c], self.partner.at[slot], self.place.core
        ).start()
        self.load(chunk, view.at[:, :, c]).start()

    def stage1(self, chunk):
        p, slot, index = self.place, chunk % self.slots, chunk % self.deep
        partner, chip, target = self.partner.at[slot], self.chip.at[index], self.first.at[slot]
        self.load(chunk, partner).wait()
        self.wait(0, slot, partner)
        chip[...] += partner[...]
        self.copy(1, slot, chip.at[:, 1 - p.x, :, pl.ds(0, 16)], target.at[0], p.side).start()
        self.copy(1, slot, chip.at[1 - p.y, :, :, pl.ds(16, 16)], target.at[1], p.over).start()

    def stage2(self, chunk):
        p, slot, index = self.place, chunk % self.slots, chunk % self.deep
        chip, arrived, target = self.chip.at[index], self.first.at[slot], self.second.at[slot]
        self.wait(1, slot, arrived)
        for k in range(2):
            chip[k, p.x, :, 0:16] += arrived[0, k]
            chip[p.y, k, :, 16:32] += arrived[1, k]
        self.copy(2, slot, chip.at[1 - p.y, p.x, :, pl.ds(0, 16)], target.at[0], p.over).start()
        self.copy(2, slot, chip.at[p.y, 1 - p.x, :, pl.ds(16, 16)], target.at[1], p.side).start()

    def stage3(self, chunk):
        p, slot, index = self.place, chunk % self.slots, chunk % self.deep
        arrived, mine, plane = self.second.at[slot], self.chip.at[index, p.y, p.x], self.plane
        self.wait(2, slot, arrived)
        plane[slot, :, 0:16] = mine[:, 0:16] + arrived[0]
        plane[slot, :, 16:32] = mine[:, 16:32] + arrived[1]
        for k in range(3):
            target = self.from_z.at[slot, k]
            self.copy(3, slot, plane.at[slot, p.ranks[k]], target, p.planes[k]).start()

    def stage4(self, chunk):
        slot = chunk % self.slots
        self.wait(3, slot, self.from_z.at[slot])
        total = self.plane[slot, self.place.z].astype(F32)
        for k in range(3):
            total = total + self.from_z[slot, k].astype(F32)
        return total

    def spread(self, chunk, total):
        slot, place = chunk % self.slots, chunk % self.keep
        self.sums[slot] = total.astype(BF)
        peer = self.place.planes[1]
        self.copy(4, place, self.sums.at[slot], self.shared.at[place, 0], peer).start()

    def stage5(self, chunk):
        slot, place, peer = chunk % self.slots, chunk % self.keep, self.place.planes[0]
        shared = self.shared.at[place]
        self.wait(4, place, shared.at[0])
        self.copy(5, place, self.sums.at[slot], shared.at[1], peer).start()
        self.copy(5, place, shared.at[0], shared.at[2], peer).start()

    def stage6(self, chunk):
        slot, place, ranks = chunk % self.slots, chunk % self.keep, self.place.ranks
        self.wait(5, place, self.shared.at[place, pl.ds(1, 2)])
        return [
            (self.place.z, self.sums[slot]),
            (ranks[1], self.shared[place, 0]),
            (ranks[0], self.shared[place, 1]),
            (ranks[2], self.shared[place, 2]),
        ]


class SmallReduction:
    @staticmethod
    def scratch():
        return [
            pltpu.VMEM((2, 2, 2, 4, 16, 512), BF),
            pltpu.VMEM((2, 2, 4, 16, 512), BF),
            pltpu.VMEM((2, 2, 4, 16, 512), BF),
            pltpu.VMEM((2, 4, 16, 512), BF),
            pltpu.VMEM((4, 16, 512), BF),
            pltpu.VMEM((3, 16, 512), BF),
            pltpu.SemaphoreType.DMA((4,)),
            pltpu.SemaphoreType.DMA((4,)),
        ]

    def __init__(self, place, refs):
        self.place = place
        self.source, self.chip, self.partner, self.first, self.second, self.from_z = refs[:6]
        self.send, self.recv = refs[6:]

    def copy(self, index, source, target, peer):
        return pltpu.make_async_remote_copy(
            src_ref=source,
            dst_ref=target,
            send_sem=self.send.at[index],
            recv_sem=self.recv.at[index],
            device_id=peer,
            device_id_type=MESH,
        )

    def wait(self, index, arrived):
        self.copy(index, arrived, arrived, self.place.core).wait()

    def stage0(self):
        p = self.place
        self.copy(0, self.source.at[:, :, 1 - p.c], self.partner, p.core).start()

    def stage1(self):
        p = self.place
        self.wait(0, self.partner)
        self.chip[...] = self.source[:, :, p.c] + self.partner[...]
        self.copy(1, self.chip.at[:, 1 - p.x], self.first, p.side).start()

    def stage2(self):
        p = self.place
        self.wait(1, self.first)
        for k in range(2):
            self.chip[k, p.x] += self.first[k]
        self.copy(2, self.chip.at[1 - p.y, p.x], self.second, p.over).start()

    def stage3(self):
        p = self.place
        self.wait(2, self.second)
        self.chip[p.y, p.x] += self.second[...]
        for k in range(3):
            block = self.chip.at[p.y, p.x, p.ranks[k]]
            self.copy(3, block, self.from_z.at[k], p.planes[k]).start()

    def stage4(self):
        p = self.place
        self.wait(3, self.from_z)
        total = self.chip[p.y, p.x, p.z].astype(F32)
        for k in range(3):
            total = total + self.from_z[k].astype(F32)
        return total


class Stream:
    def __init__(self, view, buffers, sems):
        self.view, self.buffers, self.sems = view, buffers, sems

    def copy(self, index):
        slot = index % 2
        return pltpu.make_async_copy(self.view(index), self.buffers.at[slot], self.sems.at[slot])

    def start(self, index):
        self.copy(index).start()

    def block(self, index):
        return self.buffers.at[index % 2]


def advance(streams, index, count):
    @pl.when(index + 1 < count)
    def _():
        for stream in streams:
            stream.start(index + 1)

    for stream in streams:
        stream.copy(index).wait()


def nearness(i):
    over = (i == 3) | (i >= 5)
    side = (i == 2) | (i == 4) | (i >= 6)
    other = (i == 1) | (i == 4) | (i == 5) | (i == 7)
    return over, side, other


def unit_index(i):
    wide = lax.axis_index("wide")
    y, x, c = wide // 4, wide // 2 % 2, wide % 2
    over, side, other = nearness(i)
    y, x, c = (jnp.where(flip, 1 - k, k) for flip, k in zip((over, side, other), (y, x, c)))
    return 4 * y + 2 * x + c


class NearGather:
    copies = 3

    def __init__(self, place, source, target, send, recv, first, last):
        slot = target.at[place.y, place.x, place.c]
        self.all = [
            pltpu.make_async_remote_copy(
                src_ref=source,
                dst_ref=slot,
                send_sem=send.at[first + index],
                recv_sem=recv.at[first + index],
                device_id=peer,
                device_id_type=MESH,
            )
            for index, peer in enumerate((place.side, place.over, place.core))
        ]
        self.own = pltpu.make_async_copy(source, slot, last)

    def start(self):
        self.own.start()
        for copy in self.all:
            copy.start()

    def finish(self):
        self.own.wait()
        for copy in self.all:
            copy.wait()


class LateGather:
    copies = 5

    def __init__(self, place, near, late, send, recv, first):
        rows = near.shape[-2]
        upper, lower = pl.ds(0, rows // 2), pl.ds(rows // 2, rows // 2)
        side, over = near.at[place.y, 1 - place.x, place.c], near.at[1 - place.y, place.x, place.c]

        def copy(index, source, target, peer):
            return pltpu.make_async_remote_copy(
                src_ref=source,
                dst_ref=target,
                send_sem=send.at[first + index],
                recv_sem=recv.at[first + index],
                device_id=peer,
                device_id_type=MESH,
            )

        self.all = (
            copy(0, side.at[upper], late.at[2, upper], place.over),
            copy(1, over.at[lower], late.at[2, lower], place.side),
            copy(2, side, late.at[0], place.core),
            copy(3, over, late.at[1], place.core),
            copy(4, late.at[2], late.at[3], place.core),
        )

    def start(self):
        for copy in self.all[:4]:
            copy.start()

    def relay(self):
        for copy in self.all[:2]:
            copy.wait_recv()
        self.all[4].start()

    def arrived(self, *indices):
        for index in indices:
            self.all[index].wait_recv()

    def finish(self):
        for copy in self.all:
            copy.wait_send()


class WeightStream(Stream):
    def __init__(self, near, late, buffers, sems):
        super().__init__(lambda i: late.at[0], buffers, sems)
        self.near, self.late = near, late

    def start(self, index):
        slot = index % 2
        target, sem = self.buffers.at[slot], self.sems.at[slot]

        @pl.when(index < 4)
        def _():
            block = unit_index(index)
            view = self.near.at[block // 4, block // 2 % 2, block % 2]
            pltpu.make_async_copy(view, target, sem).start()

        @pl.when(index >= 4)
        def _():
            pltpu.make_async_copy(self.late.at[index - 4], target, sem).start()


def dma_sems(count):
    return [pltpu.SemaphoreType.DMA((count,)), pltpu.SemaphoreType.DMA((count,))]


def to_planes(place, mine, landing, send, recv, first):
    return [
        pltpu.make_async_remote_copy(
            src_ref=mine,
            dst_ref=landing(k),
            send_sem=send.at[first + k],
            recv_sem=recv.at[first + k],
            device_id=place.planes[k],
            device_id_type=MESH,
        )
        for k in range(3)
    ]


class PlanesLast:
    copies = WideGather.copies + 6

    def __init__(self, place, source, target, send, recv, last):
        view = blocks_of(target.at[place.z])
        self.wide = WideGather(place, view, source.shape[0], send, recv, 0, source, last)

        def copy(index, rank, peer):
            blocks = target.at[rank, :, :, place.c]
            return pltpu.make_async_remote_copy(
                src_ref=blocks,
                dst_ref=blocks,
                send_sem=send.at[WideGather.copies + index],
                recv_sem=recv.at[WideGather.copies + index],
                device_id=peer,
                device_id_type=MESH,
            )

        self.across = [copy(k, place.z, place.planes[k]) for k in range(3)]
        self.over = [copy(3 + k, place.ranks[k], place.core) for k in range(3)]

    def start_across(self):
        self.wide.own.wait()
        for copy in self.across:
            copy.start()

    def start_over(self):
        for arrived, copy in zip(self.across, self.over):
            arrived.wait_recv()
            copy.start()

    def finish(self):
        self.wide.own = None
        self.wide.finish()
        for copy in self.across:
            copy.wait_send()
        for copy in self.over:
            copy.wait()


def first_kernel(
    lengths_ref,
    tokens_ref,
    in_ref,
    vec_ref,
    out_ref,
    up_ref,
    unit_ref,
    hs_ref,
    turned_ref,
    proj_ref,
    scaled_ref,
    scaled_turned_ref,
    attended_ref,
    lse_ref,
    vectors_ref,
    scale_ref,
    in_all,
    out_all,
    up_all,
    unit_all,
    held_ref,
    normed_ref,
    first_ref,
    vext_ref,
    send_in,
    recv_in,
    send_out,
    recv_out,
    send_ff,
    recv_ff,
    local,
):
    step = pl.program_id(0)
    place = Place()
    width = tokens_ref.shape[1]
    count = WideGather.copies
    lanes = (3 * width // 2 + 128, 3 * width // 2)
    across, early, late = [], [], None
    for group in range(2):
        held = held_ref.at[group, :, :, :, :, :, pl.ds(0, lanes[group])]
        first = group * (3 + 2 * count)

        def blocks(planes, held=held):
            return lambda y, x, c, rows: held.at[planes, y, x, c, rows]

        mine = held.at[0, place.y, place.x, place.c]
        across.append(
            to_planes(
                place,
                mine,
                lambda k, held=held: held.at[k + 1, place.y, place.x, place.c],
                send_in,
                recv_in,
                first,
            )
        )
        if group == 0:
            for part, planes in enumerate((pl.ds(0, 1), pl.ds(1, 3))):
                start = first + 3 + part * count
                early.append(WideGather(place, blocks(planes), 32, send_in, recv_in, start))
        else:
            late = WideGather(place, blocks(pl.ds(0, 4)), 32, send_in, recv_in, first + 3)
    orders = (place.z, *place.ranks)
    out = PlanesLast(place, out_ref, out_all, send_out, recv_out, local.at[2])
    up = NearGather(place, up_ref, up_all, send_ff, recv_ff, count, local.at[3])
    unit = WideGather(
        place, blocks_of(unit_all), 32, send_ff, recv_ff, 0, unit_ref, local.at[4]
    )
    keep = [
        pltpu.make_async_copy(
            held_ref.at[group, index, :, :, :, :, pl.ds(0, lanes[1])],
            in_all.at[rank, :, :, :, :, pl.ds(group * lanes[1], lanes[1])],
            local.at[12 + 4 * group + index],
        )
        for group in range(2)
        for index, rank in enumerate(orders)
    ]

    @pl.when(step == 0)
    def _():
        place.greet()
        half = width // 2
        for group in range(2):
            mine = held_ref.at[group, 0, place.y, place.x, place.c]
            fills = []
            for pair in range(4):
                for part in range(3):
                    column = part * width + (4 * group + pair) * 128
                    fills.append(
                        pltpu.make_async_copy(
                            in_ref.at[:, pl.ds(column, 128)],
                            mine.at[:, pl.ds(pair * 384 + part * 128, 128)],
                            local.at[20 + group * 12 + pair * 3 + part],
                        )
                    )
            for copy in fills:
                copy.start()
            if group == 0:
                mine[:, 3 * half : 3 * half + 128] = jnp.zeros((32, 128), BF)
                mine[:, 3 * half : 3 * half + 32] = vec_ref[...]
            for copy in fills:
                copy.wait()
            for copy in across[group]:
                copy.start()
            if group == 0:
                early[0].start()
        out.wide.start()
        scale = hs_ref[...].astype(F32)
        for pair in range(width // 128):
            own = slice(pair * 128, (pair + 1) * 128)
            low_lanes = lax.broadcasted_iota(jnp.int32, (1, 128), 1) < 64
            scale_ref[0:1, own] = jnp.where(
                low_lanes, scale[:, 2 * pair : 2 * pair + 1], scale[:, 2 * pair + 1 : 2 * pair + 2]
            )
        for start in range(0, tokens_ref.shape[0], TILE):
            rows = pl.ds(start, TILE)
            normed, _ = row_norm(tokens_ref[rows].astype(F32))
            normed_ref[rows] = normed
        early[0].relay(0)
        for copy in across[0]:
            copy.wait_recv()
        early[1].start()
        early[0].relay(1)
        early[0].relay(2)
        early[1].relay(0)
        out.wide.relay(0)
        early[1].relay(1)
        out.wide.relay(1)
        for copy in across[1]:
            copy.wait_recv()
        late.start()
        early[1].relay(2)
        out.wide.relay(2)
        out.start_across()
        unit.start()
        for part in early:
            part.finish()
        for z in range(4):
            for y in range(2):
                tile = jnp.zeros((16, 128), F32)
                for x in range(2):
                    for c in range(2):
                        piece = held_ref[
                            0, orders[z], y, x, c, 0:16, 3 * half : 3 * half + 128
                        ].astype(F32)
                        spot = 32 * (2 * x + c)
                        tile = tile + (piece if spot == 0 else pltpu.roll(piece, spot, 1))
                vectors_ref[:, (2 * z + y) * 128 : (2 * z + y + 1) * 128] = tile
        for start in range(0, tokens_ref.shape[0], TILE):
            rows = pl.ds(start, TILE)
            first_ref[rows] = (normed_ref[rows] * vectors_ref[3:4] + vectors_ref[4:5]).astype(BF)

    @pl.when((step >= 2) & (step <= 4))
    def _():
        for stage in range(3):

            @pl.when(step == 2 + stage)
            def _():
                late.relay(stage)
                unit.relay(stage)

    @pl.when(step == 2)
    def _():
        up.start()

    @pl.when(step == 5)
    def _():
        late.finish()
        for copy in keep:
            copy.start()

    @pl.when(step == 7)
    def _():
        out.start_over()

    @pl.when(step > 0)
    def _():
        pair = step - 1
        columns = pl.ds(pl.multiple_of(pair % 4 * 384, 128), 384)
        weights = jnp.concatenate(
            [held_ref[pair // 4, order, :, :, :, :, columns].reshape(TILE, 384) for order in orders]
        )
        own = pl.ds(pl.multiple_of(pair * 128, 128), 128)
        bias = jnp.concatenate(
            [vectors_ref[0:1, own], jnp.zeros((1, 128), F32), vectors_ref[1:2, own]], axis=1
        )
        project_pair(first_ref, weights, bias, proj_ref)
        attention_pair(
            cross_flag(lengths_ref, tokens_ref),
            *three(proj_ref),
            scale_ref[0:1, own],
            scaled_ref,
            attended_ref,
            lse_ref,
            vext_ref,
        )
        scaled_turned_ref[...] = scaled_ref[...].T

    @pl.when(step == pl.num_programs(0) - 1)
    def _():
        turned_ref[...] = first_ref[...].T
        for copy in (*across[0], *across[1]):
            copy.wait_send()
        for copy in keep:
            copy.wait()
        out.finish()
        unit.finish()
        up.finish()


def first_part(lengths, tokens, in_weight, vec, out_weight, up_weight, unit_rows, head_scale):
    rows, width = tokens.shape
    pairs = width // 128

    def at(step):
        return jnp.maximum(step - 1, 0)

    column = pl.BlockSpec((rows, 128), lambda s: (0, at(s)))
    held = (2, 4, 2, 2, 2, 32, 3 * width // 2 + 128)
    return pl.pallas_call(
        first_kernel,
        grid=(pairs + 1,),
        in_specs=[
            pl.BlockSpec(memory_space=pltpu.SMEM),
            whole((rows, width)),
            ANY,
            whole(vec.shape),
            ANY,
            ANY,
            ANY,
            whole(head_scale.shape),
        ],
        out_specs=[
            whole((width, rows)),
            pl.BlockSpec((1, rows, 384), lambda s: (at(s), 0, 0)),
            column,
            pl.BlockSpec((128, rows), lambda s: (at(s), 0)),
            column,
            pl.BlockSpec((1, 8, rows), lambda s: (at(s), 0, 0)),
            whole((16, width)),
            whole((8, width)),
            ANY,
            ANY,
            ANY,
            ANY,
        ],
        out_shape=[
            jax.ShapeDtypeStruct((width, rows), BF),
            jax.ShapeDtypeStruct((pairs, rows, 384), BF),
            jax.ShapeDtypeStruct((rows, width), BF),
            jax.ShapeDtypeStruct((width, rows), BF),
            jax.ShapeDtypeStruct((rows, width), F32),
            jax.ShapeDtypeStruct((pairs, 8, rows), F32),
            jax.ShapeDtypeStruct((16, width), F32),
            jax.ShapeDtypeStruct((8, width), F32),
            jax.ShapeDtypeStruct((4, 2, 2, 2, 32, 3 * width), BF),
            jax.ShapeDtypeStruct((4, 2, 2, 2, *out_weight.shape), BF),
            jax.ShapeDtypeStruct((2, 2, 2, *up_weight.shape), BF),
            jax.ShapeDtypeStruct((2, 2, 2, *unit_rows.shape), BF),
        ],
        scratch_shapes=[
            pltpu.VMEM(held, BF),
            pltpu.VMEM((rows, width), F32),
            pltpu.VMEM((rows, width), BF),
            pltpu.VMEM((rows, 256), BF),
            *dma_sems(6 + 3 * WideGather.copies),
            *dma_sems(PlanesLast.copies),
            *dma_sems(WideGather.copies + NearGather.copies),
            pltpu.SemaphoreType.DMA((44,)),
        ],
        compiler_params=params(collective_id=0, has_side_effects=True),
        name="first_part",
    )(lengths, tokens, in_weight, vec, out_weight, up_weight, unit_rows, head_scale)


def second_kernel(
    units,
    scaled_ref,
    weight_ref,
    vec_ref,
    tokens_ref,
    unit_ref,
    up_near,
    down_ref,
    branch_ref,
    middle_ref,
    turned_ref,
    act_ref,
    slope_ref,
    stats_ref,
    up_late,
    down_near,
    feed_ref,
    sums_ref,
    up_ref,
    send,
    recv,
    local,
    stream_sems,
):
    step = pl.program_id(0)
    lead = feed_ref.shape[0] // TILE
    place = Place()
    late = LateGather(place, up_near, up_late, send, recv, 0)
    down = NearGather(place, down_ref, down_near, send, recv, LateGather.copies, local.at[0])
    up = WeightStream(up_near, up_late, up_ref, stream_sems)

    @pl.when(step == 0)
    def _():
        place.greet(planes=False)
        late.start()
        up.start(0)
        sums_ref[...] = jnp.zeros_like(sums_ref)

    @pl.when(step == 2)
    def _():
        down.start()

    @pl.when(step < lead)
    def _():
        rows = pl.ds(pl.multiple_of(step * TILE, TILE), TILE)
        feed_ref[rows] = out_proj_rows(
            scaled_ref, weight_ref, vec_ref, tokens_ref, branch_ref, middle_ref
        )

    @pl.when(step >= lead)
    def _():
        block = step - lead

        @pl.when(block == 2)
        def _():
            late.relay()

        @pl.when(block == 3)
        def _():
            late.arrived(2, 3)

        @pl.when(block == 6)
        def _():
            late.arrived(4)

        advance((up,), block, 8)
        up_step(feed_ref, up.block(block), unit_ref.at[0], act_ref, slope_ref, sums_ref)

    @pl.when(step == pl.num_programs(0) - 1)
    def _():
        up_stats(units, stats_ref, sums_ref)
        turned_ref[...] = feed_ref[...].T
        late.finish()
        down.finish()


def second_part(scaled, out_weights, vectors, tokens, up_near, unit_vec, down_weight):
    rows, width = tokens.shape
    steps = 8
    lead = rows // TILE

    def early(step):
        return jnp.minimum(step, lead - 1)

    def unit(step):
        return unit_index(jnp.maximum(step - lead, 0))

    by_row = pl.BlockSpec((TILE, width), lambda s: (early(s), 0))
    block = pl.BlockSpec((1, rows, UNITS), lambda s: (unit(s), 0, 0))
    return pl.pallas_call(
        functools.partial(second_kernel, steps * UNITS),
        grid=(lead + steps,),
        in_specs=[
            by_row,
            whole((width, width)),
            whole(vectors.shape),
            by_row,
            pl.BlockSpec((1, unit_vec.shape[1], UNITS), lambda s: (unit(s), 0, 0)),
            ANY,
            ANY,
        ],
        out_specs=[
            by_row,
            by_row,
            whole((width, rows)),
            block,
            block,
            whole((rows, 128)),
            ANY,
            ANY,
        ],
        out_shape=[
            jax.ShapeDtypeStruct((rows, width), F32),
            jax.ShapeDtypeStruct((rows, width), F32),
            jax.ShapeDtypeStruct((width, rows), BF),
            jax.ShapeDtypeStruct((steps, rows, UNITS), BF),
            jax.ShapeDtypeStruct((steps, rows, UNITS), BF),
            jax.ShapeDtypeStruct((rows, 128), F32),
            jax.ShapeDtypeStruct((4, *up_near.shape[3:]), BF),
            jax.ShapeDtypeStruct((2, 2, 2, *down_weight.shape), BF),
        ],
        scratch_shapes=[
            pltpu.VMEM((rows, width), BF),
            pltpu.VMEM((2, rows, 128), F32),
            pltpu.VMEM((2, *up_near.shape[3:]), BF),
            *dma_sems(LateGather.copies + NearGather.copies),
            pltpu.SemaphoreType.DMA((1,)),
            pltpu.SemaphoreType.DMA((2,)),
        ],
        compiler_params=params(collective_id=2, has_side_effects=True),
        name="second_part",
    )(scaled, out_weights, vectors, tokens, unit_vec, up_near, down_weight)


def third_kernel(
    units,
    act_ref,
    stats_ref,
    vec_ref,
    cot_ref,
    middle_ref,
    shift_ref,
    down_near,
    mixed_ref,
    down_grad_ref,
    e_ref,
    all_stats_ref,
    vec_grad_ref,
    down_late,
    total_ref,
    sums_ref,
    low_ref,
    down_ref,
    send,
    recv,
    stream_sems,
):
    step = pl.program_id(0)
    place = Place()
    late = LateGather(place, down_near, down_late, send, recv, 0)
    down = WeightStream(down_near, down_late, down_ref, stream_sems)

    @pl.when(step == 0)
    def _():
        place.greet(planes=False)
        late.start()
        down.start(0)
        total_ref[...] = jnp.zeros_like(total_ref)
        sums_ref[...] = jnp.zeros_like(sums_ref)

    @pl.when(step == 3)
    def _():
        late.relay()
        late.arrived(2, 3)

    @pl.when(step == 6)
    def _():
        late.arrived(4)

    advance((down,), step, 8)
    down_step(
        act_ref, stats_ref, vec_ref.at[0], down.block(step), cot_ref, down_grad_ref, e_ref,
        vec_grad_ref, total_ref, sums_ref, low_ref
    )

    @pl.when(step == pl.num_programs(0) - 1)
    def _():
        down_end(
            units, stats_ref, middle_ref, shift_ref, mixed_ref, all_stats_ref, total_ref, sums_ref
        )
        late.finish()


def third_part(act, stats, vec, down_near, cotangent, middle, shift):
    rows, width = cotangent.shape
    steps = 8

    def unit(shape):
        return pl.BlockSpec((1, *shape), lambda s: (unit_index(s), 0, 0))

    block = unit((rows, UNITS))
    return pl.pallas_call(
        functools.partial(third_kernel, steps * UNITS),
        grid=(steps,),
        in_specs=[
            block,
            whole((rows, 128)),
            unit((vec.shape[1], UNITS)),
            whole((rows, width)),
            whole((rows, width)),
            whole((1, width)),
            ANY,
        ],
        out_specs=[
            whole((rows, width)),
            unit((UNITS, width)),
            block,
            whole((rows, 128)),
            unit((8, UNITS)),
            ANY,
        ],
        out_shape=[
            jax.ShapeDtypeStruct((rows, width), BF),
            jax.ShapeDtypeStruct((steps, UNITS, width), BF),
            jax.ShapeDtypeStruct((steps, rows, UNITS), BF),
            jax.ShapeDtypeStruct((rows, 128), F32),
            jax.ShapeDtypeStruct((steps, 8, UNITS), F32),
            jax.ShapeDtypeStruct((4, *down_near.shape[3:]), BF),
        ],
        scratch_shapes=[
            pltpu.VMEM((rows, width), F32),
            pltpu.VMEM((2, rows, 128), F32),
            pltpu.VMEM((rows, UNITS), BF),
            pltpu.VMEM((2, *down_near.shape[3:]), BF),
            *dma_sems(LateGather.copies),
            pltpu.SemaphoreType.DMA((2,)),
        ],
        compiler_params=params(collective_id=3, has_side_effects=True),
        name="third_part",
    )(act, stats, vec, cotangent, middle, shift, down_near)


NORMS_AT, COLUMNS_AT, HEADS_AT, TOKENS_AT, VECTORS_AT = 8, 16, 20, 28, 32
BACK_STEPS = VECTORS_AT + 7
OUT_TILE = 128


def chunk_at(time):
    chunk = jnp.where(time < 13, time, time - 1)
    chunk = jnp.where(time >= 20, (time + 17) // 2, chunk)
    return chunk, (time >= 0) & ((time < 13) | ((time >= 14) & (time < 20)) | ((time >= 20) & (time < 30) & (time % 2 == 1)))


def back_kernel(
    lengths_ref,
    unit_grad_ref,
    vec_ref,
    hs_ref,
    act_all,
    slope_all,
    e_all,
    stats_all,
    up_near,
    up_late,
    feed_turned_all,
    down_grad_all,
    cot_all,
    middle_all,
    branch_all,
    scaled_turned_all,
    attended_all,
    out_weight_all,
    proj_all,
    lse_all,
    in_weight_all,
    turned_all,
    tokens_all,
    down_out,
    up_out,
    in_out,
    out_out,
    vec_out,
    tokens_grad_all,
    up_grad_all,
    units_in_ref,
    up_ref,
    stats_ref,
    feed_turned_ref,
    cot_ref,
    norms_in_ref,
    scaled_turned_ref,
    attended_ref,
    out_weight_ref,
    proj_ref,
    lse_ref,
    in_weight_ref,
    turned_ref,
    tokens_ref,
    tokens_grad_ref,
    staged_ref,
    total_ref,
    low_ref,
    out_grad_ref,
    ga_ref,
    grad_middle_ref,
    delta_ref,
    delta_sum_ref,
    sums_ref,
    units_ref,
    dq_ref,
    dk_ref,
    dv_ref,
    chunk_ref,
    stream_sems,
    fetch_sems,
    *scratch,
):
    step = pl.program_id(0)
    place = Place()
    engine = Reduction(place, scratch[:11])
    small = SmallReduction(place, scratch[11:])
    pairs = proj_all.shape[0]

    def rows_of(array, size):
        return lambda i: array.at[pl.ds(pl.multiple_of(i * size, size), size)]

    def columns_of(array, size):
        return lambda i: array.at[:, pl.ds(pl.multiple_of(i * size, size), size)]

    def stream(number, view, buffers):
        return Stream(view, buffers, stream_sems.at[number])

    act, slope, e = (
        stream(k, lambda i, array=array: array.at[unit_index(i)], units_in_ref.at[k])
        for k, array in enumerate((act_all, slope_all, e_all))
    )
    up = WeightStream(up_near, up_late, up_ref, stream_sems.at[3])
    cot = stream(4, rows_of(cot_all, OUT_TILE), cot_ref)
    middle = stream(5, rows_of(middle_all, OUT_TILE), norms_in_ref.at[0])
    branch = stream(6, rows_of(branch_all, OUT_TILE), norms_in_ref.at[1])
    attended = stream(7, columns_of(attended_all, TILE), attended_ref)
    proj = stream(8, lambda i: proj_all.at[i], proj_ref)
    lse = stream(9, lambda i: lse_all.at[i], lse_ref)
    in_weight = stream(10, columns_of(in_weight_all, 384), in_weight_ref)
    tokens = stream(11, rows_of(tokens_all, TILE), tokens_ref)
    put = rows_of(tokens_grad_all, TILE)

    def put_tokens(i):
        return pltpu.make_async_copy(
            tokens_grad_ref.at[i % 2], put(i), stream_sems.at[12, i % 2]
        )

    fetches = [
        pltpu.make_async_copy(source, target, fetch_sems.at[index])
        for index, (source, target) in enumerate(
            (
                (stats_all, stats_ref),
                (feed_turned_all, feed_turned_ref),
                (scaled_turned_all, scaled_turned_ref),
                (out_weight_all, out_weight_ref),
                (turned_all, turned_ref),
            )
        )
    ]

    @pl.when(step == 0)
    def _():
        for item in (act, slope, e, up):
            item.start(0)
        for copy in fetches:
            copy.start()
        for item in (cot, middle, branch, attended, proj, lse, in_weight, tokens):
            item.copy(0).start()
        total_ref[...] = jnp.zeros_like(total_ref)
        sums_ref[...] = jnp.zeros_like(sums_ref)
        units_ref[...] = jnp.zeros_like(units_ref)
        place.greet()

    def store(index):
        block = unit_index(index)
        view = up_grad_all.at[block // 4, block // 2 % 2, block % 2]
        return pltpu.make_async_copy(staged_ref, view, fetch_sems.at[5])

    @pl.when((step >= 1) & (step <= NORMS_AT))
    def _():
        store(step - 1).wait()


    def stage(number, kind, action, tick):
        chunk, there = chunk_at(tick - number * LAG)
        up = ((chunk >= 8) & (chunk < 14)) | (chunk == 15) | (chunk == 17)
        wanted = {
            "all": there,
            "down": there & (chunk < 8),
            "up": there & up,
            "shared": there & ((chunk < 8) | up),
            "own": there & (chunk >= 8) & ~up,
        }

        @pl.when(wanted[kind])
        def _():
            action(chunk)

    def up_index(chunk):
        return jnp.where(chunk < 14, chunk - 8, (chunk - 3) // 2)

    def pair_index(chunk):
        return jnp.where(chunk < 18, (chunk - 14) // 2, chunk - 16)

    def put_down(chunk):
        for rank, block in engine.stage6(chunk):
            for half in range(2):

                @pl.when(chunk % 2 == half)
                def _():
                    down_out[chunk // 2, rank, :, half * 512 : half * 512 + 512] = block

    def put_up(chunk):
        for rank, block in engine.stage6(chunk):
            up_out[up_index(chunk), rank] = block

    def put_own(chunk):
        total = engine.stage4(chunk)
        first = pair_index(chunk) * 128
        for part in range(3):
            lanes = pl.ds(pl.multiple_of(part * 1024 + first, 128), 128)
            in_out[:, lanes] = total[:, part * 128 : part * 128 + 128]
        out_out[:, pl.ds(pl.multiple_of(first, 128), 128)] = total[:, 384:512]

    def take_down(chunk):
        lanes = pl.ds(pl.multiple_of(chunk % 2 * 512, 512), 512)
        engine.stage0(chunk, down_grad_all.at[:, :, :, chunk // 2, :, :, lanes])

    def take_up(chunk):
        engine.stage0(chunk, up_grad_all.at[:, :, :, up_index(chunk)])

    def take_own(chunk):
        engine.stage0(chunk, chunk_ref.at[pair_index(chunk) % 2])

    def reduce_step(tick):
        stage(6, "down", put_down, tick)
        stage(6, "up", put_up, tick)
        stage(5, "shared", engine.stage5, tick)
        stage(4, "shared", lambda chunk: engine.spread(chunk, engine.stage4(chunk)), tick)
        stage(4, "own", put_own, tick)
        stage(3, "all", engine.stage3, tick)
        stage(2, "all", engine.stage2, tick)
        stage(1, "all", engine.stage1, tick)
        stage(0, "down", take_down, tick)
        stage(0, "up", take_up, tick)

    tick = jnp.where(step < NORMS_AT, step, NORMS_AT + (step - NORMS_AT) // 4)
    tick = jnp.where(step < COLUMNS_AT, tick, step - 6)
    tick = jnp.where(step < HEADS_AT, tick, 2 * step - 26)
    tick = jnp.where(step < TOKENS_AT, tick, 30)
    tick = jnp.where(step < VECTORS_AT, tick, step - 1)
    within = (step > NORMS_AT) & (step < COLUMNS_AT) & (step % 4 != 0)
    within = within | ((step > TOKENS_AT) & (step < VECTORS_AT))

    @pl.when(~within)
    def _():
        reduce_step(tick)


    @pl.when(step < NORMS_AT)
    def _():
        advance((act, slope, e, up), step, NORMS_AT)

        @pl.when(step == 0)
        def _():
            fetches[0].wait()

        unit = unit_index(step)
        units_ref[unit, 0:1] = up_back_step(
            act.block(step),
            slope.block(step),
            e.block(step),
            stats_ref,
            up.block(step),
            low_ref,
            total_ref,
        )
        units_ref[unit, 1:3] = unit_grad_ref[unit, 0:2]

        @pl.when(step == 0)
        def _():
            fetches[1].wait()

        for left in range(0, UNITS, TILE):
            columns = slice(left, left + TILE)
            grad = dot_nn(feed_turned_ref[...], low_ref[:, columns]).astype(BF)
            staged_ref[:, :, :, columns] = grad.reshape(8, 4, 32, TILE)
        store(step).start()


    @pl.when((step >= NORMS_AT) & (step < COLUMNS_AT))
    def _():
        block = step - NORMS_AT
        rows = pl.ds(pl.multiple_of(block * OUT_TILE, OUT_TILE), OUT_TILE)
        advance((cot, middle, branch), block, COLUMNS_AT - NORMS_AT)
        grad_middle, low = norms_back(
            total_ref[rows],
            cot.block(block),
            middle.block(block),
            branch.block(block),
            vec_ref,
            sums_ref,
        )
        grad_middle_ref[rows] = grad_middle
        low_ref[rows] = low

    @pl.when((step >= COLUMNS_AT) & (step < HEADS_AT))
    def _():
        block = step - COLUMNS_AT
        columns = pl.ds(pl.multiple_of(block * TILE, TILE), TILE)
        advance((attended,), block, HEADS_AT - COLUMNS_AT)

        @pl.when(block == 0)
        def _():
            fetches[2].wait()
            fetches[3].wait()

        grad_out, delta = heads_back(
            low_ref[...],
            out_weight_ref[columns],
            hs_ref[0:1, columns],
            attended.block(block)[...],
        )
        ga_ref[:, columns] = grad_out
        delta_sum_ref[block, 0:1] = column_sum(delta)
        turned = delta.T
        for head in range(4):
            delta_ref[4 * block + head] = turned[head : head + 1]
        out_grad_ref[:, columns] = dot_nn(scaled_turned_ref[...], low_ref[:, columns]).astype(BF)

    @pl.when(step == HEADS_AT - 1)
    def _():
        total_ref[...] = jnp.zeros_like(total_ref)


    @pl.when((step >= HEADS_AT) & (step < TOKENS_AT))
    def _():
        pair = step - HEADS_AT
        columns = pl.ds(pl.multiple_of(pair * 128, 128), 128)
        advance((proj, lse, in_weight), pair, pairs)

        @pl.when(pair == 0)
        def _():
            fetches[4].wait()

        for head in range(2):
            if head == 1:
                reduce_step(tick + 1)
            attention_back_head(
                head,
                cross_flag(lengths_ref, total_ref),
                *[proj.block(pair).at[:, pl.ds(index * 128, 128)] for index in range(3)],
                ga_ref.at[:, columns],
                lse.block(pair),
                delta_ref[2 * pair + head],
                dq_ref,
                dk_ref,
                dv_ref,
            )
        query_sum, value_sum = in_back_pair(
            dq_ref,
            dk_ref,
            dv_ref,
            in_weight.block(pair)[...],
            turned_ref,
            out_grad_ref.at[:, columns],
            chunk_ref.at[pair % 2].reshape(8, 4, 32, 512),
            total_ref,
        )
        sums_ref[0:1, columns] = query_sum
        sums_ref[1:2, columns] = value_sum
        stage(0, "own", take_own, tick + 1)

    @pl.when((step >= TOKENS_AT) & (step < TOKENS_AT + 4))
    def _():
        block = step - TOKENS_AT
        rows = pl.ds(pl.multiple_of(block * TILE, TILE), TILE)
        advance((tokens,), block, 4)

        @pl.when(block >= 2)
        def _():
            put_tokens(block - 2).wait()

        result, gain_grad, shift_grad = tokens_back(
            tokens.block(block)[...], total_ref[rows], grad_middle_ref[rows], vec_ref[3:4]
        )
        tokens_grad_ref[block % 2] = result
        put_tokens(block).start()
        sums_ref[3:4] += gain_grad
        sums_ref[4:5] += shift_grad


    @pl.when(step == VECTORS_AT)
    def _():
        for y in range(2):
            for z in range(4):
                own = slice((2 * z + y) * 128, (2 * z + y + 1) * 128)
                for index in range(9):
                    lanes = slice(index % 4 * 128, index % 4 * 128 + 128)
                    row = 6 + index // 4
                    units_ref[8, row : row + 1, lanes] = sums_ref[index : index + 1, own]
                for x in range(2):
                    for c in range(2):
                        unit = 4 * y + 2 * x + c
                        units_ref[8, 0:3] = units_ref[unit, 0:3]
                        if (y, z, x, c) == (0, 0, 0, 0):
                            units_ref[8, 3:4] = sums_ref[9:10, 0:UNITS]
                            units_ref[8, 4:5] = sums_ref[9:10, UNITS : 2 * UNITS]
                            for block in range(4):
                                lanes = slice(block * 128, block * 128 + 128)
                                units_ref[8, 5:6, lanes] = delta_sum_ref[block, 0:1]
                        small.source[y, x, c, z] = units_ref[8].astype(BF)
        small.stage0()

    for index, action in enumerate((small.stage1, small.stage2, small.stage3)):

        @pl.when(step == VECTORS_AT + 1 + index)
        def _():
            action()

    @pl.when(step == VECTORS_AT + 4)
    def _():
        vec_out[...] = small.stage4()
        for block in range(2, 4):
            put_tokens(block).wait()


def back_part(
    lengths,
    act,
    slope,
    e,
    stats,
    up_near,
    up_late,
    feed_turned,
    unit_grad,
    down_grad,
    cotangent,
    middle,
    branch,
    scaled_turned,
    attended,
    out_weights,
    vectors,
    head_lanes,
    projected,
    lse,
    weights,
    turned,
    tokens,
):
    rows, width = tokens.shape
    pairs = width // 128

    return pl.pallas_call(
        back_kernel,
        grid=(BACK_STEPS,),
        in_specs=[
            pl.BlockSpec(memory_space=pltpu.SMEM),
            whole(unit_grad.shape),
            whole(vectors.shape),
            whole(head_lanes.shape),
            *[ANY] * 19,
        ],
        out_specs=[
            whole((4, 4, 32, 1024)),
            whole((8, 4, 32, 512)),
            whole((32, 3 * width)),
            whole((32, width)),
            whole((16, 512)),
            ANY,
            ANY,
        ],
        out_shape=[
            jax.ShapeDtypeStruct((4, 4, 32, 1024), BF),
            jax.ShapeDtypeStruct((8, 4, 32, 512), BF),
            jax.ShapeDtypeStruct((32, 3 * width), F32),
            jax.ShapeDtypeStruct((32, width), F32),
            jax.ShapeDtypeStruct((16, 512), F32),
            jax.ShapeDtypeStruct((rows, width), BF),
            jax.ShapeDtypeStruct((2, 2, 2, 8, 4, 32, UNITS), BF),
        ],
        scratch_shapes=[
            pltpu.VMEM((3, 2, rows, UNITS), BF),
            pltpu.VMEM((2, width, UNITS), BF),
            pltpu.VMEM((rows, 128), F32),
            pltpu.VMEM((width, rows), BF),
            pltpu.VMEM((2, OUT_TILE, width), BF),
            pltpu.VMEM((2, 2, OUT_TILE, width), F32),
            pltpu.VMEM((width, rows), BF),
            pltpu.VMEM((2, rows, TILE), F32),
            pltpu.VMEM((width, width), BF),
            pltpu.VMEM((2, rows, 384), BF),
            pltpu.VMEM((2, 8, rows), F32),
            pltpu.VMEM((2, width, 384), BF),
            pltpu.VMEM((width, rows), BF),
            pltpu.VMEM((2, TILE, width), BF),
            pltpu.VMEM((2, TILE, width), BF),
            pltpu.VMEM((8, 4, 32, UNITS), BF),
            pltpu.VMEM((rows, width), F32),
            pltpu.VMEM((rows, width), BF),
            pltpu.VMEM((width, width), BF),
            pltpu.VMEM((rows, width), BF),
            pltpu.VMEM((rows, width), F32),
            pltpu.VMEM((2 * pairs, 1, rows), F32),
            pltpu.VMEM((4, 8, 128), F32),
            pltpu.VMEM((16, width), F32),
            pltpu.VMEM((9, 16, UNITS), F32),
            pltpu.VMEM((rows, 128), F32),
            pltpu.VMEM((rows, 128), F32),
            pltpu.VMEM((rows, 128), F32),
            pltpu.VMEM((2, 2, 2, 2, 4, 32, 512), BF),
            pltpu.SemaphoreType.DMA((13, 2)),
            pltpu.SemaphoreType.DMA((6,)),
            *Reduction.scratch(),
            *SmallReduction.scratch(),
        ],
        compiler_params=params(collective_id=1, has_side_effects=True),
        name="back_part",
    )(
        lengths,
        unit_grad,
        vectors,
        head_lanes,
        act,
        slope,
        e,
        stats,
        up_near,
        up_late,
        feed_turned,
        down_grad.reshape(2, 2, 2, 4, 4, 32, width),
        cotangent,
        middle,
        branch,
        scaled_turned,
        attended,
        out_weights,
        projected,
        lse,
        weights,
        turned,
        tokens,
    )


def layer(staged, tokens, cotangent, lengths, attn, up, down, unit_vec, head_scale, down_bias):
    rows, width = tokens.shape
    heads = head_scale.shape[0]
    pairs = width // 128
    if staged:
        in_weight, out_weight, vec_block = attn
        (
            turned,
            projected,
            scaled,
            scaled_turned,
            attended,
            lse,
            vectors,
            head_lanes,
            weights,
            out_weights,
            up,
            unit_vec,
        ) = first_part(
            lengths, tokens, in_weight, vec_block, out_weight, up, unit_vec, head_scale[None, :]
        )
        weights = weights.reshape(width, 3 * width)
        out_weights = out_weights.reshape(width, width)
        unit_vec = unit_vec.reshape(-1, unit_vec.shape[-2], UNITS)
        branch, middle, feed_turned, act, slope, stats, up_late, down_near = second_part(
            scaled, out_weights, vectors, tokens, up, unit_vec, down
        )
        mixed, down_grad, e, stats, unit_grad, _ = third_part(
            act, stats, unit_vec, down_near, cotangent, middle, down_bias[None, :]
        )
    else:
        weights, out_weights, vectors = attn
        scale = head_scale.astype(F32)
        head_lanes = jnp.repeat(scale, width // heads)[None, :]
        first, projected, scaled, attended, lse = plain_first(
            lengths, tokens, weights, vectors, head_lanes
        )
        branch, middle, feed = out_proj(scaled, out_weights, vectors, tokens)
        act, slope, stats = up_pass(feed, up, unit_vec)
        mixed, down_grad, e, stats, unit_grad = down_pass(
            act, stats, unit_vec, down, cotangent, middle, down_bias[None, :]
        )
    if staged:
        down_total, up_total, in_total, out_total, vec_shares, tokens_grad, _ = back_part(
            lengths,
            act,
            slope,
            e,
            stats,
            up,
            up_late,
            feed_turned,
            unit_grad,
            down_grad,
            cotangent,
            middle,
            branch,
            scaled_turned,
            attended,
            out_weights,
            vectors,
            head_lanes,
            projected,
            lse,
            weights,
            turned,
            tokens,
        )
        return mixed, tokens_grad, down_total, up_total, in_total, out_total, vec_shares
    up_grad, up_bias_grad, grad_feed = up_back(
        act, slope, e, stats, up, feed
    )
    grad_middle, ga, out_grad, delta, sums = out_back(
        grad_feed,
        cotangent,
        middle,
        branch,
        scaled,
        attended,
        out_weights,
        vectors,
        head_lanes,
    )
    chunks, proj_bias, tokens_grad, pre_sums = in_back(
        lengths,
        projected,
        ga,
        lse,
        delta.reshape(pairs, 2, rows),
        weights,
        first,
        out_grad,
        tokens,
        vectors[3:4],
        grad_middle,
    )
    scale_grad = jnp.sum(delta, axis=1) / scale
    vec_grads = [
        proj_bias[:, 0].reshape(width),
        proj_bias[:, 1].reshape(width),
        sums[2],
        pre_sums[0],
        pre_sums[1],
        sums[5],
        sums[6],
        sums[7],
        sums[8],
    ]
    unit_grads = [up_bias_grad[:, 0], unit_grad[:, 0], unit_grad[:, 1]]
    return mixed, tokens_grad, chunks, up_grad, down_grad, vec_grads, unit_grads, sums[9], scale_grad


def body(
    axes,
    tokens,
    cotangent,
    lengths,
    in_weight,
    query_bias,
    value_bias,
    out_weight,
    out_bias,
    head_scale,
    pre_gain,
    pre_bias,
    post_gain,
    post_bias,
    feed_gain,
    feed_bias,
    up_weight,
    up_bias,
    mid_gain,
    mid_bias,
    down_weight,
    down_bias,
):
    planes, wide = axes
    every = ("dp", "wide")
    staged = (planes, wide) == (4, 8)
    rows, width = tokens.shape
    units = down_weight.shape[0] * wide
    steps = units // UNITS
    share = in_weight.shape[0]
    columns = [
        query_bias,
        value_bias,
        out_bias,
        pre_gain,
        pre_bias,
        post_gain,
        post_bias,
        feed_gain,
        feed_bias,
    ]
    index = lax.broadcasted_iota(jnp.int32, (32, up_bias.shape[0]), 0)
    unit_rows = jnp.where(index == 0, up_bias[None, :], jnp.zeros((), BF))
    unit_rows = jnp.where(index == 1, mid_gain[None, :], unit_rows)
    unit_rows = jnp.where(index == 2, mid_bias[None, :], unit_rows)
    if staged:
        index = lax.broadcasted_iota(jnp.int32, (32, share), 0)
        vec_block = jnp.zeros((32, share), BF)
        for row, column in enumerate(columns):
            vec_block = jnp.where(index == row, column[None, :], vec_block)
        attn = (in_weight, out_weight, vec_block)
        up, unit_vec, down = up_weight, unit_rows, down_weight
    else:
        flat = jnp.concatenate(columns).reshape(len(columns), share)
        attn = (
            lax.all_gather(in_weight, every, axis=0, tiled=True),
            lax.all_gather(out_weight, every, axis=0, tiled=True),
            jnp.pad(
                lax.all_gather(flat, every, axis=1, tiled=True), ((0, 16 - len(columns)), (0, 0))
            ).astype(F32),
        )
        up = lax.all_gather(up_weight, "wide", axis=1, tiled=True)
        up = up.reshape(width, steps, UNITS).transpose(1, 0, 2)
        unit_vec = lax.all_gather(unit_rows, "wide", axis=1, tiled=True)
        unit_vec = unit_vec.reshape(32, steps, UNITS).transpose(1, 0, 2)
        down = lax.all_gather(down_weight, "wide", axis=0, tiled=True)
        down = down.reshape(steps, UNITS, width)
    results = layer(
        staged,
        tokens,
        cotangent,
        lengths,
        attn,
        up,
        down,
        unit_vec,
        head_scale,
        down_bias,
    )
    heads = head_scale.shape[0]
    pairs = width // 128
    if staged:
        mixed, tokens_grad, down_total, up_total, in_total, out_total, vec_shares = results
        up_total = up_total.astype(F32).reshape(width, UNITS)
        down_total = down_total.astype(F32).reshape(UNITS, width)
        unit_totals = [vec_shares[index] for index in range(3)]
        down_sum = vec_shares[3:5].reshape(width)
        scale_sum = vec_shares[5].reshape(4, 128)[:, :4].reshape(heads) / head_scale.astype(F32)
        offset = share * lax.rem(lax.axis_index("wide"), 128 // share)
        own = vec_shares[6:9].reshape(12, 128)
        own = lax.dynamic_slice(own, (0, offset), (len(columns), share))
        vec_totals = [own[index] for index in range(len(columns))]
    else:
        (mixed, tokens_grad, chunks, up_grad, down_grad, vec_grads, unit_grads) = results[:7]
        down_sum, scale_sum = results[7:]

        def scatter(value, axis=0, over=every):
            return lax.psum_scatter(value, over, scatter_dimension=axis, tiled=True)

        def both_ways(value, axis):
            part = scatter(value.astype(BF), axis, "wide")
            return lax.psum(part, "dp").astype(F32)

        up_total = both_ways(up_grad.transpose(1, 0, 2).reshape(width, units), 1)
        down_total = both_ways(down_grad.reshape(units, width), 0)
        unit_totals = [
            lax.psum(scatter(item.reshape(units), 0, "wide"), "dp") for item in unit_grads
        ]
        down_sum, scale_sum = lax.psum((down_sum, scale_sum), every)
        vec_totals = [scatter(item) for item in vec_grads]
        natural = chunks.transpose(0, 2, 1, 3, 4).reshape(pairs, width, 512)
        in_total = natural[:, :, :384].reshape(pairs, width, 3, 128)
        in_total = scatter(in_total.transpose(1, 2, 0, 3).reshape(width, 3 * width).astype(F32))
        out_total = scatter(
            natural[:, :, 384:].transpose(1, 0, 2).reshape(width, width).astype(F32)
        )
    return (
        mixed,
        tokens_grad,
        in_total,
        vec_totals[0],
        vec_totals[1],
        out_total,
        vec_totals[2],
        scale_sum,
        vec_totals[3],
        vec_totals[4],
        vec_totals[5],
        vec_totals[6],
        vec_totals[7],
        vec_totals[8],
        up_total,
        unit_totals[0],
        unit_totals[1],
        unit_totals[2],
        down_total,
        down_sum,
    )


def solution(mesh):
    by_all = P(("dp", "wide"))
    rows_all = P(("dp", "wide"), None)
    axes = (mesh.shape["dp"], mesh.shape["wide"])
    return jax.shard_map(
        functools.partial(body, axes),
        mesh=mesh,
        in_specs=(
            rows_all,
            rows_all,
            rows_all,
            rows_all,
            by_all,
            by_all,
            rows_all,
            by_all,
            P(),
            by_all,
            by_all,
            by_all,
            by_all,
            by_all,
            by_all,
            P(None, "wide"),
            P("wide"),
            P("wide"),
            P("wide"),
            P("wide", None),
            P(),
        ),
        out_specs=(
            rows_all,
            rows_all,
            rows_all,
            by_all,
            by_all,
            rows_all,
            by_all,
            P(),
            by_all,
            by_all,
            by_all,
            by_all,
            by_all,
            by_all,
            P(None, "wide"),
            P("wide"),
            P("wide"),
            P("wide"),
            P("wide", None),
            P(),
        ),
        check_vma=False,
    )
```

```python
import functools

import jax
import jax.numpy as jnp
from jax import lax
from jax.experimental import pallas as pl
from jax.experimental.pallas import tpu as pltpu
from jax.sharding import PartitionSpec as P

EPS = 1e-05
ROOT_HALF = 0.7071067811865476
INV_ROOT_TAU = 0.3989422804014327
LOG2E = 1.4426950408889634
MASKED = -1e30
BF = jnp.bfloat16
F32 = jnp.float32
TILE = 256
UNITS = 512
SLIM = 64
MESH = pl.DeviceIdType.MESH
VMEM_LIMIT = 62 * 1024 * 1024
ANY = pl.BlockSpec(memory_space=pl.ANY)


def dot_nn(left, right):
    return lax.dot_general(left, right, (((1,), (0,)), ((), ())), preferred_element_type=F32)


def dot_nt(left, right):
    return lax.dot_general(left, right, (((1,), (1,)), ((), ())), preferred_element_type=F32)


def dot_tn(left, right):
    return lax.dot_general(left, right, (((0,), (0,)), ((), ())), preferred_element_type=F32)


def params(**more):
    return pltpu.CompilerParams(
        dimension_semantics=("arbitrary",), vmem_limit_bytes=VMEM_LIMIT, **more
    )


def whole(shape):
    zeros = (0,) * len(shape)
    return pl.BlockSpec(shape, lambda *_: zeros, pipeline_mode=pl.Buffered(1))


def row_norm(values):
    center = values - jnp.mean(values, axis=-1, keepdims=True)
    inv = lax.rsqrt(jnp.mean(center * center, axis=-1, keepdims=True) + EPS)
    return center * inv, inv


def norm_back(grad, gain, normed, inv):
    scaled = grad * gain
    first = jnp.mean(scaled, axis=-1, keepdims=True)
    cross = jnp.mean(scaled * normed, axis=-1, keepdims=True)
    return inv * (scaled - first - normed * cross)


def column_sum(values):
    return jnp.sum(values, axis=0, keepdims=True)


def lane_fold(values):
    total = values[:, :128]
    for start in range(128, values.shape[1], 128):
        total = total + values[:, start : start + 128]
    return total


def cross_flag(lengths_ref, rows_ref):
    return jnp.where(lengths_ref[0, 0] == rows_ref.shape[0], 0.0, MASKED)


def attention_pair(cross, q_ref, k_ref, v_ref, scale, scaled_ref, out_ref, lse_ref, vext_ref):
    rows = q_ref.shape[0]
    half = rows // 2
    factor = LOG2E * 64 ** (-0.5)
    low_lanes = lax.broadcasted_iota(jnp.int32, (1, 128), 1) < 64
    below = lax.broadcasted_iota(jnp.int32, (TILE, TILE), 1) <= lax.broadcasted_iota(
        jnp.int32, (TILE, TILE), 0
    )
    vext_ref[:, :128] = v_ref[...]
    vext_ref[:, 128:] = jnp.ones((rows, 128), BF)
    for start in range(0, rows, TILE):
        stop = start + TILE
        query = q_ref[start:stop]
        results = []
        for head in range(2):
            mine = low_lanes if head == 0 else ~low_lanes
            raw = dot_nt(jnp.where(mine, query, jnp.zeros_like(query)), k_ref[:stop])
            parts = []
            if start >= half:
                parts.append((raw[:, :half], cross))
                if start > half:
                    parts.append((raw[:, half:start], None))
            elif start > 0:
                parts.append((raw[:, :start], None))
            parts.append((jnp.where(below, raw[:, start:stop], MASKED), None))
            peak = None
            for piece, shift in parts:
                top = jnp.max(piece, axis=-1, keepdims=True)
                if shift is not None:
                    top = top + shift
                peak = top if peak is None else jnp.maximum(peak, top)
            weights = []
            for piece, shift in parts:
                level = peak if shift is None else peak - shift
                weights.append(jnp.exp2((piece - level) * factor).astype(BF))
            weights = weights[0] if len(weights) == 1 else jnp.concatenate(weights, axis=1)
            both = dot_nn(weights, vext_ref[:stop])
            total = both[:, 128:]
            results.append((both[:, :128] / total, peak * factor + jnp.log2(total)))
        mixed = jnp.where(low_lanes, results[0][0], results[1][0])
        out_ref[start:stop] = mixed
        scaled_ref[start:stop] = (mixed * scale).astype(BF)
        lse = jnp.where(low_lanes, results[0][1], results[1][1]).T
        lse_ref[0, 0:1, start:stop] = lse[0:1]
        lse_ref[0, 1:2, start:stop] = lse[64:65]


def project_pair(first_ref, weights, bias, proj_ref):
    proj_ref[0] = (dot_nn(first_ref[...], weights) + bias).astype(BF)


def three(proj_ref):
    return [proj_ref.at[0, :, pl.ds(part * 128, 128)] for part in range(3)]


def plain_first_kernel(
    lengths_ref,
    tokens_ref,
    wq_ref,
    wk_ref,
    wv_ref,
    vectors_ref,
    bq_ref,
    bv_ref,
    hs_ref,
    first_ref,
    proj_ref,
    scaled_ref,
    attended_ref,
    lse_ref,
    vext_ref,
):
    @pl.when(pl.program_id(0) == 0)
    def _():
        for start in range(0, tokens_ref.shape[0], TILE):
            rows = pl.ds(start, TILE)
            normed, _ = row_norm(tokens_ref[rows].astype(F32))
            first_ref[rows] = (normed * vectors_ref[3:4] + vectors_ref[4:5]).astype(BF)

    weights = jnp.concatenate([wq_ref[...], wk_ref[...], wv_ref[...]], axis=1)
    bias = jnp.concatenate([bq_ref[0:1], jnp.zeros((1, 128), F32), bv_ref[1:2]], axis=1)
    project_pair(first_ref, weights, bias, proj_ref)
    attention_pair(
        cross_flag(lengths_ref, tokens_ref), *three(proj_ref), hs_ref[...], scaled_ref, attended_ref, lse_ref, vext_ref
    )


def plain_first(lengths, tokens, weights, vectors, head_lanes):
    rows, width = tokens.shape
    pairs = width // 128
    column = pl.BlockSpec((rows, 128), lambda p: (0, p))
    bias = pl.BlockSpec((16, 128), lambda p: (0, p))
    return pl.pallas_call(
        plain_first_kernel,
        grid=(pairs,),
        in_specs=[
            pl.BlockSpec(memory_space=pltpu.SMEM),
            whole((rows, width)),
            pl.BlockSpec((width, 128), lambda p: (0, p)),
            pl.BlockSpec((width, 128), lambda p: (0, pairs + p)),
            pl.BlockSpec((width, 128), lambda p: (0, 2 * pairs + p)),
            whole(vectors.shape),
            bias,
            bias,
            pl.BlockSpec((1, 128), lambda p: (0, p)),
        ],
        out_specs=[
            whole((rows, width)),
            pl.BlockSpec((1, rows, 384), lambda p: (p, 0, 0)),
            column,
            column,
            pl.BlockSpec((1, 8, rows), lambda p: (p, 0, 0)),
        ],
        out_shape=[
            jax.ShapeDtypeStruct((rows, width), BF),
            jax.ShapeDtypeStruct((pairs, rows, 384), BF),
            jax.ShapeDtypeStruct((rows, width), BF),
            jax.ShapeDtypeStruct((rows, width), F32),
            jax.ShapeDtypeStruct((pairs, 8, rows), F32),
        ],
        scratch_shapes=[pltpu.VMEM((rows, 256), BF)],
        compiler_params=params(),
        name="plain_first",
    )(lengths, tokens, weights, weights, weights, vectors, vectors, vectors, head_lanes)


def out_proj_rows(scaled_ref, weight_ref, vec_ref, tokens_ref, branch_ref, middle_ref):
    branch = dot_nn(scaled_ref[...], weight_ref[...]) + vec_ref[2:3]
    normed, _ = row_norm(branch)
    middle = tokens_ref[...].astype(F32) + (normed * vec_ref[5:6] + vec_ref[6:7])
    again, _ = row_norm(middle)
    branch_ref[...] = branch
    middle_ref[...] = middle
    return (again * vec_ref[7:8] + vec_ref[8:9]).astype(BF)


def out_proj_kernel(scaled_ref, weight_ref, vec_ref, tokens_ref, branch_ref, middle_ref, feed_ref):
    feed_ref[...] = out_proj_rows(
        scaled_ref, weight_ref, vec_ref, tokens_ref, branch_ref, middle_ref
    )


def out_proj(scaled, weights, vectors, tokens):
    rows, width = tokens.shape
    by_row = pl.BlockSpec((TILE, width), lambda i: (i, 0))
    return pl.pallas_call(
        out_proj_kernel,
        grid=(rows // TILE,),
        in_specs=[
            by_row,
            whole((width, width)),
            whole(vectors.shape),
            by_row,
        ],
        out_specs=[by_row, by_row, by_row],
        out_shape=[
            jax.ShapeDtypeStruct((rows, width), F32),
            jax.ShapeDtypeStruct((rows, width), F32),
            jax.ShapeDtypeStruct((rows, width), BF),
        ],
        compiler_params=params(),
        name="out_proj",
    )(scaled, weights, vectors, tokens)


def phi_and_slope(value):
    bell = jnp.exp2(value * value * (-0.5 * LOG2E))
    t = 1.0 / (1.0 + (0.3275911 * ROOT_HALF) * jnp.abs(value))
    series = t * (
        0.5 * 0.254829592
        + t
        * (
            0.5 * -0.284496736
            + t * (0.5 * 1.421413741 + t * (0.5 * -1.453152027 + t * (0.5 * 1.061405429)))
        )
    )
    tail = series * bell
    area = jnp.where(value < 0.0, tail, 1.0 - tail)
    return value * area, area + value * bell * INV_ROOT_TAU


def up_step(feed_ref, up, vec, act_ref, slope_ref, sums_ref):
    for left in range(0, UNITS, TILE):
        columns = slice(left, left + TILE)
        pre = dot_nn(feed_ref[...], up[:, columns])
        bias = vec[0:1, columns].astype(F32)
        for start in range(0, feed_ref.shape[0], SLIM):
            rows = slice(start, start + SLIM)
            act, slope = phi_and_slope(pre[rows] + bias)
            act_ref[0, rows, columns] = act.astype(BF)
            slope_ref[0, rows, columns] = slope.astype(BF)
            sums_ref[0, rows] += lane_fold(act)
            sums_ref[1, rows] += lane_fold(act * act)


def side_by_side(*columns):
    lane = lax.broadcasted_iota(jnp.int32, (1, 128), 1)
    result = jnp.broadcast_to(columns[-1], (columns[-1].shape[0], 128))
    for index in range(len(columns) - 2, -1, -1):
        result = jnp.where(lane == index, columns[index], result)
    return result


def up_stats(units, stats_ref, sums_ref):
    for start in range(0, stats_ref.shape[0], TILE):
        rows = pl.ds(start, TILE)
        mean = jnp.sum(sums_ref[0, rows], axis=1, keepdims=True) / units
        square = jnp.sum(sums_ref[1, rows], axis=1, keepdims=True) / units
        inv = lax.rsqrt(square - mean * mean + EPS)
        stats_ref[rows] = side_by_side(mean, inv)


def up_kernel(units, feed_ref, up_ref, vec_ref, act_ref, slope_ref, stats_ref, sums_ref):
    step = pl.program_id(0)

    @pl.when(step == 0)
    def _():
        sums_ref[...] = jnp.zeros_like(sums_ref)

    up_step(feed_ref, up_ref.at[0], vec_ref.at[0], act_ref, slope_ref, sums_ref)

    @pl.when(step == pl.num_programs(0) - 1)
    def _():
        up_stats(units, stats_ref, sums_ref)


def up_pass(feed, up, vec):
    rows, width = feed.shape
    steps = up.shape[0]
    block = pl.BlockSpec((1, rows, UNITS), lambda j: (j, 0, 0))
    return pl.pallas_call(
        functools.partial(up_kernel, steps * UNITS),
        grid=(steps,),
        in_specs=[
            whole((rows, width)),
            pl.BlockSpec((1, width, UNITS), lambda j: (j, 0, 0)),
            pl.BlockSpec((1, vec.shape[1], UNITS), lambda j: (j, 0, 0)),
        ],
        out_specs=[block, block, whole((rows, 128))],
        out_shape=[
            jax.ShapeDtypeStruct((steps, rows, UNITS), BF),
            jax.ShapeDtypeStruct((steps, rows, UNITS), BF),
            jax.ShapeDtypeStruct((rows, 128), F32),
        ],
        scratch_shapes=[pltpu.VMEM((2, rows, 128), F32)],
        compiler_params=params(),
        name="up_pass",
    )(feed, up, vec)


def down_step(
    act_ref, stats_ref, vec, down, cot_ref, down_grad_ref, e_ref, vec_grad_ref, total_ref, sums_ref,
    low_ref
):
    gain = vec[1:2].astype(F32)
    shift = vec[2:3].astype(F32)
    slims = [slice(start, start + SLIM) for start in range(0, cot_ref.shape[0], SLIM)]

    def normalized(rows, columns):
        value = act_ref[0, rows, columns].astype(F32)
        return (value - stats_ref[rows, 0:1]) * stats_ref[rows, 1:2]

    for rows in slims:
        low_ref[rows] = (normalized(rows, slice(0, UNITS)) * gain + shift).astype(BF)
    for left in range(0, UNITS, TILE):
        columns = slice(left, left + TILE)
        grads = dot_nt(cot_ref[...], down[columns])
        gain_grad = jnp.zeros((SLIM, TILE), F32)
        bias_grad = jnp.zeros((SLIM, TILE), F32)
        for rows in slims:
            normed = normalized(rows, columns)
            grad = grads[rows]
            gain_grad = gain_grad + grad * normed
            bias_grad = bias_grad + grad
            e = grad * gain[:, columns]
            e_ref[0, rows, columns] = e.astype(BF)
            sums_ref[0, rows] += lane_fold(e)
            sums_ref[1, rows] += lane_fold(e * normed)
        vec_grad_ref[0, 0:1, columns] = column_sum(gain_grad)
        vec_grad_ref[0, 1:2, columns] = column_sum(bias_grad)
    for left in range(0, total_ref.shape[1], TILE):
        columns = slice(left, left + TILE)
        total_ref[:, columns] += dot_nn(low_ref[...], down[:, columns])
    for left in range(0, UNITS, TILE):
        columns = slice(left, left + TILE)
        down_grad_ref[0, columns] = dot_tn(low_ref[:, columns], cot_ref[...]).astype(BF)


def down_end(
    units, stats_ref, middle_ref, shift_ref, mixed_ref, all_stats_ref, total_ref, sums_ref
):
    for start in range(0, total_ref.shape[0], TILE):
        rows = pl.ds(start, TILE)
        mixed_ref[rows] = (
            middle_ref[rows] + total_ref[rows] + shift_ref[...].astype(F32)
        ).astype(BF)
        first = jnp.sum(sums_ref[0, rows], axis=1, keepdims=True) / units
        cross = jnp.sum(sums_ref[1, rows], axis=1, keepdims=True) / units
        all_stats_ref[rows] = side_by_side(stats_ref[rows, 0:1], stats_ref[rows, 1:2], first, cross)


def down_kernel(
    units,
    act_ref,
    stats_ref,
    vec_ref,
    down_ref,
    cot_ref,
    middle_ref,
    shift_ref,
    mixed_ref,
    down_grad_ref,
    e_ref,
    all_stats_ref,
    vec_grad_ref,
    total_ref,
    sums_ref,
    low_ref,
):
    step = pl.program_id(0)

    @pl.when(step == 0)
    def _():
        total_ref[...] = jnp.zeros_like(total_ref)
        sums_ref[...] = jnp.zeros_like(sums_ref)

    down_step(
        act_ref, stats_ref, vec_ref.at[0], down_ref.at[0], cot_ref, down_grad_ref, e_ref, vec_grad_ref,
        total_ref, sums_ref, low_ref
    )

    @pl.when(step == pl.num_programs(0) - 1)
    def _():
        down_end(
            units, stats_ref, middle_ref, shift_ref, mixed_ref, all_stats_ref, total_ref, sums_ref
        )


def down_pass(act, stats, vec, down, cotangent, middle, shift):
    rows, width = cotangent.shape
    steps = act.shape[0]
    block = pl.BlockSpec((1, rows, UNITS), lambda j: (j, 0, 0))
    return pl.pallas_call(
        functools.partial(down_kernel, steps * UNITS),
        grid=(steps,),
        in_specs=[
            block,
            whole((rows, 128)),
            pl.BlockSpec((1, vec.shape[1], UNITS), lambda j: (j, 0, 0)),
            pl.BlockSpec((1, UNITS, width), lambda j: (j, 0, 0)),
            whole((rows, width)),
            whole((rows, width)),
            whole((1, width)),
        ],
        out_specs=[
            whole((rows, width)),
            pl.BlockSpec((1, UNITS, width), lambda j: (j, 0, 0)),
            block,
            whole((rows, 128)),
            pl.BlockSpec((1, 8, UNITS), lambda j: (j, 0, 0)),
        ],
        out_shape=[
            jax.ShapeDtypeStruct((rows, width), BF),
            jax.ShapeDtypeStruct((steps, UNITS, width), BF),
            jax.ShapeDtypeStruct((steps, rows, UNITS), BF),
            jax.ShapeDtypeStruct((rows, 128), F32),
            jax.ShapeDtypeStruct((steps, 8, UNITS), F32),
        ],
        scratch_shapes=[
            pltpu.VMEM((rows, width), F32),
            pltpu.VMEM((2, rows, 128), F32),
            pltpu.VMEM((rows, UNITS), BF),
        ],
        compiler_params=params(),
        name="down_pass",
    )(act, stats, vec, down, cotangent, middle, shift)


def up_back_step(act, slope, e, stats_ref, up, low_ref, total_ref):
    bias_grad = jnp.zeros((SLIM, UNITS), F32)
    for start in range(0, total_ref.shape[0], SLIM):
        rows = slice(start, start + SLIM)
        inv = stats_ref[rows, 1:2]
        normed = (act[rows].astype(F32) - stats_ref[rows, 0:1]) * inv
        grad_act = inv * (
            e[rows].astype(F32) - stats_ref[rows, 2:3] - normed * stats_ref[rows, 3:4]
        )
        low = (grad_act * slope[rows].astype(F32)).astype(BF)
        bias_grad = bias_grad + low.astype(F32)
        low_ref[rows, 0:UNITS] = low
    for left in range(0, total_ref.shape[1], TILE):
        columns = slice(left, left + TILE)
        total_ref[:, columns] += dot_nt(low_ref[:, 0:UNITS], up[columns])
    return column_sum(bias_grad)


def up_back_kernel(
    act_ref,
    slope_ref,
    e_ref,
    stats_ref,
    up_ref,
    feed_ref,
    up_grad_ref,
    bias_grad_ref,
    total_ref,
    turned_ref,
    low_ref,
):
    @pl.when(pl.program_id(0) == 0)
    def _():
        total_ref[...] = jnp.zeros_like(total_ref)
        turned_ref[...] = feed_ref[...].T

    bias_grad_ref[0, 0:1] = up_back_step(
        act_ref.at[0],
        slope_ref.at[0],
        e_ref.at[0],
        stats_ref,
        up_ref.at[0],
        low_ref,
        total_ref,
    )
    up_grad_ref[0] = dot_nn(turned_ref[...], low_ref[...]).astype(BF)


def up_back(act, slope, e, stats, up, feed):
    rows, width = feed.shape
    steps = act.shape[0]
    block = pl.BlockSpec((1, rows, UNITS), lambda j: (j, 0, 0))
    narrow = whole((rows, 128))
    return pl.pallas_call(
        up_back_kernel,
        grid=(steps,),
        in_specs=[
            block,
            block,
            block,
            narrow,
            pl.BlockSpec((1, width, UNITS), lambda j: (j, 0, 0)),
            whole((rows, width)),
        ],
        out_specs=[
            pl.BlockSpec((1, width, UNITS), lambda j: (j, 0, 0)),
            pl.BlockSpec((1, 8, UNITS), lambda j: (j, 0, 0)),
            whole((rows, width)),
        ],
        out_shape=[
            jax.ShapeDtypeStruct((steps, width, UNITS), BF),
            jax.ShapeDtypeStruct((steps, 8, UNITS), F32),
            jax.ShapeDtypeStruct((rows, width), F32),
        ],
        scratch_shapes=[pltpu.VMEM((width, rows), BF), pltpu.VMEM((rows, UNITS), BF)],
        compiler_params=params(),
        name="up_back",
    )(act, slope, e, stats, up, feed)


def norms_back(grad_feed, cot_ref, middle_ref, branch_ref, vec_ref, sums_ref):
    normed, inv = row_norm(middle_ref[...])
    cot = cot_ref[...].astype(F32)
    grad_middle = cot + norm_back(grad_feed, vec_ref[7:8], normed, inv)
    sums_ref[7:8] += column_sum(grad_feed * normed)
    sums_ref[8:9] += column_sum(grad_feed)
    sums_ref[9:10] += column_sum(cot)
    normed, inv = row_norm(branch_ref[...])
    low = norm_back(grad_middle, vec_ref[5:6], normed, inv).astype(BF)
    sums_ref[5:6] += column_sum(grad_middle * normed)
    sums_ref[6:7] += column_sum(grad_middle)
    sums_ref[2:3] += column_sum(low.astype(F32))
    return grad_middle, low


def heads_back(low, weights, scale, attended):
    grad_out = (dot_nt(low, weights) * scale).astype(BF)
    product = grad_out.astype(F32) * attended
    high = product.astype(BF)
    rest = (product - high.astype(F32)).astype(BF)
    heads = (
        lax.broadcasted_iota(jnp.int32, (product.shape[1], 128), 0) // 64
        == lax.broadcasted_iota(jnp.int32, (product.shape[1], 128), 1)
    ).astype(BF)
    return grad_out, dot_nn(high, heads) + dot_nn(rest, heads)


def out_back_kernel(
    grad_feed_ref,
    cot_ref,
    middle_ref,
    branch_ref,
    scaled_ref,
    attended_ref,
    weight_ref,
    vec_ref,
    hs_ref,
    grad_middle_ref,
    ga_ref,
    out_grad_ref,
    delta_ref,
    sums_ref,
    total_ref,
):
    step = pl.program_id(0)

    @pl.when(step == 0)
    def _():
        total_ref[...] = jnp.zeros_like(total_ref)
        sums_ref[...] = jnp.zeros_like(sums_ref)

    grad_middle, low = norms_back(
        grad_feed_ref[...], cot_ref, middle_ref, branch_ref, vec_ref, sums_ref
    )
    grad_middle_ref[...] = grad_middle
    ga_ref[...], delta = heads_back(low, weight_ref[...], hs_ref[...], attended_ref[...])
    total_ref[...] += dot_tn(scaled_ref[...], low)
    delta_ref[...] = delta.T[: delta_ref.shape[0]]

    @pl.when(step == pl.num_programs(0) - 1)
    def _():
        out_grad_ref[...] = total_ref[...].astype(BF)


def out_back(
    grad_feed, cotangent, middle, branch, scaled, attended, weights, vectors, head_lanes
):
    rows, width = cotangent.shape
    heads = 2 * width // 128
    by_row = pl.BlockSpec((TILE, width), lambda i: (i, 0))
    return pl.pallas_call(
        out_back_kernel,
        grid=(rows // TILE,),
        in_specs=[
            by_row,
            by_row,
            by_row,
            by_row,
            by_row,
            by_row,
            whole((width, width)),
            whole(vectors.shape),
            whole((1, width)),
        ],
        out_specs=[
            by_row,
            by_row,
            whole((width, width)),
            pl.BlockSpec((heads, TILE), lambda i: (0, i)),
            whole((16, width)),
        ],
        out_shape=[
            jax.ShapeDtypeStruct((rows, width), F32),
            jax.ShapeDtypeStruct((rows, width), BF),
            jax.ShapeDtypeStruct((width, width), BF),
            jax.ShapeDtypeStruct((heads, rows), F32),
            jax.ShapeDtypeStruct((16, width), F32),
        ],
        scratch_shapes=[pltpu.VMEM((width, width), F32)],
        compiler_params=params(),
        name="out_back",
    )(
        grad_feed,
        cotangent,
        middle,
        branch,
        scaled,
        attended,
        weights,
        vectors,
        head_lanes,
    )


def attention_back_head(
    head, cross, q_ref, k_ref, v_ref, ga_ref, lse_ref, delta, dq_ref, dk_ref, dv_ref
):
    rows = q_ref.shape[0]
    half = rows // 2
    factor = LOG2E * 64 ** (-0.5)
    low_lanes = lax.broadcasted_iota(jnp.int32, (1, 128), 1) < 64
    mine = low_lanes if head == 0 else ~low_lanes
    above = lax.broadcasted_iota(jnp.int32, (TILE, TILE), 0) <= lax.broadcasted_iota(
        jnp.int32, (TILE, TILE), 1
    )
    zero = jnp.zeros((rows, 128), BF)
    query = jnp.where(mine, q_ref[...], zero)
    grad = jnp.where(mine, ga_ref[...], zero)
    key_own = jnp.where(mine, k_ref[...], zero)
    for start in range(0, rows, TILE):
        stop = start + TILE
        raw = dot_nt(k_ref[start:stop], query[start:])
        level = lse_ref[head : head + 1, start:]
        parts = [jnp.where(above, raw[:, :TILE] * factor - level[:, :TILE], MASKED)]
        if start < half:
            if stop < half:
                parts.append(raw[:, TILE : half - start] * factor - level[:, TILE : half - start])
            parts.append(raw[:, half - start :] * factor - (level[:, half - start :] - cross))
        elif stop < rows:
            parts.append(raw[:, TILE:] * factor - level[:, TILE:])
        exponent = parts[0] if len(parts) == 1 else jnp.concatenate(parts, axis=1)
        weights = jnp.exp2(exponent)
        grad_weights = dot_nt(v_ref[start:stop], grad[start:])
        grad_scores = (weights * (grad_weights - delta[:, start:])).astype(BF)
        dv = dot_nn(weights.astype(BF), grad[start:])
        dk = dot_nn(grad_scores, query[start:])
        dq = dot_tn(grad_scores, key_own[start:stop])
        if head == 0:
            dv_ref[start:stop] = dv
            dk_ref[start:stop] = dk
        else:
            dv_ref[start:stop] += dv
            dk_ref[start:stop] += dk
        if head == 0 and start == 0:
            dq_ref[...] = dq
        else:
            dq_ref[start:] += dq


def in_back_pair(dq_ref, dk_ref, dv_ref, weights, turned_ref, out_grad_ref, chunk_ref, total_ref):
    factor = 64 ** (-0.5)
    dq = (dq_ref[...] * factor).astype(BF)
    dk = (dk_ref[...] * factor).astype(BF)
    dv = dv_ref[...].astype(BF)
    grads = jnp.concatenate([dq, dk, dv], axis=1)
    shares = dot_nn(turned_ref[...], grads).astype(BF)
    for start in range(0, total_ref.shape[0], TILE):
        part = jnp.concatenate(
            [shares[start : start + TILE], out_grad_ref[start : start + TILE]], axis=1
        )
        chunk_ref[:, start // TILE] = part.reshape(8, 32, 512)
        columns = slice(start, start + TILE)
        total_ref[:, columns] += dot_nt(grads, weights[columns])
    return column_sum(dq.astype(F32)), column_sum(dv.astype(F32))


def tokens_back(tokens, grad, grad_middle, gain):
    normed, inv = row_norm(tokens.astype(F32))
    back = norm_back(grad, gain, normed, inv)
    return (grad_middle + back).astype(BF), column_sum(grad * normed), column_sum(grad)


def in_back_kernel(
    lengths_ref,
    proj_ref,
    ga_ref,
    lse_ref,
    delta_ref,
    wq_ref,
    wk_ref,
    wv_ref,
    first_ref,
    out_grad_ref,
    tokens_ref,
    gain_ref,
    grad_middle_ref,
    chunk_ref,
    bias_ref,
    tokens_grad_ref,
    sums_ref,
    dq_ref,
    dk_ref,
    dv_ref,
    turned_ref,
    total_ref,
):
    step = pl.program_id(0)
    q_ref, k_ref, v_ref = three(proj_ref)
    rows_all = tokens_ref.shape[0]

    @pl.when(step == 0)
    def _():
        turned_ref[...] = first_ref[...].T
        total_ref[...] = jnp.zeros_like(total_ref)

    for head in range(2):
        attention_back_head(
            head,
            cross_flag(lengths_ref, tokens_ref),
            q_ref,
            k_ref,
            v_ref,
            ga_ref,
            lse_ref.at[0],
            delta_ref[0, head : head + 1],
            dq_ref,
            dk_ref,
            dv_ref,
        )
    weights = jnp.concatenate([wq_ref[...], wk_ref[...], wv_ref[...]], axis=1)
    query_sum, value_sum = in_back_pair(
        dq_ref, dk_ref, dv_ref, weights, turned_ref, out_grad_ref, chunk_ref.at[0], total_ref
    )
    bias_ref[0, 0:1] = query_sum
    bias_ref[0, 1:2] = value_sum

    @pl.when(step == pl.num_programs(0) - 1)
    def _():
        gain_grad = jnp.zeros((1, total_ref.shape[1]), F32)
        shift_grad = jnp.zeros((1, total_ref.shape[1]), F32)
        for start in range(0, rows_all, TILE):
            rows = pl.ds(start, TILE)
            tokens_grad_ref[rows], gain_part, shift_part = tokens_back(
                tokens_ref[rows], total_ref[rows], grad_middle_ref[rows], gain_ref[...]
            )
            gain_grad = gain_grad + gain_part
            shift_grad = shift_grad + shift_part
        sums_ref[0:1] = gain_grad
        sums_ref[1:2] = shift_grad


def in_back(lengths, projected, ga, lse, delta, weights, first, out_grad, tokens, gain, grad_middle):
    rows, width = tokens.shape
    pairs = width // 128
    column = pl.BlockSpec((rows, 128), lambda p: (0, p))
    square = whole((rows, width))
    return pl.pallas_call(
        in_back_kernel,
        grid=(pairs,),
        in_specs=[
            pl.BlockSpec(memory_space=pltpu.SMEM),
            pl.BlockSpec((1, rows, 384), lambda p: (p, 0, 0)),
            column,
            pl.BlockSpec((1, 8, rows), lambda p: (p, 0, 0)),
            pl.BlockSpec((1, 2, rows), lambda p: (p, 0, 0)),
            pl.BlockSpec((width, 128), lambda p: (0, p)),
            pl.BlockSpec((width, 128), lambda p: (0, pairs + p)),
            pl.BlockSpec((width, 128), lambda p: (0, 2 * pairs + p)),
            square,
            column,
            square,
            whole((1, width)),
            square,
        ],
        out_specs=[
            pl.BlockSpec((1, 8, width // TILE, 32, 512), lambda p: (p, 0, 0, 0, 0)),
            pl.BlockSpec((1, 8, 128), lambda p: (p, 0, 0)),
            square,
            whole((8, width)),
        ],
        out_shape=[
            jax.ShapeDtypeStruct((pairs, 8, width // TILE, 32, 512), BF),
            jax.ShapeDtypeStruct((pairs, 8, 128), F32),
            jax.ShapeDtypeStruct((rows, width), BF),
            jax.ShapeDtypeStruct((8, width), F32),
        ],
        scratch_shapes=[
            pltpu.VMEM((rows, 128), F32),
            pltpu.VMEM((rows, 128), F32),
            pltpu.VMEM((rows, 128), F32),
            pltpu.VMEM((width, rows), BF),
            pltpu.VMEM((rows, width), F32),
        ],
        compiler_params=params(),
        name="in_back",
    )(
        lengths,
        projected,
        ga,
        lse,
        delta,
        weights,
        weights,
        weights,
        first,
        out_grad,
        tokens,
        gain,
        grad_middle,
    )


class Place:
    def __init__(self):
        self.z = lax.axis_index("dp")
        wide = lax.axis_index("wide")
        self.y = wide // 4
        self.x = (wide // 2) % 2
        self.c = wide % 2
        self.core = (self.z, wide + 1 - 2 * self.c)
        self.side = (self.z, wide + 2 - 4 * self.x)
        self.over = (self.z, wide + 4 - 8 * self.y)
        self.ranks = (self.z + 1 - 2 * (self.z % 2), (self.z + 2) % 4, 3 - self.z)
        self.planes = tuple((rank, wide) for rank in self.ranks)

    def greet(self, planes=True):
        barrier = pltpu.get_barrier_semaphore()
        peers = (self.core, self.side, self.over) + (self.planes if planes else ())
        for peer in peers:
            pl.semaphore_signal(barrier, inc=1, device_id=peer, device_id_type=MESH)
        pl.semaphore_wait(barrier, len(peers))


class WideGather:
    copies = 10

    def __init__(
        self, place, view, count, send, recv, first, source=None, last=None, offset=0, total=None
    ):
        y, x, c = place.y, place.x, place.c
        here, side, over, far = (y, x, c), (y, 1 - x, c), (1 - y, x, c), (1 - y, 1 - x, c)
        upper, lower = pl.ds(offset, count // 2), pl.ds(offset + count // 2, count // 2)
        both = pl.ds(offset, count)
        everything = both if total is None else pl.ds(0, total)

        def copy(index, slot, part, peer):
            destination = view(*slot, part)
            return pltpu.make_async_remote_copy(
                src_ref=source.at[part] if source is not None and slot is here else destination,
                dst_ref=destination,
                send_sem=send.at[first + index],
                recv_sem=recv.at[first + index],
                device_id=peer,
                device_id_type=MESH,
            )

        self.all = (
            copy(0, here, upper, place.side),
            copy(1, here, lower, place.over),
            copy(2, here, upper, place.over),
            copy(3, here, lower, place.side),
            None if total == 0 else copy(4, here, everything, place.core),
            copy(5, side, upper, place.over),
            copy(6, over, lower, place.side),
            copy(7, side, both, place.core),
            copy(8, over, both, place.core),
            copy(9, far, both, place.core),
        )
        self.own = None
        if source is not None and last is not None:
            self.own = pltpu.make_async_copy(source, view(*here, everything), last)

    def start(self):
        if self.own is not None:
            self.own.start()
        for copy in self.all[:5]:
            if copy is not None:
                copy.start()

    def relay(self, stage):
        waits, starts = (((0, 1), (5, 6)), ((2, 3), (7, 8)), ((5, 6), (9,)))[stage]
        for index in waits:
            self.all[index].wait_recv()
        for index in starts:
            self.all[index].start()

    def finish(self):
        for index in (4, 7, 8, 9):
            if self.all[index] is not None:
                self.all[index].wait_recv()
        for copy in self.all:
            if copy is not None:
                copy.wait_send()
        if self.own is not None:
            self.own.wait()


def blocks_of(target):
    return lambda y, x, c, rows: target.at[y, x, c, rows]


LAG = 2


class Reduction:
    slots = 2 * LAG
    deep = 3 * LAG
    keep = 3 * LAG + 2

    @classmethod
    def scratch(cls):
        n, k = cls.slots, cls.keep
        return [
            pltpu.VMEM((cls.deep, 2, 2, 4, 32, 512), BF),
            pltpu.VMEM((n, 2, 2, 4, 32, 512), BF),
            pltpu.VMEM((n, 2, 2, 4, 16, 512), BF),
            pltpu.VMEM((n, 2, 4, 16, 512), BF),
            pltpu.VMEM((n, 4, 32, 512), BF),
            pltpu.VMEM((n, 3, 32, 512), BF),
            pltpu.VMEM((n, 32, 512), BF),
            pltpu.VMEM((k, 3, 32, 512), BF),
            pltpu.SemaphoreType.DMA((6, k)),
            pltpu.SemaphoreType.DMA((6, k)),
            pltpu.SemaphoreType.DMA((cls.deep,)),
        ]

    def __init__(self, place, refs):
        self.place = place
        (
            self.chip,
            self.partner,
            self.first,
            self.second,
            self.plane,
            self.from_z,
            self.sums,
            self.shared,
            self.send,
            self.recv,
            self.local,
        ) = refs

    def copy(self, index, slot, source, target, peer):
        return pltpu.make_async_remote_copy(
            src_ref=source,
            dst_ref=target,
            send_sem=self.send.at[index, slot],
            recv_sem=self.recv.at[index, slot],
            device_id=peer,
            device_id_type=MESH,
        )

    def wait(self, index, slot, arrived):
        self.copy(index, slot, arrived, arrived, self.place.core).wait()

    def load(self, chunk, source):
        slot = chunk % self.deep
        return pltpu.make_async_copy(source, self.chip.at[slot], self.local.at[slot])

    def stage0(self, chunk, view):
        slot, c = chunk % self.slots, self.place.c
        self.copy(
            0, slot, view.at[:, :, 1 - c], self.partner.at[slot], self.place.core
        ).start()
        self.load(chunk, view.at[:, :, c]).start()

    def stage1(self, chunk):
        p, slot, index = self.place, chunk % self.slots, chunk % self.deep
        partner, chip, target = self.partner.at[slot], self.chip.at[index], self.first.at[slot]
        self.load(chunk, partner).wait()
        self.wait(0, slot, partner)
        chip[...] += partner[...]
        self.copy(1, slot, chip.at[:, 1 - p.x, :, pl.ds(0, 16)], target.at[0], p.side).start()
        self.copy(1, slot, chip.at[1 - p.y, :, :, pl.ds(16, 16)], target.at[1], p.over).start()

    def stage2(self, chunk):
        p, slot, index = self.place, chunk % self.slots, chunk % self.deep
        chip, arrived, target = self.chip.at[index], self.first.at[slot], self.second.at[slot]
        self.wait(1, slot, arrived)
        for k in range(2):
            chip[k, p.x, :, 0:16] += arrived[0, k]
            chip[p.y, k, :, 16:32] += arrived[1, k]
        self.copy(2, slot, chip.at[1 - p.y, p.x, :, pl.ds(0, 16)], target.at[0], p.over).start()
        self.copy(2, slot, chip.at[p.y, 1 - p.x, :, pl.ds(16, 16)], target.at[1], p.side).start()

    def stage3(self, chunk):
        p, slot, index = self.place, chunk % self.slots, chunk % self.deep
        arrived, mine, plane = self.second.at[slot], self.chip.at[index, p.y, p.x], self.plane
        self.wait(2, slot, arrived)
        plane[slot, :, 0:16] = mine[:, 0:16] + arrived[0]
        plane[slot, :, 16:32] = mine[:, 16:32] + arrived[1]
        for k in range(3):
            target = self.from_z.at[slot, k]
            self.copy(3, slot, plane.at[slot, p.ranks[k]], target, p.planes[k]).start()

    def stage4(self, chunk):
        slot = chunk % self.slots
        self.wait(3, slot, self.from_z.at[slot])
        total = self.plane[slot, self.place.z].astype(F32)
        for k in range(3):
            total = total + self.from_z[slot, k].astype(F32)
        return total

    def spread(self, chunk, total):
        slot, place = chunk % self.slots, chunk % self.keep
        self.sums[slot] = total.astype(BF)
        peer = self.place.planes[1]
        self.copy(4, place, self.sums.at[slot], self.shared.at[place, 0], peer).start()

    def stage5(self, chunk):
        slot, place, peer = chunk % self.slots, chunk % self.keep, self.place.planes[0]
        shared = self.shared.at[place]
        self.wait(4, place, shared.at[0])
        self.copy(5, place, self.sums.at[slot], shared.at[1], peer).start()
        self.copy(5, place, shared.at[0], shared.at[2], peer).start()

    def stage6(self, chunk):
        slot, place, ranks = chunk % self.slots, chunk % self.keep, self.place.ranks
        self.wait(5, place, self.shared.at[place, pl.ds(1, 2)])
        return [
            (self.place.z, self.sums[slot]),
            (ranks[1], self.shared[place, 0]),
            (ranks[0], self.shared[place, 1]),
            (ranks[2], self.shared[place, 2]),
        ]


class SmallReduction:
    @staticmethod
    def scratch():
        return [
            pltpu.VMEM((2, 2, 2, 4, 16, 512), BF),
            pltpu.VMEM((2, 2, 4, 16, 512), BF),
            pltpu.VMEM((2, 2, 4, 16, 512), BF),
            pltpu.VMEM((2, 4, 16, 512), BF),
            pltpu.VMEM((4, 16, 512), BF),
            pltpu.VMEM((3, 16, 512), BF),
            pltpu.SemaphoreType.DMA((4,)),
            pltpu.SemaphoreType.DMA((4,)),
        ]

    def __init__(self, place, refs):
        self.place = place
        self.source, self.chip, self.partner, self.first, self.second, self.from_z = refs[:6]
        self.send, self.recv = refs[6:]

    def copy(self, index, source, target, peer):
        return pltpu.make_async_remote_copy(
            src_ref=source,
            dst_ref=target,
            send_sem=self.send.at[index],
            recv_sem=self.recv.at[index],
            device_id=peer,
            device_id_type=MESH,
        )

    def wait(self, index, arrived):
        self.copy(index, arrived, arrived, self.place.core).wait()

    def stage0(self):
        p = self.place
        self.copy(0, self.source.at[:, :, 1 - p.c], self.partner, p.core).start()

    def stage1(self):
        p = self.place
        self.wait(0, self.partner)
        self.chip[...] = self.source[:, :, p.c] + self.partner[...]
        self.copy(1, self.chip.at[:, 1 - p.x], self.first, p.side).start()

    def stage2(self):
        p = self.place
        self.wait(1, self.first)
        for k in range(2):
            self.chip[k, p.x] += self.first[k]
        self.copy(2, self.chip.at[1 - p.y, p.x], self.second, p.over).start()

    def stage3(self):
        p = self.place
        self.wait(2, self.second)
        self.chip[p.y, p.x] += self.second[...]
        for k in range(3):
            block = self.chip.at[p.y, p.x, p.ranks[k]]
            self.copy(3, block, self.from_z.at[k], p.planes[k]).start()

    def stage4(self):
        p = self.place
        self.wait(3, self.from_z)
        total = self.chip[p.y, p.x, p.z].astype(F32)
        for k in range(3):
            total = total + self.from_z[k].astype(F32)
        return total


class Stream:
    def __init__(self, view, buffers, sems):
        self.view, self.buffers, self.sems = view, buffers, sems

    def copy(self, index):
        slot = index % 2
        return pltpu.make_async_copy(self.view(index), self.buffers.at[slot], self.sems.at[slot])

    def start(self, index):
        self.copy(index).start()

    def block(self, index):
        return self.buffers.at[index % 2]


def advance(streams, index, count):
    @pl.when(index + 1 < count)
    def _():
        for stream in streams:
            stream.start(index + 1)

    for stream in streams:
        stream.copy(index).wait()


def nearness(i):
    over = (i == 3) | (i >= 5)
    side = (i == 2) | (i == 4) | (i >= 6)
    other = (i == 1) | (i == 4) | (i == 5) | (i == 7)
    return over, side, other


def unit_index(i):
    wide = lax.axis_index("wide")
    y, x, c = wide // 4, wide // 2 % 2, wide % 2
    over, side, other = nearness(i)
    y, x, c = (jnp.where(flip, 1 - k, k) for flip, k in zip((over, side, other), (y, x, c)))
    return 4 * y + 2 * x + c


class NearGather:
    copies = 3

    def __init__(self, place, source, target, send, recv, first, last, rows=None):
        slot = target.at[place.y, place.x, place.c]
        if rows is not None:
            source, slot = source.at[rows], slot.at[rows]
        self.all = [
            pltpu.make_async_remote_copy(
                src_ref=source,
                dst_ref=slot,
                send_sem=send.at[first + index],
                recv_sem=recv.at[first + index],
                device_id=peer,
                device_id_type=MESH,
            )
            for index, peer in enumerate((place.side, place.over, place.core))
        ]
        self.own = pltpu.make_async_copy(source, slot, last)

    def start(self):
        self.own.start()
        for copy in self.all:
            copy.start()

    def finish(self):
        self.own.wait()
        for copy in self.all:
            copy.wait()


class LateGather:
    copies = 5

    def __init__(self, place, near, late, send, recv, first):
        rows = near.shape[-2]
        upper, lower = pl.ds(0, rows // 2), pl.ds(rows // 2, rows // 2)
        side, over = near.at[place.y, 1 - place.x, place.c], near.at[1 - place.y, place.x, place.c]

        def copy(index, source, target, peer):
            return pltpu.make_async_remote_copy(
                src_ref=source,
                dst_ref=target,
                send_sem=send.at[first + index],
                recv_sem=recv.at[first + index],
                device_id=peer,
                device_id_type=MESH,
            )

        self.all = (
            copy(0, side.at[upper], late.at[2, upper], place.over),
            copy(1, over.at[lower], late.at[2, lower], place.side),
            copy(2, side, late.at[0], place.core),
            copy(3, over, late.at[1], place.core),
            copy(4, late.at[2], late.at[3], place.core),
        )

    def start(self):
        for copy in self.all[:4]:
            copy.start()

    def relay(self):
        for copy in self.all[:2]:
            copy.wait_recv()
        self.all[4].start()

    def arrived(self, *indices):
        for index in indices:
            self.all[index].wait_recv()

    def finish(self):
        for copy in self.all:
            copy.wait_send()


class WeightStream(Stream):
    def __init__(self, near, late, buffers, sems):
        super().__init__(lambda i: late.at[0], buffers, sems)
        self.near, self.late = near, late

    def start(self, index):
        slot = index % 2
        target, sem = self.buffers.at[slot], self.sems.at[slot]

        @pl.when(index < 4)
        def _():
            block = unit_index(index)
            view = self.near.at[block // 4, block // 2 % 2, block % 2]
            pltpu.make_async_copy(view, target, sem).start()

        @pl.when(index >= 4)
        def _():
            pltpu.make_async_copy(self.late.at[index - 4], target, sem).start()


def dma_sems(count):
    return [pltpu.SemaphoreType.DMA((count,)), pltpu.SemaphoreType.DMA((count,))]


def to_planes(place, mine, landing, send, recv, first):
    return [
        pltpu.make_async_remote_copy(
            src_ref=mine,
            dst_ref=landing(k),
            send_sem=send.at[first + k],
            recv_sem=recv.at[first + k],
            device_id=place.planes[k],
            device_id_type=MESH,
        )
        for k in range(3)
    ]


class PlanesLast:
    copies = WideGather.copies + 6

    def __init__(self, place, source, target, send, recv, last):
        view = blocks_of(target.at[place.z])
        self.wide = WideGather(place, view, source.shape[0], send, recv, 0, source, last)

        def copy(index, rank, peer):
            blocks = target.at[rank, :, :, place.c]
            return pltpu.make_async_remote_copy(
                src_ref=blocks,
                dst_ref=blocks,
                send_sem=send.at[WideGather.copies + index],
                recv_sem=recv.at[WideGather.copies + index],
                device_id=peer,
                device_id_type=MESH,
            )

        self.across = [copy(k, place.z, place.planes[k]) for k in range(3)]
        self.over = [copy(3 + k, place.ranks[k], place.core) for k in range(3)]

    def start_across(self):
        self.wide.own.wait()
        for copy in self.across:
            copy.start()

    def start_over(self):
        for arrived, copy in zip(self.across, self.over):
            arrived.wait_recv()
            copy.start()

    def finish(self):
        self.wide.own = None
        self.wide.finish()
        for copy in self.across:
            copy.wait_send()
        for copy in self.over:
            copy.wait()


def first_kernel(
    lengths_ref,
    tokens_ref,
    in_ref,
    vec_ref,
    out_ref,
    up_ref,
    unit_ref,
    hs_ref,
    turned_ref,
    proj_ref,
    scaled_ref,
    scaled_turned_ref,
    attended_ref,
    lse_ref,
    vectors_ref,
    scale_ref,
    in_all,
    out_all,
    up_all,
    unit_all,
    held_ref,
    normed_ref,
    first_ref,
    vext_ref,
    send_in,
    recv_in,
    send_out,
    recv_out,
    send_ff,
    recv_ff,
    local,
):
    step = pl.program_id(0)
    place = Place()
    width = tokens_ref.shape[1]
    count = WideGather.copies
    lanes = (3 * width // 2 + 128, 3 * width // 2)
    across, early, late = [], [], None
    for group in range(2):
        held = held_ref.at[group, :, :, :, :, :, pl.ds(0, lanes[group])]
        first = group * (3 + 2 * count)

        def blocks(planes, held=held):
            return lambda y, x, c, rows: held.at[planes, y, x, c, rows]

        mine = held.at[0, place.y, place.x, place.c]
        across.append(
            to_planes(
                place,
                mine,
                lambda k, held=held: held.at[k + 1, place.y, place.x, place.c],
                send_in,
                recv_in,
                first,
            )
        )
        if group == 0:
            for part, planes in enumerate((pl.ds(0, 1), pl.ds(1, 3))):
                start = first + 3 + part * count
                early.append(WideGather(place, blocks(planes), 32, send_in, recv_in, start))
        else:
            late = WideGather(place, blocks(pl.ds(0, 4)), 32, send_in, recv_in, first + 3)
    orders = (place.z, *place.ranks)
    out = PlanesLast(place, out_ref, out_all, send_out, recv_out, local.at[2])
    ups = [
        NearGather(place, up_ref, up_all, send_ff, recv_ff, first, local.at[sem], rows)
        for first, sem, rows in (
            (count, 3, pl.ds(0, width // 4)),
            (count + NearGather.copies, 5, pl.ds(width // 4, width - width // 4)),
        )
    ]
    unit = WideGather(
        place, blocks_of(unit_all), 32, send_ff, recv_ff, 0, unit_ref, local.at[4]
    )
    keep = [
        pltpu.make_async_copy(
            held_ref.at[group, index, :, :, :, :, pl.ds(0, lanes[1])],
            in_all.at[rank, :, :, :, :, pl.ds(group * lanes[1], lanes[1])],
            local.at[12 + 4 * group + index],
        )
        for group in range(2)
        for index, rank in enumerate(orders)
    ]

    @pl.when(step == 0)
    def _():
        place.greet()
        half = width // 2
        for group in range(2):
            mine = held_ref.at[group, 0, place.y, place.x, place.c]
            fills = []
            for pair in range(4):
                for part in range(3):
                    column = part * width + (4 * group + pair) * 128
                    fills.append(
                        pltpu.make_async_copy(
                            in_ref.at[:, pl.ds(column, 128)],
                            mine.at[:, pl.ds(pair * 384 + part * 128, 128)],
                            local.at[20 + group * 12 + pair * 3 + part],
                        )
                    )
            for copy in fills:
                copy.start()
            if group == 0:
                mine[:, 3 * half : 3 * half + 128] = jnp.zeros((32, 128), BF)
                mine[:, 3 * half : 3 * half + 32] = vec_ref[...]
            for copy in fills:
                copy.wait()
            for copy in across[group]:
                copy.start()
            if group == 0:
                early[0].start()
        out.wide.start()
        ups[0].start()
        scale = hs_ref[...].astype(F32)
        for pair in range(width // 128):
            own = slice(pair * 128, (pair + 1) * 128)
            low_lanes = lax.broadcasted_iota(jnp.int32, (1, 128), 1) < 64
            scale_ref[0:1, own] = jnp.where(
                low_lanes, scale[:, 2 * pair : 2 * pair + 1], scale[:, 2 * pair + 1 : 2 * pair + 2]
            )
        for start in range(0, tokens_ref.shape[0], TILE):
            rows = pl.ds(start, TILE)
            normed, _ = row_norm(tokens_ref[rows].astype(F32))
            normed_ref[rows] = normed
        early[0].relay(0)
        for copy in across[0]:
            copy.wait_recv()
        early[1].start()
        early[0].relay(1)
        early[0].relay(2)
        early[1].relay(0)
        out.wide.relay(0)
        early[1].relay(1)
        out.wide.relay(1)
        for copy in across[1]:
            copy.wait_recv()
        late.start()
        early[1].relay(2)
        out.wide.relay(2)
        out.start_across()
        unit.start()
        for part in early:
            part.finish()
        for z in range(4):
            for y in range(2):
                tile = jnp.zeros((16, 128), F32)
                for x in range(2):
                    for c in range(2):
                        piece = held_ref[
                            0, orders[z], y, x, c, 0:16, 3 * half : 3 * half + 128
                        ].astype(F32)
                        spot = 32 * (2 * x + c)
                        tile = tile + (piece if spot == 0 else pltpu.roll(piece, spot, 1))
                vectors_ref[:, (2 * z + y) * 128 : (2 * z + y + 1) * 128] = tile
        for start in range(0, tokens_ref.shape[0], TILE):
            rows = pl.ds(start, TILE)
            first_ref[rows] = (normed_ref[rows] * vectors_ref[3:4] + vectors_ref[4:5]).astype(BF)

    @pl.when((step >= 2) & (step <= 4))
    def _():
        for stage in range(3):

            @pl.when(step == 2 + stage)
            def _():
                late.relay(stage)
                unit.relay(stage)

    @pl.when(step == 2)
    def _():
        ups[1].start()

    @pl.when(step == 5)
    def _():
        late.finish()
        for copy in keep:
            copy.start()

    @pl.when(step == 7)
    def _():
        out.start_over()

    @pl.when(step > 0)
    def _():
        pair = step - 1
        columns = pl.ds(pl.multiple_of(pair % 4 * 384, 128), 384)
        weights = jnp.concatenate(
            [held_ref[pair // 4, order, :, :, :, :, columns].reshape(TILE, 384) for order in orders]
        )
        own = pl.ds(pl.multiple_of(pair * 128, 128), 128)
        bias = jnp.concatenate(
            [vectors_ref[0:1, own], jnp.zeros((1, 128), F32), vectors_ref[1:2, own]], axis=1
        )
        project_pair(first_ref, weights, bias, proj_ref)
        attention_pair(
            cross_flag(lengths_ref, tokens_ref),
            *three(proj_ref),
            scale_ref[0:1, own],
            scaled_ref,
            attended_ref,
            lse_ref,
            vext_ref,
        )
        scaled_turned_ref[...] = scaled_ref[...].T

    @pl.when(step == pl.num_programs(0) - 1)
    def _():
        turned_ref[...] = first_ref[...].T
        for copy in (*across[0], *across[1]):
            copy.wait_send()
        for copy in keep:
            copy.wait()
        out.finish()
        unit.finish()
        for part in ups:
            part.finish()


def first_part(lengths, tokens, in_weight, vec, out_weight, up_weight, unit_rows, head_scale):
    rows, width = tokens.shape
    pairs = width // 128

    def at(step):
        return jnp.maximum(step - 1, 0)

    column = pl.BlockSpec((rows, 128), lambda s: (0, at(s)))
    held = (2, 4, 2, 2, 2, 32, 3 * width // 2 + 128)
    return pl.pallas_call(
        first_kernel,
        grid=(pairs + 1,),
        in_specs=[
            pl.BlockSpec(memory_space=pltpu.SMEM),
            whole((rows, width)),
            ANY,
            whole(vec.shape),
            ANY,
            ANY,
            ANY,
            whole(head_scale.shape),
        ],
        out_specs=[
            whole((width, rows)),
            pl.BlockSpec((1, rows, 384), lambda s: (at(s), 0, 0)),
            column,
            pl.BlockSpec((128, rows), lambda s: (at(s), 0)),
            column,
            pl.BlockSpec((1, 8, rows), lambda s: (at(s), 0, 0)),
            whole((16, width)),
            whole((8, width)),
            ANY,
            ANY,
            ANY,
            ANY,
        ],
        out_shape=[
            jax.ShapeDtypeStruct((width, rows), BF),
            jax.ShapeDtypeStruct((pairs, rows, 384), BF),
            jax.ShapeDtypeStruct((rows, width), BF),
            jax.ShapeDtypeStruct((width, rows), BF),
            jax.ShapeDtypeStruct((rows, width), F32),
            jax.ShapeDtypeStruct((pairs, 8, rows), F32),
            jax.ShapeDtypeStruct((16, width), F32),
            jax.ShapeDtypeStruct((8, width), F32),
            jax.ShapeDtypeStruct((4, 2, 2, 2, 32, 3 * width), BF),
            jax.ShapeDtypeStruct((4, 2, 2, 2, *out_weight.shape), BF),
            jax.ShapeDtypeStruct((2, 2, 2, *up_weight.shape), BF),
            jax.ShapeDtypeStruct((2, 2, 2, *unit_rows.shape), BF),
        ],
        scratch_shapes=[
            pltpu.VMEM(held, BF),
            pltpu.VMEM((rows, width), F32),
            pltpu.VMEM((rows, width), BF),
            pltpu.VMEM((rows, 256), BF),
            *dma_sems(6 + 3 * WideGather.copies),
            *dma_sems(PlanesLast.copies),
            *dma_sems(WideGather.copies + 2 * NearGather.copies),
            pltpu.SemaphoreType.DMA((44,)),
        ],
        compiler_params=params(collective_id=0, has_side_effects=True),
        name="first_part",
    )(lengths, tokens, in_weight, vec, out_weight, up_weight, unit_rows, head_scale)


def second_kernel(
    units,
    scaled_ref,
    weight_ref,
    vec_ref,
    tokens_ref,
    unit_ref,
    up_near,
    down_ref,
    branch_ref,
    middle_ref,
    turned_ref,
    act_ref,
    slope_ref,
    stats_ref,
    up_late,
    down_near,
    feed_ref,
    sums_ref,
    up_ref,
    send,
    recv,
    local,
    stream_sems,
):
    step = pl.program_id(0)
    lead = feed_ref.shape[0] // TILE
    place = Place()
    late = LateGather(place, up_near, up_late, send, recv, 0)
    down = NearGather(place, down_ref, down_near, send, recv, LateGather.copies, local.at[0])
    up = WeightStream(up_near, up_late, up_ref, stream_sems)

    @pl.when(step == 0)
    def _():
        place.greet(planes=False)
        late.start()
        up.start(0)
        sums_ref[...] = jnp.zeros_like(sums_ref)

    @pl.when(step == 2)
    def _():
        down.start()

    @pl.when(step < lead)
    def _():
        rows = pl.ds(pl.multiple_of(step * TILE, TILE), TILE)
        feed_ref[rows] = out_proj_rows(
            scaled_ref, weight_ref, vec_ref, tokens_ref, branch_ref, middle_ref
        )

    @pl.when(step >= lead)
    def _():
        block = step - lead

        @pl.when(block == 2)
        def _():
            late.relay()

        @pl.when(block == 3)
        def _():
            late.arrived(2, 3)

        @pl.when(block == 6)
        def _():
            late.arrived(4)

        advance((up,), block, 8)
        up_step(feed_ref, up.block(block), unit_ref.at[0], act_ref, slope_ref, sums_ref)

    @pl.when(step == pl.num_programs(0) - 1)
    def _():
        up_stats(units, stats_ref, sums_ref)
        turned_ref[...] = feed_ref[...].T
        late.finish()
        down.finish()


def second_part(scaled, out_weights, vectors, tokens, up_near, unit_vec, down_weight):
    rows, width = tokens.shape
    steps = 8
    lead = rows // TILE

    def early(step):
        return jnp.minimum(step, lead - 1)

    def unit(step):
        return unit_index(jnp.maximum(step - lead, 0))

    by_row = pl.BlockSpec((TILE, width), lambda s: (early(s), 0))
    block = pl.BlockSpec((1, rows, UNITS), lambda s: (unit(s), 0, 0))
    return pl.pallas_call(
        functools.partial(second_kernel, steps * UNITS),
        grid=(lead + steps,),
        in_specs=[
            by_row,
            whole((width, width)),
            whole(vectors.shape),
            by_row,
            pl.BlockSpec((1, unit_vec.shape[1], UNITS), lambda s: (unit(s), 0, 0)),
            ANY,
            ANY,
        ],
        out_specs=[
            by_row,
            by_row,
            whole((width, rows)),
            block,
            block,
            whole((rows, 128)),
            ANY,
            ANY,
        ],
        out_shape=[
            jax.ShapeDtypeStruct((rows, width), F32),
            jax.ShapeDtypeStruct((rows, width), F32),
            jax.ShapeDtypeStruct((width, rows), BF),
            jax.ShapeDtypeStruct((steps, rows, UNITS), BF),
            jax.ShapeDtypeStruct((steps, rows, UNITS), BF),
            jax.ShapeDtypeStruct((rows, 128), F32),
            jax.ShapeDtypeStruct((4, *up_near.shape[3:]), BF),
            jax.ShapeDtypeStruct((2, 2, 2, *down_weight.shape), BF),
        ],
        scratch_shapes=[
            pltpu.VMEM((rows, width), BF),
            pltpu.VMEM((2, rows, 128), F32),
            pltpu.VMEM((2, *up_near.shape[3:]), BF),
            *dma_sems(LateGather.copies + NearGather.copies),
            pltpu.SemaphoreType.DMA((1,)),
            pltpu.SemaphoreType.DMA((2,)),
        ],
        compiler_params=params(collective_id=2, has_side_effects=True),
        name="second_part",
    )(scaled, out_weights, vectors, tokens, unit_vec, up_near, down_weight)


def third_kernel(
    units,
    act_ref,
    stats_ref,
    vec_ref,
    cot_ref,
    middle_ref,
    shift_ref,
    down_near,
    mixed_ref,
    down_grad_ref,
    e_ref,
    all_stats_ref,
    vec_grad_ref,
    down_late,
    total_ref,
    sums_ref,
    low_ref,
    down_ref,
    send,
    recv,
    stream_sems,
):
    step = pl.program_id(0)
    place = Place()
    late = LateGather(place, down_near, down_late, send, recv, 0)
    down = WeightStream(down_near, down_late, down_ref, stream_sems)

    @pl.when(step == 0)
    def _():
        place.greet(planes=False)
        late.start()
        down.start(0)
        total_ref[...] = jnp.zeros_like(total_ref)
        sums_ref[...] = jnp.zeros_like(sums_ref)

    @pl.when(step == 3)
    def _():
        late.relay()
        late.arrived(2, 3)

    @pl.when(step == 6)
    def _():
        late.arrived(4)

    advance((down,), step, 8)
    down_step(
        act_ref, stats_ref, vec_ref.at[0], down.block(step), cot_ref, down_grad_ref, e_ref,
        vec_grad_ref, total_ref, sums_ref, low_ref
    )

    @pl.when(step == pl.num_programs(0) - 1)
    def _():
        down_end(
            units, stats_ref, middle_ref, shift_ref, mixed_ref, all_stats_ref, total_ref, sums_ref
        )
        late.finish()


def third_part(act, stats, vec, down_near, cotangent, middle, shift):
    rows, width = cotangent.shape
    steps = 8

    def unit(shape):
        return pl.BlockSpec((1, *shape), lambda s: (unit_index(s), 0, 0))

    block = unit((rows, UNITS))
    return pl.pallas_call(
        functools.partial(third_kernel, steps * UNITS),
        grid=(steps,),
        in_specs=[
            block,
            whole((rows, 128)),
            unit((vec.shape[1], UNITS)),
            whole((rows, width)),
            whole((rows, width)),
            whole((1, width)),
            ANY,
        ],
        out_specs=[
            whole((rows, width)),
            unit((UNITS, width)),
            block,
            whole((rows, 128)),
            unit((8, UNITS)),
            ANY,
        ],
        out_shape=[
            jax.ShapeDtypeStruct((rows, width), BF),
            jax.ShapeDtypeStruct((steps, UNITS, width), BF),
            jax.ShapeDtypeStruct((steps, rows, UNITS), BF),
            jax.ShapeDtypeStruct((rows, 128), F32),
            jax.ShapeDtypeStruct((steps, 8, UNITS), F32),
            jax.ShapeDtypeStruct((4, *down_near.shape[3:]), BF),
        ],
        scratch_shapes=[
            pltpu.VMEM((rows, width), F32),
            pltpu.VMEM((2, rows, 128), F32),
            pltpu.VMEM((rows, UNITS), BF),
            pltpu.VMEM((2, *down_near.shape[3:]), BF),
            *dma_sems(LateGather.copies),
            pltpu.SemaphoreType.DMA((2,)),
        ],
        compiler_params=params(collective_id=3, has_side_effects=True),
        name="third_part",
    )(act, stats, vec, cotangent, middle, shift, down_near)


NORMS_AT, COLUMNS_AT, HEADS_AT, TOKENS_AT, VECTORS_AT = 8, 16, 20, 28, 32
BACK_STEPS = VECTORS_AT + 7
OUT_TILE = 128


def chunk_at(time):
    chunk = jnp.where(time < 13, time, time - 1)
    chunk = jnp.where(time >= 20, (time + 17) // 2, chunk)
    return chunk, (time >= 0) & ((time < 13) | ((time >= 14) & (time < 20)) | ((time >= 20) & (time < 30) & (time % 2 == 1)))


def back_kernel(
    lengths_ref,
    unit_grad_ref,
    vec_ref,
    hs_ref,
    act_all,
    slope_all,
    e_all,
    stats_all,
    up_near,
    up_late,
    feed_turned_all,
    down_grad_all,
    cot_all,
    middle_all,
    branch_all,
    scaled_turned_all,
    attended_all,
    out_weight_all,
    proj_all,
    lse_all,
    in_weight_all,
    turned_all,
    tokens_all,
    down_out,
    up_out,
    in_out,
    out_out,
    vec_out,
    tokens_grad_all,
    up_grad_all,
    units_in_ref,
    up_ref,
    stats_ref,
    feed_turned_ref,
    cot_ref,
    norms_in_ref,
    scaled_turned_ref,
    attended_ref,
    out_weight_ref,
    proj_ref,
    lse_ref,
    in_weight_ref,
    turned_ref,
    tokens_ref,
    tokens_grad_ref,
    staged_ref,
    total_ref,
    low_ref,
    out_grad_ref,
    ga_ref,
    grad_middle_ref,
    delta_ref,
    delta_sum_ref,
    sums_ref,
    units_ref,
    dq_ref,
    dk_ref,
    dv_ref,
    chunk_ref,
    stream_sems,
    fetch_sems,
    *scratch,
):
    step = pl.program_id(0)
    place = Place()
    engine = Reduction(place, scratch[:11])
    small = SmallReduction(place, scratch[11:])
    pairs = proj_all.shape[0]

    def rows_of(array, size):
        return lambda i: array.at[pl.ds(pl.multiple_of(i * size, size), size)]

    def columns_of(array, size):
        return lambda i: array.at[:, pl.ds(pl.multiple_of(i * size, size), size)]

    def stream(number, view, buffers):
        return Stream(view, buffers, stream_sems.at[number])

    act, slope, e = (
        stream(k, lambda i, array=array: array.at[unit_index(i)], units_in_ref.at[k])
        for k, array in enumerate((act_all, slope_all, e_all))
    )
    up = WeightStream(up_near, up_late, up_ref, stream_sems.at[3])
    cot = stream(4, rows_of(cot_all, OUT_TILE), cot_ref)
    middle = stream(5, rows_of(middle_all, OUT_TILE), norms_in_ref.at[0])
    branch = stream(6, rows_of(branch_all, OUT_TILE), norms_in_ref.at[1])
    attended = stream(7, columns_of(attended_all, TILE), attended_ref)
    proj = stream(8, lambda i: proj_all.at[i], proj_ref)
    lse = stream(9, lambda i: lse_all.at[i], lse_ref)
    in_weight = stream(10, columns_of(in_weight_all, 384), in_weight_ref)
    tokens = stream(11, rows_of(tokens_all, TILE), tokens_ref)
    put = rows_of(tokens_grad_all, TILE)

    def put_tokens(i):
        return pltpu.make_async_copy(
            tokens_grad_ref.at[i % 2], put(i), stream_sems.at[12, i % 2]
        )

    fetches = [
        pltpu.make_async_copy(source, target, fetch_sems.at[index])
        for index, (source, target) in enumerate(
            (
                (stats_all, stats_ref),
                (feed_turned_all, feed_turned_ref),
                (scaled_turned_all, scaled_turned_ref),
                (out_weight_all, out_weight_ref),
                (turned_all, turned_ref),
            )
        )
    ]

    @pl.when(step == 0)
    def _():
        for item in (act, slope, e, up):
            item.start(0)
        for copy in fetches:
            copy.start()
        for item in (cot, middle, branch, attended, proj, lse, in_weight, tokens):
            item.copy(0).start()
        total_ref[...] = jnp.zeros_like(total_ref)
        sums_ref[...] = jnp.zeros_like(sums_ref)
        units_ref[...] = jnp.zeros_like(units_ref)
        place.greet()

    def store(index):
        block = unit_index(index)
        view = up_grad_all.at[block // 4, block // 2 % 2, block % 2]
        return pltpu.make_async_copy(staged_ref, view, fetch_sems.at[5])

    @pl.when((step >= 1) & (step <= NORMS_AT))
    def _():
        store(step - 1).wait()


    def stage(number, kind, action, tick):
        chunk, there = chunk_at(tick - number * LAG)
        up = ((chunk >= 8) & (chunk < 14)) | (chunk == 15) | (chunk == 17)
        wanted = {
            "all": there,
            "down": there & (chunk < 8),
            "up": there & up,
            "shared": there & ((chunk < 8) | up),
            "own": there & (chunk >= 8) & ~up,
        }

        @pl.when(wanted[kind])
        def _():
            action(chunk)

    def up_index(chunk):
        return jnp.where(chunk < 14, chunk - 8, (chunk - 3) // 2)

    def pair_index(chunk):
        return jnp.where(chunk < 18, (chunk - 14) // 2, chunk - 16)

    def put_down(chunk):
        for rank, block in engine.stage6(chunk):
            for half in range(2):

                @pl.when(chunk % 2 == half)
                def _():
                    down_out[chunk // 2, rank, :, half * 512 : half * 512 + 512] = block

    def put_up(chunk):
        for rank, block in engine.stage6(chunk):
            up_out[up_index(chunk), rank] = block

    def put_own(chunk):
        total = engine.stage4(chunk)
        first = pair_index(chunk) * 128
        for part in range(3):
            lanes = pl.ds(pl.multiple_of(part * 1024 + first, 128), 128)
            in_out[:, lanes] = total[:, part * 128 : part * 128 + 128]
        out_out[:, pl.ds(pl.multiple_of(first, 128), 128)] = total[:, 384:512]

    def take_down(chunk):
        lanes = pl.ds(pl.multiple_of(chunk % 2 * 512, 512), 512)
        engine.stage0(chunk, down_grad_all.at[:, :, :, chunk // 2, :, :, lanes])

    def take_up(chunk):
        engine.stage0(chunk, up_grad_all.at[:, :, :, up_index(chunk)])

    def take_own(chunk):
        engine.stage0(chunk, chunk_ref.at[pair_index(chunk) % 2])

    def reduce_step(tick):
        stage(6, "down", put_down, tick)
        stage(6, "up", put_up, tick)
        stage(5, "shared", engine.stage5, tick)
        stage(4, "shared", lambda chunk: engine.spread(chunk, engine.stage4(chunk)), tick)
        stage(4, "own", put_own, tick)
        stage(3, "all", engine.stage3, tick)
        stage(2, "all", engine.stage2, tick)
        stage(1, "all", engine.stage1, tick)
        stage(0, "down", take_down, tick)
        stage(0, "up", take_up, tick)

    tick = jnp.where(step < NORMS_AT, step, NORMS_AT + (step - NORMS_AT) // 4)
    tick = jnp.where(step < COLUMNS_AT, tick, step - 6)
    tick = jnp.where(step < HEADS_AT, tick, 2 * step - 26)
    tick = jnp.where(step < TOKENS_AT, tick, 30)
    tick = jnp.where(step < VECTORS_AT, tick, step - 1)
    within = (step > NORMS_AT) & (step < COLUMNS_AT) & (step % 4 != 0)
    within = within | ((step > TOKENS_AT) & (step < VECTORS_AT))

    @pl.when(~within)
    def _():
        reduce_step(tick)


    @pl.when(step < NORMS_AT)
    def _():
        advance((act, slope, e, up), step, NORMS_AT)

        @pl.when(step == 0)
        def _():
            fetches[0].wait()

        unit = unit_index(step)
        units_ref[unit, 0:1] = up_back_step(
            act.block(step),
            slope.block(step),
            e.block(step),
            stats_ref,
            up.block(step),
            low_ref,
            total_ref,
        )
        units_ref[unit, 1:3] = unit_grad_ref[unit, 0:2]

        @pl.when(step == 0)
        def _():
            fetches[1].wait()

        for left in range(0, UNITS, TILE):
            columns = slice(left, left + TILE)
            grad = dot_nn(feed_turned_ref[...], low_ref[:, columns]).astype(BF)
            staged_ref[:, :, :, columns] = grad.reshape(8, 4, 32, TILE)
        store(step).start()


    @pl.when((step >= NORMS_AT) & (step < COLUMNS_AT))
    def _():
        block = step - NORMS_AT
        rows = pl.ds(pl.multiple_of(block * OUT_TILE, OUT_TILE), OUT_TILE)
        advance((cot, middle, branch), block, COLUMNS_AT - NORMS_AT)
        grad_middle, low = norms_back(
            total_ref[rows],
            cot.block(block),
            middle.block(block),
            branch.block(block),
            vec_ref,
            sums_ref,
        )
        grad_middle_ref[rows] = grad_middle
        low_ref[rows] = low

    @pl.when((step >= COLUMNS_AT) & (step < HEADS_AT))
    def _():
        block = step - COLUMNS_AT
        columns = pl.ds(pl.multiple_of(block * TILE, TILE), TILE)
        advance((attended,), block, HEADS_AT - COLUMNS_AT)

        @pl.when(block == 0)
        def _():
            fetches[2].wait()
            fetches[3].wait()

        grad_out, delta = heads_back(
            low_ref[...],
            out_weight_ref[columns],
            hs_ref[0:1, columns],
            attended.block(block)[...],
        )
        ga_ref[:, columns] = grad_out
        delta_sum_ref[block, 0:1] = column_sum(delta)
        turned = delta.T
        for head in range(4):
            delta_ref[4 * block + head] = turned[head : head + 1]
        out_grad_ref[:, columns] = dot_nn(scaled_turned_ref[...], low_ref[:, columns]).astype(BF)

    @pl.when(step == HEADS_AT - 1)
    def _():
        total_ref[...] = jnp.zeros_like(total_ref)


    @pl.when((step >= HEADS_AT) & (step < TOKENS_AT))
    def _():
        pair = step - HEADS_AT
        columns = pl.ds(pl.multiple_of(pair * 128, 128), 128)
        advance((proj, lse, in_weight), pair, pairs)

        @pl.when(pair == 0)
        def _():
            fetches[4].wait()

        for head in range(2):
            if head == 1:
                reduce_step(tick + 1)
            attention_back_head(
                head,
                cross_flag(lengths_ref, total_ref),
                *[proj.block(pair).at[:, pl.ds(index * 128, 128)] for index in range(3)],
                ga_ref.at[:, columns],
                lse.block(pair),
                delta_ref[2 * pair + head],
                dq_ref,
                dk_ref,
                dv_ref,
            )
        query_sum, value_sum = in_back_pair(
            dq_ref,
            dk_ref,
            dv_ref,
            in_weight.block(pair)[...],
            turned_ref,
            out_grad_ref.at[:, columns],
            chunk_ref.at[pair % 2].reshape(8, 4, 32, 512),
            total_ref,
        )
        sums_ref[0:1, columns] = query_sum
        sums_ref[1:2, columns] = value_sum
        stage(0, "own", take_own, tick + 1)

    @pl.when((step >= TOKENS_AT) & (step < TOKENS_AT + 4))
    def _():
        block = step - TOKENS_AT
        rows = pl.ds(pl.multiple_of(block * TILE, TILE), TILE)
        advance((tokens,), block, 4)

        @pl.when(block >= 2)
        def _():
            put_tokens(block - 2).wait()

        result, gain_grad, shift_grad = tokens_back(
            tokens.block(block)[...], total_ref[rows], grad_middle_ref[rows], vec_ref[3:4]
        )
        tokens_grad_ref[block % 2] = result
        put_tokens(block).start()
        sums_ref[3:4] += gain_grad
        sums_ref[4:5] += shift_grad


    @pl.when(step == VECTORS_AT)
    def _():
        for y in range(2):
            for z in range(4):
                own = slice((2 * z + y) * 128, (2 * z + y + 1) * 128)
                for index in range(9):
                    lanes = slice(index % 4 * 128, index % 4 * 128 + 128)
                    row = 6 + index // 4
                    units_ref[8, row : row + 1, lanes] = sums_ref[index : index + 1, own]
                for x in range(2):
                    for c in range(2):
                        unit = 4 * y + 2 * x + c
                        units_ref[8, 0:3] = units_ref[unit, 0:3]
                        if (y, z, x, c) == (0, 0, 0, 0):
                            units_ref[8, 3:4] = sums_ref[9:10, 0:UNITS]
                            units_ref[8, 4:5] = sums_ref[9:10, UNITS : 2 * UNITS]
                            for block in range(4):
                                lanes = slice(block * 128, block * 128 + 128)
                                units_ref[8, 5:6, lanes] = delta_sum_ref[block, 0:1]
                        small.source[y, x, c, z] = units_ref[8].astype(BF)
        small.stage0()

    for index, action in enumerate((small.stage1, small.stage2, small.stage3)):

        @pl.when(step == VECTORS_AT + 1 + index)
        def _():
            action()

    @pl.when(step == VECTORS_AT + 4)
    def _():
        vec_out[...] = small.stage4()
        for block in range(2, 4):
            put_tokens(block).wait()


def back_part(
    lengths,
    act,
    slope,
    e,
    stats,
    up_near,
    up_late,
    feed_turned,
    unit_grad,
    down_grad,
    cotangent,
    middle,
    branch,
    scaled_turned,
    attended,
    out_weights,
    vectors,
    head_lanes,
    projected,
    lse,
    weights,
    turned,
    tokens,
):
    rows, width = tokens.shape
    pairs = width // 128

    return pl.pallas_call(
        back_kernel,
        grid=(BACK_STEPS,),
        in_specs=[
            pl.BlockSpec(memory_space=pltpu.SMEM),
            whole(unit_grad.shape),
            whole(vectors.shape),
            whole(head_lanes.shape),
            *[ANY] * 19,
        ],
        out_specs=[
            whole((4, 4, 32, 1024)),
            whole((8, 4, 32, 512)),
            whole((32, 3 * width)),
            whole((32, width)),
            whole((16, 512)),
            ANY,
            ANY,
        ],
        out_shape=[
            jax.ShapeDtypeStruct((4, 4, 32, 1024), BF),
            jax.ShapeDtypeStruct((8, 4, 32, 512), BF),
            jax.ShapeDtypeStruct((32, 3 * width), F32),
            jax.ShapeDtypeStruct((32, width), F32),
            jax.ShapeDtypeStruct((16, 512), F32),
            jax.ShapeDtypeStruct((rows, width), BF),
            jax.ShapeDtypeStruct((2, 2, 2, 8, 4, 32, UNITS), BF),
        ],
        scratch_shapes=[
            pltpu.VMEM((3, 2, rows, UNITS), BF),
            pltpu.VMEM((2, width, UNITS), BF),
            pltpu.VMEM((rows, 128), F32),
            pltpu.VMEM((width, rows), BF),
            pltpu.VMEM((2, OUT_TILE, width), BF),
            pltpu.VMEM((2, 2, OUT_TILE, width), F32),
            pltpu.VMEM((width, rows), BF),
            pltpu.VMEM((2, rows, TILE), F32),
            pltpu.VMEM((width, width), BF),
            pltpu.VMEM((2, rows, 384), BF),
            pltpu.VMEM((2, 8, rows), F32),
            pltpu.VMEM((2, width, 384), BF),
            pltpu.VMEM((width, rows), BF),
            pltpu.VMEM((2, TILE, width), BF),
            pltpu.VMEM((2, TILE, width), BF),
            pltpu.VMEM((8, 4, 32, UNITS), BF),
            pltpu.VMEM((rows, width), F32),
            pltpu.VMEM((rows, width), BF),
            pltpu.VMEM((width, width), BF),
            pltpu.VMEM((rows, width), BF),
            pltpu.VMEM((rows, width), F32),
            pltpu.VMEM((2 * pairs, 1, rows), F32),
            pltpu.VMEM((4, 8, 128), F32),
            pltpu.VMEM((16, width), F32),
            pltpu.VMEM((9, 16, UNITS), F32),
            pltpu.VMEM((rows, 128), F32),
            pltpu.VMEM((rows, 128), F32),
            pltpu.VMEM((rows, 128), F32),
            pltpu.VMEM((2, 2, 2, 2, 4, 32, 512), BF),
            pltpu.SemaphoreType.DMA((13, 2)),
            pltpu.SemaphoreType.DMA((6,)),
            *Reduction.scratch(),
            *SmallReduction.scratch(),
        ],
        compiler_params=params(collective_id=1, has_side_effects=True),
        name="back_part",
    )(
        lengths,
        unit_grad,
        vectors,
        head_lanes,
        act,
        slope,
        e,
        stats,
        up_near,
        up_late,
        feed_turned,
        down_grad.reshape(2, 2, 2, 4, 4, 32, width),
        cotangent,
        middle,
        branch,
        scaled_turned,
        attended,
        out_weights,
        projected,
        lse,
        weights,
        turned,
        tokens,
    )


def layer(staged, tokens, cotangent, lengths, attn, up, down, unit_vec, head_scale, down_bias):
    rows, width = tokens.shape
    heads = head_scale.shape[0]
    pairs = width // 128
    if staged:
        in_weight, out_weight, vec_block = attn
        (
            turned,
            projected,
            scaled,
            scaled_turned,
            attended,
            lse,
            vectors,
            head_lanes,
            weights,
            out_weights,
            up,
            unit_vec,
        ) = first_part(
            lengths, tokens, in_weight, vec_block, out_weight, up, unit_vec, head_scale[None, :]
        )
        weights = weights.reshape(width, 3 * width)
        out_weights = out_weights.reshape(width, width)
        unit_vec = unit_vec.reshape(-1, unit_vec.shape[-2], UNITS)
        branch, middle, feed_turned, act, slope, stats, up_late, down_near = second_part(
            scaled, out_weights, vectors, tokens, up, unit_vec, down
        )
        mixed, down_grad, e, stats, unit_grad, _ = third_part(
            act, stats, unit_vec, down_near, cotangent, middle, down_bias[None, :]
        )
    else:
        weights, out_weights, vectors = attn
        scale = head_scale.astype(F32)
        head_lanes = jnp.repeat(scale, width // heads)[None, :]
        first, projected, scaled, attended, lse = plain_first(
            lengths, tokens, weights, vectors, head_lanes
        )
        branch, middle, feed = out_proj(scaled, out_weights, vectors, tokens)
        act, slope, stats = up_pass(feed, up, unit_vec)
        mixed, down_grad, e, stats, unit_grad = down_pass(
            act, stats, unit_vec, down, cotangent, middle, down_bias[None, :]
        )
    if staged:
        down_total, up_total, in_total, out_total, vec_shares, tokens_grad, _ = back_part(
            lengths,
            act,
            slope,
            e,
            stats,
            up,
            up_late,
            feed_turned,
            unit_grad,
            down_grad,
            cotangent,
            middle,
            branch,
            scaled_turned,
            attended,
            out_weights,
            vectors,
            head_lanes,
            projected,
            lse,
            weights,
            turned,
            tokens,
        )
        return mixed, tokens_grad, down_total, up_total, in_total, out_total, vec_shares
    up_grad, up_bias_grad, grad_feed = up_back(
        act, slope, e, stats, up, feed
    )
    grad_middle, ga, out_grad, delta, sums = out_back(
        grad_feed,
        cotangent,
        middle,
        branch,
        scaled,
        attended,
        out_weights,
        vectors,
        head_lanes,
    )
    chunks, proj_bias, tokens_grad, pre_sums = in_back(
        lengths,
        projected,
        ga,
        lse,
        delta.reshape(pairs, 2, rows),
        weights,
        first,
        out_grad,
        tokens,
        vectors[3:4],
        grad_middle,
    )
    scale_grad = jnp.sum(delta, axis=1) / scale
    vec_grads = [
        proj_bias[:, 0].reshape(width),
        proj_bias[:, 1].reshape(width),
        sums[2],
        pre_sums[0],
        pre_sums[1],
        sums[5],
        sums[6],
        sums[7],
        sums[8],
    ]
    unit_grads = [up_bias_grad[:, 0], unit_grad[:, 0], unit_grad[:, 1]]
    return mixed, tokens_grad, chunks, up_grad, down_grad, vec_grads, unit_grads, sums[9], scale_grad


def body(
    axes,
    tokens,
    cotangent,
    lengths,
    in_weight,
    query_bias,
    value_bias,
    out_weight,
    out_bias,
    head_scale,
    pre_gain,
    pre_bias,
    post_gain,
    post_bias,
    feed_gain,
    feed_bias,
    up_weight,
    up_bias,
    mid_gain,
    mid_bias,
    down_weight,
    down_bias,
):
    planes, wide = axes
    every = ("dp", "wide")
    staged = (planes, wide) == (4, 8)
    rows, width = tokens.shape
    units = down_weight.shape[0] * wide
    steps = units // UNITS
    share = in_weight.shape[0]
    columns = [
        query_bias,
        value_bias,
        out_bias,
        pre_gain,
        pre_bias,
        post_gain,
        post_bias,
        feed_gain,
        feed_bias,
    ]
    index = lax.broadcasted_iota(jnp.int32, (32, up_bias.shape[0]), 0)
    unit_rows = jnp.where(index == 0, up_bias[None, :], jnp.zeros((), BF))
    unit_rows = jnp.where(index == 1, mid_gain[None, :], unit_rows)
    unit_rows = jnp.where(index == 2, mid_bias[None, :], unit_rows)
    if staged:
        index = lax.broadcasted_iota(jnp.int32, (32, share), 0)
        vec_block = jnp.zeros((32, share), BF)
        for row, column in enumerate(columns):
            vec_block = jnp.where(index == row, column[None, :], vec_block)
        attn = (in_weight, out_weight, vec_block)
        up, unit_vec, down = up_weight, unit_rows, down_weight
    else:
        flat = jnp.concatenate(columns).reshape(len(columns), share)
        attn = (
            lax.all_gather(in_weight, every, axis=0, tiled=True),
            lax.all_gather(out_weight, every, axis=0, tiled=True),
            jnp.pad(
                lax.all_gather(flat, every, axis=1, tiled=True), ((0, 16 - len(columns)), (0, 0))
            ).astype(F32),
        )
        up = lax.all_gather(up_weight, "wide", axis=1, tiled=True)
        up = up.reshape(width, steps, UNITS).transpose(1, 0, 2)
        unit_vec = lax.all_gather(unit_rows, "wide", axis=1, tiled=True)
        unit_vec = unit_vec.reshape(32, steps, UNITS).transpose(1, 0, 2)
        down = lax.all_gather(down_weight, "wide", axis=0, tiled=True)
        down = down.reshape(steps, UNITS, width)
    results = layer(
        staged,
        tokens,
        cotangent,
        lengths,
        attn,
        up,
        down,
        unit_vec,
        head_scale,
        down_bias,
    )
    heads = head_scale.shape[0]
    pairs = width // 128
    if staged:
        mixed, tokens_grad, down_total, up_total, in_total, out_total, vec_shares = results
        up_total = up_total.astype(F32).reshape(width, UNITS)
        down_total = down_total.astype(F32).reshape(UNITS, width)
        unit_totals = [vec_shares[index] for index in range(3)]
        down_sum = vec_shares[3:5].reshape(width)
        scale_sum = vec_shares[5].reshape(4, 128)[:, :4].reshape(heads) / head_scale.astype(F32)
        offset = share * lax.rem(lax.axis_index("wide"), 128 // share)
        own = vec_shares[6:9].reshape(12, 128)
        own = lax.dynamic_slice(own, (0, offset), (len(columns), share))
        vec_totals = [own[index] for index in range(len(columns))]
    else:
        (mixed, tokens_grad, chunks, up_grad, down_grad, vec_grads, unit_grads) = results[:7]
        down_sum, scale_sum = results[7:]

        def scatter(value, axis=0, over=every):
            return lax.psum_scatter(value, over, scatter_dimension=axis, tiled=True)

        def both_ways(value, axis):
            part = scatter(value.astype(BF), axis, "wide")
            return lax.psum(part, "dp").astype(F32)

        up_total = both_ways(up_grad.transpose(1, 0, 2).reshape(width, units), 1)
        down_total = both_ways(down_grad.reshape(units, width), 0)
        unit_totals = [
            lax.psum(scatter(item.reshape(units), 0, "wide"), "dp") for item in unit_grads
        ]
        down_sum, scale_sum = lax.psum((down_sum, scale_sum), every)
        vec_totals = [scatter(item) for item in vec_grads]
        natural = chunks.transpose(0, 2, 1, 3, 4).reshape(pairs, width, 512)
        in_total = natural[:, :, :384].reshape(pairs, width, 3, 128)
        in_total = scatter(in_total.transpose(1, 2, 0, 3).reshape(width, 3 * width).astype(F32))
        out_total = scatter(
            natural[:, :, 384:].transpose(1, 0, 2).reshape(width, width).astype(F32)
        )
    return (
        mixed,
        tokens_grad,
        in_total,
        vec_totals[0],
        vec_totals[1],
        out_total,
        vec_totals[2],
        scale_sum,
        vec_totals[3],
        vec_totals[4],
        vec_totals[5],
        vec_totals[6],
        vec_totals[7],
        vec_totals[8],
        up_total,
        unit_totals[0],
        unit_totals[1],
        unit_totals[2],
        down_total,
        down_sum,
    )


def solution(mesh):
    by_all = P(("dp", "wide"))
    rows_all = P(("dp", "wide"), None)
    axes = (mesh.shape["dp"], mesh.shape["wide"])
    return jax.shard_map(
        functools.partial(body, axes),
        mesh=mesh,
        in_specs=(
            rows_all,
            rows_all,
            rows_all,
            rows_all,
            by_all,
            by_all,
            rows_all,
            by_all,
            P(),
            by_all,
            by_all,
            by_all,
            by_all,
            by_all,
            by_all,
            P(None, "wide"),
            P("wide"),
            P("wide"),
            P("wide"),
            P("wide", None),
            P(),
        ),
        out_specs=(
            rows_all,
            rows_all,
            rows_all,
            by_all,
            by_all,
            rows_all,
            by_all,
            P(),
            by_all,
            by_all,
            by_all,
            by_all,
            by_all,
            by_all,
            P(None, "wide"),
            P("wide"),
            P("wide"),
            P("wide"),
            P("wide", None),
            P(),
        ),
        check_vma=False,
    )
```
